32 devices in a mesh: grp: 4 (over x, core), blk: 8 (over z, y).
Axes of the slice: x: 2, y: 2, z: 4, core: 2. Of those that a mesh axis runs over, the one named last changes fastest.
Arguments:
- tokens: bfloat16 [8192, 512], P(('grp', 'blk')), may hold values from -6 to 6
- seq_len: int32 [4, 4], P('grp'), may hold values from 0 to 1024, as said below
- qkv_weight: bfloat16 [2, 512, 1536], replicated, may hold values from -0.1875 to 0.1875
- out_weight: bfloat16 [2, 512, 512], replicated, may hold values from -0.75 to 0.75
- up_weight: bfloat16 [2, 512, 2048], replicated, may hold values from -0.25 to 0.25
- up_bias: float32 [2, 2048], replicated, may hold values from -3 to 3
- down_weight: bfloat16 [2, 2048, 512], replicated, may hold values from -0.125 to 0.125
- down_bias: float32 [2, 512], replicated, may hold values from -3 to 3
- alphas: float32 [2, 2], replicated, may hold values from 0.3 to 0.7
- cotangent: bfloat16 [8192, 512], P(('grp', 'blk')), may hold values from -6 to 6
Outputs:
- output: bfloat16 [8192, 512], P(('grp', 'blk'))
- input_grad: float32 [8192, 512], P(('grp', 'blk'))
- qkv_grad: float32 [2, 512, 1536], P(None, 'blk')
- out_grad: float32 [2, 512, 512], P(None, 'blk')
- up_grad: float32 [2, 512, 2048], P(None, 'blk')
- up_bias_grad: float32 [2, 2048], P(None, 'blk')
- down_grad: float32 [2, 2048, 512], P(None, 'blk')
- down_bias_grad: float32 [2, 512], P(None, 'blk')
- alpha_grad: float32 [2, 2], replicated
The draws below stay inside these ranges and needn't reach their ends.
Inputs may be any that keep to these rules, and one draw needn't show every extreme that they name: `seq_len`: each group's row holds k entries of 1024, then 4 - 2k entries of 512, then k zeros, for a k of 1 to 2 drawn for each group; the row sums to 2048.
All inputs are finite; a program needn't handle non-finite values.
Results may differ from the reference program's by a relative error of at most 0.023.
Values may be sent and summed in bfloat16 or wider, within the bound.
A program may use at most 192 MiB of HBM per device.

```python
import jax
import jax.numpy as jnp
from jax import lax

D = 512
HEADS = 8
HEAD_DIM = 64
FF = 2048
LAYERS = 2
TOK_DEV = 256
SHORT_LEN = 512
GROUPS = 4
GROUP_ROWS = 2048
SLOTS = 4
TOKENS = 8192
N_GRP = 4
N_BLK = 8


def draw_seq_len(key, part):
    key = jax.random.fold_in(key, 7)
    longer = jax.random.randint(key, (GROUPS, 1), 1, SLOTS // 2 + 1)
    slot_index = jnp.arange(SLOTS, dtype=jnp.int32)[None, :]
    shorter = SLOTS - 2 * longer
    lengths = jnp.where(slot_index < longer, 2 * SHORT_LEN, jnp.where(slot_index < longer + shorter, SHORT_LEN, 0))
    return lengths.astype(jnp.int32)


def strengthened(values, own_key, source, target, parts, factor):
    owner, partner = [(jnp.arange(values.shape[position]) // (values.shape[position] // parts)).reshape([-1 if axis == position else 1 for axis in range(values.ndim)]) for position in (source, target)]
    chosen = jax.random.permutation(own_key, parts)[partner]
    strong = (owner == chosen) | (owner == (partner + parts // 2) % parts)
    return jnp.where(strong, factor * values, values)


def level_of(rng, dims, split, least, high):
    factor_of, own = 1.0, jax.random.fold_in(rng, 6)
    for position, shards_of in split:
        draws = jnp.exp(jax.random.uniform(jax.random.fold_in(own, position), (shards_of,), jnp.float32, least / len(split), high / len(split)))
        factor_of = factor_of * jnp.repeat(draws, dims[position] // shards_of).reshape([-1 if axis == position else 1 for axis in range(len(dims))])
    return factor_of


def scatter_about(stream_key, dims, width, limit, shards=(), kind=jnp.bfloat16):
    array = jax.random.normal(stream_key, dims, jnp.float32) * width
    if len(shards) > 0:
        array = level_of(stream_key, dims, shards, -0.22, 0.18) * array
    return jnp.clip(array, min=-limit, max=limit).astype(kind)


def gaussian_with(own_key, dims, spread, most, cuts, heavy, kind=jnp.bfloat16):
    entries = spread * jax.random.normal(own_key, dims, jnp.float32)
    if cuts:
        entries = entries * level_of(own_key, dims, cuts, -0.22, 0.18)
    return jnp.clip(strengthened(entries, jax.random.fold_in(own_key, 3), *heavy), -most, most).astype(kind)


def setup_inputs(seed: int = 0) -> dict:
    splits = jax.random.split(jax.random.key(seed), 11)
    tokens = scatter_about(splits[0], (TOKENS, D), 1.0, 6.0, ((0, 32),))
    seq_len = draw_seq_len(jax.random.fold_in(splits[10], 71), 0)
    qkv_weight = scatter_about(splits[2], (LAYERS, D, 3 * D), (2 * D) ** -0.5, 0.1875)
    out_weight = scatter_about(splits[3], (LAYERS, D, D), (D // 8) ** -0.5, 0.75)
    up_weight = scatter_about(splits[4], (LAYERS, D, FF), D ** -0.5, 0.25)
    up_bias = scatter_about(splits[5], (LAYERS, FF), 0.5, 3.0, (), jnp.float32)
    down_weight = scatter_about(splits[6], (LAYERS, FF, D), FF ** -0.5, 0.125)
    down_bias = scatter_about(splits[7], (LAYERS, D), 0.5, 3.0, (), jnp.float32)
    alphas = jnp.clip(jax.random.uniform(splits[8], (LAYERS, 2), jnp.float32, 0.3, 0.7), 0.3, 0.7)
    cotangent = gaussian_with(splits[9], (TOKENS, D), 1.0, 6.0, ((0, 32),), (0, 1, 32, 2.75))
    return {"tokens": tokens, "seq_len": seq_len, "qkv_weight": qkv_weight, "out_weight": out_weight, "up_weight": up_weight, "up_bias": up_bias, "down_weight": down_weight, "down_bias": down_bias, "alphas": alphas, "cotangent": cotangent}


@jax.custom_vjp
def low(v):
    return lax.optimization_barrier(v.astype(jnp.bfloat16)).astype(jnp.float32)

@jax.custom_vjp
def low_back(v):
    return v

def low_keep(v):
    return (low(v), None)

def low_pass(kept, grad):
    return (grad,)

def back_keep(v):
    return (v, None)

def back_low(kept, grad):
    return (low(grad),)
low.defvjp(low_keep, low_pass)
low_back.defvjp(back_keep, back_low)

def layout(lengths):
    piece_rows = (lengths // N_BLK).astype(jnp.int32)
    end_rows = jnp.cumsum(piece_rows).astype(jnp.int32)
    start_rows = end_rows - piece_rows
    local_rows = jnp.arange(TOK_DEV, dtype=jnp.int32)
    segment = lax.optimization_barrier(jnp.sum((local_rows[:, None] >= end_rows[None, :]).astype(jnp.int32), axis=1)).astype(jnp.int32)
    picked = segment[:, None] == jnp.arange(SLOTS, dtype=jnp.int32)[None, :]
    offset = local_rows - lax.optimization_barrier(jnp.sum(jnp.where(picked, start_rows[None, :], 0), axis=1)).astype(jnp.int32)
    span_rows = lax.optimization_barrier(jnp.sum(jnp.where(picked, piece_rows[None, :], 0), axis=1)).astype(jnp.int32)
    return (segment, offset, span_rows)

def group_layout(lengths):
    segment, offset, span_rows = layout(lengths)
    device_rows = jnp.repeat(jnp.arange(N_BLK, dtype=jnp.int32), TOK_DEV)
    seg_all = jnp.tile(segment, N_BLK)
    pos_all = device_rows * jnp.tile(span_rows, N_BLK) + jnp.tile(offset, N_BLK)
    return (seg_all, pos_all)

def attention(queries, keys_all, values_all, seg_all, pos_all):
    total_rows = queries.shape[0]
    block_rows = min(512, total_rows)
    block_count = total_rows // block_rows
    score_scale = HEAD_DIM ** (-0.5)

    def one_block(block_args):
        query_block, query_seg, query_pos = block_args
        scores = jnp.einsum('qhd,khd->hqk', query_block, keys_all, precision=lax.Precision.HIGHEST) * score_scale
        scores = low_back(scores)
        allowed = (query_seg[:, None] == seg_all[None, :]) & (pos_all[None, :] <= query_pos[:, None])
        scores = jnp.where(allowed[None], scores, -1e+30)
        weights = low(jax.nn.softmax(scores, axis=-1))
        return jnp.einsum('hqk,khd->qhd', weights, values_all, precision=lax.Precision.HIGHEST)
    blocks = lax.map(jax.checkpoint(one_block), (queries.reshape(block_count, block_rows, HEADS, HEAD_DIM), seg_all.reshape(block_count, block_rows), pos_all.reshape(block_count, block_rows)))
    return blocks.reshape(total_rows, HEADS * HEAD_DIM)

def layer_forward(hidden, seg_all, pos_all, qkv_weight, out_weight, up_weight, up_bias, down_weight, down_bias, alpha_pair):
    total_rows = hidden.shape[0]
    rounded = low(hidden)
    projected = low_back(low(jnp.dot(rounded, qkv_weight, precision=lax.Precision.HIGHEST)))
    queries = projected[:, :D].reshape(total_rows, HEADS, HEAD_DIM)
    keys_all = projected[:, D:2 * D].reshape(total_rows, HEADS, HEAD_DIM)
    values_all = projected[:, 2 * D:].reshape(total_rows, HEADS, HEAD_DIM)
    heads_out = low_back(low(attention(queries, keys_all, values_all, seg_all, pos_all)))
    branch = low_back(jnp.dot(heads_out, out_weight, precision=lax.Precision.HIGHEST))
    middle = hidden + alpha_pair[0] * branch
    entered = low(middle)
    gate_pre = low_back(jnp.dot(entered, up_weight, precision=lax.Precision.HIGHEST) + up_bias)
    activated = low(jax.nn.gelu(gate_pre, approximate=False))
    second = low_back(jnp.dot(activated, down_weight, precision=lax.Precision.HIGHEST) + down_bias)
    return middle + alpha_pair[1] * second

def reference(tokens, seq_len, qkv_weight, out_weight, up_weight, up_bias, down_weight, down_bias, alphas, cotangent):
    seg_groups, pos_groups = jax.vmap(group_layout)(seq_len)

    def forward(inputs, qkv_all, out_all, up_all, up_bias_all, down_all, down_bias_all, alpha_all):
        grouped = inputs.reshape(N_GRP, GROUP_ROWS, D)

        def per_group(running, group_item):
            hidden, seg_all, pos_all = group_item
            for layer_index in range(LAYERS):
                hidden = layer_forward(hidden, seg_all, pos_all, qkv_all[layer_index], out_all[layer_index], up_all[layer_index], up_bias_all[layer_index], down_all[layer_index], down_bias_all[layer_index], alpha_all[layer_index])
            return (running, hidden)
        unused, outputs = lax.scan(per_group, jnp.zeros((), jnp.float32), (grouped, seg_groups, pos_groups))
        return outputs.reshape(TOKENS, D)
    result, pullback = jax.vjp(forward, tokens.astype(jnp.float32), qkv_weight.astype(jnp.float32), out_weight.astype(jnp.float32), up_weight.astype(jnp.float32), up_bias.astype(jnp.float32), down_weight.astype(jnp.float32), down_bias.astype(jnp.float32), alphas.astype(jnp.float32))
    grads = pullback(cotangent.astype(jnp.float32))
    return (result.astype(jnp.bfloat16), grads[0], grads[1], grads[2], grads[3], grads[4], grads[5], grads[6], grads[7])
```

```python
import functools

import jax
import jax.numpy as jnp
from jax import lax
from jax.experimental import pallas as pl
from jax.experimental.pallas import tpu as pltpu
from jax.sharding import PartitionSpec as P

HEADS = 8
LAYERS = 2
NEGATIVE = -1e30
MESH = pl.DeviceIdType.MESH
F32 = jnp.float32
BF16 = jnp.bfloat16

HALF = 128
RUNS = 8
DIM = 64
WIDTH = 512
FF = 2048
CUT = 512
TILE = 256
TILES = HALF * RUNS // TILE
PACK = HALF + DIM
CHUNK = 768
SMALL = FF + WIDTH + 128
EARLY = (192, 576)
LATE = (0, 192)


def nn(a, b):
    return lax.dot_general(a, b, (((1,), (0,)), ((), ())), preferred_element_type=F32)


def nt(a, b):
    return lax.dot_general(a, b, (((1,), (1,)), ((), ())), preferred_element_type=F32)


def layers_kernel(
    tokens, seq_len, alphas, up_bias, down_bias, cotangent, qkv_hbm, out_hbm, up_hbm, down_hbm,
    output, input_grad, qkv_grad, out_grad, up_grad, up_bias_grad, down_grad, down_bias_grad, alpha_grad,
    wqkv, wout, wup, wdown,
    hidden, grad, hid_t, attn_t, ent_t, act_t, branch, slope, second,
    dz, du, da, dqkv,
    pack_out, head_out, qkv_in, o_in, do_in, dqkv_in,
    kv, kv_t, rq, ro, o_t, lse, acc, dq_t, bias,
    parts, core_in, x_in, yz_in, final, small, small_grp, small_sum, small_blk,
    w_sem, a2a_send, a2a_recv, core_send, core_recv, x_send, x_recv, yz_send, yz_recv, fin_send, fin_recv,
    small_send, small_recv, wide_send, wide_recv, core_free, x_free,
):
    grp = lax.axis_index("grp")
    blk = lax.axis_index("blk")
    core = lax.rem(grp, 2)
    side = lax.div(grp, 2)
    lane = lax.broadcasted_iota(jnp.int32, (HALF, 128), 1)
    low = lane < DIM

    weight_copies = {}
    for layer in range(LAYERS):
        for number, (source, target) in enumerate(
            ((qkv_hbm, wqkv), (out_hbm, wout), (up_hbm, wup), (down_hbm, wdown))
        ):
            weight_copies[layer, number] = pltpu.make_async_copy(
                source.at[layer], target.at[layer], w_sem.at[layer, number]
            )
            weight_copies[layer, number].start()

    barrier = pltpu.get_barrier_semaphore()
    for step in range(1, RUNS):
        pl.semaphore_signal(
            barrier, inc=1, device_id=(grp, lax.rem(blk + step, RUNS)), device_id_type=MESH
        )
    for step in range(1, 4):
        pl.semaphore_signal(
            barrier, inc=1, device_id=(lax.rem(grp + step, 4), blk), device_id_type=MESH
        )

    key_row = lax.broadcasted_iota(jnp.int32, (TILE, TILE), 0)
    query_col = lax.broadcasted_iota(jnp.int32, (TILE, TILE), 1)
    later = key_row > query_col
    end_second = lax.div(seq_len[0, 0] + seq_len[0, 1], RUNS)
    key_sub = lax.rem(key_row, HALF) + HALF >= end_second
    query_sub = lax.rem(query_col, HALF) + HALF >= end_second
    apart = jnp.logical_xor(key_sub, query_sub)
    bias[0, 0] = jnp.zeros((TILE, TILE), F32)
    bias[0, 1] = jnp.where(later, NEGATIVE, 0.0)
    bias[1, 0] = jnp.where(apart, NEGATIVE, 0.0)
    bias[1, 1] = jnp.where(jnp.logical_or(later, apart), NEGATIVE, 0.0)
    for layer in range(LAYERS):
        for half in range(2):
            rq[layer, half, DIM:, :] = jnp.zeros((DIM, HALF * RUNS), BF16)
    ro[0:DIM, :] = jnp.zeros((DIM, HALF * RUNS), BF16)

    def rows_of(half):
        return pl.ds(pl.multiple_of(half * HALF, HALF), HALF)

    def slot_of(run):
        return lax.rem(run + RUNS - blk, RUNS)

    def exchange(kind, layer, half, outgoing, incoming):
        incoming[layer, half, 0] = outgoing[half, blk]
        for step in range(1, RUNS):
            peer = lax.rem(blk + step, RUNS)
            pltpu.make_async_remote_copy(
                src_ref=outgoing.at[half, peer],
                dst_ref=incoming.at[layer, half, RUNS - step],
                send_sem=a2a_send.at[kind, layer, half],
                recv_sem=a2a_recv.at[kind, layer, half],
                device_id=(grp, peer),
                device_id_type=MESH,
            ).start()

    def arrived(kind, layer, half, incoming):
        whole = incoming.at[layer, half, pl.ds(1, RUNS - 1)]
        pltpu.make_async_copy(whole, whole, a2a_recv.at[kind, layer, half]).wait()

    def left(kind, layer, half, outgoing):
        whole = outgoing.at[half, pl.ds(1, RUNS - 1)]
        pltpu.make_async_copy(whole, whole, a2a_send.at[kind, layer, half]).wait()

    def project(layer, half):
        rows = rows_of(half)
        rounded = hidden[half].astype(BF16)
        hid_t[layer, :, rows] = rounded.T
        if layer == 1:
            left(0, 0, half, pack_out)
        queries = nn(rounded, wqkv[layer, :, 0:WIDTH]) * (DIM ** -0.5)
        queries_t = queries.T.astype(BF16)
        keys = nn(rounded, wqkv[layer, :, WIDTH : 2 * WIDTH])
        values = nn(rounded, wqkv[layer, :, 2 * WIDTH : 3 * WIDTH])
        for pair in range(RUNS // 2):
            k_pair = keys[:, 128 * pair : 128 * pair + 128]
            v_pair = values[:, 128 * pair : 128 * pair + 128]
            first = jnp.where(low, k_pair, pltpu.roll(v_pair, DIM, 1))
            other = jnp.where(low, pltpu.roll(k_pair, DIM, 1), v_pair)
            pack_out[half, 2 * pair, 0:HALF, :] = first.astype(BF16)
            pack_out[half, 2 * pair + 1, 0:HALF, :] = other.astype(BF16)
        for head in range(RUNS):
            pack_out[half, head, HALF:, :] = queries_t[DIM * head : DIM * head + DIM, :]
        exchange(0, layer, half, pack_out, qkv_in)

    def attend(layer, half):
        arrived(0, layer, half, qkv_in)
        if layer == 1:
            left(1, 0, half, head_out)
        for run in range(RUNS):
            slot = slot_of(run)
            span = slice(HALF * run, HALF * run + HALF)
            block = qkv_in[layer, half, slot, 0:HALF, :]
            kv[layer, half, span, :] = block
            kv_t[layer, half, :, span] = block.T
            rq[layer, half, 0:DIM, span] = qkv_in[layer, half, slot, HALF:, :]
        for i in range(TILES):
            columns = slice(TILE * i, TILE * i + TILE)
            query_tile = rq[layer, half, :, columns]
            scores = []
            for j in range(i + 1):
                tile = nn(kv[layer, half, TILE * j : TILE * j + TILE, :], query_tile)
                scores.append(tile + bias[half, 1 if j == i else 0])
            largest = functools.reduce(
                jnp.maximum, [jnp.max(tile, axis=0, keepdims=True) for tile in scores]
            )
            total = jnp.zeros((1, TILE), F32)
            summed = jnp.zeros((DIM, TILE), F32)
            for j in range(i + 1):
                weight = jnp.exp(scores[j] - largest)
                total = total + jnp.sum(weight, axis=0, keepdims=True)
                summed = summed + nn(
                    kv_t[layer, half, DIM:, TILE * j : TILE * j + TILE], weight.astype(BF16)
                )
            summed = summed / total
            o_t[layer, half, :, columns] = summed
            lse[layer, half, :, columns] = largest + jnp.log(total)
            rounded = summed.astype(BF16)
            for run in range(2):
                head_out[half, 2 * i + run] = rounded[:, HALF * run : HALF * run + HALF]
        exchange(1, layer, half, head_out, o_in)

    def feed(layer, half):
        rows = rows_of(half)
        arrived(1, layer, half, o_in)
        for head in range(RUNS):
            attn_t[layer, DIM * head : DIM * head + DIM, rows] = o_in[layer, half, slot_of(head)]
        attn = attn_t[layer, :, rows].T
        grown = nn(attn, wout[layer])
        branch[layer, half] = grown
        middle = hidden[half] + alphas[layer, 0] * grown
        entered = middle.astype(BF16)
        ent_t[layer, :, rows] = entered.T
        total = jnp.zeros((HALF, WIDTH), F32)
        for step in range(FF // CUT):
            cut = slice(CUT * step, CUT * step + CUT)
            gate = nn(entered, wup[layer, :, cut]) + up_bias[layer : layer + 1, cut]
            risen = 0.5 * (1.0 + lax.erf(gate * (0.5 ** 0.5)))
            slope[layer, half, :, cut] = risen + gate * jnp.exp(-0.5 * gate * gate) * 0.3989422804014327
            active = (gate * risen).astype(BF16)
            act_t[layer, cut, rows] = active.T
            total = total + nn(active, wdown[layer, cut, :])
        total = total + down_bias[layer : layer + 1, :]
        second[layer, half] = total
        hidden[half] = middle + alphas[layer, 1] * total

    def total_of(values):
        return jnp.sum(jnp.sum(values, axis=0, keepdims=True), axis=1, keepdims=True)

    def feed_back(layer, half):
        rows = rows_of(half)
        start = grad[half]
        scaled = (alphas[layer, 1] * start).astype(BF16)
        dz[rows, :] = scaled
        alpha_second = total_of(start * second[layer, half])
        small[half, layer : layer + 1, FF : FF + WIDTH] = jnp.sum(scaled.astype(F32), axis=0, keepdims=True)
        middle = start
        for step in range(FF // CUT):
            cut = slice(CUT * step, CUT * step + CUT)
            gate = (nt(scaled, wdown[layer, cut, :]) * slope[layer, half, :, cut]).astype(BF16)
            du[rows, cut] = gate
            small[half, layer : layer + 1, cut] = jnp.sum(gate.astype(F32), axis=0, keepdims=True)
            middle = middle + nt(gate, wup[layer, :, cut])
        grad[half] = middle
        alpha_first = total_of(middle * branch[layer, half])
        column = lax.broadcasted_iota(jnp.int32, (1, 128), 1)
        small[half, layer : layer + 1, FF + WIDTH :] = jnp.where(
            column == 0, alpha_first, jnp.where(column == 1, alpha_second, 0.0)
        )
        mixed = (alphas[layer, 0] * middle).astype(BF16)
        da[rows, :] = mixed
        spread = nt(wout[layer], mixed).astype(BF16)
        left(*((1, 1) if layer == 1 else (2, 1)), half, head_out)
        for head in range(RUNS):
            head_out[half, head] = spread[DIM * head : DIM * head + DIM, :]
        exchange(2, layer, half, head_out, do_in)

    def attend_back(layer, half):
        arrived(2, layer, half, do_in)
        for run in range(RUNS):
            ro[DIM:, HALF * run : HALF * run + HALF] = do_in[layer, half, slot_of(run)]
        for i in range(TILES):
            columns = slice(TILE * i, TILE * i + TILE)
            query_tile = rq[layer, half, :, columns]
            grad_tile = ro[:, columns]
            log_total = lse[layer, half, :, columns]
            delta = jnp.sum(
                ro[DIM:, columns].astype(F32) * o_t[layer, half, :, columns], axis=0, keepdims=True
            )
            query_grad = jnp.zeros((DIM, TILE), F32)
            for j in range(i + 1):
                span = slice(TILE * j, TILE * j + TILE)
                keys = kv[layer, half, span, :]
                weight = jnp.exp(nn(keys, query_tile) + bias[half, 1 if j == i else 0] - log_total)
                scored = (weight * (nn(keys, grad_tile) - delta)).astype(BF16)
                term = nt(scored, query_tile) + nt(weight.astype(BF16), grad_tile)
                if j == i:
                    acc[span, :] = term
                else:
                    acc[span, :] += term
                query_grad = query_grad + nn(kv_t[layer, half, 0:DIM, span], scored)
            dq_t[:, columns] = query_grad * (DIM ** -0.5)
        left(*((0, 1) if layer == 1 else (3, 1)), half, pack_out)
        for run in range(RUNS):
            span = slice(HALF * run, HALF * run + HALF)
            pack_out[half, run, 0:HALF, :] = acc[span, :].astype(BF16)
            pack_out[half, run, HALF:, :] = dq_t[:, span].astype(BF16)
        exchange(3, layer, half, pack_out, dqkv_in)

    def project_back(layer, half):
        rows = rows_of(half)
        arrived(3, layer, half, dqkv_in)
        turned = jnp.concatenate(
            [dqkv_in[layer, half, slot_of(head), HALF:, :] for head in range(RUNS)], axis=0
        )
        dqkv[rows, 0:WIDTH] = turned.T
        for pair in range(RUNS // 2):
            first = dqkv_in[layer, half, slot_of(2 * pair), 0:HALF, :].astype(F32)
            other = dqkv_in[layer, half, slot_of(2 * pair + 1), 0:HALF, :].astype(F32)
            k_pair = jnp.where(low, first, pltpu.roll(other, DIM, 1))
            v_pair = jnp.where(low, pltpu.roll(first, DIM, 1), other)
            dqkv[rows, WIDTH + 128 * pair : WIDTH + 128 * pair + 128] = k_pair.astype(BF16)
            dqkv[rows, 2 * WIDTH + 128 * pair : 2 * WIDTH + 128 * pair + 128] = v_pair.astype(BF16)
        grad[half] = grad[half] + nt(dqkv[rows, :], wqkv[layer])

    def scatter_rows(layer, result, first_row):
        for place in range(RUNS):
            for quarter in range(4):
                parts[layer, quarter, place, first_row : first_row + DIM, :] = result[
                    DIM * place : DIM * place + DIM, 128 * quarter : 128 * quarter + 128
                ].astype(BF16)

    def early_grads(layer):
        scatter_rows(layer, nn(attn_t[layer], da[...]), 192)
        for step in range(FF // CUT):
            cut = slice(CUT * step, CUT * step + CUT)
            scatter_rows(layer, nn(ent_t[layer], du[:, cut]), 256 + DIM * step)
        for place in range(RUNS):
            result = nn(act_t[layer, TILE * place : TILE * place + TILE, :], dz[...])
            for quarter in range(4):
                parts[layer, quarter, place, 512:768, :] = result[
                    :, 128 * quarter : 128 * quarter + 128
                ].astype(BF16)

    def late_grads(layer):
        for step in range(3):
            scatter_rows(layer, nn(hid_t[layer], dqkv[:, WIDTH * step : WIDTH * step + WIDTH]), DIM * step)

    def core_copy(layer, stage, across):
        first, count = (EARLY, LATE)[stage]
        rows = pl.ds(first, count)
        return pltpu.make_async_remote_copy(
            src_ref=parts.at[layer, 2 * across + 1 - core, :, rows],
            dst_ref=core_in.at[across, :, rows],
            send_sem=core_send.at[layer, stage, across],
            recv_sem=core_recv.at[layer, stage, across],
            device_id=(2 * side + 1 - core, blk),
            device_id_type=MESH,
        )

    def x_copy(layer, stage):
        first, count = (EARLY, LATE)[stage]
        rows = pl.ds(first, count)
        return pltpu.make_async_remote_copy(
            src_ref=parts.at[layer, 2 * (1 - side) + core, :, rows],
            dst_ref=x_in.at[:, rows],
            send_sem=x_send.at[layer, stage],
            recv_sem=x_recv.at[layer, stage],
            device_id=(2 * (1 - side) + core, blk),
            device_id_type=MESH,
        )

    def yz_copy(layer, stage, step):
        first, count = (EARLY, LATE)[stage]
        rows = pl.ds(first, count)
        peer = lax.rem(blk + step, RUNS)
        return pltpu.make_async_remote_copy(
            src_ref=parts.at[layer, grp, peer, rows],
            dst_ref=yz_in.at[layer, RUNS - step, rows],
            send_sem=yz_send.at[layer, stage, step],
            recv_sem=yz_recv.at[layer, stage, RUNS - step],
            device_id=(grp, peer),
            device_id_type=MESH,
        )

    def final_copy(layer, stage, step):
        first, count = (EARLY, LATE)[stage]
        rows = pl.ds(first, count)
        return pltpu.make_async_remote_copy(
            src_ref=final.at[layer, grp, rows],
            dst_ref=final.at[layer, grp, rows],
            send_sem=fin_send.at[layer, stage, step],
            recv_sem=fin_recv.at[layer, stage, step],
            device_id=(lax.rem(grp + step, 4), blk),
            device_id_type=MESH,
        )

    def core_start(layer, stage):
        if layer == 0:
            pl.semaphore_wait(core_free.at[stage], 1)
        for across in range(2):
            core_copy(layer, stage, across).start()

    def core_done(layer, stage):
        first, count = (EARLY, LATE)[stage]
        rows = pl.ds(first, count)
        for across in range(2):
            core_copy(layer, stage, across).wait()
        for turn in range(2):
            across = 1 - side if turn == 0 else side

            def add(place, carry):
                own = parts[layer, 2 * across + core, place, rows, :].astype(F32)
                own = own + core_in[across, place, rows, :].astype(F32)
                parts[layer, 2 * across + core, place, rows, :] = own.astype(BF16)
                return carry

            lax.fori_loop(0, RUNS, add, 0)
            if turn == 0:
                if layer == 0:
                    pl.semaphore_wait(x_free.at[stage], 1)
                x_copy(layer, stage).start()
        if layer == 1:
            pl.semaphore_signal(
                core_free.at[stage],
                inc=1,
                device_id=(2 * side + 1 - core, blk),
                device_id_type=MESH,
            )

    def x_done(layer, stage):
        first, count = (EARLY, LATE)[stage]
        rows = pl.ds(first, count)
        x_copy(layer, stage).wait()

        def add(place, carry):
            own = parts[layer, grp, place, rows, :].astype(F32) + x_in[place, rows, :].astype(F32)
            parts[layer, grp, place, rows, :] = own.astype(BF16)
            return carry

        lax.fori_loop(0, RUNS, add, 0)
        if layer == 1:
            pl.semaphore_signal(
                x_free.at[stage],
                inc=1,
                device_id=(2 * (1 - side) + core, blk),
                device_id_type=MESH,
            )
        for step in range(1, RUNS):
            yz_copy(layer, stage, step).start()

    def yz_done(layer, stage):
        first, count = (EARLY, LATE)[stage]
        rows = pl.ds(first, count)
        for step in range(1, RUNS):
            yz_copy(layer, stage, step).wait()
        total = parts[layer, grp, blk, rows, :].astype(F32)
        for slot in range(1, RUNS):
            total = total + yz_in[layer, slot, rows, :].astype(F32)
        final[layer, grp, rows, :] = total.astype(BF16)
        for step in range(1, 4):
            final_copy(layer, stage, step).start()

    def final_done(layer, stage):
        for step in range(1, 4):
            final_copy(layer, stage, step).wait()
        for quarter in range(4):
            at = slice(128 * quarter, 128 * quarter + 128)

            def block(first, count):
                return final[layer, quarter, first : first + count, :].astype(F32)

            if stage == 0:
                out_grad[layer, :, at] = block(192, DIM)
                for step in range(4):
                    up_grad[layer, :, CUT * step + 128 * quarter : CUT * step + 128 * quarter + 128] = block(
                        256 + DIM * step, DIM
                    )
                down_grad[layer, :, at] = block(512, 256)
            else:
                for step in range(3):
                    qkv_grad[layer, :, WIDTH * step + 128 * quarter : WIDTH * step + 128 * quarter + 128] = block(
                        DIM * step, DIM
                    )

    def small_copy(step):
        return pltpu.make_async_remote_copy(
            src_ref=small_grp.at[grp],
            dst_ref=small_grp.at[grp],
            send_sem=small_send.at[step],
            recv_sem=small_recv.at[step],
            device_id=(lax.rem(grp + step, 4), blk),
            device_id_type=MESH,
        )

    def wide_copy(step):
        return pltpu.make_async_remote_copy(
            src_ref=small_blk.at[blk],
            dst_ref=small_blk.at[blk],
            send_sem=wide_send.at[step],
            recv_sem=wide_recv.at[step],
            device_id=(grp, lax.rem(blk + step, RUNS)),
            device_id_type=MESH,
        )

    def small_start():
        small_grp[grp] = small[0] + small[1]
        for step in range(1, 4):
            small_copy(step).start()

    def small_middle():
        for step in range(1, 4):
            small_copy(step).wait()
        small_blk[blk] = (small_grp[0] + small_grp[1]) + (small_grp[2] + small_grp[3])
        for step in range(1, RUNS):
            wide_copy(step).start()

    def small_done():
        for step in range(1, RUNS):
            wide_copy(step).wait()
        total = small_blk[0]
        for place in range(1, RUNS):
            total = total + small_blk[place]
        small_sum[...] = total
        up_bias_grad[...] = small_sum[:, pl.ds(pl.multiple_of(blk * 256, 256), 256)]
        pair = small_sum[:, pl.ds(pl.multiple_of(FF + 128 * lax.div(blk, 2), 128), 128)]
        turned = pltpu.roll(pair, DIM, 1)
        down_bias_grad[...] = jnp.where(lax.rem(blk, 2) == 1, turned, pair)[:, 0:DIM]
        alpha_grad[...] = small_sum[:, FF + WIDTH : FF + WIDTH + 2]

    def halves(*phases):
        def both(half, carry):
            for phase in phases:
                phase(half)
            return carry

        lax.fori_loop(0, 2, both, 0)

    for half in range(2):
        hidden[half] = tokens[HALF * half : HALF * half + HALF, :].astype(F32)
    pl.semaphore_wait(barrier, RUNS - 1 + 3)
    weight_copies[0, 0].wait()
    halves(functools.partial(project, 0))
    for number in range(1, 4):
        weight_copies[0, number].wait()
    halves(functools.partial(attend, 0))
    weight_copies[1, 0].wait()
    halves(functools.partial(feed, 0), functools.partial(project, 1))
    for number in range(1, 4):
        weight_copies[1, number].wait()
    halves(functools.partial(attend, 1))
    halves(functools.partial(feed, 1))
    for half in range(2):
        output[HALF * half : HALF * half + HALF, :] = hidden[half].astype(BF16)
        grad[half] = cotangent[HALF * half : HALF * half + HALF, :].astype(F32)

    halves(functools.partial(feed_back, 1))
    early_grads(1)
    core_start(1, 0)
    halves(functools.partial(attend_back, 1))
    core_done(1, 0)
    halves(functools.partial(project_back, 1), functools.partial(feed_back, 0))
    small_start()
    late_grads(1)
    core_start(1, 1)
    early_grads(0)
    core_start(0, 0)
    x_done(1, 0)
    core_done(1, 1)
    halves(functools.partial(attend_back, 0))
    small_middle()
    core_done(0, 0)
    halves(functools.partial(project_back, 0))
    for half in range(2):
        input_grad[HALF * half : HALF * half + HALF, :] = grad[half]
    late_grads(0)
    core_start(0, 1)
    x_done(1, 1)
    yz_done(1, 0)
    core_done(0, 1)
    small_done()
    x_done(0, 0)
    yz_done(1, 1)
    x_done(0, 1)
    final_done(1, 0)
    final_done(1, 1)
    yz_done(0, 0)
    yz_done(0, 1)
    final_done(0, 0)
    final_done(0, 1)

    for half in range(2):
        left(2, 0, half, head_out)
        left(3, 0, half, pack_out)


def fast_body(
    tokens, seq_len, qkv_weight, out_weight, up_weight, up_bias, down_weight, down_bias, alphas, cotangent
):
    whole = pl.BlockSpec(memory_space=pltpu.VMEM)
    scalar = pl.BlockSpec(memory_space=pltpu.SMEM)
    far = pl.BlockSpec(memory_space=pl.ANY)
    shape = jax.ShapeDtypeStruct
    rows = HALF * RUNS

    def vmem(*dims):
        return pltpu.VMEM(dims, BF16)

    def wide(*dims):
        return pltpu.VMEM(dims, F32)

    dma = pltpu.SemaphoreType.DMA
    return tuple(
        pl.pallas_call(
            layers_kernel,
            out_shape=(
                shape((2 * HALF, WIDTH), BF16),
                shape((2 * HALF, WIDTH), F32),
                shape((LAYERS, DIM, 3 * WIDTH), F32),
                shape((LAYERS, DIM, WIDTH), F32),
                shape((LAYERS, DIM, FF), F32),
                shape((LAYERS, FF // RUNS), F32),
                shape((LAYERS, FF // RUNS, WIDTH), F32),
                shape((LAYERS, DIM), F32),
                shape((LAYERS, 2), F32),
            ),
            in_specs=[whole, scalar, scalar, whole, whole, whole, far, far, far, far],
            out_specs=(whole,) * 9,
            scratch_shapes=[
                vmem(LAYERS, WIDTH, 3 * WIDTH),
                vmem(LAYERS, WIDTH, WIDTH),
                vmem(LAYERS, WIDTH, FF),
                vmem(LAYERS, FF, WIDTH),
                wide(2, HALF, WIDTH),
                wide(2, HALF, WIDTH),
                vmem(LAYERS, WIDTH, 2 * HALF),
                vmem(LAYERS, WIDTH, 2 * HALF),
                vmem(LAYERS, WIDTH, 2 * HALF),
                vmem(LAYERS, FF, 2 * HALF),
                wide(LAYERS, 2, HALF, WIDTH),
                wide(LAYERS, 2, HALF, FF),
                wide(LAYERS, 2, HALF, WIDTH),
                vmem(2 * HALF, WIDTH),
                vmem(2 * HALF, FF),
                vmem(2 * HALF, WIDTH),
                vmem(2 * HALF, 3 * WIDTH),
                vmem(2, RUNS, PACK, 128),
                vmem(2, RUNS, DIM, 128),
                vmem(LAYERS, 2, RUNS, PACK, 128),
                vmem(LAYERS, 2, RUNS, DIM, 128),
                vmem(LAYERS, 2, RUNS, DIM, 128),
                vmem(LAYERS, 2, RUNS, PACK, 128),
                vmem(LAYERS, 2, rows, 128),
                vmem(LAYERS, 2, 128, rows),
                vmem(LAYERS, 2, 128, rows),
                vmem(128, rows),
                wide(LAYERS, 2, DIM, rows),
                wide(LAYERS, 2, 1, rows),
                wide(rows, 128),
                wide(DIM, rows),
                wide(2, 2, TILE, TILE),
                vmem(LAYERS, 4, RUNS, CHUNK, 128),
                vmem(2, RUNS, CHUNK, 128),
                vmem(RUNS, CHUNK, 128),
                vmem(LAYERS, RUNS, CHUNK, 128),
                vmem(LAYERS, 4, CHUNK, 128),
                wide(2, LAYERS, SMALL),
                wide(4, LAYERS, SMALL),
                wide(LAYERS, SMALL),
                wide(RUNS, LAYERS, SMALL),
                dma((LAYERS, 4)),
                dma((4, LAYERS, 2)),
                dma((4, LAYERS, 2)),
                dma((LAYERS, 2, 2)),
                dma((LAYERS, 2, 2)),
                dma((LAYERS, 2)),
                dma((LAYERS, 2)),
                dma((LAYERS, 2, RUNS)),
                dma((LAYERS, 2, RUNS)),
                dma((LAYERS, 2, 4)),
                dma((LAYERS, 2, 4)),
                dma((4,)),
                dma((4,)),
                dma((RUNS,)),
                dma((RUNS,)),
                pltpu.SemaphoreType.REGULAR((2,)),
                pltpu.SemaphoreType.REGULAR((2,)),
            ],
            compiler_params=pltpu.CompilerParams(
                collective_id=0, has_side_effects=True, vmem_limit_bytes=63 * 1024 * 1024
            ),
            name="layers",
        )(
            tokens, seq_len, alphas, up_bias, down_bias, cotangent,
            qkv_weight, out_weight, up_weight, down_weight,
        )
    )


def layout(seq_len, local_count, cycle_size):
    piece_rows = seq_len[0] // cycle_size
    end_rows = jnp.cumsum(piece_rows)
    start_rows = end_rows - piece_rows
    local_rows = jnp.arange(local_count, dtype=jnp.int32)
    segment = jnp.sum((local_rows[:, None] >= end_rows[None, :]).astype(jnp.int32), axis=1)
    picked = segment[:, None] == jnp.arange(seq_len.shape[1], dtype=jnp.int32)[None, :]
    offset = local_rows - jnp.sum(jnp.where(picked, start_rows[None, :], 0), axis=1)
    span_rows = jnp.sum(jnp.where(picked, piece_rows[None, :], 0), axis=1)
    return (segment, offset, span_rows)


def gelu_exact(values):
    return jax.nn.gelu(values, approximate=False)


def key_block(whole, geometry, block_index, head_count):
    query_seg, query_pos, seg_all, pos_all, block_rows, score_scale = geometry
    first_row = block_index * block_rows
    key_piece = lax.dynamic_slice_in_dim(whole, first_row, block_rows, 0)
    key_seg = lax.dynamic_slice_in_dim(seg_all, first_row, block_rows, 0)
    key_pos = lax.dynamic_slice_in_dim(pos_all, first_row, block_rows, 0)
    half_width = key_piece.shape[1] // 2
    keys_part = key_piece[:, :half_width].reshape(block_rows, head_count, -1)
    values_part = key_piece[:, half_width:].reshape(block_rows, head_count, -1)
    return (keys_part, values_part, key_seg, key_pos)


def block_scores(queries, keys_part, key_seg, key_pos, geometry):
    query_seg, query_pos, seg_all, pos_all, block_rows, score_scale = geometry
    scores = (
        jnp.einsum("qhd,khd->hqk", queries, keys_part, preferred_element_type=jnp.float32)
        * score_scale
    )
    allowed = (query_seg[:, None] == key_seg[None, :]) & (key_pos[None, :] <= query_pos[:, None])
    return (scores, allowed[None])


def attend(queries, whole, geometry):
    row_count, head_count, head_dim = queries.shape
    block_count = whole.shape[0] // geometry[4]

    def statistics(running, block_index):
        largest, totals = running
        keys_part, values_part, key_seg, key_pos = key_block(
            whole, geometry, block_index, head_count
        )
        scores, allowed = block_scores(queries, keys_part, key_seg, key_pos, geometry)
        newest = jnp.maximum(largest, jnp.max(jnp.where(allowed, scores, NEGATIVE), axis=2))
        weights = jnp.where(allowed, jnp.exp(scores - newest[:, :, None]), 0.0)
        totals = totals * jnp.exp(largest - newest) + jnp.sum(weights, axis=2)
        return ((newest, totals), None)

    initial = (
        jnp.full((head_count, row_count), NEGATIVE, jnp.float32),
        jnp.zeros((head_count, row_count), jnp.float32),
    )
    (largest, totals), unused = lax.scan(statistics, initial, jnp.arange(block_count))
    log_total = largest + jnp.log(totals)

    def weighted(output_sum, block_index):
        keys_part, values_part, key_seg, key_pos = key_block(
            whole, geometry, block_index, head_count
        )
        scores, allowed = block_scores(queries, keys_part, key_seg, key_pos, geometry)
        probs = jnp.where(allowed, jnp.exp(scores - log_total[:, :, None]), 0.0).astype(
            jnp.bfloat16
        )
        output_sum = output_sum + jnp.einsum(
            "hqk,khd->qhd", probs, values_part, preferred_element_type=jnp.float32
        )
        return (output_sum, None)

    output_sum, unused = lax.scan(
        weighted, jnp.zeros((row_count, head_count, head_dim), jnp.float32), jnp.arange(block_count)
    )
    return (output_sum, log_total)


def attend_back(queries, whole, log_total, delta_sum, grad_heads, geometry):
    row_count, head_count, head_dim = queries.shape
    block_rows = geometry[4]
    score_scale = geometry[5]
    block_count = whole.shape[0] // block_rows

    def gradients(query_grad, block_index):
        keys_part, values_part, key_seg, key_pos = key_block(
            whole, geometry, block_index, head_count
        )
        scores, allowed = block_scores(queries, keys_part, key_seg, key_pos, geometry)
        probs = jnp.where(allowed, jnp.exp(scores - log_total[:, :, None]), 0.0)
        grad_probs = jnp.einsum(
            "qhd,khd->hqk", grad_heads, values_part, preferred_element_type=jnp.float32
        )
        grad_scores = (probs * (grad_probs - delta_sum[:, :, None])).astype(jnp.bfloat16)
        query_grad = (
            query_grad
            + jnp.einsum("hqk,khd->qhd", grad_scores, keys_part, preferred_element_type=jnp.float32)
            * score_scale
        )
        key_grad = (
            jnp.einsum("hqk,qhd->khd", grad_scores, queries, preferred_element_type=jnp.float32)
            * score_scale
        )
        value_grad = jnp.einsum(
            "hqk,qhd->khd",
            probs.astype(jnp.bfloat16),
            grad_heads,
            preferred_element_type=jnp.float32,
        )
        joined = jnp.concatenate(
            [key_grad.reshape(block_rows, -1), value_grad.reshape(block_rows, -1)], axis=1
        )
        return (query_grad, joined)

    query_grad, stacked = lax.scan(
        gradients,
        jnp.zeros((row_count, head_count, head_dim), jnp.float32),
        jnp.arange(block_count),
    )
    return (query_grad, stacked.reshape(whole.shape[0], -1))


def layer_forward(hidden, layer_index, weights, geometry):
    qkv_weight, out_weight, up_weight, up_bias, down_weight, down_bias, alphas = weights
    row_count, model_width = hidden.shape
    projection = qkv_weight[layer_index]
    rounded = hidden.astype(jnp.bfloat16)
    queries = (
        jnp.dot(rounded, projection[:, :model_width], preferred_element_type=jnp.float32)
        .astype(jnp.bfloat16)
        .reshape(row_count, HEADS, -1)
    )
    key_value = jnp.dot(
        rounded, projection[:, model_width:], preferred_element_type=jnp.float32
    ).astype(jnp.bfloat16)
    whole = lax.all_gather(key_value, "blk", axis=0, tiled=True)
    heads_out, log_total = attend(queries, whole, geometry)
    heads_rounded = heads_out.reshape(row_count, model_width).astype(jnp.bfloat16)
    branch = jnp.dot(heads_rounded, out_weight[layer_index], preferred_element_type=jnp.float32)
    alpha_pair = alphas[layer_index]
    middle = hidden + alpha_pair[0] * branch
    entered = middle.astype(jnp.bfloat16)
    gate_pre = (
        jnp.dot(entered, up_weight[layer_index], preferred_element_type=jnp.float32)
        + up_bias[layer_index]
    )
    activated = gelu_exact(gate_pre).astype(jnp.bfloat16)
    second = (
        jnp.dot(activated, down_weight[layer_index], preferred_element_type=jnp.float32)
        + down_bias[layer_index]
    )
    result = middle + alpha_pair[1] * second
    saved = (
        rounded,
        queries,
        key_value,
        whole,
        heads_out,
        heads_rounded,
        log_total,
        branch,
        entered,
        gate_pre,
        activated,
        second,
    )
    return (result, saved)


def layer_backward(grad_hidden, saved, layer_index, weights, geometry):
    qkv_weight, out_weight, up_weight, up_bias, down_weight, down_bias, alphas = weights
    (
        rounded,
        queries,
        key_value,
        saved_whole,
        heads_out,
        heads_rounded,
        log_total,
        branch,
        entered,
        gate_pre,
        activated,
        second,
    ) = saved
    row_count = grad_hidden.shape[0]
    alpha_pair = alphas[layer_index]
    grad_second = (alpha_pair[1] * grad_hidden).astype(jnp.bfloat16)
    alpha_second = jnp.sum(grad_hidden * second)
    bias_down = jnp.sum(grad_second.astype(jnp.float32), axis=0)
    grad_down = jnp.einsum("tf,td->fd", activated, grad_second, preferred_element_type=jnp.float32)
    grad_act = jnp.einsum(
        "td,fd->tf", grad_second, down_weight[layer_index], preferred_element_type=jnp.float32
    )
    unused, gelu_pull = jax.vjp(gelu_exact, gate_pre)
    grad_gate = gelu_pull(grad_act)[0].astype(jnp.bfloat16)
    bias_up = jnp.sum(grad_gate.astype(jnp.float32), axis=0)
    grad_up = jnp.einsum("td,tf->df", entered, grad_gate, preferred_element_type=jnp.float32)
    grad_middle = grad_hidden + jnp.einsum(
        "tf,df->td", grad_gate, up_weight[layer_index], preferred_element_type=jnp.float32
    )
    grad_branch = (alpha_pair[0] * grad_middle).astype(jnp.bfloat16)
    alpha_first = jnp.sum(grad_middle * branch)
    grad_proj_out = jnp.einsum(
        "te,td->ed", heads_rounded, grad_branch, preferred_element_type=jnp.float32
    )
    grad_heads = (
        jnp.einsum(
            "td,ed->te", grad_branch, out_weight[layer_index], preferred_element_type=jnp.float32
        )
        .astype(jnp.bfloat16)
        .reshape(queries.shape)
    )
    delta_sum = jnp.sum(grad_heads.astype(jnp.float32) * heads_out, axis=2).T
    whole = lax.all_gather(key_value, "blk", axis=0, tiled=True)
    query_grad, key_terms = attend_back(queries, whole, log_total, delta_sum, grad_heads, geometry)
    key_grads = lax.psum_scatter(
        key_terms.astype(jnp.bfloat16), "blk", scatter_dimension=0, tiled=True
    )
    grad_proj = jnp.concatenate(
        [query_grad.reshape(row_count, -1).astype(jnp.bfloat16), key_grads], axis=1
    )
    grad_qkv = jnp.einsum("td,te->de", rounded, grad_proj, preferred_element_type=jnp.float32)
    grad_input = grad_middle + jnp.einsum(
        "te,de->td", grad_proj, qkv_weight[layer_index], preferred_element_type=jnp.float32
    )
    layer_grads = (
        grad_qkv,
        grad_proj_out,
        grad_up,
        bias_up,
        grad_down,
        bias_down,
        jnp.stack([alpha_first, alpha_second]),
    )
    return (grad_input, layer_grads)


def reduce_all(layer_results, cycle_size):
    stacked = [
        jnp.stack([layer_entry[member] for layer_entry in layer_results], axis=0)
        for member in range(6)
    ]
    alpha_tiles = jnp.stack(
        [jnp.tile(layer_entry[6], cycle_size) for layer_entry in layer_results], axis=0
    )
    shares = (
        lax.psum_scatter(
            stacked[0].astype(jnp.bfloat16), "blk", scatter_dimension=1, tiled=True
        ).astype(jnp.float32),
        lax.psum_scatter(
            stacked[1].astype(jnp.bfloat16), "blk", scatter_dimension=1, tiled=True
        ).astype(jnp.float32),
        lax.psum_scatter(
            stacked[2].astype(jnp.bfloat16), "blk", scatter_dimension=1, tiled=True
        ).astype(jnp.float32),
        lax.psum_scatter(
            stacked[3].astype(jnp.bfloat16), "blk", scatter_dimension=1, tiled=True
        ).astype(jnp.float32),
        lax.psum_scatter(
            stacked[4].astype(jnp.bfloat16), "blk", scatter_dimension=1, tiled=True
        ).astype(jnp.float32),
        lax.psum_scatter(
            stacked[5].astype(jnp.bfloat16), "blk", scatter_dimension=1, tiled=True
        ).astype(jnp.float32),
        lax.psum_scatter(
            alpha_tiles.astype(jnp.bfloat16), "blk", scatter_dimension=1, tiled=True
        ).astype(jnp.float32),
    )
    return (
        lax.psum(shares[0].astype(jnp.bfloat16), "grp").astype(jnp.float32),
        lax.psum(shares[1].astype(jnp.bfloat16), "grp").astype(jnp.float32),
        lax.psum(shares[2].astype(jnp.bfloat16), "grp").astype(jnp.float32),
        lax.psum(shares[3].astype(jnp.bfloat16), "grp").astype(jnp.float32),
        lax.psum(shares[4].astype(jnp.bfloat16), "grp").astype(jnp.float32),
        lax.psum(shares[5].astype(jnp.bfloat16), "grp").astype(jnp.float32),
        lax.psum(shares[6].astype(jnp.bfloat16), "grp").astype(jnp.float32),
    )


def body(
    tokens,
    seq_len,
    qkv_weight,
    out_weight,
    up_weight,
    up_bias,
    down_weight,
    down_bias,
    alphas,
    cotangent,
):
    row_count, model_width = tokens.shape
    cycle_size = lax.axis_size("blk")
    cycle_place = lax.axis_index("blk")
    head_dim = model_width // HEADS
    total_rows = cycle_size * row_count
    block_rows = min(max(row_count, 512), total_rows)
    segment, offset, span_rows = layout(seq_len, row_count, cycle_size)
    query_pos = cycle_place * span_rows + offset
    seg_all = jnp.tile(segment, cycle_size)
    pos_all = jnp.repeat(jnp.arange(cycle_size, dtype=jnp.int32), row_count) * jnp.tile(
        span_rows, cycle_size
    ) + jnp.tile(offset, cycle_size)
    geometry = (segment, query_pos, seg_all, pos_all, block_rows, head_dim ** (-0.5))
    weights = (qkv_weight, out_weight, up_weight, up_bias, down_weight, down_bias, alphas)
    hidden = tokens.astype(jnp.float32)
    saved_layers = []
    for layer_index in range(LAYERS):
        hidden, saved = layer_forward(hidden, layer_index, weights, geometry)
        saved_layers.append(saved)
    output = hidden.astype(jnp.bfloat16)
    grad_hidden = cotangent.astype(jnp.float32)
    layer_results = []
    for layer_index in reversed(range(LAYERS)):
        grad_hidden, layer_grads = layer_backward(
            grad_hidden, saved_layers[layer_index], layer_index, weights, geometry
        )
        layer_results.insert(0, layer_grads)
    finals = reduce_all(layer_results, cycle_size)
    return (
        output,
        grad_hidden,
        finals[0],
        finals[1],
        finals[2],
        finals[3],
        finals[4],
        finals[5],
        finals[6],
    )


def solution(mesh):
    placed = (
        P(("grp", "blk"), None),
        P("grp", None),
        P(),
        P(),
        P(),
        P(),
        P(),
        P(),
        P(),
        P(("grp", "blk"), None),
    )
    sizes = (mesh.shape["grp"], mesh.shape["blk"])
    return jax.shard_map(
        fast_body if sizes == (4, RUNS) else body,
        mesh=mesh,
        in_specs=placed,
        out_specs=(
            P(("grp", "blk"), None),
            P(("grp", "blk"), None),
            P(None, "blk", None),
            P(None, "blk", None),
            P(None, "blk", None),
            P(None, "blk"),
            P(None, "blk", None),
            P(None, "blk"),
            P(),
        ),
        check_vma=False,
    )
```

```python
import functools

import jax
import jax.numpy as jnp
from jax import lax
from jax.experimental import pallas as pl
from jax.experimental.pallas import tpu as pltpu
from jax.sharding import PartitionSpec as P

HEADS = 8
LAYERS = 2
NEGATIVE = -1e30
MESH = pl.DeviceIdType.MESH
F32 = jnp.float32
BF16 = jnp.bfloat16

HALF = 128
RUNS = 8
TEAM = 4
OWN = RUNS // TEAM
DIM = 64
WIDTH = 512
FF = 2048
CUT = 512
TILE = 256
PACK = HALF + DIM
CHUNK = 768
SMALL = FF + WIDTH + 128
ROWS = (((192, 288), (480, 288)), ((0, 96), (96, 96)))
SPAN = ((192, 576), (0, 192))


def nn(a, b):
    return lax.dot_general(a, b, (((1,), (0,)), ((), ())), preferred_element_type=F32)


def nt(a, b):
    return lax.dot_general(a, b, (((1,), (1,)), ((), ())), preferred_element_type=F32)


def layers_kernel(
    tokens, seq_len, alphas, up_bias, down_bias, cotangent, qkv_hbm, out_hbm, up_hbm, down_hbm,
    final_hbm, output_hbm, input_grad_hbm, small_final,
    wqkv, wout, wup, wdown,
    tok_in, cot_in, flag_out, flag_in, back_out, out_in, grad_in,
    hidden, grad, hid_t, attn_t, ent_t, act_t, branch, slope, second,
    dz, du, da, dqkv,
    pack_out, head_out, qkv_in, o_in, do_in, dqkv_in,
    kv, kv_t, rq, ro, o_t, lse, acc, dq_t, bias,
    parts, core_in, x_in, y_in, z_in, final, small, small_in, small_z, small_sum,
    w_sem, move_send, move_recv, a2a_send, a2a_recv, core_send, core_recv, x_send, x_recv, y_send, y_recv,
    z_send, z_recv, fin_send, fin_recv, small_send, small_recv, out_sem, core_free, x_free, y_free,
):
    grp = lax.axis_index("grp")
    blk = lax.axis_index("blk")
    core = lax.rem(grp, 2)
    side = lax.div(grp, 2)
    yy = lax.rem(blk, 2)
    zz = lax.div(blk, 2)
    member = 2 * core + yy
    far_side = 2 * (1 - side) + core
    low = lax.broadcasted_iota(jnp.int32, (HALF, 128), 1) < DIM

    def place(c, x, z, y):
        return (2 * x + c, 2 * z + y)

    core_peer = place(1 - core, side, zz, yy)
    x_peer = place(core, 1 - side, zz, yy)
    y_peer = place(core, side, zz, 1 - yy)

    weight_copies = {}
    for layer in range(LAYERS):
        for number, (source, target) in enumerate(
            ((qkv_hbm, wqkv), (out_hbm, wout), (up_hbm, wup), (down_hbm, wdown))
        ):
            weight_copies[layer, number] = pltpu.make_async_copy(
                source.at[layer], target.at[layer], w_sem.at[layer, number]
            )
            weight_copies[layer, number].start()

    barrier = pltpu.get_barrier_semaphore()
    for step in range(1, 4):
        pl.semaphore_signal(
            barrier, inc=1, device_id=place(core, side, lax.rem(zz + step, 4), yy), device_id_type=MESH
        )
    for step in range(4):
        pl.semaphore_signal(
            barrier, inc=1, device_id=place(1 - core, side, lax.rem(zz + step, 4), yy), device_id_type=MESH
        )
    pl.semaphore_signal(barrier, inc=1, device_id=x_peer, device_id_type=MESH)
    pl.semaphore_signal(barrier, inc=1, device_id=y_peer, device_id_type=MESH)
    pl.semaphore_signal(
        barrier, inc=1, device_id=place(1 - core, side, zz, 1 - yy), device_id_type=MESH
    )

    end_second = lax.div(seq_len[0, 0] + seq_len[0, 1], RUNS)
    flag_out[...] = jnp.full((8, 128), end_second.astype(F32), F32)
    for layer in range(LAYERS):
        for head in range(OWN):
            rq[layer, head, DIM:, :] = jnp.zeros((DIM, HALF * RUNS), BF16)
    for head in range(OWN):
        ro[head, 0:DIM, :] = jnp.zeros((DIM, HALF * RUNS), BF16)

    def moved(kind, slot, source, target, at, core_at, z_at):
        here = jnp.logical_and(core_at == core, z_at == zz)

        @pl.when(here)
        def _():
            pltpu.make_async_copy(source, target.at[at], move_recv.at[kind, at]).start()

        @pl.when(jnp.logical_not(here))
        def _():
            pltpu.make_async_remote_copy(
                src_ref=source,
                dst_ref=target.at[at],
                send_sem=move_send.at[kind, slot],
                recv_sem=move_recv.at[kind, at],
                device_id=place(core_at, side, z_at, yy),
                device_id_type=MESH,
            ).start()

    def move_left(kind, slot, source, core_at, z_at):
        here = jnp.logical_and(core_at == core, z_at == zz)

        @pl.when(jnp.logical_not(here))
        def _():
            pltpu.make_async_copy(source, source, move_send.at[kind, slot]).wait()

    def move_arrived(kind, at, target):
        pltpu.make_async_copy(target.at[at], target.at[at], move_recv.at[kind, at]).wait()

    def to_team(kind, half, source, target):
        moved(kind, half, source, target, lax.div(zz, 2), lax.rem(zz, 2), 2 * half + core)

    def to_team_left(kind, half, source):
        move_left(kind, half, source, lax.rem(zz, 2), 2 * half + core)

    def to_owner(kind, chunk, source, target):
        moved(kind, chunk, source, target, lax.div(zz, 2), lax.rem(zz, 2), core + 2 * chunk)

    def to_owner_left(kind, chunk, source):
        move_left(kind, chunk, source, lax.rem(zz, 2), core + 2 * chunk)

    def half_of(ref, half):
        return ref.at[pl.ds(HALF * half, HALF)]

    def rows_of(half):
        return pl.ds(pl.multiple_of(half * HALF, HALF), HALF)

    def slot_of(other):
        return lax.rem(other + TEAM - member, TEAM)

    def exchange(kind, layer, half, outgoing, incoming):
        incoming[layer, half, 0] = outgoing[half, member]
        for step in range(1, TEAM):
            peer = lax.rem(member + step, TEAM)
            pltpu.make_async_remote_copy(
                src_ref=outgoing.at[half, peer],
                dst_ref=incoming.at[layer, half, TEAM - step],
                send_sem=a2a_send.at[kind, layer, half],
                recv_sem=a2a_recv.at[kind, layer, half],
                device_id=place(lax.div(peer, 2), side, zz, lax.rem(peer, 2)),
                device_id_type=MESH,
            ).start()

    def arrived(kind, layer, half, incoming):
        whole = incoming.at[layer, half, pl.ds(1, TEAM - 1)]
        pltpu.make_async_copy(whole, whole, a2a_recv.at[kind, layer, half]).wait()

    def left(kind, layer, half, outgoing):
        whole = outgoing.at[half, pl.ds(1, TEAM - 1)]
        pltpu.make_async_copy(whole, whole, a2a_send.at[kind, layer, half]).wait()

    def project(layer, half):
        rows = rows_of(half)
        rounded = hidden[half].astype(BF16)
        hid_t[layer, :, rows] = rounded.T
        if layer == 1:
            left(0, 0, half, pack_out)
        queries = nn(rounded, wqkv[layer, :, 0:WIDTH]) * (DIM ** -0.5)
        queries_t = queries.T.astype(BF16)
        keys = nn(rounded, wqkv[layer, :, WIDTH : 2 * WIDTH])
        values = nn(rounded, wqkv[layer, :, 2 * WIDTH : 3 * WIDTH])
        for pair in range(RUNS // 2):
            k_pair = keys[:, 128 * pair : 128 * pair + 128]
            v_pair = values[:, 128 * pair : 128 * pair + 128]
            first = jnp.where(low, k_pair, pltpu.roll(v_pair, DIM, 1))
            other = jnp.where(low, pltpu.roll(k_pair, DIM, 1), v_pair)
            pack_out[half, pair, 0, 0:HALF, :] = first.astype(BF16)
            pack_out[half, pair, 1, 0:HALF, :] = other.astype(BF16)
        for head in range(RUNS):
            pack_out[half, head // 2, head % 2, HALF:, :] = queries_t[DIM * head : DIM * head + DIM, :]
        exchange(0, layer, half, pack_out, qkv_in)

    def attend(layer, chunk):
        arrived(0, layer, chunk, qkv_in)
        if layer == 1:
            left(1, 0, chunk, head_out)

        def one_head(head, carry):
            for other in range(TEAM):
                slot = slot_of(other)
                start = HALF * (TEAM * chunk + other)
                span = slice(start, start + HALF)
                block = qkv_in[layer, chunk, slot, head, 0:HALF, :]
                kv[layer, head, span, :] = block
                kv_t[layer, head, :, span] = block.T
                rq[layer, head, 0:DIM, span] = qkv_in[layer, chunk, slot, head, HALF:, :]
            for i in (2 * chunk, 2 * chunk + 1):
                columns = slice(TILE * i, TILE * i + TILE)
                query_tile = rq[layer, head, :, columns]
                scores = []
                for j in range(i + 1):
                    tile = nn(kv[layer, head, TILE * j : TILE * j + TILE, :], query_tile)
                    scores.append(tile + bias[1 if j == i else 0])
                largest = functools.reduce(
                    jnp.maximum, [jnp.max(tile, axis=0, keepdims=True) for tile in scores]
                )
                total = jnp.zeros((1, TILE), F32)
                summed = jnp.zeros((DIM, TILE), F32)
                for j in range(i + 1):
                    weight = jnp.exp(scores[j] - largest)
                    total = total + jnp.sum(weight, axis=0, keepdims=True)
                    summed = summed + nn(
                        kv_t[layer, head, DIM:, TILE * j : TILE * j + TILE], weight.astype(BF16)
                    )
                summed = summed / total
                o_t[layer, head, :, columns] = summed
                lse[layer, head, :, columns] = largest + jnp.log(total)
                rounded = summed.astype(BF16)
                for part in range(2):
                    head_out[chunk, 2 * (i - 2 * chunk) + part, head] = rounded[
                        :, HALF * part : HALF * part + HALF
                    ]
            return carry

        lax.fori_loop(0, OWN, one_head, 0)
        exchange(1, layer, chunk, head_out, o_in)

    def feed(layer, half):
        rows = rows_of(half)
        arrived(1, layer, half, o_in)
        for head in range(RUNS):
            attn_t[layer, DIM * head : DIM * head + DIM, rows] = o_in[layer, half, slot_of(head // 2), head % 2]
        attn = attn_t[layer, :, rows].T
        grown = nn(attn, wout[layer])
        branch[layer, half] = grown
        middle = hidden[half] + alphas[layer, 0] * grown
        entered = middle.astype(BF16)
        ent_t[layer, :, rows] = entered.T
        total = jnp.zeros((HALF, WIDTH), F32)
        for step in range(FF // CUT):
            cut = slice(CUT * step, CUT * step + CUT)
            gate = nn(entered, wup[layer, :, cut]) + up_bias[layer : layer + 1, cut]
            risen = 0.5 * (1.0 + lax.erf(gate * (0.5 ** 0.5)))
            slope[layer, half, :, cut] = risen + gate * jnp.exp(-0.5 * gate * gate) * 0.3989422804014327
            active = (gate * risen).astype(BF16)
            act_t[layer, cut, rows] = active.T
            total = total + nn(active, wdown[layer, cut, :])
        total = total + down_bias[layer : layer + 1, :]
        second[layer, half] = total
        hidden[half] = middle + alphas[layer, 1] * total

    def total_of(values):
        return jnp.sum(jnp.sum(values, axis=0, keepdims=True), axis=1, keepdims=True)

    def feed_back(layer, half):
        rows = rows_of(half)
        start = grad[half]
        scaled = (alphas[layer, 1] * start).astype(BF16)
        dz[rows, :] = scaled
        alpha_second = total_of(start * second[layer, half])
        small[half, layer : layer + 1, FF : FF + WIDTH] = jnp.sum(scaled.astype(F32), axis=0, keepdims=True)
        middle = start
        for step in range(FF // CUT):
            cut = slice(CUT * step, CUT * step + CUT)
            gate = (nt(scaled, wdown[layer, cut, :]) * slope[layer, half, :, cut]).astype(BF16)
            du[rows, cut] = gate
            small[half, layer : layer + 1, cut] = jnp.sum(gate.astype(F32), axis=0, keepdims=True)
            middle = middle + nt(gate, wup[layer, :, cut])
        grad[half] = middle
        alpha_first = total_of(middle * branch[layer, half])
        column = lax.broadcasted_iota(jnp.int32, (1, 128), 1)
        small[half, layer : layer + 1, FF + WIDTH :] = jnp.where(
            column == 0, alpha_first, jnp.where(column == 1, alpha_second, 0.0)
        )
        mixed = (alphas[layer, 0] * middle).astype(BF16)
        da[rows, :] = mixed
        spread = nt(wout[layer], mixed).astype(BF16)
        left(*((1, 1) if layer == 1 else (2, 1)), half, head_out)
        for head in range(RUNS):
            head_out[half, head // 2, head % 2] = spread[DIM * head : DIM * head + DIM, :]
        exchange(2, layer, half, head_out, do_in)

    def attend_back(layer, chunk):
        arrived(2, layer, chunk, do_in)
        left(*((0, 1) if layer == 1 else (3, 1)), chunk, pack_out)

        def one_head(head, carry):
            for other in range(TEAM):
                start = HALF * (TEAM * chunk + other)
                ro[head, DIM:, start : start + HALF] = do_in[layer, chunk, slot_of(other), head]
            for i in (2 * chunk, 2 * chunk + 1):
                columns = slice(TILE * i, TILE * i + TILE)
                query_tile = rq[layer, head, :, columns]
                grad_tile = ro[head, :, columns]
                log_total = lse[layer, head, :, columns]
                delta = jnp.sum(
                    ro[head, DIM:, columns].astype(F32) * o_t[layer, head, :, columns],
                    axis=0,
                    keepdims=True,
                )
                query_grad = jnp.zeros((DIM, TILE), F32)
                for j in range(i + 1):
                    span = slice(TILE * j, TILE * j + TILE)
                    keys = kv[layer, head, span, :]
                    weight = jnp.exp(nn(keys, query_tile) + bias[1 if j == i else 0] - log_total)
                    scored = (weight * (nn(keys, grad_tile) - delta)).astype(BF16)
                    term = nt(scored, query_tile) + nt(weight.astype(BF16), grad_tile)
                    if chunk == 1 and (i == 2 or j == i):
                        acc[head, span, :] = term
                    else:
                        acc[head, span, :] += term
                    query_grad = query_grad + nn(kv_t[layer, head, 0:DIM, span], scored)
                dq_t[:, columns] = query_grad * (DIM ** -0.5)
            for other in range(TEAM):
                start = HALF * (TEAM * chunk + other)
                span = slice(start, start + HALF)
                pack_out[chunk, other, head, 0:HALF, :] = acc[head, span, :].astype(BF16)
                pack_out[chunk, other, head, HALF:, :] = dq_t[:, span].astype(BF16)
            return carry

        lax.fori_loop(0, OWN, one_head, 0)
        exchange(3, layer, chunk, pack_out, dqkv_in)

    def project_back(layer, half):
        rows = rows_of(half)
        arrived(3, layer, half, dqkv_in)
        turned = jnp.concatenate(
            [dqkv_in[layer, half, slot_of(head // 2), head % 2, HALF:, :] for head in range(RUNS)], axis=0
        )
        dqkv[rows, 0:WIDTH] = turned.T
        for pair in range(RUNS // 2):
            first = dqkv_in[layer, half, slot_of(pair), 0, 0:HALF, :].astype(F32)
            other = dqkv_in[layer, half, slot_of(pair), 1, 0:HALF, :].astype(F32)
            k_pair = jnp.where(low, first, pltpu.roll(other, DIM, 1))
            v_pair = jnp.where(low, pltpu.roll(first, DIM, 1), other)
            dqkv[rows, WIDTH + 128 * pair : WIDTH + 128 * pair + 128] = k_pair.astype(BF16)
            dqkv[rows, 2 * WIDTH + 128 * pair : 2 * WIDTH + 128 * pair + 128] = v_pair.astype(BF16)
        grad[half] = grad[half] + nt(dqkv[rows, :], wqkv[layer])

    def scatter_rows(layer, result, first_row):
        for run in range(RUNS):
            for quarter in range(4):
                parts[layer, quarter, run // 2, run % 2, first_row : first_row + DIM, :] = result[
                    DIM * run : DIM * run + DIM, 128 * quarter : 128 * quarter + 128
                ].astype(BF16)

    def early_grads(layer):
        scatter_rows(layer, nn(attn_t[layer], da[...]), 192)
        for step in range(FF // CUT):
            cut = slice(CUT * step, CUT * step + CUT)
            scatter_rows(layer, nn(ent_t[layer], du[:, cut]), 256 + DIM * step)
        for run in range(RUNS):
            result = nn(act_t[layer, TILE * run : TILE * run + TILE, :], dz[...])
            for quarter in range(4):
                parts[layer, quarter, run // 2, run % 2, 512:768, :] = result[
                    :, 128 * quarter : 128 * quarter + 128
                ].astype(BF16)

    def late_grads(layer):
        for step in range(3):
            scatter_rows(layer, nn(hid_t[layer], dqkv[:, WIDTH * step : WIDTH * step + WIDTH]), DIM * step)

    def remote(source, target, send, recv, peer):
        return pltpu.make_async_remote_copy(
            src_ref=source,
            dst_ref=target,
            send_sem=send,
            recv_sem=recv,
            device_id=peer,
            device_id_type=MESH,
        )

    def credit(semaphore, peer):
        pl.semaphore_signal(semaphore, inc=1, device_id=peer, device_id_type=MESH)

    def core_copy(layer, part, across):
        rows = pl.ds(*SPAN[part])
        return remote(
            parts.at[layer, 2 * across + 1 - core, :, :, rows],
            core_in.at[across, :, :, rows],
            core_send.at[layer, part, across],
            core_recv.at[layer, part, across],
            core_peer,
        )

    def x_copy(layer, part, order):
        rows = pl.ds(*ROWS[part][order])
        which = (x_send.at[layer, part, order], x_recv.at[layer, part, order], x_peer)
        if order == 0:
            return remote(parts.at[layer, far_side, :, :, rows], x_in.at[:, :, rows], *which)
        return remote(parts.at[layer, far_side, :, yy, rows], x_in.at[:, 0, rows], *which)

    def y_copy(layer, part, order, across):
        rows = pl.ds(*ROWS[part][order])
        which = (y_send.at[layer, part, order, across], y_recv.at[layer, part, order, across], y_peer)
        quarter = grp if order == 0 else 2 * across + core
        return remote(parts.at[layer, quarter, :, 1 - yy, rows], y_in.at[across, :, rows], *which)

    def z_copy(layer, part, order, step):
        rows = pl.ds(*ROWS[part][order])
        peer = lax.rem(zz + step, 4)
        return remote(
            parts.at[layer, grp, peer, yy, rows],
            z_in.at[layer, 4 - step, rows],
            z_send.at[layer, part, order, step],
            z_recv.at[layer, part, order, 4 - step],
            place(core, side, peer, yy),
        )

    def final_copy(layer, part, which):
        rows = pl.ds(*SPAN[part])
        quarter = far_side if which == 2 else grp
        block = final.at[layer, quarter, rows]
        return remote(
            block,
            block,
            fin_send.at[layer, part, which],
            fin_recv.at[layer, part, which],
            x_peer if which == 0 else core_peer,
        )

    def core_start(layer, part):
        if layer == 0:
            pl.semaphore_wait(core_free.at[part], 1)
        for across in range(2):
            core_copy(layer, part, across).start()

    def core_done(layer, part):
        rows = pl.ds(*SPAN[part])
        for across in range(2):
            core_copy(layer, part, across).wait()
        for turn in range(2):
            across = 1 - side if turn == 0 else side
            quarter = 2 * across + core

            def add(z, carry):
                for y in range(2):
                    own = parts[layer, quarter, z, y, rows, :].astype(F32)
                    own = own + core_in[across, z, y, rows, :].astype(F32)
                    parts[layer, quarter, z, y, rows, :] = own.astype(BF16)
                return carry

            lax.fori_loop(0, 4, add, 0)
            if turn == 0:
                if layer == 0:
                    pl.semaphore_wait(x_free.at[part, 0], 1)
                x_copy(layer, part, 0).start()
        if layer == 1:
            credit(core_free.at[part], core_peer)
        else:
            pl.semaphore_wait(y_free.at[part, 1], 1)
        for across in range(2):
            y_copy(layer, part, 1, across).start()

    def first_done(layer, part):
        rows = pl.ds(*ROWS[part][1])
        for across in range(2):
            y_copy(layer, part, 1, across).wait()
        for turn in range(2):
            across = 1 - side if turn == 0 else side
            quarter = 2 * across + core

            def add(z, carry):
                own = parts[layer, quarter, z, yy, rows, :].astype(F32)
                own = own + y_in[across, z, rows, :].astype(F32)
                parts[layer, quarter, z, yy, rows, :] = own.astype(BF16)
                return carry

            lax.fori_loop(0, 4, add, 0)
            if turn == 0:
                if layer == 0:
                    pl.semaphore_wait(x_free.at[part, 1], 1)
                x_copy(layer, part, 1).start()
        if layer == 1:
            credit(y_free.at[part, 1], y_peer)

        rows = pl.ds(*ROWS[part][0])
        x_copy(layer, part, 0).wait()
        for turn in range(2):
            y = 1 - yy if turn == 0 else yy

            def add(z, carry):
                own = parts[layer, grp, z, y, rows, :].astype(F32) + x_in[z, y, rows, :].astype(F32)
                parts[layer, grp, z, y, rows, :] = own.astype(BF16)
                return carry

            lax.fori_loop(0, 4, add, 0)
            if turn == 0:
                if layer == 0:
                    pl.semaphore_wait(y_free.at[part, 0], 1)
                y_copy(layer, part, 0, 0).start()
        if layer == 1:
            credit(x_free.at[part, 0], x_peer)

    def second_done(layer, part):
        for order in (1, 0):
            rows = pl.ds(*ROWS[part][order])
            (y_copy(layer, part, 0, 0) if order == 0 else x_copy(layer, part, 1)).wait()

            def add(z, carry):
                arrival = y_in[0, z, rows, :] if order == 0 else x_in[z, 0, rows, :]
                own = parts[layer, grp, z, yy, rows, :].astype(F32) + arrival.astype(F32)
                parts[layer, grp, z, yy, rows, :] = own.astype(BF16)
                return carry

            lax.fori_loop(0, 4, add, 0)
            if layer == 1:
                if order == 0:
                    credit(y_free.at[part, 0], y_peer)
                else:
                    credit(x_free.at[part, 1], x_peer)
            for step in range(1, 4):
                z_copy(layer, part, order, step).start()

    def z_done(layer, part):
        rows = pl.ds(*SPAN[part])
        for order in (1, 0):
            for step in range(1, 4):
                z_copy(layer, part, order, step).wait()
        total = parts[layer, grp, zz, yy, rows, :].astype(F32)
        for slot in range(1, 4):
            total = total + z_in[layer, slot, rows, :].astype(F32)
        final[layer, grp, rows, :] = total.astype(BF16)
        for which in range(2):
            final_copy(layer, part, which).start()

    def final_pass(layer, part):
        final_copy(layer, part, 0).wait()
        final_copy(layer, part, 2).start()

    def final_out(layer, part):
        rows = pl.ds(*SPAN[part])
        return pltpu.make_async_copy(
            final.at[layer, :, rows], final_hbm.at[layer, :, rows], out_sem.at[layer, part]
        )

    def final_done(layer, part):
        for which in range(1, 3):
            final_copy(layer, part, which).wait()
        final_out(layer, part).start()

    def small_copy(stage):
        peer = (core_peer, x_peer, y_peer)[stage]
        return remote(
            small_sum.at[stage], small_in.at[stage], small_send.at[stage], small_recv.at[stage], peer
        )

    def small_z_copy(step):
        return remote(
            small_z.at[zz],
            small_z.at[zz],
            small_send.at[2 + step],
            small_recv.at[2 + step],
            place(core, side, lax.rem(zz + step, 4), yy),
        )

    def small_start():
        small_sum[0] = small[0] + small[1]
        small_copy(0).start()

    def small_next(stage):
        small_copy(stage).wait()
        total = small_sum[stage] + small_in[stage]
        if stage < 2:
            small_sum[stage + 1] = total
            small_copy(stage + 1).start()
        else:
            small_z[zz] = total
            for step in range(1, 4):
                small_z_copy(step).start()

    def small_done():
        for step in range(1, 4):
            small_z_copy(step).wait()
        small_sum[0] = (small_z[0] + small_z[1]) + (small_z[2] + small_z[3])
        small_final[:, 0:256] = small_sum[0, :, pl.ds(pl.multiple_of(blk * 256, 256), 256)]
        pair = small_sum[0, :, pl.ds(pl.multiple_of(FF + 128 * zz, 128), 128)]
        small_final[:, 256:384] = jnp.where(yy == 1, pltpu.roll(pair, DIM, 1), pair)
        small_final[:, 384:512] = small_sum[0, :, FF + WIDTH :]

    def halves(*phases, backward=False):
        def both(step, carry):
            for phase in phases:
                phase(1 - step if backward else step)
            return carry

        lax.fori_loop(0, 2, both, 0)

    def begin(half):
        move_arrived(0, half, tok_in)
        hidden[half] = tok_in[half].astype(F32)

    def finish(half):
        back_out[0, half] = hidden[half].astype(BF16)
        to_owner(3, half, back_out.at[0, half], out_in)

    def turn_round(half):
        move_arrived(2, half, cot_in)
        grad[half] = cot_in[half].astype(F32)

    def hand_back(half):
        back_out[1, half] = grad[half].astype(BF16)
        to_owner(4, half, back_out.at[1, half], grad_in)

    pl.semaphore_wait(barrier, 10)
    for half in range(2):
        to_team(0, half, half_of(tokens, half), tok_in)
    for half in range(2):
        to_team(1, half, flag_out, flag_in)
    for half in range(2):
        to_team(2, half, half_of(cotangent, half), cot_in)
    weight_copies[0, 0].wait()
    halves(begin, functools.partial(project, 0))

    move_arrived(1, 0, flag_in)
    move_arrived(1, 1, flag_in)
    border = jnp.concatenate([flag_in[0, 0:1, :]] * 2, axis=1) - (HALF * lax.div(zz, 2)).astype(F32)
    key_row = lax.broadcasted_iota(jnp.int32, (TILE, TILE), 0)
    query_col = lax.broadcasted_iota(jnp.int32, (TILE, TILE), 1)
    later = key_row > query_col
    key_sub = lax.rem(key_row, HALF).astype(F32) >= border
    query_sub = lax.rem(query_col, HALF).astype(F32) >= border
    apart = jnp.logical_xor(key_sub, query_sub)
    bias[0] = jnp.where(apart, NEGATIVE, 0.0)
    bias[1] = jnp.where(jnp.logical_or(later, apart), NEGATIVE, 0.0)

    for number in range(1, 4):
        weight_copies[0, number].wait()
    attend(0, 0)
    attend(0, 1)
    weight_copies[1, 0].wait()
    halves(functools.partial(feed, 0), functools.partial(project, 1))
    for number in range(1, 4):
        weight_copies[1, number].wait()
    attend(1, 0)
    attend(1, 1)
    halves(functools.partial(feed, 1), finish)

    halves(turn_round, functools.partial(feed_back, 1), backward=True)
    early_grads(1)
    core_start(1, 0)
    attend_back(1, 1)
    attend_back(1, 0)
    core_done(1, 0)
    halves(functools.partial(project_back, 1), functools.partial(feed_back, 0), backward=True)
    small_start()
    late_grads(1)
    core_start(1, 1)
    early_grads(0)
    core_start(0, 0)
    attend_back(0, 1)
    small_next(0)
    core_done(1, 1)
    attend_back(0, 0)
    small_next(1)
    first_done(1, 0)
    core_done(0, 0)
    halves(functools.partial(project_back, 0), hand_back, backward=True)
    late_grads(0)
    core_start(0, 1)
    small_next(2)
    first_done(1, 1)
    second_done(1, 0)
    core_done(0, 1)
    first_done(0, 0)
    second_done(1, 1)
    z_done(1, 0)
    first_done(0, 1)
    second_done(0, 0)
    small_done()
    z_done(1, 1)
    final_pass(1, 0)
    second_done(0, 1)
    final_pass(1, 1)
    final_done(1, 0)
    final_done(1, 1)
    results = []
    for half in range(2):
        rows = pl.ds(HALF * half, HALF)
        move_arrived(3, half, out_in)
        results.append(pltpu.make_async_copy(out_in.at[half], output_hbm.at[rows], out_sem.at[2, half]))
        move_arrived(4, half, grad_in)
        results.append(pltpu.make_async_copy(grad_in.at[half], input_grad_hbm.at[rows], out_sem.at[3, half]))
    for copy in results:
        copy.start()
    z_done(0, 0)
    z_done(0, 1)
    final_pass(0, 0)
    final_pass(0, 1)
    final_done(0, 0)
    final_done(0, 1)

    for half in range(2):
        left(2, 0, half, head_out)
        left(3, 0, half, pack_out)
        to_team_left(0, half, half_of(tokens, half))
        to_team_left(1, half, flag_out)
        to_team_left(2, half, half_of(cotangent, half))
        to_owner_left(3, half, back_out.at[0, half])
        to_owner_left(4, half, back_out.at[1, half])
    for copy in results:
        copy.wait()
    for layer in range(LAYERS):
        for part in range(2):
            final_out(layer, part).wait()


def results_kernel(
    final, out_block, grad_block, small,
    output, input_grad, qkv_grad, out_grad, up_grad, up_bias_grad, down_grad, down_bias_grad, alpha_grad,
):
    output[...] = out_block[...]
    input_grad[...] = grad_block[...].astype(F32)
    up_bias_grad[...] = small[:, 0:256]
    down_bias_grad[...] = small[:, 256 : 256 + DIM]
    alpha_grad[...] = small[:, 384:386]
    for layer in range(LAYERS):
        for quarter in range(4):

            def block(first, count):
                return final[layer, quarter, first : first + count, :].astype(F32)

            def columns(step):
                return slice(WIDTH * step + 128 * quarter, WIDTH * step + 128 * quarter + 128)

            for step in range(3):
                qkv_grad[layer, :, columns(step)] = block(DIM * step, DIM)
            out_grad[layer, :, columns(0)] = block(192, DIM)
            for step in range(4):
                up_grad[layer, :, columns(step)] = block(256 + DIM * step, DIM)
            down_grad[layer, :, columns(0)] = block(512, 256)


def fast_body(
    tokens, seq_len, qkv_weight, out_weight, up_weight, up_bias, down_weight, down_bias, alphas, cotangent
):
    whole = pl.BlockSpec(memory_space=pltpu.VMEM)
    scalar = pl.BlockSpec(memory_space=pltpu.SMEM)
    far = pl.BlockSpec(memory_space=pl.ANY)
    shape = jax.ShapeDtypeStruct
    rows = HALF * RUNS

    def vmem(*dims):
        return pltpu.VMEM(dims, BF16)

    def wide(*dims):
        return pltpu.VMEM(dims, F32)

    dma = pltpu.SemaphoreType.DMA
    final, out_block, grad_block, small = pl.pallas_call(
        layers_kernel,
        out_shape=(
            shape((LAYERS, 4, CHUNK, 128), BF16),
            shape((2 * HALF, WIDTH), BF16),
            shape((2 * HALF, WIDTH), BF16),
            shape((LAYERS, WIDTH), F32),
        ),
        in_specs=[whole, scalar, scalar, whole, whole, whole, far, far, far, far],
        out_specs=(far, far, far, whole),
        scratch_shapes=[
            vmem(LAYERS, WIDTH, 3 * WIDTH),
            vmem(LAYERS, WIDTH, WIDTH),
            vmem(LAYERS, WIDTH, FF),
            vmem(LAYERS, FF, WIDTH),
            vmem(2, HALF, WIDTH),
            vmem(2, HALF, WIDTH),
            wide(8, 128),
            wide(2, 8, 128),
            vmem(2, 2, HALF, WIDTH),
            vmem(2, HALF, WIDTH),
            vmem(2, HALF, WIDTH),
            wide(2, HALF, WIDTH),
            wide(2, HALF, WIDTH),
            vmem(LAYERS, WIDTH, 2 * HALF),
            vmem(LAYERS, WIDTH, 2 * HALF),
            vmem(LAYERS, WIDTH, 2 * HALF),
            vmem(LAYERS, FF, 2 * HALF),
            wide(LAYERS, 2, HALF, WIDTH),
            wide(LAYERS, 2, HALF, FF),
            wide(LAYERS, 2, HALF, WIDTH),
            vmem(2 * HALF, WIDTH),
            vmem(2 * HALF, FF),
            vmem(2 * HALF, WIDTH),
            vmem(2 * HALF, 3 * WIDTH),
            vmem(2, TEAM, OWN, PACK, 128),
            vmem(2, TEAM, OWN, DIM, 128),
            vmem(LAYERS, 2, TEAM, OWN, PACK, 128),
            vmem(LAYERS, 2, TEAM, OWN, DIM, 128),
            vmem(LAYERS, 2, TEAM, OWN, DIM, 128),
            vmem(LAYERS, 2, TEAM, OWN, PACK, 128),
            vmem(LAYERS, OWN, rows, 128),
            vmem(LAYERS, OWN, 128, rows),
            vmem(LAYERS, OWN, 128, rows),
            vmem(OWN, 128, rows),
            wide(LAYERS, OWN, DIM, rows),
            wide(LAYERS, OWN, 1, rows),
            wide(OWN, rows, 128),
            wide(DIM, rows),
            wide(2, TILE, TILE),
            vmem(LAYERS, 4, 4, 2, CHUNK, 128),
            vmem(2, 4, 2, CHUNK, 128),
            vmem(4, 2, CHUNK, 128),
            vmem(2, 4, CHUNK, 128),
            vmem(LAYERS, 4, CHUNK, 128),
            vmem(LAYERS, 4, CHUNK, 128),
            wide(2, LAYERS, SMALL),
            wide(3, LAYERS, SMALL),
            wide(4, LAYERS, SMALL),
            wide(3, LAYERS, SMALL),
            dma((LAYERS, 4)),
            dma((5, 2)),
            dma((5, 2)),
            dma((4, LAYERS, 2)),
            dma((4, LAYERS, 2)),
            dma((LAYERS, 2, 2)),
            dma((LAYERS, 2, 2)),
            dma((LAYERS, 2, 2)),
            dma((LAYERS, 2, 2)),
            dma((LAYERS, 2, 2, 2)),
            dma((LAYERS, 2, 2, 2)),
            dma((LAYERS, 2, 2, 4)),
            dma((LAYERS, 2, 2, 4)),
            dma((LAYERS, 2, 3)),
            dma((LAYERS, 2, 3)),
            dma((6,)),
            dma((6,)),
            dma((4, 2)),
            pltpu.SemaphoreType.REGULAR((2,)),
            pltpu.SemaphoreType.REGULAR((2, 2)),
            pltpu.SemaphoreType.REGULAR((2, 2)),
        ],
        compiler_params=pltpu.CompilerParams(
            collective_id=0, has_side_effects=True, vmem_limit_bytes=63 * 1024 * 1024
        ),
        name="layers",
    )(
        tokens, seq_len, alphas, up_bias, down_bias, cotangent,
        qkv_weight, out_weight, up_weight, down_weight,
    )
    return tuple(
        pl.pallas_call(
            results_kernel,
            out_shape=(
                shape((2 * HALF, WIDTH), BF16),
                shape((2 * HALF, WIDTH), F32),
                shape((LAYERS, DIM, 3 * WIDTH), F32),
                shape((LAYERS, DIM, WIDTH), F32),
                shape((LAYERS, DIM, FF), F32),
                shape((LAYERS, FF // RUNS), F32),
                shape((LAYERS, FF // RUNS, WIDTH), F32),
                shape((LAYERS, DIM), F32),
                shape((LAYERS, 2), F32),
            ),
            in_specs=[whole] * 4,
            out_specs=(whole,) * 9,
            compiler_params=pltpu.CompilerParams(vmem_limit_bytes=24 * 1024 * 1024),
            name="results",
        )(final, out_block, grad_block, small)
    )


def layout(seq_len, local_count, cycle_size):
    piece_rows = seq_len[0] // cycle_size
    end_rows = jnp.cumsum(piece_rows)
    start_rows = end_rows - piece_rows
    local_rows = jnp.arange(local_count, dtype=jnp.int32)
    segment = jnp.sum((local_rows[:, None] >= end_rows[None, :]).astype(jnp.int32), axis=1)
    picked = segment[:, None] == jnp.arange(seq_len.shape[1], dtype=jnp.int32)[None, :]
    offset = local_rows - jnp.sum(jnp.where(picked, start_rows[None, :], 0), axis=1)
    span_rows = jnp.sum(jnp.where(picked, piece_rows[None, :], 0), axis=1)
    return (segment, offset, span_rows)


def gelu_exact(values):
    return jax.nn.gelu(values, approximate=False)


def key_block(whole, geometry, block_index, head_count):
    query_seg, query_pos, seg_all, pos_all, block_rows, score_scale = geometry
    first_row = block_index * block_rows
    key_piece = lax.dynamic_slice_in_dim(whole, first_row, block_rows, 0)
    key_seg = lax.dynamic_slice_in_dim(seg_all, first_row, block_rows, 0)
    key_pos = lax.dynamic_slice_in_dim(pos_all, first_row, block_rows, 0)
    half_width = key_piece.shape[1] // 2
    keys_part = key_piece[:, :half_width].reshape(block_rows, head_count, -1)
    values_part = key_piece[:, half_width:].reshape(block_rows, head_count, -1)
    return (keys_part, values_part, key_seg, key_pos)


def block_scores(queries, keys_part, key_seg, key_pos, geometry):
    query_seg, query_pos, seg_all, pos_all, block_rows, score_scale = geometry
    scores = (
        jnp.einsum("qhd,khd->hqk", queries, keys_part, preferred_element_type=jnp.float32)
        * score_scale
    )
    allowed = (query_seg[:, None] == key_seg[None, :]) & (key_pos[None, :] <= query_pos[:, None])
    return (scores, allowed[None])


def attend(queries, whole, geometry):
    row_count, head_count, head_dim = queries.shape
    block_count = whole.shape[0] // geometry[4]

    def statistics(running, block_index):
        largest, totals = running
        keys_part, values_part, key_seg, key_pos = key_block(
            whole, geometry, block_index, head_count
        )
        scores, allowed = block_scores(queries, keys_part, key_seg, key_pos, geometry)
        newest = jnp.maximum(largest, jnp.max(jnp.where(allowed, scores, NEGATIVE), axis=2))
        weights = jnp.where(allowed, jnp.exp(scores - newest[:, :, None]), 0.0)
        totals = totals * jnp.exp(largest - newest) + jnp.sum(weights, axis=2)
        return ((newest, totals), None)

    initial = (
        jnp.full((head_count, row_count), NEGATIVE, jnp.float32),
        jnp.zeros((head_count, row_count), jnp.float32),
    )
    (largest, totals), unused = lax.scan(statistics, initial, jnp.arange(block_count))
    log_total = largest + jnp.log(totals)

    def weighted(output_sum, block_index):
        keys_part, values_part, key_seg, key_pos = key_block(
            whole, geometry, block_index, head_count
        )
        scores, allowed = block_scores(queries, keys_part, key_seg, key_pos, geometry)
        probs = jnp.where(allowed, jnp.exp(scores - log_total[:, :, None]), 0.0).astype(
            jnp.bfloat16
        )
        output_sum = output_sum + jnp.einsum(
            "hqk,khd->qhd", probs, values_part, preferred_element_type=jnp.float32
        )
        return (output_sum, None)

    output_sum, unused = lax.scan(
        weighted, jnp.zeros((row_count, head_count, head_dim), jnp.float32), jnp.arange(block_count)
    )
    return (output_sum, log_total)


def attend_back(queries, whole, log_total, delta_sum, grad_heads, geometry):
    row_count, head_count, head_dim = queries.shape
    block_rows = geometry[4]
    score_scale = geometry[5]
    block_count = whole.shape[0] // block_rows

    def gradients(query_grad, block_index):
        keys_part, values_part, key_seg, key_pos = key_block(
            whole, geometry, block_index, head_count
        )
        scores, allowed = block_scores(queries, keys_part, key_seg, key_pos, geometry)
        probs = jnp.where(allowed, jnp.exp(scores - log_total[:, :, None]), 0.0)
        grad_probs = jnp.einsum(
            "qhd,khd->hqk", grad_heads, values_part, preferred_element_type=jnp.float32
        )
        grad_scores = (probs * (grad_probs - delta_sum[:, :, None])).astype(jnp.bfloat16)
        query_grad = (
            query_grad
            + jnp.einsum("hqk,khd->qhd", grad_scores, keys_part, preferred_element_type=jnp.float32)
            * score_scale
        )
        key_grad = (
            jnp.einsum("hqk,qhd->khd", grad_scores, queries, preferred_element_type=jnp.float32)
            * score_scale
        )
        value_grad = jnp.einsum(
            "hqk,qhd->khd",
            probs.astype(jnp.bfloat16),
            grad_heads,
            preferred_element_type=jnp.float32,
        )
        joined = jnp.concatenate(
            [key_grad.reshape(block_rows, -1), value_grad.reshape(block_rows, -1)], axis=1
        )
        return (query_grad, joined)

    query_grad, stacked = lax.scan(
        gradients,
        jnp.zeros((row_count, head_count, head_dim), jnp.float32),
        jnp.arange(block_count),
    )
    return (query_grad, stacked.reshape(whole.shape[0], -1))


def layer_forward(hidden, layer_index, weights, geometry):
    qkv_weight, out_weight, up_weight, up_bias, down_weight, down_bias, alphas = weights
    row_count, model_width = hidden.shape
    projection = qkv_weight[layer_index]
    rounded = hidden.astype(jnp.bfloat16)
    queries = (
        jnp.dot(rounded, projection[:, :model_width], preferred_element_type=jnp.float32)
        .astype(jnp.bfloat16)
        .reshape(row_count, HEADS, -1)
    )
    key_value = jnp.dot(
        rounded, projection[:, model_width:], preferred_element_type=jnp.float32
    ).astype(jnp.bfloat16)
    whole = lax.all_gather(key_value, "blk", axis=0, tiled=True)
    heads_out, log_total = attend(queries, whole, geometry)
    heads_rounded = heads_out.reshape(row_count, model_width).astype(jnp.bfloat16)
    branch = jnp.dot(heads_rounded, out_weight[layer_index], preferred_element_type=jnp.float32)
    alpha_pair = alphas[layer_index]
    middle = hidden + alpha_pair[0] * branch
    entered = middle.astype(jnp.bfloat16)
    gate_pre = (
        jnp.dot(entered, up_weight[layer_index], preferred_element_type=jnp.float32)
        + up_bias[layer_index]
    )
    activated = gelu_exact(gate_pre).astype(jnp.bfloat16)
    second = (
        jnp.dot(activated, down_weight[layer_index], preferred_element_type=jnp.float32)
        + down_bias[layer_index]
    )
    result = middle + alpha_pair[1] * second
    saved = (
        rounded,
        queries,
        key_value,
        whole,
        heads_out,
        heads_rounded,
        log_total,
        branch,
        entered,
        gate_pre,
        activated,
        second,
    )
    return (result, saved)


def layer_backward(grad_hidden, saved, layer_index, weights, geometry):
    qkv_weight, out_weight, up_weight, up_bias, down_weight, down_bias, alphas = weights
    (
        rounded,
        queries,
        key_value,
        saved_whole,
        heads_out,
        heads_rounded,
        log_total,
        branch,
        entered,
        gate_pre,
        activated,
        second,
    ) = saved
    row_count = grad_hidden.shape[0]
    alpha_pair = alphas[layer_index]
    grad_second = (alpha_pair[1] * grad_hidden).astype(jnp.bfloat16)
    alpha_second = jnp.sum(grad_hidden * second)
    bias_down = jnp.sum(grad_second.astype(jnp.float32), axis=0)
    grad_down = jnp.einsum("tf,td->fd", activated, grad_second, preferred_element_type=jnp.float32)
    grad_act = jnp.einsum(
        "td,fd->tf", grad_second, down_weight[layer_index], preferred_element_type=jnp.float32
    )
    unused, gelu_pull = jax.vjp(gelu_exact, gate_pre)
    grad_gate = gelu_pull(grad_act)[0].astype(jnp.bfloat16)
    bias_up = jnp.sum(grad_gate.astype(jnp.float32), axis=0)
    grad_up = jnp.einsum("td,tf->df", entered, grad_gate, preferred_element_type=jnp.float32)
    grad_middle = grad_hidden + jnp.einsum(
        "tf,df->td", grad_gate, up_weight[layer_index], preferred_element_type=jnp.float32
    )
    grad_branch = (alpha_pair[0] * grad_middle).astype(jnp.bfloat16)
    alpha_first = jnp.sum(grad_middle * branch)
    grad_proj_out = jnp.einsum(
        "te,td->ed", heads_rounded, grad_branch, preferred_element_type=jnp.float32
    )
    grad_heads = (
        jnp.einsum(
            "td,ed->te", grad_branch, out_weight[layer_index], preferred_element_type=jnp.float32
        )
        .astype(jnp.bfloat16)
        .reshape(queries.shape)
    )
    delta_sum = jnp.sum(grad_heads.astype(jnp.float32) * heads_out, axis=2).T
    whole = lax.all_gather(key_value, "blk", axis=0, tiled=True)
    query_grad, key_terms = attend_back(queries, whole, log_total, delta_sum, grad_heads, geometry)
    key_grads = lax.psum_scatter(
        key_terms.astype(jnp.bfloat16), "blk", scatter_dimension=0, tiled=True
    )
    grad_proj = jnp.concatenate(
        [query_grad.reshape(row_count, -1).astype(jnp.bfloat16), key_grads], axis=1
    )
    grad_qkv = jnp.einsum("td,te->de", rounded, grad_proj, preferred_element_type=jnp.float32)
    grad_input = grad_middle + jnp.einsum(
        "te,de->td", grad_proj, qkv_weight[layer_index], preferred_element_type=jnp.float32
    )
    layer_grads = (
        grad_qkv,
        grad_proj_out,
        grad_up,
        bias_up,
        grad_down,
        bias_down,
        jnp.stack([alpha_first, alpha_second]),
    )
    return (grad_input, layer_grads)


def reduce_all(layer_results, cycle_size):
    stacked = [
        jnp.stack([layer_entry[member] for layer_entry in layer_results], axis=0)
        for member in range(6)
    ]
    alpha_tiles = jnp.stack(
        [jnp.tile(layer_entry[6], cycle_size) for layer_entry in layer_results], axis=0
    )
    shares = (
        lax.psum_scatter(
            stacked[0].astype(jnp.bfloat16), "blk", scatter_dimension=1, tiled=True
        ).astype(jnp.float32),
        lax.psum_scatter(
            stacked[1].astype(jnp.bfloat16), "blk", scatter_dimension=1, tiled=True
        ).astype(jnp.float32),
        lax.psum_scatter(
            stacked[2].astype(jnp.bfloat16), "blk", scatter_dimension=1, tiled=True
        ).astype(jnp.float32),
        lax.psum_scatter(
            stacked[3].astype(jnp.bfloat16), "blk", scatter_dimension=1, tiled=True
        ).astype(jnp.float32),
        lax.psum_scatter(
            stacked[4].astype(jnp.bfloat16), "blk", scatter_dimension=1, tiled=True
        ).astype(jnp.float32),
        lax.psum_scatter(
            stacked[5].astype(jnp.bfloat16), "blk", scatter_dimension=1, tiled=True
        ).astype(jnp.float32),
        lax.psum_scatter(
            alpha_tiles.astype(jnp.bfloat16), "blk", scatter_dimension=1, tiled=True
        ).astype(jnp.float32),
    )
    return (
        lax.psum(shares[0].astype(jnp.bfloat16), "grp").astype(jnp.float32),
        lax.psum(shares[1].astype(jnp.bfloat16), "grp").astype(jnp.float32),
        lax.psum(shares[2].astype(jnp.bfloat16), "grp").astype(jnp.float32),
        lax.psum(shares[3].astype(jnp.bfloat16), "grp").astype(jnp.float32),
        lax.psum(shares[4].astype(jnp.bfloat16), "grp").astype(jnp.float32),
        lax.psum(shares[5].astype(jnp.bfloat16), "grp").astype(jnp.float32),
        lax.psum(shares[6].astype(jnp.bfloat16), "grp").astype(jnp.float32),
    )


def body(
    tokens,
    seq_len,
    qkv_weight,
    out_weight,
    up_weight,
    up_bias,
    down_weight,
    down_bias,
    alphas,
    cotangent,
):
    row_count, model_width = tokens.shape
    cycle_size = lax.axis_size("blk")
    cycle_place = lax.axis_index("blk")
    head_dim = model_width // HEADS
    total_rows = cycle_size * row_count
    block_rows = min(max(row_count, 512), total_rows)
    segment, offset, span_rows = layout(seq_len, row_count, cycle_size)
    query_pos = cycle_place * span_rows + offset
    seg_all = jnp.tile(segment, cycle_size)
    pos_all = jnp.repeat(jnp.arange(cycle_size, dtype=jnp.int32), row_count) * jnp.tile(
        span_rows, cycle_size
    ) + jnp.tile(offset, cycle_size)
    geometry = (segment, query_pos, seg_all, pos_all, block_rows, head_dim ** (-0.5))
    weights = (qkv_weight, out_weight, up_weight, up_bias, down_weight, down_bias, alphas)
    hidden = tokens.astype(jnp.float32)
    saved_layers = []
    for layer_index in range(LAYERS):
        hidden, saved = layer_forward(hidden, layer_index, weights, geometry)
        saved_layers.append(saved)
    output = hidden.astype(jnp.bfloat16)
    grad_hidden = cotangent.astype(jnp.float32)
    layer_results = []
    for layer_index in reversed(range(LAYERS)):
        grad_hidden, layer_grads = layer_backward(
            grad_hidden, saved_layers[layer_index], layer_index, weights, geometry
        )
        layer_results.insert(0, layer_grads)
    finals = reduce_all(layer_results, cycle_size)
    return (
        output,
        grad_hidden,
        finals[0],
        finals[1],
        finals[2],
        finals[3],
        finals[4],
        finals[5],
        finals[6],
    )


def solution(mesh):
    placed = (
        P(("grp", "blk"), None),
        P("grp", None),
        P(),
        P(),
        P(),
        P(),
        P(),
        P(),
        P(),
        P(("grp", "blk"), None),
    )
    sizes = (mesh.shape["grp"], mesh.shape["blk"])
    return jax.shard_map(
        fast_body if sizes == (4, RUNS) else body,
        mesh=mesh,
        in_specs=placed,
        out_specs=(
            P(("grp", "blk"), None),
            P(("grp", "blk"), None),
            P(None, "blk", None),
            P(None, "blk", None),
            P(None, "blk", None),
            P(None, "blk"),
            P(None, "blk", None),
            P(None, "blk"),
            P(),
        ),
        check_vma=False,
    )
```

```python
import functools

import jax
import jax.numpy as jnp
from jax import lax
from jax.experimental import pallas as pl
from jax.experimental.pallas import tpu as pltpu
from jax.sharding import PartitionSpec as P

HEADS = 8
LAYERS = 2
NEGATIVE = -1e30
MESH = pl.DeviceIdType.MESH
F32 = jnp.float32
BF16 = jnp.bfloat16

HALF = 128
RUNS = 8
TEAM = 4
OWN = RUNS // TEAM
DIM = 64
WIDTH = 512
FF = 2048
CUT = 512
TILE = 256
PACK = HALF + DIM
CHUNK = 768
SMALL = FF + WIDTH + 128
UP, DOWN, LATE = 256, 512, 0
PART = 256
ORDERS = ((0, 128), (128, 128))

SLOPE_AT = 0.28
TAIL = (
    0.11652077851573843,
    0.06749675579450809,
    0.2689101589486142,
    -0.23699347299932225,
    0.3898740127620002,
    -0.10580824228351815,
)


def nn(a, b):
    return lax.dot_general(a, b, (((1,), (0,)), ((), ())), preferred_element_type=F32)


def nt(a, b):
    return lax.dot_general(a, b, (((1,), (1,)), ((), ())), preferred_element_type=F32)


def layers_kernel(
    tokens, seq_len, alphas, up_bias, down_bias, cotangent, qkv_hbm, out_hbm, up_hbm, down_hbm,
    final_hbm, output_hbm, input_grad_hbm, small_final,
    wqkv, wout, wup, wdown,
    tok_in, cot_in, flag_out, flag_in, back_out, out_in, grad_in,
    hidden, grad, hid_t, attn_t, ent_t, act_t, branch, slope, second,
    dz, du, da, dqkv,
    pack_out, head_out, qkv_in, o_in, do_in, dqkv_in,
    kv, kv_t, rq, ro, o_t, lse, acc, dq_t, bias,
    parts, core_in, x_in, y_in, z_in, final, small, small_in, small_z, small_sum,
    w_sem, move_send, move_recv, a2a_send, a2a_recv, core_send, core_recv, x_send, x_recv, y_send, y_recv,
    z_send, z_recv, fin_send, fin_recv, small_send, small_recv, out_sem, core_free, x_free, y_free,
):
    grp = lax.axis_index("grp")
    blk = lax.axis_index("blk")
    core = lax.rem(grp, 2)
    side = lax.div(grp, 2)
    yy = lax.rem(blk, 2)
    zz = lax.div(blk, 2)
    member = 2 * core + yy
    far_side = 2 * (1 - side) + core
    low = lax.broadcasted_iota(jnp.int32, (HALF, 128), 1) < DIM

    def place(c, x, z, y):
        return (2 * x + c, 2 * z + y)

    core_peer = place(1 - core, side, zz, yy)
    x_peer = place(core, 1 - side, zz, yy)
    y_peer = place(core, side, zz, 1 - yy)

    weight_copies = {}
    for layer in range(LAYERS):
        for number, (source, target) in enumerate(
            ((qkv_hbm, wqkv), (out_hbm, wout), (up_hbm, wup), (down_hbm, wdown))
        ):
            weight_copies[layer, number] = pltpu.make_async_copy(
                source.at[layer], target.at[layer], w_sem.at[layer, number]
            )
            weight_copies[layer, number].start()

    barrier = pltpu.get_barrier_semaphore()
    for step in range(1, 4):
        pl.semaphore_signal(
            barrier, inc=1, device_id=place(core, side, lax.rem(zz + step, 4), yy), device_id_type=MESH
        )
    for step in range(4):
        pl.semaphore_signal(
            barrier, inc=1, device_id=place(1 - core, side, lax.rem(zz + step, 4), yy), device_id_type=MESH
        )
    pl.semaphore_signal(barrier, inc=1, device_id=x_peer, device_id_type=MESH)
    pl.semaphore_signal(barrier, inc=1, device_id=y_peer, device_id_type=MESH)
    pl.semaphore_signal(
        barrier, inc=1, device_id=place(1 - core, side, zz, 1 - yy), device_id_type=MESH
    )

    end_second = lax.div(seq_len[0, 0] + seq_len[0, 1], RUNS)
    flag_out[...] = jnp.full((8, 128), end_second.astype(F32), F32)
    for layer in range(LAYERS):
        for head in range(OWN):
            rq[layer, head, DIM:, :] = jnp.zeros((DIM, HALF * RUNS), BF16)
    for head in range(OWN):
        ro[head, 0:DIM, :] = jnp.zeros((DIM, HALF * RUNS), BF16)

    def moved(kind, slot, source, target, at, core_at, z_at):
        here = jnp.logical_and(core_at == core, z_at == zz)

        @pl.when(here)
        def _():
            pltpu.make_async_copy(source, target.at[at], move_recv.at[kind, at]).start()

        @pl.when(jnp.logical_not(here))
        def _():
            pltpu.make_async_remote_copy(
                src_ref=source,
                dst_ref=target.at[at],
                send_sem=move_send.at[kind, slot],
                recv_sem=move_recv.at[kind, at],
                device_id=place(core_at, side, z_at, yy),
                device_id_type=MESH,
            ).start()

    def move_left(kind, slot, source, core_at, z_at):
        here = jnp.logical_and(core_at == core, z_at == zz)

        @pl.when(jnp.logical_not(here))
        def _():
            pltpu.make_async_copy(source, source, move_send.at[kind, slot]).wait()

    def move_arrived(kind, at, target):
        pltpu.make_async_copy(target.at[at], target.at[at], move_recv.at[kind, at]).wait()

    def to_team(kind, half, source, target):
        moved(kind, half, source, target, lax.div(zz, 2), lax.rem(zz, 2), 2 * half + core)

    def to_team_left(kind, half, source):
        move_left(kind, half, source, lax.rem(zz, 2), 2 * half + core)

    def to_owner(kind, chunk, source, target):
        moved(kind, chunk, source, target, lax.div(zz, 2), lax.rem(zz, 2), core + 2 * chunk)

    def to_owner_left(kind, chunk, source):
        move_left(kind, chunk, source, lax.rem(zz, 2), core + 2 * chunk)

    def half_of(ref, half):
        return ref.at[pl.ds(HALF * half, HALF)]

    def rows_of(half):
        return pl.ds(pl.multiple_of(half * HALF, HALF), HALF)

    def slot_of(other):
        return lax.rem(other + TEAM - member, TEAM)

    def exchange(kind, layer, half, outgoing, incoming):
        incoming[layer, half, 0] = outgoing[half, member]
        for step in range(1, TEAM):
            peer = lax.rem(member + step, TEAM)
            pltpu.make_async_remote_copy(
                src_ref=outgoing.at[half, peer],
                dst_ref=incoming.at[layer, half, TEAM - step],
                send_sem=a2a_send.at[kind, layer, half],
                recv_sem=a2a_recv.at[kind, layer, half],
                device_id=place(lax.div(peer, 2), side, zz, lax.rem(peer, 2)),
                device_id_type=MESH,
            ).start()

    def arrived(kind, layer, half, incoming):
        whole = incoming.at[layer, half, pl.ds(1, TEAM - 1)]
        pltpu.make_async_copy(whole, whole, a2a_recv.at[kind, layer, half]).wait()

    def left(kind, layer, half, outgoing):
        whole = outgoing.at[half, pl.ds(1, TEAM - 1)]
        pltpu.make_async_copy(whole, whole, a2a_send.at[kind, layer, half]).wait()

    def project(layer, half):
        rows = rows_of(half)
        rounded = hidden[half].astype(BF16)
        hid_t[layer, :, rows] = rounded.T
        if layer == 1:
            left(0, 0, half, pack_out)
        queries = nn(rounded, wqkv[layer, :, 0:WIDTH]) * (DIM ** -0.5)
        queries_t = queries.T.astype(BF16)
        keys = nn(rounded, wqkv[layer, :, WIDTH : 2 * WIDTH])
        values = nn(rounded, wqkv[layer, :, 2 * WIDTH : 3 * WIDTH])
        for pair in range(RUNS // 2):
            k_pair = keys[:, 128 * pair : 128 * pair + 128]
            v_pair = values[:, 128 * pair : 128 * pair + 128]
            first = jnp.where(low, k_pair, pltpu.roll(v_pair, DIM, 1))
            other = jnp.where(low, pltpu.roll(k_pair, DIM, 1), v_pair)
            pack_out[half, pair, 0, 0:HALF, :] = first.astype(BF16)
            pack_out[half, pair, 1, 0:HALF, :] = other.astype(BF16)
        for head in range(RUNS):
            pack_out[half, head // 2, head % 2, HALF:, :] = queries_t[DIM * head : DIM * head + DIM, :]
        exchange(0, layer, half, pack_out, qkv_in)

    def attend(layer, chunk):
        arrived(0, layer, chunk, qkv_in)
        if layer == 1:
            left(1, 0, chunk, head_out)

        def one_head(head, carry):
            for other in range(TEAM):
                slot = slot_of(other)
                start = HALF * (TEAM * chunk + other)
                span = slice(start, start + HALF)
                block = qkv_in[layer, chunk, slot, head, 0:HALF, :]
                kv[layer, head, span, :] = block
                kv_t[layer, head, :, span] = block.T
                rq[layer, head, 0:DIM, span] = qkv_in[layer, chunk, slot, head, HALF:, :]
            for i in (2 * chunk, 2 * chunk + 1):
                columns = slice(TILE * i, TILE * i + TILE)
                query_tile = rq[layer, head, :, columns]
                scores = []
                for j in range(i + 1):
                    tile = nn(kv[layer, head, TILE * j : TILE * j + TILE, :], query_tile)
                    scores.append(tile + bias[1 if j == i else 0])
                largest = functools.reduce(
                    jnp.maximum, [jnp.max(tile, axis=0, keepdims=True) for tile in scores]
                )
                total = jnp.zeros((1, TILE), F32)
                summed = jnp.zeros((DIM, TILE), F32)
                for j in range(i + 1):
                    weight = jnp.exp(scores[j] - largest)
                    total = total + jnp.sum(weight, axis=0, keepdims=True)
                    summed = summed + nn(
                        kv_t[layer, head, DIM:, TILE * j : TILE * j + TILE], weight.astype(BF16)
                    )
                summed = summed / total
                o_t[layer, head, :, columns] = summed
                lse[layer, head, :, columns] = largest + jnp.log(total)
                rounded = summed.astype(BF16)
                for part in range(2):
                    head_out[chunk, 2 * (i - 2 * chunk) + part, head] = rounded[
                        :, HALF * part : HALF * part + HALF
                    ]
            return carry

        lax.fori_loop(0, OWN, one_head, 0)
        exchange(1, layer, chunk, head_out, o_in)

    def feed(layer, half):
        rows = rows_of(half)
        arrived(1, layer, half, o_in)
        for head in range(RUNS):
            attn_t[layer, DIM * head : DIM * head + DIM, rows] = o_in[layer, half, slot_of(head // 2), head % 2]
        attn = attn_t[layer, :, rows].T
        grown = nn(attn, wout[layer])
        branch[layer, half] = grown
        middle = hidden[half] + alphas[layer, 0] * grown
        entered = middle.astype(BF16)
        ent_t[layer, :, rows] = entered.T
        total = jnp.zeros((HALF, WIDTH), F32)
        for step in range(FF // CUT):
            cut = slice(CUT * step, CUT * step + CUT)
            gate = nn(entered, wup[layer, :, cut]) + up_bias[layer : layer + 1, cut]
            bell = jnp.exp(gate * gate * -0.5)
            near = pl.reciprocal(1.0 + SLOPE_AT * jnp.abs(gate), approx=True)
            tail = jnp.full_like(gate, TAIL[5])
            for factor in TAIL[4::-1]:
                tail = tail * near + factor
            tail = bell * (tail * near)
            risen = jnp.where(gate > 0.0, 1.0 - tail, tail)
            slope[layer, half, :, cut] = risen + gate * bell * 0.3989422804014327
            active = (gate * risen).astype(BF16)
            act_t[layer, cut, rows] = active.T
            total = total + nn(active, wdown[layer, cut, :])
        total = total + down_bias[layer : layer + 1, :]
        second[layer, half] = total
        hidden[half] = middle + alphas[layer, 1] * total

    def total_of(values):
        return jnp.sum(jnp.sum(values, axis=0, keepdims=True), axis=1, keepdims=True)

    def feed_back(layer, half):
        rows = rows_of(half)
        start = grad[half]
        scaled = (alphas[layer, 1] * start).astype(BF16)
        dz[rows, :] = scaled
        alpha_second = total_of(start * second[layer, half])
        small[half, layer : layer + 1, FF : FF + WIDTH] = jnp.sum(scaled.astype(F32), axis=0, keepdims=True)
        middle = start
        for step in range(FF // CUT):
            cut = slice(CUT * step, CUT * step + CUT)
            gate = (nt(scaled, wdown[layer, cut, :]) * slope[layer, half, :, cut]).astype(BF16)
            du[rows, cut] = gate
            small[half, layer : layer + 1, cut] = jnp.sum(gate.astype(F32), axis=0, keepdims=True)
            middle = middle + nt(gate, wup[layer, :, cut])
        grad[half] = middle
        alpha_first = total_of(middle * branch[layer, half])
        column = lax.broadcasted_iota(jnp.int32, (1, 128), 1)
        small[half, layer : layer + 1, FF + WIDTH :] = jnp.where(
            column == 0, alpha_first, jnp.where(column == 1, alpha_second, 0.0)
        )
        mixed = (alphas[layer, 0] * middle).astype(BF16)
        da[layer, rows, :] = mixed
        spread = nt(wout[layer], mixed).astype(BF16)
        left(*((1, 1) if layer == 1 else (2, 1)), half, head_out)
        for head in range(RUNS):
            head_out[half, head // 2, head % 2] = spread[DIM * head : DIM * head + DIM, :]
        exchange(2, layer, half, head_out, do_in)

    def attend_back(layer, chunk):
        arrived(2, layer, chunk, do_in)
        left(*((0, 1) if layer == 1 else (3, 1)), chunk, pack_out)

        def one_head(head, carry):
            for other in range(TEAM):
                start = HALF * (TEAM * chunk + other)
                ro[head, DIM:, start : start + HALF] = do_in[layer, chunk, slot_of(other), head]
            for i in (2 * chunk, 2 * chunk + 1):
                columns = slice(TILE * i, TILE * i + TILE)
                query_tile = rq[layer, head, :, columns]
                grad_tile = ro[head, :, columns]
                log_total = lse[layer, head, :, columns]
                delta = jnp.sum(
                    ro[head, DIM:, columns].astype(F32) * o_t[layer, head, :, columns],
                    axis=0,
                    keepdims=True,
                )
                query_grad = jnp.zeros((DIM, TILE), F32)
                for j in range(i + 1):
                    span = slice(TILE * j, TILE * j + TILE)
                    keys = kv[layer, head, span, :]
                    weight = jnp.exp(nn(keys, query_tile) + bias[1 if j == i else 0] - log_total)
                    scored = (weight * (nn(keys, grad_tile) - delta)).astype(BF16)
                    term = nt(scored, query_tile) + nt(weight.astype(BF16), grad_tile)
                    if chunk == 1 and (i == 2 or j == i):
                        acc[head, span, :] = term
                    else:
                        acc[head, span, :] += term
                    query_grad = query_grad + nn(kv_t[layer, head, 0:DIM, span], scored)
                dq_t[:, columns] = query_grad * (DIM ** -0.5)
            for other in range(TEAM):
                start = HALF * (TEAM * chunk + other)
                span = slice(start, start + HALF)
                pack_out[chunk, other, head, 0:HALF, :] = acc[head, span, :].astype(BF16)
                pack_out[chunk, other, head, HALF:, :] = dq_t[:, span].astype(BF16)
            return carry

        lax.fori_loop(0, OWN, one_head, 0)
        exchange(3, layer, chunk, pack_out, dqkv_in)

    def project_back(layer, half):
        rows = rows_of(half)
        arrived(3, layer, half, dqkv_in)
        turned = jnp.concatenate(
            [dqkv_in[layer, half, slot_of(head // 2), head % 2, HALF:, :] for head in range(RUNS)], axis=0
        )
        dqkv[rows, 0:WIDTH] = turned.T
        for pair in range(RUNS // 2):
            first = dqkv_in[layer, half, slot_of(pair), 0, 0:HALF, :].astype(F32)
            other = dqkv_in[layer, half, slot_of(pair), 1, 0:HALF, :].astype(F32)
            k_pair = jnp.where(low, first, pltpu.roll(other, DIM, 1))
            v_pair = jnp.where(low, pltpu.roll(first, DIM, 1), other)
            dqkv[rows, WIDTH + 128 * pair : WIDTH + 128 * pair + 128] = k_pair.astype(BF16)
            dqkv[rows, 2 * WIDTH + 128 * pair : 2 * WIDTH + 128 * pair + 128] = v_pair.astype(BF16)
        grad[half] = grad[half] + nt(dqkv[rows, :], wqkv[layer])

    def scatter_rows(layer, result, first_row):
        for run in range(RUNS):
            for quarter in range(4):
                parts[layer, quarter, run // 2, run % 2, first_row : first_row + DIM, :] = result[
                    DIM * run : DIM * run + DIM, 128 * quarter : 128 * quarter + 128
                ].astype(BF16)

    def up_grads(layer):
        for step in range(FF // CUT):
            cut = slice(CUT * step, CUT * step + CUT)
            scatter_rows(layer, nn(ent_t[layer], du[:, cut]), UP + DIM * step)

    def down_grads(layer):
        for run in range(RUNS):
            result = nn(act_t[layer, TILE * run : TILE * run + TILE, :], dz[...])
            for quarter in range(4):
                parts[layer, quarter, run // 2, run % 2, DOWN : DOWN + PART, :] = result[
                    :, 128 * quarter : 128 * quarter + 128
                ].astype(BF16)

    def late_grads(layer):
        scatter_rows(layer, nn(attn_t[layer], da[layer]), LATE + 192)
        for step in range(3):
            scatter_rows(
                layer, nn(hid_t[layer], dqkv[:, WIDTH * step : WIDTH * step + WIDTH]), LATE + DIM * step
            )

    def remote(source, target, send, recv, peer):
        return pltpu.make_async_remote_copy(
            src_ref=source,
            dst_ref=target,
            send_sem=send,
            recv_sem=recv,
            device_id=peer,
            device_id_type=MESH,
        )

    def credit(semaphore, peer):
        pl.semaphore_signal(semaphore, inc=1, device_id=peer, device_id_type=MESH)

    def rows_in(part, order):
        return pl.ds(part + ORDERS[order][0], ORDERS[order][1])

    def core_copy(layer, part, across):
        rows = pl.ds(part, PART)
        which = (layer, part // PART, across)
        return remote(
            parts.at[layer, 2 * across + 1 - core, :, :, rows],
            core_in.at[across, :, :, rows],
            core_send.at[which],
            core_recv.at[which],
            core_peer,
        )

    def x_copy(layer, part, order):
        rows = rows_in(part, order)
        which = (layer, part // PART, order)
        ends = (x_send.at[which], x_recv.at[which], x_peer)
        if order == 0:
            return remote(parts.at[layer, far_side, :, :, rows], x_in.at[:, :, rows], *ends)
        return remote(parts.at[layer, far_side, :, yy, rows], x_in.at[:, 0, rows], *ends)

    def y_copy(layer, part, order, across):
        rows = rows_in(part, order)
        which = (layer, part // PART, order, across)
        ends = (y_send.at[which], y_recv.at[which], y_peer)
        quarter = grp if order == 0 else 2 * across + core
        return remote(parts.at[layer, quarter, :, 1 - yy, rows], y_in.at[across, :, rows], *ends)

    def z_copy(layer, part, order, step):
        rows = rows_in(part, order)
        peer = lax.rem(zz + step, 4)
        return remote(
            parts.at[layer, grp, peer, yy, rows],
            z_in.at[layer, 4 - step, rows],
            z_send.at[layer, part // PART, order, step],
            z_recv.at[layer, part // PART, order, 4 - step],
            place(core, side, peer, yy),
        )

    def final_copy(layer, part, which):
        rows = pl.ds(part, PART)
        quarter = far_side if which == 2 else grp
        block = final.at[layer, quarter, rows]
        return remote(
            block,
            block,
            fin_send.at[layer, part // PART, which],
            fin_recv.at[layer, part // PART, which],
            x_peer if which == 0 else core_peer,
        )

    def core_start(layer, part):
        if layer == 0:
            pl.semaphore_wait(core_free.at[part // PART], 1)
        for across in range(2):
            core_copy(layer, part, across).start()

    def core_done(layer, part):
        rows = pl.ds(part, PART)
        for across in range(2):
            core_copy(layer, part, across).wait()
        if layer == 0:
            pl.semaphore_wait(x_free.at[part // PART, 0], 1)
            pl.semaphore_wait(y_free.at[part // PART, 1], 1)
        for across in (1 - side, side):
            parts[layer, 2 * across + core, :, :, rows, :] += core_in[across, :, :, rows, :]
            if across is not side:
                x_copy(layer, part, 0).start()
            y_copy(layer, part, 1, across).start()
        if layer == 1:
            credit(core_free.at[part // PART], core_peer)

    def first_done(layer, part):
        rows = rows_in(part, 1)
        for across in (1 - side, side):
            y_copy(layer, part, 1, across).wait()
        if layer == 0:
            pl.semaphore_wait(x_free.at[part // PART, 1], 1)
            pl.semaphore_wait(y_free.at[part // PART, 0], 1)
        for across in (1 - side, side):
            parts[layer, 2 * across + core, :, yy, rows, :] += y_in[across, :, rows, :]
            if across is not side:
                x_copy(layer, part, 1).start()
        if layer == 1:
            credit(y_free.at[part // PART, 1], y_peer)

        rows = rows_in(part, 0)
        x_copy(layer, part, 0).wait()
        for y in (1 - yy, yy):
            parts[layer, grp, :, y, rows, :] += x_in[:, y, rows, :]
            if y is not yy:
                y_copy(layer, part, 0, 0).start()
        if layer == 1:
            credit(x_free.at[part // PART, 0], x_peer)

    def second_done(layer, part):
        for order in (1, 0):
            rows = rows_in(part, order)
            if order == 0:
                y_copy(layer, part, 0, 0).wait()
                parts[layer, grp, :, yy, rows, :] += y_in[0, :, rows, :]
            else:
                x_copy(layer, part, 1).wait()
                parts[layer, grp, :, yy, rows, :] += x_in[:, 0, rows, :]
            for step in range(1, 4):
                z_copy(layer, part, order, step).start()
            if layer == 1:
                if order == 0:
                    credit(y_free.at[part // PART, 0], y_peer)
                else:
                    credit(x_free.at[part // PART, 1], x_peer)

    def z_done(layer, part):
        rows = pl.ds(part, PART)
        for order in (1, 0):
            for step in range(1, 4):
                z_copy(layer, part, order, step).wait()
        total = parts[layer, grp, zz, yy, rows, :].astype(F32)
        for slot in range(1, 4):
            total = total + z_in[layer, slot, rows, :].astype(F32)
        final[layer, grp, rows, :] = total.astype(BF16)
        for which in range(2):
            final_copy(layer, part, which).start()

    def final_pass(layer, part):
        final_copy(layer, part, 0).wait()
        final_copy(layer, part, 2).start()

    def final_out(layer, part):
        rows = pl.ds(part, PART)
        return pltpu.make_async_copy(
            final.at[layer, :, rows], final_hbm.at[layer, :, rows], out_sem.at[layer, part // PART]
        )

    def final_done(layer, part):
        for which in range(1, 3):
            final_copy(layer, part, which).wait()
        final_out(layer, part).start()

    def small_copy(stage):
        peer = (core_peer, x_peer, y_peer)[stage]
        return remote(
            small_sum.at[stage], small_in.at[stage], small_send.at[stage], small_recv.at[stage], peer
        )

    def small_z_copy(step):
        return remote(
            small_z.at[zz],
            small_z.at[zz],
            small_send.at[2 + step],
            small_recv.at[2 + step],
            place(core, side, lax.rem(zz + step, 4), yy),
        )

    def small_start():
        small_sum[0] = small[0] + small[1]
        small_copy(0).start()

    def small_next(stage):
        small_copy(stage).wait()
        total = small_sum[stage] + small_in[stage]
        if stage < 2:
            small_sum[stage + 1] = total
            small_copy(stage + 1).start()
        else:
            small_z[zz] = total
            for step in range(1, 4):
                small_z_copy(step).start()

    def small_done():
        for step in range(1, 4):
            small_z_copy(step).wait()
        small_sum[0] = (small_z[0] + small_z[1]) + (small_z[2] + small_z[3])
        small_final[:, 0:256] = small_sum[0, :, pl.ds(pl.multiple_of(blk * 256, 256), 256)]
        pair = small_sum[0, :, pl.ds(pl.multiple_of(FF + 128 * zz, 128), 128)]
        small_final[:, 256:384] = jnp.where(yy == 1, pltpu.roll(pair, DIM, 1), pair)
        small_final[:, 384:512] = small_sum[0, :, FF + WIDTH :]

    def halves(*phases, backward=False):
        def both(step, carry):
            for phase in phases:
                phase(1 - step if backward else step)
            return carry

        lax.fori_loop(0, 2, both, 0)

    def begin(half):
        move_arrived(0, half, tok_in)
        hidden[half] = tok_in[half].astype(F32)

    def finish(half):
        back_out[0, half] = hidden[half].astype(BF16)
        to_owner(3, half, back_out.at[0, half], out_in)

    def turn_round(half):
        move_arrived(2, half, cot_in)
        grad[half] = cot_in[half].astype(F32)

    def hand_back(half):
        back_out[1, half] = grad[half].astype(BF16)
        to_owner(4, half, back_out.at[1, half], grad_in)

    pl.semaphore_wait(barrier, 10)
    for half in range(2):
        to_team(0, half, half_of(tokens, half), tok_in)
    for half in range(2):
        to_team(1, half, flag_out, flag_in)
    for half in range(2):
        to_team(2, half, half_of(cotangent, half), cot_in)
    weight_copies[0, 0].wait()
    halves(begin, functools.partial(project, 0))

    move_arrived(1, 0, flag_in)
    move_arrived(1, 1, flag_in)
    border = jnp.concatenate([flag_in[0, 0:1, :]] * 2, axis=1) - (HALF * lax.div(zz, 2)).astype(F32)
    key_row = lax.broadcasted_iota(jnp.int32, (TILE, TILE), 0)
    query_col = lax.broadcasted_iota(jnp.int32, (TILE, TILE), 1)
    later = key_row > query_col
    key_sub = lax.rem(key_row, HALF).astype(F32) >= border
    query_sub = lax.rem(query_col, HALF).astype(F32) >= border
    apart = jnp.logical_xor(key_sub, query_sub)
    bias[0] = jnp.where(apart, NEGATIVE, 0.0)
    bias[1] = jnp.where(jnp.logical_or(later, apart), NEGATIVE, 0.0)

    for number in range(1, 4):
        weight_copies[0, number].wait()
    attend(0, 0)
    attend(0, 1)
    weight_copies[1, 0].wait()
    halves(functools.partial(feed, 0), functools.partial(project, 1))
    for number in range(1, 4):
        weight_copies[1, number].wait()
    attend(1, 0)
    attend(1, 1)
    halves(functools.partial(feed, 1), finish)

    halves(turn_round, functools.partial(feed_back, 1), backward=True)
    up_grads(1)
    core_start(1, UP)
    attend_back(1, 1)
    core_done(1, UP)
    down_grads(1)
    core_start(1, DOWN)
    attend_back(1, 0)
    core_done(1, DOWN)

    def once(half):
        @pl.when(half == 1)
        def _():
            first_done(1, UP)

    halves(functools.partial(project_back, 1), functools.partial(feed_back, 0), once, backward=True)
    up_grads(0)
    core_start(0, UP)
    small_start()
    first_done(1, DOWN)
    second_done(1, UP)
    attend_back(0, 1)
    core_done(0, UP)
    late_grads(1)
    core_start(1, LATE)
    down_grads(0)
    core_start(0, DOWN)
    small_next(0)
    attend_back(0, 0)
    core_done(1, LATE)
    core_done(0, DOWN)
    small_next(1)
    second_done(1, DOWN)
    z_done(1, UP)

    def twice(half):
        @pl.when(half == 1)
        def _():
            first_done(0, UP)
            first_done(1, LATE)

    halves(functools.partial(project_back, 0), hand_back, twice, backward=True)
    late_grads(0)
    core_start(0, LATE)
    small_next(2)
    first_done(0, DOWN)
    z_done(1, DOWN)
    second_done(0, UP)
    second_done(1, LATE)
    core_done(0, LATE)
    final_pass(1, UP)
    final_pass(1, DOWN)
    small_done()
    second_done(0, DOWN)
    first_done(0, LATE)
    z_done(0, UP)
    z_done(1, LATE)
    second_done(0, LATE)
    final_done(1, UP)
    final_done(1, DOWN)
    results = []
    for half in range(2):
        rows = pl.ds(HALF * half, HALF)
        move_arrived(3, half, out_in)
        results.append(pltpu.make_async_copy(out_in.at[half], output_hbm.at[rows], out_sem.at[2, half]))
        move_arrived(4, half, grad_in)
        results.append(pltpu.make_async_copy(grad_in.at[half], input_grad_hbm.at[rows], out_sem.at[3, half]))
    for copy in results:
        copy.start()
    z_done(0, DOWN)
    final_pass(1, LATE)
    final_pass(0, UP)
    z_done(0, LATE)
    final_pass(0, DOWN)
    final_done(1, LATE)
    final_done(0, UP)
    final_pass(0, LATE)
    final_done(0, DOWN)
    final_done(0, LATE)

    for half in range(2):
        left(2, 0, half, head_out)
        left(3, 0, half, pack_out)
        to_team_left(0, half, half_of(tokens, half))
        to_team_left(1, half, flag_out)
        to_team_left(2, half, half_of(cotangent, half))
        to_owner_left(3, half, back_out.at[0, half])
        to_owner_left(4, half, back_out.at[1, half])
    for copy in results:
        copy.wait()
    for layer in range(LAYERS):
        for part in (UP, DOWN, LATE):
            final_out(layer, part).wait()


def results_kernel(
    final_hbm, out_hbm, grad_hbm, small,
    output, input_grad, qkv_grad, out_grad, up_grad, up_bias_grad, down_grad, down_bias_grad, alpha_grad,
    final, grad_block, sem,
):
    moves = [
        pltpu.make_async_copy(final_hbm.at[1], final.at[1], sem.at[0]),
        pltpu.make_async_copy(final_hbm.at[0], final.at[0], sem.at[1]),
        pltpu.make_async_copy(grad_hbm, grad_block, sem.at[2]),
        pltpu.make_async_copy(out_hbm, output, sem.at[3]),
    ]
    for move in moves:
        move.start()
    up_bias_grad[...] = small[:, 0:256]
    down_bias_grad[...] = small[:, 256 : 256 + DIM]
    alpha_grad[...] = small[:, 384:386]
    for layer in (1, 0):
        moves[1 - layer].wait()
        for quarter in range(4):

            def block(first, count):
                return final[layer, quarter, first : first + count, :].astype(F32)

            def columns(step):
                return slice(WIDTH * step + 128 * quarter, WIDTH * step + 128 * quarter + 128)

            for step in range(3):
                qkv_grad[layer, :, columns(step)] = block(DIM * step, DIM)
            out_grad[layer, :, columns(0)] = block(192, DIM)
            for step in range(4):
                up_grad[layer, :, columns(step)] = block(UP + DIM * step, DIM)
            down_grad[layer, :, columns(0)] = block(DOWN, PART)
    moves[2].wait()
    input_grad[...] = grad_block[...].astype(F32)
    moves[3].wait()


def fast_body(
    tokens, seq_len, qkv_weight, out_weight, up_weight, up_bias, down_weight, down_bias, alphas, cotangent
):
    whole = pl.BlockSpec(memory_space=pltpu.VMEM)
    scalar = pl.BlockSpec(memory_space=pltpu.SMEM)
    far = pl.BlockSpec(memory_space=pl.ANY)
    shape = jax.ShapeDtypeStruct
    rows = HALF * RUNS

    def vmem(*dims):
        return pltpu.VMEM(dims, BF16)

    def wide(*dims):
        return pltpu.VMEM(dims, F32)

    dma = pltpu.SemaphoreType.DMA
    final, out_block, grad_block, small = pl.pallas_call(
        layers_kernel,
        out_shape=(
            shape((LAYERS, 4, CHUNK, 128), BF16),
            shape((2 * HALF, WIDTH), BF16),
            shape((2 * HALF, WIDTH), BF16),
            shape((LAYERS, WIDTH), F32),
        ),
        in_specs=[whole, scalar, scalar, whole, whole, whole, far, far, far, far],
        out_specs=(far, far, far, whole),
        scratch_shapes=[
            vmem(LAYERS, WIDTH, 3 * WIDTH),
            vmem(LAYERS, WIDTH, WIDTH),
            vmem(LAYERS, WIDTH, FF),
            vmem(LAYERS, FF, WIDTH),
            vmem(2, HALF, WIDTH),
            vmem(2, HALF, WIDTH),
            wide(8, 128),
            wide(2, 8, 128),
            vmem(2, 2, HALF, WIDTH),
            vmem(2, HALF, WIDTH),
            vmem(2, HALF, WIDTH),
            wide(2, HALF, WIDTH),
            wide(2, HALF, WIDTH),
            vmem(LAYERS, WIDTH, 2 * HALF),
            vmem(LAYERS, WIDTH, 2 * HALF),
            vmem(LAYERS, WIDTH, 2 * HALF),
            vmem(LAYERS, FF, 2 * HALF),
            wide(LAYERS, 2, HALF, WIDTH),
            wide(LAYERS, 2, HALF, FF),
            wide(LAYERS, 2, HALF, WIDTH),
            vmem(2 * HALF, WIDTH),
            vmem(2 * HALF, FF),
            vmem(LAYERS, 2 * HALF, WIDTH),
            vmem(2 * HALF, 3 * WIDTH),
            vmem(2, TEAM, OWN, PACK, 128),
            vmem(2, TEAM, OWN, DIM, 128),
            vmem(LAYERS, 2, TEAM, OWN, PACK, 128),
            vmem(LAYERS, 2, TEAM, OWN, DIM, 128),
            vmem(LAYERS, 2, TEAM, OWN, DIM, 128),
            vmem(LAYERS, 2, TEAM, OWN, PACK, 128),
            vmem(LAYERS, OWN, rows, 128),
            vmem(LAYERS, OWN, 128, rows),
            vmem(LAYERS, OWN, 128, rows),
            vmem(OWN, 128, rows),
            wide(LAYERS, OWN, DIM, rows),
            wide(LAYERS, OWN, 1, rows),
            wide(OWN, rows, 128),
            wide(DIM, rows),
            wide(2, TILE, TILE),
            vmem(LAYERS, 4, 4, 2, CHUNK, 128),
            vmem(2, 4, 2, CHUNK, 128),
            vmem(4, 2, CHUNK, 128),
            vmem(2, 4, CHUNK, 128),
            vmem(LAYERS, 4, CHUNK, 128),
            vmem(LAYERS, 4, CHUNK, 128),
            wide(2, LAYERS, SMALL),
            wide(3, LAYERS, SMALL),
            wide(4, LAYERS, SMALL),
            wide(3, LAYERS, SMALL),
            dma((LAYERS, 4)),
            dma((5, 2)),
            dma((5, 2)),
            dma((4, LAYERS, 2)),
            dma((4, LAYERS, 2)),
            dma((LAYERS, 3, 2)),
            dma((LAYERS, 3, 2)),
            dma((LAYERS, 3, 2)),
            dma((LAYERS, 3, 2)),
            dma((LAYERS, 3, 2, 2)),
            dma((LAYERS, 3, 2, 2)),
            dma((LAYERS, 3, 2, 4)),
            dma((LAYERS, 3, 2, 4)),
            dma((LAYERS, 3, 3)),
            dma((LAYERS, 3, 3)),
            dma((6,)),
            dma((6,)),
            dma((4, 3)),
            pltpu.SemaphoreType.REGULAR((3,)),
            pltpu.SemaphoreType.REGULAR((3, 2)),
            pltpu.SemaphoreType.REGULAR((3, 2)),
        ],
        compiler_params=pltpu.CompilerParams(
            collective_id=0, has_side_effects=True, vmem_limit_bytes=63 * 1024 * 1024
        ),
        name="layers",
    )(
        tokens, seq_len, alphas, up_bias, down_bias, cotangent,
        qkv_weight, out_weight, up_weight, down_weight,
    )
    return tuple(
        pl.pallas_call(
            results_kernel,
            out_shape=(
                shape((2 * HALF, WIDTH), BF16),
                shape((2 * HALF, WIDTH), F32),
                shape((LAYERS, DIM, 3 * WIDTH), F32),
                shape((LAYERS, DIM, WIDTH), F32),
                shape((LAYERS, DIM, FF), F32),
                shape((LAYERS, FF // RUNS), F32),
                shape((LAYERS, FF // RUNS, WIDTH), F32),
                shape((LAYERS, DIM), F32),
                shape((LAYERS, 2), F32),
            ),
            in_specs=[far, far, far, whole],
            out_specs=(far,) + (whole,) * 8,
            scratch_shapes=[vmem(LAYERS, 4, CHUNK, 128), vmem(2 * HALF, WIDTH), dma((4,))],
            compiler_params=pltpu.CompilerParams(vmem_limit_bytes=60 * 1024 * 1024),
            name="results",
        )(final, out_block, grad_block, small)
    )


def layout(seq_len, local_count, cycle_size):
    piece_rows = seq_len[0] // cycle_size
    end_rows = jnp.cumsum(piece_rows)
    start_rows = end_rows - piece_rows
    local_rows = jnp.arange(local_count, dtype=jnp.int32)
    segment = jnp.sum((local_rows[:, None] >= end_rows[None, :]).astype(jnp.int32), axis=1)
    picked = segment[:, None] == jnp.arange(seq_len.shape[1], dtype=jnp.int32)[None, :]
    offset = local_rows - jnp.sum(jnp.where(picked, start_rows[None, :], 0), axis=1)
    span_rows = jnp.sum(jnp.where(picked, piece_rows[None, :], 0), axis=1)
    return (segment, offset, span_rows)


def gelu_exact(values):
    return jax.nn.gelu(values, approximate=False)


def key_block(whole, geometry, block_index, head_count):
    query_seg, query_pos, seg_all, pos_all, block_rows, score_scale = geometry
    first_row = block_index * block_rows
    key_piece = lax.dynamic_slice_in_dim(whole, first_row, block_rows, 0)
    key_seg = lax.dynamic_slice_in_dim(seg_all, first_row, block_rows, 0)
    key_pos = lax.dynamic_slice_in_dim(pos_all, first_row, block_rows, 0)
    half_width = key_piece.shape[1] // 2
    keys_part = key_piece[:, :half_width].reshape(block_rows, head_count, -1)
    values_part = key_piece[:, half_width:].reshape(block_rows, head_count, -1)
    return (keys_part, values_part, key_seg, key_pos)


def block_scores(queries, keys_part, key_seg, key_pos, geometry):
    query_seg, query_pos, seg_all, pos_all, block_rows, score_scale = geometry
    scores = (
        jnp.einsum("qhd,khd->hqk", queries, keys_part, preferred_element_type=jnp.float32)
        * score_scale
    )
    allowed = (query_seg[:, None] == key_seg[None, :]) & (key_pos[None, :] <= query_pos[:, None])
    return (scores, allowed[None])


def attend(queries, whole, geometry):
    row_count, head_count, head_dim = queries.shape
    block_count = whole.shape[0] // geometry[4]

    def statistics(running, block_index):
        largest, totals = running
        keys_part, values_part, key_seg, key_pos = key_block(
            whole, geometry, block_index, head_count
        )
        scores, allowed = block_scores(queries, keys_part, key_seg, key_pos, geometry)
        newest = jnp.maximum(largest, jnp.max(jnp.where(allowed, scores, NEGATIVE), axis=2))
        weights = jnp.where(allowed, jnp.exp(scores - newest[:, :, None]), 0.0)
        totals = totals * jnp.exp(largest - newest) + jnp.sum(weights, axis=2)
        return ((newest, totals), None)

    initial = (
        jnp.full((head_count, row_count), NEGATIVE, jnp.float32),
        jnp.zeros((head_count, row_count), jnp.float32),
    )
    (largest, totals), unused = lax.scan(statistics, initial, jnp.arange(block_count))
    log_total = largest + jnp.log(totals)

    def weighted(output_sum, block_index):
        keys_part, values_part, key_seg, key_pos = key_block(
            whole, geometry, block_index, head_count
        )
        scores, allowed = block_scores(queries, keys_part, key_seg, key_pos, geometry)
        probs = jnp.where(allowed, jnp.exp(scores - log_total[:, :, None]), 0.0).astype(
            jnp.bfloat16
        )
        output_sum = output_sum + jnp.einsum(
            "hqk,khd->qhd", probs, values_part, preferred_element_type=jnp.float32
        )
        return (output_sum, None)

    output_sum, unused = lax.scan(
        weighted, jnp.zeros((row_count, head_count, head_dim), jnp.float32), jnp.arange(block_count)
    )
    return (output_sum, log_total)


def attend_back(queries, whole, log_total, delta_sum, grad_heads, geometry):
    row_count, head_count, head_dim = queries.shape
    block_rows = geometry[4]
    score_scale = geometry[5]
    block_count = whole.shape[0] // block_rows

    def gradients(query_grad, block_index):
        keys_part, values_part, key_seg, key_pos = key_block(
            whole, geometry, block_index, head_count
        )
        scores, allowed = block_scores(queries, keys_part, key_seg, key_pos, geometry)
        probs = jnp.where(allowed, jnp.exp(scores - log_total[:, :, None]), 0.0)
        grad_probs = jnp.einsum(
            "qhd,khd->hqk", grad_heads, values_part, preferred_element_type=jnp.float32
        )
        grad_scores = (probs * (grad_probs - delta_sum[:, :, None])).astype(jnp.bfloat16)
        query_grad = (
            query_grad
            + jnp.einsum("hqk,khd->qhd", grad_scores, keys_part, preferred_element_type=jnp.float32)
            * score_scale
        )
        key_grad = (
            jnp.einsum("hqk,qhd->khd", grad_scores, queries, preferred_element_type=jnp.float32)
            * score_scale
        )
        value_grad = jnp.einsum(
            "hqk,qhd->khd",
            probs.astype(jnp.bfloat16),
            grad_heads,
            preferred_element_type=jnp.float32,
        )
        joined = jnp.concatenate(
            [key_grad.reshape(block_rows, -1), value_grad.reshape(block_rows, -1)], axis=1
        )
        return (query_grad, joined)

    query_grad, stacked = lax.scan(
        gradients,
        jnp.zeros((row_count, head_count, head_dim), jnp.float32),
        jnp.arange(block_count),
    )
    return (query_grad, stacked.reshape(whole.shape[0], -1))


def layer_forward(hidden, layer_index, weights, geometry):
    qkv_weight, out_weight, up_weight, up_bias, down_weight, down_bias, alphas = weights
    row_count, model_width = hidden.shape
    projection = qkv_weight[layer_index]
    rounded = hidden.astype(jnp.bfloat16)
    queries = (
        jnp.dot(rounded, projection[:, :model_width], preferred_element_type=jnp.float32)
        .astype(jnp.bfloat16)
        .reshape(row_count, HEADS, -1)
    )
    key_value = jnp.dot(
        rounded, projection[:, model_width:], preferred_element_type=jnp.float32
    ).astype(jnp.bfloat16)
    whole = lax.all_gather(key_value, "blk", axis=0, tiled=True)
    heads_out, log_total = attend(queries, whole, geometry)
    heads_rounded = heads_out.reshape(row_count, model_width).astype(jnp.bfloat16)
    branch = jnp.dot(heads_rounded, out_weight[layer_index], preferred_element_type=jnp.float32)
    alpha_pair = alphas[layer_index]
    middle = hidden + alpha_pair[0] * branch
    entered = middle.astype(jnp.bfloat16)
    gate_pre = (
        jnp.dot(entered, up_weight[layer_index], preferred_element_type=jnp.float32)
        + up_bias[layer_index]
    )
    activated = gelu_exact(gate_pre).astype(jnp.bfloat16)
    second = (
        jnp.dot(activated, down_weight[layer_index], preferred_element_type=jnp.float32)
        + down_bias[layer_index]
    )
    result = middle + alpha_pair[1] * second
    saved = (
        rounded,
        queries,
        key_value,
        whole,
        heads_out,
        heads_rounded,
        log_total,
        branch,
        entered,
        gate_pre,
        activated,
        second,
    )
    return (result, saved)


def layer_backward(grad_hidden, saved, layer_index, weights, geometry):
    qkv_weight, out_weight, up_weight, up_bias, down_weight, down_bias, alphas = weights
    (
        rounded,
        queries,
        key_value,
        saved_whole,
        heads_out,
        heads_rounded,
        log_total,
        branch,
        entered,
        gate_pre,
        activated,
        second,
    ) = saved
    row_count = grad_hidden.shape[0]
    alpha_pair = alphas[layer_index]
    grad_second = (alpha_pair[1] * grad_hidden).astype(jnp.bfloat16)
    alpha_second = jnp.sum(grad_hidden * second)
    bias_down = jnp.sum(grad_second.astype(jnp.float32), axis=0)
    grad_down = jnp.einsum("tf,td->fd", activated, grad_second, preferred_element_type=jnp.float32)
    grad_act = jnp.einsum(
        "td,fd->tf", grad_second, down_weight[layer_index], preferred_element_type=jnp.float32
    )
    unused, gelu_pull = jax.vjp(gelu_exact, gate_pre)
    grad_gate = gelu_pull(grad_act)[0].astype(jnp.bfloat16)
    bias_up = jnp.sum(grad_gate.astype(jnp.float32), axis=0)
    grad_up = jnp.einsum("td,tf->df", entered, grad_gate, preferred_element_type=jnp.float32)
    grad_middle = grad_hidden + jnp.einsum(
        "tf,df->td", grad_gate, up_weight[layer_index], preferred_element_type=jnp.float32
    )
    grad_branch = (alpha_pair[0] * grad_middle).astype(jnp.bfloat16)
    alpha_first = jnp.sum(grad_middle * branch)
    grad_proj_out = jnp.einsum(
        "te,td->ed", heads_rounded, grad_branch, preferred_element_type=jnp.float32
    )
    grad_heads = (
        jnp.einsum(
            "td,ed->te", grad_branch, out_weight[layer_index], preferred_element_type=jnp.float32
        )
        .astype(jnp.bfloat16)
        .reshape(queries.shape)
    )
    delta_sum = jnp.sum(grad_heads.astype(jnp.float32) * heads_out, axis=2).T
    whole = lax.all_gather(key_value, "blk", axis=0, tiled=True)
    query_grad, key_terms = attend_back(queries, whole, log_total, delta_sum, grad_heads, geometry)
    key_grads = lax.psum_scatter(
        key_terms.astype(jnp.bfloat16), "blk", scatter_dimension=0, tiled=True
    )
    grad_proj = jnp.concatenate(
        [query_grad.reshape(row_count, -1).astype(jnp.bfloat16), key_grads], axis=1
    )
    grad_qkv = jnp.einsum("td,te->de", rounded, grad_proj, preferred_element_type=jnp.float32)
    grad_input = grad_middle + jnp.einsum(
        "te,de->td", grad_proj, qkv_weight[layer_index], preferred_element_type=jnp.float32
    )
    layer_grads = (
        grad_qkv,
        grad_proj_out,
        grad_up,
        bias_up,
        grad_down,
        bias_down,
        jnp.stack([alpha_first, alpha_second]),
    )
    return (grad_input, layer_grads)


def reduce_all(layer_results, cycle_size):
    stacked = [
        jnp.stack([layer_entry[member] for layer_entry in layer_results], axis=0)
        for member in range(6)
    ]
    alpha_tiles = jnp.stack(
        [jnp.tile(layer_entry[6], cycle_size) for layer_entry in layer_results], axis=0
    )
    shares = (
        lax.psum_scatter(
            stacked[0].astype(jnp.bfloat16), "blk", scatter_dimension=1, tiled=True
        ).astype(jnp.float32),
        lax.psum_scatter(
            stacked[1].astype(jnp.bfloat16), "blk", scatter_dimension=1, tiled=True
        ).astype(jnp.float32),
        lax.psum_scatter(
            stacked[2].astype(jnp.bfloat16), "blk", scatter_dimension=1, tiled=True
        ).astype(jnp.float32),
        lax.psum_scatter(
            stacked[3].astype(jnp.bfloat16), "blk", scatter_dimension=1, tiled=True
        ).astype(jnp.float32),
        lax.psum_scatter(
            stacked[4].astype(jnp.bfloat16), "blk", scatter_dimension=1, tiled=True
        ).astype(jnp.float32),
        lax.psum_scatter(
            stacked[5].astype(jnp.bfloat16), "blk", scatter_dimension=1, tiled=True
        ).astype(jnp.float32),
        lax.psum_scatter(
            alpha_tiles.astype(jnp.bfloat16), "blk", scatter_dimension=1, tiled=True
        ).astype(jnp.float32),
    )
    return (
        lax.psum(shares[0].astype(jnp.bfloat16), "grp").astype(jnp.float32),
        lax.psum(shares[1].astype(jnp.bfloat16), "grp").astype(jnp.float32),
        lax.psum(shares[2].astype(jnp.bfloat16), "grp").astype(jnp.float32),
        lax.psum(shares[3].astype(jnp.bfloat16), "grp").astype(jnp.float32),
        lax.psum(shares[4].astype(jnp.bfloat16), "grp").astype(jnp.float32),
        lax.psum(shares[5].astype(jnp.bfloat16), "grp").astype(jnp.float32),
        lax.psum(shares[6].astype(jnp.bfloat16), "grp").astype(jnp.float32),
    )


def body(
    tokens,
    seq_len,
    qkv_weight,
    out_weight,
    up_weight,
    up_bias,
    down_weight,
    down_bias,
    alphas,
    cotangent,
):
    row_count, model_width = tokens.shape
    cycle_size = lax.axis_size("blk")
    cycle_place = lax.axis_index("blk")
    head_dim = model_width // HEADS
    total_rows = cycle_size * row_count
    block_rows = min(max(row_count, 512), total_rows)
    segment, offset, span_rows = layout(seq_len, row_count, cycle_size)
    query_pos = cycle_place * span_rows + offset
    seg_all = jnp.tile(segment, cycle_size)
    pos_all = jnp.repeat(jnp.arange(cycle_size, dtype=jnp.int32), row_count) * jnp.tile(
        span_rows, cycle_size
    ) + jnp.tile(offset, cycle_size)
    geometry = (segment, query_pos, seg_all, pos_all, block_rows, head_dim ** (-0.5))
    weights = (qkv_weight, out_weight, up_weight, up_bias, down_weight, down_bias, alphas)
    hidden = tokens.astype(jnp.float32)
    saved_layers = []
    for layer_index in range(LAYERS):
        hidden, saved = layer_forward(hidden, layer_index, weights, geometry)
        saved_layers.append(saved)
    output = hidden.astype(jnp.bfloat16)
    grad_hidden = cotangent.astype(jnp.float32)
    layer_results = []
    for layer_index in reversed(range(LAYERS)):
        grad_hidden, layer_grads = layer_backward(
            grad_hidden, saved_layers[layer_index], layer_index, weights, geometry
        )
        layer_results.insert(0, layer_grads)
    finals = reduce_all(layer_results, cycle_size)
    return (
        output,
        grad_hidden,
        finals[0],
        finals[1],
        finals[2],
        finals[3],
        finals[4],
        finals[5],
        finals[6],
    )


def solution(mesh):
    placed = (
        P(("grp", "blk"), None),
        P("grp", None),
        P(),
        P(),
        P(),
        P(),
        P(),
        P(),
        P(),
        P(("grp", "blk"), None),
    )
    sizes = (mesh.shape["grp"], mesh.shape["blk"])
    return jax.shard_map(
        fast_body if sizes == (4, RUNS) else body,
        mesh=mesh,
        in_specs=placed,
        out_specs=(
            P(("grp", "blk"), None),
            P(("grp", "blk"), None),
            P(None, "blk", None),
            P(None, "blk", None),
            P(None, "blk", None),
            P(None, "blk"),
            P(None, "blk", None),
            P(None, "blk"),
            P(),
        ),
        check_vma=False,
    )
```

```python
import functools

import jax
import jax.numpy as jnp
from jax import lax
from jax.experimental import pallas as pl
from jax.experimental.pallas import tpu as pltpu
from jax.sharding import PartitionSpec as P

HEADS = 8
LAYERS = 2
NEGATIVE = -1e30
MESH = pl.DeviceIdType.MESH
F32 = jnp.float32
BF16 = jnp.bfloat16

HALF = 128
RUNS = 8
TEAM = 4
OWN = RUNS // TEAM
DIM = 64
WIDTH = 512
FF = 2048
CUT = 512
TILE = 256
PACK = HALF + DIM
CHUNK = 768
SMALL = FF + WIDTH + 128
UP, DOWN, LATE = 256, 512, 0
PART = 256
ORDERS = ((0, 144), (144, 48), (192, 64))
THIRD = ORDERS[2][1]

SLOPE_AT = 0.28
TAIL = (
    0.11652077851573843,
    0.06749675579450809,
    0.2689101589486142,
    -0.23699347299932225,
    0.3898740127620002,
    -0.10580824228351815,
)


def nn(a, b):
    return lax.dot_general(a, b, (((1,), (0,)), ((), ())), preferred_element_type=F32)


def nt(a, b):
    return lax.dot_general(a, b, (((1,), (1,)), ((), ())), preferred_element_type=F32)


def layers_kernel(
    tokens, seq_len, alphas, up_bias, down_bias, cotangent, qkv_hbm, out_hbm, up_hbm, down_hbm,
    final_hbm, output_hbm, input_grad_hbm, small_final,
    wqkv, wout, wup, wdown,
    tok_in, cot_in, flag_out, flag_in, back_out, out_in, grad_in,
    hidden, grad, hid_t, attn_t, ent_t, act_t, branch, slope, second,
    dz, du, da, dqkv,
    pack_out, head_out, qkv_in, o_in, do_in, dqkv_in,
    kv, kv_t, rq, ro, o_t, lse, acc, dq_t, bias,
    parts, core_in, x_in, y_in, z_in, third_z, third_x, third_y, final, small, small_in, small_z, small_sum,
    w_sem, move_send, move_recv, a2a_send, a2a_recv, core_send, core_recv, x_send, x_recv, y_send, y_recv,
    z_send, z_recv, tz_send, tz_recv, tx_send, tx_recv, ty_send, ty_recv, fin_send, fin_recv, small_send, small_recv, out_sem, core_free, x_free, y_free,
):
    grp = lax.axis_index("grp")
    blk = lax.axis_index("blk")
    core = lax.rem(grp, 2)
    side = lax.div(grp, 2)
    yy = lax.rem(blk, 2)
    zz = lax.div(blk, 2)
    member = 2 * core + yy
    far_side = 2 * (1 - side) + core
    low = lax.broadcasted_iota(jnp.int32, (HALF, 128), 1) < DIM

    def place(c, x, z, y):
        return (2 * x + c, 2 * z + y)

    core_peer = place(1 - core, side, zz, yy)
    x_peer = place(core, 1 - side, zz, yy)
    y_peer = place(core, side, zz, 1 - yy)

    weight_copies = {}
    for layer in range(LAYERS):
        for number, (source, target) in enumerate(
            ((qkv_hbm, wqkv), (out_hbm, wout), (up_hbm, wup), (down_hbm, wdown))
        ):
            weight_copies[layer, number] = pltpu.make_async_copy(
                source.at[layer], target.at[layer], w_sem.at[layer, number]
            )
            weight_copies[layer, number].start()

    barrier = pltpu.get_barrier_semaphore()
    for step in range(1, 4):
        pl.semaphore_signal(
            barrier, inc=1, device_id=place(core, side, lax.rem(zz + step, 4), yy), device_id_type=MESH
        )
    for step in range(4):
        pl.semaphore_signal(
            barrier, inc=1, device_id=place(1 - core, side, lax.rem(zz + step, 4), yy), device_id_type=MESH
        )
    pl.semaphore_signal(barrier, inc=1, device_id=x_peer, device_id_type=MESH)
    pl.semaphore_signal(barrier, inc=1, device_id=y_peer, device_id_type=MESH)
    pl.semaphore_signal(
        barrier, inc=1, device_id=place(1 - core, side, zz, 1 - yy), device_id_type=MESH
    )

    end_second = lax.div(seq_len[0, 0] + seq_len[0, 1], RUNS)
    flag_out[...] = jnp.full((8, 128), end_second.astype(F32), F32)
    for layer in range(LAYERS):
        for head in range(OWN):
            rq[layer, head, DIM:, :] = jnp.zeros((DIM, HALF * RUNS), BF16)
    for head in range(OWN):
        ro[head, 0:DIM, :] = jnp.zeros((DIM, HALF * RUNS), BF16)

    def moved(kind, slot, source, target, at, core_at, z_at):
        here = jnp.logical_and(core_at == core, z_at == zz)

        @pl.when(here)
        def _():
            pltpu.make_async_copy(source, target.at[at], move_recv.at[kind, at]).start()

        @pl.when(jnp.logical_not(here))
        def _():
            pltpu.make_async_remote_copy(
                src_ref=source,
                dst_ref=target.at[at],
                send_sem=move_send.at[kind, slot],
                recv_sem=move_recv.at[kind, at],
                device_id=place(core_at, side, z_at, yy),
                device_id_type=MESH,
            ).start()

    def move_left(kind, slot, source, core_at, z_at):
        here = jnp.logical_and(core_at == core, z_at == zz)

        @pl.when(jnp.logical_not(here))
        def _():
            pltpu.make_async_copy(source, source, move_send.at[kind, slot]).wait()

    def move_arrived(kind, at, target):
        pltpu.make_async_copy(target.at[at], target.at[at], move_recv.at[kind, at]).wait()

    def to_team(kind, half, source, target):
        moved(kind, half, source, target, lax.div(zz, 2), lax.rem(zz, 2), 2 * half + core)

    def to_team_left(kind, half, source):
        move_left(kind, half, source, lax.rem(zz, 2), 2 * half + core)

    def to_owner(kind, chunk, source, target):
        moved(kind, chunk, source, target, lax.div(zz, 2), lax.rem(zz, 2), core + 2 * chunk)

    def to_owner_left(kind, chunk, source):
        move_left(kind, chunk, source, lax.rem(zz, 2), core + 2 * chunk)

    def half_of(ref, half):
        return ref.at[pl.ds(HALF * half, HALF)]

    def rows_of(half):
        return pl.ds(pl.multiple_of(half * HALF, HALF), HALF)

    def slot_of(other):
        return lax.rem(other + TEAM - member, TEAM)

    def exchange(kind, layer, half, outgoing, incoming):
        incoming[layer, half, 0] = outgoing[half, member]
        for step in range(1, TEAM):
            peer = lax.rem(member + step, TEAM)
            pltpu.make_async_remote_copy(
                src_ref=outgoing.at[half, peer],
                dst_ref=incoming.at[layer, half, TEAM - step],
                send_sem=a2a_send.at[kind, layer, half],
                recv_sem=a2a_recv.at[kind, layer, half],
                device_id=place(lax.div(peer, 2), side, zz, lax.rem(peer, 2)),
                device_id_type=MESH,
            ).start()

    def arrived(kind, layer, half, incoming):
        whole = incoming.at[layer, half, pl.ds(1, TEAM - 1)]
        pltpu.make_async_copy(whole, whole, a2a_recv.at[kind, layer, half]).wait()

    def left(kind, layer, half, outgoing):
        whole = outgoing.at[half, pl.ds(1, TEAM - 1)]
        pltpu.make_async_copy(whole, whole, a2a_send.at[kind, layer, half]).wait()

    def project(layer, half):
        rows = rows_of(half)
        rounded = hidden[half].astype(BF16)
        hid_t[layer, :, rows] = rounded.T
        if layer == 1:
            left(0, 0, half, pack_out)
        queries = nn(rounded, wqkv[layer, :, 0:WIDTH]) * (DIM ** -0.5)
        queries_t = queries.T.astype(BF16)
        keys = nn(rounded, wqkv[layer, :, WIDTH : 2 * WIDTH])
        values = nn(rounded, wqkv[layer, :, 2 * WIDTH : 3 * WIDTH])
        for pair in range(RUNS // 2):
            k_pair = keys[:, 128 * pair : 128 * pair + 128]
            v_pair = values[:, 128 * pair : 128 * pair + 128]
            first = jnp.where(low, k_pair, pltpu.roll(v_pair, DIM, 1))
            other = jnp.where(low, pltpu.roll(k_pair, DIM, 1), v_pair)
            pack_out[half, pair, 0, 0:HALF, :] = first.astype(BF16)
            pack_out[half, pair, 1, 0:HALF, :] = other.astype(BF16)
        for head in range(RUNS):
            pack_out[half, head // 2, head % 2, HALF:, :] = queries_t[DIM * head : DIM * head + DIM, :]
        exchange(0, layer, half, pack_out, qkv_in)

    def attend(layer, chunk):
        arrived(0, layer, chunk, qkv_in)
        if layer == 1:
            left(1, 0, chunk, head_out)

        def one_head(head, carry):
            for other in range(TEAM):
                slot = slot_of(other)
                start = HALF * (TEAM * chunk + other)
                span = slice(start, start + HALF)
                block = qkv_in[layer, chunk, slot, head, 0:HALF, :]
                kv[layer, head, span, :] = block
                kv_t[layer, head, :, span] = block.T
                rq[layer, head, 0:DIM, span] = qkv_in[layer, chunk, slot, head, HALF:, :]
            for i in (2 * chunk, 2 * chunk + 1):
                columns = slice(TILE * i, TILE * i + TILE)
                query_tile = rq[layer, head, :, columns]
                scores = []
                for j in range(i + 1):
                    tile = nn(kv[layer, head, TILE * j : TILE * j + TILE, :], query_tile)
                    scores.append(tile + bias[1 if j == i else 0])
                largest = functools.reduce(
                    jnp.maximum, [jnp.max(tile, axis=0, keepdims=True) for tile in scores]
                )
                total = jnp.zeros((1, TILE), F32)
                summed = jnp.zeros((DIM, TILE), F32)
                for j in range(i + 1):
                    weight = jnp.exp(scores[j] - largest)
                    total = total + jnp.sum(weight, axis=0, keepdims=True)
                    summed = summed + nn(
                        kv_t[layer, head, DIM:, TILE * j : TILE * j + TILE], weight.astype(BF16)
                    )
                summed = summed / total
                o_t[layer, head, :, columns] = summed
                lse[layer, head, :, columns] = largest + jnp.log(total)
                rounded = summed.astype(BF16)
                for part in range(2):
                    head_out[chunk, 2 * (i - 2 * chunk) + part, head] = rounded[
                        :, HALF * part : HALF * part + HALF
                    ]
            return carry

        lax.fori_loop(0, OWN, one_head, 0)
        exchange(1, layer, chunk, head_out, o_in)

    def feed(layer, half):
        rows = rows_of(half)
        arrived(1, layer, half, o_in)
        for head in range(RUNS):
            attn_t[layer, DIM * head : DIM * head + DIM, rows] = o_in[layer, half, slot_of(head // 2), head % 2]
        attn = attn_t[layer, :, rows].T
        grown = nn(attn, wout[layer])
        branch[layer, half] = grown
        middle = hidden[half] + alphas[layer, 0] * grown
        entered = middle.astype(BF16)
        ent_t[layer, :, rows] = entered.T
        total = jnp.zeros((HALF, WIDTH), F32)
        for step in range(FF // CUT):
            cut = slice(CUT * step, CUT * step + CUT)
            gate = nn(entered, wup[layer, :, cut]) + up_bias[layer : layer + 1, cut]
            bell = jnp.exp(gate * gate * -0.5)
            near = pl.reciprocal(1.0 + SLOPE_AT * jnp.abs(gate), approx=True)
            tail = jnp.full_like(gate, TAIL[5])
            for factor in TAIL[4::-1]:
                tail = tail * near + factor
            tail = bell * (tail * near)
            risen = jnp.where(gate > 0.0, 1.0 - tail, tail)
            slope[layer, half, :, cut] = risen + gate * bell * 0.3989422804014327
            active = (gate * risen).astype(BF16)
            act_t[layer, cut, rows] = active.T
            total = total + nn(active, wdown[layer, cut, :])
        total = total + down_bias[layer : layer + 1, :]
        second[layer, half] = total
        hidden[half] = middle + alphas[layer, 1] * total

    def total_of(values):
        return jnp.sum(jnp.sum(values, axis=0, keepdims=True), axis=1, keepdims=True)

    def feed_back(layer, half):
        rows = rows_of(half)
        start = grad[half]
        if layer == 0:
            dz[rows, :] = (alphas[layer, 1] * start).astype(BF16)
        scaled = dz[rows, :]
        alpha_second = total_of(start * second[layer, half])
        small[half, layer : layer + 1, FF : FF + WIDTH] = jnp.sum(scaled.astype(F32), axis=0, keepdims=True)
        middle = start
        for step in range(FF // CUT):
            cut = slice(CUT * step, CUT * step + CUT)
            gate = (nt(scaled, wdown[layer, cut, :]) * slope[layer, half, :, cut]).astype(BF16)
            du[rows, cut] = gate
            small[half, layer : layer + 1, cut] = jnp.sum(gate.astype(F32), axis=0, keepdims=True)
            middle = middle + nt(gate, wup[layer, :, cut])
        grad[half] = middle
        alpha_first = total_of(middle * branch[layer, half])
        column = lax.broadcasted_iota(jnp.int32, (1, 128), 1)
        small[half, layer : layer + 1, FF + WIDTH :] = jnp.where(
            column == 0, alpha_first, jnp.where(column == 1, alpha_second, 0.0)
        )
        mixed = (alphas[layer, 0] * middle).astype(BF16)
        da[layer, rows, :] = mixed
        spread = nt(wout[layer], mixed).astype(BF16)
        left(*((1, 1) if layer == 1 else (2, 1)), half, head_out)
        for head in range(RUNS):
            head_out[half, head // 2, head % 2] = spread[DIM * head : DIM * head + DIM, :]
        exchange(2, layer, half, head_out, do_in)

    def attend_back(layer, chunk):
        arrived(2, layer, chunk, do_in)
        left(*((0, 1) if layer == 1 else (3, 1)), chunk, pack_out)

        def one_head(head, carry):
            for other in range(TEAM):
                start = HALF * (TEAM * chunk + other)
                ro[head, DIM:, start : start + HALF] = do_in[layer, chunk, slot_of(other), head]
            for i in (2 * chunk, 2 * chunk + 1):
                columns = slice(TILE * i, TILE * i + TILE)
                query_tile = rq[layer, head, :, columns]
                grad_tile = ro[head, :, columns]
                log_total = lse[layer, head, :, columns]
                delta = jnp.sum(
                    ro[head, DIM:, columns].astype(F32) * o_t[layer, head, :, columns],
                    axis=0,
                    keepdims=True,
                )
                query_grad = jnp.zeros((DIM, TILE), F32)
                for j in range(i + 1):
                    span = slice(TILE * j, TILE * j + TILE)
                    keys = kv[layer, head, span, :]
                    weight = jnp.exp(nn(keys, query_tile) + bias[1 if j == i else 0] - log_total)
                    scored = (weight * (nn(keys, grad_tile) - delta)).astype(BF16)
                    term = nt(scored, query_tile) + nt(weight.astype(BF16), grad_tile)
                    if chunk == 1 and (i == 2 or j == i):
                        acc[head, span, :] = term
                    else:
                        acc[head, span, :] += term
                    query_grad = query_grad + nn(kv_t[layer, head, 0:DIM, span], scored)
                dq_t[:, columns] = query_grad * (DIM ** -0.5)
            for other in range(TEAM):
                start = HALF * (TEAM * chunk + other)
                span = slice(start, start + HALF)
                pack_out[chunk, other, head, 0:HALF, :] = acc[head, span, :].astype(BF16)
                pack_out[chunk, other, head, HALF:, :] = dq_t[:, span].astype(BF16)
            return carry

        lax.fori_loop(0, OWN, one_head, 0)
        exchange(3, layer, chunk, pack_out, dqkv_in)

    def project_back(layer, half):
        rows = rows_of(half)
        arrived(3, layer, half, dqkv_in)
        turned = jnp.concatenate(
            [dqkv_in[layer, half, slot_of(head // 2), head % 2, HALF:, :] for head in range(RUNS)], axis=0
        )
        dqkv[rows, 0:WIDTH] = turned.T
        for pair in range(RUNS // 2):
            first = dqkv_in[layer, half, slot_of(pair), 0, 0:HALF, :].astype(F32)
            other = dqkv_in[layer, half, slot_of(pair), 1, 0:HALF, :].astype(F32)
            k_pair = jnp.where(low, first, pltpu.roll(other, DIM, 1))
            v_pair = jnp.where(low, pltpu.roll(first, DIM, 1), other)
            dqkv[rows, WIDTH + 128 * pair : WIDTH + 128 * pair + 128] = k_pair.astype(BF16)
            dqkv[rows, 2 * WIDTH + 128 * pair : 2 * WIDTH + 128 * pair + 128] = v_pair.astype(BF16)
        grad[half] = grad[half] + nt(dqkv[rows, :], wqkv[layer])

    def scatter_rows(layer, result, first_row):
        for run in range(RUNS):
            for quarter in range(4):
                parts[layer, quarter, run // 2, run % 2, first_row : first_row + DIM, :] = result[
                    DIM * run : DIM * run + DIM, 128 * quarter : 128 * quarter + 128
                ].astype(BF16)

    def up_grads(layer):
        for step in range(FF // CUT):
            cut = slice(CUT * step, CUT * step + CUT)
            scatter_rows(layer, nn(ent_t[layer], du[:, cut]), UP + DIM * step)

    def down_grads(layer):
        for run in range(RUNS):
            result = nn(act_t[layer, TILE * run : TILE * run + TILE, :], dz[...])
            for quarter in range(4):
                parts[layer, quarter, run // 2, run % 2, DOWN : DOWN + PART, :] = result[
                    :, 128 * quarter : 128 * quarter + 128
                ].astype(BF16)

    def late_grads(layer):
        scatter_rows(layer, nn(attn_t[layer], da[layer]), LATE + 192)
        for step in range(3):
            scatter_rows(
                layer, nn(hid_t[layer], dqkv[:, WIDTH * step : WIDTH * step + WIDTH]), LATE + DIM * step
            )

    def remote(source, target, send, recv, peer):
        return pltpu.make_async_remote_copy(
            src_ref=source,
            dst_ref=target,
            send_sem=send,
            recv_sem=recv,
            device_id=peer,
            device_id_type=MESH,
        )

    def credit(semaphore, peer):
        pl.semaphore_signal(semaphore, inc=1, device_id=peer, device_id_type=MESH)

    def rows_in(part, order):
        return pl.ds(part + ORDERS[order][0], ORDERS[order][1])

    def core_copy(layer, part, across):
        rows = pl.ds(part, PART)
        which = (layer, part // PART, across)
        return remote(
            parts.at[layer, 2 * across + 1 - core, :, :, rows],
            core_in.at[across, :, :, rows],
            core_send.at[which],
            core_recv.at[which],
            core_peer,
        )

    def x_copy(layer, part, order):
        rows = rows_in(part, order)
        which = (layer, part // PART, order)
        ends = (x_send.at[which], x_recv.at[which], x_peer)
        if order == 0:
            return remote(parts.at[layer, far_side, :, :, rows], x_in.at[:, :, rows], *ends)
        return remote(parts.at[layer, far_side, :, yy, rows], x_in.at[:, 0, rows], *ends)

    def y_copy(layer, part, order, across):
        rows = rows_in(part, order)
        which = (layer, part // PART, order, across)
        ends = (y_send.at[which], y_recv.at[which], y_peer)
        quarter = grp if order == 0 else 2 * across + core
        return remote(parts.at[layer, quarter, :, 1 - yy, rows], y_in.at[across, :, rows], *ends)

    def z_copy(layer, part, order, step):
        rows = rows_in(part, order)
        peer = lax.rem(zz + step, 4)
        return remote(
            parts.at[layer, grp, peer, yy, rows],
            z_in.at[layer, 4 - step, rows],
            z_send.at[layer, part // PART, order, step],
            z_recv.at[layer, part // PART, order, 4 - step],
            place(core, side, peer, yy),
        )

    def third_z_copy(layer, part, across, step):
        peer = lax.rem(zz + step, 4)
        which = (layer, part // PART, across)
        return remote(
            parts.at[layer, 2 * across + core, peer, :, rows_in(part, 2)],
            third_z.at[layer, part // PART, across, 4 - step],
            tz_send.at[(*which, step)],
            tz_recv.at[(*which, 4 - step)],
            place(core, side, peer, yy),
        )

    def third_x_copy(layer, part):
        which = (layer, part // PART)
        return remote(
            parts.at[layer, far_side, zz, :, rows_in(part, 2)],
            third_x.at[which],
            tx_send.at[which],
            tx_recv.at[which],
            x_peer,
        )

    def third_y_copy(layer, part):
        which = (layer, part // PART)
        return remote(
            parts.at[layer, grp, zz, 1 - yy, rows_in(part, 2)],
            third_y.at[which],
            ty_send.at[which],
            ty_recv.at[which],
            y_peer,
        )

    def final_copy(layer, part, which):
        rows = pl.ds(part, PART)
        quarter = far_side if which == 2 else grp
        block = final.at[layer, quarter, rows]
        return remote(
            block,
            block,
            fin_send.at[layer, part // PART, which],
            fin_recv.at[layer, part // PART, which],
            x_peer if which == 0 else core_peer,
        )

    def core_start(layer, part):
        if layer == 0:
            pl.semaphore_wait(core_free.at[part // PART], 1)
        for across in range(2):
            core_copy(layer, part, across).start()

    def core_done(layer, part):
        rows = pl.ds(part, PART)
        for across in range(2):
            core_copy(layer, part, across).wait()
        if layer == 0:
            pl.semaphore_wait(x_free.at[part // PART, 0], 1)
            pl.semaphore_wait(y_free.at[part // PART, 1], 1)
        for across in (1 - side, side):
            parts[layer, 2 * across + core, :, :, rows, :] += core_in[across, :, :, rows, :]
            if across is not side:
                x_copy(layer, part, 0).start()
            y_copy(layer, part, 1, across).start()
            for step in range(1, 4):
                third_z_copy(layer, part, across, step).start()
        if layer == 1:
            credit(core_free.at[part // PART], core_peer)

    def first_done(layer, part):
        rows = rows_in(part, 1)
        for across in (1 - side, side):
            y_copy(layer, part, 1, across).wait()
        if layer == 0:
            pl.semaphore_wait(x_free.at[part // PART, 1], 1)
            pl.semaphore_wait(y_free.at[part // PART, 0], 1)
        for across in (1 - side, side):
            parts[layer, 2 * across + core, :, yy, rows, :] += y_in[across, :, rows, :]
            if across is not side:
                x_copy(layer, part, 1).start()
        if layer == 1:
            credit(y_free.at[part // PART, 1], y_peer)

        rows = rows_in(part, 0)
        x_copy(layer, part, 0).wait()
        for y in (1 - yy, yy):
            parts[layer, grp, :, y, rows, :] += x_in[:, y, rows, :]
            if y is not yy:
                y_copy(layer, part, 0, 0).start()
        if layer == 1:
            credit(x_free.at[part // PART, 0], x_peer)

        rows = rows_in(part, 2)
        for across in (1 - side, side):
            for step in range(1, 4):
                third_z_copy(layer, part, across, step).wait()
            total = parts[layer, 2 * across + core, zz, :, rows, :].astype(F32)
            for slot in range(1, 4):
                total = total + third_z[layer, part // PART, across, slot].astype(F32)
            parts[layer, 2 * across + core, zz, :, rows, :] = total.astype(BF16)
            if across is not side:
                third_x_copy(layer, part).start()

    def second_done(layer, part):
        for order in (1, 0):
            rows = rows_in(part, order)
            if order == 0:
                y_copy(layer, part, 0, 0).wait()
                parts[layer, grp, :, yy, rows, :] += y_in[0, :, rows, :]
            else:
                x_copy(layer, part, 1).wait()
                parts[layer, grp, :, yy, rows, :] += x_in[:, 0, rows, :]
            for step in range(1, 4):
                z_copy(layer, part, order, step).start()
            if layer == 1:
                if order == 0:
                    credit(y_free.at[part // PART, 0], y_peer)
                else:
                    credit(x_free.at[part // PART, 1], x_peer)
        rows = rows_in(part, 2)
        third_x_copy(layer, part).wait()
        for y in (1 - yy, yy):
            parts[layer, grp, zz, y, rows, :] += third_x[layer, part // PART, y]
            if y is not yy:
                third_y_copy(layer, part).start()

    def z_done(layer, part):
        for order in (1, 0):
            for step in range(1, 4):
                z_copy(layer, part, order, step).wait()
        rows = pl.ds(part, ORDERS[2][0])
        total = parts[layer, grp, zz, yy, rows, :].astype(F32)
        for slot in range(1, 4):
            total = total + z_in[layer, slot, rows, :].astype(F32)
        final[layer, grp, rows, :] = total.astype(BF16)
        rows = rows_in(part, 2)
        third_y_copy(layer, part).wait()
        final[layer, grp, rows, :] = parts[layer, grp, zz, yy, rows, :] + third_y[layer, part // PART]
        for which in range(2):
            final_copy(layer, part, which).start()

    def final_pass(layer, part):
        final_copy(layer, part, 0).wait()
        final_copy(layer, part, 2).start()

    def final_out(layer, part):
        rows = pl.ds(part, PART)
        return pltpu.make_async_copy(
            final.at[layer, :, rows], final_hbm.at[layer, :, rows], out_sem.at[layer, part // PART]
        )

    def final_done(layer, part):
        for which in range(1, 3):
            final_copy(layer, part, which).wait()
        final_out(layer, part).start()

    def small_copy(stage):
        peer = (core_peer, x_peer, y_peer)[stage]
        return remote(
            small_sum.at[stage], small_in.at[stage], small_send.at[stage], small_recv.at[stage], peer
        )

    def small_z_copy(step):
        return remote(
            small_z.at[zz],
            small_z.at[zz],
            small_send.at[2 + step],
            small_recv.at[2 + step],
            place(core, side, lax.rem(zz + step, 4), yy),
        )

    def small_start():
        small_sum[0] = small[0] + small[1]
        small_copy(0).start()

    def small_next(stage):
        small_copy(stage).wait()
        total = small_sum[stage] + small_in[stage]
        if stage < 2:
            small_sum[stage + 1] = total
            small_copy(stage + 1).start()
        else:
            small_z[zz] = total
            for step in range(1, 4):
                small_z_copy(step).start()

    def small_done():
        for step in range(1, 4):
            small_z_copy(step).wait()
        small_sum[0] = (small_z[0] + small_z[1]) + (small_z[2] + small_z[3])
        small_final[:, 0:256] = small_sum[0, :, pl.ds(pl.multiple_of(blk * 256, 256), 256)]
        pair = small_sum[0, :, pl.ds(pl.multiple_of(FF + 128 * zz, 128), 128)]
        small_final[:, 256:384] = jnp.where(yy == 1, pltpu.roll(pair, DIM, 1), pair)
        small_final[:, 384:512] = small_sum[0, :, FF + WIDTH :]

    def halves(*phases, backward=False):
        def both(step, carry):
            for phase in phases:
                phase(1 - step if backward else step)
            return carry

        lax.fori_loop(0, 2, both, 0)

    def begin(half):
        move_arrived(0, half, tok_in)
        hidden[half] = tok_in[half].astype(F32)

    def finish(half):
        back_out[0, half] = hidden[half].astype(BF16)
        to_owner(3, half, back_out.at[0, half], out_in)

    def turn_round(layer, half):
        move_arrived(2, half, cot_in)
        grad[half] = cot_in[half].astype(F32)
        dz[rows_of(half), :] = (alphas[layer, 1] * grad[half]).astype(BF16)

    def hand_back(half):
        back_out[1, half] = grad[half].astype(BF16)
        to_owner(4, half, back_out.at[1, half], grad_in)

    pl.semaphore_wait(barrier, 10)
    for half in range(2):
        to_team(0, half, half_of(tokens, half), tok_in)
    for half in range(2):
        to_team(1, half, flag_out, flag_in)
    for half in range(2):
        to_team(2, half, half_of(cotangent, half), cot_in)
    weight_copies[0, 0].wait()
    halves(begin, functools.partial(project, 0))

    move_arrived(1, 0, flag_in)
    move_arrived(1, 1, flag_in)
    border = jnp.concatenate([flag_in[0, 0:1, :]] * 2, axis=1) - (HALF * lax.div(zz, 2)).astype(F32)
    key_row = lax.broadcasted_iota(jnp.int32, (TILE, TILE), 0)
    query_col = lax.broadcasted_iota(jnp.int32, (TILE, TILE), 1)
    later = key_row > query_col
    key_sub = lax.rem(key_row, HALF).astype(F32) >= border
    query_sub = lax.rem(query_col, HALF).astype(F32) >= border
    apart = jnp.logical_xor(key_sub, query_sub)
    bias[0] = jnp.where(apart, NEGATIVE, 0.0)
    bias[1] = jnp.where(jnp.logical_or(later, apart), NEGATIVE, 0.0)

    for number in range(1, 4):
        weight_copies[0, number].wait()
    attend(0, 0)
    attend(0, 1)
    weight_copies[1, 0].wait()
    halves(functools.partial(feed, 0), functools.partial(project, 1))
    for number in range(1, 4):
        weight_copies[1, number].wait()
    attend(1, 0)
    attend(1, 1)
    halves(functools.partial(feed, 1), finish)

    halves(functools.partial(turn_round, 1))
    down_grads(1)
    core_start(1, DOWN)
    halves(functools.partial(feed_back, 1), backward=True)
    core_done(1, DOWN)
    up_grads(1)
    core_start(1, UP)
    attend_back(1, 1)
    core_done(1, UP)
    attend_back(1, 0)

    def once(half):
        @pl.when(half == 1)
        def _():
            first_done(1, DOWN)

    halves(functools.partial(project_back, 1), functools.partial(feed_back, 0), once, backward=True)
    up_grads(0)
    core_start(0, UP)
    small_start()
    first_done(1, UP)
    second_done(1, DOWN)
    attend_back(0, 1)
    core_done(0, UP)
    late_grads(1)
    core_start(1, LATE)
    down_grads(0)
    core_start(0, DOWN)
    small_next(0)
    attend_back(0, 0)
    core_done(1, LATE)
    core_done(0, DOWN)
    small_next(1)
    second_done(1, UP)
    z_done(1, DOWN)

    def twice(half):
        @pl.when(half == 1)
        def _():
            first_done(0, UP)
            first_done(1, LATE)

    halves(functools.partial(project_back, 0), hand_back, twice, backward=True)
    late_grads(0)
    core_start(0, LATE)
    small_next(2)
    first_done(0, DOWN)
    z_done(1, UP)
    second_done(0, UP)
    second_done(1, LATE)
    core_done(0, LATE)
    final_pass(1, UP)
    final_pass(1, DOWN)
    small_done()
    second_done(0, DOWN)
    first_done(0, LATE)
    z_done(0, UP)
    z_done(1, LATE)
    second_done(0, LATE)
    final_done(1, UP)
    final_done(1, DOWN)
    results = []
    for half in range(2):
        rows = pl.ds(HALF * half, HALF)
        move_arrived(3, half, out_in)
        results.append(pltpu.make_async_copy(out_in.at[half], output_hbm.at[rows], out_sem.at[2, half]))
        move_arrived(4, half, grad_in)
        results.append(pltpu.make_async_copy(grad_in.at[half], input_grad_hbm.at[rows], out_sem.at[3, half]))
    for copy in results:
        copy.start()
    z_done(0, DOWN)
    final_pass(1, LATE)
    final_pass(0, UP)
    z_done(0, LATE)
    final_pass(0, DOWN)
    final_done(1, LATE)
    final_done(0, UP)
    final_pass(0, LATE)
    final_done(0, DOWN)
    final_done(0, LATE)

    for half in range(2):
        left(2, 0, half, head_out)
        left(3, 0, half, pack_out)
        to_team_left(0, half, half_of(tokens, half))
        to_team_left(1, half, flag_out)
        to_team_left(2, half, half_of(cotangent, half))
        to_owner_left(3, half, back_out.at[0, half])
        to_owner_left(4, half, back_out.at[1, half])
    for copy in results:
        copy.wait()
    for layer in range(LAYERS):
        for part in (UP, DOWN, LATE):
            final_out(layer, part).wait()


def results_kernel(
    final_hbm, out_hbm, grad_hbm, small,
    output, input_grad, qkv_grad, out_grad, up_grad, up_bias_grad, down_grad, down_bias_grad, alpha_grad,
    final, grad_block, out_block, sem,
):
    moves = [
        pltpu.make_async_copy(final_hbm.at[1], final.at[1], sem.at[0]),
        pltpu.make_async_copy(final_hbm.at[0], final.at[0], sem.at[1]),
        pltpu.make_async_copy(grad_hbm, grad_block, sem.at[2]),
        pltpu.make_async_copy(out_hbm, out_block, sem.at[3]),
    ]
    for move in moves:
        move.start()
    up_bias_grad[...] = small[:, 0:256]
    down_bias_grad[...] = small[:, 256 : 256 + DIM]
    alpha_grad[...] = small[:, 384:386]
    for layer in (1, 0):
        moves[1 - layer].wait()
        for quarter in range(4):

            def block(first, count):
                return final[layer, quarter, first : first + count, :].astype(F32)

            def columns(step):
                return slice(WIDTH * step + 128 * quarter, WIDTH * step + 128 * quarter + 128)

            for step in range(3):
                qkv_grad[layer, :, columns(step)] = block(DIM * step, DIM)
            out_grad[layer, :, columns(0)] = block(192, DIM)
            for step in range(4):
                up_grad[layer, :, columns(step)] = block(UP + DIM * step, DIM)
            down_grad[layer, :, columns(0)] = block(DOWN, PART)
    moves[2].wait()
    input_grad[...] = grad_block[...].astype(F32)
    moves[3].wait()
    output[...] = out_block[...]


def fast_body(
    tokens, seq_len, qkv_weight, out_weight, up_weight, up_bias, down_weight, down_bias, alphas, cotangent
):
    whole = pl.BlockSpec(memory_space=pltpu.VMEM)
    scalar = pl.BlockSpec(memory_space=pltpu.SMEM)
    far = pl.BlockSpec(memory_space=pl.ANY)
    shape = jax.ShapeDtypeStruct
    rows = HALF * RUNS

    def vmem(*dims):
        return pltpu.VMEM(dims, BF16)

    def wide(*dims):
        return pltpu.VMEM(dims, F32)

    dma = pltpu.SemaphoreType.DMA
    final, out_block, grad_block, small = pl.pallas_call(
        layers_kernel,
        out_shape=(
            shape((LAYERS, 4, CHUNK, 128), BF16),
            shape((2 * HALF, WIDTH), BF16),
            shape((2 * HALF, WIDTH), BF16),
            shape((LAYERS, WIDTH), F32),
        ),
        in_specs=[whole, scalar, scalar, whole, whole, whole, far, far, far, far],
        out_specs=(far, far, far, whole),
        scratch_shapes=[
            vmem(LAYERS, WIDTH, 3 * WIDTH),
            vmem(LAYERS, WIDTH, WIDTH),
            vmem(LAYERS, WIDTH, FF),
            vmem(LAYERS, FF, WIDTH),
            vmem(2, HALF, WIDTH),
            vmem(2, HALF, WIDTH),
            wide(8, 128),
            wide(2, 8, 128),
            vmem(2, 2, HALF, WIDTH),
            vmem(2, HALF, WIDTH),
            vmem(2, HALF, WIDTH),
            wide(2, HALF, WIDTH),
            wide(2, HALF, WIDTH),
            vmem(LAYERS, WIDTH, 2 * HALF),
            vmem(LAYERS, WIDTH, 2 * HALF),
            vmem(LAYERS, WIDTH, 2 * HALF),
            vmem(LAYERS, FF, 2 * HALF),
            wide(LAYERS, 2, HALF, WIDTH),
            wide(LAYERS, 2, HALF, FF),
            wide(LAYERS, 2, HALF, WIDTH),
            vmem(2 * HALF, WIDTH),
            vmem(2 * HALF, FF),
            vmem(LAYERS, 2 * HALF, WIDTH),
            vmem(2 * HALF, 3 * WIDTH),
            vmem(2, TEAM, OWN, PACK, 128),
            vmem(2, TEAM, OWN, DIM, 128),
            vmem(LAYERS, 2, TEAM, OWN, PACK, 128),
            vmem(LAYERS, 2, TEAM, OWN, DIM, 128),
            vmem(LAYERS, 2, TEAM, OWN, DIM, 128),
            vmem(LAYERS, 2, TEAM, OWN, PACK, 128),
            vmem(LAYERS, OWN, rows, 128),
            vmem(LAYERS, OWN, 128, rows),
            vmem(LAYERS, OWN, 128, rows),
            vmem(OWN, 128, rows),
            wide(LAYERS, OWN, DIM, rows),
            wide(LAYERS, OWN, 1, rows),
            wide(OWN, rows, 128),
            wide(DIM, rows),
            wide(2, TILE, TILE),
            vmem(LAYERS, 4, 4, 2, CHUNK, 128),
            vmem(2, 4, 2, CHUNK, 128),
            vmem(4, 2, CHUNK, 128),
            vmem(2, 4, CHUNK, 128),
            vmem(LAYERS, 4, CHUNK, 128),
            vmem(LAYERS, 3, 2, 4, 2, THIRD, 128),
            vmem(LAYERS, 3, 2, THIRD, 128),
            vmem(LAYERS, 3, THIRD, 128),
            vmem(LAYERS, 4, CHUNK, 128),
            wide(2, LAYERS, SMALL),
            wide(3, LAYERS, SMALL),
            wide(4, LAYERS, SMALL),
            wide(3, LAYERS, SMALL),
            dma((LAYERS, 4)),
            dma((5, 2)),
            dma((5, 2)),
            dma((4, LAYERS, 2)),
            dma((4, LAYERS, 2)),
            dma((LAYERS, 3, 2)),
            dma((LAYERS, 3, 2)),
            dma((LAYERS, 3, 2)),
            dma((LAYERS, 3, 2)),
            dma((LAYERS, 3, 2, 2)),
            dma((LAYERS, 3, 2, 2)),
            dma((LAYERS, 3, 2, 4)),
            dma((LAYERS, 3, 2, 4)),
            dma((LAYERS, 3, 2, 4)),
            dma((LAYERS, 3, 2, 4)),
            dma((LAYERS, 3)),
            dma((LAYERS, 3)),
            dma((LAYERS, 3)),
            dma((LAYERS, 3)),
            dma((LAYERS, 3, 3)),
            dma((LAYERS, 3, 3)),
            dma((6,)),
            dma((6,)),
            dma((4, 3)),
            pltpu.SemaphoreType.REGULAR((3,)),
            pltpu.SemaphoreType.REGULAR((3, 2)),
            pltpu.SemaphoreType.REGULAR((3, 2)),
        ],
        compiler_params=pltpu.CompilerParams(
            collective_id=0, has_side_effects=True, vmem_limit_bytes=63 * 1024 * 1024
        ),
        name="layers",
    )(
        tokens, seq_len, alphas, up_bias, down_bias, cotangent,
        qkv_weight, out_weight, up_weight, down_weight,
    )
    return tuple(
        pl.pallas_call(
            results_kernel,
            out_shape=(
                shape((2 * HALF, WIDTH), BF16),
                shape((2 * HALF, WIDTH), F32),
                shape((LAYERS, DIM, 3 * WIDTH), F32),
                shape((LAYERS, DIM, WIDTH), F32),
                shape((LAYERS, DIM, FF), F32),
                shape((LAYERS, FF // RUNS), F32),
                shape((LAYERS, FF // RUNS, WIDTH), F32),
                shape((LAYERS, DIM), F32),
                shape((LAYERS, 2), F32),
            ),
            in_specs=[far, far, far, whole],
            out_specs=(whole,) * 9,
            scratch_shapes=[
                vmem(LAYERS, 4, CHUNK, 128), vmem(2 * HALF, WIDTH), vmem(2 * HALF, WIDTH), dma((4,))
            ],
            compiler_params=pltpu.CompilerParams(vmem_limit_bytes=60 * 1024 * 1024),
            name="results",
        )(final, out_block, grad_block, small)
    )


def layout(seq_len, local_count, cycle_size):
    piece_rows = seq_len[0] // cycle_size
    end_rows = jnp.cumsum(piece_rows)
    start_rows = end_rows - piece_rows
    local_rows = jnp.arange(local_count, dtype=jnp.int32)
    segment = jnp.sum((local_rows[:, None] >= end_rows[None, :]).astype(jnp.int32), axis=1)
    picked = segment[:, None] == jnp.arange(seq_len.shape[1], dtype=jnp.int32)[None, :]
    offset = local_rows - jnp.sum(jnp.where(picked, start_rows[None, :], 0), axis=1)
    span_rows = jnp.sum(jnp.where(picked, piece_rows[None, :], 0), axis=1)
    return (segment, offset, span_rows)


def gelu_exact(values):
    return jax.nn.gelu(values, approximate=False)


def key_block(whole, geometry, block_index, head_count):
    query_seg, query_pos, seg_all, pos_all, block_rows, score_scale = geometry
    first_row = block_index * block_rows
    key_piece = lax.dynamic_slice_in_dim(whole, first_row, block_rows, 0)
    key_seg = lax.dynamic_slice_in_dim(seg_all, first_row, block_rows, 0)
    key_pos = lax.dynamic_slice_in_dim(pos_all, first_row, block_rows, 0)
    half_width = key_piece.shape[1] // 2
    keys_part = key_piece[:, :half_width].reshape(block_rows, head_count, -1)
    values_part = key_piece[:, half_width:].reshape(block_rows, head_count, -1)
    return (keys_part, values_part, key_seg, key_pos)


def block_scores(queries, keys_part, key_seg, key_pos, geometry):
    query_seg, query_pos, seg_all, pos_all, block_rows, score_scale = geometry
    scores = (
        jnp.einsum("qhd,khd->hqk", queries, keys_part, preferred_element_type=jnp.float32)
        * score_scale
    )
    allowed = (query_seg[:, None] == key_seg[None, :]) & (key_pos[None, :] <= query_pos[:, None])
    return (scores, allowed[None])


def attend(queries, whole, geometry):
    row_count, head_count, head_dim = queries.shape
    block_count = whole.shape[0] // geometry[4]

    def statistics(running, block_index):
        largest, totals = running
        keys_part, values_part, key_seg, key_pos = key_block(
            whole, geometry, block_index, head_count
        )
        scores, allowed = block_scores(queries, keys_part, key_seg, key_pos, geometry)
        newest = jnp.maximum(largest, jnp.max(jnp.where(allowed, scores, NEGATIVE), axis=2))
        weights = jnp.where(allowed, jnp.exp(scores - newest[:, :, None]), 0.0)
        totals = totals * jnp.exp(largest - newest) + jnp.sum(weights, axis=2)
        return ((newest, totals), None)

    initial = (
        jnp.full((head_count, row_count), NEGATIVE, jnp.float32),
        jnp.zeros((head_count, row_count), jnp.float32),
    )
    (largest, totals), unused = lax.scan(statistics, initial, jnp.arange(block_count))
    log_total = largest + jnp.log(totals)

    def weighted(output_sum, block_index):
        keys_part, values_part, key_seg, key_pos = key_block(
            whole, geometry, block_index, head_count
        )
        scores, allowed = block_scores(queries, keys_part, key_seg, key_pos, geometry)
        probs = jnp.where(allowed, jnp.exp(scores - log_total[:, :, None]), 0.0).astype(
            jnp.bfloat16
        )
        output_sum = output_sum + jnp.einsum(
            "hqk,khd->qhd", probs, values_part, preferred_element_type=jnp.float32
        )
        return (output_sum, None)

    output_sum, unused = lax.scan(
        weighted, jnp.zeros((row_count, head_count, head_dim), jnp.float32), jnp.arange(block_count)
    )
    return (output_sum, log_total)


def attend_back(queries, whole, log_total, delta_sum, grad_heads, geometry):
    row_count, head_count, head_dim = queries.shape
    block_rows = geometry[4]
    score_scale = geometry[5]
    block_count = whole.shape[0] // block_rows

    def gradients(query_grad, block_index):
        keys_part, values_part, key_seg, key_pos = key_block(
            whole, geometry, block_index, head_count
        )
        scores, allowed = block_scores(queries, keys_part, key_seg, key_pos, geometry)
        probs = jnp.where(allowed, jnp.exp(scores - log_total[:, :, None]), 0.0)
        grad_probs = jnp.einsum(
            "qhd,khd->hqk", grad_heads, values_part, preferred_element_type=jnp.float32
        )
        grad_scores = (probs * (grad_probs - delta_sum[:, :, None])).astype(jnp.bfloat16)
        query_grad = (
            query_grad
            + jnp.einsum("hqk,khd->qhd", grad_scores, keys_part, preferred_element_type=jnp.float32)
            * score_scale
        )
        key_grad = (
            jnp.einsum("hqk,qhd->khd", grad_scores, queries, preferred_element_type=jnp.float32)
            * score_scale
        )
        value_grad = jnp.einsum(
            "hqk,qhd->khd",
            probs.astype(jnp.bfloat16),
            grad_heads,
            preferred_element_type=jnp.float32,
        )
        joined = jnp.concatenate(
            [key_grad.reshape(block_rows, -1), value_grad.reshape(block_rows, -1)], axis=1
        )
        return (query_grad, joined)

    query_grad, stacked = lax.scan(
        gradients,
        jnp.zeros((row_count, head_count, head_dim), jnp.float32),
        jnp.arange(block_count),
    )
    return (query_grad, stacked.reshape(whole.shape[0], -1))


def layer_forward(hidden, layer_index, weights, geometry):
    qkv_weight, out_weight, up_weight, up_bias, down_weight, down_bias, alphas = weights
    row_count, model_width = hidden.shape
    projection = qkv_weight[layer_index]
    rounded = hidden.astype(jnp.bfloat16)
    queries = (
        jnp.dot(rounded, projection[:, :model_width], preferred_element_type=jnp.float32)
        .astype(jnp.bfloat16)
        .reshape(row_count, HEADS, -1)
    )
    key_value = jnp.dot(
        rounded, projection[:, model_width:], preferred_element_type=jnp.float32
    ).astype(jnp.bfloat16)
    whole = lax.all_gather(key_value, "blk", axis=0, tiled=True)
    heads_out, log_total = attend(queries, whole, geometry)
    heads_rounded = heads_out.reshape(row_count, model_width).astype(jnp.bfloat16)
    branch = jnp.dot(heads_rounded, out_weight[layer_index], preferred_element_type=jnp.float32)
    alpha_pair = alphas[layer_index]
    middle = hidden + alpha_pair[0] * branch
    entered = middle.astype(jnp.bfloat16)
    gate_pre = (
        jnp.dot(entered, up_weight[layer_index], preferred_element_type=jnp.float32)
        + up_bias[layer_index]
    )
    activated = gelu_exact(gate_pre).astype(jnp.bfloat16)
    second = (
        jnp.dot(activated, down_weight[layer_index], preferred_element_type=jnp.float32)
        + down_bias[layer_index]
    )
    result = middle + alpha_pair[1] * second
    saved = (
        rounded,
        queries,
        key_value,
        whole,
        heads_out,
        heads_rounded,
        log_total,
        branch,
        entered,
        gate_pre,
        activated,
        second,
    )
    return (result, saved)


def layer_backward(grad_hidden, saved, layer_index, weights, geometry):
    qkv_weight, out_weight, up_weight, up_bias, down_weight, down_bias, alphas = weights
    (
        rounded,
        queries,
        key_value,
        saved_whole,
        heads_out,
        heads_rounded,
        log_total,
        branch,
        entered,
        gate_pre,
        activated,
        second,
    ) = saved
    row_count = grad_hidden.shape[0]
    alpha_pair = alphas[layer_index]
    grad_second = (alpha_pair[1] * grad_hidden).astype(jnp.bfloat16)
    alpha_second = jnp.sum(grad_hidden * second)
    bias_down = jnp.sum(grad_second.astype(jnp.float32), axis=0)
    grad_down = jnp.einsum("tf,td->fd", activated, grad_second, preferred_element_type=jnp.float32)
    grad_act = jnp.einsum(
        "td,fd->tf", grad_second, down_weight[layer_index], preferred_element_type=jnp.float32
    )
    unused, gelu_pull = jax.vjp(gelu_exact, gate_pre)
    grad_gate = gelu_pull(grad_act)[0].astype(jnp.bfloat16)
    bias_up = jnp.sum(grad_gate.astype(jnp.float32), axis=0)
    grad_up = jnp.einsum("td,tf->df", entered, grad_gate, preferred_element_type=jnp.float32)
    grad_middle = grad_hidden + jnp.einsum(
        "tf,df->td", grad_gate, up_weight[layer_index], preferred_element_type=jnp.float32
    )
    grad_branch = (alpha_pair[0] * grad_middle).astype(jnp.bfloat16)
    alpha_first = jnp.sum(grad_middle * branch)
    grad_proj_out = jnp.einsum(
        "te,td->ed", heads_rounded, grad_branch, preferred_element_type=jnp.float32
    )
    grad_heads = (
        jnp.einsum(
            "td,ed->te", grad_branch, out_weight[layer_index], preferred_element_type=jnp.float32
        )
        .astype(jnp.bfloat16)
        .reshape(queries.shape)
    )
    delta_sum = jnp.sum(grad_heads.astype(jnp.float32) * heads_out, axis=2).T
    whole = lax.all_gather(key_value, "blk", axis=0, tiled=True)
    query_grad, key_terms = attend_back(queries, whole, log_total, delta_sum, grad_heads, geometry)
    key_grads = lax.psum_scatter(
        key_terms.astype(jnp.bfloat16), "blk", scatter_dimension=0, tiled=True
    )
    grad_proj = jnp.concatenate(
        [query_grad.reshape(row_count, -1).astype(jnp.bfloat16), key_grads], axis=1
    )
    grad_qkv = jnp.einsum("td,te->de", rounded, grad_proj, preferred_element_type=jnp.float32)
    grad_input = grad_middle + jnp.einsum(
        "te,de->td", grad_proj, qkv_weight[layer_index], preferred_element_type=jnp.float32
    )
    layer_grads = (
        grad_qkv,
        grad_proj_out,
        grad_up,
        bias_up,
        grad_down,
        bias_down,
        jnp.stack([alpha_first, alpha_second]),
    )
    return (grad_input, layer_grads)


def reduce_all(layer_results, cycle_size):
    stacked = [
        jnp.stack([layer_entry[member] for layer_entry in layer_results], axis=0)
        for member in range(6)
    ]
    alpha_tiles = jnp.stack(
        [jnp.tile(layer_entry[6], cycle_size) for layer_entry in layer_results], axis=0
    )
    shares = (
        lax.psum_scatter(
            stacked[0].astype(jnp.bfloat16), "blk", scatter_dimension=1, tiled=True
        ).astype(jnp.float32),
        lax.psum_scatter(
            stacked[1].astype(jnp.bfloat16), "blk", scatter_dimension=1, tiled=True
        ).astype(jnp.float32),
        lax.psum_scatter(
            stacked[2].astype(jnp.bfloat16), "blk", scatter_dimension=1, tiled=True
        ).astype(jnp.float32),
        lax.psum_scatter(
            stacked[3].astype(jnp.bfloat16), "blk", scatter_dimension=1, tiled=True
        ).astype(jnp.float32),
        lax.psum_scatter(
            stacked[4].astype(jnp.bfloat16), "blk", scatter_dimension=1, tiled=True
        ).astype(jnp.float32),
        lax.psum_scatter(
            stacked[5].astype(jnp.bfloat16), "blk", scatter_dimension=1, tiled=True
        ).astype(jnp.float32),
        lax.psum_scatter(
            alpha_tiles.astype(jnp.bfloat16), "blk", scatter_dimension=1, tiled=True
        ).astype(jnp.float32),
    )
    return (
        lax.psum(shares[0].astype(jnp.bfloat16), "grp").astype(jnp.float32),
        lax.psum(shares[1].astype(jnp.bfloat16), "grp").astype(jnp.float32),
        lax.psum(shares[2].astype(jnp.bfloat16), "grp").astype(jnp.float32),
        lax.psum(shares[3].astype(jnp.bfloat16), "grp").astype(jnp.float32),
        lax.psum(shares[4].astype(jnp.bfloat16), "grp").astype(jnp.float32),
        lax.psum(shares[5].astype(jnp.bfloat16), "grp").astype(jnp.float32),
        lax.psum(shares[6].astype(jnp.bfloat16), "grp").astype(jnp.float32),
    )


def body(
    tokens,
    seq_len,
    qkv_weight,
    out_weight,
    up_weight,
    up_bias,
    down_weight,
    down_bias,
    alphas,
    cotangent,
):
    row_count, model_width = tokens.shape
    cycle_size = lax.axis_size("blk")
    cycle_place = lax.axis_index("blk")
    head_dim = model_width // HEADS
    total_rows = cycle_size * row_count
    block_rows = min(max(row_count, 512), total_rows)
    segment, offset, span_rows = layout(seq_len, row_count, cycle_size)
    query_pos = cycle_place * span_rows + offset
    seg_all = jnp.tile(segment, cycle_size)
    pos_all = jnp.repeat(jnp.arange(cycle_size, dtype=jnp.int32), row_count) * jnp.tile(
        span_rows, cycle_size
    ) + jnp.tile(offset, cycle_size)
    geometry = (segment, query_pos, seg_all, pos_all, block_rows, head_dim ** (-0.5))
    weights = (qkv_weight, out_weight, up_weight, up_bias, down_weight, down_bias, alphas)
    hidden = tokens.astype(jnp.float32)
    saved_layers = []
    for layer_index in range(LAYERS):
        hidden, saved = layer_forward(hidden, layer_index, weights, geometry)
        saved_layers.append(saved)
    output = hidden.astype(jnp.bfloat16)
    grad_hidden = cotangent.astype(jnp.float32)
    layer_results = []
    for layer_index in reversed(range(LAYERS)):
        grad_hidden, layer_grads = layer_backward(
            grad_hidden, saved_layers[layer_index], layer_index, weights, geometry
        )
        layer_results.insert(0, layer_grads)
    finals = reduce_all(layer_results, cycle_size)
    return (
        output,
        grad_hidden,
        finals[0],
        finals[1],
        finals[2],
        finals[3],
        finals[4],
        finals[5],
        finals[6],
    )


def solution(mesh):
    placed = (
        P(("grp", "blk"), None),
        P("grp", None),
        P(),
        P(),
        P(),
        P(),
        P(),
        P(),
        P(),
        P(("grp", "blk"), None),
    )
    sizes = (mesh.shape["grp"], mesh.shape["blk"])
    return jax.shard_map(
        fast_body if sizes == (4, RUNS) else body,
        mesh=mesh,
        in_specs=placed,
        out_specs=(
            P(("grp", "blk"), None),
            P(("grp", "blk"), None),
            P(None, "blk", None),
            P(None, "blk", None),
            P(None, "blk", None),
            P(None, "blk"),
            P(None, "blk", None),
            P(None, "blk"),
            P(),
        ),
        check_vma=False,
    )
```

```python
import functools

import jax
import jax.numpy as jnp
from jax import lax
from jax.experimental import pallas as pl
from jax.experimental.pallas import tpu as pltpu
from jax.sharding import PartitionSpec as P

HEADS = 8
LAYERS = 2
NEGATIVE = -1e30
MESH = pl.DeviceIdType.MESH
F32 = jnp.float32
BF16 = jnp.bfloat16

HALF = 128
RUNS = 8
TEAM = 4
OWN = RUNS // TEAM
DIM = 64
WIDTH = 512
FF = 2048
CUT = 512
TILE = 256
TILES = HALF * RUNS // TILE
PACK = HALF + DIM
CHUNK = 768
SMALL = FF + WIDTH + 128
UP, DOWN, LATE = 256, 512, 0
PART = 256
ORDERS = ((0, 144), (144, 48), (192, 64))
THIRD = ORDERS[2][1]

SLOPE_AT = 0.28
TAIL = (
    0.11652077851573843,
    0.06749675579450809,
    0.2689101589486142,
    -0.23699347299932225,
    0.3898740127620002,
    -0.10580824228351815,
)


def nn(a, b):
    return lax.dot_general(a, b, (((1,), (0,)), ((), ())), preferred_element_type=F32)


def nt(a, b):
    return lax.dot_general(a, b, (((1,), (1,)), ((), ())), preferred_element_type=F32)


def layers_kernel(
    tokens, seq_len, alphas, up_bias, down_bias, cotangent, qkv_hbm, out_hbm, up_hbm, down_hbm,
    final_hbm, output_hbm, input_grad_hbm, small_final,
    wqkv, wout, wup, wdown,
    tok_in, cot_in, flag_out, flag_in, back_out, out_in, grad_in,
    hidden, grad, hid_t, attn_t, ent_t, act_t, branch, slope, second,
    dz, du, da, dqkv,
    pack_out, head_out, pack_in, o_in, do_in,
    kv, kv_t, rq, ro, o_t, lse, acc, dq_t, bias,
    parts, core_in, x_in, y_in, z_in, third_z, third_x, third_y, final, small, small_in, small_z, small_sum,
    w_sem, move_send, move_recv, a2a_send, a2a_recv, core_send, core_recv, x_send, x_recv, y_send, y_recv,
    z_send, z_recv, tz_send, tz_recv, tx_send, tx_recv, ty_send, ty_recv, fin_send, fin_recv, small_send, small_recv, out_sem, core_free, x_free, y_free,
):
    grp = lax.axis_index("grp")
    blk = lax.axis_index("blk")
    core = lax.rem(grp, 2)
    side = lax.div(grp, 2)
    yy = lax.rem(blk, 2)
    zz = lax.div(blk, 2)
    member = 2 * core + yy
    far_side = 2 * (1 - side) + core
    low = lax.broadcasted_iota(jnp.int32, (HALF, 128), 1) < DIM

    def place(c, x, z, y):
        return (2 * x + c, 2 * z + y)

    core_peer = place(1 - core, side, zz, yy)
    x_peer = place(core, 1 - side, zz, yy)
    y_peer = place(core, side, zz, 1 - yy)

    weight_copies = {}
    for layer in range(LAYERS):
        for number, (source, target) in enumerate(
            ((qkv_hbm, wqkv), (out_hbm, wout), (up_hbm, wup), (down_hbm, wdown))
        ):
            weight_copies[layer, number] = pltpu.make_async_copy(
                source.at[layer], target.at[layer], w_sem.at[layer, number]
            )
            weight_copies[layer, number].start()

    barrier = pltpu.get_barrier_semaphore()
    for step in range(1, 4):
        pl.semaphore_signal(
            barrier, inc=1, device_id=place(core, side, lax.rem(zz + step, 4), yy), device_id_type=MESH
        )
    for step in range(4):
        pl.semaphore_signal(
            barrier, inc=1, device_id=place(1 - core, side, lax.rem(zz + step, 4), yy), device_id_type=MESH
        )
    pl.semaphore_signal(barrier, inc=1, device_id=x_peer, device_id_type=MESH)
    pl.semaphore_signal(barrier, inc=1, device_id=y_peer, device_id_type=MESH)
    pl.semaphore_signal(
        barrier, inc=1, device_id=place(1 - core, side, zz, 1 - yy), device_id_type=MESH
    )

    end_second = lax.div(seq_len[0, 0] + seq_len[0, 1], RUNS)
    flag_out[...] = jnp.full((8, 128), end_second.astype(F32), F32)
    for layer in range(LAYERS):
        for head in range(OWN):
            rq[layer, head, DIM:, :] = jnp.zeros((DIM, HALF * RUNS), BF16)
    for head in range(OWN):
        ro[head, 0:DIM, :] = jnp.zeros((DIM, HALF * RUNS), BF16)

    def moved(kind, slot, source, target, at, core_at, z_at):
        here = jnp.logical_and(core_at == core, z_at == zz)

        @pl.when(here)
        def _():
            pltpu.make_async_copy(source, target.at[at], move_recv.at[kind, at]).start()

        @pl.when(jnp.logical_not(here))
        def _():
            pltpu.make_async_remote_copy(
                src_ref=source,
                dst_ref=target.at[at],
                send_sem=move_send.at[kind, slot],
                recv_sem=move_recv.at[kind, at],
                device_id=place(core_at, side, z_at, yy),
                device_id_type=MESH,
            ).start()

    def move_left(kind, slot, source, core_at, z_at):
        here = jnp.logical_and(core_at == core, z_at == zz)

        @pl.when(jnp.logical_not(here))
        def _():
            pltpu.make_async_copy(source, source, move_send.at[kind, slot]).wait()

    def move_arrived(kind, at, target):
        pltpu.make_async_copy(target.at[at], target.at[at], move_recv.at[kind, at]).wait()

    def to_team(kind, half, source, target):
        moved(kind, half, source, target, lax.div(zz, 2), lax.rem(zz, 2), 2 * half + core)

    def to_team_left(kind, half, source):
        move_left(kind, half, source, lax.rem(zz, 2), 2 * half + core)

    def to_owner(kind, chunk, source, target):
        moved(kind, chunk, source, target, lax.div(zz, 2), lax.rem(zz, 2), core + 2 * chunk)

    def to_owner_left(kind, chunk, source):
        move_left(kind, chunk, source, lax.rem(zz, 2), core + 2 * chunk)

    def half_of(ref, half):
        return ref.at[pl.ds(HALF * half, HALF)]

    def rows_of(half):
        return pl.ds(pl.multiple_of(half * HALF, HALF), HALF)

    def slot_of(other):
        return lax.rem(other + TEAM - member, TEAM)

    def exchange(kind, layer, half, outgoing, incoming):
        incoming[half, 0] = outgoing[half, member]
        for step in range(1, TEAM):
            peer = lax.rem(member + step, TEAM)
            pltpu.make_async_remote_copy(
                src_ref=outgoing.at[half, peer],
                dst_ref=incoming.at[half, TEAM - step],
                send_sem=a2a_send.at[kind, layer, half],
                recv_sem=a2a_recv.at[kind, layer, half],
                device_id=place(lax.div(peer, 2), side, zz, lax.rem(peer, 2)),
                device_id_type=MESH,
            ).start()

    def arrived(kind, layer, half, incoming):
        whole = incoming.at[half, pl.ds(1, TEAM - 1)]
        pltpu.make_async_copy(whole, whole, a2a_recv.at[kind, layer, half]).wait()

    def left(kind, layer, half, outgoing):
        whole = outgoing.at[half, pl.ds(1, TEAM - 1)]
        pltpu.make_async_copy(whole, whole, a2a_send.at[kind, layer, half]).wait()

    def project(layer, half):
        rows = rows_of(half)
        rounded = hidden[half].astype(BF16)
        hid_t[layer, :, rows] = rounded.T
        if layer == 1:
            left(0, 0, half, pack_out)
        queries = nn(rounded, wqkv[layer, :, 0:WIDTH]) * (DIM ** -0.5)
        queries_t = queries.T.astype(BF16)
        keys = nn(rounded, wqkv[layer, :, WIDTH : 2 * WIDTH])
        values = nn(rounded, wqkv[layer, :, 2 * WIDTH : 3 * WIDTH])
        for pair in range(RUNS // 2):
            k_pair = keys[:, 128 * pair : 128 * pair + 128]
            v_pair = values[:, 128 * pair : 128 * pair + 128]
            first = jnp.where(low, k_pair, pltpu.roll(v_pair, DIM, 1))
            other = jnp.where(low, pltpu.roll(k_pair, DIM, 1), v_pair)
            pack_out[half, pair, 0, 0:HALF, :] = first.astype(BF16)
            pack_out[half, pair, 1, 0:HALF, :] = other.astype(BF16)
        for head in range(RUNS):
            pack_out[half, head // 2, head % 2, HALF:, :] = queries_t[DIM * head : DIM * head + DIM, :]
        exchange(0, layer, half, pack_out, pack_in)

    def attend(layer, chunk):
        arrived(0, layer, chunk, pack_in)
        if layer == 1:
            left(1, 0, chunk, head_out)

        def one_head(head, carry):
            for other in range(TEAM):
                slot = slot_of(other)
                start = HALF * (TEAM * chunk + other)
                span = slice(start, start + HALF)
                block = pack_in[chunk, slot, head, 0:HALF, :]
                kv[layer, head, span, :] = block
                kv_t[layer, head, :, span] = block.T
                rq[layer, head, 0:DIM, span] = pack_in[chunk, slot, head, HALF:, :]
            for i in (2 * chunk, 2 * chunk + 1):
                columns = slice(TILE * i, TILE * i + TILE)
                query_tile = rq[layer, head, :, columns]
                count = TILE * (i + 1)
                scores = nn(kv[layer, head, 0:count, :], query_tile) + bias[TILE * TILES - count :, :]
                largest = jnp.max(scores, axis=0, keepdims=True)
                weight = jnp.exp(scores - largest)
                total = jnp.sum(weight, axis=0, keepdims=True)
                summed = nn(kv_t[layer, head, DIM:, 0:count], weight.astype(BF16))
                summed = summed / total
                o_t[layer, head, :, columns] = summed
                lse[layer, head, :, columns] = largest + jnp.log(total)
                rounded = summed.astype(BF16)
                for part in range(2):
                    head_out[chunk, 2 * (i - 2 * chunk) + part, head] = rounded[
                        :, HALF * part : HALF * part + HALF
                    ]
            return carry

        for head in range(OWN):
            one_head(head, 0)
        exchange(1, layer, chunk, head_out, o_in)

    def feed(layer, half):
        rows = rows_of(half)
        arrived(1, layer, half, o_in)
        for head in range(RUNS):
            attn_t[layer, DIM * head : DIM * head + DIM, rows] = o_in[half, slot_of(head // 2), head % 2]
        attn = attn_t[layer, :, rows].T
        grown = nn(attn, wout[layer])
        branch[layer, half] = grown
        middle = hidden[half] + alphas[layer, 0] * grown
        entered = middle.astype(BF16)
        ent_t[layer, :, rows] = entered.T
        total = jnp.zeros((HALF, WIDTH), F32)
        for step in range(FF // CUT):
            cut = slice(CUT * step, CUT * step + CUT)
            gate = nn(entered, wup[layer, :, cut]) + up_bias[layer : layer + 1, cut]
            bell = jnp.exp(gate * gate * -0.5)
            near = pl.reciprocal(1.0 + SLOPE_AT * jnp.abs(gate), approx=True)
            tail = jnp.full_like(gate, TAIL[5])
            for factor in TAIL[4::-1]:
                tail = tail * near + factor
            tail = bell * (tail * near)
            risen = jnp.where(gate > 0.0, 1.0 - tail, tail)
            slope[layer, half, :, cut] = risen + gate * bell * 0.3989422804014327
            active = (gate * risen).astype(BF16)
            act_t[layer, cut, rows] = active.T
            total = total + nn(active, wdown[layer, cut, :])
        total = total + down_bias[layer : layer + 1, :]
        second[layer, half] = total
        hidden[half] = middle + alphas[layer, 1] * total

    def total_of(values):
        return jnp.sum(jnp.sum(values, axis=0, keepdims=True), axis=1, keepdims=True)

    def feed_back(layer, half):
        rows = rows_of(half)
        start = grad[half]
        if layer == 0:
            dz[rows, :] = (alphas[layer, 1] * start).astype(BF16)
        scaled = dz[rows, :]
        alpha_second = total_of(start * second[layer, half])
        small[half, layer : layer + 1, FF : FF + WIDTH] = jnp.sum(scaled.astype(F32), axis=0, keepdims=True)
        middle = start
        for step in range(FF // CUT):
            cut = slice(CUT * step, CUT * step + CUT)
            gate = (nt(scaled, wdown[layer, cut, :]) * slope[layer, half, :, cut]).astype(BF16)
            du[rows, cut] = gate
            small[half, layer : layer + 1, cut] = jnp.sum(gate.astype(F32), axis=0, keepdims=True)
            middle = middle + nt(gate, wup[layer, :, cut])
        grad[half] = middle
        alpha_first = total_of(middle * branch[layer, half])
        column = lax.broadcasted_iota(jnp.int32, (1, 128), 1)
        small[half, layer : layer + 1, FF + WIDTH :] = jnp.where(
            column == 0, alpha_first, jnp.where(column == 1, alpha_second, 0.0)
        )
        mixed = (alphas[layer, 0] * middle).astype(BF16)
        da[layer, rows, :] = mixed
        spread = nt(wout[layer], mixed).astype(BF16)
        left(*((1, 1) if layer == 1 else (2, 1)), half, head_out)
        for head in range(RUNS):
            head_out[half, head // 2, head % 2] = spread[DIM * head : DIM * head + DIM, :]
        exchange(2, layer, half, head_out, do_in)

    def attend_back(layer, chunk):
        arrived(2, layer, chunk, do_in)
        left(*((0, 1) if layer == 1 else (3, 1)), chunk, pack_out)

        def one_head(head, carry):
            for other in range(TEAM):
                start = HALF * (TEAM * chunk + other)
                ro[head, DIM:, start : start + HALF] = do_in[chunk, slot_of(other), head]
            for i in (2 * chunk, 2 * chunk + 1):
                columns = slice(TILE * i, TILE * i + TILE)
                query_tile = rq[layer, head, :, columns]
                grad_tile = ro[head, :, columns]
                log_total = lse[layer, head, :, columns]
                delta = jnp.sum(
                    ro[head, DIM:, columns].astype(F32) * o_t[layer, head, :, columns],
                    axis=0,
                    keepdims=True,
                )
                count = TILE * (i + 1)
                keys = kv[layer, head, 0:count, :]
                weight = jnp.exp(nn(keys, query_tile) + bias[TILE * TILES - count :, :] - log_total)
                scored = (weight * (nn(keys, grad_tile) - delta)).astype(BF16)
                term = nt(scored, query_tile) + nt(weight.astype(BF16), grad_tile)
                if chunk == 1 and i == 2:
                    acc[head, 0:count, :] = term
                elif chunk == 1:
                    acc[head, 0 : count - TILE, :] += term[0 : count - TILE, :]
                    acc[head, count - TILE : count, :] = term[count - TILE :, :]
                else:
                    acc[head, 0:count, :] += term
                query_grad = nn(kv_t[layer, head, 0:DIM, 0:count], scored)
                dq_t[head, :, columns] = query_grad * (DIM ** -0.5)
            for other in range(TEAM):
                start = HALF * (TEAM * chunk + other)
                span = slice(start, start + HALF)
                pack_out[chunk, other, head, 0:HALF, :] = acc[head, span, :].astype(BF16)
                pack_out[chunk, other, head, HALF:, :] = dq_t[head, :, span].astype(BF16)
            return carry

        for head in range(OWN):
            one_head(head, 0)
        exchange(3, layer, chunk, pack_out, pack_in)

    def project_back(layer, half):
        rows = rows_of(half)
        arrived(3, layer, half, pack_in)
        turned = jnp.concatenate(
            [pack_in[half, slot_of(head // 2), head % 2, HALF:, :] for head in range(RUNS)], axis=0
        )
        dqkv[rows, 0:WIDTH] = turned.T
        for pair in range(RUNS // 2):
            first = pack_in[half, slot_of(pair), 0, 0:HALF, :].astype(F32)
            other = pack_in[half, slot_of(pair), 1, 0:HALF, :].astype(F32)
            k_pair = jnp.where(low, first, pltpu.roll(other, DIM, 1))
            v_pair = jnp.where(low, pltpu.roll(first, DIM, 1), other)
            dqkv[rows, WIDTH + 128 * pair : WIDTH + 128 * pair + 128] = k_pair.astype(BF16)
            dqkv[rows, 2 * WIDTH + 128 * pair : 2 * WIDTH + 128 * pair + 128] = v_pair.astype(BF16)
        grad[half] = grad[half] + nt(dqkv[rows, :], wqkv[layer])

    def scatter_rows(layer, result, first_row):
        for run in range(RUNS):
            for quarter in range(4):
                parts[layer, quarter, run // 2, run % 2, first_row : first_row + DIM, :] = result[
                    DIM * run : DIM * run + DIM, 128 * quarter : 128 * quarter + 128
                ].astype(BF16)

    def up_grads(layer):
        for step in range(FF // CUT):
            cut = slice(CUT * step, CUT * step + CUT)
            scatter_rows(layer, nn(ent_t[layer], du[:, cut]), UP + DIM * step)

    def down_grads(layer):
        for run in range(RUNS):
            result = nn(act_t[layer, TILE * run : TILE * run + TILE, :], dz[...])
            for quarter in range(4):
                parts[layer, quarter, run // 2, run % 2, DOWN : DOWN + PART, :] = result[
                    :, 128 * quarter : 128 * quarter + 128
                ].astype(BF16)

    def late_grads(layer):
        scatter_rows(layer, nn(attn_t[layer], da[layer]), LATE + 192)
        for step in range(3):
            scatter_rows(
                layer, nn(hid_t[layer], dqkv[:, WIDTH * step : WIDTH * step + WIDTH]), LATE + DIM * step
            )

    def remote(source, target, send, recv, peer):
        return pltpu.make_async_remote_copy(
            src_ref=source,
            dst_ref=target,
            send_sem=send,
            recv_sem=recv,
            device_id=peer,
            device_id_type=MESH,
        )

    def credit(semaphore, peer):
        pl.semaphore_signal(semaphore, inc=1, device_id=peer, device_id_type=MESH)

    def rows_in(part, order):
        return pl.ds(part + ORDERS[order][0], ORDERS[order][1])

    def core_copy(layer, part, across):
        rows = pl.ds(part, PART)
        which = (layer, part // PART, across)
        return remote(
            parts.at[layer, 2 * across + 1 - core, :, :, rows],
            core_in.at[across, :, :, rows],
            core_send.at[which],
            core_recv.at[which],
            core_peer,
        )

    def x_copy(layer, part, order):
        rows = rows_in(part, order)
        which = (layer, part // PART, order)
        ends = (x_send.at[which], x_recv.at[which], x_peer)
        if order == 0:
            return remote(parts.at[layer, far_side, :, :, rows], x_in.at[:, :, rows], *ends)
        return remote(parts.at[layer, far_side, :, yy, rows], x_in.at[:, 0, rows], *ends)

    def y_copy(layer, part, order, across):
        rows = rows_in(part, order)
        which = (layer, part // PART, order, across)
        ends = (y_send.at[which], y_recv.at[which], y_peer)
        quarter = grp if order == 0 else 2 * across + core
        return remote(parts.at[layer, quarter, :, 1 - yy, rows], y_in.at[across, :, rows], *ends)

    def z_copy(layer, part, order, step):
        rows = rows_in(part, order)
        peer = lax.rem(zz + step, 4)
        return remote(
            parts.at[layer, grp, peer, yy, rows],
            z_in.at[layer, 4 - step, rows],
            z_send.at[layer, part // PART, order, step],
            z_recv.at[layer, part // PART, order, 4 - step],
            place(core, side, peer, yy),
        )

    def third_z_copy(layer, part, across, step):
        peer = lax.rem(zz + step, 4)
        which = (layer, part // PART, across)
        return remote(
            parts.at[layer, 2 * across + core, peer, :, rows_in(part, 2)],
            third_z.at[layer, part // PART, across, 4 - step],
            tz_send.at[(*which, step)],
            tz_recv.at[(*which, 4 - step)],
            place(core, side, peer, yy),
        )

    def third_x_copy(layer, part):
        which = (layer, part // PART)
        return remote(
            parts.at[layer, far_side, zz, :, rows_in(part, 2)],
            third_x.at[which],
            tx_send.at[which],
            tx_recv.at[which],
            x_peer,
        )

    def third_y_copy(layer, part):
        which = (layer, part // PART)
        return remote(
            parts.at[layer, grp, zz, 1 - yy, rows_in(part, 2)],
            third_y.at[which],
            ty_send.at[which],
            ty_recv.at[which],
            y_peer,
        )

    def final_copy(layer, part, which):
        rows = pl.ds(part, PART)
        quarter = far_side if which == 2 else grp
        block = final.at[layer, quarter, rows]
        return remote(
            block,
            block,
            fin_send.at[layer, part // PART, which],
            fin_recv.at[layer, part // PART, which],
            x_peer if which == 0 else core_peer,
        )

    def core_start(layer, part):
        if layer == 0:
            pl.semaphore_wait(core_free.at[part // PART], 1)
        for across in range(2):
            core_copy(layer, part, across).start()

    def core_done(layer, part):
        rows = pl.ds(part, PART)
        for across in range(2):
            core_copy(layer, part, across).wait()
        if layer == 0:
            pl.semaphore_wait(x_free.at[part // PART, 0], 1)
            pl.semaphore_wait(y_free.at[part // PART, 1], 1)
        for across in (1 - side, side):
            parts[layer, 2 * across + core, :, :, rows, :] += core_in[across, :, :, rows, :]
            if across is not side:
                x_copy(layer, part, 0).start()
            y_copy(layer, part, 1, across).start()
            for step in range(1, 4):
                third_z_copy(layer, part, across, step).start()
        if layer == 1:
            credit(core_free.at[part // PART], core_peer)

    def first_done(layer, part):
        rows = rows_in(part, 1)
        for across in (1 - side, side):
            y_copy(layer, part, 1, across).wait()
        if layer == 0:
            pl.semaphore_wait(x_free.at[part // PART, 1], 1)
            pl.semaphore_wait(y_free.at[part // PART, 0], 1)
        for across in (1 - side, side):
            parts[layer, 2 * across + core, :, yy, rows, :] += y_in[across, :, rows, :]
            if across is not side:
                x_copy(layer, part, 1).start()
        if layer == 1:
            credit(y_free.at[part // PART, 1], y_peer)

        rows = rows_in(part, 0)
        x_copy(layer, part, 0).wait()
        for y in (1 - yy, yy):
            parts[layer, grp, :, y, rows, :] += x_in[:, y, rows, :]
            if y is not yy:
                y_copy(layer, part, 0, 0).start()
        if layer == 1:
            credit(x_free.at[part // PART, 0], x_peer)

        rows = rows_in(part, 2)
        for across in (1 - side, side):
            for step in range(1, 4):
                third_z_copy(layer, part, across, step).wait()
            total = parts[layer, 2 * across + core, zz, :, rows, :].astype(F32)
            for slot in range(1, 4):
                total = total + third_z[layer, part // PART, across, slot].astype(F32)
            parts[layer, 2 * across + core, zz, :, rows, :] = total.astype(BF16)
            if across is not side:
                third_x_copy(layer, part).start()

    def second_done(layer, part):
        for order in (1, 0):
            rows = rows_in(part, order)
            if order == 0:
                y_copy(layer, part, 0, 0).wait()
                parts[layer, grp, :, yy, rows, :] += y_in[0, :, rows, :]
            else:
                x_copy(layer, part, 1).wait()
                parts[layer, grp, :, yy, rows, :] += x_in[:, 0, rows, :]
            for step in range(1, 4):
                z_copy(layer, part, order, step).start()
            if layer == 1:
                if order == 0:
                    credit(y_free.at[part // PART, 0], y_peer)
                else:
                    credit(x_free.at[part // PART, 1], x_peer)
        rows = rows_in(part, 2)
        third_x_copy(layer, part).wait()
        for y in (1 - yy, yy):
            parts[layer, grp, zz, y, rows, :] += third_x[layer, part // PART, y]
            if y is not yy:
                third_y_copy(layer, part).start()

    def z_done(layer, part):
        for order in (1, 0):
            for step in range(1, 4):
                z_copy(layer, part, order, step).wait()
        rows = pl.ds(part, ORDERS[2][0])
        total = parts[layer, grp, zz, yy, rows, :].astype(F32)
        for slot in range(1, 4):
            total = total + z_in[layer, slot, rows, :].astype(F32)
        final[layer, grp, rows, :] = total.astype(BF16)
        rows = rows_in(part, 2)
        third_y_copy(layer, part).wait()
        final[layer, grp, rows, :] = parts[layer, grp, zz, yy, rows, :] + third_y[layer, part // PART]
        for which in range(2):
            final_copy(layer, part, which).start()

    def final_pass(layer, part):
        final_copy(layer, part, 0).wait()
        final_copy(layer, part, 2).start()

    def final_out(layer, part):
        rows = pl.ds(part, PART)
        return pltpu.make_async_copy(
            final.at[layer, :, rows], final_hbm.at[layer, :, rows], out_sem.at[layer, part // PART]
        )

    def final_done(layer, part):
        for which in range(1, 3):
            final_copy(layer, part, which).wait()
        final_out(layer, part).start()

    def small_copy(stage):
        peer = (core_peer, x_peer, y_peer)[stage]
        return remote(
            small_sum.at[stage], small_in.at[stage], small_send.at[stage], small_recv.at[stage], peer
        )

    def small_z_copy(step):
        return remote(
            small_z.at[zz],
            small_z.at[zz],
            small_send.at[2 + step],
            small_recv.at[2 + step],
            place(core, side, lax.rem(zz + step, 4), yy),
        )

    def small_start():
        small_sum[0] = small[0] + small[1]
        small_copy(0).start()

    def small_next(stage):
        small_copy(stage).wait()
        total = small_sum[stage] + small_in[stage]
        if stage < 2:
            small_sum[stage + 1] = total
            small_copy(stage + 1).start()
        else:
            small_z[zz] = total
            for step in range(1, 4):
                small_z_copy(step).start()

    def small_done():
        for step in range(1, 4):
            small_z_copy(step).wait()
        small_sum[0] = (small_z[0] + small_z[1]) + (small_z[2] + small_z[3])
        small_final[:, 0:256] = small_sum[0, :, pl.ds(pl.multiple_of(blk * 256, 256), 256)]
        pair = small_sum[0, :, pl.ds(pl.multiple_of(FF + 128 * zz, 128), 128)]
        small_final[:, 256:384] = jnp.where(yy == 1, pltpu.roll(pair, DIM, 1), pair)
        small_final[:, 384:512] = small_sum[0, :, FF + WIDTH :]

    def halves(*phases, backward=False):
        def both(step, carry):
            for phase in phases:
                phase(1 - step if backward else step)
            return carry

        lax.fori_loop(0, 2, both, 0)

    def begin(half):
        move_arrived(0, half, tok_in)
        hidden[half] = tok_in[half].astype(F32)

    def finish(half):
        back_out[0, half] = hidden[half].astype(BF16)
        to_owner(3, half, back_out.at[0, half], out_in)

    def turn_round(layer, half):
        move_arrived(2, half, cot_in)
        grad[half] = cot_in[half].astype(F32)
        dz[rows_of(half), :] = (alphas[layer, 1] * grad[half]).astype(BF16)

    def hand_back(half):
        back_out[1, half] = grad[half].astype(BF16)
        to_owner(4, half, back_out.at[1, half], grad_in)

    pl.semaphore_wait(barrier, 10)
    for half in range(2):
        to_team(0, half, half_of(tokens, half), tok_in)
    for half in range(2):
        to_team(1, half, flag_out, flag_in)
    for half in range(2):
        to_team(2, half, half_of(cotangent, half), cot_in)
    weight_copies[0, 0].wait()
    halves(begin, functools.partial(project, 0))

    move_arrived(1, 0, flag_in)
    move_arrived(1, 1, flag_in)
    border = jnp.concatenate([flag_in[0, 0:1, :]] * 2, axis=1) - (HALF * lax.div(zz, 2)).astype(F32)
    key_row = lax.broadcasted_iota(jnp.int32, (TILE, TILE), 0)
    query_col = lax.broadcasted_iota(jnp.int32, (TILE, TILE), 1)
    later = key_row > query_col
    key_sub = lax.rem(key_row, HALF).astype(F32) >= border
    query_sub = lax.rem(query_col, HALF).astype(F32) >= border
    apart = jnp.logical_xor(key_sub, query_sub)
    for tile in range(TILES - 1):
        bias[TILE * tile : TILE * tile + TILE, :] = jnp.where(apart, NEGATIVE, 0.0)
    bias[TILE * (TILES - 1) :, :] = jnp.where(jnp.logical_or(later, apart), NEGATIVE, 0.0)

    for number in range(1, 4):
        weight_copies[0, number].wait()
    attend(0, 0)
    attend(0, 1)
    weight_copies[1, 0].wait()
    halves(functools.partial(feed, 0), functools.partial(project, 1))
    for number in range(1, 4):
        weight_copies[1, number].wait()
    attend(1, 0)
    attend(1, 1)
    halves(functools.partial(feed, 1), finish)

    halves(functools.partial(turn_round, 1))
    down_grads(1)
    core_start(1, DOWN)
    halves(functools.partial(feed_back, 1), backward=True)
    core_done(1, DOWN)
    up_grads(1)
    core_start(1, UP)
    attend_back(1, 1)
    core_done(1, UP)
    attend_back(1, 0)

    def once(half):
        @pl.when(half == 1)
        def _():
            first_done(1, DOWN)

    halves(functools.partial(project_back, 1), functools.partial(feed_back, 0), once, backward=True)
    up_grads(0)
    core_start(0, UP)
    small_start()
    first_done(1, UP)
    second_done(1, DOWN)
    attend_back(0, 1)
    core_done(0, UP)
    late_grads(1)
    core_start(1, LATE)
    down_grads(0)
    core_start(0, DOWN)
    small_next(0)
    attend_back(0, 0)
    core_done(1, LATE)
    core_done(0, DOWN)
    small_next(1)
    second_done(1, UP)
    z_done(1, DOWN)

    def twice(half):
        @pl.when(half == 1)
        def _():
            first_done(0, UP)
            first_done(1, LATE)

    halves(functools.partial(project_back, 0), hand_back, twice, backward=True)
    late_grads(0)
    core_start(0, LATE)
    small_next(2)
    first_done(0, DOWN)
    z_done(1, UP)
    second_done(0, UP)
    second_done(1, LATE)
    core_done(0, LATE)
    final_pass(1, UP)
    final_pass(1, DOWN)
    small_done()
    second_done(0, DOWN)
    first_done(0, LATE)
    z_done(0, UP)
    z_done(1, LATE)
    second_done(0, LATE)
    final_done(1, UP)
    final_done(1, DOWN)
    results = []
    for half in range(2):
        rows = pl.ds(HALF * half, HALF)
        move_arrived(3, half, out_in)
        results.append(pltpu.make_async_copy(out_in.at[half], output_hbm.at[rows], out_sem.at[2, half]))
        move_arrived(4, half, grad_in)
        results.append(pltpu.make_async_copy(grad_in.at[half], input_grad_hbm.at[rows], out_sem.at[3, half]))
    for copy in results:
        copy.start()
    z_done(0, DOWN)
    final_pass(1, LATE)
    final_pass(0, UP)
    z_done(0, LATE)
    final_pass(0, DOWN)
    final_done(1, LATE)
    final_done(0, UP)
    final_pass(0, LATE)
    final_done(0, DOWN)
    final_done(0, LATE)

    for half in range(2):
        left(2, 0, half, head_out)
        left(3, 0, half, pack_out)
        to_team_left(0, half, half_of(tokens, half))
        to_team_left(1, half, flag_out)
        to_team_left(2, half, half_of(cotangent, half))
        to_owner_left(3, half, back_out.at[0, half])
        to_owner_left(4, half, back_out.at[1, half])
    for copy in results:
        copy.wait()
    for layer in range(LAYERS):
        for part in (UP, DOWN, LATE):
            final_out(layer, part).wait()


def results_kernel(
    final_hbm, out_hbm, grad_hbm, small,
    output, input_grad, qkv_grad, out_grad, up_grad, up_bias_grad, down_grad, down_bias_grad, alpha_grad,
    final, grad_block, out_block, sem,
):
    moves = [
        pltpu.make_async_copy(final_hbm.at[1], final.at[1], sem.at[0]),
        pltpu.make_async_copy(final_hbm.at[0], final.at[0], sem.at[1]),
        pltpu.make_async_copy(grad_hbm, grad_block, sem.at[2]),
        pltpu.make_async_copy(out_hbm, out_block, sem.at[3]),
    ]
    for move in moves:
        move.start()
    up_bias_grad[...] = small[:, 0:256]
    down_bias_grad[...] = small[:, 256 : 256 + DIM]
    alpha_grad[...] = small[:, 384:386]
    for layer in (1, 0):
        moves[1 - layer].wait()
        for quarter in range(4):

            def block(first, count):
                return final[layer, quarter, first : first + count, :].astype(F32)

            def columns(step):
                return slice(WIDTH * step + 128 * quarter, WIDTH * step + 128 * quarter + 128)

            for step in range(3):
                qkv_grad[layer, :, columns(step)] = block(DIM * step, DIM)
            out_grad[layer, :, columns(0)] = block(192, DIM)
            for step in range(4):
                up_grad[layer, :, columns(step)] = block(UP + DIM * step, DIM)
            down_grad[layer, :, columns(0)] = block(DOWN, PART)
    moves[2].wait()
    input_grad[...] = grad_block[...].astype(F32)
    moves[3].wait()
    output[...] = out_block[...]


def fast_body(
    tokens, seq_len, qkv_weight, out_weight, up_weight, up_bias, down_weight, down_bias, alphas, cotangent
):
    whole = pl.BlockSpec(memory_space=pltpu.VMEM)
    scalar = pl.BlockSpec(memory_space=pltpu.SMEM)
    far = pl.BlockSpec(memory_space=pl.ANY)
    shape = jax.ShapeDtypeStruct
    rows = HALF * RUNS

    def vmem(*dims):
        return pltpu.VMEM(dims, BF16)

    def wide(*dims):
        return pltpu.VMEM(dims, F32)

    dma = pltpu.SemaphoreType.DMA
    final, out_block, grad_block, small = pl.pallas_call(
        layers_kernel,
        out_shape=(
            shape((LAYERS, 4, CHUNK, 128), BF16),
            shape((2 * HALF, WIDTH), BF16),
            shape((2 * HALF, WIDTH), BF16),
            shape((LAYERS, WIDTH), F32),
        ),
        in_specs=[whole, scalar, scalar, whole, whole, whole, far, far, far, far],
        out_specs=(far, far, far, whole),
        scratch_shapes=[
            vmem(LAYERS, WIDTH, 3 * WIDTH),
            vmem(LAYERS, WIDTH, WIDTH),
            vmem(LAYERS, WIDTH, FF),
            vmem(LAYERS, FF, WIDTH),
            vmem(2, HALF, WIDTH),
            vmem(2, HALF, WIDTH),
            wide(8, 128),
            wide(2, 8, 128),
            vmem(2, 2, HALF, WIDTH),
            vmem(2, HALF, WIDTH),
            vmem(2, HALF, WIDTH),
            wide(2, HALF, WIDTH),
            wide(2, HALF, WIDTH),
            vmem(LAYERS, WIDTH, 2 * HALF),
            vmem(LAYERS, WIDTH, 2 * HALF),
            vmem(LAYERS, WIDTH, 2 * HALF),
            vmem(LAYERS, FF, 2 * HALF),
            wide(LAYERS, 2, HALF, WIDTH),
            wide(LAYERS, 2, HALF, FF),
            wide(LAYERS, 2, HALF, WIDTH),
            vmem(2 * HALF, WIDTH),
            vmem(2 * HALF, FF),
            vmem(LAYERS, 2 * HALF, WIDTH),
            vmem(2 * HALF, 3 * WIDTH),
            vmem(2, TEAM, OWN, PACK, 128),
            vmem(2, TEAM, OWN, DIM, 128),
            vmem(2, TEAM, OWN, PACK, 128),
            vmem(2, TEAM, OWN, DIM, 128),
            vmem(2, TEAM, OWN, DIM, 128),
            vmem(LAYERS, OWN, rows, 128),
            vmem(LAYERS, OWN, 128, rows),
            vmem(LAYERS, OWN, 128, rows),
            vmem(OWN, 128, rows),
            wide(LAYERS, OWN, DIM, rows),
            wide(LAYERS, OWN, 1, rows),
            wide(OWN, rows, 128),
            wide(OWN, DIM, rows),
            wide(rows, TILE),
            vmem(LAYERS, 4, 4, 2, CHUNK, 128),
            vmem(2, 4, 2, CHUNK, 128),
            vmem(4, 2, CHUNK, 128),
            vmem(2, 4, CHUNK, 128),
            vmem(LAYERS, 4, CHUNK, 128),
            vmem(LAYERS, 3, 2, 4, 2, THIRD, 128),
            vmem(LAYERS, 3, 2, THIRD, 128),
            vmem(LAYERS, 3, THIRD, 128),
            vmem(LAYERS, 4, CHUNK, 128),
            wide(2, LAYERS, SMALL),
            wide(3, LAYERS, SMALL),
            wide(4, LAYERS, SMALL),
            wide(3, LAYERS, SMALL),
            dma((LAYERS, 4)),
            dma((5, 2)),
            dma((5, 2)),
            dma((4, LAYERS, 2)),
            dma((4, LAYERS, 2)),
            dma((LAYERS, 3, 2)),
            dma((LAYERS, 3, 2)),
            dma((LAYERS, 3, 2)),
            dma((LAYERS, 3, 2)),
            dma((LAYERS, 3, 2, 2)),
            dma((LAYERS, 3, 2, 2)),
            dma((LAYERS, 3, 2, 4)),
            dma((LAYERS, 3, 2, 4)),
            dma((LAYERS, 3, 2, 4)),
            dma((LAYERS, 3, 2, 4)),
            dma((LAYERS, 3)),
            dma((LAYERS, 3)),
            dma((LAYERS, 3)),
            dma((LAYERS, 3)),
            dma((LAYERS, 3, 3)),
            dma((LAYERS, 3, 3)),
            dma((6,)),
            dma((6,)),
            dma((4, 3)),
            pltpu.SemaphoreType.REGULAR((3,)),
            pltpu.SemaphoreType.REGULAR((3, 2)),
            pltpu.SemaphoreType.REGULAR((3, 2)),
        ],
        compiler_params=pltpu.CompilerParams(
            collective_id=0, has_side_effects=True, vmem_limit_bytes=63 * 1024 * 1024
        ),
        name="layers",
    )(
        tokens, seq_len, alphas, up_bias, down_bias, cotangent,
        qkv_weight, out_weight, up_weight, down_weight,
    )
    return tuple(
        pl.pallas_call(
            results_kernel,
            out_shape=(
                shape((2 * HALF, WIDTH), BF16),
                shape((2 * HALF, WIDTH), F32),
                shape((LAYERS, DIM, 3 * WIDTH), F32),
                shape((LAYERS, DIM, WIDTH), F32),
                shape((LAYERS, DIM, FF), F32),
                shape((LAYERS, FF // RUNS), F32),
                shape((LAYERS, FF // RUNS, WIDTH), F32),
                shape((LAYERS, DIM), F32),
                shape((LAYERS, 2), F32),
            ),
            in_specs=[far, far, far, whole],
            out_specs=(whole,) * 9,
            scratch_shapes=[
                vmem(LAYERS, 4, CHUNK, 128), vmem(2 * HALF, WIDTH), vmem(2 * HALF, WIDTH), dma((4,))
            ],
            compiler_params=pltpu.CompilerParams(vmem_limit_bytes=60 * 1024 * 1024),
            name="results",
        )(final, out_block, grad_block, small)
    )


def layout(seq_len, local_count, cycle_size):
    piece_rows = seq_len[0] // cycle_size
    end_rows = jnp.cumsum(piece_rows)
    start_rows = end_rows - piece_rows
    local_rows = jnp.arange(local_count, dtype=jnp.int32)
    segment = jnp.sum((local_rows[:, None] >= end_rows[None, :]).astype(jnp.int32), axis=1)
    picked = segment[:, None] == jnp.arange(seq_len.shape[1], dtype=jnp.int32)[None, :]
    offset = local_rows - jnp.sum(jnp.where(picked, start_rows[None, :], 0), axis=1)
    span_rows = jnp.sum(jnp.where(picked, piece_rows[None, :], 0), axis=1)
    return (segment, offset, span_rows)


def gelu_exact(values):
    return jax.nn.gelu(values, approximate=False)


def key_block(whole, geometry, block_index, head_count):
    query_seg, query_pos, seg_all, pos_all, block_rows, score_scale = geometry
    first_row = block_index * block_rows
    key_piece = lax.dynamic_slice_in_dim(whole, first_row, block_rows, 0)
    key_seg = lax.dynamic_slice_in_dim(seg_all, first_row, block_rows, 0)
    key_pos = lax.dynamic_slice_in_dim(pos_all, first_row, block_rows, 0)
    half_width = key_piece.shape[1] // 2
    keys_part = key_piece[:, :half_width].reshape(block_rows, head_count, -1)
    values_part = key_piece[:, half_width:].reshape(block_rows, head_count, -1)
    return (keys_part, values_part, key_seg, key_pos)


def block_scores(queries, keys_part, key_seg, key_pos, geometry):
    query_seg, query_pos, seg_all, pos_all, block_rows, score_scale = geometry
    scores = (
        jnp.einsum("qhd,khd->hqk", queries, keys_part, preferred_element_type=jnp.float32)
        * score_scale
    )
    allowed = (query_seg[:, None] == key_seg[None, :]) & (key_pos[None, :] <= query_pos[:, None])
    return (scores, allowed[None])


def attend(queries, whole, geometry):
    row_count, head_count, head_dim = queries.shape
    block_count = whole.shape[0] // geometry[4]

    def statistics(running, block_index):
        largest, totals = running
        keys_part, values_part, key_seg, key_pos = key_block(
            whole, geometry, block_index, head_count
        )
        scores, allowed = block_scores(queries, keys_part, key_seg, key_pos, geometry)
        newest = jnp.maximum(largest, jnp.max(jnp.where(allowed, scores, NEGATIVE), axis=2))
        weights = jnp.where(allowed, jnp.exp(scores - newest[:, :, None]), 0.0)
        totals = totals * jnp.exp(largest - newest) + jnp.sum(weights, axis=2)
        return ((newest, totals), None)

    initial = (
        jnp.full((head_count, row_count), NEGATIVE, jnp.float32),
        jnp.zeros((head_count, row_count), jnp.float32),
    )
    (largest, totals), unused = lax.scan(statistics, initial, jnp.arange(block_count))
    log_total = largest + jnp.log(totals)

    def weighted(output_sum, block_index):
        keys_part, values_part, key_seg, key_pos = key_block(
            whole, geometry, block_index, head_count
        )
        scores, allowed = block_scores(queries, keys_part, key_seg, key_pos, geometry)
        probs = jnp.where(allowed, jnp.exp(scores - log_total[:, :, None]), 0.0).astype(
            jnp.bfloat16
        )
        output_sum = output_sum + jnp.einsum(
            "hqk,khd->qhd", probs, values_part, preferred_element_type=jnp.float32
        )
        return (output_sum, None)

    output_sum, unused = lax.scan(
        weighted, jnp.zeros((row_count, head_count, head_dim), jnp.float32), jnp.arange(block_count)
    )
    return (output_sum, log_total)


def attend_back(queries, whole, log_total, delta_sum, grad_heads, geometry):
    row_count, head_count, head_dim = queries.shape
    block_rows = geometry[4]
    score_scale = geometry[5]
    block_count = whole.shape[0] // block_rows

    def gradients(query_grad, block_index):
        keys_part, values_part, key_seg, key_pos = key_block(
            whole, geometry, block_index, head_count
        )
        scores, allowed = block_scores(queries, keys_part, key_seg, key_pos, geometry)
        probs = jnp.where(allowed, jnp.exp(scores - log_total[:, :, None]), 0.0)
        grad_probs = jnp.einsum(
            "qhd,khd->hqk", grad_heads, values_part, preferred_element_type=jnp.float32
        )
        grad_scores = (probs * (grad_probs - delta_sum[:, :, None])).astype(jnp.bfloat16)
        query_grad = (
            query_grad
            + jnp.einsum("hqk,khd->qhd", grad_scores, keys_part, preferred_element_type=jnp.float32)
            * score_scale
        )
        key_grad = (
            jnp.einsum("hqk,qhd->khd", grad_scores, queries, preferred_element_type=jnp.float32)
            * score_scale
        )
        value_grad = jnp.einsum(
            "hqk,qhd->khd",
            probs.astype(jnp.bfloat16),
            grad_heads,
            preferred_element_type=jnp.float32,
        )
        joined = jnp.concatenate(
            [key_grad.reshape(block_rows, -1), value_grad.reshape(block_rows, -1)], axis=1
        )
        return (query_grad, joined)

    query_grad, stacked = lax.scan(
        gradients,
        jnp.zeros((row_count, head_count, head_dim), jnp.float32),
        jnp.arange(block_count),
    )
    return (query_grad, stacked.reshape(whole.shape[0], -1))


def layer_forward(hidden, layer_index, weights, geometry):
    qkv_weight, out_weight, up_weight, up_bias, down_weight, down_bias, alphas = weights
    row_count, model_width = hidden.shape
    projection = qkv_weight[layer_index]
    rounded = hidden.astype(jnp.bfloat16)
    queries = (
        jnp.dot(rounded, projection[:, :model_width], preferred_element_type=jnp.float32)
        .astype(jnp.bfloat16)
        .reshape(row_count, HEADS, -1)
    )
    key_value = jnp.dot(
        rounded, projection[:, model_width:], preferred_element_type=jnp.float32
    ).astype(jnp.bfloat16)
    whole = lax.all_gather(key_value, "blk", axis=0, tiled=True)
    heads_out, log_total = attend(queries, whole, geometry)
    heads_rounded = heads_out.reshape(row_count, model_width).astype(jnp.bfloat16)
    branch = jnp.dot(heads_rounded, out_weight[layer_index], preferred_element_type=jnp.float32)
    alpha_pair = alphas[layer_index]
    middle = hidden + alpha_pair[0] * branch
    entered = middle.astype(jnp.bfloat16)
    gate_pre = (
        jnp.dot(entered, up_weight[layer_index], preferred_element_type=jnp.float32)
        + up_bias[layer_index]
    )
    activated = gelu_exact(gate_pre).astype(jnp.bfloat16)
    second = (
        jnp.dot(activated, down_weight[layer_index], preferred_element_type=jnp.float32)
        + down_bias[layer_index]
    )
    result = middle + alpha_pair[1] * second
    saved = (
        rounded,
        queries,
        key_value,
        whole,
        heads_out,
        heads_rounded,
        log_total,
        branch,
        entered,
        gate_pre,
        activated,
        second,
    )
    return (result, saved)


def layer_backward(grad_hidden, saved, layer_index, weights, geometry):
    qkv_weight, out_weight, up_weight, up_bias, down_weight, down_bias, alphas = weights
    (
        rounded,
        queries,
        key_value,
        saved_whole,
        heads_out,
        heads_rounded,
        log_total,
        branch,
        entered,
        gate_pre,
        activated,
        second,
    ) = saved
    row_count = grad_hidden.shape[0]
    alpha_pair = alphas[layer_index]
    grad_second = (alpha_pair[1] * grad_hidden).astype(jnp.bfloat16)
    alpha_second = jnp.sum(grad_hidden * second)
    bias_down = jnp.sum(grad_second.astype(jnp.float32), axis=0)
    grad_down = jnp.einsum("tf,td->fd", activated, grad_second, preferred_element_type=jnp.float32)
    grad_act = jnp.einsum(
        "td,fd->tf", grad_second, down_weight[layer_index], preferred_element_type=jnp.float32
    )
    unused, gelu_pull = jax.vjp(gelu_exact, gate_pre)
    grad_gate = gelu_pull(grad_act)[0].astype(jnp.bfloat16)
    bias_up = jnp.sum(grad_gate.astype(jnp.float32), axis=0)
    grad_up = jnp.einsum("td,tf->df", entered, grad_gate, preferred_element_type=jnp.float32)
    grad_middle = grad_hidden + jnp.einsum(
        "tf,df->td", grad_gate, up_weight[layer_index], preferred_element_type=jnp.float32
    )
    grad_branch = (alpha_pair[0] * grad_middle).astype(jnp.bfloat16)
    alpha_first = jnp.sum(grad_middle * branch)
    grad_proj_out = jnp.einsum(
        "te,td->ed", heads_rounded, grad_branch, preferred_element_type=jnp.float32
    )
    grad_heads = (
        jnp.einsum(
            "td,ed->te", grad_branch, out_weight[layer_index], preferred_element_type=jnp.float32
        )
        .astype(jnp.bfloat16)
        .reshape(queries.shape)
    )
    delta_sum = jnp.sum(grad_heads.astype(jnp.float32) * heads_out, axis=2).T
    whole = lax.all_gather(key_value, "blk", axis=0, tiled=True)
    query_grad, key_terms = attend_back(queries, whole, log_total, delta_sum, grad_heads, geometry)
    key_grads = lax.psum_scatter(
        key_terms.astype(jnp.bfloat16), "blk", scatter_dimension=0, tiled=True
    )
    grad_proj = jnp.concatenate(
        [query_grad.reshape(row_count, -1).astype(jnp.bfloat16), key_grads], axis=1
    )
    grad_qkv = jnp.einsum("td,te->de", rounded, grad_proj, preferred_element_type=jnp.float32)
    grad_input = grad_middle + jnp.einsum(
        "te,de->td", grad_proj, qkv_weight[layer_index], preferred_element_type=jnp.float32
    )
    layer_grads = (
        grad_qkv,
        grad_proj_out,
        grad_up,
        bias_up,
        grad_down,
        bias_down,
        jnp.stack([alpha_first, alpha_second]),
    )
    return (grad_input, layer_grads)


def reduce_all(layer_results, cycle_size):
    stacked = [
        jnp.stack([layer_entry[member] for layer_entry in layer_results], axis=0)
        for member in range(6)
    ]
    alpha_tiles = jnp.stack(
        [jnp.tile(layer_entry[6], cycle_size) for layer_entry in layer_results], axis=0
    )
    shares = (
        lax.psum_scatter(
            stacked[0].astype(jnp.bfloat16), "blk", scatter_dimension=1, tiled=True
        ).astype(jnp.float32),
        lax.psum_scatter(
            stacked[1].astype(jnp.bfloat16), "blk", scatter_dimension=1, tiled=True
        ).astype(jnp.float32),
        lax.psum_scatter(
            stacked[2].astype(jnp.bfloat16), "blk", scatter_dimension=1, tiled=True
        ).astype(jnp.float32),
        lax.psum_scatter(
            stacked[3].astype(jnp.bfloat16), "blk", scatter_dimension=1, tiled=True
        ).astype(jnp.float32),
        lax.psum_scatter(
            stacked[4].astype(jnp.bfloat16), "blk", scatter_dimension=1, tiled=True
        ).astype(jnp.float32),
        lax.psum_scatter(
            stacked[5].astype(jnp.bfloat16), "blk", scatter_dimension=1, tiled=True
        ).astype(jnp.float32),
        lax.psum_scatter(
            alpha_tiles.astype(jnp.bfloat16), "blk", scatter_dimension=1, tiled=True
        ).astype(jnp.float32),
    )
    return (
        lax.psum(shares[0].astype(jnp.bfloat16), "grp").astype(jnp.float32),
        lax.psum(shares[1].astype(jnp.bfloat16), "grp").astype(jnp.float32),
        lax.psum(shares[2].astype(jnp.bfloat16), "grp").astype(jnp.float32),
        lax.psum(shares[3].astype(jnp.bfloat16), "grp").astype(jnp.float32),
        lax.psum(shares[4].astype(jnp.bfloat16), "grp").astype(jnp.float32),
        lax.psum(shares[5].astype(jnp.bfloat16), "grp").astype(jnp.float32),
        lax.psum(shares[6].astype(jnp.bfloat16), "grp").astype(jnp.float32),
    )


def body(
    tokens,
    seq_len,
    qkv_weight,
    out_weight,
    up_weight,
    up_bias,
    down_weight,
    down_bias,
    alphas,
    cotangent,
):
    row_count, model_width = tokens.shape
    cycle_size = lax.axis_size("blk")
    cycle_place = lax.axis_index("blk")
    head_dim = model_width // HEADS
    total_rows = cycle_size * row_count
    block_rows = min(max(row_count, 512), total_rows)
    segment, offset, span_rows = layout(seq_len, row_count, cycle_size)
    query_pos = cycle_place * span_rows + offset
    seg_all = jnp.tile(segment, cycle_size)
    pos_all = jnp.repeat(jnp.arange(cycle_size, dtype=jnp.int32), row_count) * jnp.tile(
        span_rows, cycle_size
    ) + jnp.tile(offset, cycle_size)
    geometry = (segment, query_pos, seg_all, pos_all, block_rows, head_dim ** (-0.5))
    weights = (qkv_weight, out_weight, up_weight, up_bias, down_weight, down_bias, alphas)
    hidden = tokens.astype(jnp.float32)
    saved_layers = []
    for layer_index in range(LAYERS):
        hidden, saved = layer_forward(hidden, layer_index, weights, geometry)
        saved_layers.append(saved)
    output = hidden.astype(jnp.bfloat16)
    grad_hidden = cotangent.astype(jnp.float32)
    layer_results = []
    for layer_index in reversed(range(LAYERS)):
        grad_hidden, layer_grads = layer_backward(
            grad_hidden, saved_layers[layer_index], layer_index, weights, geometry
        )
        layer_results.insert(0, layer_grads)
    finals = reduce_all(layer_results, cycle_size)
    return (
        output,
        grad_hidden,
        finals[0],
        finals[1],
        finals[2],
        finals[3],
        finals[4],
        finals[5],
        finals[6],
    )


def solution(mesh):
    placed = (
        P(("grp", "blk"), None),
        P("grp", None),
        P(),
        P(),
        P(),
        P(),
        P(),
        P(),
        P(),
        P(("grp", "blk"), None),
    )
    sizes = (mesh.shape["grp"], mesh.shape["blk"])
    return jax.shard_map(
        fast_body if sizes == (4, RUNS) else body,
        mesh=mesh,
        in_specs=placed,
        out_specs=(
            P(("grp", "blk"), None),
            P(("grp", "blk"), None),
            P(None, "blk", None),
            P(None, "blk", None),
            P(None, "blk", None),
            P(None, "blk"),
            P(None, "blk", None),
            P(None, "blk"),
            P(),
        ),
        check_vma=False,
    )
```

```python
import functools

import jax
import jax.numpy as jnp
from jax import lax
from jax.experimental import pallas as pl
from jax.experimental.pallas import tpu as pltpu
from jax.sharding import PartitionSpec as P

HEADS = 8
LAYERS = 2
NEGATIVE = -1e30
MESH = pl.DeviceIdType.MESH
F32 = jnp.float32
BF16 = jnp.bfloat16

HALF = 128
RUNS = 8
TEAM = 4
OWN = RUNS // TEAM
DIM = 64
WIDTH = 512
FF = 2048
CUT = 512
TILE = 256
TILES = HALF * RUNS // TILE
PACK = HALF + DIM
CHUNK = 576
SMALL = FF + WIDTH + 128
UP, DOWN = 0, 1
PARTS = ((0, 320), (320, 256))
SHARES = {(1, UP): (176, 0, 144), (1, DOWN): (144, 32, 80), (0, UP): (112, 160, 48), (0, DOWN): (112, 144, 0)}


def spans():
    places, totals = {}, [0, 0, 0]
    for key, counts in SHARES.items():
        first = PARTS[key[1]][0]
        for route, count in enumerate(counts):
            places[(*key, route)] = (first, totals[route], count)
            first += count
            totals[route] += count
    return places, totals


SPANS, TOTALS = spans()

SLOPE_AT = 0.28
TAIL = (
    0.11652077851573843,
    0.06749675579450809,
    0.2689101589486142,
    -0.23699347299932225,
    0.3898740127620002,
    -0.10580824228351815,
)


def nn(a, b):
    return lax.dot_general(a, b, (((1,), (0,)), ((), ())), preferred_element_type=F32)


def nt(a, b):
    return lax.dot_general(a, b, (((1,), (1,)), ((), ())), preferred_element_type=F32)


def layers_kernel(
    tokens, seq_len, alphas, up_bias, down_bias, cotangent, qkv_hbm, out_hbm, up_hbm, down_hbm,
    final_hbm, heads_hbm, output_hbm, input_grad_hbm, small_final,
    wqkv, wout, wup, wdown,
    tok_in, cot_in, flag_out, flag_in, back_out, out_in, grad_in,
    hidden, grad, hid_all, attn_t, ent_t, act_t, branch, slope, second,
    dz, du, da, dqkv,
    pack_out, head_out, pack_in, o_in, do_in,
    kv, kv_t, rq, ro, o_t, lse, acc, dq_t, bias,
    parts, core_in, xa_in, xb_in, ya_in, yb_in, z_in, third_z, third_x, third_y, final,
    heads_out, heads_x, heads_z, heads_sum, heads_all, small, small_in, small_z, small_sum,
    w_sem, move_send, move_recv, a2a_send, a2a_recv, core_send, core_recv, x_send, x_recv, y_send, y_recv,
    z_send, z_recv, tz_send, tz_recv, fin_send, fin_recv, hid_send, hid_recv, hx_send, hx_recv, hz_send, hz_recv, hf_send, hf_recv,
    small_send, small_recv, out_sem, core_free,
):
    grp = lax.axis_index("grp")
    blk = lax.axis_index("blk")
    core = lax.rem(grp, 2)
    side = lax.div(grp, 2)
    yy = lax.rem(blk, 2)
    zz = lax.div(blk, 2)
    member = 2 * core + yy
    far_side = 2 * (1 - side) + core
    low = lax.broadcasted_iota(jnp.int32, (HALF, 128), 1) < DIM

    def place(c, x, z, y):
        return (2 * x + c, 2 * z + y)

    core_peer = place(1 - core, side, zz, yy)
    x_peer = place(core, 1 - side, zz, yy)
    y_peer = place(core, side, zz, 1 - yy)

    weight_copies = {}
    for layer in range(LAYERS):
        for number, (source, target) in enumerate(
            ((qkv_hbm, wqkv), (out_hbm, wout), (up_hbm, wup), (down_hbm, wdown))
        ):
            weight_copies[layer, number] = pltpu.make_async_copy(
                source.at[layer], target.at[layer], w_sem.at[layer, number]
            )
            weight_copies[layer, number].start()

    barrier = pltpu.get_barrier_semaphore()
    for step in range(1, 4):
        pl.semaphore_signal(
            barrier, inc=1, device_id=place(core, side, lax.rem(zz + step, 4), yy), device_id_type=MESH
        )
    for step in range(4):
        pl.semaphore_signal(
            barrier, inc=1, device_id=place(1 - core, side, lax.rem(zz + step, 4), yy), device_id_type=MESH
        )
    pl.semaphore_signal(barrier, inc=1, device_id=x_peer, device_id_type=MESH)
    pl.semaphore_signal(barrier, inc=1, device_id=y_peer, device_id_type=MESH)
    for peer in (
        place(1 - core, side, zz, 1 - yy),
        place(1 - core, 1 - side, zz, yy),
        place(core, 1 - side, zz, 1 - yy),
        place(1 - core, 1 - side, zz, 1 - yy),
    ):
        pl.semaphore_signal(barrier, inc=1, device_id=peer, device_id_type=MESH)

    end_second = lax.div(seq_len[0, 0] + seq_len[0, 1], RUNS)
    flag_out[...] = jnp.full((8, 128), end_second.astype(F32), F32)
    for layer in range(LAYERS):
        for head in range(OWN):
            rq[layer, head, DIM:, :] = jnp.zeros((DIM, HALF * RUNS), BF16)
    for head in range(OWN):
        ro[head, 0:DIM, :] = jnp.zeros((DIM, HALF * RUNS), BF16)

    def remote(source, target, send, recv, peer):
        return pltpu.make_async_remote_copy(
            src_ref=source,
            dst_ref=target,
            send_sem=send,
            recv_sem=recv,
            device_id=peer,
            device_id_type=MESH,
        )

    def credit(semaphore, peer):
        pl.semaphore_signal(semaphore, inc=1, device_id=peer, device_id_type=MESH)

    def moved(kind, slot, source, target, at, core_at, z_at):
        here = jnp.logical_and(core_at == core, z_at == zz)

        @pl.when(here)
        def _():
            pltpu.make_async_copy(source, target.at[at], move_recv.at[kind, at]).start()

        @pl.when(jnp.logical_not(here))
        def _():
            pltpu.make_async_remote_copy(
                src_ref=source,
                dst_ref=target.at[at],
                send_sem=move_send.at[kind, slot],
                recv_sem=move_recv.at[kind, at],
                device_id=place(core_at, side, z_at, yy),
                device_id_type=MESH,
            ).start()

    def move_left(kind, slot, source, core_at, z_at):
        here = jnp.logical_and(core_at == core, z_at == zz)

        @pl.when(jnp.logical_not(here))
        def _():
            pltpu.make_async_copy(source, source, move_send.at[kind, slot]).wait()

    def move_arrived(kind, at, target):
        pltpu.make_async_copy(target.at[at], target.at[at], move_recv.at[kind, at]).wait()

    def to_team(kind, half, source, target):
        moved(kind, half, source, target, lax.div(zz, 2), lax.rem(zz, 2), 2 * half + core)

    def to_team_left(kind, half, source):
        move_left(kind, half, source, lax.rem(zz, 2), 2 * half + core)

    def to_owner(kind, chunk, source, target):
        moved(kind, chunk, source, target, lax.div(zz, 2), lax.rem(zz, 2), core + 2 * chunk)

    def to_owner_left(kind, chunk, source):
        move_left(kind, chunk, source, lax.rem(zz, 2), core + 2 * chunk)

    def half_of(ref, half):
        return ref.at[pl.ds(HALF * half, HALF)]

    def rows_of(half):
        return pl.ds(pl.multiple_of(half * HALF, HALF), HALF)

    def slot_of(other):
        return lax.rem(other + TEAM - member, TEAM)

    def exchange(kind, layer, half, head, outgoing, incoming):
        incoming[half, 0, head] = outgoing[half, member, head]
        for step in range(1, TEAM):
            peer = lax.rem(member + step, TEAM)
            pltpu.make_async_remote_copy(
                src_ref=outgoing.at[half, peer, head],
                dst_ref=incoming.at[half, TEAM - step, head],
                send_sem=a2a_send.at[kind, layer, half, head],
                recv_sem=a2a_recv.at[kind, layer, half, head],
                device_id=place(lax.div(peer, 2), side, zz, lax.rem(peer, 2)),
                device_id_type=MESH,
            ).start()

    def arrived(kind, layer, half, head, incoming):
        whole = incoming.at[half, pl.ds(1, TEAM - 1), head]
        pltpu.make_async_copy(whole, whole, a2a_recv.at[kind, layer, half, head]).wait()

    def left(kind, layer, half, outgoing):
        for head in range(OWN):
            whole = outgoing.at[half, pl.ds(1, TEAM - 1), head]
            pltpu.make_async_copy(whole, whole, a2a_send.at[kind, layer, half, head]).wait()

    def tokens_of(chunk, other):
        return pl.ds(pl.multiple_of(HALF * (TEAM * chunk + other), HALF), HALF)

    def hidden_copy(layer, chunk, which):
        whose = 2 * core + 1 - yy if which == 2 else member
        block = hid_all.at[layer, :, tokens_of(chunk, whose)]
        return remote(
            block,
            block,
            hid_send.at[layer, chunk, which],
            hid_recv.at[layer, chunk, which],
            y_peer if which == 0 else core_peer,
        )

    def hidden_start(layer, chunk):
        for which in range(2):
            hidden_copy(layer, chunk, which).start()

    def hidden_pass(layer, chunk):
        hidden_copy(layer, chunk, 0).wait()
        hidden_copy(layer, chunk, 2).start()

    def hidden_done(layer, chunk):
        for which in range(1, 3):
            hidden_copy(layer, chunk, which).wait()

    def project(layer, half):
        rows = rows_of(half)
        rounded = hidden[half].astype(BF16)
        hid_all[layer, :, tokens_of(half, member)] = rounded.T
        if layer == 1:
            left(0, 0, half, pack_out)
        queries = nn(rounded, wqkv[layer, :, 0:WIDTH]) * (DIM ** -0.5)
        queries_t = queries.T.astype(BF16)
        keys = nn(rounded, wqkv[layer, :, WIDTH : 2 * WIDTH])
        values = nn(rounded, wqkv[layer, :, 2 * WIDTH : 3 * WIDTH])
        for pair in range(RUNS // 2):
            k_pair = keys[:, 128 * pair : 128 * pair + 128]
            v_pair = values[:, 128 * pair : 128 * pair + 128]
            first = jnp.where(low, k_pair, pltpu.roll(v_pair, DIM, 1))
            other = jnp.where(low, pltpu.roll(k_pair, DIM, 1), v_pair)
            pack_out[half, pair, 0, 0:HALF, :] = first.astype(BF16)
            pack_out[half, pair, 1, 0:HALF, :] = other.astype(BF16)
        for head in range(RUNS):
            pack_out[half, head // 2, head % 2, HALF:, :] = queries_t[DIM * head : DIM * head + DIM, :]
        for head in range(OWN):
            exchange(0, layer, half, head, pack_out, pack_in)

    def attend(layer, chunk):
        if layer == 1:
            left(1, 0, chunk, head_out)

        def one_head(head, carry):
            arrived(0, layer, chunk, head, pack_in)
            for other in range(TEAM):
                slot = slot_of(other)
                start = HALF * (TEAM * chunk + other)
                span = slice(start, start + HALF)
                block = pack_in[chunk, slot, head, 0:HALF, :]
                kv[layer, head, span, :] = block
                kv_t[layer, head, :, span] = block.T
                rq[layer, head, 0:DIM, span] = pack_in[chunk, slot, head, HALF:, :]
            for i in (2 * chunk, 2 * chunk + 1):
                columns = slice(TILE * i, TILE * i + TILE)
                query_tile = rq[layer, head, :, columns]
                count = TILE * (i + 1)
                scores = nn(kv[layer, head, 0:count, :], query_tile) + bias[TILE * TILES - count :, :]
                largest = jnp.max(scores, axis=0, keepdims=True)
                weight = jnp.exp(scores - largest)
                total = jnp.sum(weight, axis=0, keepdims=True)
                summed = nn(kv_t[layer, head, DIM:, 0:count], weight.astype(BF16))
                summed = summed / total
                o_t[layer, head, :, columns] = summed
                lse[layer, head, :, columns] = largest + jnp.log(total)
                rounded = summed.astype(BF16)
                for part in range(2):
                    head_out[chunk, 2 * (i - 2 * chunk) + part, head] = rounded[
                        :, HALF * part : HALF * part + HALF
                    ]
            exchange(1, layer, chunk, head, head_out, o_in)
            return carry

        for head in range(OWN):
            one_head(head, 0)

    def feed(layer, half):
        rows = rows_of(half)
        for head in range(OWN):
            arrived(1, layer, half, head, o_in)
        for head in range(RUNS):
            attn_t[layer, DIM * head : DIM * head + DIM, rows] = o_in[half, slot_of(head // 2), head % 2]
        attn = attn_t[layer, :, rows].T
        grown = nn(attn, wout[layer])
        branch[layer, half] = grown
        middle = hidden[half] + alphas[layer, 0] * grown
        entered = middle.astype(BF16)
        ent_t[layer, :, rows] = entered.T
        total = jnp.zeros((HALF, WIDTH), F32)
        for step in range(FF // CUT):
            cut = slice(CUT * step, CUT * step + CUT)
            gate = nn(entered, wup[layer, :, cut]) + up_bias[layer : layer + 1, cut]
            bell = jnp.exp(gate * gate * -0.5)
            near = pl.reciprocal(1.0 + SLOPE_AT * jnp.abs(gate), approx=True)
            tail = jnp.full_like(gate, TAIL[5])
            for factor in TAIL[4::-1]:
                tail = tail * near + factor
            tail = bell * (tail * near)
            risen = jnp.where(gate > 0.0, 1.0 - tail, tail)
            slope[layer, half, :, cut] = risen + gate * bell * 0.3989422804014327
            active = (gate * risen).astype(BF16)
            act_t[layer, cut, rows] = active.T
            total = total + nn(active, wdown[layer, cut, :])
        total = total + down_bias[layer : layer + 1, :]
        second[layer, half] = total
        hidden[half] = middle + alphas[layer, 1] * total

    def total_of(values):
        return jnp.sum(jnp.sum(values, axis=0, keepdims=True), axis=1, keepdims=True)

    def feed_back(layer, half):
        rows = rows_of(half)
        start = grad[half]
        if layer == 0:
            dz[rows, :] = (alphas[layer, 1] * start).astype(BF16)
        scaled = dz[rows, :]
        alpha_second = total_of(start * second[layer, half])
        small[half, layer : layer + 1, FF : FF + WIDTH] = jnp.sum(scaled.astype(F32), axis=0, keepdims=True)
        middle = start
        for step in range(FF // CUT):
            cut = slice(CUT * step, CUT * step + CUT)
            gate = (nt(scaled, wdown[layer, cut, :]) * slope[layer, half, :, cut]).astype(BF16)
            du[rows, cut] = gate
            small[half, layer : layer + 1, cut] = jnp.sum(gate.astype(F32), axis=0, keepdims=True)
            middle = middle + nt(gate, wup[layer, :, cut])
        grad[half] = middle
        alpha_first = total_of(middle * branch[layer, half])
        column = lax.broadcasted_iota(jnp.int32, (1, 128), 1)
        small[half, layer : layer + 1, FF + WIDTH :] = jnp.where(
            column == 0, alpha_first, jnp.where(column == 1, alpha_second, 0.0)
        )
        mixed = (alphas[layer, 0] * middle).astype(BF16)
        da[rows, :] = mixed
        spread = nt(wout[layer], mixed).astype(BF16)
        left(*((1, 1) if layer == 1 else (2, 1)), half, head_out)
        for head in range(RUNS):
            head_out[half, head // 2, head % 2] = spread[DIM * head : DIM * head + DIM, :]
        for head in range(OWN):
            exchange(2, layer, half, head, head_out, do_in)

    def attend_back(layer, chunk):
        left(*((0, 1) if layer == 1 else (3, 1)), chunk, pack_out)

        def one_head(head, carry):
            arrived(2, layer, chunk, head, do_in)
            for other in range(TEAM):
                start = HALF * (TEAM * chunk + other)
                ro[head, DIM:, start : start + HALF] = do_in[chunk, slot_of(other), head]
            for i in (2 * chunk, 2 * chunk + 1):
                columns = slice(TILE * i, TILE * i + TILE)
                query_tile = rq[layer, head, :, columns]
                grad_tile = ro[head, :, columns]
                log_total = lse[layer, head, :, columns]
                delta = jnp.sum(
                    ro[head, DIM:, columns].astype(F32) * o_t[layer, head, :, columns],
                    axis=0,
                    keepdims=True,
                )
                count = TILE * (i + 1)
                keys = kv[layer, head, 0:count, :]
                weight = jnp.exp(nn(keys, query_tile) + bias[TILE * TILES - count :, :] - log_total)
                scored = (weight * (nn(keys, grad_tile) - delta)).astype(BF16)
                term = nt(scored, query_tile) + nt(weight.astype(BF16), grad_tile)
                if chunk == 1 and i == 2:
                    acc[head, 0:count, :] = term
                elif chunk == 1:
                    acc[head, 0 : count - TILE, :] += term[0 : count - TILE, :]
                    acc[head, count - TILE : count, :] = term[count - TILE :, :]
                else:
                    acc[head, 0:count, :] += term
                query_grad = nn(kv_t[layer, head, 0:DIM, 0:count], scored)
                dq_t[head, :, columns] = query_grad * (DIM ** -0.5)
            for other in range(TEAM):
                start = HALF * (TEAM * chunk + other)
                span = slice(start, start + HALF)
                pack_out[chunk, other, head, 0:HALF, :] = acc[head, span, :].astype(BF16)
                pack_out[chunk, other, head, HALF:, :] = dq_t[head, :, span].astype(BF16)
            exchange(3, layer, chunk, head, pack_out, pack_in)
            return carry

        for head in range(OWN):
            one_head(head, 0)

    def project_back(layer, half):
        for head in range(OWN):
            arrived(3, layer, half, head, pack_in)
        turned = jnp.concatenate(
            [pack_in[half, slot_of(head // 2), head % 2, HALF:, :] for head in range(RUNS)], axis=0
        )
        dqkv[:, 0:WIDTH] = turned.T
        for pair in range(RUNS // 2):
            first = pack_in[half, slot_of(pair), 0, 0:HALF, :].astype(F32)
            other = pack_in[half, slot_of(pair), 1, 0:HALF, :].astype(F32)
            k_pair = jnp.where(low, first, pltpu.roll(other, DIM, 1))
            v_pair = jnp.where(low, pltpu.roll(first, DIM, 1), other)
            dqkv[:, WIDTH + 128 * pair : WIDTH + 128 * pair + 128] = k_pair.astype(BF16)
            dqkv[:, 2 * WIDTH + 128 * pair : 2 * WIDTH + 128 * pair + 128] = v_pair.astype(BF16)
        grad[half] = grad[half] + nt(dqkv[...], wqkv[layer])

    def scatter_rows(layer, result, first_row):
        for run in range(RUNS):
            for quarter in range(4):
                parts[layer, quarter, run // 2, run % 2, first_row : first_row + DIM, :] = result[
                    DIM * run : DIM * run + DIM, 128 * quarter : 128 * quarter + 128
                ].astype(BF16)

    def up_grads(layer):
        for step in range(FF // CUT):
            cut = slice(CUT * step, CUT * step + CUT)
            scatter_rows(layer, nn(ent_t[layer], du[:, cut]), DIM * step)
        scatter_rows(layer, nn(attn_t[layer], da[...]), 256)
        core_start(layer, UP)

    def down_grads(layer):
        for run in range(RUNS):
            result = nn(act_t[layer, TILE * run : TILE * run + TILE, :], dz[...])
            for quarter in range(4):
                parts[layer, quarter, run // 2, run % 2, 320:576, :] = result[
                    :, 128 * quarter : 128 * quarter + 128
                ].astype(BF16)
        core_start(layer, DOWN)

    def heads_grads(layer):
        for chunk in range(2):
            hidden_done(layer, chunk)
        blocks = [(run // TEAM, run % TEAM) for run in range(RUNS)]
        keys_values = jnp.concatenate(
            [
                jnp.concatenate([pack_out[chunk, other, head, 0:HALF, :] for chunk, other in blocks], axis=0)
                for head in range(OWN)
            ],
            axis=1,
        )
        queries = jnp.concatenate(
            [
                jnp.concatenate([pack_out[chunk, other, head, HALF:, :] for chunk, other in blocks], axis=1)
                for head in range(OWN)
            ],
            axis=0,
        )
        both = nn(hid_all[layer], keys_values)
        q_part = nt(hid_all[layer], queries)
        first, other = both[:, 0:128], both[:, 128:256]
        left_half = lax.broadcasted_iota(jnp.int32, (WIDTH, 128), 1) < DIM
        k_part = jnp.where(left_half, first, pltpu.roll(other, DIM, 1))
        v_part = jnp.where(left_half, pltpu.roll(first, DIM, 1), other)
        for number, values in enumerate((q_part, k_part, v_part)):
            for run in range(RUNS):
                heads_out[layer, run // 2, run % 2, :, 128 * number : 128 * number + 128] = values[
                    DIM * run : DIM * run + DIM, :
                ].astype(BF16)
        heads_x_copy(layer).start()

    def half_rows(which):
        return pl.ds(pl.multiple_of(32 * which, 32), 32)

    def heads_x_copy(layer):
        return remote(
            heads_out.at[layer, :, :, half_rows(1 - side)],
            heads_x.at[layer],
            hx_send.at[layer],
            hx_recv.at[layer],
            x_peer,
        )

    def heads_z_copy(layer, step):
        peer = lax.rem(zz + step, 4)
        return remote(
            heads_out.at[layer, peer, :, half_rows(side)],
            heads_z.at[layer, 4 - step],
            hz_send.at[layer, step],
            hz_recv.at[layer, 4 - step],
            place(core, side, peer, yy),
        )

    def heads_last_copy(layer, number):
        x, c, y = number // 4, number // 2 % 2, number % 2
        return remote(
            heads_sum.at[layer, 1 - yy if y else yy],
            heads_all.at[layer, side, member],
            hf_send.at[layer, number],
            hf_recv.at[layer, number],
            place(1 - core if c else core, 1 - side if x else side, zz, 1 - yy if y else yy),
        )

    def heads_second(layer):
        heads_x_copy(layer).wait()
        heads_out[layer, :, :, half_rows(side), :] += heads_x[layer]
        for step in range(1, 4):
            heads_z_copy(layer, step).start()

    def heads_third(layer):
        for step in range(1, 4):
            heads_z_copy(layer, step).wait()
        total = heads_out[layer, zz, :, half_rows(side), :].astype(F32)
        for slot in range(1, 4):
            total = total + heads_z[layer, slot].astype(F32)
        heads_sum[layer] = total.astype(BF16)
        heads_all[layer, side, member] = heads_sum[layer, yy]
        for number in range(1, 8):
            heads_last_copy(layer, number).start()

    def heads_copy_out(layer):
        return pltpu.make_async_copy(heads_all.at[layer], heads_hbm.at[layer], out_sem.at[1, layer])

    def heads_done(layer):
        for number in range(1, 8):
            heads_last_copy(layer, number).wait()
        heads_copy_out(layer).start()

    def chunk_rows(layer, part, route):
        first, _, count = SPANS[layer, part, route]
        return pl.ds(first, count)

    def route_rows(layer, part, route):
        _, first, count = SPANS[layer, part, route]
        return pl.ds(first, count)

    def rows_in(layer, part, route):
        return chunk_rows(layer, part, route), route_rows(layer, part, route)

    def used(layer, part, route):
        return SHARES[layer, part][route] > 0

    def core_copy(layer, part, across):
        rows = pl.ds(*PARTS[part])
        return remote(
            parts.at[layer, 2 * across + 1 - core, :, :, rows],
            core_in.at[across, :, :, rows],
            core_send.at[layer, part, across],
            core_recv.at[layer, part, across],
            core_peer,
        )

    def x_copy(layer, part, route):
        rows, room = rows_in(layer, part, route)
        ends = (x_send.at[layer, part, route], x_recv.at[layer, part, route], x_peer)
        if route == 0:
            return remote(parts.at[layer, far_side, :, :, rows], xa_in.at[:, :, room], *ends)
        if route == 1:
            return remote(parts.at[layer, far_side, :, yy, rows], xb_in.at[:, room], *ends)
        return remote(parts.at[layer, far_side, zz, :, rows], third_x.at[:, room], *ends)

    def y_copy(layer, part, route, across=0):
        rows, room = rows_in(layer, part, route)
        which = (layer, part, route + across)
        if route == 2:
            which = (layer, part, 3)
        ends = (y_send.at[which], y_recv.at[which], y_peer)
        if route == 0:
            return remote(parts.at[layer, grp, :, 1 - yy, rows], ya_in.at[:, room], *ends)
        if route == 1:
            return remote(parts.at[layer, 2 * across + core, :, 1 - yy, rows], yb_in.at[across, :, room], *ends)
        return remote(parts.at[layer, grp, zz, 1 - yy, rows], third_y.at[room], *ends)

    def z_copy(layer, part, route, step):
        rows = chunk_rows(layer, part, route)
        peer = lax.rem(zz + step, 4)
        return remote(
            parts.at[layer, grp, peer, yy, rows],
            z_in.at[layer, 4 - step, rows],
            z_send.at[layer, part, route, step],
            z_recv.at[layer, part, route, 4 - step],
            place(core, side, peer, yy),
        )

    def third_z_copy(layer, part, across, step):
        rows, room = rows_in(layer, part, 2)
        peer = lax.rem(zz + step, 4)
        return remote(
            parts.at[layer, 2 * across + core, peer, :, rows],
            third_z.at[across, 4 - step, :, room],
            tz_send.at[layer, part, across, step],
            tz_recv.at[layer, part, across, 4 - step],
            place(core, side, peer, yy),
        )

    def final_copy(layer, part, which):
        block = final.at[layer, far_side if which == 2 else grp, pl.ds(*PARTS[part])]
        return remote(
            block,
            block,
            fin_send.at[layer, part, which],
            fin_recv.at[layer, part, which],
            x_peer if which == 0 else core_peer,
        )

    def core_start(layer, part):
        if layer == 0:
            pl.semaphore_wait(core_free.at[part], 1)
        for across in range(2):
            core_copy(layer, part, across).start()

    def core_done(layer, part):
        rows = pl.ds(*PARTS[part])
        for across in range(2):
            core_copy(layer, part, across).wait()
        for across in (1 - side, side):
            parts[layer, 2 * across + core, :, :, rows, :] += core_in[across, :, :, rows, :]
            if used(layer, part, 0) and across is not side:
                x_copy(layer, part, 0).start()
            if used(layer, part, 1):
                y_copy(layer, part, 1, across).start()
            if used(layer, part, 2):
                for step in range(1, 4):
                    third_z_copy(layer, part, across, step).start()
        if layer == 1:
            credit(core_free.at[part], core_peer)

    def first_x(layer, part):
        if used(layer, part, 0):
            rows, room = rows_in(layer, part, 0)
            x_copy(layer, part, 0).wait()
            for y in (1 - yy, yy):
                parts[layer, grp, :, y, rows, :] += xa_in[:, y, room, :]
                if y is not yy:
                    y_copy(layer, part, 0).start()

    def first_y(layer, part):
        if used(layer, part, 1):
            rows, room = rows_in(layer, part, 1)
            for across in (1 - side, side):
                y_copy(layer, part, 1, across).wait()
            for across in (1 - side, side):
                parts[layer, 2 * across + core, :, yy, rows, :] += yb_in[across, :, room, :]
                if across is not side:
                    x_copy(layer, part, 1).start()

    def first_z(layer, part):
        if used(layer, part, 2):
            rows, room = rows_in(layer, part, 2)
            for across in (1 - side, side):
                for step in range(1, 4):
                    third_z_copy(layer, part, across, step).wait()
                total = parts[layer, 2 * across + core, zz, :, rows, :].astype(F32)
                for slot in range(1, 4):
                    total = total + third_z[across, slot, :, room, :].astype(F32)
                parts[layer, 2 * across + core, zz, :, rows, :] = total.astype(BF16)
                if across is not side:
                    x_copy(layer, part, 2).start()

    def second_x(layer, part):
        if used(layer, part, 0):
            rows, room = rows_in(layer, part, 0)
            y_copy(layer, part, 0).wait()
            parts[layer, grp, :, yy, rows, :] += ya_in[:, room, :]
            for step in range(1, 4):
                z_copy(layer, part, 0, step).start()

    def second_y(layer, part):
        if used(layer, part, 1):
            rows, room = rows_in(layer, part, 1)
            x_copy(layer, part, 1).wait()
            parts[layer, grp, :, yy, rows, :] += xb_in[:, room, :]
            for step in range(1, 4):
                z_copy(layer, part, 1, step).start()

    def second_z(layer, part):
        if used(layer, part, 2):
            rows, room = rows_in(layer, part, 2)
            x_copy(layer, part, 2).wait()
            for y in (1 - yy, yy):
                parts[layer, grp, zz, y, rows, :] += third_x[y, room, :]
                if y is not yy:
                    y_copy(layer, part, 2).start()

    def third_done(layer, part):
        for route in range(3):
            if not used(layer, part, route):
                continue
            rows, room = rows_in(layer, part, route)
            if route == 2:
                y_copy(layer, part, 2).wait()
                final[layer, grp, rows, :] = parts[layer, grp, zz, yy, rows, :] + third_y[room, :]
            else:
                for step in range(1, 4):
                    z_copy(layer, part, route, step).wait()
                total = parts[layer, grp, zz, yy, rows, :].astype(F32)
                for slot in range(1, 4):
                    total = total + z_in[layer, slot, rows, :].astype(F32)
                final[layer, grp, rows, :] = total.astype(BF16)
        for which in range(2):
            final_copy(layer, part, which).start()

    def final_pass(layer, part):
        final_copy(layer, part, 0).wait()
        final_copy(layer, part, 2).start()

    def final_out(layer, part):
        rows = pl.ds(*PARTS[part])
        return pltpu.make_async_copy(
            final.at[layer, :, rows], final_hbm.at[layer, :, rows], out_sem.at[0, 2 * layer + part]
        )

    def final_done(layer, part):
        for which in range(1, 3):
            final_copy(layer, part, which).wait()
        final_out(layer, part).start()

    def small_copy(stage):
        peer = (core_peer, x_peer, y_peer)[stage]
        return remote(
            small_sum.at[stage], small_in.at[stage], small_send.at[stage], small_recv.at[stage], peer
        )

    def small_z_copy(step):
        return remote(
            small_z.at[zz],
            small_z.at[zz],
            small_send.at[2 + step],
            small_recv.at[2 + step],
            place(core, side, lax.rem(zz + step, 4), yy),
        )

    def small_start():
        small_sum[0] = small[0] + small[1]
        small_copy(0).start()

    def small_next(stage):
        small_copy(stage).wait()
        total = small_sum[stage] + small_in[stage]
        if stage < 2:
            small_sum[stage + 1] = total
            small_copy(stage + 1).start()
        else:
            small_z[zz] = total
            for step in range(1, 4):
                small_z_copy(step).start()

    def small_done():
        for step in range(1, 4):
            small_z_copy(step).wait()
        small_sum[0] = (small_z[0] + small_z[1]) + (small_z[2] + small_z[3])
        small_final[:, 0:256] = small_sum[0, :, pl.ds(pl.multiple_of(blk * 256, 256), 256)]
        pair = small_sum[0, :, pl.ds(pl.multiple_of(FF + 128 * zz, 128), 128)]
        small_final[:, 256:384] = jnp.where(yy == 1, pltpu.roll(pair, DIM, 1), pair)
        small_final[:, 384:512] = small_sum[0, :, FF + WIDTH :]

    def halves(*phases, backward=False):
        def both(step, carry):
            for phase in phases:
                phase(1 - step if backward else step)
            return carry

        lax.fori_loop(0, 2, both, 0)

    def begin(half):
        move_arrived(0, half, tok_in)
        hidden[half] = tok_in[half].astype(F32)

    def finish(half):
        back_out[0, half] = hidden[half].astype(BF16)
        to_owner(3, half, back_out.at[0, half], out_in)

    def turn_round(layer, half):
        move_arrived(2, half, cot_in)
        grad[half] = cot_in[half].astype(F32)
        dz[rows_of(half), :] = (alphas[layer, 1] * grad[half]).astype(BF16)

    def hand_back(half):
        back_out[1, half] = grad[half].astype(BF16)
        to_owner(4, half, back_out.at[1, half], grad_in)

    pl.semaphore_wait(barrier, 13)
    for half in range(2):
        to_team(0, half, half_of(tokens, half), tok_in)
    for half in range(2):
        to_team(1, half, flag_out, flag_in)
    for half in range(2):
        to_team(2, half, half_of(cotangent, half), cot_in)
    weight_copies[0, 0].wait()
    halves(begin, functools.partial(project, 0))

    move_arrived(1, 0, flag_in)
    move_arrived(1, 1, flag_in)
    border = jnp.concatenate([flag_in[0, 0:1, :]] * 2, axis=1) - (HALF * lax.div(zz, 2)).astype(F32)
    key_row = lax.broadcasted_iota(jnp.int32, (TILE, TILE), 0)
    query_col = lax.broadcasted_iota(jnp.int32, (TILE, TILE), 1)
    later = key_row > query_col
    key_sub = lax.rem(key_row, HALF).astype(F32) >= border
    query_sub = lax.rem(query_col, HALF).astype(F32) >= border
    apart = jnp.logical_xor(key_sub, query_sub)
    for tile in range(TILES - 1):
        bias[TILE * tile : TILE * tile + TILE, :] = jnp.where(apart, NEGATIVE, 0.0)
    bias[TILE * (TILES - 1) :, :] = jnp.where(jnp.logical_or(later, apart), NEGATIVE, 0.0)

    for number in range(1, 4):
        weight_copies[0, number].wait()
    attend(0, 0)
    attend(0, 1)
    hidden_start(0, 0)
    weight_copies[1, 0].wait()
    halves(functools.partial(feed, 0), functools.partial(project, 1))
    for number in range(1, 4):
        weight_copies[1, number].wait()
    attend(1, 0)
    attend(1, 1)
    hidden_pass(0, 0)
    hidden_start(1, 0)
    halves(functools.partial(feed, 1), finish)
    hidden_start(0, 1)
    hidden_start(1, 1)
    hidden_pass(1, 0)

    halves(functools.partial(turn_round, 1))
    down_grads(1)
    feed_back(1, 1)
    hidden_pass(0, 1)
    hidden_pass(1, 1)
    feed_back(1, 0)
    core_done(1, DOWN)
    up_grads(1)
    attend_back(1, 1)
    first_y(1, DOWN)
    core_done(1, UP)
    attend_back(1, 0)
    first_z(1, DOWN)
    first_y(1, UP)
    heads_grads(1)
    project_back(1, 1)
    feed_back(0, 1)
    second_y(1, DOWN)
    first_x(1, DOWN)
    second_y(1, UP)
    project_back(1, 0)
    feed_back(0, 0)
    small_start()
    attend_back(0, 1)
    second_x(1, DOWN)
    first_z(1, UP)
    first_x(1, UP)
    small_next(0)
    attend_back(0, 0)
    heads_second(1)
    up_grads(0)
    heads_grads(0)
    small_next(1)
    project_back(0, 1)
    hand_back(1)
    down_grads(0)
    core_done(0, UP)
    heads_second(0)
    core_done(0, DOWN)
    second_x(1, UP)
    first_y(0, UP)
    small_next(2)
    project_back(0, 0)
    hand_back(0)
    second_z(1, DOWN)
    first_z(0, UP)
    first_x(0, UP)
    heads_third(1)
    second_z(1, UP)
    second_y(0, UP)
    first_y(0, DOWN)
    third_done(1, DOWN)
    first_z(0, DOWN)
    second_z(0, DOWN)
    second_z(0, UP)
    first_x(0, DOWN)
    small_done()
    second_x(0, UP)
    second_y(0, DOWN)
    heads_third(0)
    third_done(1, UP)
    final_pass(1, DOWN)
    second_x(0, DOWN)
    results = []
    for half in range(2):
        rows = pl.ds(HALF * half, HALF)
        move_arrived(3, half, out_in)
        results.append(pltpu.make_async_copy(out_in.at[half], output_hbm.at[rows], out_sem.at[2, half]))
        move_arrived(4, half, grad_in)
        results.append(pltpu.make_async_copy(grad_in.at[half], input_grad_hbm.at[rows], out_sem.at[3, half]))
    for copy in results:
        copy.start()
    third_done(0, UP)
    third_done(0, DOWN)
    final_pass(0, UP)
    heads_done(1)
    final_done(1, DOWN)
    final_pass(1, UP)
    final_done(1, UP)
    heads_done(0)
    final_pass(0, DOWN)
    final_done(0, UP)
    final_done(0, DOWN)

    for half in range(2):
        left(2, 0, half, head_out)
        left(3, 0, half, pack_out)
        to_team_left(0, half, half_of(tokens, half))
        to_team_left(1, half, flag_out)
        to_team_left(2, half, half_of(cotangent, half))
        to_owner_left(3, half, back_out.at[0, half])
        to_owner_left(4, half, back_out.at[1, half])
    for copy in results:
        copy.wait()
    for layer in range(LAYERS):
        for part in (UP, DOWN):
            final_out(layer, part).wait()
        heads_copy_out(layer).wait()


def results_kernel(
    final_hbm, heads_hbm, out_hbm, grad_hbm, small,
    output, input_grad, qkv_grad, out_grad, up_grad, up_bias_grad, down_grad, down_bias_grad, alpha_grad,
    final, heads, grad_block, out_block, sem,
):
    moves = [
        pltpu.make_async_copy(final_hbm.at[1], final.at[1], sem.at[0]),
        pltpu.make_async_copy(final_hbm.at[0], final.at[0], sem.at[1]),
        pltpu.make_async_copy(grad_hbm, grad_block, sem.at[2]),
        pltpu.make_async_copy(out_hbm, out_block, sem.at[3]),
        pltpu.make_async_copy(heads_hbm, heads, sem.at[4]),
    ]
    for move in moves:
        move.start()
    up_bias_grad[...] = small[:, 0:256]
    down_bias_grad[...] = small[:, 256 : 256 + DIM]
    alpha_grad[...] = small[:, 384:386]
    for layer in (1, 0):
        moves[1 - layer].wait()
        for quarter in range(4):

            def block(first, count):
                return final[layer, quarter, first : first + count, :].astype(F32)

            def columns(step):
                return slice(WIDTH * step + 128 * quarter, WIDTH * step + 128 * quarter + 128)

            for step in range(4):
                up_grad[layer, :, columns(step)] = block(DIM * step, DIM)
            out_grad[layer, :, columns(0)] = block(256, DIM)
            down_grad[layer, :, columns(0)] = block(320, 256)
    moves[4].wait()
    for layer in range(LAYERS):
        for side in range(2):
            for member in range(TEAM):
                for step in range(3):
                    at = WIDTH * step + 128 * member
                    qkv_grad[layer, 32 * side : 32 * side + 32, at : at + 128] = heads[
                        layer, side, member, :, 128 * step : 128 * step + 128
                    ].astype(F32)
    moves[2].wait()
    input_grad[...] = grad_block[...].astype(F32)
    moves[3].wait()
    output[...] = out_block[...]


def fast_body(
    tokens, seq_len, qkv_weight, out_weight, up_weight, up_bias, down_weight, down_bias, alphas, cotangent
):
    whole = pl.BlockSpec(memory_space=pltpu.VMEM)
    scalar = pl.BlockSpec(memory_space=pltpu.SMEM)
    far = pl.BlockSpec(memory_space=pl.ANY)
    shape = jax.ShapeDtypeStruct
    rows = HALF * RUNS

    def vmem(*dims):
        return pltpu.VMEM(dims, BF16)

    def wide(*dims):
        return pltpu.VMEM(dims, F32)

    dma = pltpu.SemaphoreType.DMA
    final, heads, out_block, grad_block, small = pl.pallas_call(
        layers_kernel,
        out_shape=(
            shape((LAYERS, 4, CHUNK, 128), BF16),
            shape((LAYERS, 2, TEAM, DIM // 2, 3 * 128), BF16),
            shape((2 * HALF, WIDTH), BF16),
            shape((2 * HALF, WIDTH), BF16),
            shape((LAYERS, WIDTH), F32),
        ),
        in_specs=[whole, scalar, scalar, whole, whole, whole, far, far, far, far],
        out_specs=(far, far, far, far, whole),
        scratch_shapes=[
            vmem(LAYERS, WIDTH, 3 * WIDTH),
            vmem(LAYERS, WIDTH, WIDTH),
            vmem(LAYERS, WIDTH, FF),
            vmem(LAYERS, FF, WIDTH),
            vmem(2, HALF, WIDTH),
            vmem(2, HALF, WIDTH),
            wide(8, 128),
            wide(2, 8, 128),
            vmem(2, 2, HALF, WIDTH),
            vmem(2, HALF, WIDTH),
            vmem(2, HALF, WIDTH),
            wide(2, HALF, WIDTH),
            wide(2, HALF, WIDTH),
            vmem(LAYERS, WIDTH, rows),
            vmem(LAYERS, WIDTH, 2 * HALF),
            vmem(LAYERS, WIDTH, 2 * HALF),
            vmem(LAYERS, FF, 2 * HALF),
            wide(LAYERS, 2, HALF, WIDTH),
            wide(LAYERS, 2, HALF, FF),
            wide(LAYERS, 2, HALF, WIDTH),
            vmem(2 * HALF, WIDTH),
            vmem(2 * HALF, FF),
            vmem(2 * HALF, WIDTH),
            vmem(HALF, 3 * WIDTH),
            vmem(2, TEAM, OWN, PACK, 128),
            vmem(2, TEAM, OWN, DIM, 128),
            vmem(2, TEAM, OWN, PACK, 128),
            vmem(2, TEAM, OWN, DIM, 128),
            vmem(2, TEAM, OWN, DIM, 128),
            vmem(LAYERS, OWN, rows, 128),
            vmem(LAYERS, OWN, 128, rows),
            vmem(LAYERS, OWN, 128, rows),
            vmem(OWN, 128, rows),
            wide(LAYERS, OWN, DIM, rows),
            wide(LAYERS, OWN, 1, rows),
            wide(OWN, rows, 128),
            wide(OWN, DIM, rows),
            wide(rows, TILE),
            vmem(LAYERS, 4, 4, 2, CHUNK, 128),
            vmem(2, 4, 2, CHUNK, 128),
            vmem(4, 2, TOTALS[0], 128),
            vmem(4, TOTALS[1], 128),
            vmem(4, TOTALS[0], 128),
            vmem(2, 4, TOTALS[1], 128),
            vmem(LAYERS, 4, CHUNK, 128),
            vmem(2, 4, 2, TOTALS[2], 128),
            vmem(2, TOTALS[2], 128),
            vmem(TOTALS[2], 128),
            vmem(LAYERS, 4, CHUNK, 128),
            vmem(LAYERS, 4, 2, DIM, 3 * 128),
            vmem(LAYERS, 4, 2, DIM // 2, 3 * 128),
            vmem(LAYERS, 4, 2, DIM // 2, 3 * 128),
            vmem(LAYERS, 2, DIM // 2, 3 * 128),
            vmem(LAYERS, 2, TEAM, DIM // 2, 3 * 128),
            wide(2, LAYERS, SMALL),
            wide(3, LAYERS, SMALL),
            wide(4, LAYERS, SMALL),
            wide(3, LAYERS, SMALL),
            dma((LAYERS, 4)),
            dma((5, 2)),
            dma((5, 2)),
            dma((4, LAYERS, 2, OWN)),
            dma((4, LAYERS, 2, OWN)),
            dma((LAYERS, 2, 2)),
            dma((LAYERS, 2, 2)),
            dma((LAYERS, 2, 3)),
            dma((LAYERS, 2, 3)),
            dma((LAYERS, 2, 4)),
            dma((LAYERS, 2, 4)),
            dma((LAYERS, 2, 2, 4)),
            dma((LAYERS, 2, 2, 4)),
            dma((LAYERS, 2, 2, 4)),
            dma((LAYERS, 2, 2, 4)),
            dma((LAYERS, 2, 3)),
            dma((LAYERS, 2, 3)),
            dma((LAYERS, 2, 3)),
            dma((LAYERS, 2, 3)),
            dma((LAYERS,)),
            dma((LAYERS,)),
            dma((LAYERS, 4)),
            dma((LAYERS, 4)),
            dma((LAYERS, 8)),
            dma((LAYERS, 8)),
            dma((6,)),
            dma((6,)),
            dma((4, 4)),
            pltpu.SemaphoreType.REGULAR((2,)),
        ],
        compiler_params=pltpu.CompilerParams(
            collective_id=0, has_side_effects=True, vmem_limit_bytes=63 * 1024 * 1024
        ),
        name="layers",
    )(
        tokens, seq_len, alphas, up_bias, down_bias, cotangent,
        qkv_weight, out_weight, up_weight, down_weight,
    )
    return tuple(
        pl.pallas_call(
            results_kernel,
            out_shape=(
                shape((2 * HALF, WIDTH), BF16),
                shape((2 * HALF, WIDTH), F32),
                shape((LAYERS, DIM, 3 * WIDTH), F32),
                shape((LAYERS, DIM, WIDTH), F32),
                shape((LAYERS, DIM, FF), F32),
                shape((LAYERS, FF // RUNS), F32),
                shape((LAYERS, FF // RUNS, WIDTH), F32),
                shape((LAYERS, DIM), F32),
                shape((LAYERS, 2), F32),
            ),
            in_specs=[far, far, far, far, whole],
            out_specs=(whole,) * 9,
            scratch_shapes=[
                vmem(LAYERS, 4, CHUNK, 128),
                vmem(LAYERS, 2, TEAM, DIM // 2, 3 * 128),
                vmem(2 * HALF, WIDTH),
                vmem(2 * HALF, WIDTH),
                dma((6,)),
            ],
            compiler_params=pltpu.CompilerParams(vmem_limit_bytes=60 * 1024 * 1024),
            name="results",
        )(final, heads, out_block, grad_block, small)
    )


def layout(seq_len, local_count, cycle_size):
    piece_rows = seq_len[0] // cycle_size
    end_rows = jnp.cumsum(piece_rows)
    start_rows = end_rows - piece_rows
    local_rows = jnp.arange(local_count, dtype=jnp.int32)
    segment = jnp.sum((local_rows[:, None] >= end_rows[None, :]).astype(jnp.int32), axis=1)
    picked = segment[:, None] == jnp.arange(seq_len.shape[1], dtype=jnp.int32)[None, :]
    offset = local_rows - jnp.sum(jnp.where(picked, start_rows[None, :], 0), axis=1)
    span_rows = jnp.sum(jnp.where(picked, piece_rows[None, :], 0), axis=1)
    return (segment, offset, span_rows)


def gelu_exact(values):
    return jax.nn.gelu(values, approximate=False)


def key_block(whole, geometry, block_index, head_count):
    query_seg, query_pos, seg_all, pos_all, block_rows, score_scale = geometry
    first_row = block_index * block_rows
    key_piece = lax.dynamic_slice_in_dim(whole, first_row, block_rows, 0)
    key_seg = lax.dynamic_slice_in_dim(seg_all, first_row, block_rows, 0)
    key_pos = lax.dynamic_slice_in_dim(pos_all, first_row, block_rows, 0)
    half_width = key_piece.shape[1] // 2
    keys_part = key_piece[:, :half_width].reshape(block_rows, head_count, -1)
    values_part = key_piece[:, half_width:].reshape(block_rows, head_count, -1)
    return (keys_part, values_part, key_seg, key_pos)


def block_scores(queries, keys_part, key_seg, key_pos, geometry):
    query_seg, query_pos, seg_all, pos_all, block_rows, score_scale = geometry
    scores = (
        jnp.einsum("qhd,khd->hqk", queries, keys_part, preferred_element_type=jnp.float32)
        * score_scale
    )
    allowed = (query_seg[:, None] == key_seg[None, :]) & (key_pos[None, :] <= query_pos[:, None])
    return (scores, allowed[None])


def attend(queries, whole, geometry):
    row_count, head_count, head_dim = queries.shape
    block_count = whole.shape[0] // geometry[4]

    def statistics(running, block_index):
        largest, totals = running
        keys_part, values_part, key_seg, key_pos = key_block(
            whole, geometry, block_index, head_count
        )
        scores, allowed = block_scores(queries, keys_part, key_seg, key_pos, geometry)
        newest = jnp.maximum(largest, jnp.max(jnp.where(allowed, scores, NEGATIVE), axis=2))
        weights = jnp.where(allowed, jnp.exp(scores - newest[:, :, None]), 0.0)
        totals = totals * jnp.exp(largest - newest) + jnp.sum(weights, axis=2)
        return ((newest, totals), None)

    initial = (
        jnp.full((head_count, row_count), NEGATIVE, jnp.float32),
        jnp.zeros((head_count, row_count), jnp.float32),
    )
    (largest, totals), unused = lax.scan(statistics, initial, jnp.arange(block_count))
    log_total = largest + jnp.log(totals)

    def weighted(output_sum, block_index):
        keys_part, values_part, key_seg, key_pos = key_block(
            whole, geometry, block_index, head_count
        )
        scores, allowed = block_scores(queries, keys_part, key_seg, key_pos, geometry)
        probs = jnp.where(allowed, jnp.exp(scores - log_total[:, :, None]), 0.0).astype(
            jnp.bfloat16
        )
        output_sum = output_sum + jnp.einsum(
            "hqk,khd->qhd", probs, values_part, preferred_element_type=jnp.float32
        )
        return (output_sum, None)

    output_sum, unused = lax.scan(
        weighted, jnp.zeros((row_count, head_count, head_dim), jnp.float32), jnp.arange(block_count)
    )
    return (output_sum, log_total)


def attend_back(queries, whole, log_total, delta_sum, grad_heads, geometry):
    row_count, head_count, head_dim = queries.shape
    block_rows = geometry[4]
    score_scale = geometry[5]
    block_count = whole.shape[0] // block_rows

    def gradients(query_grad, block_index):
        keys_part, values_part, key_seg, key_pos = key_block(
            whole, geometry, block_index, head_count
        )
        scores, allowed = block_scores(queries, keys_part, key_seg, key_pos, geometry)
        probs = jnp.where(allowed, jnp.exp(scores - log_total[:, :, None]), 0.0)
        grad_probs = jnp.einsum(
            "qhd,khd->hqk", grad_heads, values_part, preferred_element_type=jnp.float32
        )
        grad_scores = (probs * (grad_probs - delta_sum[:, :, None])).astype(jnp.bfloat16)
        query_grad = (
            query_grad
            + jnp.einsum("hqk,khd->qhd", grad_scores, keys_part, preferred_element_type=jnp.float32)
            * score_scale
        )
        key_grad = (
            jnp.einsum("hqk,qhd->khd", grad_scores, queries, preferred_element_type=jnp.float32)
            * score_scale
        )
        value_grad = jnp.einsum(
            "hqk,qhd->khd",
            probs.astype(jnp.bfloat16),
            grad_heads,
            preferred_element_type=jnp.float32,
        )
        joined = jnp.concatenate(
            [key_grad.reshape(block_rows, -1), value_grad.reshape(block_rows, -1)], axis=1
        )
        return (query_grad, joined)

    query_grad, stacked = lax.scan(
        gradients,
        jnp.zeros((row_count, head_count, head_dim), jnp.float32),
        jnp.arange(block_count),
    )
    return (query_grad, stacked.reshape(whole.shape[0], -1))


def layer_forward(hidden, layer_index, weights, geometry):
    qkv_weight, out_weight, up_weight, up_bias, down_weight, down_bias, alphas = weights
    row_count, model_width = hidden.shape
    projection = qkv_weight[layer_index]
    rounded = hidden.astype(jnp.bfloat16)
    queries = (
        jnp.dot(rounded, projection[:, :model_width], preferred_element_type=jnp.float32)
        .astype(jnp.bfloat16)
        .reshape(row_count, HEADS, -1)
    )
    key_value = jnp.dot(
        rounded, projection[:, model_width:], preferred_element_type=jnp.float32
    ).astype(jnp.bfloat16)
    whole = lax.all_gather(key_value, "blk", axis=0, tiled=True)
    heads_out, log_total = attend(queries, whole, geometry)
    heads_rounded = heads_out.reshape(row_count, model_width).astype(jnp.bfloat16)
    branch = jnp.dot(heads_rounded, out_weight[layer_index], preferred_element_type=jnp.float32)
    alpha_pair = alphas[layer_index]
    middle = hidden + alpha_pair[0] * branch
    entered = middle.astype(jnp.bfloat16)
    gate_pre = (
        jnp.dot(entered, up_weight[layer_index], preferred_element_type=jnp.float32)
        + up_bias[layer_index]
    )
    activated = gelu_exact(gate_pre).astype(jnp.bfloat16)
    second = (
        jnp.dot(activated, down_weight[layer_index], preferred_element_type=jnp.float32)
        + down_bias[layer_index]
    )
    result = middle + alpha_pair[1] * second
    saved = (
        rounded,
        queries,
        key_value,
        whole,
        heads_out,
        heads_rounded,
        log_total,
        branch,
        entered,
        gate_pre,
        activated,
        second,
    )
    return (result, saved)


def layer_backward(grad_hidden, saved, layer_index, weights, geometry):
    qkv_weight, out_weight, up_weight, up_bias, down_weight, down_bias, alphas = weights
    (
        rounded,
        queries,
        key_value,
        saved_whole,
        heads_out,
        heads_rounded,
        log_total,
        branch,
        entered,
        gate_pre,
        activated,
        second,
    ) = saved
    row_count = grad_hidden.shape[0]
    alpha_pair = alphas[layer_index]
    grad_second = (alpha_pair[1] * grad_hidden).astype(jnp.bfloat16)
    alpha_second = jnp.sum(grad_hidden * second)
    bias_down = jnp.sum(grad_second.astype(jnp.float32), axis=0)
    grad_down = jnp.einsum("tf,td->fd", activated, grad_second, preferred_element_type=jnp.float32)
    grad_act = jnp.einsum(
        "td,fd->tf", grad_second, down_weight[layer_index], preferred_element_type=jnp.float32
    )
    unused, gelu_pull = jax.vjp(gelu_exact, gate_pre)
    grad_gate = gelu_pull(grad_act)[0].astype(jnp.bfloat16)
    bias_up = jnp.sum(grad_gate.astype(jnp.float32), axis=0)
    grad_up = jnp.einsum("td,tf->df", entered, grad_gate, preferred_element_type=jnp.float32)
    grad_middle = grad_hidden + jnp.einsum(
        "tf,df->td", grad_gate, up_weight[layer_index], preferred_element_type=jnp.float32
    )
    grad_branch = (alpha_pair[0] * grad_middle).astype(jnp.bfloat16)
    alpha_first = jnp.sum(grad_middle * branch)
    grad_proj_out = jnp.einsum(
        "te,td->ed", heads_rounded, grad_branch, preferred_element_type=jnp.float32
    )
    grad_heads = (
        jnp.einsum(
            "td,ed->te", grad_branch, out_weight[layer_index], preferred_element_type=jnp.float32
        )
        .astype(jnp.bfloat16)
        .reshape(queries.shape)
    )
    delta_sum = jnp.sum(grad_heads.astype(jnp.float32) * heads_out, axis=2).T
    whole = lax.all_gather(key_value, "blk", axis=0, tiled=True)
    query_grad, key_terms = attend_back(queries, whole, log_total, delta_sum, grad_heads, geometry)
    key_grads = lax.psum_scatter(
        key_terms.astype(jnp.bfloat16), "blk", scatter_dimension=0, tiled=True
    )
    grad_proj = jnp.concatenate(
        [query_grad.reshape(row_count, -1).astype(jnp.bfloat16), key_grads], axis=1
    )
    grad_qkv = jnp.einsum("td,te->de", rounded, grad_proj, preferred_element_type=jnp.float32)
    grad_input = grad_middle + jnp.einsum(
        "te,de->td", grad_proj, qkv_weight[layer_index], preferred_element_type=jnp.float32
    )
    layer_grads = (
        grad_qkv,
        grad_proj_out,
        grad_up,
        bias_up,
        grad_down,
        bias_down,
        jnp.stack([alpha_first, alpha_second]),
    )
    return (grad_input, layer_grads)


def reduce_all(layer_results, cycle_size):
    stacked = [
        jnp.stack([layer_entry[member] for layer_entry in layer_results], axis=0)
        for member in range(6)
    ]
    alpha_tiles = jnp.stack(
        [jnp.tile(layer_entry[6], cycle_size) for layer_entry in layer_results], axis=0
    )
    shares = (
        lax.psum_scatter(
            stacked[0].astype(jnp.bfloat16), "blk", scatter_dimension=1, tiled=True
        ).astype(jnp.float32),
        lax.psum_scatter(
            stacked[1].astype(jnp.bfloat16), "blk", scatter_dimension=1, tiled=True
        ).astype(jnp.float32),
        lax.psum_scatter(
            stacked[2].astype(jnp.bfloat16), "blk", scatter_dimension=1, tiled=True
        ).astype(jnp.float32),
        lax.psum_scatter(
            stacked[3].astype(jnp.bfloat16), "blk", scatter_dimension=1, tiled=True
        ).astype(jnp.float32),
        lax.psum_scatter(
            stacked[4].astype(jnp.bfloat16), "blk", scatter_dimension=1, tiled=True
        ).astype(jnp.float32),
        lax.psum_scatter(
            stacked[5].astype(jnp.bfloat16), "blk", scatter_dimension=1, tiled=True
        ).astype(jnp.float32),
        lax.psum_scatter(
            alpha_tiles.astype(jnp.bfloat16), "blk", scatter_dimension=1, tiled=True
        ).astype(jnp.float32),
    )
    return (
        lax.psum(shares[0].astype(jnp.bfloat16), "grp").astype(jnp.float32),
        lax.psum(shares[1].astype(jnp.bfloat16), "grp").astype(jnp.float32),
        lax.psum(shares[2].astype(jnp.bfloat16), "grp").astype(jnp.float32),
        lax.psum(shares[3].astype(jnp.bfloat16), "grp").astype(jnp.float32),
        lax.psum(shares[4].astype(jnp.bfloat16), "grp").astype(jnp.float32),
        lax.psum(shares[5].astype(jnp.bfloat16), "grp").astype(jnp.float32),
        lax.psum(shares[6].astype(jnp.bfloat16), "grp").astype(jnp.float32),
    )


def body(
    tokens,
    seq_len,
    qkv_weight,
    out_weight,
    up_weight,
    up_bias,
    down_weight,
    down_bias,
    alphas,
    cotangent,
):
    row_count, model_width = tokens.shape
    cycle_size = lax.axis_size("blk")
    cycle_place = lax.axis_index("blk")
    head_dim = model_width // HEADS
    total_rows = cycle_size * row_count
    block_rows = min(max(row_count, 512), total_rows)
    segment, offset, span_rows = layout(seq_len, row_count, cycle_size)
    query_pos = cycle_place * span_rows + offset
    seg_all = jnp.tile(segment, cycle_size)
    pos_all = jnp.repeat(jnp.arange(cycle_size, dtype=jnp.int32), row_count) * jnp.tile(
        span_rows, cycle_size
    ) + jnp.tile(offset, cycle_size)
    geometry = (segment, query_pos, seg_all, pos_all, block_rows, head_dim ** (-0.5))
    weights = (qkv_weight, out_weight, up_weight, up_bias, down_weight, down_bias, alphas)
    hidden = tokens.astype(jnp.float32)
    saved_layers = []
    for layer_index in range(LAYERS):
        hidden, saved = layer_forward(hidden, layer_index, weights, geometry)
        saved_layers.append(saved)
    output = hidden.astype(jnp.bfloat16)
    grad_hidden = cotangent.astype(jnp.float32)
    layer_results = []
    for layer_index in reversed(range(LAYERS)):
        grad_hidden, layer_grads = layer_backward(
            grad_hidden, saved_layers[layer_index], layer_index, weights, geometry
        )
        layer_results.insert(0, layer_grads)
    finals = reduce_all(layer_results, cycle_size)
    return (
        output,
        grad_hidden,
        finals[0],
        finals[1],
        finals[2],
        finals[3],
        finals[4],
        finals[5],
        finals[6],
    )


def solution(mesh):
    placed = (
        P(("grp", "blk"), None),
        P("grp", None),
        P(),
        P(),
        P(),
        P(),
        P(),
        P(),
        P(),
        P(("grp", "blk"), None),
    )
    sizes = (mesh.shape["grp"], mesh.shape["blk"])
    return jax.shard_map(
        fast_body if sizes == (4, RUNS) else body,
        mesh=mesh,
        in_specs=placed,
        out_specs=(
            P(("grp", "blk"), None),
            P(("grp", "blk"), None),
            P(None, "blk", None),
            P(None, "blk", None),
            P(None, "blk", None),
            P(None, "blk"),
            P(None, "blk", None),
            P(None, "blk"),
            P(),
        ),
        check_vma=False,
    )
```

```python
import functools

import jax
import jax.numpy as jnp
from jax import lax
from jax.experimental import pallas as pl
from jax.experimental.pallas import tpu as pltpu
from jax.sharding import PartitionSpec as P

HEADS = 8
LAYERS = 2
NEGATIVE = -1e30
MESH = pl.DeviceIdType.MESH
F32 = jnp.float32
BF16 = jnp.bfloat16

HALF = 128
RUNS = 8
TEAM = 4
OWN = RUNS // TEAM
DIM = 64
WIDTH = 512
FF = 2048
CUT = 512
TILE = 256
TILES = HALF * RUNS // TILE
PACK = HALF + DIM
CHUNK = 576
SMALL = FF + WIDTH + 128
UP, DOWN = 0, 1
PARTS = ((0, 320), (320, 256))
SHARES = {(1, UP): (192, 0, 128), (1, DOWN): (160, 16, 80), (0, UP): (160, 112, 48), (0, DOWN): (128, 96, 32)}


def spans():
    places, totals = {}, [0, 0, 0]
    for key, counts in SHARES.items():
        first = PARTS[key[1]][0]
        for route, count in enumerate(counts):
            places[(*key, route)] = (first, totals[route], count)
            first += count
            totals[route] += count
    return places, totals


SPANS, TOTALS = spans()

SLOPE_AT = 0.28
TAIL = (
    0.11652077851573843,
    0.06749675579450809,
    0.2689101589486142,
    -0.23699347299932225,
    0.3898740127620002,
    -0.10580824228351815,
)


def nn(a, b):
    return lax.dot_general(a, b, (((1,), (0,)), ((), ())), preferred_element_type=F32)


def nt(a, b):
    return lax.dot_general(a, b, (((1,), (1,)), ((), ())), preferred_element_type=F32)


def layers_kernel(
    tokens, seq_len, alphas, up_bias, down_bias, cotangent, qkv_hbm, out_hbm, up_hbm, down_hbm,
    final_hbm, heads_hbm, output_hbm, input_grad_hbm, small_final,
    wqkv, wout, wup, wdown,
    tok_in, cot_in, flag_out, flag_in, back_out, out_in, grad_in,
    hidden, grad, hid_all, attn_t, ent_t, act_t, branch, slope, second,
    dz, du, da, dqkv,
    pack_out, head_out, pack_in, o_in, do_in,
    kv, kv_t, rq, ro, o_t, lse, acc, dq_t, bias,
    parts, core_in, xa_in, xb_in, ya_in, yb_in, z_in, third_z, third_x, third_y, final,
    heads_out, heads_x, heads_z, heads_sum, heads_all, small, small_in, small_z, small_sum,
    w_sem, move_send, move_recv, a2a_send, a2a_recv, core_send, core_recv, x_send, x_recv, y_send, y_recv,
    z_send, z_recv, tz_send, tz_recv, fin_send, fin_recv, hid_send, hid_recv, hx_send, hx_recv, hz_send, hz_recv, hf_send, hf_recv,
    small_send, small_recv, out_sem, core_free,
):
    grp = lax.axis_index("grp")
    blk = lax.axis_index("blk")
    core = lax.rem(grp, 2)
    side = lax.div(grp, 2)
    yy = lax.rem(blk, 2)
    zz = lax.div(blk, 2)
    member = 2 * core + yy
    far_side = 2 * (1 - side) + core
    low = lax.broadcasted_iota(jnp.int32, (HALF, 128), 1) < DIM

    def place(c, x, z, y):
        return (2 * x + c, 2 * z + y)

    core_peer = place(1 - core, side, zz, yy)
    x_peer = place(core, 1 - side, zz, yy)
    y_peer = place(core, side, zz, 1 - yy)

    weight_copies = {}
    for layer in range(LAYERS):
        for number, (source, target) in enumerate(
            ((qkv_hbm, wqkv), (out_hbm, wout), (up_hbm, wup), (down_hbm, wdown))
        ):
            weight_copies[layer, number] = pltpu.make_async_copy(
                source.at[layer], target.at[layer], w_sem.at[layer, number]
            )
            weight_copies[layer, number].start()

    barrier = pltpu.get_barrier_semaphore()
    for step in range(1, 4):
        pl.semaphore_signal(
            barrier, inc=1, device_id=place(core, side, lax.rem(zz + step, 4), yy), device_id_type=MESH
        )
    for step in range(4):
        pl.semaphore_signal(
            barrier, inc=1, device_id=place(1 - core, side, lax.rem(zz + step, 4), yy), device_id_type=MESH
        )
    pl.semaphore_signal(barrier, inc=1, device_id=x_peer, device_id_type=MESH)
    pl.semaphore_signal(barrier, inc=1, device_id=y_peer, device_id_type=MESH)
    for peer in (
        place(1 - core, side, zz, 1 - yy),
        place(1 - core, 1 - side, zz, yy),
        place(core, 1 - side, zz, 1 - yy),
        place(1 - core, 1 - side, zz, 1 - yy),
    ):
        pl.semaphore_signal(barrier, inc=1, device_id=peer, device_id_type=MESH)

    end_second = lax.div(seq_len[0, 0] + seq_len[0, 1], RUNS)
    flag_out[...] = jnp.full((8, 128), end_second.astype(F32), F32)
    for layer in range(LAYERS):
        for head in range(OWN):
            rq[layer, head, DIM:, :] = jnp.zeros((DIM, HALF * RUNS), BF16)
    for head in range(OWN):
        ro[head, 0:DIM, :] = jnp.zeros((DIM, HALF * RUNS), BF16)

    def remote(source, target, send, recv, peer):
        return pltpu.make_async_remote_copy(
            src_ref=source,
            dst_ref=target,
            send_sem=send,
            recv_sem=recv,
            device_id=peer,
            device_id_type=MESH,
        )

    def credit(semaphore, peer):
        pl.semaphore_signal(semaphore, inc=1, device_id=peer, device_id_type=MESH)

    def moved(kind, slot, source, target, at, core_at, z_at):
        here = jnp.logical_and(core_at == core, z_at == zz)

        @pl.when(here)
        def _():
            pltpu.make_async_copy(source, target.at[at], move_recv.at[kind, at]).start()

        @pl.when(jnp.logical_not(here))
        def _():
            pltpu.make_async_remote_copy(
                src_ref=source,
                dst_ref=target.at[at],
                send_sem=move_send.at[kind, slot],
                recv_sem=move_recv.at[kind, at],
                device_id=place(core_at, side, z_at, yy),
                device_id_type=MESH,
            ).start()

    def move_left(kind, slot, source, core_at, z_at):
        here = jnp.logical_and(core_at == core, z_at == zz)

        @pl.when(jnp.logical_not(here))
        def _():
            pltpu.make_async_copy(source, source, move_send.at[kind, slot]).wait()

    def move_arrived(kind, at, target):
        pltpu.make_async_copy(target.at[at], target.at[at], move_recv.at[kind, at]).wait()

    def to_team(kind, half, source, target):
        moved(kind, half, source, target, lax.div(zz, 2), lax.rem(zz, 2), 2 * half + core)

    def to_team_left(kind, half, source):
        move_left(kind, half, source, lax.rem(zz, 2), 2 * half + core)

    def to_owner(kind, chunk, source, target):
        moved(kind, chunk, source, target, lax.div(zz, 2), lax.rem(zz, 2), core + 2 * chunk)

    def to_owner_left(kind, chunk, source):
        move_left(kind, chunk, source, lax.rem(zz, 2), core + 2 * chunk)

    def half_of(ref, half):
        return ref.at[pl.ds(pl.multiple_of(HALF * half, HALF), HALF)]

    def rows_of(half):
        return pl.ds(pl.multiple_of(half * HALF, HALF), HALF)

    def slot_of(other):
        return lax.rem(other + TEAM - member, TEAM)

    def exchange(kind, layer, half, head, outgoing, incoming):
        incoming[half, 0, head] = outgoing[half, member, head]
        for step in range(1, TEAM):
            peer = lax.rem(member + step, TEAM)
            pltpu.make_async_remote_copy(
                src_ref=outgoing.at[half, peer, head],
                dst_ref=incoming.at[half, TEAM - step, head],
                send_sem=a2a_send.at[kind, layer, half, head],
                recv_sem=a2a_recv.at[kind, layer, half, head],
                device_id=place(lax.div(peer, 2), side, zz, lax.rem(peer, 2)),
                device_id_type=MESH,
            ).start()

    def arrived(kind, layer, half, head, incoming):
        whole = incoming.at[half, pl.ds(1, TEAM - 1), head]
        pltpu.make_async_copy(whole, whole, a2a_recv.at[kind, layer, half, head]).wait()

    def left(kind, layer, half, outgoing):
        for head in range(OWN):
            whole = outgoing.at[half, pl.ds(1, TEAM - 1), head]
            pltpu.make_async_copy(whole, whole, a2a_send.at[kind, layer, half, head]).wait()

    def tokens_of(chunk, other):
        return pl.ds(pl.multiple_of(HALF * (TEAM * chunk + other), HALF), HALF)

    def hidden_copy(layer, chunk, which):
        whose = 2 * core + 1 - yy if which == 2 else member
        block = hid_all.at[layer, :, tokens_of(chunk, whose)]
        return remote(
            block,
            block,
            hid_send.at[layer, chunk, which],
            hid_recv.at[layer, chunk, which],
            y_peer if which == 0 else core_peer,
        )

    def hidden_start(layer, chunk):
        for which in range(2):
            hidden_copy(layer, chunk, which).start()

    def hidden_pass(layer, chunk):
        hidden_copy(layer, chunk, 0).wait()
        hidden_copy(layer, chunk, 2).start()

    def hidden_done(layer, chunk):
        for which in range(1, 3):
            hidden_copy(layer, chunk, which).wait()

    def project(layer, half):
        rows = rows_of(half)
        rounded = hidden[rows, :].astype(BF16)
        hid_all[layer, :, tokens_of(half, member)] = rounded.T
        if layer == 1:
            left(0, 0, half, pack_out)
        queries = nn(rounded, wqkv[layer, :, 0:WIDTH]) * (DIM ** -0.5)
        queries_t = queries.T.astype(BF16)
        keys = nn(rounded, wqkv[layer, :, WIDTH : 2 * WIDTH])
        values = nn(rounded, wqkv[layer, :, 2 * WIDTH : 3 * WIDTH])
        for pair in range(RUNS // 2):
            k_pair = keys[:, 128 * pair : 128 * pair + 128]
            v_pair = values[:, 128 * pair : 128 * pair + 128]
            first = jnp.where(low, k_pair, pltpu.roll(v_pair, DIM, 1))
            other = jnp.where(low, pltpu.roll(k_pair, DIM, 1), v_pair)
            pack_out[half, pair, 0, 0:HALF, :] = first.astype(BF16)
            pack_out[half, pair, 1, 0:HALF, :] = other.astype(BF16)
        for head in range(RUNS):
            pack_out[half, head // 2, head % 2, HALF:, :] = queries_t[DIM * head : DIM * head + DIM, :]
        for head in range(OWN):
            exchange(0, layer, half, head, pack_out, pack_in)

    def attend(layer, chunk):
        if layer == 1:
            left(1, 0, chunk, head_out)

        def one_head(head, carry):
            arrived(0, layer, chunk, head, pack_in)
            for other in range(TEAM):
                slot = slot_of(other)
                start = HALF * (TEAM * chunk + other)
                span = slice(start, start + HALF)
                block = pack_in[chunk, slot, head, 0:HALF, :]
                kv[layer, head, span, :] = block
                kv_t[layer, head, :, span] = block.T
                rq[layer, head, 0:DIM, span] = pack_in[chunk, slot, head, HALF:, :]
            for i in (2 * chunk, 2 * chunk + 1):
                columns = slice(TILE * i, TILE * i + TILE)
                query_tile = rq[layer, head, :, columns]
                count = TILE * (i + 1)
                scores = nn(kv[layer, head, 0:count, :], query_tile) + bias[TILE * TILES - count :, :]
                largest = jnp.max(scores, axis=0, keepdims=True)
                weight = jnp.exp(scores - largest)
                total = jnp.sum(weight, axis=0, keepdims=True)
                summed = nn(kv_t[layer, head, DIM:, 0:count], weight.astype(BF16))
                summed = summed / total
                o_t[layer, head, :, columns] = summed
                lse[layer, head, :, columns] = largest + jnp.log(total)
                rounded = summed.astype(BF16)
                for part in range(2):
                    head_out[chunk, 2 * (i - 2 * chunk) + part, head] = rounded[
                        :, HALF * part : HALF * part + HALF
                    ]
            exchange(1, layer, chunk, head, head_out, o_in)
            return carry

        for head in range(OWN):
            one_head(head, 0)

    def feed(layer, half):
        rows = rows_of(half)
        for head in range(OWN):
            arrived(1, layer, half, head, o_in)
        for head in range(RUNS):
            attn_t[layer, DIM * head : DIM * head + DIM, rows] = o_in[half, slot_of(head // 2), head % 2]
        attn = attn_t[layer, :, rows].T
        grown = nn(attn, wout[layer])
        branch[layer, rows, :] = grown
        middle = hidden[rows, :] + alphas[layer, 0] * grown
        entered = middle.astype(BF16)
        ent_t[layer, :, rows] = entered.T
        total = jnp.zeros((HALF, WIDTH), F32)
        for step in range(FF // CUT):
            cut = slice(CUT * step, CUT * step + CUT)
            gate = nn(entered, wup[layer, :, cut]) + up_bias[layer : layer + 1, cut]
            bell = jnp.exp(gate * gate * -0.5)
            near = pl.reciprocal(1.0 + SLOPE_AT * jnp.abs(gate), approx=True)
            tail = jnp.full_like(gate, TAIL[5])
            for factor in TAIL[4::-1]:
                tail = tail * near + factor
            tail = bell * (tail * near)
            risen = jnp.where(gate > 0.0, 1.0 - tail, tail)
            slope[layer, rows, cut] = risen + gate * bell * 0.3989422804014327
            active = (gate * risen).astype(BF16)
            act_t[layer, cut, rows] = active.T
            total = total + nn(active, wdown[layer, cut, :])
        total = total + down_bias[layer : layer + 1, :]
        second[layer, rows, :] = total
        hidden[rows, :] = middle + alphas[layer, 1] * total

    def total_of(values):
        return jnp.sum(jnp.sum(values, axis=0, keepdims=True), axis=1, keepdims=True)

    def feed_back(layer):
        start = grad[...]
        if layer == 0:
            dz[...] = (alphas[layer, 1] * start).astype(BF16)
        scaled = dz[...]
        alpha_second = total_of(start * second[layer])
        small[layer : layer + 1, FF : FF + WIDTH] = jnp.sum(scaled.astype(F32), axis=0, keepdims=True)
        middle = start
        for step in range(FF // CUT):
            cut = slice(CUT * step, CUT * step + CUT)
            gate = (nt(scaled, wdown[layer, cut, :]) * slope[layer, :, cut]).astype(BF16)
            du[:, cut] = gate
            small[layer : layer + 1, cut] = jnp.sum(gate.astype(F32), axis=0, keepdims=True)
            middle = middle + nt(gate, wup[layer, :, cut])
        grad[...] = middle
        mixed = (alphas[layer, 0] * middle).astype(BF16)
        da[...] = mixed
        spread = nt(wout[layer], mixed).astype(BF16)
        for chunk in (1, 0):
            left(*((1, 1) if layer == 1 else (2, 1)), chunk, head_out)
            for head in range(RUNS):
                head_out[chunk, head // 2, head % 2] = spread[
                    DIM * head : DIM * head + DIM, HALF * chunk : HALF * chunk + HALF
                ]
            for head in range(OWN):
                exchange(2, layer, chunk, head, head_out, do_in)
        alpha_first = total_of(middle * branch[layer])
        column = lax.broadcasted_iota(jnp.int32, (1, 128), 1)
        small[layer : layer + 1, FF + WIDTH :] = jnp.where(
            column == 0, alpha_first, jnp.where(column == 1, alpha_second, 0.0)
        )

    def attend_back(layer, chunk):
        left(*((0, 1) if layer == 1 else (3, 1)), chunk, pack_out)

        def one_head(head, carry):
            arrived(2, layer, chunk, head, do_in)
            for other in range(TEAM):
                start = HALF * (TEAM * chunk + other)
                ro[head, DIM:, start : start + HALF] = do_in[chunk, slot_of(other), head]
            for i in (2 * chunk, 2 * chunk + 1):
                columns = slice(TILE * i, TILE * i + TILE)
                query_tile = rq[layer, head, :, columns]
                grad_tile = ro[head, :, columns]
                log_total = lse[layer, head, :, columns]
                delta = jnp.sum(
                    ro[head, DIM:, columns].astype(F32) * o_t[layer, head, :, columns],
                    axis=0,
                    keepdims=True,
                )
                count = TILE * (i + 1)
                keys = kv[layer, head, 0:count, :]
                weight = jnp.exp(nn(keys, query_tile) + bias[TILE * TILES - count :, :] - log_total)
                scored = (weight * (nn(keys, grad_tile) - delta)).astype(BF16)
                term = nt(scored, query_tile) + nt(weight.astype(BF16), grad_tile)
                if chunk == 1 and i == 2:
                    acc[head, 0:count, :] = term
                elif chunk == 1:
                    acc[head, 0 : count - TILE, :] += term[0 : count - TILE, :]
                    acc[head, count - TILE : count, :] = term[count - TILE :, :]
                else:
                    acc[head, 0:count, :] += term
                query_grad = nn(kv_t[layer, head, 0:DIM, 0:count], scored)
                dq_t[head, :, columns] = query_grad * (DIM ** -0.5)
            for other in range(TEAM):
                start = HALF * (TEAM * chunk + other)
                span = slice(start, start + HALF)
                pack_out[chunk, other, head, 0:HALF, :] = acc[head, span, :].astype(BF16)
                pack_out[chunk, other, head, HALF:, :] = dq_t[head, :, span].astype(BF16)
            exchange(3, layer, chunk, head, pack_out, pack_in)
            return carry

        for head in range(OWN):
            one_head(head, 0)

    def project_back(layer, half):
        for head in range(OWN):
            arrived(3, layer, half, head, pack_in)
        turned = jnp.concatenate(
            [pack_in[half, slot_of(head // 2), head % 2, HALF:, :] for head in range(RUNS)], axis=0
        )
        dqkv[:, 0:WIDTH] = turned.T
        for pair in range(RUNS // 2):
            first = pack_in[half, slot_of(pair), 0, 0:HALF, :].astype(F32)
            other = pack_in[half, slot_of(pair), 1, 0:HALF, :].astype(F32)
            k_pair = jnp.where(low, first, pltpu.roll(other, DIM, 1))
            v_pair = jnp.where(low, pltpu.roll(first, DIM, 1), other)
            dqkv[:, WIDTH + 128 * pair : WIDTH + 128 * pair + 128] = k_pair.astype(BF16)
            dqkv[:, 2 * WIDTH + 128 * pair : 2 * WIDTH + 128 * pair + 128] = v_pair.astype(BF16)
        rows = rows_of(half)
        grad[rows, :] = grad[rows, :] + nt(dqkv[...], wqkv[layer])

    def scatter_rows(layer, result, first_row):
        for run in range(RUNS):
            for quarter in range(4):
                parts[layer, quarter, run // 2, run % 2, first_row : first_row + DIM, :] = result[
                    DIM * run : DIM * run + DIM, 128 * quarter : 128 * quarter + 128
                ].astype(BF16)

    def up_grads(layer):
        for step in range(FF // CUT):
            cut = slice(CUT * step, CUT * step + CUT)
            scatter_rows(layer, nn(ent_t[layer], du[:, cut]), DIM * step)
        scatter_rows(layer, nn(attn_t[layer], da[...]), 256)
        core_start(layer, UP)

    def down_grads(layer):
        for run in range(RUNS):
            result = nn(act_t[layer, TILE * run : TILE * run + TILE, :], dz[...])
            for quarter in range(4):
                parts[layer, quarter, run // 2, run % 2, 320:576, :] = result[
                    :, 128 * quarter : 128 * quarter + 128
                ].astype(BF16)
        core_start(layer, DOWN)

    def heads_grads(layer):
        for chunk in range(2):
            hidden_done(layer, chunk)
        blocks = [(run // TEAM, run % TEAM) for run in range(RUNS)]
        keys_values = jnp.concatenate(
            [
                jnp.concatenate([pack_out[chunk, other, head, 0:HALF, :] for chunk, other in blocks], axis=0)
                for head in range(OWN)
            ],
            axis=1,
        )
        queries = jnp.concatenate(
            [
                jnp.concatenate([pack_out[chunk, other, head, HALF:, :] for chunk, other in blocks], axis=1)
                for head in range(OWN)
            ],
            axis=0,
        )
        both = nn(hid_all[layer], keys_values)
        q_part = nt(hid_all[layer], queries)
        first, other = both[:, 0:128], both[:, 128:256]
        left_half = lax.broadcasted_iota(jnp.int32, (WIDTH, 128), 1) < DIM
        k_part = jnp.where(left_half, first, pltpu.roll(other, DIM, 1))
        v_part = jnp.where(left_half, pltpu.roll(first, DIM, 1), other)
        for number, values in enumerate((q_part, k_part, v_part)):
            for run in range(RUNS):
                heads_out[layer, run // 2, run % 2, :, 128 * number : 128 * number + 128] = values[
                    DIM * run : DIM * run + DIM, :
                ].astype(BF16)
        heads_x_copy(layer).start()

    def half_rows(which):
        return pl.ds(pl.multiple_of(32 * which, 32), 32)

    def heads_x_copy(layer):
        return remote(
            heads_out.at[layer, :, :, half_rows(1 - side)],
            heads_x.at[layer],
            hx_send.at[layer],
            hx_recv.at[layer],
            x_peer,
        )

    def heads_z_copy(layer, step):
        peer = lax.rem(zz + step, 4)
        return remote(
            heads_out.at[layer, peer, :, half_rows(side)],
            heads_z.at[layer, 4 - step],
            hz_send.at[layer, step],
            hz_recv.at[layer, 4 - step],
            place(core, side, peer, yy),
        )

    def heads_last_copy(layer, number):
        x, c, y = number // 4, number // 2 % 2, number % 2
        return remote(
            heads_sum.at[layer, 1 - yy if y else yy],
            heads_all.at[layer, side, member],
            hf_send.at[layer, number],
            hf_recv.at[layer, number],
            place(1 - core if c else core, 1 - side if x else side, zz, 1 - yy if y else yy),
        )

    def heads_second(layer):
        heads_x_copy(layer).wait()
        heads_out[layer, :, :, half_rows(side), :] += heads_x[layer]
        for step in range(1, 4):
            heads_z_copy(layer, step).start()

    def heads_third(layer):
        for step in range(1, 4):
            heads_z_copy(layer, step).wait()
        total = heads_out[layer, zz, :, half_rows(side), :].astype(F32)
        for slot in range(1, 4):
            total = total + heads_z[layer, slot].astype(F32)
        heads_sum[layer] = total.astype(BF16)
        heads_all[layer, side, member] = heads_sum[layer, yy]
        for number in range(1, 8):
            heads_last_copy(layer, number).start()

    def heads_copy_out(layer):
        return pltpu.make_async_copy(heads_all.at[layer], heads_hbm.at[layer], out_sem.at[1, layer])

    def heads_done(layer):
        for number in range(1, 8):
            heads_last_copy(layer, number).wait()
        heads_copy_out(layer).start()

    def chunk_rows(layer, part, route):
        first, _, count = SPANS[layer, part, route]
        return pl.ds(first, count)

    def route_rows(layer, part, route):
        _, first, count = SPANS[layer, part, route]
        return pl.ds(first, count)

    def rows_in(layer, part, route):
        return chunk_rows(layer, part, route), route_rows(layer, part, route)

    def used(layer, part, route):
        return SHARES[layer, part][route] > 0

    def core_copy(layer, part, across):
        rows = pl.ds(*PARTS[part])
        return remote(
            parts.at[layer, 2 * across + 1 - core, :, :, rows],
            core_in.at[across, :, :, rows],
            core_send.at[layer, part, across],
            core_recv.at[layer, part, across],
            core_peer,
        )

    def x_copy(layer, part, route):
        rows, room = rows_in(layer, part, route)
        ends = (x_send.at[layer, part, route], x_recv.at[layer, part, route], x_peer)
        if route == 0:
            return remote(parts.at[layer, far_side, :, :, rows], xa_in.at[:, :, room], *ends)
        if route == 1:
            return remote(parts.at[layer, far_side, :, yy, rows], xb_in.at[:, room], *ends)
        return remote(parts.at[layer, far_side, zz, :, rows], third_x.at[:, room], *ends)

    def y_copy(layer, part, route, across=0):
        rows, room = rows_in(layer, part, route)
        which = (layer, part, route + across)
        if route == 2:
            which = (layer, part, 3)
        ends = (y_send.at[which], y_recv.at[which], y_peer)
        if route == 0:
            return remote(parts.at[layer, grp, :, 1 - yy, rows], ya_in.at[:, room], *ends)
        if route == 1:
            return remote(parts.at[layer, 2 * across + core, :, 1 - yy, rows], yb_in.at[across, :, room], *ends)
        return remote(parts.at[layer, grp, zz, 1 - yy, rows], third_y.at[room], *ends)

    def z_copy(layer, part, route, step):
        rows = chunk_rows(layer, part, route)
        peer = lax.rem(zz + step, 4)
        return remote(
            parts.at[layer, grp, peer, yy, rows],
            z_in.at[layer, 4 - step, rows],
            z_send.at[layer, part, route, step],
            z_recv.at[layer, part, route, 4 - step],
            place(core, side, peer, yy),
        )

    def third_z_copy(layer, part, across, step):
        rows, room = rows_in(layer, part, 2)
        peer = lax.rem(zz + step, 4)
        return remote(
            parts.at[layer, 2 * across + core, peer, :, rows],
            third_z.at[across, 4 - step, :, room],
            tz_send.at[layer, part, across, step],
            tz_recv.at[layer, part, across, 4 - step],
            place(core, side, peer, yy),
        )

    def final_copy(layer, part, which):
        block = final.at[layer, far_side if which == 2 else grp, pl.ds(*PARTS[part])]
        return remote(
            block,
            block,
            fin_send.at[layer, part, which],
            fin_recv.at[layer, part, which],
            x_peer if which == 0 else core_peer,
        )

    def core_start(layer, part):
        if layer == 0:
            pl.semaphore_wait(core_free.at[part], 1)
        for across in range(2):
            core_copy(layer, part, across).start()

    def core_done(layer, part):
        rows = pl.ds(*PARTS[part])
        for across in range(2):
            core_copy(layer, part, across).wait()
        for across in (1 - side, side):
            parts[layer, 2 * across + core, :, :, rows, :] += core_in[across, :, :, rows, :]
            if used(layer, part, 0) and across is not side:
                x_copy(layer, part, 0).start()
            if used(layer, part, 1):
                y_copy(layer, part, 1, across).start()
            if used(layer, part, 2):
                for step in range(1, 4):
                    third_z_copy(layer, part, across, step).start()
        if layer == 1:
            credit(core_free.at[part], core_peer)

    def first_x(layer, part):
        if used(layer, part, 0):
            rows, room = rows_in(layer, part, 0)
            x_copy(layer, part, 0).wait()
            for y in (1 - yy, yy):
                parts[layer, grp, :, y, rows, :] += xa_in[:, y, room, :]
                if y is not yy:
                    y_copy(layer, part, 0).start()

    def first_y(layer, part):
        if used(layer, part, 1):
            rows, room = rows_in(layer, part, 1)
            for across in (1 - side, side):
                y_copy(layer, part, 1, across).wait()
            for across in (1 - side, side):
                parts[layer, 2 * across + core, :, yy, rows, :] += yb_in[across, :, room, :]
                if across is not side:
                    x_copy(layer, part, 1).start()

    def first_z(layer, part):
        if used(layer, part, 2):
            rows, room = rows_in(layer, part, 2)
            for across in (1 - side, side):
                for step in range(1, 4):
                    third_z_copy(layer, part, across, step).wait()
                total = parts[layer, 2 * across + core, zz, :, rows, :].astype(F32)
                for slot in range(1, 4):
                    total = total + third_z[across, slot, :, room, :].astype(F32)
                parts[layer, 2 * across + core, zz, :, rows, :] = total.astype(BF16)
                if across is not side:
                    x_copy(layer, part, 2).start()

    def second_x(layer, part):
        if used(layer, part, 0):
            rows, room = rows_in(layer, part, 0)
            y_copy(layer, part, 0).wait()
            parts[layer, grp, :, yy, rows, :] += ya_in[:, room, :]
            for step in range(1, 4):
                z_copy(layer, part, 0, step).start()

    def second_y(layer, part):
        if used(layer, part, 1):
            rows, room = rows_in(layer, part, 1)
            x_copy(layer, part, 1).wait()
            parts[layer, grp, :, yy, rows, :] += xb_in[:, room, :]
            for step in range(1, 4):
                z_copy(layer, part, 1, step).start()

    def second_z(layer, part):
        if used(layer, part, 2):
            rows, room = rows_in(layer, part, 2)
            x_copy(layer, part, 2).wait()
            for y in (1 - yy, yy):
                parts[layer, grp, zz, y, rows, :] += third_x[y, room, :]
                if y is not yy:
                    y_copy(layer, part, 2).start()

    def third_done(layer, part):
        for route in range(3):
            if not used(layer, part, route):
                continue
            rows, room = rows_in(layer, part, route)
            if route == 2:
                y_copy(layer, part, 2).wait()
                final[layer, grp, rows, :] = parts[layer, grp, zz, yy, rows, :] + third_y[room, :]
            else:
                for step in range(1, 4):
                    z_copy(layer, part, route, step).wait()
                total = parts[layer, grp, zz, yy, rows, :].astype(F32)
                for slot in range(1, 4):
                    total = total + z_in[layer, slot, rows, :].astype(F32)
                final[layer, grp, rows, :] = total.astype(BF16)
        for which in range(2):
            final_copy(layer, part, which).start()

    def final_pass(layer, part):
        final_copy(layer, part, 0).wait()
        final_copy(layer, part, 2).start()

    def final_out(layer, part):
        rows = pl.ds(*PARTS[part])
        return pltpu.make_async_copy(
            final.at[layer, :, rows], final_hbm.at[layer, :, rows], out_sem.at[0, 2 * layer + part]
        )

    def final_done(layer, part):
        for which in range(1, 3):
            final_copy(layer, part, which).wait()
        final_out(layer, part).start()

    def small_copy(stage):
        peer = (core_peer, x_peer, y_peer)[stage]
        return remote(
            small_sum.at[stage], small_in.at[stage], small_send.at[stage], small_recv.at[stage], peer
        )

    def small_z_copy(step):
        return remote(
            small_z.at[zz],
            small_z.at[zz],
            small_send.at[2 + step],
            small_recv.at[2 + step],
            place(core, side, lax.rem(zz + step, 4), yy),
        )

    def small_start():
        small_sum[0] = small[...]
        small_copy(0).start()

    def small_next(stage):
        small_copy(stage).wait()
        total = small_sum[stage] + small_in[stage]
        if stage < 2:
            small_sum[stage + 1] = total
            small_copy(stage + 1).start()
        else:
            small_z[zz] = total
            for step in range(1, 4):
                small_z_copy(step).start()

    def small_done():
        for step in range(1, 4):
            small_z_copy(step).wait()
        small_sum[0] = (small_z[0] + small_z[1]) + (small_z[2] + small_z[3])
        small_final[:, 0:256] = small_sum[0, :, pl.ds(pl.multiple_of(blk * 256, 256), 256)]
        pair = small_sum[0, :, pl.ds(pl.multiple_of(FF + 128 * zz, 128), 128)]
        small_final[:, 256:384] = jnp.where(yy == 1, pltpu.roll(pair, DIM, 1), pair)
        small_final[:, 384:512] = small_sum[0, :, FF + WIDTH :]

    def halves(*phases, first=0):
        def both(step, carry):
            for phase in phases:
                phase(lax.rem(step + first, 2))
            return carry

        lax.fori_loop(0, 2, both, 0)

    def begin(half):
        move_arrived(0, half, tok_in)
        hidden[rows_of(half), :] = tok_in[half].astype(F32)

    def finish(half):
        back_out[0, half] = hidden[rows_of(half), :].astype(BF16)
        to_owner(3, half, back_out.at[0, half], out_in)

    def turn_round(layer, half):
        move_arrived(2, half, cot_in)
        rows = rows_of(half)
        grad[rows, :] = cot_in[half].astype(F32)
        dz[rows, :] = (alphas[layer, 1] * grad[rows, :]).astype(BF16)

    def hand_back(half):
        back_out[1, half] = grad[rows_of(half), :].astype(BF16)
        to_owner(4, half, back_out.at[1, half], grad_in)

    pl.semaphore_wait(barrier, 13)
    upper = lax.div(zz, 2)
    for half in (1 - upper, upper):
        to_team(0, half, half_of(tokens, half), tok_in)
    for half in (1 - upper, upper):
        to_team(1, half, flag_out, flag_in)
    weight_copies[0, 0].wait()
    halves(begin, functools.partial(project, 0), first=upper)
    for half in (1 - upper, upper):
        to_team(2, half, half_of(cotangent, half), cot_in)

    move_arrived(1, 0, flag_in)
    move_arrived(1, 1, flag_in)
    border = jnp.concatenate([flag_in[0, 0:1, :]] * 2, axis=1) - (HALF * lax.div(zz, 2)).astype(F32)
    key_row = lax.broadcasted_iota(jnp.int32, (TILE, TILE), 0)
    query_col = lax.broadcasted_iota(jnp.int32, (TILE, TILE), 1)
    later = key_row > query_col
    key_sub = lax.rem(key_row, HALF).astype(F32) >= border
    query_sub = lax.rem(query_col, HALF).astype(F32) >= border
    apart = jnp.logical_xor(key_sub, query_sub)
    for tile in range(TILES - 1):
        bias[TILE * tile : TILE * tile + TILE, :] = jnp.where(apart, NEGATIVE, 0.0)
    bias[TILE * (TILES - 1) :, :] = jnp.where(jnp.logical_or(later, apart), NEGATIVE, 0.0)

    for number in range(1, 4):
        weight_copies[0, number].wait()
    attend(0, 0)
    attend(0, 1)
    hidden_start(0, 0)
    weight_copies[1, 0].wait()
    halves(functools.partial(feed, 0), functools.partial(project, 1))
    for number in range(1, 4):
        weight_copies[1, number].wait()
    attend(1, 0)
    attend(1, 1)
    hidden_pass(0, 0)
    hidden_start(1, 0)
    halves(functools.partial(feed, 1), finish)
    hidden_start(0, 1)
    hidden_start(1, 1)
    hidden_pass(1, 0)

    halves(functools.partial(turn_round, 1))
    down_grads(1)
    feed_back(1)
    hidden_pass(0, 1)
    hidden_pass(1, 1)
    core_done(1, DOWN)
    up_grads(1)
    attend_back(1, 1)
    first_y(1, DOWN)
    core_done(1, UP)
    attend_back(1, 0)
    second_y(1, DOWN)
    first_y(1, UP)
    first_x(1, DOWN)
    project_back(1, 1)
    heads_grads(1)
    first_z(1, DOWN)
    project_back(1, 0)
    feed_back(0)
    small_start()
    second_x(1, DOWN)
    second_y(1, UP)
    up_grads(0)
    first_x(1, UP)
    heads_second(1)
    first_z(1, UP)
    attend_back(0, 1)
    small_next(0)
    core_done(0, UP)
    second_x(1, UP)
    down_grads(0)
    attend_back(0, 0)
    small_next(1)
    project_back(0, 1)
    hand_back(1)
    first_z(0, UP)
    heads_grads(0)
    small_next(2)
    first_x(0, UP)
    core_done(0, DOWN)
    first_y(0, UP)
    heads_second(0)
    small_done()
    first_z(0, DOWN)
    second_x(0, UP)
    first_x(0, DOWN)
    second_z(0, UP)
    second_z(1, UP)
    heads_third(1)
    second_z(1, DOWN)
    first_y(0, DOWN)
    heads_third(0)
    second_y(0, UP)
    second_x(0, DOWN)
    second_z(0, DOWN)
    third_done(1, UP)
    third_done(0, UP)
    second_y(0, DOWN)
    project_back(0, 0)
    hand_back(0)
    heads_done(1)
    third_done(1, DOWN)
    third_done(0, DOWN)
    final_pass(1, UP)
    final_pass(0, UP)
    final_pass(1, DOWN)
    final_pass(0, DOWN)
    results = []
    for half in range(2):
        rows = pl.ds(HALF * half, HALF)
        move_arrived(3, half, out_in)
        results.append(pltpu.make_async_copy(out_in.at[half], output_hbm.at[rows], out_sem.at[2, half]))
        move_arrived(4, half, grad_in)
        results.append(pltpu.make_async_copy(grad_in.at[half], input_grad_hbm.at[rows], out_sem.at[3, half]))
    for copy in results:
        copy.start()
    final_done(0, UP)
    final_done(1, DOWN)
    heads_done(0)
    final_done(1, UP)
    final_done(0, DOWN)

    for half in range(2):
        left(2, 0, half, head_out)
        left(3, 0, half, pack_out)
        to_team_left(0, half, half_of(tokens, half))
        to_team_left(1, half, flag_out)
        to_team_left(2, half, half_of(cotangent, half))
        to_owner_left(3, half, back_out.at[0, half])
        to_owner_left(4, half, back_out.at[1, half])
    for copy in results:
        copy.wait()
    for layer in range(LAYERS):
        for part in (UP, DOWN):
            final_out(layer, part).wait()
        heads_copy_out(layer).wait()


def results_kernel(
    final_hbm, heads_hbm, out_hbm, grad_hbm, small,
    output, input_grad, qkv_grad, out_grad, up_grad, up_bias_grad, down_grad, down_bias_grad, alpha_grad,
    final, heads, grad_block, out_block, grad_wide, qkv_wide, out_wide, up_wide, down_wide, sem, out_sem,
):
    order = [(layer, part) for layer in (1, 0) for part in (UP, DOWN)]
    pieces = []
    for number, (layer, part) in enumerate(order):
        rows = pl.ds(*PARTS[part])
        pieces.append(pltpu.make_async_copy(final_hbm.at[layer, :, rows], final.at[layer, :, rows], sem.at[number]))
    grad_move = pltpu.make_async_copy(grad_hbm, grad_block, sem.at[4])
    out_move = pltpu.make_async_copy(out_hbm, out_block, sem.at[5])
    heads_move = pltpu.make_async_copy(heads_hbm, heads, sem.at[6])
    for move in (*pieces, grad_move, heads_move, out_move):
        move.start()
    ends = []

    def write(source, target):
        ends.append(pltpu.make_async_copy(source, target, out_sem.at[len(ends)]))
        ends[-1].start()

    up_bias_grad[...] = small[:, 0:256]
    down_bias_grad[...] = small[:, 256 : 256 + DIM]
    alpha_grad[...] = small[:, 384:386]
    for (layer, part), piece in zip(order, pieces):
        piece.wait()
        for quarter in range(4):

            def block(first, count):
                return final[layer, quarter, first : first + count, :].astype(F32)

            def columns(step):
                return slice(WIDTH * step + 128 * quarter, WIDTH * step + 128 * quarter + 128)

            if part == UP:
                for step in range(4):
                    up_wide[layer, :, columns(step)] = block(DIM * step, DIM)
                out_wide[layer, :, columns(0)] = block(256, DIM)
            else:
                down_wide[layer, :, columns(0)] = block(320, 256)
        if part == UP:
            write(up_wide.at[layer], up_grad.at[layer])
            write(out_wide.at[layer], out_grad.at[layer])
        else:
            write(down_wide.at[layer], down_grad.at[layer])
    grad_move.wait()
    grad_wide[...] = grad_block[...].astype(F32)
    write(grad_wide, input_grad)
    heads_move.wait()
    for layer in range(LAYERS):
        for side in range(2):
            for member in range(TEAM):
                for step in range(3):
                    at = WIDTH * step + 128 * member
                    qkv_wide[layer, 32 * side : 32 * side + 32, at : at + 128] = heads[
                        layer, side, member, :, 128 * step : 128 * step + 128
                    ].astype(F32)
        write(qkv_wide.at[layer], qkv_grad.at[layer])
    out_move.wait()
    write(out_block, output)
    for end in ends:
        end.wait()


def fast_body(
    tokens, seq_len, qkv_weight, out_weight, up_weight, up_bias, down_weight, down_bias, alphas, cotangent
):
    whole = pl.BlockSpec(memory_space=pltpu.VMEM)
    scalar = pl.BlockSpec(memory_space=pltpu.SMEM)
    far = pl.BlockSpec(memory_space=pl.ANY)
    shape = jax.ShapeDtypeStruct
    rows = HALF * RUNS

    def vmem(*dims):
        return pltpu.VMEM(dims, BF16)

    def wide(*dims):
        return pltpu.VMEM(dims, F32)

    dma = pltpu.SemaphoreType.DMA
    final, heads, out_block, grad_block, small = pl.pallas_call(
        layers_kernel,
        out_shape=(
            shape((LAYERS, 4, CHUNK, 128), BF16),
            shape((LAYERS, 2, TEAM, DIM // 2, 3 * 128), BF16),
            shape((2 * HALF, WIDTH), BF16),
            shape((2 * HALF, WIDTH), BF16),
            shape((LAYERS, WIDTH), F32),
        ),
        in_specs=[far, scalar, scalar, whole, whole, far, far, far, far, far],
        out_specs=(far, far, far, far, whole),
        scratch_shapes=[
            vmem(LAYERS, WIDTH, 3 * WIDTH),
            vmem(LAYERS, WIDTH, WIDTH),
            vmem(LAYERS, WIDTH, FF),
            vmem(LAYERS, FF, WIDTH),
            vmem(2, HALF, WIDTH),
            vmem(2, HALF, WIDTH),
            wide(8, 128),
            wide(2, 8, 128),
            vmem(2, 2, HALF, WIDTH),
            vmem(2, HALF, WIDTH),
            vmem(2, HALF, WIDTH),
            wide(2 * HALF, WIDTH),
            wide(2 * HALF, WIDTH),
            vmem(LAYERS, WIDTH, rows),
            vmem(LAYERS, WIDTH, 2 * HALF),
            vmem(LAYERS, WIDTH, 2 * HALF),
            vmem(LAYERS, FF, 2 * HALF),
            wide(LAYERS, 2 * HALF, WIDTH),
            wide(LAYERS, 2 * HALF, FF),
            wide(LAYERS, 2 * HALF, WIDTH),
            vmem(2 * HALF, WIDTH),
            vmem(2 * HALF, FF),
            vmem(2 * HALF, WIDTH),
            vmem(HALF, 3 * WIDTH),
            vmem(2, TEAM, OWN, PACK, 128),
            vmem(2, TEAM, OWN, DIM, 128),
            vmem(2, TEAM, OWN, PACK, 128),
            vmem(2, TEAM, OWN, DIM, 128),
            vmem(2, TEAM, OWN, DIM, 128),
            vmem(LAYERS, OWN, rows, 128),
            vmem(LAYERS, OWN, 128, rows),
            vmem(LAYERS, OWN, 128, rows),
            vmem(OWN, 128, rows),
            wide(LAYERS, OWN, DIM, rows),
            wide(LAYERS, OWN, 1, rows),
            wide(OWN, rows, 128),
            wide(OWN, DIM, rows),
            wide(rows, TILE),
            vmem(LAYERS, 4, 4, 2, CHUNK, 128),
            vmem(2, 4, 2, CHUNK, 128),
            vmem(4, 2, TOTALS[0], 128),
            vmem(4, TOTALS[1], 128),
            vmem(4, TOTALS[0], 128),
            vmem(2, 4, TOTALS[1], 128),
            vmem(LAYERS, 4, CHUNK, 128),
            vmem(2, 4, 2, TOTALS[2], 128),
            vmem(2, TOTALS[2], 128),
            vmem(TOTALS[2], 128),
            vmem(LAYERS, 4, CHUNK, 128),
            vmem(LAYERS, 4, 2, DIM, 3 * 128),
            vmem(LAYERS, 4, 2, DIM // 2, 3 * 128),
            vmem(LAYERS, 4, 2, DIM // 2, 3 * 128),
            vmem(LAYERS, 2, DIM // 2, 3 * 128),
            vmem(LAYERS, 2, TEAM, DIM // 2, 3 * 128),
            wide(LAYERS, SMALL),
            wide(3, LAYERS, SMALL),
            wide(4, LAYERS, SMALL),
            wide(3, LAYERS, SMALL),
            dma((LAYERS, 4)),
            dma((5, 2)),
            dma((5, 2)),
            dma((4, LAYERS, 2, OWN)),
            dma((4, LAYERS, 2, OWN)),
            dma((LAYERS, 2, 2)),
            dma((LAYERS, 2, 2)),
            dma((LAYERS, 2, 3)),
            dma((LAYERS, 2, 3)),
            dma((LAYERS, 2, 4)),
            dma((LAYERS, 2, 4)),
            dma((LAYERS, 2, 2, 4)),
            dma((LAYERS, 2, 2, 4)),
            dma((LAYERS, 2, 2, 4)),
            dma((LAYERS, 2, 2, 4)),
            dma((LAYERS, 2, 3)),
            dma((LAYERS, 2, 3)),
            dma((LAYERS, 2, 3)),
            dma((LAYERS, 2, 3)),
            dma((LAYERS,)),
            dma((LAYERS,)),
            dma((LAYERS, 4)),
            dma((LAYERS, 4)),
            dma((LAYERS, 8)),
            dma((LAYERS, 8)),
            dma((6,)),
            dma((6,)),
            dma((4, 4)),
            pltpu.SemaphoreType.REGULAR((2,)),
        ],
        compiler_params=pltpu.CompilerParams(
            collective_id=0, has_side_effects=True, vmem_limit_bytes=63 * 1024 * 1024
        ),
        name="layers",
    )(
        tokens, seq_len, alphas, up_bias, down_bias, cotangent,
        qkv_weight, out_weight, up_weight, down_weight,
    )
    return tuple(
        pl.pallas_call(
            results_kernel,
            out_shape=(
                shape((2 * HALF, WIDTH), BF16),
                shape((2 * HALF, WIDTH), F32),
                shape((LAYERS, DIM, 3 * WIDTH), F32),
                shape((LAYERS, DIM, WIDTH), F32),
                shape((LAYERS, DIM, FF), F32),
                shape((LAYERS, FF // RUNS), F32),
                shape((LAYERS, FF // RUNS, WIDTH), F32),
                shape((LAYERS, DIM), F32),
                shape((LAYERS, 2), F32),
            ),
            in_specs=[far, far, far, far, whole],
            out_specs=(far, far, far, far, far, whole, far, whole, whole),
            scratch_shapes=[
                vmem(LAYERS, 4, CHUNK, 128),
                vmem(LAYERS, 2, TEAM, DIM // 2, 3 * 128),
                vmem(2 * HALF, WIDTH),
                vmem(2 * HALF, WIDTH),
                wide(2 * HALF, WIDTH),
                wide(LAYERS, DIM, 3 * WIDTH),
                wide(LAYERS, DIM, WIDTH),
                wide(LAYERS, DIM, FF),
                wide(LAYERS, FF // RUNS, WIDTH),
                dma((7,)),
                dma((10,)),
            ],
            compiler_params=pltpu.CompilerParams(vmem_limit_bytes=60 * 1024 * 1024),
            name="results",
        )(final, heads, out_block, grad_block, small)
    )


def layout(seq_len, local_count, cycle_size):
    piece_rows = seq_len[0] // cycle_size
    end_rows = jnp.cumsum(piece_rows)
    start_rows = end_rows - piece_rows
    local_rows = jnp.arange(local_count, dtype=jnp.int32)
    segment = jnp.sum((local_rows[:, None] >= end_rows[None, :]).astype(jnp.int32), axis=1)
    picked = segment[:, None] == jnp.arange(seq_len.shape[1], dtype=jnp.int32)[None, :]
    offset = local_rows - jnp.sum(jnp.where(picked, start_rows[None, :], 0), axis=1)
    span_rows = jnp.sum(jnp.where(picked, piece_rows[None, :], 0), axis=1)
    return (segment, offset, span_rows)


def gelu_exact(values):
    return jax.nn.gelu(values, approximate=False)


def key_block(whole, geometry, block_index, head_count):
    query_seg, query_pos, seg_all, pos_all, block_rows, score_scale = geometry
    first_row = block_index * block_rows
    key_piece = lax.dynamic_slice_in_dim(whole, first_row, block_rows, 0)
    key_seg = lax.dynamic_slice_in_dim(seg_all, first_row, block_rows, 0)
    key_pos = lax.dynamic_slice_in_dim(pos_all, first_row, block_rows, 0)
    half_width = key_piece.shape[1] // 2
    keys_part = key_piece[:, :half_width].reshape(block_rows, head_count, -1)
    values_part = key_piece[:, half_width:].reshape(block_rows, head_count, -1)
    return (keys_part, values_part, key_seg, key_pos)


def block_scores(queries, keys_part, key_seg, key_pos, geometry):
    query_seg, query_pos, seg_all, pos_all, block_rows, score_scale = geometry
    scores = (
        jnp.einsum("qhd,khd->hqk", queries, keys_part, preferred_element_type=jnp.float32)
        * score_scale
    )
    allowed = (query_seg[:, None] == key_seg[None, :]) & (key_pos[None, :] <= query_pos[:, None])
    return (scores, allowed[None])


def attend(queries, whole, geometry):
    row_count, head_count, head_dim = queries.shape
    block_count = whole.shape[0] // geometry[4]

    def statistics(running, block_index):
        largest, totals = running
        keys_part, values_part, key_seg, key_pos = key_block(
            whole, geometry, block_index, head_count
        )
        scores, allowed = block_scores(queries, keys_part, key_seg, key_pos, geometry)
        newest = jnp.maximum(largest, jnp.max(jnp.where(allowed, scores, NEGATIVE), axis=2))
        weights = jnp.where(allowed, jnp.exp(scores - newest[:, :, None]), 0.0)
        totals = totals * jnp.exp(largest - newest) + jnp.sum(weights, axis=2)
        return ((newest, totals), None)

    initial = (
        jnp.full((head_count, row_count), NEGATIVE, jnp.float32),
        jnp.zeros((head_count, row_count), jnp.float32),
    )
    (largest, totals), unused = lax.scan(statistics, initial, jnp.arange(block_count))
    log_total = largest + jnp.log(totals)

    def weighted(output_sum, block_index):
        keys_part, values_part, key_seg, key_pos = key_block(
            whole, geometry, block_index, head_count
        )
        scores, allowed = block_scores(queries, keys_part, key_seg, key_pos, geometry)
        probs = jnp.where(allowed, jnp.exp(scores - log_total[:, :, None]), 0.0).astype(
            jnp.bfloat16
        )
        output_sum = output_sum + jnp.einsum(
            "hqk,khd->qhd", probs, values_part, preferred_element_type=jnp.float32
        )
        return (output_sum, None)

    output_sum, unused = lax.scan(
        weighted, jnp.zeros((row_count, head_count, head_dim), jnp.float32), jnp.arange(block_count)
    )
    return (output_sum, log_total)


def attend_back(queries, whole, log_total, delta_sum, grad_heads, geometry):
    row_count, head_count, head_dim = queries.shape
    block_rows = geometry[4]
    score_scale = geometry[5]
    block_count = whole.shape[0] // block_rows

    def gradients(query_grad, block_index):
        keys_part, values_part, key_seg, key_pos = key_block(
            whole, geometry, block_index, head_count
        )
        scores, allowed = block_scores(queries, keys_part, key_seg, key_pos, geometry)
        probs = jnp.where(allowed, jnp.exp(scores - log_total[:, :, None]), 0.0)
        grad_probs = jnp.einsum(
            "qhd,khd->hqk", grad_heads, values_part, preferred_element_type=jnp.float32
        )
        grad_scores = (probs * (grad_probs - delta_sum[:, :, None])).astype(jnp.bfloat16)
        query_grad = (
            query_grad
            + jnp.einsum("hqk,khd->qhd", grad_scores, keys_part, preferred_element_type=jnp.float32)
            * score_scale
        )
        key_grad = (
            jnp.einsum("hqk,qhd->khd", grad_scores, queries, preferred_element_type=jnp.float32)
            * score_scale
        )
        value_grad = jnp.einsum(
            "hqk,qhd->khd",
            probs.astype(jnp.bfloat16),
            grad_heads,
            preferred_element_type=jnp.float32,
        )
        joined = jnp.concatenate(
            [key_grad.reshape(block_rows, -1), value_grad.reshape(block_rows, -1)], axis=1
        )
        return (query_grad, joined)

    query_grad, stacked = lax.scan(
        gradients,
        jnp.zeros((row_count, head_count, head_dim), jnp.float32),
        jnp.arange(block_count),
    )
    return (query_grad, stacked.reshape(whole.shape[0], -1))


def layer_forward(hidden, layer_index, weights, geometry):
    qkv_weight, out_weight, up_weight, up_bias, down_weight, down_bias, alphas = weights
    row_count, model_width = hidden.shape
    projection = qkv_weight[layer_index]
    rounded = hidden.astype(jnp.bfloat16)
    queries = (
        jnp.dot(rounded, projection[:, :model_width], preferred_element_type=jnp.float32)
        .astype(jnp.bfloat16)
        .reshape(row_count, HEADS, -1)
    )
    key_value = jnp.dot(
        rounded, projection[:, model_width:], preferred_element_type=jnp.float32
    ).astype(jnp.bfloat16)
    whole = lax.all_gather(key_value, "blk", axis=0, tiled=True)
    heads_out, log_total = attend(queries, whole, geometry)
    heads_rounded = heads_out.reshape(row_count, model_width).astype(jnp.bfloat16)
    branch = jnp.dot(heads_rounded, out_weight[layer_index], preferred_element_type=jnp.float32)
    alpha_pair = alphas[layer_index]
    middle = hidden + alpha_pair[0] * branch
    entered = middle.astype(jnp.bfloat16)
    gate_pre = (
        jnp.dot(entered, up_weight[layer_index], preferred_element_type=jnp.float32)
        + up_bias[layer_index]
    )
    activated = gelu_exact(gate_pre).astype(jnp.bfloat16)
    second = (
        jnp.dot(activated, down_weight[layer_index], preferred_element_type=jnp.float32)
        + down_bias[layer_index]
    )
    result = middle + alpha_pair[1] * second
    saved = (
        rounded,
        queries,
        key_value,
        whole,
        heads_out,
        heads_rounded,
        log_total,
        branch,
        entered,
        gate_pre,
        activated,
        second,
    )
    return (result, saved)


def layer_backward(grad_hidden, saved, layer_index, weights, geometry):
    qkv_weight, out_weight, up_weight, up_bias, down_weight, down_bias, alphas = weights
    (
        rounded,
        queries,
        key_value,
        saved_whole,
        heads_out,
        heads_rounded,
        log_total,
        branch,
        entered,
        gate_pre,
        activated,
        second,
    ) = saved
    row_count = grad_hidden.shape[0]
    alpha_pair = alphas[layer_index]
    grad_second = (alpha_pair[1] * grad_hidden).astype(jnp.bfloat16)
    alpha_second = jnp.sum(grad_hidden * second)
    bias_down = jnp.sum(grad_second.astype(jnp.float32), axis=0)
    grad_down = jnp.einsum("tf,td->fd", activated, grad_second, preferred_element_type=jnp.float32)
    grad_act = jnp.einsum(
        "td,fd->tf", grad_second, down_weight[layer_index], preferred_element_type=jnp.float32
    )
    unused, gelu_pull = jax.vjp(gelu_exact, gate_pre)
    grad_gate = gelu_pull(grad_act)[0].astype(jnp.bfloat16)
    bias_up = jnp.sum(grad_gate.astype(jnp.float32), axis=0)
    grad_up = jnp.einsum("td,tf->df", entered, grad_gate, preferred_element_type=jnp.float32)
    grad_middle = grad_hidden + jnp.einsum(
        "tf,df->td", grad_gate, up_weight[layer_index], preferred_element_type=jnp.float32
    )
    grad_branch = (alpha_pair[0] * grad_middle).astype(jnp.bfloat16)
    alpha_first = jnp.sum(grad_middle * branch)
    grad_proj_out = jnp.einsum(
        "te,td->ed", heads_rounded, grad_branch, preferred_element_type=jnp.float32
    )
    grad_heads = (
        jnp.einsum(
            "td,ed->te", grad_branch, out_weight[layer_index], preferred_element_type=jnp.float32
        )
        .astype(jnp.bfloat16)
        .reshape(queries.shape)
    )
    delta_sum = jnp.sum(grad_heads.astype(jnp.float32) * heads_out, axis=2).T
    whole = lax.all_gather(key_value, "blk", axis=0, tiled=True)
    query_grad, key_terms = attend_back(queries, whole, log_total, delta_sum, grad_heads, geometry)
    key_grads = lax.psum_scatter(
        key_terms.astype(jnp.bfloat16), "blk", scatter_dimension=0, tiled=True
    )
    grad_proj = jnp.concatenate(
        [query_grad.reshape(row_count, -1).astype(jnp.bfloat16), key_grads], axis=1
    )
    grad_qkv = jnp.einsum("td,te->de", rounded, grad_proj, preferred_element_type=jnp.float32)
    grad_input = grad_middle + jnp.einsum(
        "te,de->td", grad_proj, qkv_weight[layer_index], preferred_element_type=jnp.float32
    )
    layer_grads = (
        grad_qkv,
        grad_proj_out,
        grad_up,
        bias_up,
        grad_down,
        bias_down,
        jnp.stack([alpha_first, alpha_second]),
    )
    return (grad_input, layer_grads)


def reduce_all(layer_results, cycle_size):
    stacked = [
        jnp.stack([layer_entry[member] for layer_entry in layer_results], axis=0)
        for member in range(6)
    ]
    alpha_tiles = jnp.stack(
        [jnp.tile(layer_entry[6], cycle_size) for layer_entry in layer_results], axis=0
    )
    shares = (
        lax.psum_scatter(
            stacked[0].astype(jnp.bfloat16), "blk", scatter_dimension=1, tiled=True
        ).astype(jnp.float32),
        lax.psum_scatter(
            stacked[1].astype(jnp.bfloat16), "blk", scatter_dimension=1, tiled=True
        ).astype(jnp.float32),
        lax.psum_scatter(
            stacked[2].astype(jnp.bfloat16), "blk", scatter_dimension=1, tiled=True
        ).astype(jnp.float32),
        lax.psum_scatter(
            stacked[3].astype(jnp.bfloat16), "blk", scatter_dimension=1, tiled=True
        ).astype(jnp.float32),
        lax.psum_scatter(
            stacked[4].astype(jnp.bfloat16), "blk", scatter_dimension=1, tiled=True
        ).astype(jnp.float32),
        lax.psum_scatter(
            stacked[5].astype(jnp.bfloat16), "blk", scatter_dimension=1, tiled=True
        ).astype(jnp.float32),
        lax.psum_scatter(
            alpha_tiles.astype(jnp.bfloat16), "blk", scatter_dimension=1, tiled=True
        ).astype(jnp.float32),
    )
    return (
        lax.psum(shares[0].astype(jnp.bfloat16), "grp").astype(jnp.float32),
        lax.psum(shares[1].astype(jnp.bfloat16), "grp").astype(jnp.float32),
        lax.psum(shares[2].astype(jnp.bfloat16), "grp").astype(jnp.float32),
        lax.psum(shares[3].astype(jnp.bfloat16), "grp").astype(jnp.float32),
        lax.psum(shares[4].astype(jnp.bfloat16), "grp").astype(jnp.float32),
        lax.psum(shares[5].astype(jnp.bfloat16), "grp").astype(jnp.float32),
        lax.psum(shares[6].astype(jnp.bfloat16), "grp").astype(jnp.float32),
    )


def body(
    tokens,
    seq_len,
    qkv_weight,
    out_weight,
    up_weight,
    up_bias,
    down_weight,
    down_bias,
    alphas,
    cotangent,
):
    row_count, model_width = tokens.shape
    cycle_size = lax.axis_size("blk")
    cycle_place = lax.axis_index("blk")
    head_dim = model_width // HEADS
    total_rows = cycle_size * row_count
    block_rows = min(max(row_count, 512), total_rows)
    segment, offset, span_rows = layout(seq_len, row_count, cycle_size)
    query_pos = cycle_place * span_rows + offset
    seg_all = jnp.tile(segment, cycle_size)
    pos_all = jnp.repeat(jnp.arange(cycle_size, dtype=jnp.int32), row_count) * jnp.tile(
        span_rows, cycle_size
    ) + jnp.tile(offset, cycle_size)
    geometry = (segment, query_pos, seg_all, pos_all, block_rows, head_dim ** (-0.5))
    weights = (qkv_weight, out_weight, up_weight, up_bias, down_weight, down_bias, alphas)
    hidden = tokens.astype(jnp.float32)
    saved_layers = []
    for layer_index in range(LAYERS):
        hidden, saved = layer_forward(hidden, layer_index, weights, geometry)
        saved_layers.append(saved)
    output = hidden.astype(jnp.bfloat16)
    grad_hidden = cotangent.astype(jnp.float32)
    layer_results = []
    for layer_index in reversed(range(LAYERS)):
        grad_hidden, layer_grads = layer_backward(
            grad_hidden, saved_layers[layer_index], layer_index, weights, geometry
        )
        layer_results.insert(0, layer_grads)
    finals = reduce_all(layer_results, cycle_size)
    return (
        output,
        grad_hidden,
        finals[0],
        finals[1],
        finals[2],
        finals[3],
        finals[4],
        finals[5],
        finals[6],
    )


def solution(mesh):
    placed = (
        P(("grp", "blk"), None),
        P("grp", None),
        P(),
        P(),
        P(),
        P(),
        P(),
        P(),
        P(),
        P(("grp", "blk"), None),
    )
    sizes = (mesh.shape["grp"], mesh.shape["blk"])
    return jax.shard_map(
        fast_body if sizes == (4, RUNS) else body,
        mesh=mesh,
        in_specs=placed,
        out_specs=(
            P(("grp", "blk"), None),
            P(("grp", "blk"), None),
            P(None, "blk", None),
            P(None, "blk", None),
            P(None, "blk", None),
            P(None, "blk"),
            P(None, "blk", None),
            P(None, "blk"),
            P(),
        ),
        check_vma=False,
    )
```

```python
import functools

import jax
import jax.numpy as jnp
from jax import lax
from jax.experimental import pallas as pl
from jax.experimental.pallas import tpu as pltpu
from jax.sharding import PartitionSpec as P

HEADS = 8
LAYERS = 2
NEGATIVE = -1e30
MESH = pl.DeviceIdType.MESH
F32 = jnp.float32
BF16 = jnp.bfloat16

HALF = 128
RUNS = 8
TEAM = 4
OWN = RUNS // TEAM
DIM = 64
WIDTH = 512
FF = 2048
CUT = 512
TILE = 256
TILES = HALF * RUNS // TILE
PACK = HALF + DIM
CHUNK = 576
SMALL = FF + WIDTH + 128
UP, DOWN = 0, 1
PARTS = ((0, 320), (320, 256))
SHARES = {(1, UP): (192, 0, 128), (1, DOWN): (160, 16, 80), (0, UP): (160, 112, 48), (0, DOWN): (128, 96, 32)}


def spans():
    places, totals = {}, [0, 0, 0]
    for key, counts in SHARES.items():
        first = PARTS[key[1]][0]
        for route, count in enumerate(counts):
            places[(*key, route)] = (first, totals[route], count)
            first += count
            totals[route] += count
    return places, totals


SPANS, TOTALS = spans()

SLOPE_AT = 0.28
TAIL = (
    0.11652077851573843,
    0.06749675579450809,
    0.2689101589486142,
    -0.23699347299932225,
    0.3898740127620002,
    -0.10580824228351815,
)


def nn(a, b):
    return lax.dot_general(a, b, (((1,), (0,)), ((), ())), preferred_element_type=F32)


def nt(a, b):
    return lax.dot_general(a, b, (((1,), (1,)), ((), ())), preferred_element_type=F32)


def layers_kernel(
    tokens, seq_len, alphas, up_bias, down_bias, cotangent, qkv_hbm, out_hbm, up_hbm, down_hbm,
    final, heads_all, out_in, grad_in, small_final,
    wqkv, wout, wup, wdown,
    tok_in, cot_in, flag_out, flag_in, back_out,
    hidden, grad, hid_all, attn_t, entered, act, branch, slope, second,
    dz, du, da, dqkv,
    pack_out, head_out, pack_in, o_in, do_in,
    kv, kv_t, rq, ro, o_t, lse, acc, dq_t, bias,
    parts, core_in, xa_in, xb_in, ya_in, yb_in, z_in, third_z, third_x, third_y,
    heads_out, heads_x, heads_z, heads_sum, small, small_in, small_z, small_sum,
    w_sem, move_send, move_recv, a2a_send, a2a_recv, core_send, core_recv, x_send, x_recv, y_send, y_recv,
    z_send, z_recv, tz_send, tz_recv, fin_send, fin_recv, hid_send, hid_recv, hx_send, hx_recv, hz_send, hz_recv, hf_send, hf_recv,
    small_send, small_recv, core_free,
):
    grp = lax.axis_index("grp")
    blk = lax.axis_index("blk")
    core = lax.rem(grp, 2)
    side = lax.div(grp, 2)
    yy = lax.rem(blk, 2)
    zz = lax.div(blk, 2)
    member = 2 * core + yy
    far_side = 2 * (1 - side) + core
    low = lax.broadcasted_iota(jnp.int32, (HALF, 128), 1) < DIM

    def place(c, x, z, y):
        return (2 * x + c, 2 * z + y)

    core_peer = place(1 - core, side, zz, yy)
    x_peer = place(core, 1 - side, zz, yy)
    y_peer = place(core, side, zz, 1 - yy)

    weight_copies = {}
    for layer in range(LAYERS):
        for number, (source, target) in enumerate(
            ((qkv_hbm, wqkv), (out_hbm, wout), (up_hbm, wup), (down_hbm, wdown))
        ):
            weight_copies[layer, number] = pltpu.make_async_copy(
                source.at[layer], target.at[layer], w_sem.at[layer, number]
            )
            weight_copies[layer, number].start()

    barrier = pltpu.get_barrier_semaphore()
    for step in range(1, 4):
        pl.semaphore_signal(
            barrier, inc=1, device_id=place(core, side, lax.rem(zz + step, 4), yy), device_id_type=MESH
        )
    for step in range(4):
        pl.semaphore_signal(
            barrier, inc=1, device_id=place(1 - core, side, lax.rem(zz + step, 4), yy), device_id_type=MESH
        )
    pl.semaphore_signal(barrier, inc=1, device_id=x_peer, device_id_type=MESH)
    pl.semaphore_signal(barrier, inc=1, device_id=y_peer, device_id_type=MESH)
    for peer in (
        place(1 - core, side, zz, 1 - yy),
        place(1 - core, 1 - side, zz, yy),
        place(core, 1 - side, zz, 1 - yy),
        place(1 - core, 1 - side, zz, 1 - yy),
    ):
        pl.semaphore_signal(barrier, inc=1, device_id=peer, device_id_type=MESH)

    end_second = lax.div(seq_len[0, 0] + seq_len[0, 1], RUNS)
    flag_out[...] = jnp.full((8, 128), end_second.astype(F32), F32)
    for layer in range(LAYERS):
        for head in range(OWN):
            rq[layer, head, DIM:, :] = jnp.zeros((DIM, HALF * RUNS), BF16)
    for head in range(OWN):
        ro[head, 0:DIM, :] = jnp.zeros((DIM, HALF * RUNS), BF16)

    def remote(source, target, send, recv, peer):
        return pltpu.make_async_remote_copy(
            src_ref=source,
            dst_ref=target,
            send_sem=send,
            recv_sem=recv,
            device_id=peer,
            device_id_type=MESH,
        )

    def credit(semaphore, peer):
        pl.semaphore_signal(semaphore, inc=1, device_id=peer, device_id_type=MESH)

    def moved(kind, slot, source, target, at, core_at, z_at):
        here = jnp.logical_and(core_at == core, z_at == zz)

        @pl.when(here)
        def _():
            pltpu.make_async_copy(source, target.at[at], move_recv.at[kind, at]).start()

        @pl.when(jnp.logical_not(here))
        def _():
            pltpu.make_async_remote_copy(
                src_ref=source,
                dst_ref=target.at[at],
                send_sem=move_send.at[kind, slot],
                recv_sem=move_recv.at[kind, at],
                device_id=place(core_at, side, z_at, yy),
                device_id_type=MESH,
            ).start()

    def move_left(kind, slot, source, core_at, z_at):
        here = jnp.logical_and(core_at == core, z_at == zz)

        @pl.when(jnp.logical_not(here))
        def _():
            pltpu.make_async_copy(source, source, move_send.at[kind, slot]).wait()

    def move_arrived(kind, at, target):
        pltpu.make_async_copy(target.at[at], target.at[at], move_recv.at[kind, at]).wait()

    def to_team(kind, half, source, target):
        moved(kind, half, source, target, lax.div(zz, 2), lax.rem(zz, 2), 2 * half + core)

    def to_team_left(kind, half, source):
        move_left(kind, half, source, lax.rem(zz, 2), 2 * half + core)

    def to_owner(kind, chunk, source, target):
        moved(kind, chunk, source, target, lax.div(zz, 2), lax.rem(zz, 2), core + 2 * chunk)

    def to_owner_left(kind, chunk, source):
        move_left(kind, chunk, source, lax.rem(zz, 2), core + 2 * chunk)

    def half_of(ref, half):
        return ref.at[pl.ds(pl.multiple_of(HALF * half, HALF), HALF)]

    def rows_of(half):
        return pl.ds(pl.multiple_of(half * HALF, HALF), HALF)

    def slot_of(other):
        return lax.rem(other + TEAM - member, TEAM)

    def exchange(kind, layer, half, head, outgoing, incoming):
        incoming[half, 0, head] = outgoing[half, member, head]
        for step in range(1, TEAM):
            peer = lax.rem(member + step, TEAM)
            pltpu.make_async_remote_copy(
                src_ref=outgoing.at[half, peer, head],
                dst_ref=incoming.at[half, TEAM - step, head],
                send_sem=a2a_send.at[kind, layer, half, head],
                recv_sem=a2a_recv.at[kind, layer, half, head],
                device_id=place(lax.div(peer, 2), side, zz, lax.rem(peer, 2)),
                device_id_type=MESH,
            ).start()

    def arrived(kind, layer, half, head, incoming):
        whole = incoming.at[half, pl.ds(1, TEAM - 1), head]
        pltpu.make_async_copy(whole, whole, a2a_recv.at[kind, layer, half, head]).wait()

    def left(kind, layer, half, outgoing):
        for head in range(OWN):
            whole = outgoing.at[half, pl.ds(1, TEAM - 1), head]
            pltpu.make_async_copy(whole, whole, a2a_send.at[kind, layer, half, head]).wait()

    def tokens_of(chunk, other):
        return pl.ds(pl.multiple_of(HALF * (TEAM * chunk + other), HALF), HALF)

    def hidden_copy(layer, chunk, which):
        whose = 2 * core + 1 - yy if which == 2 else member
        block = hid_all.at[layer, :, tokens_of(chunk, whose)]
        return remote(
            block,
            block,
            hid_send.at[layer, chunk, which],
            hid_recv.at[layer, chunk, which],
            y_peer if which == 0 else core_peer,
        )

    def hidden_start(layer, chunk):
        for which in range(2):
            hidden_copy(layer, chunk, which).start()

    def hidden_pass(layer, chunk):
        hidden_copy(layer, chunk, 0).wait()
        hidden_copy(layer, chunk, 2).start()

    def hidden_done(layer, chunk):
        for which in range(1, 3):
            hidden_copy(layer, chunk, which).wait()

    def project(layer, half):
        rows = rows_of(half)
        rounded = hidden[rows, :].astype(BF16)
        if layer == 1:
            left(0, 0, half, pack_out)
        queries = nn(rounded, wqkv[layer, :, 0:WIDTH]) * (DIM ** -0.5)
        queries_t = queries.T.astype(BF16)
        keys = nn(rounded, wqkv[layer, :, WIDTH : 2 * WIDTH])
        values = nn(rounded, wqkv[layer, :, 2 * WIDTH : 3 * WIDTH])
        for pair in range(RUNS // 2):
            k_pair = keys[:, 128 * pair : 128 * pair + 128]
            v_pair = values[:, 128 * pair : 128 * pair + 128]
            first = jnp.where(low, k_pair, pltpu.roll(v_pair, DIM, 1))
            other = jnp.where(low, pltpu.roll(k_pair, DIM, 1), v_pair)
            pack_out[half, pair, 0, 0:HALF, :] = first.astype(BF16)
            pack_out[half, pair, 1, 0:HALF, :] = other.astype(BF16)
        for head in range(RUNS):
            pack_out[half, head // 2, head % 2, HALF:, :] = queries_t[DIM * head : DIM * head + DIM, :]
        for head in range(OWN):
            exchange(0, layer, half, head, pack_out, pack_in)
        hid_all[layer, :, tokens_of(half, member)] = rounded.T

    def attend(layer, chunk):
        if layer == 1:
            left(1, 0, chunk, head_out)

        def one_head(head, carry):
            arrived(0, layer, chunk, head, pack_in)
            for other in range(TEAM):
                slot = slot_of(other)
                start = HALF * (TEAM * chunk + other)
                span = slice(start, start + HALF)
                block = pack_in[chunk, slot, head, 0:HALF, :]
                kv[layer, head, span, :] = block
                kv_t[layer, head, :, span] = block.T
                rq[layer, head, 0:DIM, span] = pack_in[chunk, slot, head, HALF:, :]

            def scores_of(i):
                count = TILE * (i + 1)
                tile = rq[layer, head, :, TILE * i : TILE * i + TILE]
                return nn(kv[layer, head, 0:count, :], tile) + bias[TILE * TILES - count :, :]

            ahead = [scores_of(i) for i in (2 * chunk, 2 * chunk + 1)]
            for i in (2 * chunk, 2 * chunk + 1):
                columns = slice(TILE * i, TILE * i + TILE)
                count = TILE * (i + 1)
                scores = ahead[i - 2 * chunk]
                largest = jnp.max(scores, axis=0, keepdims=True)
                weight = jnp.exp(scores - largest)
                total = jnp.sum(weight, axis=0, keepdims=True)
                summed = nn(kv_t[layer, head, DIM:, 0:count], weight.astype(BF16))
                summed = summed / total
                o_t[layer, head, :, columns] = summed
                lse[layer, head, :, columns] = largest + jnp.log(total)
                rounded = summed.astype(BF16)
                for part in range(2):
                    head_out[chunk, 2 * (i - 2 * chunk) + part, head] = rounded[
                        :, HALF * part : HALF * part + HALF
                    ]
            exchange(1, layer, chunk, head, head_out, o_in)
            return carry

        for head in range(OWN):
            one_head(head, 0)

    def feed(layer, half):
        rows = rows_of(half)
        for head in range(OWN):
            arrived(1, layer, half, head, o_in)
        for head in range(RUNS):
            attn_t[layer, DIM * head : DIM * head + DIM, rows] = o_in[half, slot_of(head // 2), head % 2]
        attn = attn_t[layer, :, rows].T
        grown = nn(attn, wout[layer])
        branch[layer, rows, :] = grown
        middle = hidden[rows, :] + alphas[layer, 0] * grown
        rounded = middle.astype(BF16)
        entered[layer, rows, :] = rounded
        total = jnp.zeros((HALF, WIDTH), F32)

        def gate_of(step):
            cut = slice(CUT * step, CUT * step + CUT)
            return nn(rounded, wup[layer, :, cut]) + up_bias[layer : layer + 1, cut]

        coming = gate_of(0)
        for step in range(FF // CUT):
            cut = slice(CUT * step, CUT * step + CUT)
            gate = coming
            if step + 1 < FF // CUT:
                coming = gate_of(step + 1)
            bell = jnp.exp(gate * gate * -0.5)
            near = pl.reciprocal(1.0 + SLOPE_AT * jnp.abs(gate), approx=True)
            tail = jnp.full_like(gate, TAIL[5])
            for factor in TAIL[4::-1]:
                tail = tail * near + factor
            tail = bell * (tail * near)
            risen = jnp.where(gate > 0.0, 1.0 - tail, tail)
            slope[layer, rows, cut] = risen + gate * bell * 0.3989422804014327
            active = (gate * risen).astype(BF16)
            act[layer, rows, cut] = active
            total = total + nn(active, wdown[layer, cut, :])
        total = total + down_bias[layer : layer + 1, :]
        second[layer, rows, :] = total
        hidden[rows, :] = middle + alphas[layer, 1] * total

    def total_of(values):
        return jnp.sum(jnp.sum(values, axis=0, keepdims=True), axis=1, keepdims=True)

    def feed_back(layer):
        start = grad[...]
        if layer == 0:
            dz[...] = (alphas[layer, 1] * start).astype(BF16)
        scaled = dz[...]
        alpha_second = total_of(start * second[layer])
        small[layer : layer + 1, FF : FF + WIDTH] = jnp.sum(scaled.astype(F32), axis=0, keepdims=True)
        middle = start
        coming = nt(scaled, wdown[layer, 0:CUT, :])
        for step in range(FF // CUT):
            cut = slice(CUT * step, CUT * step + CUT)
            raw = coming
            if step + 1 < FF // CUT:
                coming = nt(scaled, wdown[layer, CUT * (step + 1) : CUT * (step + 2), :])
            gate = (raw * slope[layer, :, cut]).astype(BF16)
            du[:, cut] = gate
            small[layer : layer + 1, cut] = jnp.sum(gate.astype(F32), axis=0, keepdims=True)
            middle = middle + nt(gate, wup[layer, :, cut])
        grad[...] = middle
        mixed = (alphas[layer, 0] * middle).astype(BF16)
        da[...] = mixed
        spread = nt(wout[layer], mixed).astype(BF16)
        for chunk in (1, 0):
            left(*((1, 1) if layer == 1 else (2, 1)), chunk, head_out)
            for head in range(RUNS):
                head_out[chunk, head // 2, head % 2] = spread[
                    DIM * head : DIM * head + DIM, HALF * chunk : HALF * chunk + HALF
                ]
            for head in range(OWN):
                exchange(2, layer, chunk, head, head_out, do_in)
        alpha_first = total_of(middle * branch[layer])
        column = lax.broadcasted_iota(jnp.int32, (1, 128), 1)
        small[layer : layer + 1, FF + WIDTH :] = jnp.where(
            column == 0, alpha_first, jnp.where(column == 1, alpha_second, 0.0)
        )

    def attend_back(layer, chunk):
        left(*((0, 1) if layer == 1 else (3, 1)), chunk, pack_out)

        def one_head(head, carry):
            arrived(2, layer, chunk, head, do_in)
            for other in range(TEAM):
                start = HALF * (TEAM * chunk + other)
                ro[head, DIM:, start : start + HALF] = do_in[chunk, slot_of(other), head]
            for i in (2 * chunk, 2 * chunk + 1):
                columns = slice(TILE * i, TILE * i + TILE)
                query_tile = rq[layer, head, :, columns]
                grad_tile = ro[head, :, columns]
                log_total = lse[layer, head, :, columns]
                delta = jnp.sum(
                    ro[head, DIM:, columns].astype(F32) * o_t[layer, head, :, columns],
                    axis=0,
                    keepdims=True,
                )
                count = TILE * (i + 1)
                keys = kv[layer, head, 0:count, :]
                weight = jnp.exp(nn(keys, query_tile) + bias[TILE * TILES - count :, :] - log_total)
                scored = (weight * (nn(keys, grad_tile) - delta)).astype(BF16)
                term = nt(scored, query_tile) + nt(weight.astype(BF16), grad_tile)
                if chunk == 1 and i == 2:
                    acc[head, 0:count, :] = term
                elif chunk == 1:
                    acc[head, 0 : count - TILE, :] += term[0 : count - TILE, :]
                    acc[head, count - TILE : count, :] = term[count - TILE :, :]
                else:
                    acc[head, 0:count, :] += term
                query_grad = nn(kv_t[layer, head, 0:DIM, 0:count], scored)
                dq_t[head, :, columns] = query_grad * (DIM ** -0.5)
            for other in range(TEAM):
                start = HALF * (TEAM * chunk + other)
                span = slice(start, start + HALF)
                pack_out[chunk, other, head, 0:HALF, :] = acc[head, span, :].astype(BF16)
                pack_out[chunk, other, head, HALF:, :] = dq_t[head, :, span].astype(BF16)
            exchange(3, layer, chunk, head, pack_out, pack_in)
            return carry

        for head in range(OWN):
            one_head(head, 0)

    def project_back(layer, half):
        for head in range(OWN):
            arrived(3, layer, half, head, pack_in)
        turned = jnp.concatenate(
            [pack_in[half, slot_of(head // 2), head % 2, HALF:, :] for head in range(RUNS)], axis=0
        )
        dqkv[:, 0:WIDTH] = turned.T
        for pair in range(RUNS // 2):
            first = pack_in[half, slot_of(pair), 0, 0:HALF, :].astype(F32)
            other = pack_in[half, slot_of(pair), 1, 0:HALF, :].astype(F32)
            k_pair = jnp.where(low, first, pltpu.roll(other, DIM, 1))
            v_pair = jnp.where(low, pltpu.roll(first, DIM, 1), other)
            dqkv[:, WIDTH + 128 * pair : WIDTH + 128 * pair + 128] = k_pair.astype(BF16)
            dqkv[:, 2 * WIDTH + 128 * pair : 2 * WIDTH + 128 * pair + 128] = v_pair.astype(BF16)
        rows = rows_of(half)
        grad[rows, :] = grad[rows, :] + nt(dqkv[...], wqkv[layer])

    def scatter_rows(layer, result, first_row):
        for run in range(RUNS):
            for quarter in range(4):
                parts[layer, quarter, run // 2, run % 2, first_row : first_row + DIM, :] = result[
                    DIM * run : DIM * run + DIM, 128 * quarter : 128 * quarter + 128
                ].astype(BF16)

    def up_grads(layer):
        turned = entered[layer].T
        for step in range(FF // CUT):
            cut = slice(CUT * step, CUT * step + CUT)
            scatter_rows(layer, nn(turned, du[:, cut]), DIM * step)
        scatter_rows(layer, nn(attn_t[layer], da[...]), 256)
        core_start(layer, UP)

    def down_grads(layer):
        for run in range(RUNS):
            result = nn(act[layer, :, TILE * run : TILE * run + TILE].T, dz[...])
            for quarter in range(4):
                parts[layer, quarter, run // 2, run % 2, 320:576, :] = result[
                    :, 128 * quarter : 128 * quarter + 128
                ].astype(BF16)
        core_start(layer, DOWN)

    def heads_grads(layer):
        for chunk in range(2):
            hidden_done(layer, chunk)
        blocks = [(run // TEAM, run % TEAM) for run in range(RUNS)]
        keys_values = jnp.concatenate(
            [
                jnp.concatenate([pack_out[chunk, other, head, 0:HALF, :] for chunk, other in blocks], axis=0)
                for head in range(OWN)
            ],
            axis=1,
        )
        queries = jnp.concatenate(
            [
                jnp.concatenate([pack_out[chunk, other, head, HALF:, :] for chunk, other in blocks], axis=1)
                for head in range(OWN)
            ],
            axis=0,
        )
        both = nn(hid_all[layer], keys_values)
        q_part = nt(hid_all[layer], queries)
        first, other = both[:, 0:128], both[:, 128:256]
        left_half = lax.broadcasted_iota(jnp.int32, (WIDTH, 128), 1) < DIM
        k_part = jnp.where(left_half, first, pltpu.roll(other, DIM, 1))
        v_part = jnp.where(left_half, pltpu.roll(first, DIM, 1), other)
        for number, values in enumerate((q_part, k_part, v_part)):
            for run in range(RUNS):
                heads_out[layer, run // 2, run % 2, :, 128 * number : 128 * number + 128] = values[
                    DIM * run : DIM * run + DIM, :
                ].astype(BF16)
        heads_x_copy(layer).start()

    def half_rows(which):
        return pl.ds(pl.multiple_of(32 * which, 32), 32)

    def heads_x_copy(layer):
        return remote(
            heads_out.at[layer, :, :, half_rows(1 - side)],
            heads_x.at[layer],
            hx_send.at[layer],
            hx_recv.at[layer],
            x_peer,
        )

    def heads_z_copy(layer, step):
        peer = lax.rem(zz + step, 4)
        return remote(
            heads_out.at[layer, peer, :, half_rows(side)],
            heads_z.at[layer, 4 - step],
            hz_send.at[layer, step],
            hz_recv.at[layer, 4 - step],
            place(core, side, peer, yy),
        )

    def heads_last_copy(layer, number):
        x, c, y = number // 4, number // 2 % 2, number % 2
        return remote(
            heads_sum.at[layer, 1 - yy if y else yy],
            heads_all.at[layer, side, member],
            hf_send.at[layer, number],
            hf_recv.at[layer, number],
            place(1 - core if c else core, 1 - side if x else side, zz, 1 - yy if y else yy),
        )

    def heads_second(layer):
        heads_x_copy(layer).wait()
        heads_out[layer, :, :, half_rows(side), :] += heads_x[layer]
        for step in range(1, 4):
            heads_z_copy(layer, step).start()

    def heads_third(layer):
        for step in range(1, 4):
            heads_z_copy(layer, step).wait()
        total = heads_out[layer, zz, :, half_rows(side), :].astype(F32)
        for slot in range(1, 4):
            total = total + heads_z[layer, slot].astype(F32)
        heads_sum[layer] = total.astype(BF16)
        heads_all[layer, side, member] = heads_sum[layer, yy]
        for number in range(1, 8):
            heads_last_copy(layer, number).start()

    def heads_done(layer):
        for number in range(1, 8):
            heads_last_copy(layer, number).wait()

    def chunk_rows(layer, part, route):
        first, _, count = SPANS[layer, part, route]
        return pl.ds(first, count)

    def route_rows(layer, part, route):
        _, first, count = SPANS[layer, part, route]
        return pl.ds(first, count)

    def rows_in(layer, part, route):
        return chunk_rows(layer, part, route), route_rows(layer, part, route)

    def used(layer, part, route):
        return SHARES[layer, part][route] > 0

    def core_copy(layer, part, across):
        rows = pl.ds(*PARTS[part])
        return remote(
            parts.at[layer, 2 * across + 1 - core, :, :, rows],
            core_in.at[across, :, :, rows],
            core_send.at[layer, part, across],
            core_recv.at[layer, part, across],
            core_peer,
        )

    def x_copy(layer, part, route):
        rows, room = rows_in(layer, part, route)
        ends = (x_send.at[layer, part, route], x_recv.at[layer, part, route], x_peer)
        if route == 0:
            return remote(parts.at[layer, far_side, :, :, rows], xa_in.at[:, :, room], *ends)
        if route == 1:
            return remote(parts.at[layer, far_side, :, yy, rows], xb_in.at[:, room], *ends)
        return remote(parts.at[layer, far_side, zz, :, rows], third_x.at[:, room], *ends)

    def y_copy(layer, part, route, across=0):
        rows, room = rows_in(layer, part, route)
        which = (layer, part, route + across)
        if route == 2:
            which = (layer, part, 3)
        ends = (y_send.at[which], y_recv.at[which], y_peer)
        if route == 0:
            return remote(parts.at[layer, grp, :, 1 - yy, rows], ya_in.at[:, room], *ends)
        if route == 1:
            return remote(parts.at[layer, 2 * across + core, :, 1 - yy, rows], yb_in.at[across, :, room], *ends)
        return remote(parts.at[layer, grp, zz, 1 - yy, rows], third_y.at[room], *ends)

    def z_copy(layer, part, route, step):
        rows = chunk_rows(layer, part, route)
        peer = lax.rem(zz + step, 4)
        return remote(
            parts.at[layer, grp, peer, yy, rows],
            z_in.at[layer, 4 - step, rows],
            z_send.at[layer, part, route, step],
            z_recv.at[layer, part, route, 4 - step],
            place(core, side, peer, yy),
        )

    def third_z_copy(layer, part, across, step):
        rows, room = rows_in(layer, part, 2)
        peer = lax.rem(zz + step, 4)
        return remote(
            parts.at[layer, 2 * across + core, peer, :, rows],
            third_z.at[across, 4 - step, :, room],
            tz_send.at[layer, part, across, step],
            tz_recv.at[layer, part, across, 4 - step],
            place(core, side, peer, yy),
        )

    def final_copy(layer, part, which):
        block = final.at[layer, far_side if which == 2 else grp, pl.ds(*PARTS[part])]
        return remote(
            block,
            block,
            fin_send.at[layer, part, which],
            fin_recv.at[layer, part, which],
            x_peer if which == 0 else core_peer,
        )

    def core_start(layer, part):
        if layer == 0:
            pl.semaphore_wait(core_free.at[part], 1)
        for across in range(2):
            core_copy(layer, part, across).start()

    def core_done(layer, part):
        rows = pl.ds(*PARTS[part])
        for across in range(2):
            core_copy(layer, part, across).wait()
        for across in (1 - side, side):
            parts[layer, 2 * across + core, :, :, rows, :] += core_in[across, :, :, rows, :]
            if used(layer, part, 0) and across is not side:
                x_copy(layer, part, 0).start()
            if used(layer, part, 1):
                y_copy(layer, part, 1, across).start()
            if used(layer, part, 2):
                for step in range(1, 4):
                    third_z_copy(layer, part, across, step).start()
        if layer == 1:
            credit(core_free.at[part], core_peer)

    def first_x(layer, part):
        if used(layer, part, 0):
            rows, room = rows_in(layer, part, 0)
            x_copy(layer, part, 0).wait()
            for y in (1 - yy, yy):
                parts[layer, grp, :, y, rows, :] += xa_in[:, y, room, :]
                if y is not yy:
                    y_copy(layer, part, 0).start()

    def first_y(layer, part):
        if used(layer, part, 1):
            rows, room = rows_in(layer, part, 1)
            for across in (1 - side, side):
                y_copy(layer, part, 1, across).wait()
            for across in (1 - side, side):
                parts[layer, 2 * across + core, :, yy, rows, :] += yb_in[across, :, room, :]
                if across is not side:
                    x_copy(layer, part, 1).start()

    def first_z(layer, part):
        if used(layer, part, 2):
            rows, room = rows_in(layer, part, 2)
            for across in (1 - side, side):
                for step in range(1, 4):
                    third_z_copy(layer, part, across, step).wait()
                total = parts[layer, 2 * across + core, zz, :, rows, :].astype(F32)
                for slot in range(1, 4):
                    total = total + third_z[across, slot, :, room, :].astype(F32)
                parts[layer, 2 * across + core, zz, :, rows, :] = total.astype(BF16)
                if across is not side:
                    x_copy(layer, part, 2).start()

    def second_x(layer, part):
        if used(layer, part, 0):
            rows, room = rows_in(layer, part, 0)
            y_copy(layer, part, 0).wait()
            parts[layer, grp, :, yy, rows, :] += ya_in[:, room, :]
            for step in range(1, 4):
                z_copy(layer, part, 0, step).start()

    def second_y(layer, part):
        if used(layer, part, 1):
            rows, room = rows_in(layer, part, 1)
            x_copy(layer, part, 1).wait()
            parts[layer, grp, :, yy, rows, :] += xb_in[:, room, :]
            for step in range(1, 4):
                z_copy(layer, part, 1, step).start()

    def second_z(layer, part):
        if used(layer, part, 2):
            rows, room = rows_in(layer, part, 2)
            x_copy(layer, part, 2).wait()
            for y in (1 - yy, yy):
                parts[layer, grp, zz, y, rows, :] += third_x[y, room, :]
                if y is not yy:
                    y_copy(layer, part, 2).start()

    def third_done(layer, part):
        for route in range(3):
            if not used(layer, part, route):
                continue
            rows, room = rows_in(layer, part, route)
            if route == 2:
                y_copy(layer, part, 2).wait()
                final[layer, grp, rows, :] = parts[layer, grp, zz, yy, rows, :] + third_y[room, :]
            else:
                for step in range(1, 4):
                    z_copy(layer, part, route, step).wait()
                total = parts[layer, grp, zz, yy, rows, :].astype(F32)
                for slot in range(1, 4):
                    total = total + z_in[layer, slot, rows, :].astype(F32)
                final[layer, grp, rows, :] = total.astype(BF16)
        for which in range(2):
            final_copy(layer, part, which).start()

    def final_pass(layer, part):
        final_copy(layer, part, 0).wait()
        final_copy(layer, part, 2).start()

    def final_done(layer, part):
        for which in range(1, 3):
            final_copy(layer, part, which).wait()

    def small_copy(stage):
        peer = (core_peer, x_peer, y_peer)[stage]
        return remote(
            small_sum.at[stage], small_in.at[stage], small_send.at[stage], small_recv.at[stage], peer
        )

    def small_z_copy(step):
        return remote(
            small_z.at[zz],
            small_z.at[zz],
            small_send.at[2 + step],
            small_recv.at[2 + step],
            place(core, side, lax.rem(zz + step, 4), yy),
        )

    def small_start():
        small_sum[0] = small[...]
        small_copy(0).start()

    def small_next(stage):
        small_copy(stage).wait()
        total = small_sum[stage] + small_in[stage]
        if stage < 2:
            small_sum[stage + 1] = total
            small_copy(stage + 1).start()
        else:
            small_z[zz] = total
            for step in range(1, 4):
                small_z_copy(step).start()

    def small_done():
        for step in range(1, 4):
            small_z_copy(step).wait()
        small_sum[0] = (small_z[0] + small_z[1]) + (small_z[2] + small_z[3])
        small_final[:, 0:256] = small_sum[0, :, pl.ds(pl.multiple_of(blk * 256, 256), 256)]
        pair = small_sum[0, :, pl.ds(pl.multiple_of(FF + 128 * zz, 128), 128)]
        small_final[:, 256:384] = jnp.where(yy == 1, pltpu.roll(pair, DIM, 1), pair)
        small_final[:, 384:512] = small_sum[0, :, FF + WIDTH :]

    def halves(*phases, first=0):
        def both(step, carry):
            for phase in phases:
                phase(lax.rem(step + first, 2))
            return carry

        lax.fori_loop(0, 2, both, 0)

    def begin(half):
        move_arrived(0, half, tok_in)
        hidden[rows_of(half), :] = tok_in[half].astype(F32)

    def finish(half):
        back_out[0, half] = hidden[rows_of(half), :].astype(BF16)
        to_owner(3, half, back_out.at[0, half], out_in)

    def turn_round(layer, half):
        move_arrived(2, half, cot_in)
        rows = rows_of(half)
        grad[rows, :] = cot_in[half].astype(F32)
        dz[rows, :] = (alphas[layer, 1] * grad[rows, :]).astype(BF16)

    def hand_back(half):
        back_out[1, half] = grad[rows_of(half), :].astype(BF16)
        to_owner(4, half, back_out.at[1, half], grad_in)

    pl.semaphore_wait(barrier, 13)
    upper = lax.div(zz, 2)
    for half in (1 - upper, upper):
        to_team(0, half, half_of(tokens, half), tok_in)
    for half in (1 - upper, upper):
        to_team(1, half, flag_out, flag_in)
    weight_copies[0, 0].wait()
    halves(begin, functools.partial(project, 0), first=upper)
    for half in (1 - upper, upper):
        to_team(2, half, half_of(cotangent, half), cot_in)

    move_arrived(1, 0, flag_in)
    move_arrived(1, 1, flag_in)
    border = jnp.concatenate([flag_in[0, 0:1, :]] * 2, axis=1) - (HALF * lax.div(zz, 2)).astype(F32)
    key_row = lax.broadcasted_iota(jnp.int32, (TILE, TILE), 0)
    query_col = lax.broadcasted_iota(jnp.int32, (TILE, TILE), 1)
    later = key_row > query_col
    key_sub = lax.rem(key_row, HALF).astype(F32) >= border
    query_sub = lax.rem(query_col, HALF).astype(F32) >= border
    apart = jnp.logical_xor(key_sub, query_sub)
    for tile in range(TILES - 1):
        bias[TILE * tile : TILE * tile + TILE, :] = jnp.where(apart, NEGATIVE, 0.0)
    bias[TILE * (TILES - 1) :, :] = jnp.where(jnp.logical_or(later, apart), NEGATIVE, 0.0)

    for number in range(1, 4):
        weight_copies[0, number].wait()
    attend(0, 0)
    attend(0, 1)
    hidden_start(0, 0)
    weight_copies[1, 0].wait()
    halves(functools.partial(feed, 0), functools.partial(project, 1))
    for number in range(1, 4):
        weight_copies[1, number].wait()
    attend(1, 0)
    attend(1, 1)
    hidden_pass(0, 0)
    hidden_start(1, 0)
    halves(functools.partial(feed, 1), finish)
    hidden_start(0, 1)
    hidden_start(1, 1)
    hidden_pass(1, 0)

    halves(functools.partial(turn_round, 1))
    down_grads(1)
    feed_back(1)
    hidden_pass(0, 1)
    hidden_pass(1, 1)
    core_done(1, DOWN)
    up_grads(1)
    attend_back(1, 1)
    first_y(1, DOWN)
    core_done(1, UP)
    attend_back(1, 0)
    second_y(1, DOWN)
    first_y(1, UP)
    first_x(1, DOWN)
    project_back(1, 1)
    heads_grads(1)
    first_z(1, DOWN)
    project_back(1, 0)
    feed_back(0)
    small_start()
    second_x(1, DOWN)
    second_y(1, UP)
    up_grads(0)
    first_x(1, UP)
    heads_second(1)
    first_z(1, UP)
    attend_back(0, 1)
    small_next(0)
    core_done(0, UP)
    second_x(1, UP)
    down_grads(0)
    attend_back(0, 0)
    small_next(1)
    project_back(0, 1)
    hand_back(1)
    first_z(0, UP)
    heads_grads(0)
    small_next(2)
    first_x(0, UP)
    core_done(0, DOWN)
    first_y(0, UP)
    heads_second(0)
    small_done()
    first_z(0, DOWN)
    second_x(0, UP)
    first_x(0, DOWN)
    second_z(0, UP)
    second_z(1, UP)
    heads_third(1)
    second_z(1, DOWN)
    first_y(0, DOWN)
    heads_third(0)
    second_y(0, UP)
    second_x(0, DOWN)
    second_z(0, DOWN)
    third_done(1, UP)
    third_done(0, UP)
    second_y(0, DOWN)
    project_back(0, 0)
    hand_back(0)
    heads_done(1)
    third_done(1, DOWN)
    third_done(0, DOWN)
    final_pass(1, UP)
    final_pass(0, UP)
    final_pass(1, DOWN)
    final_pass(0, DOWN)
    for half in range(2):
        move_arrived(3, half, out_in)
        move_arrived(4, half, grad_in)
    final_done(0, UP)
    final_done(1, DOWN)
    heads_done(0)
    final_done(1, UP)
    final_done(0, DOWN)

    for half in range(2):
        left(2, 0, half, head_out)
        left(3, 0, half, pack_out)
        to_team_left(0, half, half_of(tokens, half))
        to_team_left(1, half, flag_out)
        to_team_left(2, half, half_of(cotangent, half))
        to_owner_left(3, half, back_out.at[0, half])
        to_owner_left(4, half, back_out.at[1, half])


def results_kernel(
    final, heads, out_block, grad_block, small,
    output, input_grad, qkv_grad, out_grad, up_grad, up_bias_grad, down_grad, down_bias_grad, alpha_grad,
    out_flat, grad_wide, qkv_wide, out_wide, up_wide, down_wide, out_sem,
):
    ends = []

    def write(source, target):
        ends.append(pltpu.make_async_copy(source, target, out_sem.at[len(ends)]))
        ends[-1].start()

    up_bias_grad[...] = small[:, 0:256]
    down_bias_grad[...] = small[:, 256 : 256 + DIM]
    alpha_grad[...] = small[:, 384:386]
    for layer, part in [(layer, part) for layer in range(LAYERS) for part in (UP, DOWN)]:
        for quarter in range(4):

            def block(first, count):
                return final[layer, quarter, first : first + count, :].astype(F32)

            def columns(step):
                return slice(WIDTH * step + 128 * quarter, WIDTH * step + 128 * quarter + 128)

            if part == UP:
                for step in range(4):
                    up_wide[layer, :, columns(step)] = block(DIM * step, DIM)
                out_wide[layer, :, columns(0)] = block(256, DIM)
            else:
                down_wide[layer, :, columns(0)] = block(320, 256)
        if part == UP:
            write(up_wide.at[layer], up_grad.at[layer])
            write(out_wide.at[layer], out_grad.at[layer])
        else:
            write(down_wide.at[layer], down_grad.at[layer])
    for half in range(2):
        rows = slice(HALF * half, HALF * half + HALF)
        grad_wide[rows, :] = grad_block[half].astype(F32)
        out_flat[rows, :] = out_block[half]
    write(grad_wide, input_grad)
    write(out_flat, output)
    for layer in range(LAYERS):
        for side in range(2):
            for member in range(TEAM):
                for step in range(3):
                    at = WIDTH * step + 128 * member
                    qkv_wide[layer, 32 * side : 32 * side + 32, at : at + 128] = heads[
                        layer, side, member, :, 128 * step : 128 * step + 128
                    ].astype(F32)
        write(qkv_wide.at[layer], qkv_grad.at[layer])
    for end in ends:
        end.wait()


def fast_body(
    tokens, seq_len, qkv_weight, out_weight, up_weight, up_bias, down_weight, down_bias, alphas, cotangent
):
    whole = pl.BlockSpec(memory_space=pltpu.VMEM)
    scalar = pl.BlockSpec(memory_space=pltpu.SMEM)
    far = pl.BlockSpec(memory_space=pl.ANY)
    shape = jax.ShapeDtypeStruct
    rows = HALF * RUNS

    def vmem(*dims):
        return pltpu.VMEM(dims, BF16)

    def wide(*dims):
        return pltpu.VMEM(dims, F32)

    dma = pltpu.SemaphoreType.DMA
    final, heads, out_block, grad_block, small = pl.pallas_call(
        layers_kernel,
        out_shape=(
            vmem(LAYERS, 4, CHUNK, 128),
            vmem(LAYERS, 2, TEAM, DIM // 2, 3 * 128),
            vmem(2, HALF, WIDTH),
            vmem(2, HALF, WIDTH),
            wide(LAYERS, WIDTH),
        ),
        in_specs=[far, scalar, scalar, whole, whole, far, far, far, far, far],
        out_specs=(whole,) * 5,
        scratch_shapes=[
            vmem(LAYERS, WIDTH, 3 * WIDTH),
            vmem(LAYERS, WIDTH, WIDTH),
            vmem(LAYERS, WIDTH, FF),
            vmem(LAYERS, FF, WIDTH),
            vmem(2, HALF, WIDTH),
            vmem(2, HALF, WIDTH),
            wide(8, 128),
            wide(2, 8, 128),
            vmem(2, 2, HALF, WIDTH),
            wide(2 * HALF, WIDTH),
            wide(2 * HALF, WIDTH),
            vmem(LAYERS, WIDTH, rows),
            vmem(LAYERS, WIDTH, 2 * HALF),
            vmem(LAYERS, 2 * HALF, WIDTH),
            vmem(LAYERS, 2 * HALF, FF),
            wide(LAYERS, 2 * HALF, WIDTH),
            wide(LAYERS, 2 * HALF, FF),
            wide(LAYERS, 2 * HALF, WIDTH),
            vmem(2 * HALF, WIDTH),
            vmem(2 * HALF, FF),
            vmem(2 * HALF, WIDTH),
            vmem(HALF, 3 * WIDTH),
            vmem(2, TEAM, OWN, PACK, 128),
            vmem(2, TEAM, OWN, DIM, 128),
            vmem(2, TEAM, OWN, PACK, 128),
            vmem(2, TEAM, OWN, DIM, 128),
            vmem(2, TEAM, OWN, DIM, 128),
            vmem(LAYERS, OWN, rows, 128),
            vmem(LAYERS, OWN, 128, rows),
            vmem(LAYERS, OWN, 128, rows),
            vmem(OWN, 128, rows),
            wide(LAYERS, OWN, DIM, rows),
            wide(LAYERS, OWN, 1, rows),
            wide(OWN, rows, 128),
            wide(OWN, DIM, rows),
            wide(rows, TILE),
            vmem(LAYERS, 4, 4, 2, CHUNK, 128),
            vmem(2, 4, 2, CHUNK, 128),
            vmem(4, 2, TOTALS[0], 128),
            vmem(4, TOTALS[1], 128),
            vmem(4, TOTALS[0], 128),
            vmem(2, 4, TOTALS[1], 128),
            vmem(LAYERS, 4, CHUNK, 128),
            vmem(2, 4, 2, TOTALS[2], 128),
            vmem(2, TOTALS[2], 128),
            vmem(TOTALS[2], 128),
            vmem(LAYERS, 4, 2, DIM, 3 * 128),
            vmem(LAYERS, 4, 2, DIM // 2, 3 * 128),
            vmem(LAYERS, 4, 2, DIM // 2, 3 * 128),
            vmem(LAYERS, 2, DIM // 2, 3 * 128),
            wide(LAYERS, SMALL),
            wide(3, LAYERS, SMALL),
            wide(4, LAYERS, SMALL),
            wide(3, LAYERS, SMALL),
            dma((LAYERS, 4)),
            dma((5, 2)),
            dma((5, 2)),
            dma((4, LAYERS, 2, OWN)),
            dma((4, LAYERS, 2, OWN)),
            dma((LAYERS, 2, 2)),
            dma((LAYERS, 2, 2)),
            dma((LAYERS, 2, 3)),
            dma((LAYERS, 2, 3)),
            dma((LAYERS, 2, 4)),
            dma((LAYERS, 2, 4)),
            dma((LAYERS, 2, 2, 4)),
            dma((LAYERS, 2, 2, 4)),
            dma((LAYERS, 2, 2, 4)),
            dma((LAYERS, 2, 2, 4)),
            dma((LAYERS, 2, 3)),
            dma((LAYERS, 2, 3)),
            dma((LAYERS, 2, 3)),
            dma((LAYERS, 2, 3)),
            dma((LAYERS,)),
            dma((LAYERS,)),
            dma((LAYERS, 4)),
            dma((LAYERS, 4)),
            dma((LAYERS, 8)),
            dma((LAYERS, 8)),
            dma((6,)),
            dma((6,)),
            pltpu.SemaphoreType.REGULAR((2,)),
        ],
        compiler_params=pltpu.CompilerParams(
            collective_id=0, has_side_effects=True, vmem_limit_bytes=61 * 1024 * 1024
        ),
        name="layers",
    )(
        tokens, seq_len, alphas, up_bias, down_bias, cotangent,
        qkv_weight, out_weight, up_weight, down_weight,
    )
    return tuple(
        pl.pallas_call(
            results_kernel,
            out_shape=(
                shape((2 * HALF, WIDTH), BF16),
                shape((2 * HALF, WIDTH), F32),
                shape((LAYERS, DIM, 3 * WIDTH), F32),
                shape((LAYERS, DIM, WIDTH), F32),
                shape((LAYERS, DIM, FF), F32),
                shape((LAYERS, FF // RUNS), F32),
                shape((LAYERS, FF // RUNS, WIDTH), F32),
                shape((LAYERS, DIM), F32),
                shape((LAYERS, 2), F32),
            ),
            in_specs=[whole] * 5,
            out_specs=(far, far, far, far, far, whole, far, whole, whole),
            scratch_shapes=[
                vmem(2 * HALF, WIDTH),
                wide(2 * HALF, WIDTH),
                wide(LAYERS, DIM, 3 * WIDTH),
                wide(LAYERS, DIM, WIDTH),
                wide(LAYERS, DIM, FF),
                wide(LAYERS, FF // RUNS, WIDTH),
                dma((10,)),
            ],
            compiler_params=pltpu.CompilerParams(vmem_limit_bytes=24 * 1024 * 1024),
            name="results",
        )(final, heads, out_block, grad_block, small)
    )


def layout(seq_len, local_count, cycle_size):
    piece_rows = seq_len[0] // cycle_size
    end_rows = jnp.cumsum(piece_rows)
    start_rows = end_rows - piece_rows
    local_rows = jnp.arange(local_count, dtype=jnp.int32)
    segment = jnp.sum((local_rows[:, None] >= end_rows[None, :]).astype(jnp.int32), axis=1)
    picked = segment[:, None] == jnp.arange(seq_len.shape[1], dtype=jnp.int32)[None, :]
    offset = local_rows - jnp.sum(jnp.where(picked, start_rows[None, :], 0), axis=1)
    span_rows = jnp.sum(jnp.where(picked, piece_rows[None, :], 0), axis=1)
    return (segment, offset, span_rows)


def gelu_exact(values):
    return jax.nn.gelu(values, approximate=False)


def key_block(whole, geometry, block_index, head_count):
    query_seg, query_pos, seg_all, pos_all, block_rows, score_scale = geometry
    first_row = block_index * block_rows
    key_piece = lax.dynamic_slice_in_dim(whole, first_row, block_rows, 0)
    key_seg = lax.dynamic_slice_in_dim(seg_all, first_row, block_rows, 0)
    key_pos = lax.dynamic_slice_in_dim(pos_all, first_row, block_rows, 0)
    half_width = key_piece.shape[1] // 2
    keys_part = key_piece[:, :half_width].reshape(block_rows, head_count, -1)
    values_part = key_piece[:, half_width:].reshape(block_rows, head_count, -1)
    return (keys_part, values_part, key_seg, key_pos)


def block_scores(queries, keys_part, key_seg, key_pos, geometry):
    query_seg, query_pos, seg_all, pos_all, block_rows, score_scale = geometry
    scores = (
        jnp.einsum("qhd,khd->hqk", queries, keys_part, preferred_element_type=jnp.float32)
        * score_scale
    )
    allowed = (query_seg[:, None] == key_seg[None, :]) & (key_pos[None, :] <= query_pos[:, None])
    return (scores, allowed[None])


def attend(queries, whole, geometry):
    row_count, head_count, head_dim = queries.shape
    block_count = whole.shape[0] // geometry[4]

    def statistics(running, block_index):
        largest, totals = running
        keys_part, values_part, key_seg, key_pos = key_block(
            whole, geometry, block_index, head_count
        )
        scores, allowed = block_scores(queries, keys_part, key_seg, key_pos, geometry)
        newest = jnp.maximum(largest, jnp.max(jnp.where(allowed, scores, NEGATIVE), axis=2))
        weights = jnp.where(allowed, jnp.exp(scores - newest[:, :, None]), 0.0)
        totals = totals * jnp.exp(largest - newest) + jnp.sum(weights, axis=2)
        return ((newest, totals), None)

    initial = (
        jnp.full((head_count, row_count), NEGATIVE, jnp.float32),
        jnp.zeros((head_count, row_count), jnp.float32),
    )
    (largest, totals), unused = lax.scan(statistics, initial, jnp.arange(block_count))
    log_total = largest + jnp.log(totals)

    def weighted(output_sum, block_index):
        keys_part, values_part, key_seg, key_pos = key_block(
            whole, geometry, block_index, head_count
        )
        scores, allowed = block_scores(queries, keys_part, key_seg, key_pos, geometry)
        probs = jnp.where(allowed, jnp.exp(scores - log_total[:, :, None]), 0.0).astype(
            jnp.bfloat16
        )
        output_sum = output_sum + jnp.einsum(
            "hqk,khd->qhd", probs, values_part, preferred_element_type=jnp.float32
        )
        return (output_sum, None)

    output_sum, unused = lax.scan(
        weighted, jnp.zeros((row_count, head_count, head_dim), jnp.float32), jnp.arange(block_count)
    )
    return (output_sum, log_total)


def attend_back(queries, whole, log_total, delta_sum, grad_heads, geometry):
    row_count, head_count, head_dim = queries.shape
    block_rows = geometry[4]
    score_scale = geometry[5]
    block_count = whole.shape[0] // block_rows

    def gradients(query_grad, block_index):
        keys_part, values_part, key_seg, key_pos = key_block(
            whole, geometry, block_index, head_count
        )
        scores, allowed = block_scores(queries, keys_part, key_seg, key_pos, geometry)
        probs = jnp.where(allowed, jnp.exp(scores - log_total[:, :, None]), 0.0)
        grad_probs = jnp.einsum(
            "qhd,khd->hqk", grad_heads, values_part, preferred_element_type=jnp.float32
        )
        grad_scores = (probs * (grad_probs - delta_sum[:, :, None])).astype(jnp.bfloat16)
        query_grad = (
            query_grad
            + jnp.einsum("hqk,khd->qhd", grad_scores, keys_part, preferred_element_type=jnp.float32)
            * score_scale
        )
        key_grad = (
            jnp.einsum("hqk,qhd->khd", grad_scores, queries, preferred_element_type=jnp.float32)
            * score_scale
        )
        value_grad = jnp.einsum(
            "hqk,qhd->khd",
            probs.astype(jnp.bfloat16),
            grad_heads,
            preferred_element_type=jnp.float32,
        )
        joined = jnp.concatenate(
            [key_grad.reshape(block_rows, -1), value_grad.reshape(block_rows, -1)], axis=1
        )
        return (query_grad, joined)

    query_grad, stacked = lax.scan(
        gradients,
        jnp.zeros((row_count, head_count, head_dim), jnp.float32),
        jnp.arange(block_count),
    )
    return (query_grad, stacked.reshape(whole.shape[0], -1))


def layer_forward(hidden, layer_index, weights, geometry):
    qkv_weight, out_weight, up_weight, up_bias, down_weight, down_bias, alphas = weights
    row_count, model_width = hidden.shape
    projection = qkv_weight[layer_index]
    rounded = hidden.astype(jnp.bfloat16)
    queries = (
        jnp.dot(rounded, projection[:, :model_width], preferred_element_type=jnp.float32)
        .astype(jnp.bfloat16)
        .reshape(row_count, HEADS, -1)
    )
    key_value = jnp.dot(
        rounded, projection[:, model_width:], preferred_element_type=jnp.float32
    ).astype(jnp.bfloat16)
    whole = lax.all_gather(key_value, "blk", axis=0, tiled=True)
    heads_out, log_total = attend(queries, whole, geometry)
    heads_rounded = heads_out.reshape(row_count, model_width).astype(jnp.bfloat16)
    branch = jnp.dot(heads_rounded, out_weight[layer_index], preferred_element_type=jnp.float32)
    alpha_pair = alphas[layer_index]
    middle = hidden + alpha_pair[0] * branch
    entered = middle.astype(jnp.bfloat16)
    gate_pre = (
        jnp.dot(entered, up_weight[layer_index], preferred_element_type=jnp.float32)
        + up_bias[layer_index]
    )
    activated = gelu_exact(gate_pre).astype(jnp.bfloat16)
    second = (
        jnp.dot(activated, down_weight[layer_index], preferred_element_type=jnp.float32)
        + down_bias[layer_index]
    )
    result = middle + alpha_pair[1] * second
    saved = (
        rounded,
        queries,
        key_value,
        whole,
        heads_out,
        heads_rounded,
        log_total,
        branch,
        entered,
        gate_pre,
        activated,
        second,
    )
    return (result, saved)


def layer_backward(grad_hidden, saved, layer_index, weights, geometry):
    qkv_weight, out_weight, up_weight, up_bias, down_weight, down_bias, alphas = weights
    (
        rounded,
        queries,
        key_value,
        saved_whole,
        heads_out,
        heads_rounded,
        log_total,
        branch,
        entered,
        gate_pre,
        activated,
        second,
    ) = saved
    row_count = grad_hidden.shape[0]
    alpha_pair = alphas[layer_index]
    grad_second = (alpha_pair[1] * grad_hidden).astype(jnp.bfloat16)
    alpha_second = jnp.sum(grad_hidden * second)
    bias_down = jnp.sum(grad_second.astype(jnp.float32), axis=0)
    grad_down = jnp.einsum("tf,td->fd", activated, grad_second, preferred_element_type=jnp.float32)
    grad_act = jnp.einsum(
        "td,fd->tf", grad_second, down_weight[layer_index], preferred_element_type=jnp.float32
    )
    unused, gelu_pull = jax.vjp(gelu_exact, gate_pre)
    grad_gate = gelu_pull(grad_act)[0].astype(jnp.bfloat16)
    bias_up = jnp.sum(grad_gate.astype(jnp.float32), axis=0)
    grad_up = jnp.einsum("td,tf->df", entered, grad_gate, preferred_element_type=jnp.float32)
    grad_middle = grad_hidden + jnp.einsum(
        "tf,df->td", grad_gate, up_weight[layer_index], preferred_element_type=jnp.float32
    )
    grad_branch = (alpha_pair[0] * grad_middle).astype(jnp.bfloat16)
    alpha_first = jnp.sum(grad_middle * branch)
    grad_proj_out = jnp.einsum(
        "te,td->ed", heads_rounded, grad_branch, preferred_element_type=jnp.float32
    )
    grad_heads = (
        jnp.einsum(
            "td,ed->te", grad_branch, out_weight[layer_index], preferred_element_type=jnp.float32
        )
        .astype(jnp.bfloat16)
        .reshape(queries.shape)
    )
    delta_sum = jnp.sum(grad_heads.astype(jnp.float32) * heads_out, axis=2).T
    whole = lax.all_gather(key_value, "blk", axis=0, tiled=True)
    query_grad, key_terms = attend_back(queries, whole, log_total, delta_sum, grad_heads, geometry)
    key_grads = lax.psum_scatter(
        key_terms.astype(jnp.bfloat16), "blk", scatter_dimension=0, tiled=True
    )
    grad_proj = jnp.concatenate(
        [query_grad.reshape(row_count, -1).astype(jnp.bfloat16), key_grads], axis=1
    )
    grad_qkv = jnp.einsum("td,te->de", rounded, grad_proj, preferred_element_type=jnp.float32)
    grad_input = grad_middle + jnp.einsum(
        "te,de->td", grad_proj, qkv_weight[layer_index], preferred_element_type=jnp.float32
    )
    layer_grads = (
        grad_qkv,
        grad_proj_out,
        grad_up,
        bias_up,
        grad_down,
        bias_down,
        jnp.stack([alpha_first, alpha_second]),
    )
    return (grad_input, layer_grads)


def reduce_all(layer_results, cycle_size):
    stacked = [
        jnp.stack([layer_entry[member] for layer_entry in layer_results], axis=0)
        for member in range(6)
    ]
    alpha_tiles = jnp.stack(
        [jnp.tile(layer_entry[6], cycle_size) for layer_entry in layer_results], axis=0
    )
    shares = (
        lax.psum_scatter(
            stacked[0].astype(jnp.bfloat16), "blk", scatter_dimension=1, tiled=True
        ).astype(jnp.float32),
        lax.psum_scatter(
            stacked[1].astype(jnp.bfloat16), "blk", scatter_dimension=1, tiled=True
        ).astype(jnp.float32),
        lax.psum_scatter(
            stacked[2].astype(jnp.bfloat16), "blk", scatter_dimension=1, tiled=True
        ).astype(jnp.float32),
        lax.psum_scatter(
            stacked[3].astype(jnp.bfloat16), "blk", scatter_dimension=1, tiled=True
        ).astype(jnp.float32),
        lax.psum_scatter(
            stacked[4].astype(jnp.bfloat16), "blk", scatter_dimension=1, tiled=True
        ).astype(jnp.float32),
        lax.psum_scatter(
            stacked[5].astype(jnp.bfloat16), "blk", scatter_dimension=1, tiled=True
        ).astype(jnp.float32),
        lax.psum_scatter(
            alpha_tiles.astype(jnp.bfloat16), "blk", scatter_dimension=1, tiled=True
        ).astype(jnp.float32),
    )
    return (
        lax.psum(shares[0].astype(jnp.bfloat16), "grp").astype(jnp.float32),
        lax.psum(shares[1].astype(jnp.bfloat16), "grp").astype(jnp.float32),
        lax.psum(shares[2].astype(jnp.bfloat16), "grp").astype(jnp.float32),
        lax.psum(shares[3].astype(jnp.bfloat16), "grp").astype(jnp.float32),
        lax.psum(shares[4].astype(jnp.bfloat16), "grp").astype(jnp.float32),
        lax.psum(shares[5].astype(jnp.bfloat16), "grp").astype(jnp.float32),
        lax.psum(shares[6].astype(jnp.bfloat16), "grp").astype(jnp.float32),
    )


def body(
    tokens,
    seq_len,
    qkv_weight,
    out_weight,
    up_weight,
    up_bias,
    down_weight,
    down_bias,
    alphas,
    cotangent,
):
    row_count, model_width = tokens.shape
    cycle_size = lax.axis_size("blk")
    cycle_place = lax.axis_index("blk")
    head_dim = model_width // HEADS
    total_rows = cycle_size * row_count
    block_rows = min(max(row_count, 512), total_rows)
    segment, offset, span_rows = layout(seq_len, row_count, cycle_size)
    query_pos = cycle_place * span_rows + offset
    seg_all = jnp.tile(segment, cycle_size)
    pos_all = jnp.repeat(jnp.arange(cycle_size, dtype=jnp.int32), row_count) * jnp.tile(
        span_rows, cycle_size
    ) + jnp.tile(offset, cycle_size)
    geometry = (segment, query_pos, seg_all, pos_all, block_rows, head_dim ** (-0.5))
    weights = (qkv_weight, out_weight, up_weight, up_bias, down_weight, down_bias, alphas)
    hidden = tokens.astype(jnp.float32)
    saved_layers = []
    for layer_index in range(LAYERS):
        hidden, saved = layer_forward(hidden, layer_index, weights, geometry)
        saved_layers.append(saved)
    output = hidden.astype(jnp.bfloat16)
    grad_hidden = cotangent.astype(jnp.float32)
    layer_results = []
    for layer_index in reversed(range(LAYERS)):
        grad_hidden, layer_grads = layer_backward(
            grad_hidden, saved_layers[layer_index], layer_index, weights, geometry
        )
        layer_results.insert(0, layer_grads)
    finals = reduce_all(layer_results, cycle_size)
    return (
        output,
        grad_hidden,
        finals[0],
        finals[1],
        finals[2],
        finals[3],
        finals[4],
        finals[5],
        finals[6],
    )


def solution(mesh):
    placed = (
        P(("grp", "blk"), None),
        P("grp", None),
        P(),
        P(),
        P(),
        P(),
        P(),
        P(),
        P(),
        P(("grp", "blk"), None),
    )
    sizes = (mesh.shape["grp"], mesh.shape["blk"])
    return jax.shard_map(
        fast_body if sizes == (4, RUNS) else body,
        mesh=mesh,
        in_specs=placed,
        out_specs=(
            P(("grp", "blk"), None),
            P(("grp", "blk"), None),
            P(None, "blk", None),
            P(None, "blk", None),
            P(None, "blk", None),
            P(None, "blk"),
            P(None, "blk", None),
            P(None, "blk"),
            P(),
        ),
        check_vma=False,
    )
```

```python
import functools

import jax
import jax.numpy as jnp
from jax import lax
from jax.experimental import pallas as pl
from jax.experimental.pallas import tpu as pltpu
from jax.sharding import PartitionSpec as P

HEADS = 8
LAYERS = 2
NEGATIVE = -1e30
MESH = pl.DeviceIdType.MESH
F32 = jnp.float32
BF16 = jnp.bfloat16

HALF = 128
RUNS = 8
TEAM = 4
OWN = RUNS // TEAM
DIM = 64
WIDTH = 512
FF = 2048
CUT = 512
TILE = 256
TILES = HALF * RUNS // TILE
PACK = HALF + DIM
CHUNK = 576
SMALL = FF + WIDTH + 128
PARTS = ((1, 0, 320), (1, 320, 256), (0, 0, 128), (0, 128, 192), (0, 320, 128), (0, 448, 128))
SHARES = ((176, 0, 144), (176, 0, 80), (64, 0, 64), (128, 64, 0), (128, 0, 0), (0, 128, 0))


def spans():
    places, totals = {}, [0, 0, 0]
    for part, counts in enumerate(SHARES):
        first = PARTS[part][1]
        for route, count in enumerate(counts):
            places[part, route] = (first, totals[route], count)
            first += count
            totals[route] += count
    return places, totals


SPANS, TOTALS = spans()

SLOPE_AT = 0.28
TAIL = (
    0.11652077851573843,
    0.06749675579450809,
    0.2689101589486142,
    -0.23699347299932225,
    0.3898740127620002,
    -0.10580824228351815,
)


def nn(a, b):
    return lax.dot_general(a, b, (((1,), (0,)), ((), ())), preferred_element_type=F32)


def nt(a, b):
    return lax.dot_general(a, b, (((1,), (1,)), ((), ())), preferred_element_type=F32)


def layers_kernel(
    tokens, seq_len, alphas, up_bias_hbm, down_bias_hbm, cotangent, qkv_hbm, out_hbm, up_hbm, down_hbm,
    final, heads_all, out_in, grad_in, small_final,
    wqkv, wout, wup, wdown, up_bias, down_bias,
    tok_in, cot_in, flag_out, flag_in, back_out,
    hidden, grad, hid_all, attn_t, entered, act, branch, slope, second,
    dz, du, da, dqkv,
    pack_out, head_out, pack_in, o_in, do_in,
    kv, kv_t, rq, ro, o_t, lse, acc, dq_t, bias,
    parts, core_in, xa_in, xb_in, ya_in, yb_in, z_in, third_z, third_x, third_y,
    heads_out, heads_x, heads_z, heads_sum, small, small_in, small_z, small_sum,
    w_sem, move_send, move_recv, a2a_send, a2a_recv, core_send, core_recv, x_send, x_recv, y_send, y_recv,
    z_send, z_recv, fin_send, fin_recv, hid_send, hid_recv, hx_send, hx_recv, hz_send, hz_recv, hf_send, hf_recv,
    small_send, small_recv, core_free,
):
    grp = lax.axis_index("grp")
    blk = lax.axis_index("blk")
    core = lax.rem(grp, 2)
    side = lax.div(grp, 2)
    yy = lax.rem(blk, 2)
    zz = lax.div(blk, 2)
    member = 2 * core + yy
    far_side = 2 * (1 - side) + core
    low = lax.broadcasted_iota(jnp.int32, (HALF, 128), 1) < DIM

    def place(c, x, z, y):
        return (2 * x + c, 2 * z + y)

    core_peer = place(1 - core, side, zz, yy)
    x_peer = place(core, 1 - side, zz, yy)
    y_peer = place(core, side, zz, 1 - yy)

    def remote(source, target, send, recv, peer):
        return pltpu.make_async_remote_copy(
            src_ref=source,
            dst_ref=target,
            send_sem=send,
            recv_sem=recv,
            device_id=peer,
            device_id_type=MESH,
        )

    def credit(semaphore, peer, count=1):
        pl.semaphore_signal(semaphore, inc=count, device_id=peer, device_id_type=MESH)

    def moved(kind, slot, source, target, at, core_at, z_at):
        here = jnp.logical_and(core_at == core, z_at == zz)

        @pl.when(here)
        def _():
            pltpu.make_async_copy(source, target.at[at], move_recv.at[kind, at]).start()

        @pl.when(jnp.logical_not(here))
        def _():
            pltpu.make_async_remote_copy(
                src_ref=source,
                dst_ref=target.at[at],
                send_sem=move_send.at[kind, slot],
                recv_sem=move_recv.at[kind, at],
                device_id=place(core_at, side, z_at, yy),
                device_id_type=MESH,
            ).start()

    def move_left(kind, slot, source, core_at, z_at):
        here = jnp.logical_and(core_at == core, z_at == zz)

        @pl.when(jnp.logical_not(here))
        def _():
            pltpu.make_async_copy(source, source, move_send.at[kind, slot]).wait()

    def move_arrived(kind, at, target):
        pltpu.make_async_copy(target.at[at], target.at[at], move_recv.at[kind, at]).wait()

    def to_team(kind, half, source, target):
        moved(kind, half, source, target, lax.div(zz, 2), lax.rem(zz, 2), 2 * half + core)

    def to_team_left(kind, half, source):
        move_left(kind, half, source, lax.rem(zz, 2), 2 * half + core)

    def to_owner(kind, chunk, source, target):
        moved(kind, chunk, source, target, lax.div(zz, 2), lax.rem(zz, 2), core + 2 * chunk)

    def to_owner_left(kind, chunk, source):
        move_left(kind, chunk, source, lax.rem(zz, 2), core + 2 * chunk)

    def half_of(ref, half):
        return ref.at[pl.ds(pl.multiple_of(HALF * half, HALF), HALF)]

    def rows_of(half):
        return pl.ds(pl.multiple_of(half * HALF, HALF), HALF)

    def slot_of(other):
        return lax.rem(other + TEAM - member, TEAM)

    def exchange(kind, layer, half, outgoing, incoming, head=None):
        at = () if head is None else (head,)
        incoming[(half, 0, *at)] = outgoing[(half, member, *at)]
        for step in range(1, TEAM):
            peer = lax.rem(member + step, TEAM)
            remote(
                outgoing.at[(half, peer, *at)],
                incoming.at[(half, TEAM - step, *at)],
                a2a_send.at[kind, layer, half, head or 0],
                a2a_recv.at[kind, layer, half, head or 0],
                place(lax.div(peer, 2), side, zz, lax.rem(peer, 2)),
            ).start()

    def arrived(kind, layer, half, incoming, head=None):
        at = () if head is None else (head,)
        whole = incoming.at[(half, pl.ds(1, TEAM - 1), *at)]
        pltpu.make_async_copy(whole, whole, a2a_recv.at[kind, layer, half, head or 0]).wait()

    def left(kind, layer, half, outgoing):
        for head in range(OWN) if kind in (0, 3) else (None,):
            at = () if head is None else (head,)
            whole = outgoing.at[(half, pl.ds(1, TEAM - 1), *at)]
            pltpu.make_async_copy(whole, whole, a2a_send.at[kind, layer, half, head or 0]).wait()

    def tokens_of(chunk, other):
        return pl.ds(pl.multiple_of(HALF * (TEAM * chunk + other), HALF), HALF)

    def hidden_copy(layer, chunk, which):
        whose = 2 * core + 1 - yy if which == 2 else member
        block = hid_all.at[layer, :, tokens_of(chunk, whose)]
        return remote(
            block,
            block,
            hid_send.at[layer, chunk, which],
            hid_recv.at[layer, chunk, which],
            y_peer if which == 0 else core_peer,
        )

    def hidden_start(layer, chunk):
        for which in range(2):
            hidden_copy(layer, chunk, which).start()

    def hidden_pass(layer, chunk):
        hidden_copy(layer, chunk, 0).wait()
        hidden_copy(layer, chunk, 2).start()

    def hidden_done(layer, chunk):
        for which in range(1, 3):
            hidden_copy(layer, chunk, which).wait()

    def project(layer, half):
        rows = rows_of(half)
        rounded = hidden[rows, :].astype(BF16)
        if layer == 1:
            left(0, 0, half, pack_out)
        queries = nn(rounded, wqkv[layer, :, 0:WIDTH]) * (DIM ** -0.5)
        queries_t = queries.T.astype(BF16)
        keys = nn(rounded, wqkv[layer, :, WIDTH : 2 * WIDTH])
        values = nn(rounded, wqkv[layer, :, 2 * WIDTH : 3 * WIDTH])
        for pair in range(RUNS // 2):
            k_pair = keys[:, 128 * pair : 128 * pair + 128]
            v_pair = values[:, 128 * pair : 128 * pair + 128]
            first = jnp.where(low, k_pair, pltpu.roll(v_pair, DIM, 1))
            other = jnp.where(low, pltpu.roll(k_pair, DIM, 1), v_pair)
            pack_out[half, pair, 0, 0:HALF, :] = first.astype(BF16)
            pack_out[half, pair, 1, 0:HALF, :] = other.astype(BF16)
        for head in range(RUNS):
            pack_out[half, head // 2, head % 2, HALF:, :] = queries_t[DIM * head : DIM * head + DIM, :]
        for head in range(OWN):
            exchange(0, layer, half, pack_out, pack_in, head)
        hid_all[layer, :, tokens_of(half, member)] = rounded.T

    def attend(layer, chunk):
        if layer == 1:
            left(1, 0, chunk, head_out)

        def one_head(head, carry):
            arrived(0, layer, chunk, pack_in, head)
            for other in range(TEAM):
                slot = slot_of(other)
                start = HALF * (TEAM * chunk + other)
                span = slice(start, start + HALF)
                block = pack_in[chunk, slot, head, 0:HALF, :]
                kv[layer, head, span, :] = block
                kv_t[layer, head, :, span] = block.T
                rq[layer, head, 0:DIM, span] = pack_in[chunk, slot, head, HALF:, :]

            def scores_of(i):
                count = TILE * (i + 1)
                tile = rq[layer, head, :, TILE * i : TILE * i + TILE]
                return nn(kv[layer, head, 0:count, :], tile) + bias[TILE * TILES - count :, :]

            ahead = [scores_of(i) for i in (2 * chunk, 2 * chunk + 1)]
            for i in (2 * chunk, 2 * chunk + 1):
                columns = slice(TILE * i, TILE * i + TILE)
                count = TILE * (i + 1)
                scores = ahead[i - 2 * chunk]
                largest = jnp.max(scores, axis=0, keepdims=True)
                weight = jnp.exp(scores - largest)
                total = jnp.sum(weight, axis=0, keepdims=True)
                summed = nn(kv_t[layer, head, DIM:, 0:count], weight.astype(BF16))
                summed = summed / total
                o_t[layer, head, :, columns] = summed
                lse[layer, head, :, columns] = largest + jnp.log(total)
                rounded = summed.astype(BF16)
                for part in range(2):
                    head_out[chunk, 2 * (i - 2 * chunk) + part, head] = rounded[
                        :, HALF * part : HALF * part + HALF
                    ]
            return carry

        for head in range(OWN):
            one_head(head, 0)
        exchange(1, layer, chunk, head_out, o_in)

    def feed(layer, half):
        rows = rows_of(half)
        arrived(1, layer, half, o_in)
        for head in range(RUNS):
            attn_t[layer, DIM * head : DIM * head + DIM, rows] = o_in[half, slot_of(head // 2), head % 2]
        attn = attn_t[layer, :, rows].T
        grown = nn(attn, wout[layer])
        branch[layer, rows, :] = grown
        middle = hidden[rows, :] + alphas[layer, 0] * grown
        rounded = middle.astype(BF16)
        entered[layer, rows, :] = rounded
        total = jnp.zeros((HALF, WIDTH), F32)

        def gate_of(step):
            cut = slice(CUT * step, CUT * step + CUT)
            return nn(rounded, wup[layer, :, cut]) + up_bias[layer : layer + 1, cut]

        coming = gate_of(0)
        for step in range(FF // CUT):
            cut = slice(CUT * step, CUT * step + CUT)
            gate = coming
            if step + 1 < FF // CUT:
                coming = gate_of(step + 1)
            bell = jnp.exp(gate * gate * -0.5)
            near = pl.reciprocal(1.0 + SLOPE_AT * jnp.abs(gate), approx=True)
            tail = jnp.full_like(gate, TAIL[5])
            for factor in TAIL[4::-1]:
                tail = tail * near + factor
            tail = bell * (tail * near)
            risen = jnp.where(gate > 0.0, 1.0 - tail, tail)
            slope[layer, rows, cut] = risen + gate * bell * 0.3989422804014327
            active = (gate * risen).astype(BF16)
            act[layer, rows, cut] = active
            total = total + nn(active, wdown[layer, cut, :])
        total = total + down_bias[layer : layer + 1, :]
        second[layer, rows, :] = total
        hidden[rows, :] = middle + alphas[layer, 1] * total

    def total_of(values):
        return jnp.sum(jnp.sum(values, axis=0, keepdims=True), axis=1, keepdims=True)

    def feed_back(layer):
        start = grad[...]
        if layer == 0:
            dz[...] = (alphas[layer, 1] * start).astype(BF16)
        scaled = dz[...]
        alpha_second = total_of(start * second[layer])
        small[layer : layer + 1, FF : FF + WIDTH] = jnp.sum(scaled.astype(F32), axis=0, keepdims=True)
        middle = start
        coming = nt(scaled, wdown[layer, 0:CUT, :])
        for step in range(FF // CUT):
            cut = slice(CUT * step, CUT * step + CUT)
            raw = coming
            if step + 1 < FF // CUT:
                coming = nt(scaled, wdown[layer, CUT * (step + 1) : CUT * (step + 2), :])
            gate = (raw * slope[layer, :, cut]).astype(BF16)
            du[:, cut] = gate
            small[layer : layer + 1, cut] = jnp.sum(gate.astype(F32), axis=0, keepdims=True)
            middle = middle + nt(gate, wup[layer, :, cut])
        grad[...] = middle
        mixed = (alphas[layer, 0] * middle).astype(BF16)
        da[...] = mixed
        spread = nt(wout[layer], mixed).astype(BF16)
        for chunk in (1, 0):
            left(*((1, 1) if layer == 1 else (2, 1)), chunk, head_out)
            for head in range(RUNS):
                head_out[chunk, head // 2, head % 2] = spread[
                    DIM * head : DIM * head + DIM, HALF * chunk : HALF * chunk + HALF
                ]
            exchange(2, layer, chunk, head_out, do_in)
        alpha_first = total_of(middle * branch[layer])
        column = lax.broadcasted_iota(jnp.int32, (1, 128), 1)
        small[layer : layer + 1, FF + WIDTH :] = jnp.where(
            column == 0, alpha_first, jnp.where(column == 1, alpha_second, 0.0)
        )

    def attend_back(layer, chunk):
        arrived(2, layer, chunk, do_in)
        left(*((0, 1) if layer == 1 else (3, 1)), chunk, pack_out)

        def one_head(head, carry):
            for other in range(TEAM):
                start = HALF * (TEAM * chunk + other)
                ro[head, DIM:, start : start + HALF] = do_in[chunk, slot_of(other), head]
            for i in (2 * chunk, 2 * chunk + 1):
                columns = slice(TILE * i, TILE * i + TILE)
                query_tile = rq[layer, head, :, columns]
                grad_tile = ro[head, :, columns]
                log_total = lse[layer, head, :, columns]
                delta = jnp.sum(
                    ro[head, DIM:, columns].astype(F32) * o_t[layer, head, :, columns],
                    axis=0,
                    keepdims=True,
                )
                count = TILE * (i + 1)
                keys = kv[layer, head, 0:count, :]
                weight = jnp.exp(nn(keys, query_tile) + bias[TILE * TILES - count :, :] - log_total)
                scored = (weight * (nn(keys, grad_tile) - delta)).astype(BF16)
                term = nt(scored, query_tile) + nt(weight.astype(BF16), grad_tile)
                if chunk == 1 and i == 2:
                    acc[head, 0:count, :] = term
                elif chunk == 1:
                    acc[head, 0 : count - TILE, :] += term[0 : count - TILE, :]
                    acc[head, count - TILE : count, :] = term[count - TILE :, :]
                else:
                    acc[head, 0:count, :] += term
                query_grad = nn(kv_t[layer, head, 0:DIM, 0:count], scored)
                dq_t[head, :, columns] = query_grad * (DIM ** -0.5)
            for other in range(TEAM):
                start = HALF * (TEAM * chunk + other)
                span = slice(start, start + HALF)
                pack_out[chunk, other, head, 0:HALF, :] = acc[head, span, :].astype(BF16)
                pack_out[chunk, other, head, HALF:, :] = dq_t[head, :, span].astype(BF16)
            exchange(3, layer, chunk, pack_out, pack_in, head)
            return carry

        for head in range(OWN):
            one_head(head, 0)

    def project_back(layer, half):
        for head in range(OWN):
            arrived(3, layer, half, pack_in, head)
        turned = jnp.concatenate(
            [pack_in[half, slot_of(head // 2), head % 2, HALF:, :] for head in range(RUNS)], axis=0
        )
        dqkv[:, 0:WIDTH] = turned.T
        for pair in range(RUNS // 2):
            first = pack_in[half, slot_of(pair), 0, 0:HALF, :].astype(F32)
            other = pack_in[half, slot_of(pair), 1, 0:HALF, :].astype(F32)
            k_pair = jnp.where(low, first, pltpu.roll(other, DIM, 1))
            v_pair = jnp.where(low, pltpu.roll(first, DIM, 1), other)
            dqkv[:, WIDTH + 128 * pair : WIDTH + 128 * pair + 128] = k_pair.astype(BF16)
            dqkv[:, 2 * WIDTH + 128 * pair : 2 * WIDTH + 128 * pair + 128] = v_pair.astype(BF16)
        rows = rows_of(half)
        grad[rows, :] = grad[rows, :] + nt(dqkv[...], wqkv[layer])

    def scatter_rows(layer, result, first_row):
        for run in range(RUNS):
            for quarter in range(4):
                parts[layer, quarter % 2, quarter // 2, run // 2, run % 2, first_row : first_row + DIM, :] = result[
                    DIM * run : DIM * run + DIM, 128 * quarter : 128 * quarter + 128
                ].astype(BF16)

    def make(part):
        layer, first, count = PARTS[part]
        if first < 256:
            turned = entered[layer].T
        for row in range(first, min(first + count, 256), DIM):
            step = row // DIM
            scatter_rows(layer, nn(turned, du[:, CUT * step : CUT * step + CUT]), row)
        if first <= 256 < first + count:
            scatter_rows(layer, nn(attn_t[layer], da[...]), 256)
        if first >= 320:
            for run in range(RUNS):
                at = TILE * run + first - 320
                result = nn(act[layer, :, at : at + count].T, dz[...])
                for quarter in range(4):
                    parts[layer, quarter % 2, quarter // 2, run // 2, run % 2, first : first + count, :] = result[
                        :, 128 * quarter : 128 * quarter + 128
                    ].astype(BF16)
        if layer == 0:
            pl.semaphore_wait(core_free.at[0 if first < 320 else 1], 1)
        core_copy(part).start()

    def heads_grads(layer):
        for chunk in range(2):
            hidden_done(layer, chunk)
        blocks = [(run // TEAM, run % TEAM) for run in range(RUNS)]
        keys_values = jnp.concatenate(
            [
                jnp.concatenate([pack_out[chunk, other, head, 0:HALF, :] for chunk, other in blocks], axis=0)
                for head in range(OWN)
            ],
            axis=1,
        )
        queries = jnp.concatenate(
            [
                jnp.concatenate([pack_out[chunk, other, head, HALF:, :] for chunk, other in blocks], axis=1)
                for head in range(OWN)
            ],
            axis=0,
        )
        both = nn(hid_all[layer], keys_values)
        q_part = nt(hid_all[layer], queries)
        first, other = both[:, 0:128], both[:, 128:256]
        left_half = lax.broadcasted_iota(jnp.int32, (WIDTH, 128), 1) < DIM
        k_part = jnp.where(left_half, first, pltpu.roll(other, DIM, 1))
        v_part = jnp.where(left_half, pltpu.roll(first, DIM, 1), other)
        for number, values in enumerate((q_part, k_part, v_part)):
            for run in range(RUNS):
                heads_out[layer, run // 2, run % 2, :, 128 * number : 128 * number + 128] = values[
                    DIM * run : DIM * run + DIM, :
                ].astype(BF16)
        heads_x_copy(layer).start()

    def half_rows(which):
        return pl.ds(pl.multiple_of(32 * which, 32), 32)

    def heads_x_copy(layer):
        return remote(
            heads_out.at[layer, :, :, half_rows(1 - side)],
            heads_x.at[layer],
            hx_send.at[layer],
            hx_recv.at[layer],
            x_peer,
        )

    def heads_z_copy(layer, step):
        peer = lax.rem(zz + step, 4)
        return remote(
            heads_out.at[layer, peer, :, half_rows(side)],
            heads_z.at[layer, 4 - step],
            hz_send.at[layer, step],
            hz_recv.at[layer, 4 - step],
            place(core, side, peer, yy),
        )

    def heads_last_copy(layer, number):
        x, c, y = number // 4, number // 2 % 2, number % 2
        return remote(
            heads_sum.at[layer, 1 - yy if y else yy],
            heads_all.at[layer, side, member],
            hf_send.at[layer, number],
            hf_recv.at[layer, number],
            place(1 - core if c else core, 1 - side if x else side, zz, 1 - yy if y else yy),
        )

    def heads_second(layer):
        heads_x_copy(layer).wait()
        heads_out[layer, :, :, half_rows(side), :] += heads_x[layer]
        for step in range(1, 4):
            heads_z_copy(layer, step).start()

    def heads_third(layer):
        for step in range(1, 4):
            heads_z_copy(layer, step).wait()
        total = heads_out[layer, zz, :, half_rows(side), :].astype(F32)
        for slot in range(1, 4):
            total = total + heads_z[layer, slot].astype(F32)
        heads_sum[layer] = total.astype(BF16)
        heads_all[layer, side, member] = heads_sum[layer, yy]
        for number in range(1, 8):
            heads_last_copy(layer, number).start()

    def heads_done(layer):
        for number in range(1, 8):
            heads_last_copy(layer, number).wait()

    def rows_in(part, route):
        first, room, count = SPANS[part, route]
        return pl.ds(first, count), pl.ds(room, count)

    def used(part, route):
        return SHARES[part][route] > 0

    def core_copy(part):
        layer, first, count = PARTS[part]
        rows = pl.ds(first, count)
        return remote(
            parts.at[layer, 1 - core, :, :, :, rows],
            core_in.at[:, :, :, rows],
            core_send.at[part],
            core_recv.at[part],
            core_peer,
        )

    def x_copy(part, route):
        layer = PARTS[part][0]
        rows, room = rows_in(part, route)
        ends = (x_send.at[part, route], x_recv.at[part, route], x_peer)
        mine = parts.at[layer, core, 1 - side]
        if route == 0:
            return remote(mine.at[:, :, rows], xa_in.at[:, :, room], *ends)
        if route == 1:
            return remote(mine.at[:, yy, rows], xb_in.at[:, room], *ends)
        return remote(mine.at[zz, :, rows], third_x.at[:, room], *ends)

    def y_copy(part, route):
        layer = PARTS[part][0]
        rows, room = rows_in(part, route)
        ends = (y_send.at[part, route], y_recv.at[part, route], y_peer)
        mine = parts.at[layer, core]
        if route == 0:
            return remote(mine.at[side, :, 1 - yy, rows], ya_in.at[:, room], *ends)
        if route == 1:
            return remote(mine.at[:, :, 1 - yy, rows], yb_in.at[:, :, room], *ends)
        return remote(mine.at[side, zz, 1 - yy, rows], third_y.at[room], *ends)

    def z_copy(part, route, step):
        layer = PARTS[part][0]
        rows, room = rows_in(part, route)
        peer = lax.rem(zz + step, 4)
        ends = (z_send.at[part, route, step], z_recv.at[part, route, 4 - step], place(core, side, peer, yy))
        if route == 2:
            return remote(parts.at[layer, core, :, peer, :, rows], third_z.at[4 - step, :, :, room], *ends)
        return remote(parts.at[layer, core, side, peer, yy, rows], z_in.at[layer, 4 - step, rows], *ends)

    def final_copy(part, which):
        layer, first, count = PARTS[part]
        block = final.at[layer, far_side if which == 2 else grp, pl.ds(first, count)]
        return remote(
            block,
            block,
            fin_send.at[part, which],
            fin_recv.at[part, which],
            x_peer if which == 0 else core_peer,
        )

    def core_done(part):
        layer, first, count = PARTS[part]
        rows = pl.ds(first, count)
        core_copy(part).wait()
        for across in (1 - side, side):
            parts[layer, core, across, :, :, rows, :] += core_in[across, :, :, rows, :]
            if used(part, 0) and across is not side:
                x_copy(part, 0).start()
        if used(part, 1):
            y_copy(part, 1).start()
        if used(part, 2):
            for step in range(1, 4):
                z_copy(part, 2, step).start()
        if layer == 1:
            freed = 0 if first < 320 else 1
            followers = [1 for other in PARTS if other[0] == 0 and (other[1] >= 320) == (freed == 1)]
            credit(core_free.at[freed], core_peer, len(followers))

    def first_x(part):
        if used(part, 0):
            layer = PARTS[part][0]
            rows, room = rows_in(part, 0)
            x_copy(part, 0).wait()
            for y in (1 - yy, yy):
                parts[layer, core, side, :, y, rows, :] += xa_in[:, y, room, :]
                if y is not yy:
                    y_copy(part, 0).start()

    def first_y(part):
        if used(part, 1):
            layer = PARTS[part][0]
            rows, room = rows_in(part, 1)
            y_copy(part, 1).wait()
            for across in (1 - side, side):
                parts[layer, core, across, :, yy, rows, :] += yb_in[across, :, room, :]
                if across is not side:
                    x_copy(part, 1).start()

    def first_z(part):
        if used(part, 2):
            layer = PARTS[part][0]
            rows, room = rows_in(part, 2)
            for step in range(1, 4):
                z_copy(part, 2, step).wait()
            for across in (1 - side, side):
                total = parts[layer, core, across, zz, :, rows, :].astype(F32)
                for slot in range(1, 4):
                    total = total + third_z[slot, across, :, room, :].astype(F32)
                parts[layer, core, across, zz, :, rows, :] = total.astype(BF16)
                if across is not side:
                    x_copy(part, 2).start()

    def second_x(part):
        if used(part, 0):
            layer = PARTS[part][0]
            rows, room = rows_in(part, 0)
            y_copy(part, 0).wait()
            parts[layer, core, side, :, yy, rows, :] += ya_in[:, room, :]
            for step in range(1, 4):
                z_copy(part, 0, step).start()

    def second_y(part):
        if used(part, 1):
            layer = PARTS[part][0]
            rows, room = rows_in(part, 1)
            x_copy(part, 1).wait()
            parts[layer, core, side, :, yy, rows, :] += xb_in[:, room, :]
            for step in range(1, 4):
                z_copy(part, 1, step).start()

    def second_z(part):
        if used(part, 2):
            layer = PARTS[part][0]
            rows, room = rows_in(part, 2)
            x_copy(part, 2).wait()
            for y in (1 - yy, yy):
                parts[layer, core, side, zz, y, rows, :] += third_x[y, room, :]
                if y is not yy:
                    y_copy(part, 2).start()

    def third_done(part):
        layer = PARTS[part][0]
        for route in range(3):
            if not used(part, route):
                continue
            rows, room = rows_in(part, route)
            if route == 2:
                y_copy(part, 2).wait()
                final[layer, grp, rows, :] = parts[layer, core, side, zz, yy, rows, :] + third_y[room, :]
            else:
                for step in range(1, 4):
                    z_copy(part, route, step).wait()
                total = parts[layer, core, side, zz, yy, rows, :].astype(F32)
                for slot in range(1, 4):
                    total = total + z_in[layer, slot, rows, :].astype(F32)
                final[layer, grp, rows, :] = total.astype(BF16)
        for which in range(2):
            final_copy(part, which).start()

    def final_pass(part):
        final_copy(part, 0).wait()
        final_copy(part, 2).start()

    def final_done(part):
        for which in range(1, 3):
            final_copy(part, which).wait()

    def small_copy(stage):
        peer = (core_peer, x_peer, y_peer)[stage]
        return remote(
            small_sum.at[stage], small_in.at[stage], small_send.at[stage], small_recv.at[stage], peer
        )

    def small_z_copy(step):
        return remote(
            small_z.at[zz],
            small_z.at[zz],
            small_send.at[2 + step],
            small_recv.at[2 + step],
            place(core, side, lax.rem(zz + step, 4), yy),
        )

    def small_start():
        small_sum[0] = small[...]
        small_copy(0).start()

    def small_next(stage):
        small_copy(stage).wait()
        total = small_sum[stage] + small_in[stage]
        if stage < 2:
            small_sum[stage + 1] = total
            small_copy(stage + 1).start()
        else:
            small_z[zz] = total
            for step in range(1, 4):
                small_z_copy(step).start()

    def small_done():
        for step in range(1, 4):
            small_z_copy(step).wait()
        small_sum[0] = (small_z[0] + small_z[1]) + (small_z[2] + small_z[3])
        small_final[:, 0:256] = small_sum[0, :, pl.ds(pl.multiple_of(blk * 256, 256), 256)]
        pair = small_sum[0, :, pl.ds(pl.multiple_of(FF + 128 * zz, 128), 128)]
        small_final[:, 256:384] = jnp.where(yy == 1, pltpu.roll(pair, DIM, 1), pair)
        small_final[:, 384:512] = small_sum[0, :, FF + WIDTH :]

    def halves(*phases, first=0):
        def both(step, carry):
            for phase in phases:
                phase(lax.rem(step + first, 2))
            return carry

        lax.fori_loop(0, 2, both, 0)

    def begin(half):
        move_arrived(0, half, tok_in)
        hidden[rows_of(half), :] = tok_in[half].astype(F32)

    def finish(half):
        back_out[0, half] = hidden[rows_of(half), :].astype(BF16)
        to_owner(3, half, back_out.at[0, half], out_in)

    def turn_round(layer, half):
        move_arrived(2, half, cot_in)
        rows = rows_of(half)
        grad[rows, :] = cot_in[half].astype(F32)
        dz[rows, :] = (alphas[layer, 1] * grad[rows, :]).astype(BF16)

    def hand_back(half):
        back_out[1, half] = grad[rows_of(half), :].astype(BF16)
        to_owner(4, half, back_out.at[1, half], grad_in)

    barrier = pltpu.get_barrier_semaphore()
    for step in range(1, 4):
        credit(barrier, place(core, side, lax.rem(zz + step, 4), yy))
    for step in range(4):
        credit(barrier, place(1 - core, side, lax.rem(zz + step, 4), yy))
    for peer in (
        x_peer,
        y_peer,
        place(1 - core, side, zz, 1 - yy),
        place(1 - core, 1 - side, zz, yy),
        place(core, 1 - side, zz, 1 - yy),
        place(1 - core, 1 - side, zz, 1 - yy),
    ):
        credit(barrier, peer)

    weight_copies = {}
    for layer in range(LAYERS):
        for number, (source, target) in enumerate(
            ((qkv_hbm, wqkv), (out_hbm, wout), (up_hbm, wup), (down_hbm, wdown))
        ):
            weight_copies[layer, number] = pltpu.make_async_copy(
                source.at[layer], target.at[layer], w_sem.at[layer, number]
            )
    bias_copies = [
        pltpu.make_async_copy(up_bias_hbm, up_bias, w_sem.at[2, 0]),
        pltpu.make_async_copy(down_bias_hbm, down_bias, w_sem.at[2, 1]),
    ]
    weight_copies[0, 0].start()
    pl.semaphore_wait(barrier, 13)
    upper = lax.div(zz, 2)
    for half in (1 - upper, upper):
        to_team(0, half, half_of(tokens, half), tok_in)
    for copy in (*list(weight_copies.values())[1:], *bias_copies):
        copy.start()
    end_second = lax.div(seq_len[0, 0] + seq_len[0, 1], RUNS)
    flag_out[...] = jnp.full((8, 128), end_second.astype(F32), F32)
    for half in (1 - upper, upper):
        to_team(1, half, flag_out, flag_in)
    for layer in range(LAYERS):
        for head in range(OWN):
            rq[layer, head, DIM:, :] = jnp.zeros((DIM, HALF * RUNS), BF16)
    for head in range(OWN):
        ro[head, 0:DIM, :] = jnp.zeros((DIM, HALF * RUNS), BF16)
    weight_copies[0, 0].wait()
    halves(begin, functools.partial(project, 0), first=upper)
    for half in (1 - upper, upper):
        to_team(2, half, half_of(cotangent, half), cot_in)

    move_arrived(1, 0, flag_in)
    move_arrived(1, 1, flag_in)
    border = jnp.concatenate([flag_in[0, 0:1, :]] * 2, axis=1) - (HALF * lax.div(zz, 2)).astype(F32)
    key_row = lax.broadcasted_iota(jnp.int32, (TILE, TILE), 0)
    query_col = lax.broadcasted_iota(jnp.int32, (TILE, TILE), 1)
    later = key_row > query_col
    key_sub = lax.rem(key_row, HALF).astype(F32) >= border
    query_sub = lax.rem(query_col, HALF).astype(F32) >= border
    apart = jnp.logical_xor(key_sub, query_sub)
    for tile in range(TILES - 1):
        bias[TILE * tile : TILE * tile + TILE, :] = jnp.where(apart, NEGATIVE, 0.0)
    bias[TILE * (TILES - 1) :, :] = jnp.where(jnp.logical_or(later, apart), NEGATIVE, 0.0)

    for copy in (*bias_copies, *(weight_copies[0, number] for number in range(1, 4))):
        copy.wait()
    attend(0, 0)
    attend(0, 1)
    hidden_start(0, 0)
    weight_copies[1, 0].wait()
    halves(functools.partial(feed, 0), functools.partial(project, 1))
    for number in range(1, 4):
        weight_copies[1, number].wait()
    attend(1, 0)
    attend(1, 1)
    hidden_pass(0, 0)
    hidden_start(1, 0)
    halves(functools.partial(feed, 1), finish)
    hidden_start(0, 1)
    hidden_start(1, 1)
    hidden_pass(1, 0)

    halves(functools.partial(turn_round, 1))
    make(1)
    feed_back(1)
    hidden_pass(0, 1)
    hidden_pass(1, 1)
    core_done(1)
    make(0)
    attend_back(1, 1)
    core_done(0)
    attend_back(1, 0)
    project_back(1, 1)
    first_x(1)
    heads_grads(1)
    project_back(1, 0)
    feed_back(0)
    small_start()
    make(4)
    second_x(1)
    make(5)
    first_x(0)
    first_z(1)
    make(2)
    core_done(4)
    core_done(5)
    make(3)
    core_done(2)
    core_done(3)
    heads_second(1)
    second_x(0)
    first_x(4)
    attend_back(0, 1)
    small_next(0)
    first_y(3)
    first_y(5)
    first_x(2)
    first_z(2)
    first_z(0)
    second_x(4)
    first_x(3)
    attend_back(0, 0)
    small_next(1)
    second_y(3)
    heads_grads(0)
    small_next(2)
    second_y(5)
    second_z(1)
    second_z(0)
    second_x(2)
    second_x(3)
    third_done(5)
    second_z(2)
    heads_third(1)
    heads_second(0)
    small_done()
    third_done(1)
    third_done(4)
    project_back(0, 1)
    hand_back(1)
    third_done(2)
    third_done(0)
    third_done(3)
    project_back(0, 0)
    hand_back(0)
    heads_third(0)
    final_pass(2)
    final_pass(4)
    final_pass(5)
    final_pass(3)
    final_done(4)
    final_pass(0)
    final_pass(1)
    heads_done(0)
    heads_done(1)
    final_done(2)
    final_done(0)
    final_done(1)
    final_done(3)
    final_done(5)
    for half in range(2):
        move_arrived(3, half, out_in)
        move_arrived(4, half, grad_in)

    for half in range(2):
        left(2, 0, half, head_out)
        left(3, 0, half, pack_out)
        to_team_left(0, half, half_of(tokens, half))
        to_team_left(1, half, flag_out)
        to_team_left(2, half, half_of(cotangent, half))
        to_owner_left(3, half, back_out.at[0, half])
        to_owner_left(4, half, back_out.at[1, half])


def results_kernel(
    final, heads, out_block, grad_block, small,
    output, input_grad, qkv_grad, out_grad, up_grad, up_bias_grad, down_grad, down_bias_grad, alpha_grad,
    out_flat, grad_wide, qkv_wide, out_wide, up_wide, down_wide, out_sem,
):
    ends = []

    def write(source, target):
        ends.append(pltpu.make_async_copy(source, target, out_sem.at[len(ends)]))
        ends[-1].start()

    up_bias_grad[...] = small[:, 0:256]
    down_bias_grad[...] = small[:, 256 : 256 + DIM]
    alpha_grad[...] = small[:, 384:386]
    for layer in range(LAYERS):
        for quarter in range(4):

            def block(first, count):
                return final[layer, quarter, first : first + count, :].astype(F32)

            def columns(step):
                return slice(WIDTH * step + 128 * quarter, WIDTH * step + 128 * quarter + 128)

            for step in range(4):
                up_wide[layer, :, columns(step)] = block(DIM * step, DIM)
            out_wide[layer, :, columns(0)] = block(256, DIM)
            down_wide[layer, :, columns(0)] = block(320, 256)
        write(up_wide.at[layer], up_grad.at[layer])
        write(out_wide.at[layer], out_grad.at[layer])
        write(down_wide.at[layer], down_grad.at[layer])
    for half in range(2):
        rows = slice(HALF * half, HALF * half + HALF)
        grad_wide[rows, :] = grad_block[half].astype(F32)
        out_flat[rows, :] = out_block[half]
    write(grad_wide, input_grad)
    write(out_flat, output)
    for layer in range(LAYERS):
        for side in range(2):
            for member in range(TEAM):
                for step in range(3):
                    at = WIDTH * step + 128 * member
                    qkv_wide[layer, 32 * side : 32 * side + 32, at : at + 128] = heads[
                        layer, side, member, :, 128 * step : 128 * step + 128
                    ].astype(F32)
        write(qkv_wide.at[layer], qkv_grad.at[layer])
    for end in ends:
        end.wait()


def fast_body(
    tokens, seq_len, qkv_weight, out_weight, up_weight, up_bias, down_weight, down_bias, alphas, cotangent
):
    whole = pl.BlockSpec(memory_space=pltpu.VMEM)
    scalar = pl.BlockSpec(memory_space=pltpu.SMEM)
    far = pl.BlockSpec(memory_space=pl.ANY)
    shape = jax.ShapeDtypeStruct
    rows = HALF * RUNS

    def vmem(*dims):
        return pltpu.VMEM(dims, BF16)

    def wide(*dims):
        return pltpu.VMEM(dims, F32)

    dma = pltpu.SemaphoreType.DMA
    final, heads, out_block, grad_block, small = pl.pallas_call(
        layers_kernel,
        out_shape=(
            vmem(LAYERS, 4, CHUNK, 128),
            vmem(LAYERS, 2, TEAM, DIM // 2, 3 * 128),
            vmem(2, HALF, WIDTH),
            vmem(2, HALF, WIDTH),
            wide(LAYERS, WIDTH),
        ),
        in_specs=[far, scalar, scalar, far, far, far, far, far, far, far],
        out_specs=(whole,) * 5,
        scratch_shapes=[
            vmem(LAYERS, WIDTH, 3 * WIDTH),
            vmem(LAYERS, WIDTH, WIDTH),
            vmem(LAYERS, WIDTH, FF),
            vmem(LAYERS, FF, WIDTH),
            wide(LAYERS, FF),
            wide(LAYERS, WIDTH),
            vmem(2, HALF, WIDTH),
            vmem(2, HALF, WIDTH),
            wide(8, 128),
            wide(2, 8, 128),
            vmem(2, 2, HALF, WIDTH),
            wide(2 * HALF, WIDTH),
            wide(2 * HALF, WIDTH),
            vmem(LAYERS, WIDTH, rows),
            vmem(LAYERS, WIDTH, 2 * HALF),
            vmem(LAYERS, 2 * HALF, WIDTH),
            vmem(LAYERS, 2 * HALF, FF),
            wide(LAYERS, 2 * HALF, WIDTH),
            wide(LAYERS, 2 * HALF, FF),
            wide(LAYERS, 2 * HALF, WIDTH),
            vmem(2 * HALF, WIDTH),
            vmem(2 * HALF, FF),
            vmem(2 * HALF, WIDTH),
            vmem(HALF, 3 * WIDTH),
            vmem(2, TEAM, OWN, PACK, 128),
            vmem(2, TEAM, OWN, DIM, 128),
            vmem(2, TEAM, OWN, PACK, 128),
            vmem(2, TEAM, OWN, DIM, 128),
            vmem(2, TEAM, OWN, DIM, 128),
            vmem(LAYERS, OWN, rows, 128),
            vmem(LAYERS, OWN, 128, rows),
            vmem(LAYERS, OWN, 128, rows),
            vmem(OWN, 128, rows),
            wide(LAYERS, OWN, DIM, rows),
            wide(LAYERS, OWN, 1, rows),
            wide(OWN, rows, 128),
            wide(OWN, DIM, rows),
            wide(rows, TILE),
            vmem(LAYERS, 2, 2, 4, 2, CHUNK, 128),
            vmem(2, 4, 2, CHUNK, 128),
            vmem(4, 2, TOTALS[0], 128),
            vmem(4, TOTALS[1], 128),
            vmem(4, TOTALS[0], 128),
            vmem(2, 4, TOTALS[1], 128),
            vmem(LAYERS, 4, CHUNK, 128),
            vmem(4, 2, 2, TOTALS[2], 128),
            vmem(2, TOTALS[2], 128),
            vmem(TOTALS[2], 128),
            vmem(LAYERS, 4, 2, DIM, 3 * 128),
            vmem(LAYERS, 4, 2, DIM // 2, 3 * 128),
            vmem(LAYERS, 4, 2, DIM // 2, 3 * 128),
            vmem(LAYERS, 2, DIM // 2, 3 * 128),
            wide(LAYERS, SMALL),
            wide(3, LAYERS, SMALL),
            wide(4, LAYERS, SMALL),
            wide(3, LAYERS, SMALL),
            dma((LAYERS + 1, 4)),
            dma((5, 2)),
            dma((5, 2)),
            dma((4, LAYERS, 2, OWN)),
            dma((4, LAYERS, 2, OWN)),
            dma((len(PARTS),)),
            dma((len(PARTS),)),
            dma((len(PARTS), 3)),
            dma((len(PARTS), 3)),
            dma((len(PARTS), 3)),
            dma((len(PARTS), 3)),
            dma((len(PARTS), 3, 4)),
            dma((len(PARTS), 3, 4)),
            dma((len(PARTS), 3)),
            dma((len(PARTS), 3)),
            dma((LAYERS, 2, 3)),
            dma((LAYERS, 2, 3)),
            dma((LAYERS,)),
            dma((LAYERS,)),
            dma((LAYERS, 4)),
            dma((LAYERS, 4)),
            dma((LAYERS, 8)),
            dma((LAYERS, 8)),
            dma((6,)),
            dma((6,)),
            pltpu.SemaphoreType.REGULAR((2,)),
        ],
        compiler_params=pltpu.CompilerParams(
            collective_id=0, has_side_effects=True, vmem_limit_bytes=61 * 1024 * 1024
        ),
        name="layers",
    )(
        tokens, seq_len, alphas, up_bias, down_bias, cotangent,
        qkv_weight, out_weight, up_weight, down_weight,
    )
    return tuple(
        pl.pallas_call(
            results_kernel,
            out_shape=(
                shape((2 * HALF, WIDTH), BF16),
                shape((2 * HALF, WIDTH), F32),
                shape((LAYERS, DIM, 3 * WIDTH), F32),
                shape((LAYERS, DIM, WIDTH), F32),
                shape((LAYERS, DIM, FF), F32),
                shape((LAYERS, FF // RUNS), F32),
                shape((LAYERS, FF // RUNS, WIDTH), F32),
                shape((LAYERS, DIM), F32),
                shape((LAYERS, 2), F32),
            ),
            in_specs=[whole] * 5,
            out_specs=(far, far, far, far, far, whole, far, whole, whole),
            scratch_shapes=[
                vmem(2 * HALF, WIDTH),
                wide(2 * HALF, WIDTH),
                wide(LAYERS, DIM, 3 * WIDTH),
                wide(LAYERS, DIM, WIDTH),
                wide(LAYERS, DIM, FF),
                wide(LAYERS, FF // RUNS, WIDTH),
                dma((10,)),
            ],
            compiler_params=pltpu.CompilerParams(vmem_limit_bytes=24 * 1024 * 1024),
            name="results",
        )(final, heads, out_block, grad_block, small)
    )


def layout(seq_len, local_count, cycle_size):
    piece_rows = seq_len[0] // cycle_size
    end_rows = jnp.cumsum(piece_rows)
    start_rows = end_rows - piece_rows
    local_rows = jnp.arange(local_count, dtype=jnp.int32)
    segment = jnp.sum((local_rows[:, None] >= end_rows[None, :]).astype(jnp.int32), axis=1)
    picked = segment[:, None] == jnp.arange(seq_len.shape[1], dtype=jnp.int32)[None, :]
    offset = local_rows - jnp.sum(jnp.where(picked, start_rows[None, :], 0), axis=1)
    span_rows = jnp.sum(jnp.where(picked, piece_rows[None, :], 0), axis=1)
    return (segment, offset, span_rows)


def gelu_exact(values):
    return jax.nn.gelu(values, approximate=False)


def key_block(whole, geometry, block_index, head_count):
    query_seg, query_pos, seg_all, pos_all, block_rows, score_scale = geometry
    first_row = block_index * block_rows
    key_piece = lax.dynamic_slice_in_dim(whole, first_row, block_rows, 0)
    key_seg = lax.dynamic_slice_in_dim(seg_all, first_row, block_rows, 0)
    key_pos = lax.dynamic_slice_in_dim(pos_all, first_row, block_rows, 0)
    half_width = key_piece.shape[1] // 2
    keys_part = key_piece[:, :half_width].reshape(block_rows, head_count, -1)
    values_part = key_piece[:, half_width:].reshape(block_rows, head_count, -1)
    return (keys_part, values_part, key_seg, key_pos)


def block_scores(queries, keys_part, key_seg, key_pos, geometry):
    query_seg, query_pos, seg_all, pos_all, block_rows, score_scale = geometry
    scores = (
        jnp.einsum("qhd,khd->hqk", queries, keys_part, preferred_element_type=jnp.float32)
        * score_scale
    )
    allowed = (query_seg[:, None] == key_seg[None, :]) & (key_pos[None, :] <= query_pos[:, None])
    return (scores, allowed[None])


def attend(queries, whole, geometry):
    row_count, head_count, head_dim = queries.shape
    block_count = whole.shape[0] // geometry[4]

    def statistics(running, block_index):
        largest, totals = running
        keys_part, values_part, key_seg, key_pos = key_block(
            whole, geometry, block_index, head_count
        )
        scores, allowed = block_scores(queries, keys_part, key_seg, key_pos, geometry)
        newest = jnp.maximum(largest, jnp.max(jnp.where(allowed, scores, NEGATIVE), axis=2))
        weights = jnp.where(allowed, jnp.exp(scores - newest[:, :, None]), 0.0)
        totals = totals * jnp.exp(largest - newest) + jnp.sum(weights, axis=2)
        return ((newest, totals), None)

    initial = (
        jnp.full((head_count, row_count), NEGATIVE, jnp.float32),
        jnp.zeros((head_count, row_count), jnp.float32),
    )
    (largest, totals), unused = lax.scan(statistics, initial, jnp.arange(block_count))
    log_total = largest + jnp.log(totals)

    def weighted(output_sum, block_index):
        keys_part, values_part, key_seg, key_pos = key_block(
            whole, geometry, block_index, head_count
        )
        scores, allowed = block_scores(queries, keys_part, key_seg, key_pos, geometry)
        probs = jnp.where(allowed, jnp.exp(scores - log_total[:, :, None]), 0.0).astype(
            jnp.bfloat16
        )
        output_sum = output_sum + jnp.einsum(
            "hqk,khd->qhd", probs, values_part, preferred_element_type=jnp.float32
        )
        return (output_sum, None)

    output_sum, unused = lax.scan(
        weighted, jnp.zeros((row_count, head_count, head_dim), jnp.float32), jnp.arange(block_count)
    )
    return (output_sum, log_total)


def attend_back(queries, whole, log_total, delta_sum, grad_heads, geometry):
    row_count, head_count, head_dim = queries.shape
    block_rows = geometry[4]
    score_scale = geometry[5]
    block_count = whole.shape[0] // block_rows

    def gradients(query_grad, block_index):
        keys_part, values_part, key_seg, key_pos = key_block(
            whole, geometry, block_index, head_count
        )
        scores, allowed = block_scores(queries, keys_part, key_seg, key_pos, geometry)
        probs = jnp.where(allowed, jnp.exp(scores - log_total[:, :, None]), 0.0)
        grad_probs = jnp.einsum(
            "qhd,khd->hqk", grad_heads, values_part, preferred_element_type=jnp.float32
        )
        grad_scores = (probs * (grad_probs - delta_sum[:, :, None])).astype(jnp.bfloat16)
        query_grad = (
            query_grad
            + jnp.einsum("hqk,khd->qhd", grad_scores, keys_part, preferred_element_type=jnp.float32)
            * score_scale
        )
        key_grad = (
            jnp.einsum("hqk,qhd->khd", grad_scores, queries, preferred_element_type=jnp.float32)
            * score_scale
        )
        value_grad = jnp.einsum(
            "hqk,qhd->khd",
            probs.astype(jnp.bfloat16),
            grad_heads,
            preferred_element_type=jnp.float32,
        )
        joined = jnp.concatenate(
            [key_grad.reshape(block_rows, -1), value_grad.reshape(block_rows, -1)], axis=1
        )
        return (query_grad, joined)

    query_grad, stacked = lax.scan(
        gradients,
        jnp.zeros((row_count, head_count, head_dim), jnp.float32),
        jnp.arange(block_count),
    )
    return (query_grad, stacked.reshape(whole.shape[0], -1))


def layer_forward(hidden, layer_index, weights, geometry):
    qkv_weight, out_weight, up_weight, up_bias, down_weight, down_bias, alphas = weights
    row_count, model_width = hidden.shape
    projection = qkv_weight[layer_index]
    rounded = hidden.astype(jnp.bfloat16)
    queries = (
        jnp.dot(rounded, projection[:, :model_width], preferred_element_type=jnp.float32)
        .astype(jnp.bfloat16)
        .reshape(row_count, HEADS, -1)
    )
    key_value = jnp.dot(
        rounded, projection[:, model_width:], preferred_element_type=jnp.float32
    ).astype(jnp.bfloat16)
    whole = lax.all_gather(key_value, "blk", axis=0, tiled=True)
    heads_out, log_total = attend(queries, whole, geometry)
    heads_rounded = heads_out.reshape(row_count, model_width).astype(jnp.bfloat16)
    branch = jnp.dot(heads_rounded, out_weight[layer_index], preferred_element_type=jnp.float32)
    alpha_pair = alphas[layer_index]
    middle = hidden + alpha_pair[0] * branch
    entered = middle.astype(jnp.bfloat16)
    gate_pre = (
        jnp.dot(entered, up_weight[layer_index], preferred_element_type=jnp.float32)
        + up_bias[layer_index]
    )
    activated = gelu_exact(gate_pre).astype(jnp.bfloat16)
    second = (
        jnp.dot(activated, down_weight[layer_index], preferred_element_type=jnp.float32)
        + down_bias[layer_index]
    )
    result = middle + alpha_pair[1] * second
    saved = (
        rounded,
        queries,
        key_value,
        whole,
        heads_out,
        heads_rounded,
        log_total,
        branch,
        entered,
        gate_pre,
        activated,
        second,
    )
    return (result, saved)


def layer_backward(grad_hidden, saved, layer_index, weights, geometry):
    qkv_weight, out_weight, up_weight, up_bias, down_weight, down_bias, alphas = weights
    (
        rounded,
        queries,
        key_value,
        saved_whole,
        heads_out,
        heads_rounded,
        log_total,
        branch,
        entered,
        gate_pre,
        activated,
        second,
    ) = saved
    row_count = grad_hidden.shape[0]
    alpha_pair = alphas[layer_index]
    grad_second = (alpha_pair[1] * grad_hidden).astype(jnp.bfloat16)
    alpha_second = jnp.sum(grad_hidden * second)
    bias_down = jnp.sum(grad_second.astype(jnp.float32), axis=0)
    grad_down = jnp.einsum("tf,td->fd", activated, grad_second, preferred_element_type=jnp.float32)
    grad_act = jnp.einsum(
        "td,fd->tf", grad_second, down_weight[layer_index], preferred_element_type=jnp.float32
    )
    unused, gelu_pull = jax.vjp(gelu_exact, gate_pre)
    grad_gate = gelu_pull(grad_act)[0].astype(jnp.bfloat16)
    bias_up = jnp.sum(grad_gate.astype(jnp.float32), axis=0)
    grad_up = jnp.einsum("td,tf->df", entered, grad_gate, preferred_element_type=jnp.float32)
    grad_middle = grad_hidden + jnp.einsum(
        "tf,df->td", grad_gate, up_weight[layer_index], preferred_element_type=jnp.float32
    )
    grad_branch = (alpha_pair[0] * grad_middle).astype(jnp.bfloat16)
    alpha_first = jnp.sum(grad_middle * branch)
    grad_proj_out = jnp.einsum(
        "te,td->ed", heads_rounded, grad_branch, preferred_element_type=jnp.float32
    )
    grad_heads = (
        jnp.einsum(
            "td,ed->te", grad_branch, out_weight[layer_index], preferred_element_type=jnp.float32
        )
        .astype(jnp.bfloat16)
        .reshape(queries.shape)
    )
    delta_sum = jnp.sum(grad_heads.astype(jnp.float32) * heads_out, axis=2).T
    whole = lax.all_gather(key_value, "blk", axis=0, tiled=True)
    query_grad, key_terms = attend_back(queries, whole, log_total, delta_sum, grad_heads, geometry)
    key_grads = lax.psum_scatter(
        key_terms.astype(jnp.bfloat16), "blk", scatter_dimension=0, tiled=True
    )
    grad_proj = jnp.concatenate(
        [query_grad.reshape(row_count, -1).astype(jnp.bfloat16), key_grads], axis=1
    )
    grad_qkv = jnp.einsum("td,te->de", rounded, grad_proj, preferred_element_type=jnp.float32)
    grad_input = grad_middle + jnp.einsum(
        "te,de->td", grad_proj, qkv_weight[layer_index], preferred_element_type=jnp.float32
    )
    layer_grads = (
        grad_qkv,
        grad_proj_out,
        grad_up,
        bias_up,
        grad_down,
        bias_down,
        jnp.stack([alpha_first, alpha_second]),
    )
    return (grad_input, layer_grads)


def reduce_all(layer_results, cycle_size):
    stacked = [
        jnp.stack([layer_entry[member] for layer_entry in layer_results], axis=0)
        for member in range(6)
    ]
    alpha_tiles = jnp.stack(
        [jnp.tile(layer_entry[6], cycle_size) for layer_entry in layer_results], axis=0
    )
    shares = (
        lax.psum_scatter(
            stacked[0].astype(jnp.bfloat16), "blk", scatter_dimension=1, tiled=True
        ).astype(jnp.float32),
        lax.psum_scatter(
            stacked[1].astype(jnp.bfloat16), "blk", scatter_dimension=1, tiled=True
        ).astype(jnp.float32),
        lax.psum_scatter(
            stacked[2].astype(jnp.bfloat16), "blk", scatter_dimension=1, tiled=True
        ).astype(jnp.float32),
        lax.psum_scatter(
            stacked[3].astype(jnp.bfloat16), "blk", scatter_dimension=1, tiled=True
        ).astype(jnp.float32),
        lax.psum_scatter(
            stacked[4].astype(jnp.bfloat16), "blk", scatter_dimension=1, tiled=True
        ).astype(jnp.float32),
        lax.psum_scatter(
            stacked[5].astype(jnp.bfloat16), "blk", scatter_dimension=1, tiled=True
        ).astype(jnp.float32),
        lax.psum_scatter(
            alpha_tiles.astype(jnp.bfloat16), "blk", scatter_dimension=1, tiled=True
        ).astype(jnp.float32),
    )
    return (
        lax.psum(shares[0].astype(jnp.bfloat16), "grp").astype(jnp.float32),
        lax.psum(shares[1].astype(jnp.bfloat16), "grp").astype(jnp.float32),
        lax.psum(shares[2].astype(jnp.bfloat16), "grp").astype(jnp.float32),
        lax.psum(shares[3].astype(jnp.bfloat16), "grp").astype(jnp.float32),
        lax.psum(shares[4].astype(jnp.bfloat16), "grp").astype(jnp.float32),
        lax.psum(shares[5].astype(jnp.bfloat16), "grp").astype(jnp.float32),
        lax.psum(shares[6].astype(jnp.bfloat16), "grp").astype(jnp.float32),
    )


def body(
    tokens,
    seq_len,
    qkv_weight,
    out_weight,
    up_weight,
    up_bias,
    down_weight,
    down_bias,
    alphas,
    cotangent,
):
    row_count, model_width = tokens.shape
    cycle_size = lax.axis_size("blk")
    cycle_place = lax.axis_index("blk")
    head_dim = model_width // HEADS
    total_rows = cycle_size * row_count
    block_rows = min(max(row_count, 512), total_rows)
    segment, offset, span_rows = layout(seq_len, row_count, cycle_size)
    query_pos = cycle_place * span_rows + offset
    seg_all = jnp.tile(segment, cycle_size)
    pos_all = jnp.repeat(jnp.arange(cycle_size, dtype=jnp.int32), row_count) * jnp.tile(
        span_rows, cycle_size
    ) + jnp.tile(offset, cycle_size)
    geometry = (segment, query_pos, seg_all, pos_all, block_rows, head_dim ** (-0.5))
    weights = (qkv_weight, out_weight, up_weight, up_bias, down_weight, down_bias, alphas)
    hidden = tokens.astype(jnp.float32)
    saved_layers = []
    for layer_index in range(LAYERS):
        hidden, saved = layer_forward(hidden, layer_index, weights, geometry)
        saved_layers.append(saved)
    output = hidden.astype(jnp.bfloat16)
    grad_hidden = cotangent.astype(jnp.float32)
    layer_results = []
    for layer_index in reversed(range(LAYERS)):
        grad_hidden, layer_grads = layer_backward(
            grad_hidden, saved_layers[layer_index], layer_index, weights, geometry
        )
        layer_results.insert(0, layer_grads)
    finals = reduce_all(layer_results, cycle_size)
    return (
        output,
        grad_hidden,
        finals[0],
        finals[1],
        finals[2],
        finals[3],
        finals[4],
        finals[5],
        finals[6],
    )


def solution(mesh):
    placed = (
        P(("grp", "blk"), None),
        P("grp", None),
        P(),
        P(),
        P(),
        P(),
        P(),
        P(),
        P(),
        P(("grp", "blk"), None),
    )
    sizes = (mesh.shape["grp"], mesh.shape["blk"])
    return jax.shard_map(
        fast_body if sizes == (4, RUNS) else body,
        mesh=mesh,
        in_specs=placed,
        out_specs=(
            P(("grp", "blk"), None),
            P(("grp", "blk"), None),
            P(None, "blk", None),
            P(None, "blk", None),
            P(None, "blk", None),
            P(None, "blk"),
            P(None, "blk", None),
            P(None, "blk"),
            P(),
        ),
        check_vma=False,
    )
```

```python
import functools

import jax
import jax.numpy as jnp
from jax import lax
from jax.experimental import pallas as pl
from jax.experimental.pallas import tpu as pltpu
from jax.sharding import PartitionSpec as P

HEADS = 8
LAYERS = 2
NEGATIVE = -1e30
MESH = pl.DeviceIdType.MESH
F32 = jnp.float32
BF16 = jnp.bfloat16

HALF = 128
RUNS = 8
TEAM = 4
OWN = RUNS // TEAM
DIM = 64
WIDTH = 512
FF = 2048
CUT = 512
TILE = 256
TILES = HALF * RUNS // TILE
PACK = HALF + DIM
CHUNK = 576
SMALL = FF + WIDTH + 128
PARTS = ((1, 0, 320), (1, 320, 256), (0, 0, 320), (0, 320, 256))
SHARES = ((192, 0, 128), (160, 16, 80), (160, 112, 48), (128, 96, 32))


def spans():
    places, totals = {}, [0, 0, 0]
    for part, counts in enumerate(SHARES):
        first = PARTS[part][1]
        for route, count in enumerate(counts):
            places[part, route] = (first, totals[route], count)
            first += count
            totals[route] += count
    return places, totals


SPANS, TOTALS = spans()

SLOPE_AT = 0.28
TAIL = (
    0.11652077851573843,
    0.06749675579450809,
    0.2689101589486142,
    -0.23699347299932225,
    0.3898740127620002,
    -0.10580824228351815,
)


def nn(a, b):
    return lax.dot_general(a, b, (((1,), (0,)), ((), ())), preferred_element_type=F32)


def nt(a, b):
    return lax.dot_general(a, b, (((1,), (1,)), ((), ())), preferred_element_type=F32)


def layers_kernel(
    tokens, seq_len, alphas, up_bias_hbm, down_bias_hbm, cotangent, qkv_hbm, out_hbm, up_hbm, down_hbm,
    final, heads_all, out_in, grad_in, small_final,
    wqkv, wout, wup, wdown, up_bias, down_bias,
    tok_in, cot_in, flag_out, flag_in, back_out,
    hidden, grad, hid_all, attn_t, entered, act, branch, slope, second,
    dz, du, da, dqkv,
    pack_out, head_out, pack_in, o_in, do_in,
    kv, kv_t, rq, ro, o_t, lse, acc, dq_t, bias,
    parts, core_in, xa_in, xb_in, ya_in, yb_in, z_in, third_z, third_x, third_y,
    heads_out, heads_x, heads_z, heads_sum, small, small_in, small_z, small_sum,
    w_sem, move_send, move_recv, a2a_send, a2a_recv, core_send, core_recv, x_send, x_recv, y_send, y_recv,
    z_send, z_recv, fin_send, fin_recv, hid_send, hid_recv, hx_send, hx_recv, hz_send, hz_recv, hf_send, hf_recv,
    small_send, small_recv, core_free,
):
    grp = lax.axis_index("grp")
    blk = lax.axis_index("blk")
    core = lax.rem(grp, 2)
    side = lax.div(grp, 2)
    yy = lax.rem(blk, 2)
    zz = lax.div(blk, 2)
    member = 2 * core + yy
    far_side = 2 * (1 - side) + core
    low = lax.broadcasted_iota(jnp.int32, (HALF, 128), 1) < DIM

    def place(c, x, z, y):
        return (2 * x + c, 2 * z + y)

    core_peer = place(1 - core, side, zz, yy)
    x_peer = place(core, 1 - side, zz, yy)
    y_peer = place(core, side, zz, 1 - yy)

    def remote(source, target, send, recv, peer):
        return pltpu.make_async_remote_copy(
            src_ref=source,
            dst_ref=target,
            send_sem=send,
            recv_sem=recv,
            device_id=peer,
            device_id_type=MESH,
        )

    def credit(semaphore, peer, count=1):
        pl.semaphore_signal(semaphore, inc=count, device_id=peer, device_id_type=MESH)

    def moved(kind, slot, source, target, at, core_at, z_at):
        here = jnp.logical_and(core_at == core, z_at == zz)

        @pl.when(here)
        def _():
            pltpu.make_async_copy(source, target.at[at], move_recv.at[kind, at]).start()

        @pl.when(jnp.logical_not(here))
        def _():
            pltpu.make_async_remote_copy(
                src_ref=source,
                dst_ref=target.at[at],
                send_sem=move_send.at[kind, slot],
                recv_sem=move_recv.at[kind, at],
                device_id=place(core_at, side, z_at, yy),
                device_id_type=MESH,
            ).start()

    def move_left(kind, slot, source, core_at, z_at):
        here = jnp.logical_and(core_at == core, z_at == zz)

        @pl.when(jnp.logical_not(here))
        def _():
            pltpu.make_async_copy(source, source, move_send.at[kind, slot]).wait()

    def move_arrived(kind, at, target):
        pltpu.make_async_copy(target.at[at], target.at[at], move_recv.at[kind, at]).wait()

    def to_team(kind, half, source, target):
        moved(kind, half, source, target, lax.div(zz, 2), lax.rem(zz, 2), 2 * half + core)

    def to_team_left(kind, half, source):
        move_left(kind, half, source, lax.rem(zz, 2), 2 * half + core)

    def to_owner(kind, chunk, source, target):
        moved(kind, chunk, source, target, lax.div(zz, 2), lax.rem(zz, 2), core + 2 * chunk)

    def to_owner_left(kind, chunk, source):
        move_left(kind, chunk, source, lax.rem(zz, 2), core + 2 * chunk)

    def half_of(ref, half):
        return ref.at[pl.ds(pl.multiple_of(HALF * half, HALF), HALF)]

    def rows_of(half):
        return pl.ds(pl.multiple_of(half * HALF, HALF), HALF)

    def slot_of(other):
        return lax.rem(other + TEAM - member, TEAM)

    def exchange(kind, layer, half, outgoing, incoming, head=None):
        at = () if head is None else (head,)
        incoming[(half, 0, *at)] = outgoing[(half, member, *at)]
        for step in range(1, TEAM):
            peer = lax.rem(member + step, TEAM)
            remote(
                outgoing.at[(half, peer, *at)],
                incoming.at[(half, TEAM - step, *at)],
                a2a_send.at[kind, layer, half, head or 0],
                a2a_recv.at[kind, layer, half, head or 0],
                place(lax.div(peer, 2), side, zz, lax.rem(peer, 2)),
            ).start()

    def arrived(kind, layer, half, incoming, head=None):
        at = () if head is None else (head,)
        whole = incoming.at[(half, pl.ds(1, TEAM - 1), *at)]
        pltpu.make_async_copy(whole, whole, a2a_recv.at[kind, layer, half, head or 0]).wait()

    def left(kind, layer, half, outgoing):
        for head in range(OWN) if kind in (0, 3) else (None,):
            at = () if head is None else (head,)
            whole = outgoing.at[(half, pl.ds(1, TEAM - 1), *at)]
            pltpu.make_async_copy(whole, whole, a2a_send.at[kind, layer, half, head or 0]).wait()

    def tokens_of(chunk, other):
        return pl.ds(pl.multiple_of(HALF * (TEAM * chunk + other), HALF), HALF)

    def hidden_copy(layer, chunk, which):
        whose = 2 * core + 1 - yy if which == 2 else member
        block = hid_all.at[layer, :, tokens_of(chunk, whose)]
        return remote(
            block,
            block,
            hid_send.at[layer, chunk, which],
            hid_recv.at[layer, chunk, which],
            y_peer if which == 0 else core_peer,
        )

    def hidden_start(layer, chunk):
        for which in range(2):
            hidden_copy(layer, chunk, which).start()

    def hidden_pass(layer, chunk):
        hidden_copy(layer, chunk, 0).wait()
        hidden_copy(layer, chunk, 2).start()

    def hidden_done(layer, chunk):
        for which in range(1, 3):
            hidden_copy(layer, chunk, which).wait()

    def project(layer, half):
        rows = rows_of(half)
        rounded = hidden[rows, :].astype(BF16)
        if layer == 1:
            left(0, 0, half, pack_out)
        queries = nn(rounded, wqkv[layer, :, 0:WIDTH]) * (DIM ** -0.5)
        queries_t = queries.T.astype(BF16)
        keys = nn(rounded, wqkv[layer, :, WIDTH : 2 * WIDTH])
        values = nn(rounded, wqkv[layer, :, 2 * WIDTH : 3 * WIDTH])
        for pair in range(RUNS // 2):
            k_pair = keys[:, 128 * pair : 128 * pair + 128]
            v_pair = values[:, 128 * pair : 128 * pair + 128]
            first = jnp.where(low, k_pair, pltpu.roll(v_pair, DIM, 1))
            other = jnp.where(low, pltpu.roll(k_pair, DIM, 1), v_pair)
            pack_out[half, pair, 0, 0:HALF, :] = first.astype(BF16)
            pack_out[half, pair, 1, 0:HALF, :] = other.astype(BF16)
        for head in range(RUNS):
            pack_out[half, head // 2, head % 2, HALF:, :] = queries_t[DIM * head : DIM * head + DIM, :]
        for head in range(OWN):
            exchange(0, layer, half, pack_out, pack_in, head)
        hid_all[layer, :, tokens_of(half, member)] = rounded.T

    def attend(layer, chunk):
        if layer == 1:
            left(1, 0, chunk, head_out)

        def one_head(head, carry):
            arrived(0, layer, chunk, pack_in, head)
            for other in range(TEAM):
                slot = slot_of(other)
                start = HALF * (TEAM * chunk + other)
                span = slice(start, start + HALF)
                block = pack_in[chunk, slot, head, 0:HALF, :]
                kv[layer, head, span, :] = block
                kv_t[layer, head, :, span] = block.T
                rq[layer, head, 0:DIM, span] = pack_in[chunk, slot, head, HALF:, :]

            def scores_of(i):
                count = TILE * (i + 1)
                tile = rq[layer, head, :, TILE * i : TILE * i + TILE]
                return nn(kv[layer, head, 0:count, :], tile) + bias[TILE * TILES - count :, :]

            ahead = [scores_of(i) for i in (2 * chunk, 2 * chunk + 1)]
            for i in (2 * chunk, 2 * chunk + 1):
                columns = slice(TILE * i, TILE * i + TILE)
                count = TILE * (i + 1)
                scores = ahead[i - 2 * chunk]
                largest = jnp.max(scores, axis=0, keepdims=True)
                weight = jnp.exp(scores - largest)
                total = jnp.sum(weight, axis=0, keepdims=True)
                summed = nn(kv_t[layer, head, DIM:, 0:count], weight.astype(BF16))
                summed = summed / total
                o_t[layer, head, :, columns] = summed
                lse[layer, head, :, columns] = largest + jnp.log(total)
                rounded = summed.astype(BF16)
                for part in range(2):
                    head_out[chunk, 2 * (i - 2 * chunk) + part, head] = rounded[
                        :, HALF * part : HALF * part + HALF
                    ]
            return carry

        for head in range(OWN):
            one_head(head, 0)
        exchange(1, layer, chunk, head_out, o_in)

    def feed(layer, half):
        rows = rows_of(half)
        arrived(1, layer, half, o_in)
        for head in range(RUNS):
            attn_t[layer, DIM * head : DIM * head + DIM, rows] = o_in[half, slot_of(head // 2), head % 2]
        attn = attn_t[layer, :, rows].T
        grown = nn(attn, wout[layer])
        branch[layer, rows, :] = grown
        middle = hidden[rows, :] + alphas[layer, 0] * grown
        rounded = middle.astype(BF16)
        entered[layer, rows, :] = rounded
        total = jnp.zeros((HALF, WIDTH), F32)

        def gate_of(step):
            cut = slice(CUT * step, CUT * step + CUT)
            return nn(rounded, wup[layer, :, cut]) + up_bias[layer : layer + 1, cut]

        coming = gate_of(0)
        for step in range(FF // CUT):
            cut = slice(CUT * step, CUT * step + CUT)
            gate = coming
            if step + 1 < FF // CUT:
                coming = gate_of(step + 1)
            bell = jnp.exp(gate * gate * -0.5)
            near = pl.reciprocal(1.0 + SLOPE_AT * jnp.abs(gate), approx=True)
            tail = jnp.full_like(gate, TAIL[5])
            for factor in TAIL[4::-1]:
                tail = tail * near + factor
            tail = bell * (tail * near)
            risen = jnp.where(gate > 0.0, 1.0 - tail, tail)
            slope[layer, rows, cut] = risen + gate * bell * 0.3989422804014327
            active = (gate * risen).astype(BF16)
            act[layer, rows, cut] = active
            total = total + nn(active, wdown[layer, cut, :])
        total = total + down_bias[layer : layer + 1, :]
        second[layer, rows, :] = total
        hidden[rows, :] = middle + alphas[layer, 1] * total

    def total_of(values):
        return jnp.sum(jnp.sum(values, axis=0, keepdims=True), axis=1, keepdims=True)

    def feed_back(layer):
        start = grad[...]
        if layer == 0:
            dz[...] = (alphas[layer, 1] * start).astype(BF16)
        scaled = dz[...]
        alpha_second = total_of(start * second[layer])
        small[layer : layer + 1, FF : FF + WIDTH] = jnp.sum(scaled.astype(F32), axis=0, keepdims=True)
        middle = start
        coming = nt(scaled, wdown[layer, 0:CUT, :])
        for step in range(FF // CUT):
            cut = slice(CUT * step, CUT * step + CUT)
            raw = coming
            if step + 1 < FF // CUT:
                coming = nt(scaled, wdown[layer, CUT * (step + 1) : CUT * (step + 2), :])
            gate = (raw * slope[layer, :, cut]).astype(BF16)
            du[:, cut] = gate
            small[layer : layer + 1, cut] = jnp.sum(gate.astype(F32), axis=0, keepdims=True)
            middle = middle + nt(gate, wup[layer, :, cut])
        grad[...] = middle
        mixed = (alphas[layer, 0] * middle).astype(BF16)
        da[...] = mixed
        spread = nt(wout[layer], mixed).astype(BF16)
        for chunk in (1, 0):
            left(*((1, 1) if layer == 1 else (2, 1)), chunk, head_out)
            for head in range(RUNS):
                head_out[chunk, head // 2, head % 2] = spread[
                    DIM * head : DIM * head + DIM, HALF * chunk : HALF * chunk + HALF
                ]
            exchange(2, layer, chunk, head_out, do_in)
        alpha_first = total_of(middle * branch[layer])
        column = lax.broadcasted_iota(jnp.int32, (1, 128), 1)
        small[layer : layer + 1, FF + WIDTH :] = jnp.where(
            column == 0, alpha_first, jnp.where(column == 1, alpha_second, 0.0)
        )

    def attend_back(layer, chunk):
        arrived(2, layer, chunk, do_in)
        left(*((0, 1) if layer == 1 else (3, 1)), chunk, pack_out)

        def one_head(head, carry):
            for other in range(TEAM):
                start = HALF * (TEAM * chunk + other)
                ro[head, DIM:, start : start + HALF] = do_in[chunk, slot_of(other), head]
            for i in (2 * chunk, 2 * chunk + 1):
                columns = slice(TILE * i, TILE * i + TILE)
                query_tile = rq[layer, head, :, columns]
                grad_tile = ro[head, :, columns]
                log_total = lse[layer, head, :, columns]
                delta = jnp.sum(
                    ro[head, DIM:, columns].astype(F32) * o_t[layer, head, :, columns],
                    axis=0,
                    keepdims=True,
                )
                count = TILE * (i + 1)
                keys = kv[layer, head, 0:count, :]
                weight = jnp.exp(nn(keys, query_tile) + bias[TILE * TILES - count :, :] - log_total)
                scored = (weight * (nn(keys, grad_tile) - delta)).astype(BF16)
                term = nt(scored, query_tile) + nt(weight.astype(BF16), grad_tile)
                if chunk == 1 and i == 2:
                    acc[head, 0:count, :] = term
                elif chunk == 1:
                    acc[head, 0 : count - TILE, :] += term[0 : count - TILE, :]
                    acc[head, count - TILE : count, :] = term[count - TILE :, :]
                else:
                    acc[head, 0:count, :] += term
                query_grad = nn(kv_t[layer, head, 0:DIM, 0:count], scored)
                dq_t[head, :, columns] = query_grad * (DIM ** -0.5)
            for other in range(TEAM):
                start = HALF * (TEAM * chunk + other)
                span = slice(start, start + HALF)
                pack_out[chunk, other, head, 0:HALF, :] = acc[head, span, :].astype(BF16)
                pack_out[chunk, other, head, HALF:, :] = dq_t[head, :, span].astype(BF16)
            exchange(3, layer, chunk, pack_out, pack_in, head)
            return carry

        for head in range(OWN):
            one_head(head, 0)

    def project_back(layer, half):
        for head in range(OWN):
            arrived(3, layer, half, pack_in, head)
        turned = jnp.concatenate(
            [pack_in[half, slot_of(head // 2), head % 2, HALF:, :] for head in range(RUNS)], axis=0
        )
        dqkv[:, 0:WIDTH] = turned.T
        for pair in range(RUNS // 2):
            first = pack_in[half, slot_of(pair), 0, 0:HALF, :].astype(F32)
            other = pack_in[half, slot_of(pair), 1, 0:HALF, :].astype(F32)
            k_pair = jnp.where(low, first, pltpu.roll(other, DIM, 1))
            v_pair = jnp.where(low, pltpu.roll(first, DIM, 1), other)
            dqkv[:, WIDTH + 128 * pair : WIDTH + 128 * pair + 128] = k_pair.astype(BF16)
            dqkv[:, 2 * WIDTH + 128 * pair : 2 * WIDTH + 128 * pair + 128] = v_pair.astype(BF16)
        rows = rows_of(half)
        grad[rows, :] = grad[rows, :] + nt(dqkv[...], wqkv[layer])

    def scatter_rows(layer, result, first_row):
        for run in range(RUNS):
            for quarter in range(4):
                parts[layer, quarter % 2, quarter // 2, run // 2, run % 2, first_row : first_row + DIM, :] = result[
                    DIM * run : DIM * run + DIM, 128 * quarter : 128 * quarter + 128
                ].astype(BF16)

    def make(part):
        layer, first, count = PARTS[part]
        if first < 256:
            turned = entered[layer].T
        for row in range(first, min(first + count, 256), DIM):
            step = row // DIM
            scatter_rows(layer, nn(turned, du[:, CUT * step : CUT * step + CUT]), row)
        if first <= 256 < first + count:
            scatter_rows(layer, nn(attn_t[layer], da[...]), 256)
        if first >= 320:
            for run in range(RUNS):
                at = TILE * run + first - 320
                result = nn(act[layer, :, at : at + count].T, dz[...])
                for quarter in range(4):
                    parts[layer, quarter % 2, quarter // 2, run // 2, run % 2, first : first + count, :] = result[
                        :, 128 * quarter : 128 * quarter + 128
                    ].astype(BF16)
        if layer == 0:
            pl.semaphore_wait(core_free.at[0 if first < 320 else 1], 1)
        core_copy(part).start()

    def heads_grads(layer):
        for chunk in range(2):
            hidden_done(layer, chunk)
        blocks = [(run // TEAM, run % TEAM) for run in range(RUNS)]
        keys_values = jnp.concatenate(
            [
                jnp.concatenate([pack_out[chunk, other, head, 0:HALF, :] for chunk, other in blocks], axis=0)
                for head in range(OWN)
            ],
            axis=1,
        )
        queries = jnp.concatenate(
            [
                jnp.concatenate([pack_out[chunk, other, head, HALF:, :] for chunk, other in blocks], axis=1)
                for head in range(OWN)
            ],
            axis=0,
        )
        both = nn(hid_all[layer], keys_values)
        q_part = nt(hid_all[layer], queries)
        first, other = both[:, 0:128], both[:, 128:256]
        left_half = lax.broadcasted_iota(jnp.int32, (WIDTH, 128), 1) < DIM
        k_part = jnp.where(left_half, first, pltpu.roll(other, DIM, 1))
        v_part = jnp.where(left_half, pltpu.roll(first, DIM, 1), other)
        for number, values in enumerate((q_part, k_part, v_part)):
            for run in range(RUNS):
                heads_out[layer, run // 2, run % 2, :, 128 * number : 128 * number + 128] = values[
                    DIM * run : DIM * run + DIM, :
                ].astype(BF16)
        heads_x_copy(layer).start()

    def half_rows(which):
        return pl.ds(pl.multiple_of(32 * which, 32), 32)

    def heads_x_copy(layer):
        return remote(
            heads_out.at[layer, :, :, half_rows(1 - side)],
            heads_x.at[layer],
            hx_send.at[layer],
            hx_recv.at[layer],
            x_peer,
        )

    def heads_z_copy(layer, step):
        peer = lax.rem(zz + step, 4)
        return remote(
            heads_out.at[layer, peer, :, half_rows(side)],
            heads_z.at[layer, 4 - step],
            hz_send.at[layer, step],
            hz_recv.at[layer, 4 - step],
            place(core, side, peer, yy),
        )

    def heads_last_copy(layer, number):
        x, c, y = number // 4, number // 2 % 2, number % 2
        return remote(
            heads_sum.at[layer, 1 - yy if y else yy],
            heads_all.at[layer, side, member],
            hf_send.at[layer, number],
            hf_recv.at[layer, number],
            place(1 - core if c else core, 1 - side if x else side, zz, 1 - yy if y else yy),
        )

    def heads_second(layer):
        heads_x_copy(layer).wait()
        heads_out[layer, :, :, half_rows(side), :] += heads_x[layer]
        for step in range(1, 4):
            heads_z_copy(layer, step).start()

    def heads_third(layer):
        for step in range(1, 4):
            heads_z_copy(layer, step).wait()
        total = heads_out[layer, zz, :, half_rows(side), :].astype(F32)
        for slot in range(1, 4):
            total = total + heads_z[layer, slot].astype(F32)
        heads_sum[layer] = total.astype(BF16)
        heads_all[layer, side, member] = heads_sum[layer, yy]
        for number in range(1, 8):
            heads_last_copy(layer, number).start()

    def heads_done(layer):
        for number in range(1, 8):
            heads_last_copy(layer, number).wait()

    def rows_in(part, route):
        first, room, count = SPANS[part, route]
        return pl.ds(first, count), pl.ds(room, count)

    def used(part, route):
        return SHARES[part][route] > 0

    def core_copy(part):
        layer, first, count = PARTS[part]
        rows = pl.ds(first, count)
        return remote(
            parts.at[layer, 1 - core, :, :, :, rows],
            core_in.at[:, :, :, rows],
            core_send.at[part],
            core_recv.at[part],
            core_peer,
        )

    def x_copy(part, route):
        layer = PARTS[part][0]
        rows, room = rows_in(part, route)
        ends = (x_send.at[part, route], x_recv.at[part, route], x_peer)
        mine = parts.at[layer, core, 1 - side]
        if route == 0:
            return remote(mine.at[:, :, rows], xa_in.at[:, :, room], *ends)
        if route == 1:
            return remote(mine.at[:, yy, rows], xb_in.at[:, room], *ends)
        return remote(mine.at[zz, :, rows], third_x.at[:, room], *ends)

    def y_copy(part, route):
        layer = PARTS[part][0]
        rows, room = rows_in(part, route)
        ends = (y_send.at[part, route], y_recv.at[part, route], y_peer)
        mine = parts.at[layer, core]
        if route == 0:
            return remote(mine.at[side, :, 1 - yy, rows], ya_in.at[:, room], *ends)
        if route == 1:
            return remote(mine.at[:, :, 1 - yy, rows], yb_in.at[:, :, room], *ends)
        return remote(mine.at[side, zz, 1 - yy, rows], third_y.at[room], *ends)

    def z_copy(part, route, step):
        layer = PARTS[part][0]
        rows, room = rows_in(part, route)
        peer = lax.rem(zz + step, 4)
        ends = (z_send.at[part, route, step], z_recv.at[part, route, 4 - step], place(core, side, peer, yy))
        if route == 2:
            return remote(parts.at[layer, core, :, peer, :, rows], third_z.at[4 - step, :, :, room], *ends)
        return remote(parts.at[layer, core, side, peer, yy, rows], z_in.at[layer, 4 - step, rows], *ends)

    def final_copy(part, which):
        layer, first, count = PARTS[part]
        block = final.at[layer, far_side if which == 2 else grp, pl.ds(first, count)]
        return remote(
            block,
            block,
            fin_send.at[part, which],
            fin_recv.at[part, which],
            x_peer if which == 0 else core_peer,
        )

    def core_done(part):
        layer, first, count = PARTS[part]
        rows = pl.ds(first, count)
        core_copy(part).wait()
        for across in (1 - side, side):
            parts[layer, core, across, :, :, rows, :] += core_in[across, :, :, rows, :]
            if used(part, 0) and across is not side:
                x_copy(part, 0).start()
        if used(part, 1):
            y_copy(part, 1).start()
        if used(part, 2):
            for step in range(1, 4):
                z_copy(part, 2, step).start()
        if layer == 1:
            freed = 0 if first < 320 else 1
            followers = [1 for other in PARTS if other[0] == 0 and (other[1] >= 320) == (freed == 1)]
            credit(core_free.at[freed], core_peer, len(followers))

    def first_x(part):
        if used(part, 0):
            layer = PARTS[part][0]
            rows, room = rows_in(part, 0)
            x_copy(part, 0).wait()
            for y in (1 - yy, yy):
                parts[layer, core, side, :, y, rows, :] += xa_in[:, y, room, :]
                if y is not yy:
                    y_copy(part, 0).start()

    def first_y(part):
        if used(part, 1):
            layer = PARTS[part][0]
            rows, room = rows_in(part, 1)
            y_copy(part, 1).wait()
            for across in (1 - side, side):
                parts[layer, core, across, :, yy, rows, :] += yb_in[across, :, room, :]
                if across is not side:
                    x_copy(part, 1).start()

    def first_z(part):
        if used(part, 2):
            layer = PARTS[part][0]
            rows, room = rows_in(part, 2)
            for step in range(1, 4):
                z_copy(part, 2, step).wait()
            for across in (1 - side, side):
                total = parts[layer, core, across, zz, :, rows, :].astype(F32)
                for slot in range(1, 4):
                    total = total + third_z[slot, across, :, room, :].astype(F32)
                parts[layer, core, across, zz, :, rows, :] = total.astype(BF16)
                if across is not side:
                    x_copy(part, 2).start()

    def second_x(part):
        if used(part, 0):
            layer = PARTS[part][0]
            rows, room = rows_in(part, 0)
            y_copy(part, 0).wait()
            parts[layer, core, side, :, yy, rows, :] += ya_in[:, room, :]
            for step in range(1, 4):
                z_copy(part, 0, step).start()

    def second_y(part):
        if used(part, 1):
            layer = PARTS[part][0]
            rows, room = rows_in(part, 1)
            x_copy(part, 1).wait()
            parts[layer, core, side, :, yy, rows, :] += xb_in[:, room, :]
            for step in range(1, 4):
                z_copy(part, 1, step).start()

    def second_z(part):
        if used(part, 2):
            layer = PARTS[part][0]
            rows, room = rows_in(part, 2)
            x_copy(part, 2).wait()
            for y in (1 - yy, yy):
                parts[layer, core, side, zz, y, rows, :] += third_x[y, room, :]
                if y is not yy:
                    y_copy(part, 2).start()

    def third_done(part):
        layer = PARTS[part][0]
        for route in range(3):
            if not used(part, route):
                continue
            rows, room = rows_in(part, route)
            if route == 2:
                y_copy(part, 2).wait()
                final[layer, grp, rows, :] = parts[layer, core, side, zz, yy, rows, :] + third_y[room, :]
            else:
                for step in range(1, 4):
                    z_copy(part, route, step).wait()
                total = parts[layer, core, side, zz, yy, rows, :].astype(F32)
                for slot in range(1, 4):
                    total = total + z_in[layer, slot, rows, :].astype(F32)
                final[layer, grp, rows, :] = total.astype(BF16)
        for which in range(2):
            final_copy(part, which).start()

    def final_pass(part):
        final_copy(part, 0).wait()
        final_copy(part, 2).start()

    def final_done(part):
        for which in range(1, 3):
            final_copy(part, which).wait()

    def small_copy(stage):
        peer = (core_peer, x_peer, y_peer)[stage]
        return remote(
            small_sum.at[stage], small_in.at[stage], small_send.at[stage], small_recv.at[stage], peer
        )

    def small_z_copy(step):
        return remote(
            small_z.at[zz],
            small_z.at[zz],
            small_send.at[2 + step],
            small_recv.at[2 + step],
            place(core, side, lax.rem(zz + step, 4), yy),
        )

    def small_start():
        small_sum[0] = small[...]
        small_copy(0).start()

    def small_next(stage):
        small_copy(stage).wait()
        total = small_sum[stage] + small_in[stage]
        if stage < 2:
            small_sum[stage + 1] = total
            small_copy(stage + 1).start()
        else:
            small_z[zz] = total
            for step in range(1, 4):
                small_z_copy(step).start()

    def small_done():
        for step in range(1, 4):
            small_z_copy(step).wait()
        small_sum[0] = (small_z[0] + small_z[1]) + (small_z[2] + small_z[3])
        small_final[:, 0:256] = small_sum[0, :, pl.ds(pl.multiple_of(blk * 256, 256), 256)]
        pair = small_sum[0, :, pl.ds(pl.multiple_of(FF + 128 * zz, 128), 128)]
        small_final[:, 256:384] = jnp.where(yy == 1, pltpu.roll(pair, DIM, 1), pair)
        small_final[:, 384:512] = small_sum[0, :, FF + WIDTH :]

    def halves(*phases, first=0):
        def both(step, carry):
            for phase in phases:
                phase(lax.rem(step + first, 2))
            return carry

        lax.fori_loop(0, 2, both, 0)

    def begin(half):
        move_arrived(0, half, tok_in)
        hidden[rows_of(half), :] = tok_in[half].astype(F32)

    def finish(half):
        back_out[0, half] = hidden[rows_of(half), :].astype(BF16)
        to_owner(3, half, back_out.at[0, half], out_in)

    def turn_round(layer, half):
        move_arrived(2, half, cot_in)
        rows = rows_of(half)
        grad[rows, :] = cot_in[half].astype(F32)
        dz[rows, :] = (alphas[layer, 1] * grad[rows, :]).astype(BF16)

    def hand_back(half):
        back_out[1, half] = grad[rows_of(half), :].astype(BF16)
        to_owner(4, half, back_out.at[1, half], grad_in)

    barrier = pltpu.get_barrier_semaphore()
    for step in range(1, 4):
        credit(barrier, place(core, side, lax.rem(zz + step, 4), yy))
    for step in range(4):
        credit(barrier, place(1 - core, side, lax.rem(zz + step, 4), yy))
    for peer in (
        x_peer,
        y_peer,
        place(1 - core, side, zz, 1 - yy),
        place(1 - core, 1 - side, zz, yy),
        place(core, 1 - side, zz, 1 - yy),
        place(1 - core, 1 - side, zz, 1 - yy),
    ):
        credit(barrier, peer)

    weight_copies = {}
    for layer in range(LAYERS):
        for number, (source, target) in enumerate(
            ((qkv_hbm, wqkv), (out_hbm, wout), (up_hbm, wup), (down_hbm, wdown))
        ):
            weight_copies[layer, number] = pltpu.make_async_copy(
                source.at[layer], target.at[layer], w_sem.at[layer, number]
            )
    bias_copies = [
        pltpu.make_async_copy(up_bias_hbm, up_bias, w_sem.at[2, 0]),
        pltpu.make_async_copy(down_bias_hbm, down_bias, w_sem.at[2, 1]),
    ]
    weight_copies[0, 0].start()
    pl.semaphore_wait(barrier, 13)
    upper = lax.div(zz, 2)
    for half in (1 - upper, upper):
        to_team(0, half, half_of(tokens, half), tok_in)
    for copy in (*list(weight_copies.values())[1:], *bias_copies):
        copy.start()
    end_second = lax.div(seq_len[0, 0] + seq_len[0, 1], RUNS)
    flag_out[...] = jnp.full((8, 128), end_second.astype(F32), F32)
    for half in (1 - upper, upper):
        to_team(1, half, flag_out, flag_in)
    for layer in range(LAYERS):
        for head in range(OWN):
            rq[layer, head, DIM:, :] = jnp.zeros((DIM, HALF * RUNS), BF16)
    for head in range(OWN):
        ro[head, 0:DIM, :] = jnp.zeros((DIM, HALF * RUNS), BF16)
    weight_copies[0, 0].wait()
    halves(begin, functools.partial(project, 0), first=upper)
    for half in (1 - upper, upper):
        to_team(2, half, half_of(cotangent, half), cot_in)

    move_arrived(1, 0, flag_in)
    move_arrived(1, 1, flag_in)
    border = jnp.concatenate([flag_in[0, 0:1, :]] * 2, axis=1) - (HALF * lax.div(zz, 2)).astype(F32)
    key_row = lax.broadcasted_iota(jnp.int32, (TILE, TILE), 0)
    query_col = lax.broadcasted_iota(jnp.int32, (TILE, TILE), 1)
    later = key_row > query_col
    key_sub = lax.rem(key_row, HALF).astype(F32) >= border
    query_sub = lax.rem(query_col, HALF).astype(F32) >= border
    apart = jnp.logical_xor(key_sub, query_sub)
    for tile in range(TILES - 1):
        bias[TILE * tile : TILE * tile + TILE, :] = jnp.where(apart, NEGATIVE, 0.0)
    bias[TILE * (TILES - 1) :, :] = jnp.where(jnp.logical_or(later, apart), NEGATIVE, 0.0)

    for copy in (*bias_copies, *(weight_copies[0, number] for number in range(1, 4))):
        copy.wait()
    attend(0, 0)
    attend(0, 1)
    hidden_start(0, 0)
    weight_copies[1, 0].wait()
    halves(functools.partial(feed, 0), functools.partial(project, 1))
    for number in range(1, 4):
        weight_copies[1, number].wait()
    attend(1, 0)
    attend(1, 1)
    hidden_pass(0, 0)
    hidden_start(1, 0)
    halves(functools.partial(feed, 1), finish)
    hidden_start(0, 1)
    hidden_start(1, 1)
    hidden_pass(1, 0)

    halves(functools.partial(turn_round, 1))
    make(1)
    feed_back(1)
    hidden_pass(0, 1)
    hidden_pass(1, 1)
    core_done(1)
    make(0)
    attend_back(1, 1)
    first_y(1)
    core_done(0)
    attend_back(1, 0)
    second_y(1)
    first_x(1)
    project_back(1, 1)
    heads_grads(1)
    first_z(1)
    project_back(1, 0)
    feed_back(0)
    small_start()
    second_x(1)
    make(2)
    first_x(0)
    heads_second(1)
    first_z(0)
    attend_back(0, 1)
    small_next(0)
    core_done(2)
    second_x(0)
    make(3)
    attend_back(0, 0)
    small_next(1)
    project_back(0, 1)
    hand_back(1)
    first_z(2)
    heads_grads(0)
    small_next(2)
    first_x(2)
    core_done(3)
    first_y(2)
    heads_second(0)
    small_done()
    first_z(3)
    second_x(2)
    first_x(3)
    second_z(2)
    second_z(0)
    heads_third(1)
    second_z(1)
    first_y(3)
    heads_third(0)
    second_y(2)
    second_x(3)
    second_z(3)
    third_done(0)
    third_done(2)
    second_y(3)
    project_back(0, 0)
    hand_back(0)
    heads_done(1)
    third_done(1)
    third_done(3)
    final_pass(0)
    final_pass(2)
    final_pass(1)
    final_pass(3)
    final_done(2)
    final_done(1)
    heads_done(0)
    final_done(0)
    final_done(3)
    for half in range(2):
        move_arrived(3, half, out_in)
        move_arrived(4, half, grad_in)

    for half in range(2):
        left(2, 0, half, head_out)
        left(3, 0, half, pack_out)
        to_team_left(0, half, half_of(tokens, half))
        to_team_left(1, half, flag_out)
        to_team_left(2, half, half_of(cotangent, half))
        to_owner_left(3, half, back_out.at[0, half])
        to_owner_left(4, half, back_out.at[1, half])


def results_kernel(
    final, heads, out_block, grad_block, small,
    output, input_grad, qkv_grad, out_grad, up_grad, up_bias_grad, down_grad, down_bias_grad, alpha_grad,
    out_flat, grad_wide, qkv_wide, out_wide, up_wide, down_wide, out_sem,
):
    ends = []

    def write(source, target):
        ends.append(pltpu.make_async_copy(source, target, out_sem.at[len(ends)]))
        ends[-1].start()

    up_bias_grad[...] = small[:, 0:256]
    down_bias_grad[...] = small[:, 256 : 256 + DIM]
    alpha_grad[...] = small[:, 384:386]
    for layer in range(LAYERS):
        for quarter in range(4):

            def block(first, count):
                return final[layer, quarter, first : first + count, :].astype(F32)

            def columns(step):
                return slice(WIDTH * step + 128 * quarter, WIDTH * step + 128 * quarter + 128)

            for step in range(4):
                up_wide[layer, :, columns(step)] = block(DIM * step, DIM)
            out_wide[layer, :, columns(0)] = block(256, DIM)
            down_wide[layer, :, columns(0)] = block(320, 256)
        write(up_wide.at[layer], up_grad.at[layer])
        write(out_wide.at[layer], out_grad.at[layer])
        write(down_wide.at[layer], down_grad.at[layer])
    for half in range(2):
        rows = slice(HALF * half, HALF * half + HALF)
        grad_wide[rows, :] = grad_block[half].astype(F32)
        out_flat[rows, :] = out_block[half]
    write(grad_wide, input_grad)
    write(out_flat, output)
    for layer in range(LAYERS):
        for side in range(2):
            for member in range(TEAM):
                for step in range(3):
                    at = WIDTH * step + 128 * member
                    qkv_wide[layer, 32 * side : 32 * side + 32, at : at + 128] = heads[
                        layer, side, member, :, 128 * step : 128 * step + 128
                    ].astype(F32)
        write(qkv_wide.at[layer], qkv_grad.at[layer])
    for end in ends:
        end.wait()


def fast_body(
    tokens, seq_len, qkv_weight, out_weight, up_weight, up_bias, down_weight, down_bias, alphas, cotangent
):
    whole = pl.BlockSpec(memory_space=pltpu.VMEM)
    scalar = pl.BlockSpec(memory_space=pltpu.SMEM)
    far = pl.BlockSpec(memory_space=pl.ANY)
    shape = jax.ShapeDtypeStruct
    rows = HALF * RUNS

    def vmem(*dims):
        return pltpu.VMEM(dims, BF16)

    def wide(*dims):
        return pltpu.VMEM(dims, F32)

    dma = pltpu.SemaphoreType.DMA
    final, heads, out_block, grad_block, small = pl.pallas_call(
        layers_kernel,
        out_shape=(
            vmem(LAYERS, 4, CHUNK, 128),
            vmem(LAYERS, 2, TEAM, DIM // 2, 3 * 128),
            vmem(2, HALF, WIDTH),
            vmem(2, HALF, WIDTH),
            wide(LAYERS, WIDTH),
        ),
        in_specs=[far, scalar, scalar, far, far, far, far, far, far, far],
        out_specs=(whole,) * 5,
        scratch_shapes=[
            vmem(LAYERS, WIDTH, 3 * WIDTH),
            vmem(LAYERS, WIDTH, WIDTH),
            vmem(LAYERS, WIDTH, FF),
            vmem(LAYERS, FF, WIDTH),
            wide(LAYERS, FF),
            wide(LAYERS, WIDTH),
            vmem(2, HALF, WIDTH),
            vmem(2, HALF, WIDTH),
            wide(8, 128),
            wide(2, 8, 128),
            vmem(2, 2, HALF, WIDTH),
            wide(2 * HALF, WIDTH),
            wide(2 * HALF, WIDTH),
            vmem(LAYERS, WIDTH, rows),
            vmem(LAYERS, WIDTH, 2 * HALF),
            vmem(LAYERS, 2 * HALF, WIDTH),
            vmem(LAYERS, 2 * HALF, FF),
            wide(LAYERS, 2 * HALF, WIDTH),
            wide(LAYERS, 2 * HALF, FF),
            wide(LAYERS, 2 * HALF, WIDTH),
            vmem(2 * HALF, WIDTH),
            vmem(2 * HALF, FF),
            vmem(2 * HALF, WIDTH),
            vmem(HALF, 3 * WIDTH),
            vmem(2, TEAM, OWN, PACK, 128),
            vmem(2, TEAM, OWN, DIM, 128),
            vmem(2, TEAM, OWN, PACK, 128),
            vmem(2, TEAM, OWN, DIM, 128),
            vmem(2, TEAM, OWN, DIM, 128),
            vmem(LAYERS, OWN, rows, 128),
            vmem(LAYERS, OWN, 128, rows),
            vmem(LAYERS, OWN, 128, rows),
            vmem(OWN, 128, rows),
            wide(LAYERS, OWN, DIM, rows),
            wide(LAYERS, OWN, 1, rows),
            wide(OWN, rows, 128),
            wide(OWN, DIM, rows),
            wide(rows, TILE),
            vmem(LAYERS, 2, 2, 4, 2, CHUNK, 128),
            vmem(2, 4, 2, CHUNK, 128),
            vmem(4, 2, TOTALS[0], 128),
            vmem(4, TOTALS[1], 128),
            vmem(4, TOTALS[0], 128),
            vmem(2, 4, TOTALS[1], 128),
            vmem(LAYERS, 4, CHUNK, 128),
            vmem(4, 2, 2, TOTALS[2], 128),
            vmem(2, TOTALS[2], 128),
            vmem(TOTALS[2], 128),
            vmem(LAYERS, 4, 2, DIM, 3 * 128),
            vmem(LAYERS, 4, 2, DIM // 2, 3 * 128),
            vmem(LAYERS, 4, 2, DIM // 2, 3 * 128),
            vmem(LAYERS, 2, DIM // 2, 3 * 128),
            wide(LAYERS, SMALL),
            wide(3, LAYERS, SMALL),
            wide(4, LAYERS, SMALL),
            wide(3, LAYERS, SMALL),
            dma((LAYERS + 1, 4)),
            dma((5, 2)),
            dma((5, 2)),
            dma((4, LAYERS, 2, OWN)),
            dma((4, LAYERS, 2, OWN)),
            dma((len(PARTS),)),
            dma((len(PARTS),)),
            dma((len(PARTS), 3)),
            dma((len(PARTS), 3)),
            dma((len(PARTS), 3)),
            dma((len(PARTS), 3)),
            dma((len(PARTS), 3, 4)),
            dma((len(PARTS), 3, 4)),
            dma((len(PARTS), 3)),
            dma((len(PARTS), 3)),
            dma((LAYERS, 2, 3)),
            dma((LAYERS, 2, 3)),
            dma((LAYERS,)),
            dma((LAYERS,)),
            dma((LAYERS, 4)),
            dma((LAYERS, 4)),
            dma((LAYERS, 8)),
            dma((LAYERS, 8)),
            dma((6,)),
            dma((6,)),
            pltpu.SemaphoreType.REGULAR((2,)),
        ],
        compiler_params=pltpu.CompilerParams(
            collective_id=0, has_side_effects=True, vmem_limit_bytes=61 * 1024 * 1024
        ),
        name="layers",
    )(
        tokens, seq_len, alphas, up_bias, down_bias, cotangent,
        qkv_weight, out_weight, up_weight, down_weight,
    )
    return tuple(
        pl.pallas_call(
            results_kernel,
            out_shape=(
                shape((2 * HALF, WIDTH), BF16),
                shape((2 * HALF, WIDTH), F32),
                shape((LAYERS, DIM, 3 * WIDTH), F32),
                shape((LAYERS, DIM, WIDTH), F32),
                shape((LAYERS, DIM, FF), F32),
                shape((LAYERS, FF // RUNS), F32),
                shape((LAYERS, FF // RUNS, WIDTH), F32),
                shape((LAYERS, DIM), F32),
                shape((LAYERS, 2), F32),
            ),
            in_specs=[whole] * 5,
            out_specs=(far, far, far, far, far, whole, far, whole, whole),
            scratch_shapes=[
                vmem(2 * HALF, WIDTH),
                wide(2 * HALF, WIDTH),
                wide(LAYERS, DIM, 3 * WIDTH),
                wide(LAYERS, DIM, WIDTH),
                wide(LAYERS, DIM, FF),
                wide(LAYERS, FF // RUNS, WIDTH),
                dma((10,)),
            ],
            compiler_params=pltpu.CompilerParams(vmem_limit_bytes=24 * 1024 * 1024),
            name="results",
        )(final, heads, out_block, grad_block, small)
    )


def layout(seq_len, local_count, cycle_size):
    piece_rows = seq_len[0] // cycle_size
    end_rows = jnp.cumsum(piece_rows)
    start_rows = end_rows - piece_rows
    local_rows = jnp.arange(local_count, dtype=jnp.int32)
    segment = jnp.sum((local_rows[:, None] >= end_rows[None, :]).astype(jnp.int32), axis=1)
    picked = segment[:, None] == jnp.arange(seq_len.shape[1], dtype=jnp.int32)[None, :]
    offset = local_rows - jnp.sum(jnp.where(picked, start_rows[None, :], 0), axis=1)
    span_rows = jnp.sum(jnp.where(picked, piece_rows[None, :], 0), axis=1)
    return (segment, offset, span_rows)


def gelu_exact(values):
    return jax.nn.gelu(values, approximate=False)


def key_block(whole, geometry, block_index, head_count):
    query_seg, query_pos, seg_all, pos_all, block_rows, score_scale = geometry
    first_row = block_index * block_rows
    key_piece = lax.dynamic_slice_in_dim(whole, first_row, block_rows, 0)
    key_seg = lax.dynamic_slice_in_dim(seg_all, first_row, block_rows, 0)
    key_pos = lax.dynamic_slice_in_dim(pos_all, first_row, block_rows, 0)
    half_width = key_piece.shape[1] // 2
    keys_part = key_piece[:, :half_width].reshape(block_rows, head_count, -1)
    values_part = key_piece[:, half_width:].reshape(block_rows, head_count, -1)
    return (keys_part, values_part, key_seg, key_pos)


def block_scores(queries, keys_part, key_seg, key_pos, geometry):
    query_seg, query_pos, seg_all, pos_all, block_rows, score_scale = geometry
    scores = (
        jnp.einsum("qhd,khd->hqk", queries, keys_part, preferred_element_type=jnp.float32)
        * score_scale
    )
    allowed = (query_seg[:, None] == key_seg[None, :]) & (key_pos[None, :] <= query_pos[:, None])
    return (scores, allowed[None])


def attend(queries, whole, geometry):
    row_count, head_count, head_dim = queries.shape
    block_count = whole.shape[0] // geometry[4]

    def statistics(running, block_index):
        largest, totals = running
        keys_part, values_part, key_seg, key_pos = key_block(
            whole, geometry, block_index, head_count
        )
        scores, allowed = block_scores(queries, keys_part, key_seg, key_pos, geometry)
        newest = jnp.maximum(largest, jnp.max(jnp.where(allowed, scores, NEGATIVE), axis=2))
        weights = jnp.where(allowed, jnp.exp(scores - newest[:, :, None]), 0.0)
        totals = totals * jnp.exp(largest - newest) + jnp.sum(weights, axis=2)
        return ((newest, totals), None)

    initial = (
        jnp.full((head_count, row_count), NEGATIVE, jnp.float32),
        jnp.zeros((head_count, row_count), jnp.float32),
    )
    (largest, totals), unused = lax.scan(statistics, initial, jnp.arange(block_count))
    log_total = largest + jnp.log(totals)

    def weighted(output_sum, block_index):
        keys_part, values_part, key_seg, key_pos = key_block(
            whole, geometry, block_index, head_count
        )
        scores, allowed = block_scores(queries, keys_part, key_seg, key_pos, geometry)
        probs = jnp.where(allowed, jnp.exp(scores - log_total[:, :, None]), 0.0).astype(
            jnp.bfloat16
        )
        output_sum = output_sum + jnp.einsum(
            "hqk,khd->qhd", probs, values_part, preferred_element_type=jnp.float32
        )
        return (output_sum, None)

    output_sum, unused = lax.scan(
        weighted, jnp.zeros((row_count, head_count, head_dim), jnp.float32), jnp.arange(block_count)
    )
    return (output_sum, log_total)


def attend_back(queries, whole, log_total, delta_sum, grad_heads, geometry):
    row_count, head_count, head_dim = queries.shape
    block_rows = geometry[4]
    score_scale = geometry[5]
    block_count = whole.shape[0] // block_rows

    def gradients(query_grad, block_index):
        keys_part, values_part, key_seg, key_pos = key_block(
            whole, geometry, block_index, head_count
        )
        scores, allowed = block_scores(queries, keys_part, key_seg, key_pos, geometry)
        probs = jnp.where(allowed, jnp.exp(scores - log_total[:, :, None]), 0.0)
        grad_probs = jnp.einsum(
            "qhd,khd->hqk", grad_heads, values_part, preferred_element_type=jnp.float32
        )
        grad_scores = (probs * (grad_probs - delta_sum[:, :, None])).astype(jnp.bfloat16)
        query_grad = (
            query_grad
            + jnp.einsum("hqk,khd->qhd", grad_scores, keys_part, preferred_element_type=jnp.float32)
            * score_scale
        )
        key_grad = (
            jnp.einsum("hqk,qhd->khd", grad_scores, queries, preferred_element_type=jnp.float32)
            * score_scale
        )
        value_grad = jnp.einsum(
            "hqk,qhd->khd",
            probs.astype(jnp.bfloat16),
            grad_heads,
            preferred_element_type=jnp.float32,
        )
        joined = jnp.concatenate(
            [key_grad.reshape(block_rows, -1), value_grad.reshape(block_rows, -1)], axis=1
        )
        return (query_grad, joined)

    query_grad, stacked = lax.scan(
        gradients,
        jnp.zeros((row_count, head_count, head_dim), jnp.float32),
        jnp.arange(block_count),
    )
    return (query_grad, stacked.reshape(whole.shape[0], -1))


def layer_forward(hidden, layer_index, weights, geometry):
    qkv_weight, out_weight, up_weight, up_bias, down_weight, down_bias, alphas = weights
    row_count, model_width = hidden.shape
    projection = qkv_weight[layer_index]
    rounded = hidden.astype(jnp.bfloat16)
    queries = (
        jnp.dot(rounded, projection[:, :model_width], preferred_element_type=jnp.float32)
        .astype(jnp.bfloat16)
        .reshape(row_count, HEADS, -1)
    )
    key_value = jnp.dot(
        rounded, projection[:, model_width:], preferred_element_type=jnp.float32
    ).astype(jnp.bfloat16)
    whole = lax.all_gather(key_value, "blk", axis=0, tiled=True)
    heads_out, log_total = attend(queries, whole, geometry)
    heads_rounded = heads_out.reshape(row_count, model_width).astype(jnp.bfloat16)
    branch = jnp.dot(heads_rounded, out_weight[layer_index], preferred_element_type=jnp.float32)
    alpha_pair = alphas[layer_index]
    middle = hidden + alpha_pair[0] * branch
    entered = middle.astype(jnp.bfloat16)
    gate_pre = (
        jnp.dot(entered, up_weight[layer_index], preferred_element_type=jnp.float32)
        + up_bias[layer_index]
    )
    activated = gelu_exact(gate_pre).astype(jnp.bfloat16)
    second = (
        jnp.dot(activated, down_weight[layer_index], preferred_element_type=jnp.float32)
        + down_bias[layer_index]
    )
    result = middle + alpha_pair[1] * second
    saved = (
        rounded,
        queries,
        key_value,
        whole,
        heads_out,
        heads_rounded,
        log_total,
        branch,
        entered,
        gate_pre,
        activated,
        second,
    )
    return (result, saved)


def layer_backward(grad_hidden, saved, layer_index, weights, geometry):
    qkv_weight, out_weight, up_weight, up_bias, down_weight, down_bias, alphas = weights
    (
        rounded,
        queries,
        key_value,
        saved_whole,
        heads_out,
        heads_rounded,
        log_total,
        branch,
        entered,
        gate_pre,
        activated,
        second,
    ) = saved
    row_count = grad_hidden.shape[0]
    alpha_pair = alphas[layer_index]
    grad_second = (alpha_pair[1] * grad_hidden).astype(jnp.bfloat16)
    alpha_second = jnp.sum(grad_hidden * second)
    bias_down = jnp.sum(grad_second.astype(jnp.float32), axis=0)
    grad_down = jnp.einsum("tf,td->fd", activated, grad_second, preferred_element_type=jnp.float32)
    grad_act = jnp.einsum(
        "td,fd->tf", grad_second, down_weight[layer_index], preferred_element_type=jnp.float32
    )
    unused, gelu_pull = jax.vjp(gelu_exact, gate_pre)
    grad_gate = gelu_pull(grad_act)[0].astype(jnp.bfloat16)
    bias_up = jnp.sum(grad_gate.astype(jnp.float32), axis=0)
    grad_up = jnp.einsum("td,tf->df", entered, grad_gate, preferred_element_type=jnp.float32)
    grad_middle = grad_hidden + jnp.einsum(
        "tf,df->td", grad_gate, up_weight[layer_index], preferred_element_type=jnp.float32
    )
    grad_branch = (alpha_pair[0] * grad_middle).astype(jnp.bfloat16)
    alpha_first = jnp.sum(grad_middle * branch)
    grad_proj_out = jnp.einsum(
        "te,td->ed", heads_rounded, grad_branch, preferred_element_type=jnp.float32
    )
    grad_heads = (
        jnp.einsum(
            "td,ed->te", grad_branch, out_weight[layer_index], preferred_element_type=jnp.float32
        )
        .astype(jnp.bfloat16)
        .reshape(queries.shape)
    )
    delta_sum = jnp.sum(grad_heads.astype(jnp.float32) * heads_out, axis=2).T
    whole = lax.all_gather(key_value, "blk", axis=0, tiled=True)
    query_grad, key_terms = attend_back(queries, whole, log_total, delta_sum, grad_heads, geometry)
    key_grads = lax.psum_scatter(
        key_terms.astype(jnp.bfloat16), "blk", scatter_dimension=0, tiled=True
    )
    grad_proj = jnp.concatenate(
        [query_grad.reshape(row_count, -1).astype(jnp.bfloat16), key_grads], axis=1
    )
    grad_qkv = jnp.einsum("td,te->de", rounded, grad_proj, preferred_element_type=jnp.float32)
    grad_input = grad_middle + jnp.einsum(
        "te,de->td", grad_proj, qkv_weight[layer_index], preferred_element_type=jnp.float32
    )
    layer_grads = (
        grad_qkv,
        grad_proj_out,
        grad_up,
        bias_up,
        grad_down,
        bias_down,
        jnp.stack([alpha_first, alpha_second]),
    )
    return (grad_input, layer_grads)


def reduce_all(layer_results, cycle_size):
    stacked = [
        jnp.stack([layer_entry[member] for layer_entry in layer_results], axis=0)
        for member in range(6)
    ]
    alpha_tiles = jnp.stack(
        [jnp.tile(layer_entry[6], cycle_size) for layer_entry in layer_results], axis=0
    )
    shares = (
        lax.psum_scatter(
            stacked[0].astype(jnp.bfloat16), "blk", scatter_dimension=1, tiled=True
        ).astype(jnp.float32),
        lax.psum_scatter(
            stacked[1].astype(jnp.bfloat16), "blk", scatter_dimension=1, tiled=True
        ).astype(jnp.float32),
        lax.psum_scatter(
            stacked[2].astype(jnp.bfloat16), "blk", scatter_dimension=1, tiled=True
        ).astype(jnp.float32),
        lax.psum_scatter(
            stacked[3].astype(jnp.bfloat16), "blk", scatter_dimension=1, tiled=True
        ).astype(jnp.float32),
        lax.psum_scatter(
            stacked[4].astype(jnp.bfloat16), "blk", scatter_dimension=1, tiled=True
        ).astype(jnp.float32),
        lax.psum_scatter(
            stacked[5].astype(jnp.bfloat16), "blk", scatter_dimension=1, tiled=True
        ).astype(jnp.float32),
        lax.psum_scatter(
            alpha_tiles.astype(jnp.bfloat16), "blk", scatter_dimension=1, tiled=True
        ).astype(jnp.float32),
    )
    return (
        lax.psum(shares[0].astype(jnp.bfloat16), "grp").astype(jnp.float32),
        lax.psum(shares[1].astype(jnp.bfloat16), "grp").astype(jnp.float32),
        lax.psum(shares[2].astype(jnp.bfloat16), "grp").astype(jnp.float32),
        lax.psum(shares[3].astype(jnp.bfloat16), "grp").astype(jnp.float32),
        lax.psum(shares[4].astype(jnp.bfloat16), "grp").astype(jnp.float32),
        lax.psum(shares[5].astype(jnp.bfloat16), "grp").astype(jnp.float32),
        lax.psum(shares[6].astype(jnp.bfloat16), "grp").astype(jnp.float32),
    )


def body(
    tokens,
    seq_len,
    qkv_weight,
    out_weight,
    up_weight,
    up_bias,
    down_weight,
    down_bias,
    alphas,
    cotangent,
):
    row_count, model_width = tokens.shape
    cycle_size = lax.axis_size("blk")
    cycle_place = lax.axis_index("blk")
    head_dim = model_width // HEADS
    total_rows = cycle_size * row_count
    block_rows = min(max(row_count, 512), total_rows)
    segment, offset, span_rows = layout(seq_len, row_count, cycle_size)
    query_pos = cycle_place * span_rows + offset
    seg_all = jnp.tile(segment, cycle_size)
    pos_all = jnp.repeat(jnp.arange(cycle_size, dtype=jnp.int32), row_count) * jnp.tile(
        span_rows, cycle_size
    ) + jnp.tile(offset, cycle_size)
    geometry = (segment, query_pos, seg_all, pos_all, block_rows, head_dim ** (-0.5))
    weights = (qkv_weight, out_weight, up_weight, up_bias, down_weight, down_bias, alphas)
    hidden = tokens.astype(jnp.float32)
    saved_layers = []
    for layer_index in range(LAYERS):
        hidden, saved = layer_forward(hidden, layer_index, weights, geometry)
        saved_layers.append(saved)
    output = hidden.astype(jnp.bfloat16)
    grad_hidden = cotangent.astype(jnp.float32)
    layer_results = []
    for layer_index in reversed(range(LAYERS)):
        grad_hidden, layer_grads = layer_backward(
            grad_hidden, saved_layers[layer_index], layer_index, weights, geometry
        )
        layer_results.insert(0, layer_grads)
    finals = reduce_all(layer_results, cycle_size)
    return (
        output,
        grad_hidden,
        finals[0],
        finals[1],
        finals[2],
        finals[3],
        finals[4],
        finals[5],
        finals[6],
    )


def solution(mesh):
    placed = (
        P(("grp", "blk"), None),
        P("grp", None),
        P(),
        P(),
        P(),
        P(),
        P(),
        P(),
        P(),
        P(("grp", "blk"), None),
    )
    sizes = (mesh.shape["grp"], mesh.shape["blk"])
    return jax.shard_map(
        fast_body if sizes == (4, RUNS) else body,
        mesh=mesh,
        in_specs=placed,
        out_specs=(
            P(("grp", "blk"), None),
            P(("grp", "blk"), None),
            P(None, "blk", None),
            P(None, "blk", None),
            P(None, "blk", None),
            P(None, "blk"),
            P(None, "blk", None),
            P(None, "blk"),
            P(),
        ),
        check_vma=False,
    )
```

```python
import functools

import jax
import jax.numpy as jnp
from jax import lax
from jax.experimental import pallas as pl
from jax.experimental.pallas import tpu as pltpu
from jax.sharding import PartitionSpec as P

HEADS = 8
LAYERS = 2
NEGATIVE = -1e30
MESH = pl.DeviceIdType.MESH
F32 = jnp.float32
BF16 = jnp.bfloat16

HALF = 128
RUNS = 8
TEAM = 4
OWN = RUNS // TEAM
DIM = 64
WIDTH = 512
FF = 2048
CUT = 512
TILE = 256
TILES = HALF * RUNS // TILE
PACK = HALF + DIM
CHUNK = 576
SMALL = FF + WIDTH + 128
PARTS = ((1, 0, 320), (1, 320, 256), (0, 0, 320), (0, 320, 256))
SHARES = ((192, 0, 128), (160, 16, 80), (160, 112, 48), (128, 96, 32))


def spans():
    places, totals = {}, [0, 0, 0]
    for part, counts in enumerate(SHARES):
        first = PARTS[part][1]
        for route, count in enumerate(counts):
            places[part, route] = (first, totals[route], count)
            first += count
            totals[route] += count
    return places, totals


SPANS, TOTALS = spans()

SLOPE_AT = 0.28
TAIL = (
    0.11652077851573843,
    0.06749675579450809,
    0.2689101589486142,
    -0.23699347299932225,
    0.3898740127620002,
    -0.10580824228351815,
)


def nn(a, b):
    return lax.dot_general(a, b, (((1,), (0,)), ((), ())), preferred_element_type=F32)


def nt(a, b):
    return lax.dot_general(a, b, (((1,), (1,)), ((), ())), preferred_element_type=F32)


def layers_kernel(
    tokens, seq_len, alphas, up_bias_hbm, down_bias_hbm, cotangent, qkv_hbm, out_hbm, up_hbm, down_hbm,
    final, heads_all, out_in, grad_in, small_final,
    wqkv, wout, wup, wdown, up_bias, down_bias,
    tok_in, cot_in, flag_out, flag_in, back_out,
    hidden, grad, hid_all, attn_t, entered, act, branch, slope, second,
    dz, du, da, dqkv,
    pack_out, head_out, pack_in, o_in, do_in,
    kv, kv_t, rq, ro, o_t, lse, acc, dq_t, bias,
    parts, core_in, xa_in, xb_in, ya_in, yb_in, z_in, third_z, third_x, third_y,
    heads_out, heads_x, heads_z, heads_sum, small, small_in, small_z, small_sum,
    w_sem, move_send, move_recv, a2a_send, a2a_recv, core_send, core_recv, x_send, x_recv, y_send, y_recv,
    z_send, z_recv, fin_send, fin_recv, hid_send, hid_recv, hx_send, hx_recv, hz_send, hz_recv, hf_send, hf_recv,
    small_send, small_recv, core_free,
):
    grp = lax.axis_index("grp")
    blk = lax.axis_index("blk")
    core = lax.rem(grp, 2)
    side = lax.div(grp, 2)
    yy = lax.rem(blk, 2)
    zz = lax.div(blk, 2)
    member = 2 * core + yy
    far_side = 2 * (1 - side) + core
    low = lax.broadcasted_iota(jnp.int32, (HALF, 128), 1) < DIM

    def place(c, x, z, y):
        return (2 * x + c, 2 * z + y)

    core_peer = place(1 - core, side, zz, yy)
    x_peer = place(core, 1 - side, zz, yy)
    y_peer = place(core, side, zz, 1 - yy)

    def remote(source, target, send, recv, peer):
        return pltpu.make_async_remote_copy(
            src_ref=source,
            dst_ref=target,
            send_sem=send,
            recv_sem=recv,
            device_id=peer,
            device_id_type=MESH,
        )

    def credit(semaphore, peer, count=1):
        pl.semaphore_signal(semaphore, inc=count, device_id=peer, device_id_type=MESH)

    def moved(kind, slot, source, target, at, core_at, z_at):
        here = jnp.logical_and(core_at == core, z_at == zz)

        @pl.when(here)
        def _():
            pltpu.make_async_copy(source, target.at[at], move_recv.at[kind, at]).start()

        @pl.when(jnp.logical_not(here))
        def _():
            pltpu.make_async_remote_copy(
                src_ref=source,
                dst_ref=target.at[at],
                send_sem=move_send.at[kind, slot],
                recv_sem=move_recv.at[kind, at],
                device_id=place(core_at, side, z_at, yy),
                device_id_type=MESH,
            ).start()

    def move_left(kind, slot, source, core_at, z_at):
        here = jnp.logical_and(core_at == core, z_at == zz)

        @pl.when(jnp.logical_not(here))
        def _():
            pltpu.make_async_copy(source, source, move_send.at[kind, slot]).wait()

    def move_arrived(kind, at, target):
        pltpu.make_async_copy(target.at[at], target.at[at], move_recv.at[kind, at]).wait()

    def to_team(kind, half, source, target):
        moved(kind, half, source, target, lax.div(zz, 2), lax.rem(zz, 2), 2 * half + core)

    def to_team_left(kind, half, source):
        move_left(kind, half, source, lax.rem(zz, 2), 2 * half + core)

    def to_owner(kind, chunk, source, target):
        moved(kind, chunk, source, target, lax.div(zz, 2), lax.rem(zz, 2), core + 2 * chunk)

    def to_owner_left(kind, chunk, source):
        move_left(kind, chunk, source, lax.rem(zz, 2), core + 2 * chunk)

    def half_of(ref, half):
        return ref.at[pl.ds(pl.multiple_of(HALF * half, HALF), HALF)]

    def rows_of(half):
        return pl.ds(pl.multiple_of(half * HALF, HALF), HALF)

    def slot_of(other):
        return lax.rem(other + TEAM - member, TEAM)

    def exchange(kind, layer, half, outgoing, incoming, head=None):
        at = () if head is None else (head,)
        incoming[(half, 0, *at)] = outgoing[(half, member, *at)]
        for step in range(1, TEAM):
            peer = lax.rem(member + step, TEAM)
            remote(
                outgoing.at[(half, peer, *at)],
                incoming.at[(half, TEAM - step, *at)],
                a2a_send.at[kind, layer, half, head or 0],
                a2a_recv.at[kind, layer, half, head or 0],
                place(lax.div(peer, 2), side, zz, lax.rem(peer, 2)),
            ).start()

    def arrived(kind, layer, half, incoming, head=None):
        at = () if head is None else (head,)
        whole = incoming.at[(half, pl.ds(1, TEAM - 1), *at)]
        pltpu.make_async_copy(whole, whole, a2a_recv.at[kind, layer, half, head or 0]).wait()

    def left(kind, layer, half, outgoing):
        for head in range(OWN) if kind in (0, 3) else (None,):
            at = () if head is None else (head,)
            whole = outgoing.at[(half, pl.ds(1, TEAM - 1), *at)]
            pltpu.make_async_copy(whole, whole, a2a_send.at[kind, layer, half, head or 0]).wait()

    def tokens_of(chunk, other):
        return pl.ds(pl.multiple_of(HALF * (TEAM * chunk + other), HALF), HALF)

    def hidden_copy(layer, chunk, which):
        whose = 2 * core + 1 - yy if which == 2 else member
        block = hid_all.at[layer, :, tokens_of(chunk, whose)]
        return remote(
            block,
            block,
            hid_send.at[layer, chunk, which],
            hid_recv.at[layer, chunk, which],
            y_peer if which == 0 else core_peer,
        )

    def hidden_start(layer, chunk):
        for which in range(2):
            hidden_copy(layer, chunk, which).start()

    def hidden_pass(layer, chunk):
        hidden_copy(layer, chunk, 0).wait()
        hidden_copy(layer, chunk, 2).start()

    def hidden_done(layer, chunk):
        for which in range(1, 3):
            hidden_copy(layer, chunk, which).wait()

    def project(layer, half):
        rows = rows_of(half)
        rounded = hidden[rows, :].astype(BF16)
        if layer == 1:
            left(0, 0, half, pack_out)
        queries = nn(rounded, wqkv[layer, :, 0:WIDTH]) * (DIM ** -0.5)
        queries_t = queries.T.astype(BF16)
        keys = nn(rounded, wqkv[layer, :, WIDTH : 2 * WIDTH])
        values = nn(rounded, wqkv[layer, :, 2 * WIDTH : 3 * WIDTH])
        for pair in range(RUNS // 2):
            k_pair = keys[:, 128 * pair : 128 * pair + 128]
            v_pair = values[:, 128 * pair : 128 * pair + 128]
            first = jnp.where(low, k_pair, pltpu.roll(v_pair, DIM, 1))
            other = jnp.where(low, pltpu.roll(k_pair, DIM, 1), v_pair)
            pack_out[half, pair, 0, 0:HALF, :] = first.astype(BF16)
            pack_out[half, pair, 1, 0:HALF, :] = other.astype(BF16)
        for head in range(RUNS):
            pack_out[half, head // 2, head % 2, HALF:, :] = queries_t[DIM * head : DIM * head + DIM, :]
        for head in range(OWN):
            exchange(0, layer, half, pack_out, pack_in, head)
        hid_all[layer, :, tokens_of(half, member)] = rounded.T

    def attend(layer, chunk):
        if layer == 1:
            left(1, 0, chunk, head_out)

        def one_head(head, carry):
            arrived(0, layer, chunk, pack_in, head)
            for other in range(TEAM):
                slot = slot_of(other)
                start = HALF * (TEAM * chunk + other)
                span = slice(start, start + HALF)
                block = pack_in[chunk, slot, head, 0:HALF, :]
                kv[layer, head, span, :] = block
                kv_t[layer, head, :, span] = block.T
                rq[layer, head, 0:DIM, span] = pack_in[chunk, slot, head, HALF:, :]

            def scores_of(i):
                count = TILE * (i + 1)
                tile = rq[layer, head, :, TILE * i : TILE * i + TILE]
                return nn(kv[layer, head, 0:count, :], tile) + bias[TILE * TILES - count :, :]

            ahead = [scores_of(i) for i in (2 * chunk, 2 * chunk + 1)]
            for i in (2 * chunk, 2 * chunk + 1):
                columns = slice(TILE * i, TILE * i + TILE)
                count = TILE * (i + 1)
                scores = ahead[i - 2 * chunk]
                largest = jnp.max(scores, axis=0, keepdims=True)
                weight = jnp.exp(scores - largest)
                total = jnp.sum(weight, axis=0, keepdims=True)
                summed = nn(kv_t[layer, head, DIM:, 0:count], weight.astype(BF16))
                summed = summed / total
                o_t[layer, head, :, columns] = summed
                lse[layer, head, :, columns] = largest + jnp.log(total)
                rounded = summed.astype(BF16)
                for part in range(2):
                    head_out[chunk, 2 * (i - 2 * chunk) + part, head] = rounded[
                        :, HALF * part : HALF * part + HALF
                    ]
            return carry

        for head in range(OWN):
            one_head(head, 0)
        exchange(1, layer, chunk, head_out, o_in)

    def feed(layer, half):
        rows = rows_of(half)
        arrived(1, layer, half, o_in)
        for head in range(RUNS):
            attn_t[layer, DIM * head : DIM * head + DIM, rows] = o_in[half, slot_of(head // 2), head % 2]
        attn = attn_t[layer, :, rows].T
        grown = nn(attn, wout[layer])
        branch[layer, rows, :] = grown
        middle = hidden[rows, :] + alphas[layer, 0] * grown
        rounded = middle.astype(BF16)
        entered[layer, rows, :] = rounded
        total = jnp.zeros((HALF, WIDTH), F32)

        def gate_of(step):
            cut = slice(CUT * step, CUT * step + CUT)
            return nn(rounded, wup[layer, :, cut]) + up_bias[layer : layer + 1, cut]

        coming = gate_of(0)
        for step in range(FF // CUT):
            cut = slice(CUT * step, CUT * step + CUT)
            gate = coming
            if step + 1 < FF // CUT:
                coming = gate_of(step + 1)
            bell = jnp.exp(gate * gate * -0.5)
            near = pl.reciprocal(1.0 + SLOPE_AT * jnp.abs(gate), approx=True)
            tail = jnp.full_like(gate, TAIL[5])
            for factor in TAIL[4::-1]:
                tail = tail * near + factor
            tail = bell * (tail * near)
            risen = jnp.where(gate > 0.0, 1.0 - tail, tail)
            slope[layer, rows, cut] = risen + gate * bell * 0.3989422804014327
            active = (gate * risen).astype(BF16)
            act[layer, rows, cut] = active
            total = total + nn(active, wdown[layer, cut, :])
        total = total + down_bias[layer : layer + 1, :]
        second[layer, rows, :] = total
        hidden[rows, :] = middle + alphas[layer, 1] * total

    def total_of(values):
        return jnp.sum(jnp.sum(values, axis=0, keepdims=True), axis=1, keepdims=True)

    def feed_back(layer):
        start = grad[...]
        if layer == 0:
            dz[...] = (alphas[layer, 1] * start).astype(BF16)
        scaled = dz[...]
        alpha_second = total_of(start * second[layer])
        small[layer : layer + 1, FF : FF + WIDTH] = jnp.sum(scaled.astype(F32), axis=0, keepdims=True)
        middle = start
        coming = nt(scaled, wdown[layer, 0:CUT, :])
        for step in range(FF // CUT):
            cut = slice(CUT * step, CUT * step + CUT)
            raw = coming
            if step + 1 < FF // CUT:
                coming = nt(scaled, wdown[layer, CUT * (step + 1) : CUT * (step + 2), :])
            gate = (raw * slope[layer, :, cut]).astype(BF16)
            du[:, cut] = gate
            small[layer : layer + 1, cut] = jnp.sum(gate.astype(F32), axis=0, keepdims=True)
            middle = middle + nt(gate, wup[layer, :, cut])
        grad[...] = middle
        mixed = (alphas[layer, 0] * middle).astype(BF16)
        da[...] = mixed
        spread = nt(wout[layer], mixed).astype(BF16)
        for chunk in (1, 0):
            left(*((1, 1) if layer == 1 else (2, 1)), chunk, head_out)
            for head in range(RUNS):
                head_out[chunk, head // 2, head % 2] = spread[
                    DIM * head : DIM * head + DIM, HALF * chunk : HALF * chunk + HALF
                ]
            exchange(2, layer, chunk, head_out, do_in)
        alpha_first = total_of(middle * branch[layer])
        column = lax.broadcasted_iota(jnp.int32, (1, 128), 1)
        small[layer : layer + 1, FF + WIDTH :] = jnp.where(
            column == 0, alpha_first, jnp.where(column == 1, alpha_second, 0.0)
        )

    def attend_back(layer, chunk):
        arrived(2, layer, chunk, do_in)
        left(*((0, 1) if layer == 1 else (3, 1)), chunk, pack_out)

        def one_head(head, carry):
            for other in range(TEAM):
                start = HALF * (TEAM * chunk + other)
                ro[head, DIM:, start : start + HALF] = do_in[chunk, slot_of(other), head]
            for i in (2 * chunk, 2 * chunk + 1):
                columns = slice(TILE * i, TILE * i + TILE)
                query_tile = rq[layer, head, :, columns]
                grad_tile = ro[head, :, columns]
                log_total = lse[layer, head, :, columns]
                delta = jnp.sum(
                    ro[head, DIM:, columns].astype(F32) * o_t[layer, head, :, columns],
                    axis=0,
                    keepdims=True,
                )
                count = TILE * (i + 1)
                keys = kv[layer, head, 0:count, :]
                weight = jnp.exp(nn(keys, query_tile) + bias[TILE * TILES - count :, :] - log_total)
                scored = (weight * (nn(keys, grad_tile) - delta)).astype(BF16)
                term = nt(scored, query_tile) + nt(weight.astype(BF16), grad_tile)
                if chunk == 1 and i == 2:
                    acc[head, 0:count, :] = term
                elif chunk == 1:
                    acc[head, 0 : count - TILE, :] += term[0 : count - TILE, :]
                    acc[head, count - TILE : count, :] = term[count - TILE :, :]
                else:
                    acc[head, 0:count, :] += term
                query_grad = nn(kv_t[layer, head, 0:DIM, 0:count], scored)
                dq_t[head, :, columns] = query_grad * (DIM ** -0.5)
            for other in range(TEAM):
                start = HALF * (TEAM * chunk + other)
                span = slice(start, start + HALF)
                pack_out[chunk, other, head, 0:HALF, :] = acc[head, span, :].astype(BF16)
                pack_out[chunk, other, head, HALF:, :] = dq_t[head, :, span].astype(BF16)
            exchange(3, layer, chunk, pack_out, pack_in, head)
            return carry

        for head in range(OWN):
            one_head(head, 0)

    def project_back(layer, half):
        for head in range(OWN):
            arrived(3, layer, half, pack_in, head)
        turned = jnp.concatenate(
            [pack_in[half, slot_of(head // 2), head % 2, HALF:, :] for head in range(RUNS)], axis=0
        )
        dqkv[:, 0:WIDTH] = turned.T
        for pair in range(RUNS // 2):
            first = pack_in[half, slot_of(pair), 0, 0:HALF, :].astype(F32)
            other = pack_in[half, slot_of(pair), 1, 0:HALF, :].astype(F32)
            k_pair = jnp.where(low, first, pltpu.roll(other, DIM, 1))
            v_pair = jnp.where(low, pltpu.roll(first, DIM, 1), other)
            dqkv[:, WIDTH + 128 * pair : WIDTH + 128 * pair + 128] = k_pair.astype(BF16)
            dqkv[:, 2 * WIDTH + 128 * pair : 2 * WIDTH + 128 * pair + 128] = v_pair.astype(BF16)
        rows = rows_of(half)
        grad[rows, :] = grad[rows, :] + nt(dqkv[...], wqkv[layer])

    def scatter_rows(layer, result, first_row):
        for run in range(RUNS):
            for quarter in range(4):
                parts[layer, quarter % 2, quarter // 2, run // 2, run % 2, first_row : first_row + DIM, :] = result[
                    DIM * run : DIM * run + DIM, 128 * quarter : 128 * quarter + 128
                ].astype(BF16)

    def make(part):
        layer, first, count = PARTS[part]
        if first < 256:
            turned = entered[layer].T
        for row in range(first, min(first + count, 256), DIM):
            step = row // DIM
            scatter_rows(layer, nn(turned, du[:, CUT * step : CUT * step + CUT]), row)
        if first <= 256 < first + count:
            scatter_rows(layer, nn(attn_t[layer], da[...]), 256)
        if first >= 320:
            turned = dz[...].T
            for step in range(FF // CUT):
                result = nn(turned, act[layer, :, CUT * step : CUT * step + CUT])
                for block in range(CUT // 128):
                    run, row = 2 * step + block // 2, 320 + 128 * (block % 2)
                    for quarter in range(4):
                        parts[layer, quarter % 2, quarter // 2, run // 2, run % 2, row : row + 128, :] = result[
                            128 * quarter : 128 * quarter + 128, 128 * block : 128 * block + 128
                        ].astype(BF16)
        if layer == 0:
            pl.semaphore_wait(core_free.at[0 if first < 320 else 1], 1)
        core_copy(part).start()

    def heads_grads(layer):
        for chunk in range(2):
            hidden_done(layer, chunk)
        blocks = [(run // TEAM, run % TEAM) for run in range(RUNS)]
        keys_values = jnp.concatenate(
            [
                jnp.concatenate([pack_out[chunk, other, head, 0:HALF, :] for chunk, other in blocks], axis=0)
                for head in range(OWN)
            ],
            axis=1,
        )
        queries = jnp.concatenate(
            [
                jnp.concatenate([pack_out[chunk, other, head, HALF:, :] for chunk, other in blocks], axis=1)
                for head in range(OWN)
            ],
            axis=0,
        )
        both = nn(hid_all[layer], keys_values)
        q_part = nt(hid_all[layer], queries)
        first, other = both[:, 0:128], both[:, 128:256]
        left_half = lax.broadcasted_iota(jnp.int32, (WIDTH, 128), 1) < DIM
        k_part = jnp.where(left_half, first, pltpu.roll(other, DIM, 1))
        v_part = jnp.where(left_half, pltpu.roll(first, DIM, 1), other)
        for number, values in enumerate((q_part, k_part, v_part)):
            for run in range(RUNS):
                heads_out[layer, run // 2, run % 2, :, 128 * number : 128 * number + 128] = values[
                    DIM * run : DIM * run + DIM, :
                ].astype(BF16)
        heads_x_copy(layer).start()

    def half_rows(which):
        return pl.ds(pl.multiple_of(32 * which, 32), 32)

    def heads_x_copy(layer):
        return remote(
            heads_out.at[layer, :, :, half_rows(1 - side)],
            heads_x.at[layer],
            hx_send.at[layer],
            hx_recv.at[layer],
            x_peer,
        )

    def heads_z_copy(layer, step):
        peer = lax.rem(zz + step, 4)
        return remote(
            heads_out.at[layer, peer, :, half_rows(side)],
            heads_z.at[layer, 4 - step],
            hz_send.at[layer, step],
            hz_recv.at[layer, 4 - step],
            place(core, side, peer, yy),
        )

    def heads_last_copy(layer, number):
        x, c, y = number // 4, number // 2 % 2, number % 2
        return remote(
            heads_sum.at[layer, 1 - yy if y else yy],
            heads_all.at[layer, side, member],
            hf_send.at[layer, number],
            hf_recv.at[layer, number],
            place(1 - core if c else core, 1 - side if x else side, zz, 1 - yy if y else yy),
        )

    def heads_second(layer):
        heads_x_copy(layer).wait()
        heads_out[layer, :, :, half_rows(side), :] += heads_x[layer]
        for step in range(1, 4):
            heads_z_copy(layer, step).start()

    def heads_third(layer):
        for step in range(1, 4):
            heads_z_copy(layer, step).wait()
        total = heads_out[layer, zz, :, half_rows(side), :].astype(F32)
        for slot in range(1, 4):
            total = total + heads_z[layer, slot].astype(F32)
        heads_sum[layer] = total.astype(BF16)
        heads_all[layer, side, member] = heads_sum[layer, yy]
        for number in range(1, 8):
            heads_last_copy(layer, number).start()

    def heads_done(layer):
        for number in range(1, 8):
            heads_last_copy(layer, number).wait()

    def rows_in(part, route):
        first, room, count = SPANS[part, route]
        return pl.ds(first, count), pl.ds(room, count)

    def used(part, route):
        return SHARES[part][route] > 0

    def core_copy(part):
        layer, first, count = PARTS[part]
        rows = pl.ds(first, count)
        return remote(
            parts.at[layer, 1 - core, :, :, :, rows],
            core_in.at[:, :, :, rows],
            core_send.at[part],
            core_recv.at[part],
            core_peer,
        )

    def x_copy(part, route):
        layer = PARTS[part][0]
        rows, room = rows_in(part, route)
        ends = (x_send.at[part, route], x_recv.at[part, route], x_peer)
        mine = parts.at[layer, core, 1 - side]
        if route == 0:
            return remote(mine.at[:, :, rows], xa_in.at[:, :, room], *ends)
        if route == 1:
            return remote(mine.at[:, yy, rows], xb_in.at[:, room], *ends)
        return remote(mine.at[zz, :, rows], third_x.at[:, room], *ends)

    def y_copy(part, route):
        layer = PARTS[part][0]
        rows, room = rows_in(part, route)
        ends = (y_send.at[part, route], y_recv.at[part, route], y_peer)
        mine = parts.at[layer, core]
        if route == 0:
            return remote(mine.at[side, :, 1 - yy, rows], ya_in.at[:, room], *ends)
        if route == 1:
            return remote(mine.at[:, :, 1 - yy, rows], yb_in.at[:, :, room], *ends)
        return remote(mine.at[side, zz, 1 - yy, rows], third_y.at[room], *ends)

    def z_copy(part, route, step):
        layer = PARTS[part][0]
        rows, room = rows_in(part, route)
        peer = lax.rem(zz + step, 4)
        ends = (z_send.at[part, route, step], z_recv.at[part, route, 4 - step], place(core, side, peer, yy))
        if route == 2:
            return remote(parts.at[layer, core, :, peer, :, rows], third_z.at[4 - step, :, :, room], *ends)
        return remote(parts.at[layer, core, side, peer, yy, rows], z_in.at[layer, 4 - step, rows], *ends)

    def final_copy(part, which):
        layer, first, count = PARTS[part]
        block = final.at[layer, far_side if which == 2 else grp, pl.ds(first, count)]
        return remote(
            block,
            block,
            fin_send.at[part, which],
            fin_recv.at[part, which],
            x_peer if which == 0 else core_peer,
        )

    def core_done(part):
        layer, first, count = PARTS[part]
        rows = pl.ds(first, count)
        core_copy(part).wait()
        for across in (1 - side, side):
            parts[layer, core, across, :, :, rows, :] += core_in[across, :, :, rows, :]
            if used(part, 0) and across is not side:
                x_copy(part, 0).start()
        if used(part, 1):
            y_copy(part, 1).start()
        if used(part, 2):
            for step in range(1, 4):
                z_copy(part, 2, step).start()
        if layer == 1:
            freed = 0 if first < 320 else 1
            followers = [1 for other in PARTS if other[0] == 0 and (other[1] >= 320) == (freed == 1)]
            credit(core_free.at[freed], core_peer, len(followers))

    def first_x(part):
        if used(part, 0):
            layer = PARTS[part][0]
            rows, room = rows_in(part, 0)
            x_copy(part, 0).wait()
            for y in (1 - yy, yy):
                parts[layer, core, side, :, y, rows, :] += xa_in[:, y, room, :]
                if y is not yy:
                    y_copy(part, 0).start()

    def first_y(part):
        if used(part, 1):
            layer = PARTS[part][0]
            rows, room = rows_in(part, 1)
            y_copy(part, 1).wait()
            for across in (1 - side, side):
                parts[layer, core, across, :, yy, rows, :] += yb_in[across, :, room, :]
                if across is not side:
                    x_copy(part, 1).start()

    def first_z(part):
        if used(part, 2):
            layer = PARTS[part][0]
            rows, room = rows_in(part, 2)
            for step in range(1, 4):
                z_copy(part, 2, step).wait()
            for across in (1 - side, side):
                total = parts[layer, core, across, zz, :, rows, :].astype(F32)
                for slot in range(1, 4):
                    total = total + third_z[slot, across, :, room, :].astype(F32)
                parts[layer, core, across, zz, :, rows, :] = total.astype(BF16)
                if across is not side:
                    x_copy(part, 2).start()

    def second_x(part):
        if used(part, 0):
            layer = PARTS[part][0]
            rows, room = rows_in(part, 0)
            y_copy(part, 0).wait()
            parts[layer, core, side, :, yy, rows, :] += ya_in[:, room, :]
            for step in range(1, 4):
                z_copy(part, 0, step).start()

    def second_y(part):
        if used(part, 1):
            layer = PARTS[part][0]
            rows, room = rows_in(part, 1)
            x_copy(part, 1).wait()
            parts[layer, core, side, :, yy, rows, :] += xb_in[:, room, :]
            for step in range(1, 4):
                z_copy(part, 1, step).start()

    def second_z(part):
        if used(part, 2):
            layer = PARTS[part][0]
            rows, room = rows_in(part, 2)
            x_copy(part, 2).wait()
            for y in (1 - yy, yy):
                parts[layer, core, side, zz, y, rows, :] += third_x[y, room, :]
                if y is not yy:
                    y_copy(part, 2).start()

    def third_done(part):
        layer = PARTS[part][0]
        for route in range(3):
            if not used(part, route):
                continue
            rows, room = rows_in(part, route)
            if route == 2:
                y_copy(part, 2).wait()
                final[layer, grp, rows, :] = parts[layer, core, side, zz, yy, rows, :] + third_y[room, :]
            else:
                for step in range(1, 4):
                    z_copy(part, route, step).wait()
                total = parts[layer, core, side, zz, yy, rows, :].astype(F32)
                for slot in range(1, 4):
                    total = total + z_in[layer, slot, rows, :].astype(F32)
                final[layer, grp, rows, :] = total.astype(BF16)
        if PARTS[part][1] >= 320:
            for row in (320, 448):
                final[layer, grp, row : row + 128, :] = final[layer, grp, row : row + 128, :].T
        for which in range(2):
            final_copy(part, which).start()

    def final_pass(part):
        final_copy(part, 0).wait()
        final_copy(part, 2).start()

    def final_done(part):
        for which in range(1, 3):
            final_copy(part, which).wait()

    def small_copy(stage):
        peer = (core_peer, x_peer, y_peer)[stage]
        return remote(
            small_sum.at[stage], small_in.at[stage], small_send.at[stage], small_recv.at[stage], peer
        )

    def small_z_copy(step):
        return remote(
            small_z.at[zz],
            small_z.at[zz],
            small_send.at[2 + step],
            small_recv.at[2 + step],
            place(core, side, lax.rem(zz + step, 4), yy),
        )

    def small_start():
        small_sum[0] = small[...]
        small_copy(0).start()

    def small_next(stage):
        small_copy(stage).wait()
        total = small_sum[stage] + small_in[stage]
        if stage < 2:
            small_sum[stage + 1] = total
            small_copy(stage + 1).start()
        else:
            small_z[zz] = total
            for step in range(1, 4):
                small_z_copy(step).start()

    def small_done():
        for step in range(1, 4):
            small_z_copy(step).wait()
        small_sum[0] = (small_z[0] + small_z[1]) + (small_z[2] + small_z[3])
        small_final[:, 0:256] = small_sum[0, :, pl.ds(pl.multiple_of(blk * 256, 256), 256)]
        pair = small_sum[0, :, pl.ds(pl.multiple_of(FF + 128 * zz, 128), 128)]
        small_final[:, 256:384] = jnp.where(yy == 1, pltpu.roll(pair, DIM, 1), pair)
        small_final[:, 384:512] = small_sum[0, :, FF + WIDTH :]

    def halves(*phases, first=0):
        def both(step, carry):
            for phase in phases:
                phase(lax.rem(step + first, 2))
            return carry

        lax.fori_loop(0, 2, both, 0)

    def begin(half):
        move_arrived(0, half, tok_in)
        hidden[rows_of(half), :] = tok_in[half].astype(F32)

    def finish(half):
        back_out[0, half] = hidden[rows_of(half), :].astype(BF16)
        to_owner(3, half, back_out.at[0, half], out_in)

    def turn_round(layer, half):
        move_arrived(2, half, cot_in)
        rows = rows_of(half)
        grad[rows, :] = cot_in[half].astype(F32)
        dz[rows, :] = (alphas[layer, 1] * grad[rows, :]).astype(BF16)

    def hand_back(half):
        back_out[1, half] = grad[rows_of(half), :].astype(BF16)
        to_owner(4, half, back_out.at[1, half], grad_in)

    barrier = pltpu.get_barrier_semaphore()
    for step in range(1, 4):
        credit(barrier, place(core, side, lax.rem(zz + step, 4), yy))
    for step in range(4):
        credit(barrier, place(1 - core, side, lax.rem(zz + step, 4), yy))
    for peer in (
        x_peer,
        y_peer,
        place(1 - core, side, zz, 1 - yy),
        place(1 - core, 1 - side, zz, yy),
        place(core, 1 - side, zz, 1 - yy),
        place(1 - core, 1 - side, zz, 1 - yy),
    ):
        credit(barrier, peer)

    weight_copies = {}
    for layer in range(LAYERS):
        for number, (source, target) in enumerate(
            ((qkv_hbm, wqkv), (out_hbm, wout), (up_hbm, wup), (down_hbm, wdown))
        ):
            weight_copies[layer, number] = pltpu.make_async_copy(
                source.at[layer], target.at[layer], w_sem.at[layer, number]
            )
    bias_copies = [
        pltpu.make_async_copy(up_bias_hbm, up_bias, w_sem.at[2, 0]),
        pltpu.make_async_copy(down_bias_hbm, down_bias, w_sem.at[2, 1]),
    ]
    weight_copies[0, 0].start()
    pl.semaphore_wait(barrier, 13)
    upper = lax.div(zz, 2)
    for half in (1 - upper, upper):
        to_team(0, half, half_of(tokens, half), tok_in)
    for copy in (*list(weight_copies.values())[1:], *bias_copies):
        copy.start(priority=1)
    end_second = lax.div(seq_len[0, 0] + seq_len[0, 1], RUNS)
    flag_out[...] = jnp.full((8, 128), end_second.astype(F32), F32)
    for half in (1 - upper, upper):
        to_team(1, half, flag_out, flag_in)
    for layer in range(LAYERS):
        for head in range(OWN):
            rq[layer, head, DIM:, :] = jnp.zeros((DIM, HALF * RUNS), BF16)
    for head in range(OWN):
        ro[head, 0:DIM, :] = jnp.zeros((DIM, HALF * RUNS), BF16)
    weight_copies[0, 0].wait()
    halves(begin, functools.partial(project, 0), first=upper)
    for half in (1 - upper, upper):
        to_team(2, half, half_of(cotangent, half), cot_in)

    move_arrived(1, 0, flag_in)
    move_arrived(1, 1, flag_in)
    border = jnp.concatenate([flag_in[0, 0:1, :]] * 2, axis=1) - (HALF * lax.div(zz, 2)).astype(F32)
    key_row = lax.broadcasted_iota(jnp.int32, (TILE, TILE), 0)
    query_col = lax.broadcasted_iota(jnp.int32, (TILE, TILE), 1)
    later = key_row > query_col
    key_sub = lax.rem(key_row, HALF).astype(F32) >= border
    query_sub = lax.rem(query_col, HALF).astype(F32) >= border
    apart = jnp.logical_xor(key_sub, query_sub)
    for tile in range(TILES - 1):
        bias[TILE * tile : TILE * tile + TILE, :] = jnp.where(apart, NEGATIVE, 0.0)
    bias[TILE * (TILES - 1) :, :] = jnp.where(jnp.logical_or(later, apart), NEGATIVE, 0.0)

    for copy in (*bias_copies, *(weight_copies[0, number] for number in range(1, 4))):
        copy.wait()
    attend(0, 0)
    attend(0, 1)
    hidden_start(0, 0)
    weight_copies[1, 0].wait()
    halves(functools.partial(feed, 0), functools.partial(project, 1))
    for number in range(1, 4):
        weight_copies[1, number].wait()
    attend(1, 0)
    attend(1, 1)
    hidden_pass(0, 0)
    hidden_start(1, 0)
    halves(functools.partial(feed, 1), finish)
    hidden_start(0, 1)
    hidden_start(1, 1)
    hidden_pass(1, 0)

    halves(functools.partial(turn_round, 1))
    make(1)
    feed_back(1)
    hidden_pass(0, 1)
    hidden_pass(1, 1)
    core_done(1)
    make(0)
    attend_back(1, 1)
    first_y(1)
    core_done(0)
    attend_back(1, 0)
    second_y(1)
    first_x(1)
    project_back(1, 1)
    heads_grads(1)
    first_z(1)
    project_back(1, 0)
    feed_back(0)
    small_start()
    second_x(1)
    make(2)
    first_x(0)
    heads_second(1)
    first_z(0)
    attend_back(0, 1)
    small_next(0)
    core_done(2)
    second_x(0)
    make(3)
    attend_back(0, 0)
    small_next(1)
    project_back(0, 1)
    hand_back(1)
    first_z(2)
    heads_grads(0)
    small_next(2)
    first_x(2)
    core_done(3)
    first_y(2)
    heads_second(0)
    small_done()
    first_z(3)
    second_x(2)
    first_x(3)
    second_z(2)
    second_z(0)
    heads_third(1)
    second_z(1)
    first_y(3)
    heads_third(0)
    second_y(2)
    second_x(3)
    second_z(3)
    third_done(0)
    third_done(2)
    second_y(3)
    project_back(0, 0)
    hand_back(0)
    heads_done(1)
    third_done(1)
    third_done(3)
    final_pass(0)
    final_pass(2)
    final_pass(1)
    final_pass(3)
    final_done(2)
    final_done(1)
    heads_done(0)
    final_done(0)
    final_done(3)
    for half in range(2):
        move_arrived(3, half, out_in)
        move_arrived(4, half, grad_in)

    for half in range(2):
        left(2, 0, half, head_out)
        left(3, 0, half, pack_out)
        to_team_left(0, half, half_of(tokens, half))
        to_team_left(1, half, flag_out)
        to_team_left(2, half, half_of(cotangent, half))
        to_owner_left(3, half, back_out.at[0, half])
        to_owner_left(4, half, back_out.at[1, half])


def results_kernel(
    final, heads, out_block, grad_block, small,
    output, input_grad, qkv_grad, out_grad, up_grad, up_bias_grad, down_grad, down_bias_grad, alpha_grad,
    out_flat, grad_wide, qkv_wide, out_wide, up_wide, down_wide, out_sem,
):
    ends = []

    def write(source, target):
        ends.append(pltpu.make_async_copy(source, target, out_sem.at[len(ends)]))
        ends[-1].start()

    up_bias_grad[...] = small[:, 0:256]
    down_bias_grad[...] = small[:, 256 : 256 + DIM]
    alpha_grad[...] = small[:, 384:386]
    for layer in range(LAYERS):
        for quarter in range(4):

            def block(first, count):
                return final[layer, quarter, first : first + count, :].astype(F32)

            def columns(step):
                return slice(WIDTH * step + 128 * quarter, WIDTH * step + 128 * quarter + 128)

            for step in range(4):
                up_wide[layer, :, columns(step)] = block(DIM * step, DIM)
            out_wide[layer, :, columns(0)] = block(256, DIM)
            down_wide[layer, :, columns(0)] = block(320, 256)
        write(up_wide.at[layer], up_grad.at[layer])
        write(out_wide.at[layer], out_grad.at[layer])
        write(down_wide.at[layer], down_grad.at[layer])
    for half in range(2):
        rows = slice(HALF * half, HALF * half + HALF)
        grad_wide[rows, :] = grad_block[half].astype(F32)
        out_flat[rows, :] = out_block[half]
    write(grad_wide, input_grad)
    write(out_flat, output)
    for layer in range(LAYERS):
        for side in range(2):
            for member in range(TEAM):
                for step in range(3):
                    at = WIDTH * step + 128 * member
                    qkv_wide[layer, 32 * side : 32 * side + 32, at : at + 128] = heads[
                        layer, side, member, :, 128 * step : 128 * step + 128
                    ].astype(F32)
        write(qkv_wide.at[layer], qkv_grad.at[layer])
    for end in ends:
        end.wait()


def fast_body(
    tokens, seq_len, qkv_weight, out_weight, up_weight, up_bias, down_weight, down_bias, alphas, cotangent
):
    whole = pl.BlockSpec(memory_space=pltpu.VMEM)
    scalar = pl.BlockSpec(memory_space=pltpu.SMEM)
    far = pl.BlockSpec(memory_space=pl.ANY)
    shape = jax.ShapeDtypeStruct
    rows = HALF * RUNS

    def vmem(*dims):
        return pltpu.VMEM(dims, BF16)

    def wide(*dims):
        return pltpu.VMEM(dims, F32)

    dma = pltpu.SemaphoreType.DMA
    final, heads, out_block, grad_block, small = pl.pallas_call(
        layers_kernel,
        out_shape=(
            vmem(LAYERS, 4, CHUNK, 128),
            vmem(LAYERS, 2, TEAM, DIM // 2, 3 * 128),
            vmem(2, HALF, WIDTH),
            vmem(2, HALF, WIDTH),
            wide(LAYERS, WIDTH),
        ),
        in_specs=[far, scalar, scalar, far, far, far, far, far, far, far],
        out_specs=(whole,) * 5,
        scratch_shapes=[
            vmem(LAYERS, WIDTH, 3 * WIDTH),
            vmem(LAYERS, WIDTH, WIDTH),
            vmem(LAYERS, WIDTH, FF),
            vmem(LAYERS, FF, WIDTH),
            wide(LAYERS, FF),
            wide(LAYERS, WIDTH),
            vmem(2, HALF, WIDTH),
            vmem(2, HALF, WIDTH),
            wide(8, 128),
            wide(2, 8, 128),
            vmem(2, 2, HALF, WIDTH),
            wide(2 * HALF, WIDTH),
            wide(2 * HALF, WIDTH),
            vmem(LAYERS, WIDTH, rows),
            vmem(LAYERS, WIDTH, 2 * HALF),
            vmem(LAYERS, 2 * HALF, WIDTH),
            vmem(LAYERS, 2 * HALF, FF),
            wide(LAYERS, 2 * HALF, WIDTH),
            wide(LAYERS, 2 * HALF, FF),
            wide(LAYERS, 2 * HALF, WIDTH),
            vmem(2 * HALF, WIDTH),
            vmem(2 * HALF, FF),
            vmem(2 * HALF, WIDTH),
            vmem(HALF, 3 * WIDTH),
            vmem(2, TEAM, OWN, PACK, 128),
            vmem(2, TEAM, OWN, DIM, 128),
            vmem(2, TEAM, OWN, PACK, 128),
            vmem(2, TEAM, OWN, DIM, 128),
            vmem(2, TEAM, OWN, DIM, 128),
            vmem(LAYERS, OWN, rows, 128),
            vmem(LAYERS, OWN, 128, rows),
            vmem(LAYERS, OWN, 128, rows),
            vmem(OWN, 128, rows),
            wide(LAYERS, OWN, DIM, rows),
            wide(LAYERS, OWN, 1, rows),
            wide(OWN, rows, 128),
            wide(OWN, DIM, rows),
            wide(rows, TILE),
            vmem(LAYERS, 2, 2, 4, 2, CHUNK, 128),
            vmem(2, 4, 2, CHUNK, 128),
            vmem(4, 2, TOTALS[0], 128),
            vmem(4, TOTALS[1], 128),
            vmem(4, TOTALS[0], 128),
            vmem(2, 4, TOTALS[1], 128),
            vmem(LAYERS, 4, CHUNK, 128),
            vmem(4, 2, 2, TOTALS[2], 128),
            vmem(2, TOTALS[2], 128),
            vmem(TOTALS[2], 128),
            vmem(LAYERS, 4, 2, DIM, 3 * 128),
            vmem(LAYERS, 4, 2, DIM // 2, 3 * 128),
            vmem(LAYERS, 4, 2, DIM // 2, 3 * 128),
            vmem(LAYERS, 2, DIM // 2, 3 * 128),
            wide(LAYERS, SMALL),
            wide(3, LAYERS, SMALL),
            wide(4, LAYERS, SMALL),
            wide(3, LAYERS, SMALL),
            dma((LAYERS + 1, 4)),
            dma((5, 2)),
            dma((5, 2)),
            dma((4, LAYERS, 2, OWN)),
            dma((4, LAYERS, 2, OWN)),
            dma((len(PARTS),)),
            dma((len(PARTS),)),
            dma((len(PARTS), 3)),
            dma((len(PARTS), 3)),
            dma((len(PARTS), 3)),
            dma((len(PARTS), 3)),
            dma((len(PARTS), 3, 4)),
            dma((len(PARTS), 3, 4)),
            dma((len(PARTS), 3)),
            dma((len(PARTS), 3)),
            dma((LAYERS, 2, 3)),
            dma((LAYERS, 2, 3)),
            dma((LAYERS,)),
            dma((LAYERS,)),
            dma((LAYERS, 4)),
            dma((LAYERS, 4)),
            dma((LAYERS, 8)),
            dma((LAYERS, 8)),
            dma((6,)),
            dma((6,)),
            pltpu.SemaphoreType.REGULAR((2,)),
        ],
        compiler_params=pltpu.CompilerParams(
            collective_id=0, has_side_effects=True, vmem_limit_bytes=61 * 1024 * 1024
        ),
        name="layers",
    )(
        tokens, seq_len, alphas, up_bias, down_bias, cotangent,
        qkv_weight, out_weight, up_weight, down_weight,
    )
    return tuple(
        pl.pallas_call(
            results_kernel,
            out_shape=(
                shape((2 * HALF, WIDTH), BF16),
                shape((2 * HALF, WIDTH), F32),
                shape((LAYERS, DIM, 3 * WIDTH), F32),
                shape((LAYERS, DIM, WIDTH), F32),
                shape((LAYERS, DIM, FF), F32),
                shape((LAYERS, FF // RUNS), F32),
                shape((LAYERS, FF // RUNS, WIDTH), F32),
                shape((LAYERS, DIM), F32),
                shape((LAYERS, 2), F32),
            ),
            in_specs=[whole] * 5,
            out_specs=(far, far, far, far, far, whole, far, whole, whole),
            scratch_shapes=[
                vmem(2 * HALF, WIDTH),
                wide(2 * HALF, WIDTH),
                wide(LAYERS, DIM, 3 * WIDTH),
                wide(LAYERS, DIM, WIDTH),
                wide(LAYERS, DIM, FF),
                wide(LAYERS, FF // RUNS, WIDTH),
                dma((10,)),
            ],
            compiler_params=pltpu.CompilerParams(vmem_limit_bytes=24 * 1024 * 1024),
            name="results",
        )(final, heads, out_block, grad_block, small)
    )


def layout(seq_len, local_count, cycle_size):
    piece_rows = seq_len[0] // cycle_size
    end_rows = jnp.cumsum(piece_rows)
    start_rows = end_rows - piece_rows
    local_rows = jnp.arange(local_count, dtype=jnp.int32)
    segment = jnp.sum((local_rows[:, None] >= end_rows[None, :]).astype(jnp.int32), axis=1)
    picked = segment[:, None] == jnp.arange(seq_len.shape[1], dtype=jnp.int32)[None, :]
    offset = local_rows - jnp.sum(jnp.where(picked, start_rows[None, :], 0), axis=1)
    span_rows = jnp.sum(jnp.where(picked, piece_rows[None, :], 0), axis=1)
    return (segment, offset, span_rows)


def gelu_exact(values):
    return jax.nn.gelu(values, approximate=False)


def key_block(whole, geometry, block_index, head_count):
    query_seg, query_pos, seg_all, pos_all, block_rows, score_scale = geometry
    first_row = block_index * block_rows
    key_piece = lax.dynamic_slice_in_dim(whole, first_row, block_rows, 0)
    key_seg = lax.dynamic_slice_in_dim(seg_all, first_row, block_rows, 0)
    key_pos = lax.dynamic_slice_in_dim(pos_all, first_row, block_rows, 0)
    half_width = key_piece.shape[1] // 2
    keys_part = key_piece[:, :half_width].reshape(block_rows, head_count, -1)
    values_part = key_piece[:, half_width:].reshape(block_rows, head_count, -1)
    return (keys_part, values_part, key_seg, key_pos)


def block_scores(queries, keys_part, key_seg, key_pos, geometry):
    query_seg, query_pos, seg_all, pos_all, block_rows, score_scale = geometry
    scores = (
        jnp.einsum("qhd,khd->hqk", queries, keys_part, preferred_element_type=jnp.float32)
        * score_scale
    )
    allowed = (query_seg[:, None] == key_seg[None, :]) & (key_pos[None, :] <= query_pos[:, None])
    return (scores, allowed[None])


def attend(queries, whole, geometry):
    row_count, head_count, head_dim = queries.shape
    block_count = whole.shape[0] // geometry[4]

    def statistics(running, block_index):
        largest, totals = running
        keys_part, values_part, key_seg, key_pos = key_block(
            whole, geometry, block_index, head_count
        )
        scores, allowed = block_scores(queries, keys_part, key_seg, key_pos, geometry)
        newest = jnp.maximum(largest, jnp.max(jnp.where(allowed, scores, NEGATIVE), axis=2))
        weights = jnp.where(allowed, jnp.exp(scores - newest[:, :, None]), 0.0)
        totals = totals * jnp.exp(largest - newest) + jnp.sum(weights, axis=2)
        return ((newest, totals), None)

    initial = (
        jnp.full((head_count, row_count), NEGATIVE, jnp.float32),
        jnp.zeros((head_count, row_count), jnp.float32),
    )
    (largest, totals), unused = lax.scan(statistics, initial, jnp.arange(block_count))
    log_total = largest + jnp.log(totals)

    def weighted(output_sum, block_index):
        keys_part, values_part, key_seg, key_pos = key_block(
            whole, geometry, block_index, head_count
        )
        scores, allowed = block_scores(queries, keys_part, key_seg, key_pos, geometry)
        probs = jnp.where(allowed, jnp.exp(scores - log_total[:, :, None]), 0.0).astype(
            jnp.bfloat16
        )
        output_sum = output_sum + jnp.einsum(
            "hqk,khd->qhd", probs, values_part, preferred_element_type=jnp.float32
        )
        return (output_sum, None)

    output_sum, unused = lax.scan(
        weighted, jnp.zeros((row_count, head_count, head_dim), jnp.float32), jnp.arange(block_count)
    )
    return (output_sum, log_total)


def attend_back(queries, whole, log_total, delta_sum, grad_heads, geometry):
    row_count, head_count, head_dim = queries.shape
    block_rows = geometry[4]
    score_scale = geometry[5]
    block_count = whole.shape[0] // block_rows

    def gradients(query_grad, block_index):
        keys_part, values_part, key_seg, key_pos = key_block(
            whole, geometry, block_index, head_count
        )
        scores, allowed = block_scores(queries, keys_part, key_seg, key_pos, geometry)
        probs = jnp.where(allowed, jnp.exp(scores - log_total[:, :, None]), 0.0)
        grad_probs = jnp.einsum(
            "qhd,khd->hqk", grad_heads, values_part, preferred_element_type=jnp.float32
        )
        grad_scores = (probs * (grad_probs - delta_sum[:, :, None])).astype(jnp.bfloat16)
        query_grad = (
            query_grad
            + jnp.einsum("hqk,khd->qhd", grad_scores, keys_part, preferred_element_type=jnp.float32)
            * score_scale
        )
        key_grad = (
            jnp.einsum("hqk,qhd->khd", grad_scores, queries, preferred_element_type=jnp.float32)
            * score_scale
        )
        value_grad = jnp.einsum(
            "hqk,qhd->khd",
            probs.astype(jnp.bfloat16),
            grad_heads,
            preferred_element_type=jnp.float32,
        )
        joined = jnp.concatenate(
            [key_grad.reshape(block_rows, -1), value_grad.reshape(block_rows, -1)], axis=1
        )
        return (query_grad, joined)

    query_grad, stacked = lax.scan(
        gradients,
        jnp.zeros((row_count, head_count, head_dim), jnp.float32),
        jnp.arange(block_count),
    )
    return (query_grad, stacked.reshape(whole.shape[0], -1))


def layer_forward(hidden, layer_index, weights, geometry):
    qkv_weight, out_weight, up_weight, up_bias, down_weight, down_bias, alphas = weights
    row_count, model_width = hidden.shape
    projection = qkv_weight[layer_index]
    rounded = hidden.astype(jnp.bfloat16)
    queries = (
        jnp.dot(rounded, projection[:, :model_width], preferred_element_type=jnp.float32)
        .astype(jnp.bfloat16)
        .reshape(row_count, HEADS, -1)
    )
    key_value = jnp.dot(
        rounded, projection[:, model_width:], preferred_element_type=jnp.float32
    ).astype(jnp.bfloat16)
    whole = lax.all_gather(key_value, "blk", axis=0, tiled=True)
    heads_out, log_total = attend(queries, whole, geometry)
    heads_rounded = heads_out.reshape(row_count, model_width).astype(jnp.bfloat16)
    branch = jnp.dot(heads_rounded, out_weight[layer_index], preferred_element_type=jnp.float32)
    alpha_pair = alphas[layer_index]
    middle = hidden + alpha_pair[0] * branch
    entered = middle.astype(jnp.bfloat16)
    gate_pre = (
        jnp.dot(entered, up_weight[layer_index], preferred_element_type=jnp.float32)
        + up_bias[layer_index]
    )
    activated = gelu_exact(gate_pre).astype(jnp.bfloat16)
    second = (
        jnp.dot(activated, down_weight[layer_index], preferred_element_type=jnp.float32)
        + down_bias[layer_index]
    )
    result = middle + alpha_pair[1] * second
    saved = (
        rounded,
        queries,
        key_value,
        whole,
        heads_out,
        heads_rounded,
        log_total,
        branch,
        entered,
        gate_pre,
        activated,
        second,
    )
    return (result, saved)


def layer_backward(grad_hidden, saved, layer_index, weights, geometry):
    qkv_weight, out_weight, up_weight, up_bias, down_weight, down_bias, alphas = weights
    (
        rounded,
        queries,
        key_value,
        saved_whole,
        heads_out,
        heads_rounded,
        log_total,
        branch,
        entered,
        gate_pre,
        activated,
        second,
    ) = saved
    row_count = grad_hidden.shape[0]
    alpha_pair = alphas[layer_index]
    grad_second = (alpha_pair[1] * grad_hidden).astype(jnp.bfloat16)
    alpha_second = jnp.sum(grad_hidden * second)
    bias_down = jnp.sum(grad_second.astype(jnp.float32), axis=0)
    grad_down = jnp.einsum("tf,td->fd", activated, grad_second, preferred_element_type=jnp.float32)
    grad_act = jnp.einsum(
        "td,fd->tf", grad_second, down_weight[layer_index], preferred_element_type=jnp.float32
    )
    unused, gelu_pull = jax.vjp(gelu_exact, gate_pre)
    grad_gate = gelu_pull(grad_act)[0].astype(jnp.bfloat16)
    bias_up = jnp.sum(grad_gate.astype(jnp.float32), axis=0)
    grad_up = jnp.einsum("td,tf->df", entered, grad_gate, preferred_element_type=jnp.float32)
    grad_middle = grad_hidden + jnp.einsum(
        "tf,df->td", grad_gate, up_weight[layer_index], preferred_element_type=jnp.float32
    )
    grad_branch = (alpha_pair[0] * grad_middle).astype(jnp.bfloat16)
    alpha_first = jnp.sum(grad_middle * branch)
    grad_proj_out = jnp.einsum(
        "te,td->ed", heads_rounded, grad_branch, preferred_element_type=jnp.float32
    )
    grad_heads = (
        jnp.einsum(
            "td,ed->te", grad_branch, out_weight[layer_index], preferred_element_type=jnp.float32
        )
        .astype(jnp.bfloat16)
        .reshape(queries.shape)
    )
    delta_sum = jnp.sum(grad_heads.astype(jnp.float32) * heads_out, axis=2).T
    whole = lax.all_gather(key_value, "blk", axis=0, tiled=True)
    query_grad, key_terms = attend_back(queries, whole, log_total, delta_sum, grad_heads, geometry)
    key_grads = lax.psum_scatter(
        key_terms.astype(jnp.bfloat16), "blk", scatter_dimension=0, tiled=True
    )
    grad_proj = jnp.concatenate(
        [query_grad.reshape(row_count, -1).astype(jnp.bfloat16), key_grads], axis=1
    )
    grad_qkv = jnp.einsum("td,te->de", rounded, grad_proj, preferred_element_type=jnp.float32)
    grad_input = grad_middle + jnp.einsum(
        "te,de->td", grad_proj, qkv_weight[layer_index], preferred_element_type=jnp.float32
    )
    layer_grads = (
        grad_qkv,
        grad_proj_out,
        grad_up,
        bias_up,
        grad_down,
        bias_down,
        jnp.stack([alpha_first, alpha_second]),
    )
    return (grad_input, layer_grads)


def reduce_all(layer_results, cycle_size):
    stacked = [
        jnp.stack([layer_entry[member] for layer_entry in layer_results], axis=0)
        for member in range(6)
    ]
    alpha_tiles = jnp.stack(
        [jnp.tile(layer_entry[6], cycle_size) for layer_entry in layer_results], axis=0
    )
    shares = (
        lax.psum_scatter(
            stacked[0].astype(jnp.bfloat16), "blk", scatter_dimension=1, tiled=True
        ).astype(jnp.float32),
        lax.psum_scatter(
            stacked[1].astype(jnp.bfloat16), "blk", scatter_dimension=1, tiled=True
        ).astype(jnp.float32),
        lax.psum_scatter(
            stacked[2].astype(jnp.bfloat16), "blk", scatter_dimension=1, tiled=True
        ).astype(jnp.float32),
        lax.psum_scatter(
            stacked[3].astype(jnp.bfloat16), "blk", scatter_dimension=1, tiled=True
        ).astype(jnp.float32),
        lax.psum_scatter(
            stacked[4].astype(jnp.bfloat16), "blk", scatter_dimension=1, tiled=True
        ).astype(jnp.float32),
        lax.psum_scatter(
            stacked[5].astype(jnp.bfloat16), "blk", scatter_dimension=1, tiled=True
        ).astype(jnp.float32),
        lax.psum_scatter(
            alpha_tiles.astype(jnp.bfloat16), "blk", scatter_dimension=1, tiled=True
        ).astype(jnp.float32),
    )
    return (
        lax.psum(shares[0].astype(jnp.bfloat16), "grp").astype(jnp.float32),
        lax.psum(shares[1].astype(jnp.bfloat16), "grp").astype(jnp.float32),
        lax.psum(shares[2].astype(jnp.bfloat16), "grp").astype(jnp.float32),
        lax.psum(shares[3].astype(jnp.bfloat16), "grp").astype(jnp.float32),
        lax.psum(shares[4].astype(jnp.bfloat16), "grp").astype(jnp.float32),
        lax.psum(shares[5].astype(jnp.bfloat16), "grp").astype(jnp.float32),
        lax.psum(shares[6].astype(jnp.bfloat16), "grp").astype(jnp.float32),
    )


def body(
    tokens,
    seq_len,
    qkv_weight,
    out_weight,
    up_weight,
    up_bias,
    down_weight,
    down_bias,
    alphas,
    cotangent,
):
    row_count, model_width = tokens.shape
    cycle_size = lax.axis_size("blk")
    cycle_place = lax.axis_index("blk")
    head_dim = model_width // HEADS
    total_rows = cycle_size * row_count
    block_rows = min(max(row_count, 512), total_rows)
    segment, offset, span_rows = layout(seq_len, row_count, cycle_size)
    query_pos = cycle_place * span_rows + offset
    seg_all = jnp.tile(segment, cycle_size)
    pos_all = jnp.repeat(jnp.arange(cycle_size, dtype=jnp.int32), row_count) * jnp.tile(
        span_rows, cycle_size
    ) + jnp.tile(offset, cycle_size)
    geometry = (segment, query_pos, seg_all, pos_all, block_rows, head_dim ** (-0.5))
    weights = (qkv_weight, out_weight, up_weight, up_bias, down_weight, down_bias, alphas)
    hidden = tokens.astype(jnp.float32)
    saved_layers = []
    for layer_index in range(LAYERS):
        hidden, saved = layer_forward(hidden, layer_index, weights, geometry)
        saved_layers.append(saved)
    output = hidden.astype(jnp.bfloat16)
    grad_hidden = cotangent.astype(jnp.float32)
    layer_results = []
    for layer_index in reversed(range(LAYERS)):
        grad_hidden, layer_grads = layer_backward(
            grad_hidden, saved_layers[layer_index], layer_index, weights, geometry
        )
        layer_results.insert(0, layer_grads)
    finals = reduce_all(layer_results, cycle_size)
    return (
        output,
        grad_hidden,
        finals[0],
        finals[1],
        finals[2],
        finals[3],
        finals[4],
        finals[5],
        finals[6],
    )


def solution(mesh):
    placed = (
        P(("grp", "blk"), None),
        P("grp", None),
        P(),
        P(),
        P(),
        P(),
        P(),
        P(),
        P(),
        P(("grp", "blk"), None),
    )
    sizes = (mesh.shape["grp"], mesh.shape["blk"])
    return jax.shard_map(
        fast_body if sizes == (4, RUNS) else body,
        mesh=mesh,
        in_specs=placed,
        out_specs=(
            P(("grp", "blk"), None),
            P(("grp", "blk"), None),
            P(None, "blk", None),
            P(None, "blk", None),
            P(None, "blk", None),
            P(None, "blk"),
            P(None, "blk", None),
            P(None, "blk"),
            P(),
        ),
        check_vma=False,
    )
```

```python
import functools

import jax
import jax.numpy as jnp
from jax import lax
from jax.experimental import pallas as pl
from jax.experimental.pallas import tpu as pltpu
from jax.sharding import PartitionSpec as P

HEADS = 8
LAYERS = 2
NEGATIVE = -1e30
MESH = pl.DeviceIdType.MESH
F32 = jnp.float32
BF16 = jnp.bfloat16

HALF = 128
RUNS = 8
TEAM = 4
OWN = RUNS // TEAM
DIM = 64
WIDTH = 512
FF = 2048
CUT = 512
TILE = 256
TILES = HALF * RUNS // TILE
CHUNK = 576
SMALL = FF + WIDTH + 128
PARTS = ((1, 0, 320), (1, 320, 256), (0, 0, 320), (0, 320, 256))
SHARES = ((192, 0, 128), (160, 16, 80), (160, 112, 48), (128, 96, 32))


def spans():
    places, totals = {}, [0, 0, 0]
    for part, counts in enumerate(SHARES):
        first = PARTS[part][1]
        for route, count in enumerate(counts):
            places[part, route] = (first, totals[route], count)
            first += count
            totals[route] += count
    return places, totals


SPANS, TOTALS = spans()

SLOPE_AT = 0.28
TAIL = (
    0.11652077851573843,
    0.06749675579450809,
    0.2689101589486142,
    -0.23699347299932225,
    0.3898740127620002,
    -0.10580824228351815,
)


def nn(a, b):
    return lax.dot_general(a, b, (((1,), (0,)), ((), ())), preferred_element_type=F32)


def nt(a, b):
    return lax.dot_general(a, b, (((1,), (1,)), ((), ())), preferred_element_type=F32)


def layers_kernel(
    tokens, seq_len, alphas, up_bias_hbm, down_bias_hbm, cotangent, qkv_hbm, out_hbm, up_hbm, down_hbm,
    final, heads_all, out_in, grad_in, small_final,
    wqkv, wout, wup, wdown, up_bias, down_bias,
    tok_in, cot_in, flag_out, flag_in, back_out,
    hidden, grad, hid_all, attn_t, entered, act, branch, slope, second,
    dz, du, da, dqkv,
    pack_out, head_out, pack_in, o_in, do_in,
    kp, kt, vp, vt, rq, ro, o_t, lse, acc_k, acc_v, dq_t, bias,
    parts, core_in, xa_in, xb_in, ya_in, yb_in, z_in, third_z, third_x, third_y,
    heads_out, heads_x, heads_z, heads_sum, small, small_in, small_z, small_sum,
    w_sem, move_send, move_recv, a2a_send, a2a_recv, core_send, core_recv, x_send, x_recv, y_send, y_recv,
    z_send, z_recv, fin_send, fin_recv, hid_send, hid_recv, hx_send, hx_recv, hz_send, hz_recv, hf_send, hf_recv,
    small_send, small_recv, core_free,
):
    grp = lax.axis_index("grp")
    blk = lax.axis_index("blk")
    core = lax.rem(grp, 2)
    side = lax.div(grp, 2)
    yy = lax.rem(blk, 2)
    zz = lax.div(blk, 2)
    member = 2 * core + yy
    far_side = 2 * (1 - side) + core

    def place(c, x, z, y):
        return (2 * x + c, 2 * z + y)

    core_peer = place(1 - core, side, zz, yy)
    x_peer = place(core, 1 - side, zz, yy)
    y_peer = place(core, side, zz, 1 - yy)

    def remote(source, target, send, recv, peer):
        return pltpu.make_async_remote_copy(
            src_ref=source,
            dst_ref=target,
            send_sem=send,
            recv_sem=recv,
            device_id=peer,
            device_id_type=MESH,
        )

    def credit(semaphore, peer, count=1):
        pl.semaphore_signal(semaphore, inc=count, device_id=peer, device_id_type=MESH)

    def moved(kind, slot, source, target, at, core_at, z_at):
        here = jnp.logical_and(core_at == core, z_at == zz)

        @pl.when(here)
        def _():
            pltpu.make_async_copy(source, target.at[at], move_recv.at[kind, at]).start()

        @pl.when(jnp.logical_not(here))
        def _():
            pltpu.make_async_remote_copy(
                src_ref=source,
                dst_ref=target.at[at],
                send_sem=move_send.at[kind, slot],
                recv_sem=move_recv.at[kind, at],
                device_id=place(core_at, side, z_at, yy),
                device_id_type=MESH,
            ).start()

    def move_left(kind, slot, source, core_at, z_at):
        here = jnp.logical_and(core_at == core, z_at == zz)

        @pl.when(jnp.logical_not(here))
        def _():
            pltpu.make_async_copy(source, source, move_send.at[kind, slot]).wait()

    def move_arrived(kind, at, target):
        pltpu.make_async_copy(target.at[at], target.at[at], move_recv.at[kind, at]).wait()

    def to_team(kind, half, source, target):
        moved(kind, half, source, target, lax.div(zz, 2), lax.rem(zz, 2), 2 * half + core)

    def to_team_left(kind, half, source):
        move_left(kind, half, source, lax.rem(zz, 2), 2 * half + core)

    def to_owner(kind, chunk, source, target):
        moved(kind, chunk, source, target, lax.div(zz, 2), lax.rem(zz, 2), core + 2 * chunk)

    def to_owner_left(kind, chunk, source):
        move_left(kind, chunk, source, lax.rem(zz, 2), core + 2 * chunk)

    def half_of(ref, half):
        return ref.at[pl.ds(pl.multiple_of(HALF * half, HALF), HALF)]

    def rows_of(half):
        return pl.ds(pl.multiple_of(half * HALF, HALF), HALF)

    def slot_of(other):
        return lax.rem(other + TEAM - member, TEAM)

    def exchange(kind, layer, half, outgoing, incoming, blocks=()):
        incoming[(half, 0, *blocks)] = outgoing[(half, member, *blocks)]
        for step in range(1, TEAM):
            peer = lax.rem(member + step, TEAM)
            remote(
                outgoing.at[(half, peer, *blocks)],
                incoming.at[(half, TEAM - step, *blocks)],
                a2a_send.at[kind, layer, half],
                a2a_recv.at[kind, layer, half],
                place(lax.div(peer, 2), side, zz, lax.rem(peer, 2)),
            ).start()

    def give(kind, layer, half, outgoing, incoming, peer):
        @pl.when(member == peer)
        def _():
            incoming[half, 0] = outgoing[half, peer]

        @pl.when(member != peer)
        def _():
            remote(
                outgoing.at[half, peer],
                incoming.at[half, lax.rem(member + TEAM - peer, TEAM)],
                a2a_send.at[kind, layer, half],
                a2a_recv.at[kind, layer, half],
                place(peer // 2, side, zz, peer % 2),
            ).start()

    def arrived(kind, layer, half, incoming, blocks=()):
        whole = incoming.at[(half, pl.ds(1, TEAM - 1), *blocks)]
        pltpu.make_async_copy(whole, whole, a2a_recv.at[kind, layer, half]).wait()

    def left(kind, layer, half, outgoing, blocks=()):
        whole = outgoing.at[(half, pl.ds(1, TEAM - 1), *blocks)]
        pltpu.make_async_copy(whole, whole, a2a_send.at[kind, layer, half]).wait()

    def tokens_of(chunk, other):
        return pl.ds(pl.multiple_of(HALF * (TEAM * chunk + other), HALF), HALF)

    def hidden_copy(layer, chunk, which):
        whose = 2 * core + 1 - yy if which == 2 else member
        block = hid_all.at[layer, :, tokens_of(chunk, whose)]
        return remote(
            block,
            block,
            hid_send.at[layer, chunk, which],
            hid_recv.at[layer, chunk, which],
            y_peer if which == 0 else core_peer,
        )

    def hidden_start(layer, chunk):
        for which in range(2):
            hidden_copy(layer, chunk, which).start()

    def hidden_pass(layer, chunk):
        hidden_copy(layer, chunk, 0).wait()
        hidden_copy(layer, chunk, 2).start()

    def hidden_done(layer, chunk):
        for which in range(1, 3):
            hidden_copy(layer, chunk, which).wait()

    keys_queries, only_values = (pl.ds(0, 2),), (2,)

    def project(layer, half):
        rows = rows_of(half)
        rounded = hidden[rows, :].astype(BF16)
        if layer == 1:
            left(0, 0, half, pack_out, keys_queries)
            left(4, 0, half, pack_out, only_values)
        queries = (nn(rounded, wqkv[layer, :, 0:WIDTH]) * (DIM ** -0.5)).astype(BF16).T
        keys = nn(rounded, wqkv[layer, :, WIDTH : 2 * WIDTH]).astype(BF16)
        for pair in range(TEAM):
            pack_out[half, pair, 0] = keys[:, 128 * pair : 128 * pair + 128]
            pack_out[half, pair, 1] = queries[128 * pair : 128 * pair + 128, :]
        exchange(0, layer, half, pack_out, pack_in, keys_queries)
        values = nn(rounded, wqkv[layer, :, 2 * WIDTH : 3 * WIDTH]).astype(BF16)
        for pair in range(TEAM):
            pack_out[half, pair, 2] = values[:, 128 * pair : 128 * pair + 128]
        exchange(4, layer, half, pack_out, pack_in, only_values)
        hid_all[layer, :, tokens_of(half, member)] = rounded.T

    def span_of(chunk, other):
        start = HALF * (TEAM * chunk + other)
        return slice(start, start + HALF)

    def attend(layer, chunk):
        if layer == 1:
            left(1, 0, chunk, head_out)
        arrived(0, layer, chunk, pack_in, keys_queries)
        for other in range(TEAM):
            slot, span = slot_of(other), span_of(chunk, other)
            kp[layer, span, :] = pack_in[chunk, slot, 0]
            for head in range(OWN):
                lanes = slice(DIM * head, DIM * head + DIM)
                rq[layer, head, lanes, span] = pack_in[chunk, slot, 1, lanes, :]

        def scores_of(head, i):
            count = TILE * (i + 1)
            tile = rq[layer, head, :, TILE * i : TILE * i + TILE]
            return nn(kp[layer, 0:count, :], tile) + bias[TILE * TILES - count :, :]

        order = [(head, i) for head in range(OWN) for i in (2 * chunk, 2 * chunk + 1)]
        coming = scores_of(*order[0])
        arrived(4, layer, chunk, pack_in, only_values)
        for other in range(TEAM):
            span = span_of(chunk, other)
            block = pack_in[chunk, slot_of(other), 2]
            vp[layer, span, :] = block
            vt[layer, :, span] = block.T
        for number, (head, i) in enumerate(order):
            lanes = slice(DIM * head, DIM * head + DIM)
            columns = slice(TILE * i, TILE * i + TILE)
            scores = coming
            if number + 1 < len(order):
                coming = scores_of(*order[number + 1])
            largest = jnp.max(scores, axis=0, keepdims=True)
            weight = jnp.exp(scores - largest)
            total = jnp.sum(weight, axis=0, keepdims=True)
            summed = nn(vt[layer, lanes, 0 : TILE * (i + 1)], weight.astype(BF16)) / total
            o_t[layer, head, :, columns] = summed
            lse[layer, head, :, columns] = largest + jnp.log(total)
            rounded = summed.astype(BF16)
            for part in range(2):
                head_out[chunk, 2 * (i - 2 * chunk) + part, head] = rounded[
                    :, HALF * part : HALF * part + HALF
                ]
        exchange(1, layer, chunk, head_out, o_in)
        for other in range(TEAM):
            span = span_of(chunk, other)
            kt[layer, :, span] = kp[layer, span, :].T

    def feed(layer, half):
        rows = rows_of(half)
        arrived(1, layer, half, o_in)
        for head in range(RUNS):
            attn_t[layer, DIM * head : DIM * head + DIM, rows] = o_in[half, slot_of(head // 2), head % 2]
        attn = attn_t[layer, :, rows].T
        grown = nn(attn, wout[layer])
        branch[layer, rows, :] = grown
        middle = hidden[rows, :] + alphas[layer, 0] * grown
        rounded = middle.astype(BF16)
        entered[layer, rows, :] = rounded
        total = jnp.zeros((HALF, WIDTH), F32)

        def gate_of(step):
            cut = slice(CUT * step, CUT * step + CUT)
            return nn(rounded, wup[layer, :, cut]) + up_bias[layer : layer + 1, cut]

        coming = gate_of(0)
        for step in range(FF // CUT):
            cut = slice(CUT * step, CUT * step + CUT)
            gate = coming
            if step + 1 < FF // CUT:
                coming = gate_of(step + 1)
            bell = jnp.exp(gate * gate * -0.5)
            near = pl.reciprocal(1.0 + SLOPE_AT * jnp.abs(gate), approx=True)
            tail = jnp.full_like(gate, TAIL[5])
            for factor in TAIL[4::-1]:
                tail = tail * near + factor
            tail = bell * (tail * near)
            risen = jnp.where(gate > 0.0, 1.0 - tail, tail)
            slope[layer, rows, cut] = risen + gate * bell * 0.3989422804014327
            active = (gate * risen).astype(BF16)
            act[layer, rows, cut] = active
            total = total + nn(active, wdown[layer, cut, :])
        total = total + down_bias[layer : layer + 1, :]
        second[layer, rows, :] = total
        hidden[rows, :] = middle + alphas[layer, 1] * total

    def total_of(values):
        return jnp.sum(jnp.sum(values, axis=0, keepdims=True), axis=1, keepdims=True)

    def feed_back(layer):
        start = grad[...]
        if layer == 0:
            dz[...] = (alphas[layer, 1] * start).astype(BF16)
        scaled = dz[...]
        alpha_second = total_of(start * second[layer])
        small[layer : layer + 1, FF : FF + WIDTH] = jnp.sum(scaled.astype(F32), axis=0, keepdims=True)
        middle = start
        coming = nt(scaled, wdown[layer, 0:CUT, :])
        for step in range(FF // CUT):
            cut = slice(CUT * step, CUT * step + CUT)
            raw = coming
            if step + 1 < FF // CUT:
                coming = nt(scaled, wdown[layer, CUT * (step + 1) : CUT * (step + 2), :])
            gate = (raw * slope[layer, :, cut]).astype(BF16)
            du[:, cut] = gate
            small[layer : layer + 1, cut] = jnp.sum(gate.astype(F32), axis=0, keepdims=True)
            middle = middle + nt(gate, wup[layer, :, cut])
        grad[...] = middle
        mixed = (alphas[layer, 0] * middle).astype(BF16)
        da[...] = mixed
        spread = nt(wout[layer], mixed).astype(BF16)
        for chunk in (1, 0):
            left(*((1, 1) if layer == 1 else (2, 1)), chunk, head_out)
            for head in range(RUNS):
                head_out[chunk, head // 2, head % 2] = spread[
                    DIM * head : DIM * head + DIM, HALF * chunk : HALF * chunk + HALF
                ]
            exchange(2, layer, chunk, head_out, do_in)
        alpha_first = total_of(middle * branch[layer])
        column = lax.broadcasted_iota(jnp.int32, (1, 128), 1)
        small[layer : layer + 1, FF + WIDTH :] = jnp.where(
            column == 0, alpha_first, jnp.where(column == 1, alpha_second, 0.0)
        )

    def attend_back(layer, chunk):
        arrived(2, layer, chunk, do_in)
        if layer == 1:
            left(0, 1, chunk, pack_out, keys_queries)
            left(4, 1, chunk, pack_out, only_values)
        else:
            left(3, 1, chunk, pack_out)
        for other in range(TEAM):
            for head in range(OWN):
                lanes = slice(DIM * head, DIM * head + DIM)
                ro[head, lanes, span_of(chunk, other)] = do_in[chunk, slot_of(other), head]
        for i in (2 * chunk + 1, 2 * chunk):
            columns = slice(TILE * i, TILE * i + TILE)
            count = TILE * (i + 1)
            for head in range(OWN):
                lanes = slice(DIM * head, DIM * head + DIM)
                query_tile = rq[layer, head, :, columns]
                grad_tile = ro[head, :, columns]
                delta = jnp.sum(
                    ro[head, lanes, columns].astype(F32) * o_t[layer, head, :, columns],
                    axis=0,
                    keepdims=True,
                )
                scores = nn(kp[layer, 0:count, :], query_tile) + bias[TILE * TILES - count :, :]
                weight = jnp.exp(scores - lse[layer, head, :, columns])
                scored = (weight * (nn(vp[layer, 0:count, :], grad_tile) - delta)).astype(BF16)
                key_term = nt(scored, query_tile)
                value_term = nt(weight.astype(BF16), grad_tile)
                if i == TILES - 1 and head == 0:
                    acc_k[...] = key_term
                    acc_v[...] = value_term
                else:
                    acc_k[0:count, :] += key_term
                    acc_v[0:count, :] += value_term
                dq_t[lanes, columns] = nn(kt[layer, lanes, 0:count], scored) * (DIM ** -0.5)
            for run in (2 * i, 2 * i + 1):
                span = slice(HALF * run, HALF * run + HALF)
                pack_out[chunk, run % TEAM, 0] = acc_k[span, :].astype(BF16)
                pack_out[chunk, run % TEAM, 1] = dq_t[:, span].astype(BF16)
                pack_out[chunk, run % TEAM, 2] = acc_v[span, :].astype(BF16)
                give(3, layer, chunk, pack_out, pack_in, run % TEAM)

    def project_back(layer, half):
        arrived(3, layer, half, pack_in)
        turned = jnp.concatenate([pack_in[half, slot_of(other), 1] for other in range(TEAM)], axis=0)
        dqkv[:, 0:WIDTH] = turned.T
        for other in range(TEAM):
            at = WIDTH + 128 * other
            dqkv[:, at : at + 128] = pack_in[half, slot_of(other), 0]
            dqkv[:, WIDTH + at : WIDTH + at + 128] = pack_in[half, slot_of(other), 2]
        rows = rows_of(half)
        grad[rows, :] = grad[rows, :] + nt(dqkv[...], wqkv[layer])

    def scatter_rows(layer, result, first_row):
        for run in range(RUNS):
            for quarter in range(4):
                parts[layer, quarter % 2, quarter // 2, run // 2, run % 2, first_row : first_row + DIM, :] = result[
                    DIM * run : DIM * run + DIM, 128 * quarter : 128 * quarter + 128
                ].astype(BF16)

    def make(part):
        layer, first, count = PARTS[part]
        if first < 256:
            turned = entered[layer].T
        for row in range(first, min(first + count, 256), DIM):
            step = row // DIM
            scatter_rows(layer, nn(turned, du[:, CUT * step : CUT * step + CUT]), row)
        if first <= 256 < first + count:
            scatter_rows(layer, nn(attn_t[layer], da[...]), 256)
        if first >= 320:
            turned = dz[...].T
            for step in range(FF // CUT):
                result = nn(turned, act[layer, :, CUT * step : CUT * step + CUT])
                for block in range(CUT // 128):
                    run, row = 2 * step + block // 2, 320 + 128 * (block % 2)
                    for quarter in range(4):
                        parts[layer, quarter % 2, quarter // 2, run // 2, run % 2, row : row + 128, :] = result[
                            128 * quarter : 128 * quarter + 128, 128 * block : 128 * block + 128
                        ].astype(BF16)
        if layer == 0:
            pl.semaphore_wait(core_free.at[0 if first < 320 else 1], 1)
        core_copy(part).start()

    def heads_grads(layer):
        for chunk in range(2):
            hidden_done(layer, chunk)
        blocks = [(run // TEAM, run % TEAM) for run in range(RUNS)]
        keys_values = jnp.concatenate(
            [
                jnp.concatenate([pack_out[chunk, other, number] for chunk, other in blocks], axis=0)
                for number in (0, 2)
            ],
            axis=1,
        )
        queries = jnp.concatenate([pack_out[chunk, other, 1] for chunk, other in blocks], axis=1)
        both = nn(hid_all[layer], keys_values)
        q_part = nt(hid_all[layer], queries)
        k_part, v_part = both[:, 0:128], both[:, 128:256]
        for number, values in enumerate((q_part, k_part, v_part)):
            for run in range(RUNS):
                heads_out[layer, run // 2, run % 2, :, 128 * number : 128 * number + 128] = values[
                    DIM * run : DIM * run + DIM, :
                ].astype(BF16)
        heads_x_copy(layer).start()

    def half_rows(which):
        return pl.ds(pl.multiple_of(32 * which, 32), 32)

    def heads_x_copy(layer):
        return remote(
            heads_out.at[layer, :, :, half_rows(1 - side)],
            heads_x.at[layer],
            hx_send.at[layer],
            hx_recv.at[layer],
            x_peer,
        )

    def heads_z_copy(layer, step):
        peer = lax.rem(zz + step, 4)
        return remote(
            heads_out.at[layer, peer, :, half_rows(side)],
            heads_z.at[layer, 4 - step],
            hz_send.at[layer, step],
            hz_recv.at[layer, 4 - step],
            place(core, side, peer, yy),
        )

    def heads_last_copy(layer, number):
        x, c, y = number // 4, number // 2 % 2, number % 2
        return remote(
            heads_sum.at[layer, 1 - yy if y else yy],
            heads_all.at[layer, side, member],
            hf_send.at[layer, number],
            hf_recv.at[layer, number],
            place(1 - core if c else core, 1 - side if x else side, zz, 1 - yy if y else yy),
        )

    def heads_second(layer):
        heads_x_copy(layer).wait()
        heads_out[layer, :, :, half_rows(side), :] += heads_x[layer]
        for step in range(1, 4):
            heads_z_copy(layer, step).start()

    def heads_third(layer):
        for step in range(1, 4):
            heads_z_copy(layer, step).wait()
        total = heads_out[layer, zz, :, half_rows(side), :].astype(F32)
        for slot in range(1, 4):
            total = total + heads_z[layer, slot].astype(F32)
        heads_sum[layer] = total.astype(BF16)
        heads_all[layer, side, member] = heads_sum[layer, yy]
        for number in range(1, 8):
            heads_last_copy(layer, number).start()

    def heads_done(layer):
        for number in range(1, 8):
            heads_last_copy(layer, number).wait()

    def rows_in(part, route):
        first, room, count = SPANS[part, route]
        return pl.ds(first, count), pl.ds(room, count)

    def used(part, route):
        return SHARES[part][route] > 0

    def core_copy(part):
        layer, first, count = PARTS[part]
        rows = pl.ds(first, count)
        return remote(
            parts.at[layer, 1 - core, :, :, :, rows],
            core_in.at[:, :, :, rows],
            core_send.at[part],
            core_recv.at[part],
            core_peer,
        )

    def x_copy(part, route):
        layer = PARTS[part][0]
        rows, room = rows_in(part, route)
        ends = (x_send.at[part, route], x_recv.at[part, route], x_peer)
        mine = parts.at[layer, core, 1 - side]
        if route == 0:
            return remote(mine.at[:, :, rows], xa_in.at[:, :, room], *ends)
        if route == 1:
            return remote(mine.at[:, yy, rows], xb_in.at[:, room], *ends)
        return remote(mine.at[zz, :, rows], third_x.at[:, room], *ends)

    def y_copy(part, route):
        layer = PARTS[part][0]
        rows, room = rows_in(part, route)
        ends = (y_send.at[part, route], y_recv.at[part, route], y_peer)
        mine = parts.at[layer, core]
        if route == 0:
            return remote(mine.at[side, :, 1 - yy, rows], ya_in.at[:, room], *ends)
        if route == 1:
            return remote(mine.at[:, :, 1 - yy, rows], yb_in.at[:, :, room], *ends)
        return remote(mine.at[side, zz, 1 - yy, rows], third_y.at[room], *ends)

    def z_copy(part, route, step):
        layer = PARTS[part][0]
        rows, room = rows_in(part, route)
        peer = lax.rem(zz + step, 4)
        ends = (z_send.at[part, route, step], z_recv.at[part, route, 4 - step], place(core, side, peer, yy))
        if route == 2:
            return remote(parts.at[layer, core, :, peer, :, rows], third_z.at[4 - step, :, :, room], *ends)
        return remote(parts.at[layer, core, side, peer, yy, rows], z_in.at[layer, 4 - step, rows], *ends)

    def final_copy(part, which):
        layer, first, count = PARTS[part]
        block = final.at[layer, far_side if which == 2 else grp, pl.ds(first, count)]
        return remote(
            block,
            block,
            fin_send.at[part, which],
            fin_recv.at[part, which],
            x_peer if which == 0 else core_peer,
        )

    def core_done(part):
        layer, first, count = PARTS[part]
        rows = pl.ds(first, count)
        core_copy(part).wait()
        for across in (1 - side, side):
            parts[layer, core, across, :, :, rows, :] += core_in[across, :, :, rows, :]
            if used(part, 0) and across is not side:
                x_copy(part, 0).start()
        if used(part, 1):
            y_copy(part, 1).start()
        if used(part, 2):
            for step in range(1, 4):
                z_copy(part, 2, step).start()
        if layer == 1:
            freed = 0 if first < 320 else 1
            followers = [1 for other in PARTS if other[0] == 0 and (other[1] >= 320) == (freed == 1)]
            credit(core_free.at[freed], core_peer, len(followers))

    def first_x(part):
        if used(part, 0):
            layer = PARTS[part][0]
            rows, room = rows_in(part, 0)
            x_copy(part, 0).wait()
            for y in (1 - yy, yy):
                parts[layer, core, side, :, y, rows, :] += xa_in[:, y, room, :]
                if y is not yy:
                    y_copy(part, 0).start()

    def first_y(part):
        if used(part, 1):
            layer = PARTS[part][0]
            rows, room = rows_in(part, 1)
            y_copy(part, 1).wait()
            for across in (1 - side, side):
                parts[layer, core, across, :, yy, rows, :] += yb_in[across, :, room, :]
                if across is not side:
                    x_copy(part, 1).start()

    def first_z(part):
        if used(part, 2):
            layer = PARTS[part][0]
            rows, room = rows_in(part, 2)
            for step in range(1, 4):
                z_copy(part, 2, step).wait()
            for across in (1 - side, side):
                total = parts[layer, core, across, zz, :, rows, :].astype(F32)
                for slot in range(1, 4):
                    total = total + third_z[slot, across, :, room, :].astype(F32)
                parts[layer, core, across, zz, :, rows, :] = total.astype(BF16)
                if across is not side:
                    x_copy(part, 2).start()

    def second_x(part):
        if used(part, 0):
            layer = PARTS[part][0]
            rows, room = rows_in(part, 0)
            y_copy(part, 0).wait()
            parts[layer, core, side, :, yy, rows, :] += ya_in[:, room, :]
            for step in range(1, 4):
                z_copy(part, 0, step).start()

    def second_y(part):
        if used(part, 1):
            layer = PARTS[part][0]
            rows, room = rows_in(part, 1)
            x_copy(part, 1).wait()
            parts[layer, core, side, :, yy, rows, :] += xb_in[:, room, :]
            for step in range(1, 4):
                z_copy(part, 1, step).start()

    def second_z(part):
        if used(part, 2):
            layer = PARTS[part][0]
            rows, room = rows_in(part, 2)
            x_copy(part, 2).wait()
            for y in (1 - yy, yy):
                parts[layer, core, side, zz, y, rows, :] += third_x[y, room, :]
                if y is not yy:
                    y_copy(part, 2).start()

    def third_done(part):
        layer = PARTS[part][0]
        for route in range(3):
            if not used(part, route):
                continue
            rows, room = rows_in(part, route)
            if route == 2:
                y_copy(part, 2).wait()
                final[layer, grp, rows, :] = parts[layer, core, side, zz, yy, rows, :] + third_y[room, :]
            else:
                for step in range(1, 4):
                    z_copy(part, route, step).wait()
                total = parts[layer, core, side, zz, yy, rows, :].astype(F32)
                for slot in range(1, 4):
                    total = total + z_in[layer, slot, rows, :].astype(F32)
                final[layer, grp, rows, :] = total.astype(BF16)
        if PARTS[part][1] >= 320:
            for row in (320, 448):
                final[layer, grp, row : row + 128, :] = final[layer, grp, row : row + 128, :].T
        for which in range(2):
            final_copy(part, which).start()

    def final_pass(part):
        final_copy(part, 0).wait()
        final_copy(part, 2).start()

    def final_done(part):
        for which in range(1, 3):
            final_copy(part, which).wait()

    def small_copy(stage):
        peer = (core_peer, x_peer, y_peer)[stage]
        return remote(
            small_sum.at[stage], small_in.at[stage], small_send.at[stage], small_recv.at[stage], peer
        )

    def small_z_copy(step):
        return remote(
            small_z.at[zz],
            small_z.at[zz],
            small_send.at[2 + step],
            small_recv.at[2 + step],
            place(core, side, lax.rem(zz + step, 4), yy),
        )

    def small_start():
        small_sum[0] = small[...]
        small_copy(0).start()

    def small_next(stage):
        small_copy(stage).wait()
        total = small_sum[stage] + small_in[stage]
        if stage < 2:
            small_sum[stage + 1] = total
            small_copy(stage + 1).start()
        else:
            small_z[zz] = total
            for step in range(1, 4):
                small_z_copy(step).start()

    def small_done():
        for step in range(1, 4):
            small_z_copy(step).wait()
        small_sum[0] = (small_z[0] + small_z[1]) + (small_z[2] + small_z[3])
        small_final[:, 0:256] = small_sum[0, :, pl.ds(pl.multiple_of(blk * 256, 256), 256)]
        pair = small_sum[0, :, pl.ds(pl.multiple_of(FF + 128 * zz, 128), 128)]
        small_final[:, 256:384] = jnp.where(yy == 1, pltpu.roll(pair, DIM, 1), pair)
        small_final[:, 384:512] = small_sum[0, :, FF + WIDTH :]

    def halves(*phases, first=0):
        def both(step, carry):
            for phase in phases:
                phase(lax.rem(step + first, 2))
            return carry

        lax.fori_loop(0, 2, both, 0)

    def begin(half):
        move_arrived(0, half, tok_in)
        hidden[rows_of(half), :] = tok_in[half].astype(F32)

    def finish(half):
        back_out[0, half] = hidden[rows_of(half), :].astype(BF16)
        to_owner(3, half, back_out.at[0, half], out_in)

    def turn_round(layer, half):
        move_arrived(2, half, cot_in)
        rows = rows_of(half)
        grad[rows, :] = cot_in[half].astype(F32)
        dz[rows, :] = (alphas[layer, 1] * grad[rows, :]).astype(BF16)

    def hand_back(half):
        back_out[1, half] = grad[rows_of(half), :].astype(BF16)
        to_owner(4, half, back_out.at[1, half], grad_in)

    barrier = pltpu.get_barrier_semaphore()
    for step in range(1, 4):
        credit(barrier, place(core, side, lax.rem(zz + step, 4), yy))
    for step in range(4):
        credit(barrier, place(1 - core, side, lax.rem(zz + step, 4), yy))
    for peer in (
        x_peer,
        y_peer,
        place(1 - core, side, zz, 1 - yy),
        place(1 - core, 1 - side, zz, yy),
        place(core, 1 - side, zz, 1 - yy),
        place(1 - core, 1 - side, zz, 1 - yy),
    ):
        credit(barrier, peer)

    weight_copies = {}
    for layer in range(LAYERS):
        for number, (source, target) in enumerate(
            ((qkv_hbm, wqkv), (out_hbm, wout), (up_hbm, wup), (down_hbm, wdown))
        ):
            weight_copies[layer, number] = pltpu.make_async_copy(
                source.at[layer], target.at[layer], w_sem.at[layer, number]
            )
    bias_copies = [
        pltpu.make_async_copy(up_bias_hbm, up_bias, w_sem.at[2, 0]),
        pltpu.make_async_copy(down_bias_hbm, down_bias, w_sem.at[2, 1]),
    ]
    weight_copies[0, 0].start()
    pl.semaphore_wait(barrier, 13)
    upper = lax.div(zz, 2)
    for half in (1 - upper, upper):
        to_team(0, half, half_of(tokens, half), tok_in)
    for copy in (*list(weight_copies.values())[1:], *bias_copies):
        copy.start(priority=1)
    end_second = lax.div(seq_len[0, 0] + seq_len[0, 1], RUNS)
    flag_out[...] = jnp.full((8, 128), end_second.astype(F32), F32)
    for half in (1 - upper, upper):
        to_team(1, half, flag_out, flag_in)
    for head in range(OWN):
        other = slice(DIM * (1 - head), DIM * (1 - head) + DIM)
        for layer in range(LAYERS):
            rq[layer, head, other, :] = jnp.zeros((DIM, HALF * RUNS), BF16)
        ro[head, other, :] = jnp.zeros((DIM, HALF * RUNS), BF16)
    weight_copies[0, 0].wait()
    halves(begin, functools.partial(project, 0), first=upper)
    for half in (1 - upper, upper):
        to_team(2, half, half_of(cotangent, half), cot_in)

    move_arrived(1, 0, flag_in)
    move_arrived(1, 1, flag_in)
    border = jnp.concatenate([flag_in[0, 0:1, :]] * 2, axis=1) - (HALF * lax.div(zz, 2)).astype(F32)
    key_row = lax.broadcasted_iota(jnp.int32, (TILE, TILE), 0)
    query_col = lax.broadcasted_iota(jnp.int32, (TILE, TILE), 1)
    later = key_row > query_col
    key_sub = lax.rem(key_row, HALF).astype(F32) >= border
    query_sub = lax.rem(query_col, HALF).astype(F32) >= border
    apart = jnp.logical_xor(key_sub, query_sub)
    for tile in range(TILES - 1):
        bias[TILE * tile : TILE * tile + TILE, :] = jnp.where(apart, NEGATIVE, 0.0)
    bias[TILE * (TILES - 1) :, :] = jnp.where(jnp.logical_or(later, apart), NEGATIVE, 0.0)

    for copy in (*bias_copies, *(weight_copies[0, number] for number in range(1, 4))):
        copy.wait()
    attend(0, 0)
    attend(0, 1)
    hidden_start(0, 0)
    weight_copies[1, 0].wait()
    halves(functools.partial(feed, 0), functools.partial(project, 1))
    for number in range(1, 4):
        weight_copies[1, number].wait()
    attend(1, 0)
    attend(1, 1)
    hidden_pass(0, 0)
    hidden_start(1, 0)
    halves(functools.partial(feed, 1), finish)
    hidden_start(0, 1)
    hidden_start(1, 1)
    hidden_pass(1, 0)

    halves(functools.partial(turn_round, 1))
    make(1)
    feed_back(1)
    hidden_pass(0, 1)
    hidden_pass(1, 1)
    core_done(1)
    make(0)
    attend_back(1, 1)
    first_y(1)
    core_done(0)
    attend_back(1, 0)
    second_y(1)
    first_x(1)
    project_back(1, 1)
    heads_grads(1)
    first_z(1)
    project_back(1, 0)
    feed_back(0)
    small_start()
    second_x(1)
    make(2)
    first_x(0)
    heads_second(1)
    first_z(0)
    attend_back(0, 1)
    small_next(0)
    core_done(2)
    second_x(0)
    make(3)
    attend_back(0, 0)
    small_next(1)
    project_back(0, 1)
    hand_back(1)
    first_z(2)
    heads_grads(0)
    small_next(2)
    first_x(2)
    core_done(3)
    first_y(2)
    heads_second(0)
    small_done()
    first_z(3)
    second_x(2)
    first_x(3)
    second_z(2)
    second_z(0)
    heads_third(1)
    second_z(1)
    first_y(3)
    heads_third(0)
    second_y(2)
    second_x(3)
    second_z(3)
    third_done(0)
    third_done(2)
    second_y(3)
    project_back(0, 0)
    hand_back(0)
    heads_done(1)
    third_done(1)
    third_done(3)
    final_pass(0)
    final_pass(2)
    final_pass(1)
    final_pass(3)
    final_done(2)
    final_done(1)
    heads_done(0)
    final_done(0)
    final_done(3)
    for half in range(2):
        move_arrived(3, half, out_in)
        move_arrived(4, half, grad_in)

    for half in range(2):
        left(2, 0, half, head_out)
        left(3, 0, half, pack_out)
        to_team_left(0, half, half_of(tokens, half))
        to_team_left(1, half, flag_out)
        to_team_left(2, half, half_of(cotangent, half))
        to_owner_left(3, half, back_out.at[0, half])
        to_owner_left(4, half, back_out.at[1, half])


def results_kernel(
    final, heads, out_block, grad_block, small,
    output, input_grad, qkv_grad, out_grad, up_grad, up_bias_grad, down_grad, down_bias_grad, alpha_grad,
    out_flat, grad_wide, qkv_wide, out_wide, up_wide, down_wide, out_sem,
):
    ends = []

    def write(source, target):
        ends.append(pltpu.make_async_copy(source, target, out_sem.at[len(ends)]))
        ends[-1].start()

    up_bias_grad[...] = small[:, 0:256]
    down_bias_grad[...] = small[:, 256 : 256 + DIM]
    alpha_grad[...] = small[:, 384:386]
    for layer in range(LAYERS):
        for quarter in range(4):

            def block(first, count):
                return final[layer, quarter, first : first + count, :].astype(F32)

            def columns(step):
                return slice(WIDTH * step + 128 * quarter, WIDTH * step + 128 * quarter + 128)

            for step in range(4):
                up_wide[layer, :, columns(step)] = block(DIM * step, DIM)
            out_wide[layer, :, columns(0)] = block(256, DIM)
            down_wide[layer, :, columns(0)] = block(320, 256)
        write(up_wide.at[layer], up_grad.at[layer])
        write(out_wide.at[layer], out_grad.at[layer])
        write(down_wide.at[layer], down_grad.at[layer])
    for half in range(2):
        rows = slice(HALF * half, HALF * half + HALF)
        grad_wide[rows, :] = grad_block[half].astype(F32)
        out_flat[rows, :] = out_block[half]
    write(grad_wide, input_grad)
    write(out_flat, output)
    for layer in range(LAYERS):
        for side in range(2):
            for member in range(TEAM):
                for step in range(3):
                    at = WIDTH * step + 128 * member
                    qkv_wide[layer, 32 * side : 32 * side + 32, at : at + 128] = heads[
                        layer, side, member, :, 128 * step : 128 * step + 128
                    ].astype(F32)
        write(qkv_wide.at[layer], qkv_grad.at[layer])
    for end in ends:
        end.wait()


def fast_body(
    tokens, seq_len, qkv_weight, out_weight, up_weight, up_bias, down_weight, down_bias, alphas, cotangent
):
    whole = pl.BlockSpec(memory_space=pltpu.VMEM)
    scalar = pl.BlockSpec(memory_space=pltpu.SMEM)
    far = pl.BlockSpec(memory_space=pl.ANY)
    shape = jax.ShapeDtypeStruct
    rows = HALF * RUNS

    def vmem(*dims):
        return pltpu.VMEM(dims, BF16)

    def wide(*dims):
        return pltpu.VMEM(dims, F32)

    dma = pltpu.SemaphoreType.DMA
    final, heads, out_block, grad_block, small = pl.pallas_call(
        layers_kernel,
        out_shape=(
            vmem(LAYERS, 4, CHUNK, 128),
            vmem(LAYERS, 2, TEAM, DIM // 2, 3 * 128),
            vmem(2, HALF, WIDTH),
            vmem(2, HALF, WIDTH),
            wide(LAYERS, WIDTH),
        ),
        in_specs=[far, scalar, scalar, far, far, far, far, far, far, far],
        out_specs=(whole,) * 5,
        scratch_shapes=[
            vmem(LAYERS, WIDTH, 3 * WIDTH),
            vmem(LAYERS, WIDTH, WIDTH),
            vmem(LAYERS, WIDTH, FF),
            vmem(LAYERS, FF, WIDTH),
            wide(LAYERS, FF),
            wide(LAYERS, WIDTH),
            vmem(2, HALF, WIDTH),
            vmem(2, HALF, WIDTH),
            wide(8, 128),
            wide(2, 8, 128),
            vmem(2, 2, HALF, WIDTH),
            wide(2 * HALF, WIDTH),
            wide(2 * HALF, WIDTH),
            vmem(LAYERS, WIDTH, rows),
            vmem(LAYERS, WIDTH, 2 * HALF),
            vmem(LAYERS, 2 * HALF, WIDTH),
            vmem(LAYERS, 2 * HALF, FF),
            wide(LAYERS, 2 * HALF, WIDTH),
            wide(LAYERS, 2 * HALF, FF),
            wide(LAYERS, 2 * HALF, WIDTH),
            vmem(2 * HALF, WIDTH),
            vmem(2 * HALF, FF),
            vmem(2 * HALF, WIDTH),
            vmem(HALF, 3 * WIDTH),
            vmem(2, TEAM, 3, 128, 128),
            vmem(2, TEAM, OWN, DIM, 128),
            vmem(2, TEAM, 3, 128, 128),
            vmem(2, TEAM, OWN, DIM, 128),
            vmem(2, TEAM, OWN, DIM, 128),
            vmem(LAYERS, rows, 128),
            vmem(LAYERS, 128, rows),
            vmem(LAYERS, rows, 128),
            vmem(LAYERS, 128, rows),
            vmem(LAYERS, OWN, 128, rows),
            vmem(OWN, 128, rows),
            wide(LAYERS, OWN, DIM, rows),
            wide(LAYERS, OWN, 1, rows),
            wide(rows, 128),
            wide(rows, 128),
            wide(128, rows),
            wide(rows, TILE),
            vmem(LAYERS, 2, 2, 4, 2, CHUNK, 128),
            vmem(2, 4, 2, CHUNK, 128),
            vmem(4, 2, TOTALS[0], 128),
            vmem(4, TOTALS[1], 128),
            vmem(4, TOTALS[0], 128),
            vmem(2, 4, TOTALS[1], 128),
            vmem(LAYERS, 4, CHUNK, 128),
            vmem(4, 2, 2, TOTALS[2], 128),
            vmem(2, TOTALS[2], 128),
            vmem(TOTALS[2], 128),
            vmem(LAYERS, 4, 2, DIM, 3 * 128),
            vmem(LAYERS, 4, 2, DIM // 2, 3 * 128),
            vmem(LAYERS, 4, 2, DIM // 2, 3 * 128),
            vmem(LAYERS, 2, DIM // 2, 3 * 128),
            wide(LAYERS, SMALL),
            wide(3, LAYERS, SMALL),
            wide(4, LAYERS, SMALL),
            wide(3, LAYERS, SMALL),
            dma((LAYERS + 1, 4)),
            dma((5, 2)),
            dma((5, 2)),
            dma((5, LAYERS, 2)),
            dma((5, LAYERS, 2)),
            dma((len(PARTS),)),
            dma((len(PARTS),)),
            dma((len(PARTS), 3)),
            dma((len(PARTS), 3)),
            dma((len(PARTS), 3)),
            dma((len(PARTS), 3)),
            dma((len(PARTS), 3, 4)),
            dma((len(PARTS), 3, 4)),
            dma((len(PARTS), 3)),
            dma((len(PARTS), 3)),
            dma((LAYERS, 2, 3)),
            dma((LAYERS, 2, 3)),
            dma((LAYERS,)),
            dma((LAYERS,)),
            dma((LAYERS, 4)),
            dma((LAYERS, 4)),
            dma((LAYERS, 8)),
            dma((LAYERS, 8)),
            dma((6,)),
            dma((6,)),
            pltpu.SemaphoreType.REGULAR((2,)),
        ],
        compiler_params=pltpu.CompilerParams(
            collective_id=0, has_side_effects=True, vmem_limit_bytes=61 * 1024 * 1024
        ),
        name="layers",
    )(
        tokens, seq_len, alphas, up_bias, down_bias, cotangent,
        qkv_weight, out_weight, up_weight, down_weight,
    )
    return tuple(
        pl.pallas_call(
            results_kernel,
            out_shape=(
                shape((2 * HALF, WIDTH), BF16),
                shape((2 * HALF, WIDTH), F32),
                shape((LAYERS, DIM, 3 * WIDTH), F32),
                shape((LAYERS, DIM, WIDTH), F32),
                shape((LAYERS, DIM, FF), F32),
                shape((LAYERS, FF // RUNS), F32),
                shape((LAYERS, FF // RUNS, WIDTH), F32),
                shape((LAYERS, DIM), F32),
                shape((LAYERS, 2), F32),
            ),
            in_specs=[whole] * 5,
            out_specs=(far, far, far, far, far, whole, far, whole, whole),
            scratch_shapes=[
                vmem(2 * HALF, WIDTH),
                wide(2 * HALF, WIDTH),
                wide(LAYERS, DIM, 3 * WIDTH),
                wide(LAYERS, DIM, WIDTH),
                wide(LAYERS, DIM, FF),
                wide(LAYERS, FF // RUNS, WIDTH),
                dma((10,)),
            ],
            compiler_params=pltpu.CompilerParams(vmem_limit_bytes=24 * 1024 * 1024),
            name="results",
        )(final, heads, out_block, grad_block, small)
    )


def layout(seq_len, local_count, cycle_size):
    piece_rows = seq_len[0] // cycle_size
    end_rows = jnp.cumsum(piece_rows)
    start_rows = end_rows - piece_rows
    local_rows = jnp.arange(local_count, dtype=jnp.int32)
    segment = jnp.sum((local_rows[:, None] >= end_rows[None, :]).astype(jnp.int32), axis=1)
    picked = segment[:, None] == jnp.arange(seq_len.shape[1], dtype=jnp.int32)[None, :]
    offset = local_rows - jnp.sum(jnp.where(picked, start_rows[None, :], 0), axis=1)
    span_rows = jnp.sum(jnp.where(picked, piece_rows[None, :], 0), axis=1)
    return (segment, offset, span_rows)


def gelu_exact(values):
    return jax.nn.gelu(values, approximate=False)


def key_block(whole, geometry, block_index, head_count):
    query_seg, query_pos, seg_all, pos_all, block_rows, score_scale = geometry
    first_row = block_index * block_rows
    key_piece = lax.dynamic_slice_in_dim(whole, first_row, block_rows, 0)
    key_seg = lax.dynamic_slice_in_dim(seg_all, first_row, block_rows, 0)
    key_pos = lax.dynamic_slice_in_dim(pos_all, first_row, block_rows, 0)
    half_width = key_piece.shape[1] // 2
    keys_part = key_piece[:, :half_width].reshape(block_rows, head_count, -1)
    values_part = key_piece[:, half_width:].reshape(block_rows, head_count, -1)
    return (keys_part, values_part, key_seg, key_pos)


def block_scores(queries, keys_part, key_seg, key_pos, geometry):
    query_seg, query_pos, seg_all, pos_all, block_rows, score_scale = geometry
    scores = (
        jnp.einsum("qhd,khd->hqk", queries, keys_part, preferred_element_type=jnp.float32)
        * score_scale
    )
    allowed = (query_seg[:, None] == key_seg[None, :]) & (key_pos[None, :] <= query_pos[:, None])
    return (scores, allowed[None])


def attend(queries, whole, geometry):
    row_count, head_count, head_dim = queries.shape
    block_count = whole.shape[0] // geometry[4]

    def statistics(running, block_index):
        largest, totals = running
        keys_part, values_part, key_seg, key_pos = key_block(
            whole, geometry, block_index, head_count
        )
        scores, allowed = block_scores(queries, keys_part, key_seg, key_pos, geometry)
        newest = jnp.maximum(largest, jnp.max(jnp.where(allowed, scores, NEGATIVE), axis=2))
        weights = jnp.where(allowed, jnp.exp(scores - newest[:, :, None]), 0.0)
        totals = totals * jnp.exp(largest - newest) + jnp.sum(weights, axis=2)
        return ((newest, totals), None)

    initial = (
        jnp.full((head_count, row_count), NEGATIVE, jnp.float32),
        jnp.zeros((head_count, row_count), jnp.float32),
    )
    (largest, totals), unused = lax.scan(statistics, initial, jnp.arange(block_count))
    log_total = largest + jnp.log(totals)

    def weighted(output_sum, block_index):
        keys_part, values_part, key_seg, key_pos = key_block(
            whole, geometry, block_index, head_count
        )
        scores, allowed = block_scores(queries, keys_part, key_seg, key_pos, geometry)
        probs = jnp.where(allowed, jnp.exp(scores - log_total[:, :, None]), 0.0).astype(
            jnp.bfloat16
        )
        output_sum = output_sum + jnp.einsum(
            "hqk,khd->qhd", probs, values_part, preferred_element_type=jnp.float32
        )
        return (output_sum, None)

    output_sum, unused = lax.scan(
        weighted, jnp.zeros((row_count, head_count, head_dim), jnp.float32), jnp.arange(block_count)
    )
    return (output_sum, log_total)


def attend_back(queries, whole, log_total, delta_sum, grad_heads, geometry):
    row_count, head_count, head_dim = queries.shape
    block_rows = geometry[4]
    score_scale = geometry[5]
    block_count = whole.shape[0] // block_rows

    def gradients(query_grad, block_index):
        keys_part, values_part, key_seg, key_pos = key_block(
            whole, geometry, block_index, head_count
        )
        scores, allowed = block_scores(queries, keys_part, key_seg, key_pos, geometry)
        probs = jnp.where(allowed, jnp.exp(scores - log_total[:, :, None]), 0.0)
        grad_probs = jnp.einsum(
            "qhd,khd->hqk", grad_heads, values_part, preferred_element_type=jnp.float32
        )
        grad_scores = (probs * (grad_probs - delta_sum[:, :, None])).astype(jnp.bfloat16)
        query_grad = (
            query_grad
            + jnp.einsum("hqk,khd->qhd", grad_scores, keys_part, preferred_element_type=jnp.float32)
            * score_scale
        )
        key_grad = (
            jnp.einsum("hqk,qhd->khd", grad_scores, queries, preferred_element_type=jnp.float32)
            * score_scale
        )
        value_grad = jnp.einsum(
            "hqk,qhd->khd",
            probs.astype(jnp.bfloat16),
            grad_heads,
            preferred_element_type=jnp.float32,
        )
        joined = jnp.concatenate(
            [key_grad.reshape(block_rows, -1), value_grad.reshape(block_rows, -1)], axis=1
        )
        return (query_grad, joined)

    query_grad, stacked = lax.scan(
        gradients,
        jnp.zeros((row_count, head_count, head_dim), jnp.float32),
        jnp.arange(block_count),
    )
    return (query_grad, stacked.reshape(whole.shape[0], -1))


def layer_forward(hidden, layer_index, weights, geometry):
    qkv_weight, out_weight, up_weight, up_bias, down_weight, down_bias, alphas = weights
    row_count, model_width = hidden.shape
    projection = qkv_weight[layer_index]
    rounded = hidden.astype(jnp.bfloat16)
    queries = (
        jnp.dot(rounded, projection[:, :model_width], preferred_element_type=jnp.float32)
        .astype(jnp.bfloat16)
        .reshape(row_count, HEADS, -1)
    )
    key_value = jnp.dot(
        rounded, projection[:, model_width:], preferred_element_type=jnp.float32
    ).astype(jnp.bfloat16)
    whole = lax.all_gather(key_value, "blk", axis=0, tiled=True)
    heads_out, log_total = attend(queries, whole, geometry)
    heads_rounded = heads_out.reshape(row_count, model_width).astype(jnp.bfloat16)
    branch = jnp.dot(heads_rounded, out_weight[layer_index], preferred_element_type=jnp.float32)
    alpha_pair = alphas[layer_index]
    middle = hidden + alpha_pair[0] * branch
    entered = middle.astype(jnp.bfloat16)
    gate_pre = (
        jnp.dot(entered, up_weight[layer_index], preferred_element_type=jnp.float32)
        + up_bias[layer_index]
    )
    activated = gelu_exact(gate_pre).astype(jnp.bfloat16)
    second = (
        jnp.dot(activated, down_weight[layer_index], preferred_element_type=jnp.float32)
        + down_bias[layer_index]
    )
    result = middle + alpha_pair[1] * second
    saved = (
        rounded,
        queries,
        key_value,
        whole,
        heads_out,
        heads_rounded,
        log_total,
        branch,
        entered,
        gate_pre,
        activated,
        second,
    )
    return (result, saved)


def layer_backward(grad_hidden, saved, layer_index, weights, geometry):
    qkv_weight, out_weight, up_weight, up_bias, down_weight, down_bias, alphas = weights
    (
        rounded,
        queries,
        key_value,
        saved_whole,
        heads_out,
        heads_rounded,
        log_total,
        branch,
        entered,
        gate_pre,
        activated,
        second,
    ) = saved
    row_count = grad_hidden.shape[0]
    alpha_pair = alphas[layer_index]
    grad_second = (alpha_pair[1] * grad_hidden).astype(jnp.bfloat16)
    alpha_second = jnp.sum(grad_hidden * second)
    bias_down = jnp.sum(grad_second.astype(jnp.float32), axis=0)
    grad_down = jnp.einsum("tf,td->fd", activated, grad_second, preferred_element_type=jnp.float32)
    grad_act = jnp.einsum(
        "td,fd->tf", grad_second, down_weight[layer_index], preferred_element_type=jnp.float32
    )
    unused, gelu_pull = jax.vjp(gelu_exact, gate_pre)
    grad_gate = gelu_pull(grad_act)[0].astype(jnp.bfloat16)
    bias_up = jnp.sum(grad_gate.astype(jnp.float32), axis=0)
    grad_up = jnp.einsum("td,tf->df", entered, grad_gate, preferred_element_type=jnp.float32)
    grad_middle = grad_hidden + jnp.einsum(
        "tf,df->td", grad_gate, up_weight[layer_index], preferred_element_type=jnp.float32
    )
    grad_branch = (alpha_pair[0] * grad_middle).astype(jnp.bfloat16)
    alpha_first = jnp.sum(grad_middle * branch)
    grad_proj_out = jnp.einsum(
        "te,td->ed", heads_rounded, grad_branch, preferred_element_type=jnp.float32
    )
    grad_heads = (
        jnp.einsum(
            "td,ed->te", grad_branch, out_weight[layer_index], preferred_element_type=jnp.float32
        )
        .astype(jnp.bfloat16)
        .reshape(queries.shape)
    )
    delta_sum = jnp.sum(grad_heads.astype(jnp.float32) * heads_out, axis=2).T
    whole = lax.all_gather(key_value, "blk", axis=0, tiled=True)
    query_grad, key_terms = attend_back(queries, whole, log_total, delta_sum, grad_heads, geometry)
    key_grads = lax.psum_scatter(
        key_terms.astype(jnp.bfloat16), "blk", scatter_dimension=0, tiled=True
    )
    grad_proj = jnp.concatenate(
        [query_grad.reshape(row_count, -1).astype(jnp.bfloat16), key_grads], axis=1
    )
    grad_qkv = jnp.einsum("td,te->de", rounded, grad_proj, preferred_element_type=jnp.float32)
    grad_input = grad_middle + jnp.einsum(
        "te,de->td", grad_proj, qkv_weight[layer_index], preferred_element_type=jnp.float32
    )
    layer_grads = (
        grad_qkv,
        grad_proj_out,
        grad_up,
        bias_up,
        grad_down,
        bias_down,
        jnp.stack([alpha_first, alpha_second]),
    )
    return (grad_input, layer_grads)


def reduce_all(layer_results, cycle_size):
    stacked = [
        jnp.stack([layer_entry[member] for layer_entry in layer_results], axis=0)
        for member in range(6)
    ]
    alpha_tiles = jnp.stack(
        [jnp.tile(layer_entry[6], cycle_size) for layer_entry in layer_results], axis=0
    )
    shares = (
        lax.psum_scatter(
            stacked[0].astype(jnp.bfloat16), "blk", scatter_dimension=1, tiled=True
        ).astype(jnp.float32),
        lax.psum_scatter(
            stacked[1].astype(jnp.bfloat16), "blk", scatter_dimension=1, tiled=True
        ).astype(jnp.float32),
        lax.psum_scatter(
            stacked[2].astype(jnp.bfloat16), "blk", scatter_dimension=1, tiled=True
        ).astype(jnp.float32),
        lax.psum_scatter(
            stacked[3].astype(jnp.bfloat16), "blk", scatter_dimension=1, tiled=True
        ).astype(jnp.float32),
        lax.psum_scatter(
            stacked[4].astype(jnp.bfloat16), "blk", scatter_dimension=1, tiled=True
        ).astype(jnp.float32),
        lax.psum_scatter(
            stacked[5].astype(jnp.bfloat16), "blk", scatter_dimension=1, tiled=True
        ).astype(jnp.float32),
        lax.psum_scatter(
            alpha_tiles.astype(jnp.bfloat16), "blk", scatter_dimension=1, tiled=True
        ).astype(jnp.float32),
    )
    return (
        lax.psum(shares[0].astype(jnp.bfloat16), "grp").astype(jnp.float32),
        lax.psum(shares[1].astype(jnp.bfloat16), "grp").astype(jnp.float32),
        lax.psum(shares[2].astype(jnp.bfloat16), "grp").astype(jnp.float32),
        lax.psum(shares[3].astype(jnp.bfloat16), "grp").astype(jnp.float32),
        lax.psum(shares[4].astype(jnp.bfloat16), "grp").astype(jnp.float32),
        lax.psum(shares[5].astype(jnp.bfloat16), "grp").astype(jnp.float32),
        lax.psum(shares[6].astype(jnp.bfloat16), "grp").astype(jnp.float32),
    )


def body(
    tokens,
    seq_len,
    qkv_weight,
    out_weight,
    up_weight,
    up_bias,
    down_weight,
    down_bias,
    alphas,
    cotangent,
):
    row_count, model_width = tokens.shape
    cycle_size = lax.axis_size("blk")
    cycle_place = lax.axis_index("blk")
    head_dim = model_width // HEADS
    total_rows = cycle_size * row_count
    block_rows = min(max(row_count, 512), total_rows)
    segment, offset, span_rows = layout(seq_len, row_count, cycle_size)
    query_pos = cycle_place * span_rows + offset
    seg_all = jnp.tile(segment, cycle_size)
    pos_all = jnp.repeat(jnp.arange(cycle_size, dtype=jnp.int32), row_count) * jnp.tile(
        span_rows, cycle_size
    ) + jnp.tile(offset, cycle_size)
    geometry = (segment, query_pos, seg_all, pos_all, block_rows, head_dim ** (-0.5))
    weights = (qkv_weight, out_weight, up_weight, up_bias, down_weight, down_bias, alphas)
    hidden = tokens.astype(jnp.float32)
    saved_layers = []
    for layer_index in range(LAYERS):
        hidden, saved = layer_forward(hidden, layer_index, weights, geometry)
        saved_layers.append(saved)
    output = hidden.astype(jnp.bfloat16)
    grad_hidden = cotangent.astype(jnp.float32)
    layer_results = []
    for layer_index in reversed(range(LAYERS)):
        grad_hidden, layer_grads = layer_backward(
            grad_hidden, saved_layers[layer_index], layer_index, weights, geometry
        )
        layer_results.insert(0, layer_grads)
    finals = reduce_all(layer_results, cycle_size)
    return (
        output,
        grad_hidden,
        finals[0],
        finals[1],
        finals[2],
        finals[3],
        finals[4],
        finals[5],
        finals[6],
    )


def solution(mesh):
    placed = (
        P(("grp", "blk"), None),
        P("grp", None),
        P(),
        P(),
        P(),
        P(),
        P(),
        P(),
        P(),
        P(("grp", "blk"), None),
    )
    sizes = (mesh.shape["grp"], mesh.shape["blk"])
    return jax.shard_map(
        fast_body if sizes == (4, RUNS) else body,
        mesh=mesh,
        in_specs=placed,
        out_specs=(
            P(("grp", "blk"), None),
            P(("grp", "blk"), None),
            P(None, "blk", None),
            P(None, "blk", None),
            P(None, "blk", None),
            P(None, "blk"),
            P(None, "blk", None),
            P(None, "blk"),
            P(),
        ),
        check_vma=False,
    )
```

```python
import functools

import jax
import jax.numpy as jnp
from jax import lax
from jax.experimental import pallas as pl
from jax.experimental.pallas import tpu as pltpu
from jax.sharding import PartitionSpec as P

HEADS = 8
LAYERS = 2
NEGATIVE = -1e30
MESH = pl.DeviceIdType.MESH
F32 = jnp.float32
BF16 = jnp.bfloat16

HALF = 128
RUNS = 8
TEAM = 4
OWN = RUNS // TEAM
DIM = 64
WIDTH = 512
FF = 2048
CUT = 512
TILE = 256
TILES = HALF * RUNS // TILE
PACK = HALF + DIM
CHUNK = 576
SMALL = FF + WIDTH + 128
PARTS = ((1, 0, 320), (1, 320, 256), (0, 0, 320), (0, 320, 256))
SHARES = ((192, 0, 128), (160, 16, 80), (160, 112, 48), (128, 96, 32))


def spans():
    places, totals = {}, [0, 0, 0]
    for part, counts in enumerate(SHARES):
        first = PARTS[part][1]
        for route, count in enumerate(counts):
            places[part, route] = (first, totals[route], count)
            first += count
            totals[route] += count
    return places, totals


SPANS, TOTALS = spans()

SLOPE_AT = 0.28
TAIL = (
    0.11652077851573843,
    0.06749675579450809,
    0.2689101589486142,
    -0.23699347299932225,
    0.3898740127620002,
    -0.10580824228351815,
)


def nn(a, b):
    return lax.dot_general(a, b, (((1,), (0,)), ((), ())), preferred_element_type=F32)


def nt(a, b):
    return lax.dot_general(a, b, (((1,), (1,)), ((), ())), preferred_element_type=F32)


def beside(first, other):
    low = lax.broadcasted_iota(jnp.int32, first.shape, 1) < DIM
    return (
        jnp.where(low, first, pltpu.roll(other, DIM, 1)),
        jnp.where(low, pltpu.roll(first, DIM, 1), other),
    )


def layers_kernel(
    tokens, seq_len, alphas, up_bias_hbm, down_bias_hbm, cotangent, qkv_hbm, out_hbm, up_hbm, down_hbm,
    final, heads_all, out_in, grad_in, small_final,
    wqkv, wout, wup, wdown, up_bias, down_bias,
    tok_in, cot_in, flag_out, flag_in, back_out,
    hidden, grad, hid_all, attn_t, entered, act, branch, slope, second,
    dz, du, da, dqkv,
    pack_out, head_out, pack_in, o_in, do_in,
    kv, kv_t, rq, ro, o_t, lse, acc, dq_t, bias,
    parts, core_in, xa_in, xb_in, ya_in, yb_in, z_in, third_z, third_x, third_y,
    heads_out, heads_x, heads_z, heads_sum, small, small_in, small_z, small_sum,
    w_sem, move_send, move_recv, a2a_send, a2a_recv, core_send, core_recv, x_send, x_recv, y_send, y_recv,
    z_send, z_recv, fin_send, fin_recv, hid_send, hid_recv, hx_send, hx_recv, hz_send, hz_recv, hf_send, hf_recv,
    small_send, small_recv, core_free,
):
    grp = lax.axis_index("grp")
    blk = lax.axis_index("blk")
    core = lax.rem(grp, 2)
    side = lax.div(grp, 2)
    yy = lax.rem(blk, 2)
    zz = lax.div(blk, 2)
    member = 2 * core + yy
    far_side = 2 * (1 - side) + core

    def place(c, x, z, y):
        return (2 * x + c, 2 * z + y)

    core_peer = place(1 - core, side, zz, yy)
    x_peer = place(core, 1 - side, zz, yy)
    y_peer = place(core, side, zz, 1 - yy)

    def remote(source, target, send, recv, peer):
        return pltpu.make_async_remote_copy(
            src_ref=source,
            dst_ref=target,
            send_sem=send,
            recv_sem=recv,
            device_id=peer,
            device_id_type=MESH,
        )

    def credit(semaphore, peer, count=1):
        pl.semaphore_signal(semaphore, inc=count, device_id=peer, device_id_type=MESH)

    def moved(kind, slot, source, target, at, core_at, z_at):
        here = jnp.logical_and(core_at == core, z_at == zz)

        @pl.when(here)
        def _():
            pltpu.make_async_copy(source, target.at[at], move_recv.at[kind, at]).start()

        @pl.when(jnp.logical_not(here))
        def _():
            pltpu.make_async_remote_copy(
                src_ref=source,
                dst_ref=target.at[at],
                send_sem=move_send.at[kind, slot],
                recv_sem=move_recv.at[kind, at],
                device_id=place(core_at, side, z_at, yy),
                device_id_type=MESH,
            ).start()

    def move_left(kind, slot, source, core_at, z_at):
        here = jnp.logical_and(core_at == core, z_at == zz)

        @pl.when(jnp.logical_not(here))
        def _():
            pltpu.make_async_copy(source, source, move_send.at[kind, slot]).wait()

    def move_arrived(kind, at, target):
        pltpu.make_async_copy(target.at[at], target.at[at], move_recv.at[kind, at]).wait()

    def to_team(kind, half, source, target):
        moved(kind, half, source, target, lax.div(zz, 2), lax.rem(zz, 2), 2 * half + core)

    def to_team_left(kind, half, source):
        move_left(kind, half, source, lax.rem(zz, 2), 2 * half + core)

    def to_owner(kind, chunk, source, target):
        moved(kind, chunk, source, target, lax.div(zz, 2), lax.rem(zz, 2), core + 2 * chunk)

    def to_owner_left(kind, chunk, source):
        move_left(kind, chunk, source, lax.rem(zz, 2), core + 2 * chunk)

    def half_of(ref, half):
        return ref.at[pl.ds(pl.multiple_of(HALF * half, HALF), HALF)]

    def rows_of(half):
        return pl.ds(pl.multiple_of(half * HALF, HALF), HALF)

    def slot_of(other):
        return lax.rem(other + TEAM - member, TEAM)

    def exchange(kind, layer, half, outgoing, incoming, head=None):
        at = () if head is None else (head,)
        incoming[(half, 0, *at)] = outgoing[(half, member, *at)]
        for step in range(1, TEAM):
            peer = lax.rem(member + step, TEAM)
            remote(
                outgoing.at[(half, peer, *at)],
                incoming.at[(half, TEAM - step, *at)],
                a2a_send.at[kind, layer, half, head or 0],
                a2a_recv.at[kind, layer, half, head or 0],
                place(lax.div(peer, 2), side, zz, lax.rem(peer, 2)),
            ).start()

    def arrived(kind, layer, half, incoming, head=None):
        at = () if head is None else (head,)
        whole = incoming.at[(half, pl.ds(1, TEAM - 1), *at)]
        pltpu.make_async_copy(whole, whole, a2a_recv.at[kind, layer, half, head or 0]).wait()

    def left(kind, layer, half, outgoing):
        for head in range(OWN) if kind in (0, 3) else (None,):
            at = () if head is None else (head,)
            whole = outgoing.at[(half, pl.ds(1, TEAM - 1), *at)]
            pltpu.make_async_copy(whole, whole, a2a_send.at[kind, layer, half, head or 0]).wait()

    def tokens_of(chunk, other):
        return pl.ds(pl.multiple_of(HALF * (TEAM * chunk + other), HALF), HALF)

    def hidden_copy(layer, chunk, which):
        whose = 2 * core + 1 - yy if which == 2 else member
        block = hid_all.at[layer, :, tokens_of(chunk, whose)]
        return remote(
            block,
            block,
            hid_send.at[layer, chunk, which],
            hid_recv.at[layer, chunk, which],
            y_peer if which == 0 else core_peer,
        )

    def hidden_start(layer, chunk):
        for which in range(2):
            hidden_copy(layer, chunk, which).start()

    def hidden_pass(layer, chunk):
        hidden_copy(layer, chunk, 0).wait()
        hidden_copy(layer, chunk, 2).start()

    def hidden_done(layer, chunk):
        for which in range(1, 3):
            hidden_copy(layer, chunk, which).wait()

    def project(layer, half):
        rows = rows_of(half)
        rounded = hidden[rows, :].astype(BF16)
        if layer == 1:
            left(0, 0, half, pack_out)
        queries = (nn(rounded, wqkv[layer, :, 0:WIDTH]) * (DIM ** -0.5)).astype(BF16).T
        for head in range(RUNS):
            pack_out[half, head // 2, head % 2, HALF:, :] = queries[DIM * head : DIM * head + DIM, :]
        for step in range(2):
            at = WIDTH * (step + 1)
            keys_values = nn(rounded, wqkv[layer, :, at : at + WIDTH]).astype(BF16)
            for head in range(4):
                pack_out[half, 2 * step + head // 2, head % 2, 0:HALF, :] = keys_values[
                    :, 128 * head : 128 * head + 128
                ]
        for head in range(OWN):
            exchange(0, layer, half, pack_out, pack_in, head)
        hid_all[layer, :, tokens_of(half, member)] = rounded.T

    def attend(layer, chunk):
        if layer == 1:
            left(1, 0, chunk, head_out)

        def one_head(head, carry):
            arrived(0, layer, chunk, pack_in, head)
            for other in range(TEAM):
                slot = slot_of(other)
                start = HALF * (TEAM * chunk + other)
                span = slice(start, start + HALF)
                block = pack_in[chunk, slot, head, 0:HALF, :]
                kv[layer, head, span, :] = block
                kv_t[layer, head, :, span] = block.T
                rq[layer, head, 0:DIM, span] = pack_in[chunk, slot, head, HALF:, :]

            def scores_of(i):
                count = TILE * (i + 1)
                tile = rq[layer, head, :, TILE * i : TILE * i + TILE]
                return nn(kv[layer, head, 0:count, :], tile) + bias[TILE * TILES - count :, :]

            ahead = [scores_of(i) for i in (2 * chunk, 2 * chunk + 1)]
            for i in (2 * chunk, 2 * chunk + 1):
                columns = slice(TILE * i, TILE * i + TILE)
                count = TILE * (i + 1)
                scores = ahead[i - 2 * chunk]
                largest = jnp.max(scores, axis=0, keepdims=True)
                weight = jnp.exp(scores - largest)
                total = jnp.sum(weight, axis=0, keepdims=True)
                summed = nn(kv_t[layer, head, DIM:, 0:count], weight.astype(BF16))
                summed = summed / total
                o_t[layer, head, :, columns] = summed
                lse[layer, head, :, columns] = largest + jnp.log(total)
                rounded = summed.astype(BF16)
                for part in range(2):
                    head_out[chunk, 2 * (i - 2 * chunk) + part, head] = rounded[
                        :, HALF * part : HALF * part + HALF
                    ]
            return carry

        for head in range(OWN):
            one_head(head, 0)
        exchange(1, layer, chunk, head_out, o_in)

    def feed(layer, half):
        rows = rows_of(half)
        arrived(1, layer, half, o_in)
        for head in range(RUNS):
            attn_t[layer, DIM * head : DIM * head + DIM, rows] = o_in[half, slot_of(head // 2), head % 2]
        attn = attn_t[layer, :, rows].T
        grown = nn(attn, wout[layer])
        branch[layer, rows, :] = grown
        middle = hidden[rows, :] + alphas[layer, 0] * grown
        rounded = middle.astype(BF16)
        entered[layer, rows, :] = rounded
        total = jnp.zeros((HALF, WIDTH), F32)

        def gate_of(step):
            cut = slice(CUT * step, CUT * step + CUT)
            return nn(rounded, wup[layer, :, cut]) + up_bias[layer : layer + 1, cut]

        coming = gate_of(0)
        for step in range(FF // CUT):
            cut = slice(CUT * step, CUT * step + CUT)
            gate = coming
            if step + 1 < FF // CUT:
                coming = gate_of(step + 1)
            bell = jnp.exp(gate * gate * -0.5)
            near = pl.reciprocal(1.0 + SLOPE_AT * jnp.abs(gate), approx=True)
            tail = jnp.full_like(gate, TAIL[5])
            for factor in TAIL[4::-1]:
                tail = tail * near + factor
            tail = bell * (tail * near)
            risen = jnp.where(gate > 0.0, 1.0 - tail, tail)
            slope[layer, rows, cut] = risen + gate * bell * 0.3989422804014327
            active = (gate * risen).astype(BF16)
            act[layer, rows, cut] = active
            total = total + nn(active, wdown[layer, cut, :])
        total = total + down_bias[layer : layer + 1, :]
        second[layer, rows, :] = total
        hidden[rows, :] = middle + alphas[layer, 1] * total

    def total_of(values):
        return jnp.sum(jnp.sum(values, axis=0, keepdims=True), axis=1, keepdims=True)

    def feed_back(layer):
        start = grad[...]
        if layer == 0:
            dz[...] = (alphas[layer, 1] * start).astype(BF16)
        scaled = dz[...]
        alpha_second = total_of(start * second[layer])
        small[layer : layer + 1, FF : FF + WIDTH] = jnp.sum(scaled.astype(F32), axis=0, keepdims=True)
        middle = start
        coming = nt(scaled, wdown[layer, 0:CUT, :])
        for step in range(FF // CUT):
            cut = slice(CUT * step, CUT * step + CUT)
            raw = coming
            if step + 1 < FF // CUT:
                coming = nt(scaled, wdown[layer, CUT * (step + 1) : CUT * (step + 2), :])
            gate = (raw * slope[layer, :, cut]).astype(BF16)
            du[:, cut] = gate
            small[layer : layer + 1, cut] = jnp.sum(gate.astype(F32), axis=0, keepdims=True)
            middle = middle + nt(gate, wup[layer, :, cut])
        grad[...] = middle
        mixed = (alphas[layer, 0] * middle).astype(BF16)
        da[...] = mixed
        spread = nt(wout[layer], mixed).astype(BF16)
        for chunk in (1, 0):
            left(*((1, 1) if layer == 1 else (2, 1)), chunk, head_out)
            for head in range(RUNS):
                head_out[chunk, head // 2, head % 2] = spread[
                    DIM * head : DIM * head + DIM, HALF * chunk : HALF * chunk + HALF
                ]
            exchange(2, layer, chunk, head_out, do_in)
        alpha_first = total_of(middle * branch[layer])
        column = lax.broadcasted_iota(jnp.int32, (1, 128), 1)
        small[layer : layer + 1, FF + WIDTH :] = jnp.where(
            column == 0, alpha_first, jnp.where(column == 1, alpha_second, 0.0)
        )

    def attend_back(layer, chunk):
        arrived(2, layer, chunk, do_in)
        left(*((0, 1) if layer == 1 else (3, 1)), chunk, pack_out)

        def one_head(head, carry):
            for other in range(TEAM):
                start = HALF * (TEAM * chunk + other)
                ro[head, DIM:, start : start + HALF] = do_in[chunk, slot_of(other), head]
            for i in (2 * chunk, 2 * chunk + 1):
                columns = slice(TILE * i, TILE * i + TILE)
                query_tile = rq[layer, head, :, columns]
                grad_tile = ro[head, :, columns]
                log_total = lse[layer, head, :, columns]
                delta = jnp.sum(
                    ro[head, DIM:, columns].astype(F32) * o_t[layer, head, :, columns],
                    axis=0,
                    keepdims=True,
                )
                count = TILE * (i + 1)
                keys = kv[layer, head, 0:count, :]
                weight = jnp.exp(nn(keys, query_tile) + bias[TILE * TILES - count :, :] - log_total)
                scored = (weight * (nn(keys, grad_tile) - delta)).astype(BF16)
                term = nt(scored, query_tile) + nt(weight.astype(BF16), grad_tile)
                if chunk == 1 and i == 2:
                    acc[head, 0:count, :] = term
                elif chunk == 1:
                    acc[head, 0 : count - TILE, :] += term[0 : count - TILE, :]
                    acc[head, count - TILE : count, :] = term[count - TILE :, :]
                else:
                    acc[head, 0:count, :] += term
                query_grad = nn(kv_t[layer, head, 0:DIM, 0:count], scored)
                dq_t[head, :, columns] = query_grad * (DIM ** -0.5)
            for other in range(TEAM):
                start = HALF * (TEAM * chunk + other)
                span = slice(start, start + HALF)
                pack_out[chunk, other, head, 0:HALF, :] = acc[head, span, :].astype(BF16)
                pack_out[chunk, other, head, HALF:, :] = dq_t[head, :, span].astype(BF16)
            exchange(3, layer, chunk, pack_out, pack_in, head)
            return carry

        for head in range(OWN):
            one_head(head, 0)

    def project_back(layer, half):
        for head in range(OWN):
            arrived(3, layer, half, pack_in, head)
        turned = jnp.concatenate(
            [pack_in[half, slot_of(head // 2), head % 2, HALF:, :] for head in range(RUNS)], axis=0
        )
        dqkv[:, 0:WIDTH] = turned.T
        for head in range(RUNS):
            at = WIDTH + 128 * head
            dqkv[:, at : at + 128] = pack_in[half, slot_of(head // 2), head % 2, 0:HALF, :]
        rows = rows_of(half)
        grad[rows, :] = grad[rows, :] + nt(dqkv[...], wqkv[layer])

    def scatter_rows(layer, result, first_row):
        for run in range(RUNS):
            for quarter in range(4):
                parts[layer, quarter % 2, quarter // 2, run // 2, run % 2, first_row : first_row + DIM, :] = result[
                    DIM * run : DIM * run + DIM, 128 * quarter : 128 * quarter + 128
                ].astype(BF16)

    def make(part):
        layer, first, count = PARTS[part]
        if first < 256:
            turned = entered[layer].T
        for row in range(first, min(first + count, 256), DIM):
            step = row // DIM
            scatter_rows(layer, nn(turned, du[:, CUT * step : CUT * step + CUT]), row)
        if first <= 256 < first + count:
            scatter_rows(layer, nn(attn_t[layer], da[...]), 256)
        if first >= 320:
            turned = dz[...].T
            for step in range(FF // CUT):
                result = nn(turned, act[layer, :, CUT * step : CUT * step + CUT])
                for block in range(CUT // 128):
                    run, row = 2 * step + block // 2, 320 + 128 * (block % 2)
                    for quarter in range(4):
                        parts[layer, quarter % 2, quarter // 2, run // 2, run % 2, row : row + 128, :] = result[
                            128 * quarter : 128 * quarter + 128, 128 * block : 128 * block + 128
                        ].astype(BF16)
        if layer == 0:
            pl.semaphore_wait(core_free.at[0 if first < 320 else 1], 1)
        core_copy(part).start()

    def heads_grads(layer):
        for chunk in range(2):
            hidden_done(layer, chunk)
        blocks = [(run // TEAM, run % TEAM) for run in range(RUNS)]
        keys_values = jnp.concatenate(
            [
                jnp.concatenate([pack_out[chunk, other, head, 0:HALF, :] for chunk, other in blocks], axis=0)
                for head in range(OWN)
            ],
            axis=1,
        )
        queries = jnp.concatenate(
            [
                jnp.concatenate([pack_out[chunk, other, head, HALF:, :] for chunk, other in blocks], axis=1)
                for head in range(OWN)
            ],
            axis=0,
        )
        both = nn(hid_all[layer], keys_values)
        q_part = nt(hid_all[layer], queries)
        for number, values in enumerate((q_part, both[:, 0:128], both[:, 128:256])):
            for run in range(RUNS):
                heads_out[layer, run // 2, run % 2, :, 128 * number : 128 * number + 128] = values[
                    DIM * run : DIM * run + DIM, :
                ].astype(BF16)
        heads_x_copy(layer).start()

    def half_rows(which):
        return pl.ds(pl.multiple_of(32 * which, 32), 32)

    def heads_x_copy(layer):
        return remote(
            heads_out.at[layer, :, :, half_rows(1 - side)],
            heads_x.at[layer],
            hx_send.at[layer],
            hx_recv.at[layer],
            x_peer,
        )

    def heads_z_copy(layer, step):
        peer = lax.rem(zz + step, 4)
        return remote(
            heads_out.at[layer, peer, :, half_rows(side)],
            heads_z.at[layer, 4 - step],
            hz_send.at[layer, step],
            hz_recv.at[layer, 4 - step],
            place(core, side, peer, yy),
        )

    def heads_last_copy(layer, number):
        x, c, y = number // 4, number // 2 % 2, number % 2
        return remote(
            heads_sum.at[layer, 1 - yy if y else yy],
            heads_all.at[layer, side, member],
            hf_send.at[layer, number],
            hf_recv.at[layer, number],
            place(1 - core if c else core, 1 - side if x else side, zz, 1 - yy if y else yy),
        )

    def heads_second(layer):
        heads_x_copy(layer).wait()
        heads_out[layer, :, :, half_rows(side), :] += heads_x[layer]
        for step in range(1, 4):
            heads_z_copy(layer, step).start()

    def heads_third(layer):
        for step in range(1, 4):
            heads_z_copy(layer, step).wait()
        total = heads_out[layer, zz, :, half_rows(side), :].astype(F32)
        for slot in range(1, 4):
            total = total + heads_z[layer, slot].astype(F32)
        heads_sum[layer] = total.astype(BF16)
        heads_all[layer, side, member] = heads_sum[layer, yy]
        for number in range(1, 8):
            heads_last_copy(layer, number).start()

    def heads_done(layer):
        for number in range(1, 8):
            heads_last_copy(layer, number).wait()

    def rows_in(part, route):
        first, room, count = SPANS[part, route]
        return pl.ds(first, count), pl.ds(room, count)

    def used(part, route):
        return SHARES[part][route] > 0

    def core_copy(part):
        layer, first, count = PARTS[part]
        rows = pl.ds(first, count)
        return remote(
            parts.at[layer, 1 - core, :, :, :, rows],
            core_in.at[:, :, :, rows],
            core_send.at[part],
            core_recv.at[part],
            core_peer,
        )

    def x_copy(part, route):
        layer = PARTS[part][0]
        rows, room = rows_in(part, route)
        ends = (x_send.at[part, route], x_recv.at[part, route], x_peer)
        mine = parts.at[layer, core, 1 - side]
        if route == 0:
            return remote(mine.at[:, :, rows], xa_in.at[:, :, room], *ends)
        if route == 1:
            return remote(mine.at[:, yy, rows], xb_in.at[:, room], *ends)
        return remote(mine.at[zz, :, rows], third_x.at[:, room], *ends)

    def y_copy(part, route):
        layer = PARTS[part][0]
        rows, room = rows_in(part, route)
        ends = (y_send.at[part, route], y_recv.at[part, route], y_peer)
        mine = parts.at[layer, core]
        if route == 0:
            return remote(mine.at[side, :, 1 - yy, rows], ya_in.at[:, room], *ends)
        if route == 1:
            return remote(mine.at[:, :, 1 - yy, rows], yb_in.at[:, :, room], *ends)
        return remote(mine.at[side, zz, 1 - yy, rows], third_y.at[room], *ends)

    def z_copy(part, route, step):
        layer = PARTS[part][0]
        rows, room = rows_in(part, route)
        peer = lax.rem(zz + step, 4)
        ends = (z_send.at[part, route, step], z_recv.at[part, route, 4 - step], place(core, side, peer, yy))
        if route == 2:
            return remote(parts.at[layer, core, :, peer, :, rows], third_z.at[4 - step, :, :, room], *ends)
        return remote(parts.at[layer, core, side, peer, yy, rows], z_in.at[layer, 4 - step, rows], *ends)

    def final_copy(part, which):
        layer, first, count = PARTS[part]
        block = final.at[layer, far_side if which == 2 else grp, pl.ds(first, count)]
        return remote(
            block,
            block,
            fin_send.at[part, which],
            fin_recv.at[part, which],
            x_peer if which == 0 else core_peer,
        )

    def core_done(part):
        layer, first, count = PARTS[part]
        rows = pl.ds(first, count)
        core_copy(part).wait()
        for across in (1 - side, side):
            parts[layer, core, across, :, :, rows, :] += core_in[across, :, :, rows, :]
            if used(part, 0) and across is not side:
                x_copy(part, 0).start()
        if used(part, 1):
            y_copy(part, 1).start()
        if used(part, 2):
            for step in range(1, 4):
                z_copy(part, 2, step).start()
        if layer == 1:
            freed = 0 if first < 320 else 1
            followers = [1 for other in PARTS if other[0] == 0 and (other[1] >= 320) == (freed == 1)]
            credit(core_free.at[freed], core_peer, len(followers))

    def first_x(part):
        if used(part, 0):
            layer = PARTS[part][0]
            rows, room = rows_in(part, 0)
            x_copy(part, 0).wait()
            for y in (1 - yy, yy):
                parts[layer, core, side, :, y, rows, :] += xa_in[:, y, room, :]
                if y is not yy:
                    y_copy(part, 0).start()

    def first_y(part):
        if used(part, 1):
            layer = PARTS[part][0]
            rows, room = rows_in(part, 1)
            y_copy(part, 1).wait()
            for across in (1 - side, side):
                parts[layer, core, across, :, yy, rows, :] += yb_in[across, :, room, :]
                if across is not side:
                    x_copy(part, 1).start()

    def first_z(part):
        if used(part, 2):
            layer = PARTS[part][0]
            rows, room = rows_in(part, 2)
            for step in range(1, 4):
                z_copy(part, 2, step).wait()
            for across in (1 - side, side):
                total = parts[layer, core, across, zz, :, rows, :].astype(F32)
                for slot in range(1, 4):
                    total = total + third_z[slot, across, :, room, :].astype(F32)
                parts[layer, core, across, zz, :, rows, :] = total.astype(BF16)
                if across is not side:
                    x_copy(part, 2).start()

    def second_x(part):
        if used(part, 0):
            layer = PARTS[part][0]
            rows, room = rows_in(part, 0)
            y_copy(part, 0).wait()
            parts[layer, core, side, :, yy, rows, :] += ya_in[:, room, :]
            for step in range(1, 4):
                z_copy(part, 0, step).start()

    def second_y(part):
        if used(part, 1):
            layer = PARTS[part][0]
            rows, room = rows_in(part, 1)
            x_copy(part, 1).wait()
            parts[layer, core, side, :, yy, rows, :] += xb_in[:, room, :]
            for step in range(1, 4):
                z_copy(part, 1, step).start()

    def second_z(part):
        if used(part, 2):
            layer = PARTS[part][0]
            rows, room = rows_in(part, 2)
            x_copy(part, 2).wait()
            for y in (1 - yy, yy):
                parts[layer, core, side, zz, y, rows, :] += third_x[y, room, :]
                if y is not yy:
                    y_copy(part, 2).start()

    def third_done(part):
        layer = PARTS[part][0]
        for route in range(3):
            if not used(part, route):
                continue
            rows, room = rows_in(part, route)
            if route == 2:
                y_copy(part, 2).wait()
                final[layer, grp, rows, :] = parts[layer, core, side, zz, yy, rows, :] + third_y[room, :]
            else:
                for step in range(1, 4):
                    z_copy(part, route, step).wait()
                total = parts[layer, core, side, zz, yy, rows, :].astype(F32)
                for slot in range(1, 4):
                    total = total + z_in[layer, slot, rows, :].astype(F32)
                final[layer, grp, rows, :] = total.astype(BF16)
        if PARTS[part][1] >= 320:
            for row in (320, 448):
                final[layer, grp, row : row + 128, :] = final[layer, grp, row : row + 128, :].T
        for which in range(2):
            final_copy(part, which).start()

    def final_pass(part):
        final_copy(part, 0).wait()
        final_copy(part, 2).start()

    def final_done(part):
        for which in range(1, 3):
            final_copy(part, which).wait()

    def small_copy(stage):
        peer = (core_peer, x_peer, y_peer)[stage]
        return remote(
            small_sum.at[stage], small_in.at[stage], small_send.at[stage], small_recv.at[stage], peer
        )

    def small_z_copy(step):
        return remote(
            small_z.at[zz],
            small_z.at[zz],
            small_send.at[2 + step],
            small_recv.at[2 + step],
            place(core, side, lax.rem(zz + step, 4), yy),
        )

    def small_start():
        small_sum[0] = small[...]
        small_copy(0).start()

    def small_next(stage):
        small_copy(stage).wait()
        total = small_sum[stage] + small_in[stage]
        if stage < 2:
            small_sum[stage + 1] = total
            small_copy(stage + 1).start()
        else:
            small_z[zz] = total
            for step in range(1, 4):
                small_z_copy(step).start()

    def small_done():
        for step in range(1, 4):
            small_z_copy(step).wait()
        small_sum[0] = (small_z[0] + small_z[1]) + (small_z[2] + small_z[3])
        small_final[:, 0:256] = small_sum[0, :, pl.ds(pl.multiple_of(blk * 256, 256), 256)]
        pair = small_sum[0, :, pl.ds(pl.multiple_of(FF + 128 * zz, 128), 128)]
        small_final[:, 256:384] = jnp.where(yy == 1, pltpu.roll(pair, DIM, 1), pair)
        small_final[:, 384:512] = small_sum[0, :, FF + WIDTH :]

    def halves(*phases, first=0):
        def both(step, carry):
            for phase in phases:
                phase(lax.rem(step + first, 2))
            return carry

        lax.fori_loop(0, 2, both, 0)

    def begin(half):
        move_arrived(0, half, tok_in)
        hidden[rows_of(half), :] = tok_in[half].astype(F32)

    def finish(half):
        back_out[0, half] = hidden[rows_of(half), :].astype(BF16)
        to_owner(3, half, back_out.at[0, half], out_in)

    def turn_round(layer, half):
        move_arrived(2, half, cot_in)
        rows = rows_of(half)
        grad[rows, :] = cot_in[half].astype(F32)
        dz[rows, :] = (alphas[layer, 1] * grad[rows, :]).astype(BF16)

    def hand_back(half):
        back_out[1, half] = grad[rows_of(half), :].astype(BF16)
        to_owner(4, half, back_out.at[1, half], grad_in)

    barrier = pltpu.get_barrier_semaphore()
    for step in range(1, 4):
        credit(barrier, place(core, side, lax.rem(zz + step, 4), yy))
    for step in range(4):
        credit(barrier, place(1 - core, side, lax.rem(zz + step, 4), yy))
    for peer in (
        x_peer,
        y_peer,
        place(1 - core, side, zz, 1 - yy),
        place(1 - core, 1 - side, zz, yy),
        place(core, 1 - side, zz, 1 - yy),
        place(1 - core, 1 - side, zz, 1 - yy),
    ):
        credit(barrier, peer)

    weight_copies = {}
    for layer in range(LAYERS):
        for number, (source, target) in enumerate(
            ((qkv_hbm, wqkv), (out_hbm, wout), (up_hbm, wup), (down_hbm, wdown))
        ):
            weight_copies[layer, number] = pltpu.make_async_copy(
                source.at[layer], target.at[layer], w_sem.at[layer, number]
            )
    bias_copies = [
        pltpu.make_async_copy(up_bias_hbm, up_bias, w_sem.at[2, 0]),
        pltpu.make_async_copy(down_bias_hbm, down_bias, w_sem.at[2, 1]),
    ]
    weight_copies[0, 0].start()
    pl.semaphore_wait(barrier, 13)
    upper = lax.div(zz, 2)
    for half in (1 - upper, upper):
        to_team(0, half, half_of(tokens, half), tok_in)
    for layer, number in ((1, 0), (0, 1), (0, 2), (0, 3), (1, 1), (1, 2), (1, 3)):
        weight_copies[layer, number].start(priority=1)
    for copy in bias_copies:
        copy.start(priority=1)
    end_second = lax.div(seq_len[0, 0] + seq_len[0, 1], RUNS)
    flag_out[...] = jnp.full((8, 128), end_second.astype(F32), F32)
    for half in (1 - upper, upper):
        to_team(1, half, flag_out, flag_in)
    for layer in range(LAYERS):
        for head in range(OWN):
            rq[layer, head, DIM:, :] = jnp.zeros((DIM, HALF * RUNS), BF16)
    for head in range(OWN):
        ro[head, 0:DIM, :] = jnp.zeros((DIM, HALF * RUNS), BF16)
    for layer in range(LAYERS):
        weight_copies[layer, 0].wait()
        pairs = [
            beside(
                wqkv[layer, :, WIDTH + 128 * pair : WIDTH + 128 * pair + 128].astype(F32),
                wqkv[layer, :, 2 * WIDTH + 128 * pair : 2 * WIDTH + 128 * pair + 128].astype(F32),
            )
            for pair in range(TEAM)
        ]
        for head in range(RUNS):
            at = WIDTH + 128 * head
            wqkv[layer, :, at : at + 128] = pairs[head // 2][head % 2].astype(BF16)
    halves(begin, functools.partial(project, 0), first=upper)
    for half in (1 - upper, upper):
        to_team(2, half, half_of(cotangent, half), cot_in)

    move_arrived(1, 0, flag_in)
    move_arrived(1, 1, flag_in)
    border = jnp.concatenate([flag_in[0, 0:1, :]] * 2, axis=1) - (HALF * lax.div(zz, 2)).astype(F32)
    key_row = lax.broadcasted_iota(jnp.int32, (TILE, TILE), 0)
    query_col = lax.broadcasted_iota(jnp.int32, (TILE, TILE), 1)
    later = key_row > query_col
    key_sub = lax.rem(key_row, HALF).astype(F32) >= border
    query_sub = lax.rem(query_col, HALF).astype(F32) >= border
    apart = jnp.logical_xor(key_sub, query_sub)
    for tile in range(TILES - 1):
        bias[TILE * tile : TILE * tile + TILE, :] = jnp.where(apart, NEGATIVE, 0.0)
    bias[TILE * (TILES - 1) :, :] = jnp.where(jnp.logical_or(later, apart), NEGATIVE, 0.0)

    for copy in (*bias_copies, *(weight_copies[0, number] for number in range(1, 4))):
        copy.wait()
    attend(0, 0)
    attend(0, 1)
    hidden_start(0, 0)
    halves(functools.partial(feed, 0), functools.partial(project, 1))
    for number in range(1, 4):
        weight_copies[1, number].wait()
    attend(1, 0)
    attend(1, 1)
    hidden_pass(0, 0)
    hidden_start(1, 0)
    halves(functools.partial(feed, 1), finish)
    hidden_start(0, 1)
    hidden_start(1, 1)
    hidden_pass(1, 0)

    halves(functools.partial(turn_round, 1))
    make(1)
    feed_back(1)
    hidden_pass(0, 1)
    hidden_pass(1, 1)
    core_done(1)
    make(0)
    attend_back(1, 1)
    first_y(1)
    core_done(0)
    attend_back(1, 0)
    second_y(1)
    first_x(1)
    project_back(1, 1)
    heads_grads(1)
    first_z(1)
    project_back(1, 0)
    feed_back(0)
    small_start()
    second_x(1)
    make(2)
    first_x(0)
    heads_second(1)
    first_z(0)
    attend_back(0, 1)
    small_next(0)
    core_done(2)
    second_x(0)
    make(3)
    attend_back(0, 0)
    small_next(1)
    project_back(0, 1)
    hand_back(1)
    first_z(2)
    heads_grads(0)
    small_next(2)
    first_x(2)
    core_done(3)
    first_y(2)
    heads_second(0)
    small_done()
    first_z(3)
    second_x(2)
    first_x(3)
    second_z(2)
    second_z(0)
    heads_third(1)
    second_z(1)
    first_y(3)
    heads_third(0)
    second_y(2)
    second_x(3)
    second_z(3)
    third_done(0)
    third_done(2)
    second_y(3)
    project_back(0, 0)
    hand_back(0)
    heads_done(1)
    third_done(1)
    third_done(3)
    final_pass(0)
    final_pass(2)
    final_pass(1)
    final_pass(3)
    final_done(2)
    final_done(1)
    heads_done(0)
    final_done(0)
    final_done(3)
    for half in range(2):
        move_arrived(3, half, out_in)
        move_arrived(4, half, grad_in)

    for half in range(2):
        left(2, 0, half, head_out)
        left(3, 0, half, pack_out)
        to_team_left(0, half, half_of(tokens, half))
        to_team_left(1, half, flag_out)
        to_team_left(2, half, half_of(cotangent, half))
        to_owner_left(3, half, back_out.at[0, half])
        to_owner_left(4, half, back_out.at[1, half])


def results_kernel(
    final, heads, out_block, grad_block, small,
    output, input_grad, qkv_grad, out_grad, up_grad, up_bias_grad, down_grad, down_bias_grad, alpha_grad,
    out_flat, grad_wide, qkv_wide, out_wide, up_wide, down_wide, out_sem,
):
    ends = []

    def write(source, target):
        ends.append(pltpu.make_async_copy(source, target, out_sem.at[len(ends)]))
        ends[-1].start()

    up_bias_grad[...] = small[:, 0:256]
    down_bias_grad[...] = small[:, 256 : 256 + DIM]
    alpha_grad[...] = small[:, 384:386]
    for layer in range(LAYERS):
        for quarter in range(4):

            def block(first, count):
                return final[layer, quarter, first : first + count, :].astype(F32)

            def columns(step):
                return slice(WIDTH * step + 128 * quarter, WIDTH * step + 128 * quarter + 128)

            for step in range(4):
                up_wide[layer, :, columns(step)] = block(DIM * step, DIM)
            out_wide[layer, :, columns(0)] = block(256, DIM)
            down_wide[layer, :, columns(0)] = block(320, 256)
        write(up_wide.at[layer], up_grad.at[layer])
        write(out_wide.at[layer], out_grad.at[layer])
        write(down_wide.at[layer], down_grad.at[layer])
    for half in range(2):
        rows = slice(HALF * half, HALF * half + HALF)
        grad_wide[rows, :] = grad_block[half].astype(F32)
        out_flat[rows, :] = out_block[half]
    write(grad_wide, input_grad)
    write(out_flat, output)
    for layer in range(LAYERS):
        for side in range(2):
            for member in range(TEAM):
                block = heads[layer, side, member].astype(F32)
                columns = (block[:, 0:128], *beside(block[:, 128:256], block[:, 256:384]))
                for step in range(3):
                    at = WIDTH * step + 128 * member
                    qkv_wide[layer, 32 * side : 32 * side + 32, at : at + 128] = columns[step]
        write(qkv_wide.at[layer], qkv_grad.at[layer])
    for end in ends:
        end.wait()


def fast_body(
    tokens, seq_len, qkv_weight, out_weight, up_weight, up_bias, down_weight, down_bias, alphas, cotangent
):
    whole = pl.BlockSpec(memory_space=pltpu.VMEM)
    scalar = pl.BlockSpec(memory_space=pltpu.SMEM)
    far = pl.BlockSpec(memory_space=pl.ANY)
    shape = jax.ShapeDtypeStruct
    rows = HALF * RUNS

    def vmem(*dims):
        return pltpu.VMEM(dims, BF16)

    def wide(*dims):
        return pltpu.VMEM(dims, F32)

    dma = pltpu.SemaphoreType.DMA
    final, heads, out_block, grad_block, small = pl.pallas_call(
        layers_kernel,
        out_shape=(
            vmem(LAYERS, 4, CHUNK, 128),
            vmem(LAYERS, 2, TEAM, DIM // 2, 3 * 128),
            vmem(2, HALF, WIDTH),
            vmem(2, HALF, WIDTH),
            wide(LAYERS, WIDTH),
        ),
        in_specs=[far, scalar, scalar, far, far, far, far, far, far, far],
        out_specs=(whole,) * 5,
        scratch_shapes=[
            vmem(LAYERS, WIDTH, 3 * WIDTH),
            vmem(LAYERS, WIDTH, WIDTH),
            vmem(LAYERS, WIDTH, FF),
            vmem(LAYERS, FF, WIDTH),
            wide(LAYERS, FF),
            wide(LAYERS, WIDTH),
            vmem(2, HALF, WIDTH),
            vmem(2, HALF, WIDTH),
            wide(8, 128),
            wide(2, 8, 128),
            vmem(2, 2, HALF, WIDTH),
            wide(2 * HALF, WIDTH),
            wide(2 * HALF, WIDTH),
            vmem(LAYERS, WIDTH, rows),
            vmem(LAYERS, WIDTH, 2 * HALF),
            vmem(LAYERS, 2 * HALF, WIDTH),
            vmem(LAYERS, 2 * HALF, FF),
            wide(LAYERS, 2 * HALF, WIDTH),
            wide(LAYERS, 2 * HALF, FF),
            wide(LAYERS, 2 * HALF, WIDTH),
            vmem(2 * HALF, WIDTH),
            vmem(2 * HALF, FF),
            vmem(2 * HALF, WIDTH),
            vmem(HALF, 3 * WIDTH),
            vmem(2, TEAM, OWN, PACK, 128),
            vmem(2, TEAM, OWN, DIM, 128),
            vmem(2, TEAM, OWN, PACK, 128),
            vmem(2, TEAM, OWN, DIM, 128),
            vmem(2, TEAM, OWN, DIM, 128),
            vmem(LAYERS, OWN, rows, 128),
            vmem(LAYERS, OWN, 128, rows),
            vmem(LAYERS, OWN, 128, rows),
            vmem(OWN, 128, rows),
            wide(LAYERS, OWN, DIM, rows),
            wide(LAYERS, OWN, 1, rows),
            wide(OWN, rows, 128),
            wide(OWN, DIM, rows),
            wide(rows, TILE),
            vmem(LAYERS, 2, 2, 4, 2, CHUNK, 128),
            vmem(2, 4, 2, CHUNK, 128),
            vmem(4, 2, TOTALS[0], 128),
            vmem(4, TOTALS[1], 128),
            vmem(4, TOTALS[0], 128),
            vmem(2, 4, TOTALS[1], 128),
            vmem(LAYERS, 4, CHUNK, 128),
            vmem(4, 2, 2, TOTALS[2], 128),
            vmem(2, TOTALS[2], 128),
            vmem(TOTALS[2], 128),
            vmem(LAYERS, 4, 2, DIM, 3 * 128),
            vmem(LAYERS, 4, 2, DIM // 2, 3 * 128),
            vmem(LAYERS, 4, 2, DIM // 2, 3 * 128),
            vmem(LAYERS, 2, DIM // 2, 3 * 128),
            wide(LAYERS, SMALL),
            wide(3, LAYERS, SMALL),
            wide(4, LAYERS, SMALL),
            wide(3, LAYERS, SMALL),
            dma((LAYERS + 1, 4)),
            dma((5, 2)),
            dma((5, 2)),
            dma((4, LAYERS, 2, OWN)),
            dma((4, LAYERS, 2, OWN)),
            dma((len(PARTS),)),
            dma((len(PARTS),)),
            dma((len(PARTS), 3)),
            dma((len(PARTS), 3)),
            dma((len(PARTS), 3)),
            dma((len(PARTS), 3)),
            dma((len(PARTS), 3, 4)),
            dma((len(PARTS), 3, 4)),
            dma((len(PARTS), 3)),
            dma((len(PARTS), 3)),
            dma((LAYERS, 2, 3)),
            dma((LAYERS, 2, 3)),
            dma((LAYERS,)),
            dma((LAYERS,)),
            dma((LAYERS, 4)),
            dma((LAYERS, 4)),
            dma((LAYERS, 8)),
            dma((LAYERS, 8)),
            dma((6,)),
            dma((6,)),
            pltpu.SemaphoreType.REGULAR((2,)),
        ],
        compiler_params=pltpu.CompilerParams(
            collective_id=0, has_side_effects=True, vmem_limit_bytes=61 * 1024 * 1024
        ),
        name="layers",
    )(
        tokens, seq_len, alphas, up_bias, down_bias, cotangent,
        qkv_weight, out_weight, up_weight, down_weight,
    )
    return tuple(
        pl.pallas_call(
            results_kernel,
            out_shape=(
                shape((2 * HALF, WIDTH), BF16),
                shape((2 * HALF, WIDTH), F32),
                shape((LAYERS, DIM, 3 * WIDTH), F32),
                shape((LAYERS, DIM, WIDTH), F32),
                shape((LAYERS, DIM, FF), F32),
                shape((LAYERS, FF // RUNS), F32),
                shape((LAYERS, FF // RUNS, WIDTH), F32),
                shape((LAYERS, DIM), F32),
                shape((LAYERS, 2), F32),
            ),
            in_specs=[whole] * 5,
            out_specs=(far, far, far, far, far, whole, far, whole, whole),
            scratch_shapes=[
                vmem(2 * HALF, WIDTH),
                wide(2 * HALF, WIDTH),
                wide(LAYERS, DIM, 3 * WIDTH),
                wide(LAYERS, DIM, WIDTH),
                wide(LAYERS, DIM, FF),
                wide(LAYERS, FF // RUNS, WIDTH),
                dma((10,)),
            ],
            compiler_params=pltpu.CompilerParams(vmem_limit_bytes=24 * 1024 * 1024),
            name="results",
        )(final, heads, out_block, grad_block, small)
    )


def layout(seq_len, local_count, cycle_size):
    piece_rows = seq_len[0] // cycle_size
    end_rows = jnp.cumsum(piece_rows)
    start_rows = end_rows - piece_rows
    local_rows = jnp.arange(local_count, dtype=jnp.int32)
    segment = jnp.sum((local_rows[:, None] >= end_rows[None, :]).astype(jnp.int32), axis=1)
    picked = segment[:, None] == jnp.arange(seq_len.shape[1], dtype=jnp.int32)[None, :]
    offset = local_rows - jnp.sum(jnp.where(picked, start_rows[None, :], 0), axis=1)
    span_rows = jnp.sum(jnp.where(picked, piece_rows[None, :], 0), axis=1)
    return (segment, offset, span_rows)


def gelu_exact(values):
    return jax.nn.gelu(values, approximate=False)


def key_block(whole, geometry, block_index, head_count):
    query_seg, query_pos, seg_all, pos_all, block_rows, score_scale = geometry
    first_row = block_index * block_rows
    key_piece = lax.dynamic_slice_in_dim(whole, first_row, block_rows, 0)
    key_seg = lax.dynamic_slice_in_dim(seg_all, first_row, block_rows, 0)
    key_pos = lax.dynamic_slice_in_dim(pos_all, first_row, block_rows, 0)
    half_width = key_piece.shape[1] // 2
    keys_part = key_piece[:, :half_width].reshape(block_rows, head_count, -1)
    values_part = key_piece[:, half_width:].reshape(block_rows, head_count, -1)
    return (keys_part, values_part, key_seg, key_pos)


def block_scores(queries, keys_part, key_seg, key_pos, geometry):
    query_seg, query_pos, seg_all, pos_all, block_rows, score_scale = geometry
    scores = (
        jnp.einsum("qhd,khd->hqk", queries, keys_part, preferred_element_type=jnp.float32)
        * score_scale
    )
    allowed = (query_seg[:, None] == key_seg[None, :]) & (key_pos[None, :] <= query_pos[:, None])
    return (scores, allowed[None])


def attend(queries, whole, geometry):
    row_count, head_count, head_dim = queries.shape
    block_count = whole.shape[0] // geometry[4]

    def statistics(running, block_index):
        largest, totals = running
        keys_part, values_part, key_seg, key_pos = key_block(
            whole, geometry, block_index, head_count
        )
        scores, allowed = block_scores(queries, keys_part, key_seg, key_pos, geometry)
        newest = jnp.maximum(largest, jnp.max(jnp.where(allowed, scores, NEGATIVE), axis=2))
        weights = jnp.where(allowed, jnp.exp(scores - newest[:, :, None]), 0.0)
        totals = totals * jnp.exp(largest - newest) + jnp.sum(weights, axis=2)
        return ((newest, totals), None)

    initial = (
        jnp.full((head_count, row_count), NEGATIVE, jnp.float32),
        jnp.zeros((head_count, row_count), jnp.float32),
    )
    (largest, totals), unused = lax.scan(statistics, initial, jnp.arange(block_count))
    log_total = largest + jnp.log(totals)

    def weighted(output_sum, block_index):
        keys_part, values_part, key_seg, key_pos = key_block(
            whole, geometry, block_index, head_count
        )
        scores, allowed = block_scores(queries, keys_part, key_seg, key_pos, geometry)
        probs = jnp.where(allowed, jnp.exp(scores - log_total[:, :, None]), 0.0).astype(
            jnp.bfloat16
        )
        output_sum = output_sum + jnp.einsum(
            "hqk,khd->qhd", probs, values_part, preferred_element_type=jnp.float32
        )
        return (output_sum, None)

    output_sum, unused = lax.scan(
        weighted, jnp.zeros((row_count, head_count, head_dim), jnp.float32), jnp.arange(block_count)
    )
    return (output_sum, log_total)


def attend_back(queries, whole, log_total, delta_sum, grad_heads, geometry):
    row_count, head_count, head_dim = queries.shape
    block_rows = geometry[4]
    score_scale = geometry[5]
    block_count = whole.shape[0] // block_rows

    def gradients(query_grad, block_index):
        keys_part, values_part, key_seg, key_pos = key_block(
            whole, geometry, block_index, head_count
        )
        scores, allowed = block_scores(queries, keys_part, key_seg, key_pos, geometry)
        probs = jnp.where(allowed, jnp.exp(scores - log_total[:, :, None]), 0.0)
        grad_probs = jnp.einsum(
            "qhd,khd->hqk", grad_heads, values_part, preferred_element_type=jnp.float32
        )
        grad_scores = (probs * (grad_probs - delta_sum[:, :, None])).astype(jnp.bfloat16)
        query_grad = (
            query_grad
            + jnp.einsum("hqk,khd->qhd", grad_scores, keys_part, preferred_element_type=jnp.float32)
            * score_scale
        )
        key_grad = (
            jnp.einsum("hqk,qhd->khd", grad_scores, queries, preferred_element_type=jnp.float32)
            * score_scale
        )
        value_grad = jnp.einsum(
            "hqk,qhd->khd",
            probs.astype(jnp.bfloat16),
            grad_heads,
            preferred_element_type=jnp.float32,
        )
        joined = jnp.concatenate(
            [key_grad.reshape(block_rows, -1), value_grad.reshape(block_rows, -1)], axis=1
        )
        return (query_grad, joined)

    query_grad, stacked = lax.scan(
        gradients,
        jnp.zeros((row_count, head_count, head_dim), jnp.float32),
        jnp.arange(block_count),
    )
    return (query_grad, stacked.reshape(whole.shape[0], -1))


def layer_forward(hidden, layer_index, weights, geometry):
    qkv_weight, out_weight, up_weight, up_bias, down_weight, down_bias, alphas = weights
    row_count, model_width = hidden.shape
    projection = qkv_weight[layer_index]
    rounded = hidden.astype(jnp.bfloat16)
    queries = (
        jnp.dot(rounded, projection[:, :model_width], preferred_element_type=jnp.float32)
        .astype(jnp.bfloat16)
        .reshape(row_count, HEADS, -1)
    )
    key_value = jnp.dot(
        rounded, projection[:, model_width:], preferred_element_type=jnp.float32
    ).astype(jnp.bfloat16)
    whole = lax.all_gather(key_value, "blk", axis=0, tiled=True)
    heads_out, log_total = attend(queries, whole, geometry)
    heads_rounded = heads_out.reshape(row_count, model_width).astype(jnp.bfloat16)
    branch = jnp.dot(heads_rounded, out_weight[layer_index], preferred_element_type=jnp.float32)
    alpha_pair = alphas[layer_index]
    middle = hidden + alpha_pair[0] * branch
    entered = middle.astype(jnp.bfloat16)
    gate_pre = (
        jnp.dot(entered, up_weight[layer_index], preferred_element_type=jnp.float32)
        + up_bias[layer_index]
    )
    activated = gelu_exact(gate_pre).astype(jnp.bfloat16)
    second = (
        jnp.dot(activated, down_weight[layer_index], preferred_element_type=jnp.float32)
        + down_bias[layer_index]
    )
    result = middle + alpha_pair[1] * second
    saved = (
        rounded,
        queries,
        key_value,
        whole,
        heads_out,
        heads_rounded,
        log_total,
        branch,
        entered,
        gate_pre,
        activated,
        second,
    )
    return (result, saved)


def layer_backward(grad_hidden, saved, layer_index, weights, geometry):
    qkv_weight, out_weight, up_weight, up_bias, down_weight, down_bias, alphas = weights
    (
        rounded,
        queries,
        key_value,
        saved_whole,
        heads_out,
        heads_rounded,
        log_total,
        branch,
        entered,
        gate_pre,
        activated,
        second,
    ) = saved
    row_count = grad_hidden.shape[0]
    alpha_pair = alphas[layer_index]
    grad_second = (alpha_pair[1] * grad_hidden).astype(jnp.bfloat16)
    alpha_second = jnp.sum(grad_hidden * second)
    bias_down = jnp.sum(grad_second.astype(jnp.float32), axis=0)
    grad_down = jnp.einsum("tf,td->fd", activated, grad_second, preferred_element_type=jnp.float32)
    grad_act = jnp.einsum(
        "td,fd->tf", grad_second, down_weight[layer_index], preferred_element_type=jnp.float32
    )
    unused, gelu_pull = jax.vjp(gelu_exact, gate_pre)
    grad_gate = gelu_pull(grad_act)[0].astype(jnp.bfloat16)
    bias_up = jnp.sum(grad_gate.astype(jnp.float32), axis=0)
    grad_up = jnp.einsum("td,tf->df", entered, grad_gate, preferred_element_type=jnp.float32)
    grad_middle = grad_hidden + jnp.einsum(
        "tf,df->td", grad_gate, up_weight[layer_index], preferred_element_type=jnp.float32
    )
    grad_branch = (alpha_pair[0] * grad_middle).astype(jnp.bfloat16)
    alpha_first = jnp.sum(grad_middle * branch)
    grad_proj_out = jnp.einsum(
        "te,td->ed", heads_rounded, grad_branch, preferred_element_type=jnp.float32
    )
    grad_heads = (
        jnp.einsum(
            "td,ed->te", grad_branch, out_weight[layer_index], preferred_element_type=jnp.float32
        )
        .astype(jnp.bfloat16)
        .reshape(queries.shape)
    )
    delta_sum = jnp.sum(grad_heads.astype(jnp.float32) * heads_out, axis=2).T
    whole = lax.all_gather(key_value, "blk", axis=0, tiled=True)
    query_grad, key_terms = attend_back(queries, whole, log_total, delta_sum, grad_heads, geometry)
    key_grads = lax.psum_scatter(
        key_terms.astype(jnp.bfloat16), "blk", scatter_dimension=0, tiled=True
    )
    grad_proj = jnp.concatenate(
        [query_grad.reshape(row_count, -1).astype(jnp.bfloat16), key_grads], axis=1
    )
    grad_qkv = jnp.einsum("td,te->de", rounded, grad_proj, preferred_element_type=jnp.float32)
    grad_input = grad_middle + jnp.einsum(
        "te,de->td", grad_proj, qkv_weight[layer_index], preferred_element_type=jnp.float32
    )
    layer_grads = (
        grad_qkv,
        grad_proj_out,
        grad_up,
        bias_up,
        grad_down,
        bias_down,
        jnp.stack([alpha_first, alpha_second]),
    )
    return (grad_input, layer_grads)


def reduce_all(layer_results, cycle_size):
    stacked = [
        jnp.stack([layer_entry[member] for layer_entry in layer_results], axis=0)
        for member in range(6)
    ]
    alpha_tiles = jnp.stack(
        [jnp.tile(layer_entry[6], cycle_size) for layer_entry in layer_results], axis=0
    )
    shares = (
        lax.psum_scatter(
            stacked[0].astype(jnp.bfloat16), "blk", scatter_dimension=1, tiled=True
        ).astype(jnp.float32),
        lax.psum_scatter(
            stacked[1].astype(jnp.bfloat16), "blk", scatter_dimension=1, tiled=True
        ).astype(jnp.float32),
        lax.psum_scatter(
            stacked[2].astype(jnp.bfloat16), "blk", scatter_dimension=1, tiled=True
        ).astype(jnp.float32),
        lax.psum_scatter(
            stacked[3].astype(jnp.bfloat16), "blk", scatter_dimension=1, tiled=True
        ).astype(jnp.float32),
        lax.psum_scatter(
            stacked[4].astype(jnp.bfloat16), "blk", scatter_dimension=1, tiled=True
        ).astype(jnp.float32),
        lax.psum_scatter(
            stacked[5].astype(jnp.bfloat16), "blk", scatter_dimension=1, tiled=True
        ).astype(jnp.float32),
        lax.psum_scatter(
            alpha_tiles.astype(jnp.bfloat16), "blk", scatter_dimension=1, tiled=True
        ).astype(jnp.float32),
    )
    return (
        lax.psum(shares[0].astype(jnp.bfloat16), "grp").astype(jnp.float32),
        lax.psum(shares[1].astype(jnp.bfloat16), "grp").astype(jnp.float32),
        lax.psum(shares[2].astype(jnp.bfloat16), "grp").astype(jnp.float32),
        lax.psum(shares[3].astype(jnp.bfloat16), "grp").astype(jnp.float32),
        lax.psum(shares[4].astype(jnp.bfloat16), "grp").astype(jnp.float32),
        lax.psum(shares[5].astype(jnp.bfloat16), "grp").astype(jnp.float32),
        lax.psum(shares[6].astype(jnp.bfloat16), "grp").astype(jnp.float32),
    )


def body(
    tokens,
    seq_len,
    qkv_weight,
    out_weight,
    up_weight,
    up_bias,
    down_weight,
    down_bias,
    alphas,
    cotangent,
):
    row_count, model_width = tokens.shape
    cycle_size = lax.axis_size("blk")
    cycle_place = lax.axis_index("blk")
    head_dim = model_width // HEADS
    total_rows = cycle_size * row_count
    block_rows = min(max(row_count, 512), total_rows)
    segment, offset, span_rows = layout(seq_len, row_count, cycle_size)
    query_pos = cycle_place * span_rows + offset
    seg_all = jnp.tile(segment, cycle_size)
    pos_all = jnp.repeat(jnp.arange(cycle_size, dtype=jnp.int32), row_count) * jnp.tile(
        span_rows, cycle_size
    ) + jnp.tile(offset, cycle_size)
    geometry = (segment, query_pos, seg_all, pos_all, block_rows, head_dim ** (-0.5))
    weights = (qkv_weight, out_weight, up_weight, up_bias, down_weight, down_bias, alphas)
    hidden = tokens.astype(jnp.float32)
    saved_layers = []
    for layer_index in range(LAYERS):
        hidden, saved = layer_forward(hidden, layer_index, weights, geometry)
        saved_layers.append(saved)
    output = hidden.astype(jnp.bfloat16)
    grad_hidden = cotangent.astype(jnp.float32)
    layer_results = []
    for layer_index in reversed(range(LAYERS)):
        grad_hidden, layer_grads = layer_backward(
            grad_hidden, saved_layers[layer_index], layer_index, weights, geometry
        )
        layer_results.insert(0, layer_grads)
    finals = reduce_all(layer_results, cycle_size)
    return (
        output,
        grad_hidden,
        finals[0],
        finals[1],
        finals[2],
        finals[3],
        finals[4],
        finals[5],
        finals[6],
    )


def solution(mesh):
    placed = (
        P(("grp", "blk"), None),
        P("grp", None),
        P(),
        P(),
        P(),
        P(),
        P(),
        P(),
        P(),
        P(("grp", "blk"), None),
    )
    sizes = (mesh.shape["grp"], mesh.shape["blk"])
    return jax.shard_map(
        fast_body if sizes == (4, RUNS) else body,
        mesh=mesh,
        in_specs=placed,
        out_specs=(
            P(("grp", "blk"), None),
            P(("grp", "blk"), None),
            P(None, "blk", None),
            P(None, "blk", None),
            P(None, "blk", None),
            P(None, "blk"),
            P(None, "blk", None),
            P(None, "blk"),
            P(),
        ),
        check_vma=False,
    )
```

```python
import functools

import jax
import jax.numpy as jnp
from jax import lax
from jax.experimental import pallas as pl
from jax.experimental.pallas import tpu as pltpu
from jax.sharding import PartitionSpec as P

HEADS = 8
LAYERS = 2
NEGATIVE = -1e30
MESH = pl.DeviceIdType.MESH
F32 = jnp.float32
BF16 = jnp.bfloat16

HALF = 128
RUNS = 8
TEAM = 4
OWN = RUNS // TEAM
DIM = 64
WIDTH = 512
FF = 2048
CUT = 512
TILE = 256
TILES = HALF * RUNS // TILE
PACK = HALF + DIM
CHUNK = 576
SMALL = FF + WIDTH + 128
PARTS = ((1, 0, 320), (1, 320, 256), (0, 0, 320), (0, 320, 256))
SHARES = ((192, 64, 64), (160, 64, 32), (176, 112, 32), (144, 96, 16))


def spans():
    places, totals = {}, [0, 0, 0]
    for part, counts in enumerate(SHARES):
        first = PARTS[part][1]
        for route, count in enumerate(counts):
            places[part, route] = (first, totals[route], count)
            first += count
            totals[route] += count
    return places, totals


SPANS, TOTALS = spans()

SLOPE_AT = 0.28
TAIL = (
    0.11652077851573843,
    0.06749675579450809,
    0.2689101589486142,
    -0.23699347299932225,
    0.3898740127620002,
    -0.10580824228351815,
)


def nn(a, b):
    return lax.dot_general(a, b, (((1,), (0,)), ((), ())), preferred_element_type=F32)


def nt(a, b):
    return lax.dot_general(a, b, (((1,), (1,)), ((), ())), preferred_element_type=F32)


def beside(first, other):
    low = lax.broadcasted_iota(jnp.int32, first.shape, 1) < DIM
    return (
        jnp.where(low, first, pltpu.roll(other, DIM, 1)),
        jnp.where(low, pltpu.roll(first, DIM, 1), other),
    )


def layers_kernel(
    tokens, seq_len, alphas, up_bias_hbm, down_bias_hbm, cotangent, qkv_hbm, out_hbm, up_hbm, down_hbm,
    final, heads_all, out_in, grad_in, small_final,
    wqkv, wout, wup, wdown, up_bias, down_bias,
    tok_in, cot_in, flag_out, flag_in, back_out,
    hidden, grad, hid_all, attn_t, entered, act, branch, slope, second,
    dz, du, da, dqkv,
    pack_out, head_out, pack_in, o_in, do_in,
    kv, kv_t, rq, ro, o_t, lse, acc, dq_t, bias,
    parts, core_in, xa_in, xb_in, ya_in, yb_in, z_in, third_z, third_x, third_y,
    heads_out, heads_x, heads_z, heads_sum, small, small_in, small_z, small_sum,
    w_sem, move_send, move_recv, a2a_send, a2a_recv, core_send, core_recv, x_send, x_recv, y_send, y_recv,
    z_send, z_recv, fin_send, fin_recv, hid_send, hid_recv, hx_send, hx_recv, hz_send, hz_recv, hf_send, hf_recv,
    small_send, small_recv, core_free,
):
    grp = lax.axis_index("grp")
    blk = lax.axis_index("blk")
    core = lax.rem(grp, 2)
    side = lax.div(grp, 2)
    yy = lax.rem(blk, 2)
    zz = lax.div(blk, 2)
    member = 2 * core + yy
    far_side = 2 * (1 - side) + core

    def place(c, x, z, y):
        return (2 * x + c, 2 * z + y)

    core_peer = place(1 - core, side, zz, yy)
    x_peer = place(core, 1 - side, zz, yy)
    y_peer = place(core, side, zz, 1 - yy)

    def remote(source, target, send, recv, peer):
        return pltpu.make_async_remote_copy(
            src_ref=source,
            dst_ref=target,
            send_sem=send,
            recv_sem=recv,
            device_id=peer,
            device_id_type=MESH,
        )

    def credit(semaphore, peer, count=1):
        pl.semaphore_signal(semaphore, inc=count, device_id=peer, device_id_type=MESH)

    def moved(kind, slot, source, target, at, core_at, z_at):
        here = jnp.logical_and(core_at == core, z_at == zz)

        @pl.when(here)
        def _():
            pltpu.make_async_copy(source, target.at[at], move_recv.at[kind, at]).start()

        @pl.when(jnp.logical_not(here))
        def _():
            pltpu.make_async_remote_copy(
                src_ref=source,
                dst_ref=target.at[at],
                send_sem=move_send.at[kind, slot],
                recv_sem=move_recv.at[kind, at],
                device_id=place(core_at, side, z_at, yy),
                device_id_type=MESH,
            ).start()

    def move_left(kind, slot, source, core_at, z_at):
        here = jnp.logical_and(core_at == core, z_at == zz)

        @pl.when(jnp.logical_not(here))
        def _():
            pltpu.make_async_copy(source, source, move_send.at[kind, slot]).wait()

    def move_arrived(kind, at, target):
        pltpu.make_async_copy(target.at[at], target.at[at], move_recv.at[kind, at]).wait()

    def to_team(kind, half, source, target):
        moved(kind, half, source, target, lax.div(zz, 2), lax.rem(zz, 2), 2 * half + core)

    def to_team_left(kind, half, source):
        move_left(kind, half, source, lax.rem(zz, 2), 2 * half + core)

    def to_owner(kind, chunk, source, target):
        moved(kind, chunk, source, target, lax.div(zz, 2), lax.rem(zz, 2), core + 2 * chunk)

    def to_owner_left(kind, chunk, source):
        move_left(kind, chunk, source, lax.rem(zz, 2), core + 2 * chunk)

    def half_of(ref, half):
        return ref.at[pl.ds(pl.multiple_of(HALF * half, HALF), HALF)]

    def rows_of(half):
        return pl.ds(pl.multiple_of(half * HALF, HALF), HALF)

    def slot_of(other):
        return lax.rem(other + TEAM - member, TEAM)

    def exchange(kind, layer, half, outgoing, incoming, head=None):
        at = () if head is None else (head,)
        incoming[(half, 0, *at)] = outgoing[(half, member, *at)]
        for step in range(1, TEAM):
            peer = lax.rem(member + step, TEAM)
            remote(
                outgoing.at[(half, peer, *at)],
                incoming.at[(half, TEAM - step, *at)],
                a2a_send.at[kind, layer, half, head or 0],
                a2a_recv.at[kind, layer, half, head or 0],
                place(lax.div(peer, 2), side, zz, lax.rem(peer, 2)),
            ).start()

    def arrived(kind, layer, half, incoming, head=None):
        at = () if head is None else (head,)
        whole = incoming.at[(half, pl.ds(1, TEAM - 1), *at)]
        pltpu.make_async_copy(whole, whole, a2a_recv.at[kind, layer, half, head or 0]).wait()

    def left(kind, layer, half, outgoing):
        for head in range(OWN) if kind in (0, 3) else (None,):
            at = () if head is None else (head,)
            whole = outgoing.at[(half, pl.ds(1, TEAM - 1), *at)]
            pltpu.make_async_copy(whole, whole, a2a_send.at[kind, layer, half, head or 0]).wait()

    def tokens_of(chunk, other):
        return pl.ds(pl.multiple_of(HALF * (TEAM * chunk + other), HALF), HALF)

    def hidden_copy(layer, chunk, which):
        whose = 2 * core + 1 - yy if which == 2 else member
        block = hid_all.at[layer, :, tokens_of(chunk, whose)]
        return remote(
            block,
            block,
            hid_send.at[layer, chunk, which],
            hid_recv.at[layer, chunk, which],
            y_peer if which == 0 else core_peer,
        )

    def hidden_start(layer, chunk):
        for which in range(2):
            hidden_copy(layer, chunk, which).start()

    def hidden_pass(layer, chunk):
        hidden_copy(layer, chunk, 0).wait()
        hidden_copy(layer, chunk, 2).start()

    def hidden_done(layer, chunk):
        for which in range(1, 3):
            hidden_copy(layer, chunk, which).wait()

    def project(layer, half):
        rows = rows_of(half)
        rounded = hidden[rows, :].astype(BF16)
        if layer == 1:
            left(0, 0, half, pack_out)
        queries = (nn(rounded, wqkv[layer, :, 0:WIDTH]) * (DIM ** -0.5)).astype(BF16).T
        for head in range(RUNS):
            pack_out[half, head // 2, head % 2, HALF:, :] = queries[DIM * head : DIM * head + DIM, :]
        for step in range(2):
            at = WIDTH * (step + 1)
            keys_values = nn(rounded, wqkv[layer, :, at : at + WIDTH]).astype(BF16)
            for head in range(4):
                pack_out[half, 2 * step + head // 2, head % 2, 0:HALF, :] = keys_values[
                    :, 128 * head : 128 * head + 128
                ]
        for head in range(OWN):
            exchange(0, layer, half, pack_out, pack_in, head)
        hid_all[layer, :, tokens_of(half, member)] = rounded.T

    def attend(layer, chunk):
        if layer == 1:
            left(1, 0, chunk, head_out)

        def one_head(head, carry):
            arrived(0, layer, chunk, pack_in, head)
            for other in range(TEAM):
                slot = slot_of(other)
                start = HALF * (TEAM * chunk + other)
                span = slice(start, start + HALF)
                block = pack_in[chunk, slot, head, 0:HALF, :]
                kv[layer, head, span, :] = block
                kv_t[layer, head, :, span] = block.T
                rq[layer, head, 0:DIM, span] = pack_in[chunk, slot, head, HALF:, :]

            def scores_of(i):
                count = TILE * (i + 1)
                tile = rq[layer, head, :, TILE * i : TILE * i + TILE]
                return nn(kv[layer, head, 0:count, :], tile) + bias[TILE * TILES - count :, :]

            ahead = [scores_of(i) for i in (2 * chunk, 2 * chunk + 1)]
            for i in (2 * chunk, 2 * chunk + 1):
                columns = slice(TILE * i, TILE * i + TILE)
                count = TILE * (i + 1)
                scores = ahead[i - 2 * chunk]
                largest = jnp.max(scores, axis=0, keepdims=True)
                weight = jnp.exp(scores - largest)
                total = jnp.sum(weight, axis=0, keepdims=True)
                summed = nn(kv_t[layer, head, DIM:, 0:count], weight.astype(BF16))
                summed = summed / total
                o_t[layer, head, :, columns] = summed
                lse[layer, head, :, columns] = largest + jnp.log(total)
                rounded = summed.astype(BF16)
                for part in range(2):
                    head_out[chunk, 2 * (i - 2 * chunk) + part, head] = rounded[
                        :, HALF * part : HALF * part + HALF
                    ]
            return carry

        for head in range(OWN):
            one_head(head, 0)
        exchange(1, layer, chunk, head_out, o_in)

    def feed(layer, half):
        rows = rows_of(half)
        arrived(1, layer, half, o_in)
        for head in range(RUNS):
            attn_t[layer, DIM * head : DIM * head + DIM, rows] = o_in[half, slot_of(head // 2), head % 2]
        attn = attn_t[layer, :, rows].T
        grown = nn(attn, wout[layer])
        branch[layer, rows, :] = grown
        middle = hidden[rows, :] + alphas[layer, 0] * grown
        rounded = middle.astype(BF16)
        entered[layer, rows, :] = rounded
        total = jnp.zeros((HALF, WIDTH), F32)

        def gate_of(step):
            cut = slice(CUT * step, CUT * step + CUT)
            return nn(rounded, wup[layer, :, cut]) + up_bias[layer : layer + 1, cut]

        coming = gate_of(0)
        for step in range(FF // CUT):
            cut = slice(CUT * step, CUT * step + CUT)
            gate = coming
            if step + 1 < FF // CUT:
                coming = gate_of(step + 1)
            bell = jnp.exp(gate * gate * -0.5)
            near = pl.reciprocal(1.0 + SLOPE_AT * jnp.abs(gate), approx=True)
            tail = jnp.full_like(gate, TAIL[5])
            for factor in TAIL[4::-1]:
                tail = tail * near + factor
            tail = bell * (tail * near)
            risen = jnp.where(gate > 0.0, 1.0 - tail, tail)
            slope[layer, rows, cut] = risen + gate * bell * 0.3989422804014327
            active = (gate * risen).astype(BF16)
            act[layer, rows, cut] = active
            total = total + nn(active, wdown[layer, cut, :])
        total = total + down_bias[layer : layer + 1, :]
        second[layer, rows, :] = total
        hidden[rows, :] = middle + alphas[layer, 1] * total

    def total_of(values):
        return jnp.sum(jnp.sum(values, axis=0, keepdims=True), axis=1, keepdims=True)

    def feed_back(layer):
        start = grad[...]
        if layer == 0:
            dz[...] = (alphas[layer, 1] * start).astype(BF16)
        scaled = dz[...]
        alpha_second = total_of(start * second[layer])
        small[layer : layer + 1, FF : FF + WIDTH] = jnp.sum(scaled.astype(F32), axis=0, keepdims=True)
        middle = start
        coming = nt(scaled, wdown[layer, 0:CUT, :])
        for step in range(FF // CUT):
            cut = slice(CUT * step, CUT * step + CUT)
            raw = coming
            if step + 1 < FF // CUT:
                coming = nt(scaled, wdown[layer, CUT * (step + 1) : CUT * (step + 2), :])
            gate = (raw * slope[layer, :, cut]).astype(BF16)
            du[:, cut] = gate
            small[layer : layer + 1, cut] = jnp.sum(gate.astype(F32), axis=0, keepdims=True)
            middle = middle + nt(gate, wup[layer, :, cut])
        grad[...] = middle
        mixed = (alphas[layer, 0] * middle).astype(BF16)
        da[...] = mixed
        spread = nt(wout[layer], mixed).astype(BF16)
        for chunk in (1, 0):
            left(*((1, 1) if layer == 1 else (2, 1)), chunk, head_out)
            for head in range(RUNS):
                head_out[chunk, head // 2, head % 2] = spread[
                    DIM * head : DIM * head + DIM, HALF * chunk : HALF * chunk + HALF
                ]
            exchange(2, layer, chunk, head_out, do_in)
        alpha_first = total_of(middle * branch[layer])
        column = lax.broadcasted_iota(jnp.int32, (1, 128), 1)
        small[layer : layer + 1, FF + WIDTH :] = jnp.where(
            column == 0, alpha_first, jnp.where(column == 1, alpha_second, 0.0)
        )

    def attend_back(layer, chunk):
        arrived(2, layer, chunk, do_in)
        left(*((0, 1) if layer == 1 else (3, 1)), chunk, pack_out)

        def one_head(head, carry):
            for other in range(TEAM):
                start = HALF * (TEAM * chunk + other)
                ro[head, DIM:, start : start + HALF] = do_in[chunk, slot_of(other), head]
            for i in (2 * chunk, 2 * chunk + 1):
                columns = slice(TILE * i, TILE * i + TILE)
                query_tile = rq[layer, head, :, columns]
                grad_tile = ro[head, :, columns]
                log_total = lse[layer, head, :, columns]
                delta = jnp.sum(
                    ro[head, DIM:, columns].astype(F32) * o_t[layer, head, :, columns],
                    axis=0,
                    keepdims=True,
                )
                count = TILE * (i + 1)
                keys = kv[layer, head, 0:count, :]
                weight = jnp.exp(nn(keys, query_tile) + bias[TILE * TILES - count :, :] - log_total)
                scored = (weight * (nn(keys, grad_tile) - delta)).astype(BF16)
                term = nt(scored, query_tile) + nt(weight.astype(BF16), grad_tile)
                if chunk == 1 and i == 2:
                    acc[head, 0:count, :] = term
                elif chunk == 1:
                    acc[head, 0 : count - TILE, :] += term[0 : count - TILE, :]
                    acc[head, count - TILE : count, :] = term[count - TILE :, :]
                else:
                    acc[head, 0:count, :] += term
                query_grad = nn(kv_t[layer, head, 0:DIM, 0:count], scored)
                dq_t[head, :, columns] = query_grad * (DIM ** -0.5)
            for other in range(TEAM):
                start = HALF * (TEAM * chunk + other)
                span = slice(start, start + HALF)
                pack_out[chunk, other, head, 0:HALF, :] = acc[head, span, :].astype(BF16)
                pack_out[chunk, other, head, HALF:, :] = dq_t[head, :, span].astype(BF16)
            exchange(3, layer, chunk, pack_out, pack_in, head)
            return carry

        for head in range(OWN):
            one_head(head, 0)

    def project_back(layer, half):
        for head in range(OWN):
            arrived(3, layer, half, pack_in, head)
        turned = jnp.concatenate(
            [pack_in[half, slot_of(head // 2), head % 2, HALF:, :] for head in range(RUNS)], axis=0
        )
        dqkv[:, 0:WIDTH] = turned.T
        for head in range(RUNS):
            at = WIDTH + 128 * head
            dqkv[:, at : at + 128] = pack_in[half, slot_of(head // 2), head % 2, 0:HALF, :]
        rows = rows_of(half)
        grad[rows, :] = grad[rows, :] + nt(dqkv[...], wqkv[layer])

    def scatter_rows(layer, result, first_row):
        for run in range(RUNS):
            for quarter in range(4):
                parts[layer, quarter % 2, quarter // 2, run // 2, run % 2, first_row : first_row + DIM, :] = result[
                    DIM * run : DIM * run + DIM, 128 * quarter : 128 * quarter + 128
                ].astype(BF16)

    def make(part):
        layer, first, count = PARTS[part]
        if first < 256:
            turned = entered[layer].T
        for row in range(first, min(first + count, 256), DIM):
            step = row // DIM
            scatter_rows(layer, nn(turned, du[:, CUT * step : CUT * step + CUT]), row)
        if first <= 256 < first + count:
            scatter_rows(layer, nn(attn_t[layer], da[...]), 256)
        if first >= 320:
            turned = dz[...].T
            for step in range(FF // CUT):
                result = nn(turned, act[layer, :, CUT * step : CUT * step + CUT])
                for block in range(CUT // 128):
                    run, row = 2 * step + block // 2, 320 + 128 * (block % 2)
                    for quarter in range(4):
                        parts[layer, quarter % 2, quarter // 2, run // 2, run % 2, row : row + 128, :] = result[
                            128 * quarter : 128 * quarter + 128, 128 * block : 128 * block + 128
                        ].astype(BF16)
        if layer == 0:
            pl.semaphore_wait(core_free.at[0 if first < 320 else 1], 1)
        core_copy(part).start()

    def heads_grads(layer):
        for chunk in range(2):
            hidden_done(layer, chunk)
        blocks = [(run // TEAM, run % TEAM) for run in range(RUNS)]
        keys_values = jnp.concatenate(
            [
                jnp.concatenate([pack_out[chunk, other, head, 0:HALF, :] for chunk, other in blocks], axis=0)
                for head in range(OWN)
            ],
            axis=1,
        )
        queries = jnp.concatenate(
            [
                jnp.concatenate([pack_out[chunk, other, head, HALF:, :] for chunk, other in blocks], axis=1)
                for head in range(OWN)
            ],
            axis=0,
        )
        both = nn(hid_all[layer], keys_values)
        q_part = nt(hid_all[layer], queries)
        for number, values in enumerate((q_part, both[:, 0:128], both[:, 128:256])):
            for run in range(RUNS):
                heads_out[layer, run // 2, run % 2, :, 128 * number : 128 * number + 128] = values[
                    DIM * run : DIM * run + DIM, :
                ].astype(BF16)
        heads_x_copy(layer).start()

    def half_rows(which):
        return pl.ds(pl.multiple_of(32 * which, 32), 32)

    def heads_x_copy(layer):
        return remote(
            heads_out.at[layer, :, :, half_rows(1 - side)],
            heads_x.at[layer],
            hx_send.at[layer],
            hx_recv.at[layer],
            x_peer,
        )

    def heads_z_copy(layer, step):
        peer = lax.rem(zz + step, 4)
        return remote(
            heads_out.at[layer, peer, :, half_rows(side)],
            heads_z.at[layer, 4 - step],
            hz_send.at[layer, step],
            hz_recv.at[layer, 4 - step],
            place(core, side, peer, yy),
        )

    def heads_last_copy(layer, number):
        x, c, y = number // 4, number // 2 % 2, number % 2
        return remote(
            heads_sum.at[layer, 1 - yy if y else yy],
            heads_all.at[layer, side, member],
            hf_send.at[layer, number],
            hf_recv.at[layer, number],
            place(1 - core if c else core, 1 - side if x else side, zz, 1 - yy if y else yy),
        )

    def heads_second(layer):
        heads_x_copy(layer).wait()
        heads_out[layer, :, :, half_rows(side), :] += heads_x[layer]
        for step in range(1, 4):
            heads_z_copy(layer, step).start()

    def heads_third(layer):
        for step in range(1, 4):
            heads_z_copy(layer, step).wait()
        total = heads_out[layer, zz, :, half_rows(side), :].astype(F32)
        for slot in range(1, 4):
            total = total + heads_z[layer, slot].astype(F32)
        heads_sum[layer] = total.astype(BF16)
        heads_all[layer, side, member] = heads_sum[layer, yy]
        for number in range(1, 8):
            heads_last_copy(layer, number).start()

    def heads_done(layer):
        for number in range(1, 8):
            heads_last_copy(layer, number).wait()

    def rows_in(part, route):
        first, room, count = SPANS[part, route]
        return pl.ds(first, count), pl.ds(room, count)

    def used(part, route):
        return SHARES[part][route] > 0

    def core_copy(part):
        layer, first, count = PARTS[part]
        rows = pl.ds(first, count)
        return remote(
            parts.at[layer, 1 - core, :, :, :, rows],
            core_in.at[:, :, :, rows],
            core_send.at[part],
            core_recv.at[part],
            core_peer,
        )

    def x_copy(part, route):
        layer = PARTS[part][0]
        rows, room = rows_in(part, route)
        ends = (x_send.at[part, route], x_recv.at[part, route], x_peer)
        mine = parts.at[layer, core, 1 - side]
        if route == 0:
            return remote(mine.at[:, :, rows], xa_in.at[:, :, room], *ends)
        if route == 1:
            return remote(mine.at[:, yy, rows], xb_in.at[:, room], *ends)
        return remote(mine.at[zz, :, rows], third_x.at[:, room], *ends)

    def y_copy(part, route):
        layer = PARTS[part][0]
        rows, room = rows_in(part, route)
        ends = (y_send.at[part, route], y_recv.at[part, route], y_peer)
        mine = parts.at[layer, core]
        if route == 0:
            return remote(mine.at[side, :, 1 - yy, rows], ya_in.at[:, room], *ends)
        if route == 1:
            return remote(mine.at[:, :, 1 - yy, rows], yb_in.at[:, :, room], *ends)
        return remote(mine.at[side, zz, 1 - yy, rows], third_y.at[room], *ends)

    def z_copy(part, route, step):
        layer = PARTS[part][0]
        rows, room = rows_in(part, route)
        peer = lax.rem(zz + step, 4)
        ends = (z_send.at[part, route, step], z_recv.at[part, route, 4 - step], place(core, side, peer, yy))
        if route == 2:
            return remote(parts.at[layer, core, :, peer, :, rows], third_z.at[4 - step, :, :, room], *ends)
        return remote(parts.at[layer, core, side, peer, yy, rows], z_in.at[layer, 4 - step, rows], *ends)

    def final_copy(part, which):
        layer, first, count = PARTS[part]
        block = final.at[layer, far_side if which == 2 else grp, pl.ds(first, count)]
        return remote(
            block,
            block,
            fin_send.at[part, which],
            fin_recv.at[part, which],
            x_peer if which == 0 else core_peer,
        )

    def core_done(part):
        layer, first, count = PARTS[part]
        rows = pl.ds(first, count)
        core_copy(part).wait()
        for across in (1 - side, side):
            parts[layer, core, across, :, :, rows, :] += core_in[across, :, :, rows, :]
            if used(part, 0) and across is not side:
                x_copy(part, 0).start()
        if used(part, 1):
            y_copy(part, 1).start()
        if used(part, 2):
            for step in range(1, 4):
                z_copy(part, 2, step).start()
        if layer == 1:
            freed = 0 if first < 320 else 1
            followers = [1 for other in PARTS if other[0] == 0 and (other[1] >= 320) == (freed == 1)]
            credit(core_free.at[freed], core_peer, len(followers))

    def first_x(part):
        if used(part, 0):
            layer = PARTS[part][0]
            rows, room = rows_in(part, 0)
            x_copy(part, 0).wait()
            for y in (1 - yy, yy):
                parts[layer, core, side, :, y, rows, :] += xa_in[:, y, room, :]
                if y is not yy:
                    y_copy(part, 0).start()

    def first_y(part):
        if used(part, 1):
            layer = PARTS[part][0]
            rows, room = rows_in(part, 1)
            y_copy(part, 1).wait()
            for across in (1 - side, side):
                parts[layer, core, across, :, yy, rows, :] += yb_in[across, :, room, :]
                if across is not side:
                    x_copy(part, 1).start()

    def first_z(part):
        if used(part, 2):
            layer = PARTS[part][0]
            rows, room = rows_in(part, 2)
            for step in range(1, 4):
                z_copy(part, 2, step).wait()
            for across in (1 - side, side):
                total = parts[layer, core, across, zz, :, rows, :].astype(F32)
                for slot in range(1, 4):
                    total = total + third_z[slot, across, :, room, :].astype(F32)
                parts[layer, core, across, zz, :, rows, :] = total.astype(BF16)
                if across is not side:
                    x_copy(part, 2).start()

    def second_x(part):
        if used(part, 0):
            layer = PARTS[part][0]
            rows, room = rows_in(part, 0)
            y_copy(part, 0).wait()
            parts[layer, core, side, :, yy, rows, :] += ya_in[:, room, :]
            for step in range(1, 4):
                z_copy(part, 0, step).start()

    def second_y(part):
        if used(part, 1):
            layer = PARTS[part][0]
            rows, room = rows_in(part, 1)
            x_copy(part, 1).wait()
            parts[layer, core, side, :, yy, rows, :] += xb_in[:, room, :]
            for step in range(1, 4):
                z_copy(part, 1, step).start()

    def second_z(part):
        if used(part, 2):
            layer = PARTS[part][0]
            rows, room = rows_in(part, 2)
            x_copy(part, 2).wait()
            for y in (1 - yy, yy):
                parts[layer, core, side, zz, y, rows, :] += third_x[y, room, :]
                if y is not yy:
                    y_copy(part, 2).start()

    def third_done(part):
        layer = PARTS[part][0]
        for route in range(3):
            if not used(part, route):
                continue
            rows, room = rows_in(part, route)
            if route == 2:
                y_copy(part, 2).wait()
                final[layer, grp, rows, :] = parts[layer, core, side, zz, yy, rows, :] + third_y[room, :]
            else:
                for step in range(1, 4):
                    z_copy(part, route, step).wait()
                total = parts[layer, core, side, zz, yy, rows, :].astype(F32)
                for slot in range(1, 4):
                    total = total + z_in[layer, slot, rows, :].astype(F32)
                final[layer, grp, rows, :] = total.astype(BF16)
        if PARTS[part][1] >= 320:
            for row in (320, 448):
                final[layer, grp, row : row + 128, :] = final[layer, grp, row : row + 128, :].T
        for which in range(2):
            final_copy(part, which).start()

    def final_pass(part):
        final_copy(part, 0).wait()
        final_copy(part, 2).start()

    def final_done(part):
        for which in range(1, 3):
            final_copy(part, which).wait()

    def small_copy(stage):
        peer = (core_peer, x_peer, y_peer)[stage]
        return remote(
            small_sum.at[stage], small_in.at[stage], small_send.at[stage], small_recv.at[stage], peer
        )

    def small_z_copy(step):
        return remote(
            small_z.at[zz],
            small_z.at[zz],
            small_send.at[2 + step],
            small_recv.at[2 + step],
            place(core, side, lax.rem(zz + step, 4), yy),
        )

    def small_start():
        small_sum[0] = small[...]
        small_copy(0).start()

    def small_next(stage):
        small_copy(stage).wait()
        total = small_sum[stage] + small_in[stage]
        if stage < 2:
            small_sum[stage + 1] = total
            small_copy(stage + 1).start()
        else:
            small_z[zz] = total
            for step in range(1, 4):
                small_z_copy(step).start()

    def small_done():
        for step in range(1, 4):
            small_z_copy(step).wait()
        small_sum[0] = (small_z[0] + small_z[1]) + (small_z[2] + small_z[3])
        small_final[:, 0:256] = small_sum[0, :, pl.ds(pl.multiple_of(blk * 256, 256), 256)]
        pair = small_sum[0, :, pl.ds(pl.multiple_of(FF + 128 * zz, 128), 128)]
        small_final[:, 256:384] = jnp.where(yy == 1, pltpu.roll(pair, DIM, 1), pair)
        small_final[:, 384:512] = small_sum[0, :, FF + WIDTH :]

    def halves(*phases, first=0):
        def both(step, carry):
            for phase in phases:
                phase(lax.rem(step + first, 2))
            return carry

        lax.fori_loop(0, 2, both, 0)

    def begin(half):
        move_arrived(0, half, tok_in)
        hidden[rows_of(half), :] = tok_in[half].astype(F32)

    def finish(half):
        back_out[0, half] = hidden[rows_of(half), :].astype(BF16)
        to_owner(3, half, back_out.at[0, half], out_in)

    def turn_round(layer, half):
        move_arrived(2, half, cot_in)
        rows = rows_of(half)
        grad[rows, :] = cot_in[half].astype(F32)
        dz[rows, :] = (alphas[layer, 1] * grad[rows, :]).astype(BF16)

    def hand_back(half):
        back_out[1, half] = grad[rows_of(half), :].astype(BF16)
        to_owner(4, half, back_out.at[1, half], grad_in)

    barrier = pltpu.get_barrier_semaphore()
    for step in range(1, 4):
        credit(barrier, place(core, side, lax.rem(zz + step, 4), yy))
    for step in range(4):
        credit(barrier, place(1 - core, side, lax.rem(zz + step, 4), yy))
    for peer in (
        x_peer,
        y_peer,
        place(1 - core, side, zz, 1 - yy),
        place(1 - core, 1 - side, zz, yy),
        place(core, 1 - side, zz, 1 - yy),
        place(1 - core, 1 - side, zz, 1 - yy),
    ):
        credit(barrier, peer)

    weight_copies = {}
    for layer in range(LAYERS):
        for number, (source, target) in enumerate(
            ((qkv_hbm, wqkv), (out_hbm, wout), (up_hbm, wup), (down_hbm, wdown))
        ):
            weight_copies[layer, number] = pltpu.make_async_copy(
                source.at[layer], target.at[layer], w_sem.at[layer, number]
            )
    bias_copies = [
        pltpu.make_async_copy(up_bias_hbm, up_bias, w_sem.at[2, 0]),
        pltpu.make_async_copy(down_bias_hbm, down_bias, w_sem.at[2, 1]),
    ]
    weight_copies[0, 0].start()
    pl.semaphore_wait(barrier, 13)
    upper = lax.div(zz, 2)
    for half in (1 - upper, upper):
        to_team(0, half, half_of(tokens, half), tok_in)
    for layer, number in ((1, 0), (0, 1), (0, 2), (0, 3), (1, 1), (1, 2), (1, 3)):
        weight_copies[layer, number].start(priority=1)
    for copy in bias_copies:
        copy.start(priority=1)
    end_second = lax.div(seq_len[0, 0] + seq_len[0, 1], RUNS)
    flag_out[...] = jnp.full((8, 128), end_second.astype(F32), F32)
    for half in (1 - upper, upper):
        to_team(1, half, flag_out, flag_in)
    for layer in range(LAYERS):
        for head in range(OWN):
            rq[layer, head, DIM:, :] = jnp.zeros((DIM, HALF * RUNS), BF16)
    for head in range(OWN):
        ro[head, 0:DIM, :] = jnp.zeros((DIM, HALF * RUNS), BF16)
    for layer in range(LAYERS):
        weight_copies[layer, 0].wait()
        pairs = [
            beside(
                wqkv[layer, :, WIDTH + 128 * pair : WIDTH + 128 * pair + 128].astype(F32),
                wqkv[layer, :, 2 * WIDTH + 128 * pair : 2 * WIDTH + 128 * pair + 128].astype(F32),
            )
            for pair in range(TEAM)
        ]
        for head in range(RUNS):
            at = WIDTH + 128 * head
            wqkv[layer, :, at : at + 128] = pairs[head // 2][head % 2].astype(BF16)
    halves(begin, functools.partial(project, 0), first=upper)
    for half in (1 - upper, upper):
        to_team(2, half, half_of(cotangent, half), cot_in)

    move_arrived(1, 0, flag_in)
    move_arrived(1, 1, flag_in)
    border = jnp.concatenate([flag_in[0, 0:1, :]] * 2, axis=1) - (HALF * lax.div(zz, 2)).astype(F32)
    key_row = lax.broadcasted_iota(jnp.int32, (TILE, TILE), 0)
    query_col = lax.broadcasted_iota(jnp.int32, (TILE, TILE), 1)
    later = key_row > query_col
    key_sub = lax.rem(key_row, HALF).astype(F32) >= border
    query_sub = lax.rem(query_col, HALF).astype(F32) >= border
    apart = jnp.logical_xor(key_sub, query_sub)
    for tile in range(TILES - 1):
        bias[TILE * tile : TILE * tile + TILE, :] = jnp.where(apart, NEGATIVE, 0.0)
    bias[TILE * (TILES - 1) :, :] = jnp.where(jnp.logical_or(later, apart), NEGATIVE, 0.0)

    for copy in (*bias_copies, *(weight_copies[0, number] for number in range(1, 4))):
        copy.wait()
    attend(0, 0)
    attend(0, 1)
    hidden_start(0, 0)
    halves(functools.partial(feed, 0), functools.partial(project, 1))
    for number in range(1, 4):
        weight_copies[1, number].wait()
    attend(1, 0)
    attend(1, 1)
    hidden_pass(0, 0)
    hidden_start(1, 0)
    halves(functools.partial(feed, 1), finish)
    hidden_start(0, 1)
    hidden_start(1, 1)
    hidden_pass(1, 0)

    halves(functools.partial(turn_round, 1))
    make(1)
    feed_back(1)
    hidden_pass(0, 1)
    hidden_pass(1, 1)
    core_done(1)
    make(0)
    attend_back(1, 1)
    first_y(1)
    core_done(0)
    attend_back(1, 0)
    second_y(1)
    first_y(0)
    first_x(1)
    project_back(1, 1)
    heads_grads(1)
    first_z(1)
    project_back(1, 0)
    feed_back(0)
    small_start()
    second_x(1)
    second_y(0)
    make(2)
    first_x(0)
    heads_second(1)
    first_z(0)
    attend_back(0, 1)
    small_next(0)
    core_done(2)
    second_x(0)
    make(3)
    attend_back(0, 0)
    small_next(1)
    project_back(0, 1)
    hand_back(1)
    first_z(2)
    heads_grads(0)
    small_next(2)
    first_x(2)
    core_done(3)
    first_y(2)
    heads_second(0)
    small_done()
    first_z(3)
    second_x(2)
    first_x(3)
    second_z(2)
    second_z(0)
    heads_third(1)
    second_z(1)
    first_y(3)
    heads_third(0)
    second_y(2)
    second_x(3)
    second_z(3)
    third_done(0)
    third_done(2)
    second_y(3)
    project_back(0, 0)
    hand_back(0)
    heads_done(1)
    third_done(1)
    third_done(3)
    final_pass(0)
    final_pass(2)
    final_pass(1)
    final_pass(3)
    final_done(2)
    final_done(1)
    heads_done(0)
    final_done(0)
    final_done(3)
    for half in range(2):
        move_arrived(3, half, out_in)
        move_arrived(4, half, grad_in)

    for half in range(2):
        left(2, 0, half, head_out)
        left(3, 0, half, pack_out)
        to_team_left(0, half, half_of(tokens, half))
        to_team_left(1, half, flag_out)
        to_team_left(2, half, half_of(cotangent, half))
        to_owner_left(3, half, back_out.at[0, half])
        to_owner_left(4, half, back_out.at[1, half])


def results_kernel(
    final, heads, out_block, grad_block, small,
    output, input_grad, qkv_grad, out_grad, up_grad, up_bias_grad, down_grad, down_bias_grad, alpha_grad,
    out_flat, grad_wide, qkv_wide, out_wide, up_wide, down_wide, out_sem,
):
    ends = []

    def write(source, target):
        ends.append(pltpu.make_async_copy(source, target, out_sem.at[len(ends)]))
        ends[-1].start()

    up_bias_grad[...] = small[:, 0:256]
    down_bias_grad[...] = small[:, 256 : 256 + DIM]
    alpha_grad[...] = small[:, 384:386]
    for layer in range(LAYERS):
        for quarter in range(4):

            def block(first, count):
                return final[layer, quarter, first : first + count, :].astype(F32)

            def columns(step):
                return slice(WIDTH * step + 128 * quarter, WIDTH * step + 128 * quarter + 128)

            for step in range(4):
                up_wide[layer, :, columns(step)] = block(DIM * step, DIM)
            out_wide[layer, :, columns(0)] = block(256, DIM)
            down_wide[layer, :, columns(0)] = block(320, 256)
        write(up_wide.at[layer], up_grad.at[layer])
        write(out_wide.at[layer], out_grad.at[layer])
        write(down_wide.at[layer], down_grad.at[layer])
    for half in range(2):
        rows = slice(HALF * half, HALF * half + HALF)
        grad_wide[rows, :] = grad_block[half].astype(F32)
        out_flat[rows, :] = out_block[half]
    write(grad_wide, input_grad)
    write(out_flat, output)
    for layer in range(LAYERS):
        for side in range(2):
            for member in range(TEAM):
                block = heads[layer, side, member].astype(F32)
                columns = (block[:, 0:128], *beside(block[:, 128:256], block[:, 256:384]))
                for step in range(3):
                    at = WIDTH * step + 128 * member
                    qkv_wide[layer, 32 * side : 32 * side + 32, at : at + 128] = columns[step]
        write(qkv_wide.at[layer], qkv_grad.at[layer])
    for end in ends:
        end.wait()


def fast_body(
    tokens, seq_len, qkv_weight, out_weight, up_weight, up_bias, down_weight, down_bias, alphas, cotangent
):
    whole = pl.BlockSpec(memory_space=pltpu.VMEM)
    scalar = pl.BlockSpec(memory_space=pltpu.SMEM)
    far = pl.BlockSpec(memory_space=pl.ANY)
    shape = jax.ShapeDtypeStruct
    rows = HALF * RUNS

    def vmem(*dims):
        return pltpu.VMEM(dims, BF16)

    def wide(*dims):
        return pltpu.VMEM(dims, F32)

    dma = pltpu.SemaphoreType.DMA
    final, heads, out_block, grad_block, small = pl.pallas_call(
        layers_kernel,
        out_shape=(
            vmem(LAYERS, 4, CHUNK, 128),
            vmem(LAYERS, 2, TEAM, DIM // 2, 3 * 128),
            vmem(2, HALF, WIDTH),
            vmem(2, HALF, WIDTH),
            wide(LAYERS, WIDTH),
        ),
        in_specs=[far, scalar, scalar, far, far, far, far, far, far, far],
        out_specs=(whole,) * 5,
        scratch_shapes=[
            vmem(LAYERS, WIDTH, 3 * WIDTH),
            vmem(LAYERS, WIDTH, WIDTH),
            vmem(LAYERS, WIDTH, FF),
            vmem(LAYERS, FF, WIDTH),
            wide(LAYERS, FF),
            wide(LAYERS, WIDTH),
            vmem(2, HALF, WIDTH),
            vmem(2, HALF, WIDTH),
            wide(8, 128),
            wide(2, 8, 128),
            vmem(2, 2, HALF, WIDTH),
            wide(2 * HALF, WIDTH),
            wide(2 * HALF, WIDTH),
            vmem(LAYERS, WIDTH, rows),
            vmem(LAYERS, WIDTH, 2 * HALF),
            vmem(LAYERS, 2 * HALF, WIDTH),
            vmem(LAYERS, 2 * HALF, FF),
            wide(LAYERS, 2 * HALF, WIDTH),
            wide(LAYERS, 2 * HALF, FF),
            wide(LAYERS, 2 * HALF, WIDTH),
            vmem(2 * HALF, WIDTH),
            vmem(2 * HALF, FF),
            vmem(2 * HALF, WIDTH),
            vmem(HALF, 3 * WIDTH),
            vmem(2, TEAM, OWN, PACK, 128),
            vmem(2, TEAM, OWN, DIM, 128),
            vmem(2, TEAM, OWN, PACK, 128),
            vmem(2, TEAM, OWN, DIM, 128),
            vmem(2, TEAM, OWN, DIM, 128),
            vmem(LAYERS, OWN, rows, 128),
            vmem(LAYERS, OWN, 128, rows),
            vmem(LAYERS, OWN, 128, rows),
            vmem(OWN, 128, rows),
            wide(LAYERS, OWN, DIM, rows),
            wide(LAYERS, OWN, 1, rows),
            wide(OWN, rows, 128),
            wide(OWN, DIM, rows),
            wide(rows, TILE),
            vmem(LAYERS, 2, 2, 4, 2, CHUNK, 128),
            vmem(2, 4, 2, CHUNK, 128),
            vmem(4, 2, TOTALS[0], 128),
            vmem(4, TOTALS[1], 128),
            vmem(4, TOTALS[0], 128),
            vmem(2, 4, TOTALS[1], 128),
            vmem(LAYERS, 4, CHUNK, 128),
            vmem(4, 2, 2, TOTALS[2], 128),
            vmem(2, TOTALS[2], 128),
            vmem(TOTALS[2], 128),
            vmem(LAYERS, 4, 2, DIM, 3 * 128),
            vmem(LAYERS, 4, 2, DIM // 2, 3 * 128),
            vmem(LAYERS, 4, 2, DIM // 2, 3 * 128),
            vmem(LAYERS, 2, DIM // 2, 3 * 128),
            wide(LAYERS, SMALL),
            wide(3, LAYERS, SMALL),
            wide(4, LAYERS, SMALL),
            wide(3, LAYERS, SMALL),
            dma((LAYERS + 1, 4)),
            dma((5, 2)),
            dma((5, 2)),
            dma((4, LAYERS, 2, OWN)),
            dma((4, LAYERS, 2, OWN)),
            dma((len(PARTS),)),
            dma((len(PARTS),)),
            dma((len(PARTS), 3)),
            dma((len(PARTS), 3)),
            dma((len(PARTS), 3)),
            dma((len(PARTS), 3)),
            dma((len(PARTS), 3, 4)),
            dma((len(PARTS), 3, 4)),
            dma((len(PARTS), 3)),
            dma((len(PARTS), 3)),
            dma((LAYERS, 2, 3)),
            dma((LAYERS, 2, 3)),
            dma((LAYERS,)),
            dma((LAYERS,)),
            dma((LAYERS, 4)),
            dma((LAYERS, 4)),
            dma((LAYERS, 8)),
            dma((LAYERS, 8)),
            dma((6,)),
            dma((6,)),
            pltpu.SemaphoreType.REGULAR((2,)),
        ],
        compiler_params=pltpu.CompilerParams(
            collective_id=0, has_side_effects=True, vmem_limit_bytes=61 * 1024 * 1024
        ),
        name="layers",
    )(
        tokens, seq_len, alphas, up_bias, down_bias, cotangent,
        qkv_weight, out_weight, up_weight, down_weight,
    )
    return tuple(
        pl.pallas_call(
            results_kernel,
            out_shape=(
                shape((2 * HALF, WIDTH), BF16),
                shape((2 * HALF, WIDTH), F32),
                shape((LAYERS, DIM, 3 * WIDTH), F32),
                shape((LAYERS, DIM, WIDTH), F32),
                shape((LAYERS, DIM, FF), F32),
                shape((LAYERS, FF // RUNS), F32),
                shape((LAYERS, FF // RUNS, WIDTH), F32),
                shape((LAYERS, DIM), F32),
                shape((LAYERS, 2), F32),
            ),
            in_specs=[whole] * 5,
            out_specs=(far, far, far, far, far, whole, far, whole, whole),
            scratch_shapes=[
                vmem(2 * HALF, WIDTH),
                wide(2 * HALF, WIDTH),
                wide(LAYERS, DIM, 3 * WIDTH),
                wide(LAYERS, DIM, WIDTH),
                wide(LAYERS, DIM, FF),
                wide(LAYERS, FF // RUNS, WIDTH),
                dma((10,)),
            ],
            compiler_params=pltpu.CompilerParams(vmem_limit_bytes=24 * 1024 * 1024),
            name="results",
        )(final, heads, out_block, grad_block, small)
    )


def layout(seq_len, local_count, cycle_size):
    piece_rows = seq_len[0] // cycle_size
    end_rows = jnp.cumsum(piece_rows)
    start_rows = end_rows - piece_rows
    local_rows = jnp.arange(local_count, dtype=jnp.int32)
    segment = jnp.sum((local_rows[:, None] >= end_rows[None, :]).astype(jnp.int32), axis=1)
    picked = segment[:, None] == jnp.arange(seq_len.shape[1], dtype=jnp.int32)[None, :]
    offset = local_rows - jnp.sum(jnp.where(picked, start_rows[None, :], 0), axis=1)
    span_rows = jnp.sum(jnp.where(picked, piece_rows[None, :], 0), axis=1)
    return (segment, offset, span_rows)


def gelu_exact(values):
    return jax.nn.gelu(values, approximate=False)


def key_block(whole, geometry, block_index, head_count):
    query_seg, query_pos, seg_all, pos_all, block_rows, score_scale = geometry
    first_row = block_index * block_rows
    key_piece = lax.dynamic_slice_in_dim(whole, first_row, block_rows, 0)
    key_seg = lax.dynamic_slice_in_dim(seg_all, first_row, block_rows, 0)
    key_pos = lax.dynamic_slice_in_dim(pos_all, first_row, block_rows, 0)
    half_width = key_piece.shape[1] // 2
    keys_part = key_piece[:, :half_width].reshape(block_rows, head_count, -1)
    values_part = key_piece[:, half_width:].reshape(block_rows, head_count, -1)
    return (keys_part, values_part, key_seg, key_pos)


def block_scores(queries, keys_part, key_seg, key_pos, geometry):
    query_seg, query_pos, seg_all, pos_all, block_rows, score_scale = geometry
    scores = (
        jnp.einsum("qhd,khd->hqk", queries, keys_part, preferred_element_type=jnp.float32)
        * score_scale
    )
    allowed = (query_seg[:, None] == key_seg[None, :]) & (key_pos[None, :] <= query_pos[:, None])
    return (scores, allowed[None])


def attend(queries, whole, geometry):
    row_count, head_count, head_dim = queries.shape
    block_count = whole.shape[0] // geometry[4]

    def statistics(running, block_index):
        largest, totals = running
        keys_part, values_part, key_seg, key_pos = key_block(
            whole, geometry, block_index, head_count
        )
        scores, allowed = block_scores(queries, keys_part, key_seg, key_pos, geometry)
        newest = jnp.maximum(largest, jnp.max(jnp.where(allowed, scores, NEGATIVE), axis=2))
        weights = jnp.where(allowed, jnp.exp(scores - newest[:, :, None]), 0.0)
        totals = totals * jnp.exp(largest - newest) + jnp.sum(weights, axis=2)
        return ((newest, totals), None)

    initial = (
        jnp.full((head_count, row_count), NEGATIVE, jnp.float32),
        jnp.zeros((head_count, row_count), jnp.float32),
    )
    (largest, totals), unused = lax.scan(statistics, initial, jnp.arange(block_count))
    log_total = largest + jnp.log(totals)

    def weighted(output_sum, block_index):
        keys_part, values_part, key_seg, key_pos = key_block(
            whole, geometry, block_index, head_count
        )
        scores, allowed = block_scores(queries, keys_part, key_seg, key_pos, geometry)
        probs = jnp.where(allowed, jnp.exp(scores - log_total[:, :, None]), 0.0).astype(
            jnp.bfloat16
        )
        output_sum = output_sum + jnp.einsum(
            "hqk,khd->qhd", probs, values_part, preferred_element_type=jnp.float32
        )
        return (output_sum, None)

    output_sum, unused = lax.scan(
        weighted, jnp.zeros((row_count, head_count, head_dim), jnp.float32), jnp.arange(block_count)
    )
    return (output_sum, log_total)


def attend_back(queries, whole, log_total, delta_sum, grad_heads, geometry):
    row_count, head_count, head_dim = queries.shape
    block_rows = geometry[4]
    score_scale = geometry[5]
    block_count = whole.shape[0] // block_rows

    def gradients(query_grad, block_index):
        keys_part, values_part, key_seg, key_pos = key_block(
            whole, geometry, block_index, head_count
        )
        scores, allowed = block_scores(queries, keys_part, key_seg, key_pos, geometry)
        probs = jnp.where(allowed, jnp.exp(scores - log_total[:, :, None]), 0.0)
        grad_probs = jnp.einsum(
            "qhd,khd->hqk", grad_heads, values_part, preferred_element_type=jnp.float32
        )
        grad_scores = (probs * (grad_probs - delta_sum[:, :, None])).astype(jnp.bfloat16)
        query_grad = (
            query_grad
            + jnp.einsum("hqk,khd->qhd", grad_scores, keys_part, preferred_element_type=jnp.float32)
            * score_scale
        )
        key_grad = (
            jnp.einsum("hqk,qhd->khd", grad_scores, queries, preferred_element_type=jnp.float32)
            * score_scale
        )
        value_grad = jnp.einsum(
            "hqk,qhd->khd",
            probs.astype(jnp.bfloat16),
            grad_heads,
            preferred_element_type=jnp.float32,
        )
        joined = jnp.concatenate(
            [key_grad.reshape(block_rows, -1), value_grad.reshape(block_rows, -1)], axis=1
        )
        return (query_grad, joined)

    query_grad, stacked = lax.scan(
        gradients,
        jnp.zeros((row_count, head_count, head_dim), jnp.float32),
        jnp.arange(block_count),
    )
    return (query_grad, stacked.reshape(whole.shape[0], -1))


def layer_forward(hidden, layer_index, weights, geometry):
    qkv_weight, out_weight, up_weight, up_bias, down_weight, down_bias, alphas = weights
    row_count, model_width = hidden.shape
    projection = qkv_weight[layer_index]
    rounded = hidden.astype(jnp.bfloat16)
    queries = (
        jnp.dot(rounded, projection[:, :model_width], preferred_element_type=jnp.float32)
        .astype(jnp.bfloat16)
        .reshape(row_count, HEADS, -1)
    )
    key_value = jnp.dot(
        rounded, projection[:, model_width:], preferred_element_type=jnp.float32
    ).astype(jnp.bfloat16)
    whole = lax.all_gather(key_value, "blk", axis=0, tiled=True)
    heads_out, log_total = attend(queries, whole, geometry)
    heads_rounded = heads_out.reshape(row_count, model_width).astype(jnp.bfloat16)
    branch = jnp.dot(heads_rounded, out_weight[layer_index], preferred_element_type=jnp.float32)
    alpha_pair = alphas[layer_index]
    middle = hidden + alpha_pair[0] * branch
    entered = middle.astype(jnp.bfloat16)
    gate_pre = (
        jnp.dot(entered, up_weight[layer_index], preferred_element_type=jnp.float32)
        + up_bias[layer_index]
    )
    activated = gelu_exact(gate_pre).astype(jnp.bfloat16)
    second = (
        jnp.dot(activated, down_weight[layer_index], preferred_element_type=jnp.float32)
        + down_bias[layer_index]
    )
    result = middle + alpha_pair[1] * second
    saved = (
        rounded,
        queries,
        key_value,
        whole,
        heads_out,
        heads_rounded,
        log_total,
        branch,
        entered,
        gate_pre,
        activated,
        second,
    )
    return (result, saved)


def layer_backward(grad_hidden, saved, layer_index, weights, geometry):
    qkv_weight, out_weight, up_weight, up_bias, down_weight, down_bias, alphas = weights
    (
        rounded,
        queries,
        key_value,
        saved_whole,
        heads_out,
        heads_rounded,
        log_total,
        branch,
        entered,
        gate_pre,
        activated,
        second,
    ) = saved
    row_count = grad_hidden.shape[0]
    alpha_pair = alphas[layer_index]
    grad_second = (alpha_pair[1] * grad_hidden).astype(jnp.bfloat16)
    alpha_second = jnp.sum(grad_hidden * second)
    bias_down = jnp.sum(grad_second.astype(jnp.float32), axis=0)
    grad_down = jnp.einsum("tf,td->fd", activated, grad_second, preferred_element_type=jnp.float32)
    grad_act = jnp.einsum(
        "td,fd->tf", grad_second, down_weight[layer_index], preferred_element_type=jnp.float32
    )
    unused, gelu_pull = jax.vjp(gelu_exact, gate_pre)
    grad_gate = gelu_pull(grad_act)[0].astype(jnp.bfloat16)
    bias_up = jnp.sum(grad_gate.astype(jnp.float32), axis=0)
    grad_up = jnp.einsum("td,tf->df", entered, grad_gate, preferred_element_type=jnp.float32)
    grad_middle = grad_hidden + jnp.einsum(
        "tf,df->td", grad_gate, up_weight[layer_index], preferred_element_type=jnp.float32
    )
    grad_branch = (alpha_pair[0] * grad_middle).astype(jnp.bfloat16)
    alpha_first = jnp.sum(grad_middle * branch)
    grad_proj_out = jnp.einsum(
        "te,td->ed", heads_rounded, grad_branch, preferred_element_type=jnp.float32
    )
    grad_heads = (
        jnp.einsum(
            "td,ed->te", grad_branch, out_weight[layer_index], preferred_element_type=jnp.float32
        )
        .astype(jnp.bfloat16)
        .reshape(queries.shape)
    )
    delta_sum = jnp.sum(grad_heads.astype(jnp.float32) * heads_out, axis=2).T
    whole = lax.all_gather(key_value, "blk", axis=0, tiled=True)
    query_grad, key_terms = attend_back(queries, whole, log_total, delta_sum, grad_heads, geometry)
    key_grads = lax.psum_scatter(
        key_terms.astype(jnp.bfloat16), "blk", scatter_dimension=0, tiled=True
    )
    grad_proj = jnp.concatenate(
        [query_grad.reshape(row_count, -1).astype(jnp.bfloat16), key_grads], axis=1
    )
    grad_qkv = jnp.einsum("td,te->de", rounded, grad_proj, preferred_element_type=jnp.float32)
    grad_input = grad_middle + jnp.einsum(
        "te,de->td", grad_proj, qkv_weight[layer_index], preferred_element_type=jnp.float32
    )
    layer_grads = (
        grad_qkv,
        grad_proj_out,
        grad_up,
        bias_up,
        grad_down,
        bias_down,
        jnp.stack([alpha_first, alpha_second]),
    )
    return (grad_input, layer_grads)


def reduce_all(layer_results, cycle_size):
    stacked = [
        jnp.stack([layer_entry[member] for layer_entry in layer_results], axis=0)
        for member in range(6)
    ]
    alpha_tiles = jnp.stack(
        [jnp.tile(layer_entry[6], cycle_size) for layer_entry in layer_results], axis=0
    )
    shares = (
        lax.psum_scatter(
            stacked[0].astype(jnp.bfloat16), "blk", scatter_dimension=1, tiled=True
        ).astype(jnp.float32),
        lax.psum_scatter(
            stacked[1].astype(jnp.bfloat16), "blk", scatter_dimension=1, tiled=True
        ).astype(jnp.float32),
        lax.psum_scatter(
            stacked[2].astype(jnp.bfloat16), "blk", scatter_dimension=1, tiled=True
        ).astype(jnp.float32),
        lax.psum_scatter(
            stacked[3].astype(jnp.bfloat16), "blk", scatter_dimension=1, tiled=True
        ).astype(jnp.float32),
        lax.psum_scatter(
            stacked[4].astype(jnp.bfloat16), "blk", scatter_dimension=1, tiled=True
        ).astype(jnp.float32),
        lax.psum_scatter(
            stacked[5].astype(jnp.bfloat16), "blk", scatter_dimension=1, tiled=True
        ).astype(jnp.float32),
        lax.psum_scatter(
            alpha_tiles.astype(jnp.bfloat16), "blk", scatter_dimension=1, tiled=True
        ).astype(jnp.float32),
    )
    return (
        lax.psum(shares[0].astype(jnp.bfloat16), "grp").astype(jnp.float32),
        lax.psum(shares[1].astype(jnp.bfloat16), "grp").astype(jnp.float32),
        lax.psum(shares[2].astype(jnp.bfloat16), "grp").astype(jnp.float32),
        lax.psum(shares[3].astype(jnp.bfloat16), "grp").astype(jnp.float32),
        lax.psum(shares[4].astype(jnp.bfloat16), "grp").astype(jnp.float32),
        lax.psum(shares[5].astype(jnp.bfloat16), "grp").astype(jnp.float32),
        lax.psum(shares[6].astype(jnp.bfloat16), "grp").astype(jnp.float32),
    )


def body(
    tokens,
    seq_len,
    qkv_weight,
    out_weight,
    up_weight,
    up_bias,
    down_weight,
    down_bias,
    alphas,
    cotangent,
):
    row_count, model_width = tokens.shape
    cycle_size = lax.axis_size("blk")
    cycle_place = lax.axis_index("blk")
    head_dim = model_width // HEADS
    total_rows = cycle_size * row_count
    block_rows = min(max(row_count, 512), total_rows)
    segment, offset, span_rows = layout(seq_len, row_count, cycle_size)
    query_pos = cycle_place * span_rows + offset
    seg_all = jnp.tile(segment, cycle_size)
    pos_all = jnp.repeat(jnp.arange(cycle_size, dtype=jnp.int32), row_count) * jnp.tile(
        span_rows, cycle_size
    ) + jnp.tile(offset, cycle_size)
    geometry = (segment, query_pos, seg_all, pos_all, block_rows, head_dim ** (-0.5))
    weights = (qkv_weight, out_weight, up_weight, up_bias, down_weight, down_bias, alphas)
    hidden = tokens.astype(jnp.float32)
    saved_layers = []
    for layer_index in range(LAYERS):
        hidden, saved = layer_forward(hidden, layer_index, weights, geometry)
        saved_layers.append(saved)
    output = hidden.astype(jnp.bfloat16)
    grad_hidden = cotangent.astype(jnp.float32)
    layer_results = []
    for layer_index in reversed(range(LAYERS)):
        grad_hidden, layer_grads = layer_backward(
            grad_hidden, saved_layers[layer_index], layer_index, weights, geometry
        )
        layer_results.insert(0, layer_grads)
    finals = reduce_all(layer_results, cycle_size)
    return (
        output,
        grad_hidden,
        finals[0],
        finals[1],
        finals[2],
        finals[3],
        finals[4],
        finals[5],
        finals[6],
    )


def solution(mesh):
    placed = (
        P(("grp", "blk"), None),
        P("grp", None),
        P(),
        P(),
        P(),
        P(),
        P(),
        P(),
        P(),
        P(("grp", "blk"), None),
    )
    sizes = (mesh.shape["grp"], mesh.shape["blk"])
    return jax.shard_map(
        fast_body if sizes == (4, RUNS) else body,
        mesh=mesh,
        in_specs=placed,
        out_specs=(
            P(("grp", "blk"), None),
            P(("grp", "blk"), None),
            P(None, "blk", None),
            P(None, "blk", None),
            P(None, "blk", None),
            P(None, "blk"),
            P(None, "blk", None),
            P(None, "blk"),
            P(),
        ),
        check_vma=False,
    )
```

```python
import functools

import jax
import jax.numpy as jnp
from jax import lax
from jax.experimental import pallas as pl
from jax.experimental.pallas import tpu as pltpu
from jax.sharding import PartitionSpec as P

HEADS = 8
LAYERS = 2
NEGATIVE = -1e30
MESH = pl.DeviceIdType.MESH
F32 = jnp.float32
BF16 = jnp.bfloat16

HALF = 128
RUNS = 8
TEAM = 4
OWN = RUNS // TEAM
DIM = 64
WIDTH = 512
FF = 2048
CUT = 512
TILE = 256
TILES = HALF * RUNS // TILE
PACK = HALF + DIM
CHUNK = 576
SMALL = FF + WIDTH + 128
PARTS = ((1, 0, 320), (1, 320, 256), (0, 0, 320), (0, 320, 256))
SHARES = ((160, 0, 160), (128, 16, 112), (144, 80, 96), (112, 80, 64))


def spans():
    places, totals = {}, [0, 0, 0]
    for part, counts in enumerate(SHARES):
        first = PARTS[part][1]
        for route, count in enumerate(counts):
            places[part, route] = (first, totals[route], count)
            first += count
            totals[route] += count
    return places, totals


SPANS, TOTALS = spans()

SLOPE_AT = 0.28
TAIL = (
    0.11652077851573843,
    0.06749675579450809,
    0.2689101589486142,
    -0.23699347299932225,
    0.3898740127620002,
    -0.10580824228351815,
)


def nn(a, b):
    return lax.dot_general(a, b, (((1,), (0,)), ((), ())), preferred_element_type=F32)


def nt(a, b):
    return lax.dot_general(a, b, (((1,), (1,)), ((), ())), preferred_element_type=F32)


def beside(first, other):
    low = lax.broadcasted_iota(jnp.int32, first.shape, 1) < DIM
    return (
        jnp.where(low, first, pltpu.roll(other, DIM, 1)),
        jnp.where(low, pltpu.roll(first, DIM, 1), other),
    )


def layers_kernel(
    tokens, seq_len, alphas, up_bias_hbm, down_bias_hbm, cotangent, qkv_hbm, out_hbm, up_hbm, down_hbm,
    final, heads_all, out_in, grad_in, small_final,
    wqkv, wout, wup, wdown, up_bias, down_bias,
    tok_in, cot_in, flag_out, flag_in, back_out,
    hidden, grad, hid_all, attn_t, entered, act, branch, slope, second,
    dz, du, da, dqkv,
    pack_out, head_out, pack_in, o_in, do_in,
    kv, kv_t, rq, ro, o_t, lse, acc, dq_t, bias,
    parts, core_in, xa_in, xb_in, ya_in, yb_in, z_in, third_z, third_x, third_y,
    heads_out, heads_x, heads_z, heads_sum, small, small_in, small_z, small_sum,
    w_sem, move_send, move_recv, a2a_send, a2a_recv, core_send, core_recv, x_send, x_recv, y_send, y_recv,
    z_send, z_recv, fin_send, fin_recv, hid_send, hid_recv, hx_send, hx_recv, hz_send, hz_recv, hf_send, hf_recv,
    small_send, small_recv, core_free,
):
    grp = lax.axis_index("grp")
    blk = lax.axis_index("blk")
    core = lax.rem(grp, 2)
    side = lax.div(grp, 2)
    yy = lax.rem(blk, 2)
    zz = lax.div(blk, 2)
    member = 2 * core + yy
    far_side = 2 * (1 - side) + core

    def place(c, x, z, y):
        return (2 * x + c, 2 * z + y)

    core_peer = place(1 - core, side, zz, yy)
    x_peer = place(core, 1 - side, zz, yy)
    y_peer = place(core, side, zz, 1 - yy)

    def remote(source, target, send, recv, peer):
        return pltpu.make_async_remote_copy(
            src_ref=source,
            dst_ref=target,
            send_sem=send,
            recv_sem=recv,
            device_id=peer,
            device_id_type=MESH,
        )

    def credit(semaphore, peer, count=1):
        pl.semaphore_signal(semaphore, inc=count, device_id=peer, device_id_type=MESH)

    def moved(kind, slot, source, target, at, core_at, z_at):
        here = jnp.logical_and(core_at == core, z_at == zz)

        @pl.when(here)
        def _():
            pltpu.make_async_copy(source, target.at[at], move_recv.at[kind, at]).start()

        @pl.when(jnp.logical_not(here))
        def _():
            pltpu.make_async_remote_copy(
                src_ref=source,
                dst_ref=target.at[at],
                send_sem=move_send.at[kind, slot],
                recv_sem=move_recv.at[kind, at],
                device_id=place(core_at, side, z_at, yy),
                device_id_type=MESH,
            ).start()

    def move_left(kind, slot, source, core_at, z_at):
        here = jnp.logical_and(core_at == core, z_at == zz)

        @pl.when(jnp.logical_not(here))
        def _():
            pltpu.make_async_copy(source, source, move_send.at[kind, slot]).wait()

    def move_arrived(kind, at, target):
        pltpu.make_async_copy(target.at[at], target.at[at], move_recv.at[kind, at]).wait()

    def to_team(kind, half, source, target):
        moved(kind, half, source, target, lax.div(zz, 2), lax.rem(zz, 2), 2 * half + core)

    def to_team_left(kind, half, source):
        move_left(kind, half, source, lax.rem(zz, 2), 2 * half + core)

    def to_owner(kind, chunk, source, target):
        moved(kind, chunk, source, target, lax.div(zz, 2), lax.rem(zz, 2), core + 2 * chunk)

    def to_owner_left(kind, chunk, source):
        move_left(kind, chunk, source, lax.rem(zz, 2), core + 2 * chunk)

    def half_of(ref, half):
        return ref.at[pl.ds(pl.multiple_of(HALF * half, HALF), HALF)]

    def rows_of(half):
        return pl.ds(pl.multiple_of(half * HALF, HALF), HALF)

    def slot_of(other):
        return lax.rem(other + TEAM - member, TEAM)

    def exchange(kind, layer, half, outgoing, incoming, head=None):
        at = () if head is None else (head,)
        incoming[(half, 0, *at)] = outgoing[(half, member, *at)]
        for step in range(1, TEAM):
            peer = lax.rem(member + step, TEAM)
            remote(
                outgoing.at[(half, peer, *at)],
                incoming.at[(half, TEAM - step, *at)],
                a2a_send.at[kind, layer, half, head or 0],
                a2a_recv.at[kind, layer, half, head or 0],
                place(lax.div(peer, 2), side, zz, lax.rem(peer, 2)),
            ).start()

    def arrived(kind, layer, half, incoming, head=None):
        at = () if head is None else (head,)
        whole = incoming.at[(half, pl.ds(1, TEAM - 1), *at)]
        pltpu.make_async_copy(whole, whole, a2a_recv.at[kind, layer, half, head or 0]).wait()

    def left(kind, layer, half, outgoing):
        for head in range(OWN) if kind in (0, 3) else (None,):
            at = () if head is None else (head,)
            whole = outgoing.at[(half, pl.ds(1, TEAM - 1), *at)]
            pltpu.make_async_copy(whole, whole, a2a_send.at[kind, layer, half, head or 0]).wait()

    def tokens_of(chunk, other):
        return pl.ds(pl.multiple_of(HALF * (TEAM * chunk + other), HALF), HALF)

    def hidden_copy(layer, chunk, which):
        whose = 2 * core + 1 - yy if which == 2 else member
        block = hid_all.at[layer, :, tokens_of(chunk, whose)]
        return remote(
            block,
            block,
            hid_send.at[layer, chunk, which],
            hid_recv.at[layer, chunk, which],
            y_peer if which == 0 else core_peer,
        )

    def hidden_start(layer, chunk):
        for which in range(2):
            hidden_copy(layer, chunk, which).start()

    def hidden_pass(layer, chunk):
        hidden_copy(layer, chunk, 0).wait()
        hidden_copy(layer, chunk, 2).start()

    def hidden_done(layer, chunk):
        for which in range(1, 3):
            hidden_copy(layer, chunk, which).wait()

    def project(layer, half):
        rows = rows_of(half)
        rounded = hidden[rows, :].astype(BF16)
        if layer == 1:
            left(0, 0, half, pack_out)
        queries = (nn(rounded, wqkv[layer, :, 0:WIDTH]) * (DIM ** -0.5)).astype(BF16).T
        for head in range(RUNS):
            pack_out[half, head // 2, head % 2, HALF:, :] = queries[DIM * head : DIM * head + DIM, :]
        for step in range(2):
            at = WIDTH * (step + 1)
            keys_values = nn(rounded, wqkv[layer, :, at : at + WIDTH]).astype(BF16)
            for head in range(4):
                pack_out[half, 2 * step + head // 2, head % 2, 0:HALF, :] = keys_values[
                    :, 128 * head : 128 * head + 128
                ]
        for head in range(OWN):
            exchange(0, layer, half, pack_out, pack_in, head)
        hid_all[layer, :, tokens_of(half, member)] = rounded.T

    def attend(layer, chunk):
        if layer == 1:
            left(1, 0, chunk, head_out)

        def one_head(head, carry):
            arrived(0, layer, chunk, pack_in, head)
            for other in range(TEAM):
                slot = slot_of(other)
                start = HALF * (TEAM * chunk + other)
                span = slice(start, start + HALF)
                block = pack_in[chunk, slot, head, 0:HALF, :]
                kv[layer, head, span, :] = block
                kv_t[layer, head, :, span] = block.T
                rq[layer, head, 0:DIM, span] = pack_in[chunk, slot, head, HALF:, :]

            def scores_of(i):
                count = TILE * (i + 1)
                tile = rq[layer, head, :, TILE * i : TILE * i + TILE]
                return nn(kv[layer, head, 0:count, :], tile) + bias[TILE * TILES - count :, :]

            ahead = [scores_of(i) for i in (2 * chunk, 2 * chunk + 1)]
            for i in (2 * chunk, 2 * chunk + 1):
                columns = slice(TILE * i, TILE * i + TILE)
                count = TILE * (i + 1)
                scores = ahead[i - 2 * chunk]
                largest = jnp.max(scores, axis=0, keepdims=True)
                weight = jnp.exp(scores - largest)
                total = jnp.sum(weight, axis=0, keepdims=True)
                summed = nn(kv_t[layer, head, DIM:, 0:count], weight.astype(BF16))
                summed = summed / total
                o_t[layer, head, :, columns] = summed
                lse[layer, head, :, columns] = largest + jnp.log(total)
                rounded = summed.astype(BF16)
                for part in range(2):
                    head_out[chunk, 2 * (i - 2 * chunk) + part, head] = rounded[
                        :, HALF * part : HALF * part + HALF
                    ]
            return carry

        for head in range(OWN):
            one_head(head, 0)
        exchange(1, layer, chunk, head_out, o_in)

    def feed(layer, half):
        rows = rows_of(half)
        arrived(1, layer, half, o_in)
        for head in range(RUNS):
            attn_t[layer, DIM * head : DIM * head + DIM, rows] = o_in[half, slot_of(head // 2), head % 2]
        attn = attn_t[layer, :, rows].T
        grown = nn(attn, wout[layer])
        branch[layer, rows, :] = grown
        middle = hidden[rows, :] + alphas[layer, 0] * grown
        rounded = middle.astype(BF16)
        entered[layer, rows, :] = rounded
        total = jnp.zeros((HALF, WIDTH), F32)

        def gate_of(step):
            cut = slice(CUT * step, CUT * step + CUT)
            return nn(rounded, wup[layer, :, cut]) + up_bias[layer : layer + 1, cut]

        coming = gate_of(0)
        for step in range(FF // CUT):
            cut = slice(CUT * step, CUT * step + CUT)
            gate = coming
            if step + 1 < FF // CUT:
                coming = gate_of(step + 1)
            bell = jnp.exp(gate * gate * -0.5)
            near = pl.reciprocal(1.0 + SLOPE_AT * jnp.abs(gate), approx=True)
            tail = jnp.full_like(gate, TAIL[5])
            for factor in TAIL[4::-1]:
                tail = tail * near + factor
            tail = bell * (tail * near)
            risen = jnp.where(gate > 0.0, 1.0 - tail, tail)
            slope[layer, rows, cut] = risen + gate * bell * 0.3989422804014327
            active = (gate * risen).astype(BF16)
            act[layer, rows, cut] = active
            total = total + nn(active, wdown[layer, cut, :])
        total = total + down_bias[layer : layer + 1, :]
        second[layer, rows, :] = total
        hidden[rows, :] = middle + alphas[layer, 1] * total

    def total_of(values):
        return jnp.sum(jnp.sum(values, axis=0, keepdims=True), axis=1, keepdims=True)

    def feed_back(layer):
        start = grad[...]
        if layer == 0:
            dz[...] = (alphas[layer, 1] * start).astype(BF16)
        scaled = dz[...]
        alpha_second = total_of(start * second[layer])
        small[layer : layer + 1, FF : FF + WIDTH] = jnp.sum(scaled.astype(F32), axis=0, keepdims=True)
        middle = start
        coming = nt(scaled, wdown[layer, 0:CUT, :])
        for step in range(FF // CUT):
            cut = slice(CUT * step, CUT * step + CUT)
            raw = coming
            if step + 1 < FF // CUT:
                coming = nt(scaled, wdown[layer, CUT * (step + 1) : CUT * (step + 2), :])
            gate = (raw * slope[layer, :, cut]).astype(BF16)
            du[:, cut] = gate
            small[layer : layer + 1, cut] = jnp.sum(gate.astype(F32), axis=0, keepdims=True)
            middle = middle + nt(gate, wup[layer, :, cut])
        grad[...] = middle
        mixed = (alphas[layer, 0] * middle).astype(BF16)
        da[...] = mixed
        spread = nt(wout[layer], mixed).astype(BF16)
        for chunk in (1, 0):
            left(*((1, 1) if layer == 1 else (2, 1)), chunk, head_out)
            for head in range(RUNS):
                head_out[chunk, head // 2, head % 2] = spread[
                    DIM * head : DIM * head + DIM, HALF * chunk : HALF * chunk + HALF
                ]
            exchange(2, layer, chunk, head_out, do_in)
        alpha_first = total_of(middle * branch[layer])
        column = lax.broadcasted_iota(jnp.int32, (1, 128), 1)
        small[layer : layer + 1, FF + WIDTH :] = jnp.where(
            column == 0, alpha_first, jnp.where(column == 1, alpha_second, 0.0)
        )

    def attend_back(layer, chunk):
        arrived(2, layer, chunk, do_in)
        left(*((0, 1) if layer == 1 else (3, 1)), chunk, pack_out)

        def one_head(head, carry):
            for other in range(TEAM):
                start = HALF * (TEAM * chunk + other)
                ro[head, DIM:, start : start + HALF] = do_in[chunk, slot_of(other), head]
            for i in (2 * chunk, 2 * chunk + 1):
                columns = slice(TILE * i, TILE * i + TILE)
                query_tile = rq[layer, head, :, columns]
                grad_tile = ro[head, :, columns]
                log_total = lse[layer, head, :, columns]
                delta = jnp.sum(
                    ro[head, DIM:, columns].astype(F32) * o_t[layer, head, :, columns],
                    axis=0,
                    keepdims=True,
                )
                count = TILE * (i + 1)
                keys = kv[layer, head, 0:count, :]
                weight = jnp.exp(nn(keys, query_tile) + bias[TILE * TILES - count :, :] - log_total)
                scored = (weight * (nn(keys, grad_tile) - delta)).astype(BF16)
                term = nt(scored, query_tile) + nt(weight.astype(BF16), grad_tile)
                if chunk == 1 and i == 2:
                    acc[head, 0:count, :] = term
                elif chunk == 1:
                    acc[head, 0 : count - TILE, :] += term[0 : count - TILE, :]
                    acc[head, count - TILE : count, :] = term[count - TILE :, :]
                else:
                    acc[head, 0:count, :] += term
                query_grad = nn(kv_t[layer, head, 0:DIM, 0:count], scored)
                dq_t[head, :, columns] = query_grad * (DIM ** -0.5)
            for other in range(TEAM):
                start = HALF * (TEAM * chunk + other)
                span = slice(start, start + HALF)
                pack_out[chunk, other, head, 0:HALF, :] = acc[head, span, :].astype(BF16)
                pack_out[chunk, other, head, HALF:, :] = dq_t[head, :, span].astype(BF16)
            exchange(3, layer, chunk, pack_out, pack_in, head)
            return carry

        for head in range(OWN):
            one_head(head, 0)

    def project_back(layer, half):
        for head in range(OWN):
            arrived(3, layer, half, pack_in, head)
        turned = jnp.concatenate(
            [pack_in[half, slot_of(head // 2), head % 2, HALF:, :] for head in range(RUNS)], axis=0
        )
        dqkv[:, 0:WIDTH] = turned.T
        for head in range(RUNS):
            at = WIDTH + 128 * head
            dqkv[:, at : at + 128] = pack_in[half, slot_of(head // 2), head % 2, 0:HALF, :]
        rows = rows_of(half)
        grad[rows, :] = grad[rows, :] + nt(dqkv[...], wqkv[layer])

    def scatter_rows(layer, result, first_row):
        for run in range(RUNS):
            for quarter in range(4):
                parts[layer, quarter % 2, quarter // 2, run // 2, run % 2, first_row : first_row + DIM, :] = result[
                    DIM * run : DIM * run + DIM, 128 * quarter : 128 * quarter + 128
                ].astype(BF16)

    def make(part):
        layer, first, count = PARTS[part]
        if first < 256:
            turned = entered[layer].T
        for row in range(first, min(first + count, 256), DIM):
            step = row // DIM
            scatter_rows(layer, nn(turned, du[:, CUT * step : CUT * step + CUT]), row)
        if first <= 256 < first + count:
            scatter_rows(layer, nn(attn_t[layer], da[...]), 256)
        if first >= 320:
            turned = dz[...].T
            for step in range(FF // CUT):
                result = nn(turned, act[layer, :, CUT * step : CUT * step + CUT])
                for block in range(CUT // 128):
                    run, row = 2 * step + block // 2, 320 + 128 * (block % 2)
                    for quarter in range(4):
                        parts[layer, quarter % 2, quarter // 2, run // 2, run % 2, row : row + 128, :] = result[
                            128 * quarter : 128 * quarter + 128, 128 * block : 128 * block + 128
                        ].astype(BF16)
        if layer == 0:
            pl.semaphore_wait(core_free.at[0 if first < 320 else 1], 1)
        core_copy(part).start()

    def heads_grads(layer):
        for chunk in range(2):
            hidden_done(layer, chunk)
        blocks = [(run // TEAM, run % TEAM) for run in range(RUNS)]
        keys_values = jnp.concatenate(
            [
                jnp.concatenate([pack_out[chunk, other, head, 0:HALF, :] for chunk, other in blocks], axis=0)
                for head in range(OWN)
            ],
            axis=1,
        )
        queries = jnp.concatenate(
            [
                jnp.concatenate([pack_out[chunk, other, head, HALF:, :] for chunk, other in blocks], axis=1)
                for head in range(OWN)
            ],
            axis=0,
        )
        both = nn(hid_all[layer], keys_values)
        q_part = nt(hid_all[layer], queries)
        for number, values in enumerate((q_part, both[:, 0:128], both[:, 128:256])):
            for run in range(RUNS):
                heads_out[layer, run // 2, run % 2, :, 128 * number : 128 * number + 128] = values[
                    DIM * run : DIM * run + DIM, :
                ].astype(BF16)
        heads_x_copy(layer).start()

    def half_rows(which):
        return pl.ds(pl.multiple_of(32 * which, 32), 32)

    def heads_x_copy(layer):
        return remote(
            heads_out.at[layer, :, :, half_rows(1 - side)],
            heads_x.at[layer],
            hx_send.at[layer],
            hx_recv.at[layer],
            x_peer,
        )

    def heads_z_copy(layer, step):
        peer = lax.rem(zz + step, 4)
        return remote(
            heads_out.at[layer, peer, :, half_rows(side)],
            heads_z.at[layer, 4 - step],
            hz_send.at[layer, step],
            hz_recv.at[layer, 4 - step],
            place(core, side, peer, yy),
        )

    def heads_last_copy(layer, number):
        x, c, y = number // 4, number // 2 % 2, number % 2
        return remote(
            heads_sum.at[layer, 1 - yy if y else yy],
            heads_all.at[layer, side, member],
            hf_send.at[layer, number],
            hf_recv.at[layer, number],
            place(1 - core if c else core, 1 - side if x else side, zz, 1 - yy if y else yy),
        )

    def heads_second(layer):
        heads_x_copy(layer).wait()
        heads_out[layer, :, :, half_rows(side), :] += heads_x[layer]
        for step in range(1, 4):
            heads_z_copy(layer, step).start()

    def heads_third(layer):
        for step in range(1, 4):
            heads_z_copy(layer, step).wait()
        total = heads_out[layer, zz, :, half_rows(side), :].astype(F32)
        for slot in range(1, 4):
            total = total + heads_z[layer, slot].astype(F32)
        heads_sum[layer] = total.astype(BF16)
        heads_all[layer, side, member] = heads_sum[layer, yy]
        for number in range(1, 8):
            heads_last_copy(layer, number).start()

    def heads_done(layer):
        for number in range(1, 8):
            heads_last_copy(layer, number).wait()

    def rows_in(part, route):
        first, room, count = SPANS[part, route]
        return pl.ds(first, count), pl.ds(room, count)

    def used(part, route):
        return SHARES[part][route] > 0

    def core_copy(part):
        layer, first, count = PARTS[part]
        rows = pl.ds(first, count)
        return remote(
            parts.at[layer, 1 - core, :, :, :, rows],
            core_in.at[:, :, :, rows],
            core_send.at[part],
            core_recv.at[part],
            core_peer,
        )

    def x_copy(part, route):
        layer = PARTS[part][0]
        rows, room = rows_in(part, route)
        ends = (x_send.at[part, route], x_recv.at[part, route], x_peer)
        mine = parts.at[layer, core, 1 - side]
        if route == 0:
            return remote(mine.at[:, :, rows], xa_in.at[:, :, room], *ends)
        if route == 1:
            return remote(mine.at[:, yy, rows], xb_in.at[:, room], *ends)
        return remote(mine.at[zz, :, rows], third_x.at[:, room], *ends)

    def y_copy(part, route):
        layer = PARTS[part][0]
        rows, room = rows_in(part, route)
        ends = (y_send.at[part, route], y_recv.at[part, route], y_peer)
        mine = parts.at[layer, core]
        if route == 0:
            return remote(mine.at[side, :, 1 - yy, rows], ya_in.at[:, room], *ends)
        if route == 1:
            return remote(mine.at[:, :, 1 - yy, rows], yb_in.at[:, :, room], *ends)
        return remote(mine.at[side, zz, 1 - yy, rows], third_y.at[room], *ends)

    def z_copy(part, route, step):
        layer = PARTS[part][0]
        rows, room = rows_in(part, route)
        peer = lax.rem(zz + step, 4)
        ends = (z_send.at[part, route, step], z_recv.at[part, route, 4 - step], place(core, side, peer, yy))
        if route == 2:
            return remote(parts.at[layer, core, :, peer, :, rows], third_z.at[4 - step, :, :, room], *ends)
        return remote(parts.at[layer, core, side, peer, yy, rows], z_in.at[layer, 4 - step, rows], *ends)

    def final_copy(part, which):
        layer, first, count = PARTS[part]
        block = final.at[layer, far_side if which == 2 else grp, pl.ds(first, count)]
        return remote(
            block,
            block,
            fin_send.at[part, which],
            fin_recv.at[part, which],
            x_peer if which == 0 else core_peer,
        )

    def core_done(part):
        layer, first, count = PARTS[part]
        rows = pl.ds(first, count)
        core_copy(part).wait()
        for across in (1 - side, side):
            parts[layer, core, across, :, :, rows, :] += core_in[across, :, :, rows, :]
            if used(part, 0) and across is not side:
                x_copy(part, 0).start()
        if used(part, 1):
            y_copy(part, 1).start()
        if used(part, 2):
            for step in range(1, 4):
                z_copy(part, 2, step).start()
        if layer == 1:
            freed = 0 if first < 320 else 1
            followers = [1 for other in PARTS if other[0] == 0 and (other[1] >= 320) == (freed == 1)]
            credit(core_free.at[freed], core_peer, len(followers))

    def first_x(part):
        if used(part, 0):
            layer = PARTS[part][0]
            rows, room = rows_in(part, 0)
            x_copy(part, 0).wait()
            for y in (1 - yy, yy):
                parts[layer, core, side, :, y, rows, :] += xa_in[:, y, room, :]
                if y is not yy:
                    y_copy(part, 0).start()

    def first_y(part):
        if used(part, 1):
            layer = PARTS[part][0]
            rows, room = rows_in(part, 1)
            y_copy(part, 1).wait()
            for across in (1 - side, side):
                parts[layer, core, across, :, yy, rows, :] += yb_in[across, :, room, :]
                if across is not side:
                    x_copy(part, 1).start()

    def first_z(part):
        if used(part, 2):
            layer = PARTS[part][0]
            rows, room = rows_in(part, 2)
            for step in range(1, 4):
                z_copy(part, 2, step).wait()
            for across in (1 - side, side):
                total = parts[layer, core, across, zz, :, rows, :].astype(F32)
                for slot in range(1, 4):
                    total = total + third_z[slot, across, :, room, :].astype(F32)
                parts[layer, core, across, zz, :, rows, :] = total.astype(BF16)
                if across is not side:
                    x_copy(part, 2).start()

    def second_x(part):
        if used(part, 0):
            layer = PARTS[part][0]
            rows, room = rows_in(part, 0)
            y_copy(part, 0).wait()
            parts[layer, core, side, :, yy, rows, :] += ya_in[:, room, :]
            for step in range(1, 4):
                z_copy(part, 0, step).start()

    def second_y(part):
        if used(part, 1):
            layer = PARTS[part][0]
            rows, room = rows_in(part, 1)
            x_copy(part, 1).wait()
            parts[layer, core, side, :, yy, rows, :] += xb_in[:, room, :]
            for step in range(1, 4):
                z_copy(part, 1, step).start()

    def second_z(part):
        if used(part, 2):
            layer = PARTS[part][0]
            rows, room = rows_in(part, 2)
            x_copy(part, 2).wait()
            for y in (1 - yy, yy):
                parts[layer, core, side, zz, y, rows, :] += third_x[y, room, :]
                if y is not yy:
                    y_copy(part, 2).start()

    def third_done(part):
        layer = PARTS[part][0]
        for route in range(3):
            if not used(part, route):
                continue
            rows, room = rows_in(part, route)
            if route == 2:
                y_copy(part, 2).wait()
                final[layer, grp, rows, :] = parts[layer, core, side, zz, yy, rows, :] + third_y[room, :]
            else:
                for step in range(1, 4):
                    z_copy(part, route, step).wait()
                total = parts[layer, core, side, zz, yy, rows, :].astype(F32)
                for slot in range(1, 4):
                    total = total + z_in[layer, slot, rows, :].astype(F32)
                final[layer, grp, rows, :] = total.astype(BF16)
        if PARTS[part][1] >= 320:
            for row in (320, 448):
                final[layer, grp, row : row + 128, :] = final[layer, grp, row : row + 128, :].T
        for which in range(2):
            final_copy(part, which).start()

    def final_pass(part):
        final_copy(part, 0).wait()
        final_copy(part, 2).start()

    def final_done(part):
        for which in range(1, 3):
            final_copy(part, which).wait()

    def small_copy(stage):
        peer = (core_peer, x_peer, y_peer)[stage]
        return remote(
            small_sum.at[stage], small_in.at[stage], small_send.at[stage], small_recv.at[stage], peer
        )

    def small_z_copy(step):
        return remote(
            small_z.at[zz],
            small_z.at[zz],
            small_send.at[2 + step],
            small_recv.at[2 + step],
            place(core, side, lax.rem(zz + step, 4), yy),
        )

    def small_start():
        small_sum[0] = small[...]
        small_copy(0).start()

    def small_next(stage):
        small_copy(stage).wait()
        total = small_sum[stage] + small_in[stage]
        if stage < 2:
            small_sum[stage + 1] = total
            small_copy(stage + 1).start()
        else:
            small_z[zz] = total
            for step in range(1, 4):
                small_z_copy(step).start()

    def small_done():
        for step in range(1, 4):
            small_z_copy(step).wait()
        small_sum[0] = (small_z[0] + small_z[1]) + (small_z[2] + small_z[3])
        small_final[:, 0:256] = small_sum[0, :, pl.ds(pl.multiple_of(blk * 256, 256), 256)]
        pair = small_sum[0, :, pl.ds(pl.multiple_of(FF + 128 * zz, 128), 128)]
        small_final[:, 256:384] = jnp.where(yy == 1, pltpu.roll(pair, DIM, 1), pair)
        small_final[:, 384:512] = small_sum[0, :, FF + WIDTH :]

    def halves(*phases, first=0):
        def both(step, carry):
            for phase in phases:
                phase(lax.rem(step + first, 2))
            return carry

        lax.fori_loop(0, 2, both, 0)

    def begin(half):
        move_arrived(0, half, tok_in)
        hidden[rows_of(half), :] = tok_in[half].astype(F32)

    def finish(half):
        back_out[0, half] = hidden[rows_of(half), :].astype(BF16)
        to_owner(3, half, back_out.at[0, half], out_in)

    def turn_round(layer, half):
        move_arrived(2, half, cot_in)
        rows = rows_of(half)
        grad[rows, :] = cot_in[half].astype(F32)
        dz[rows, :] = (alphas[layer, 1] * grad[rows, :]).astype(BF16)

    def hand_back(half):
        back_out[1, half] = grad[rows_of(half), :].astype(BF16)
        to_owner(4, half, back_out.at[1, half], grad_in)

    barrier = pltpu.get_barrier_semaphore()
    for step in range(1, 4):
        credit(barrier, place(core, side, lax.rem(zz + step, 4), yy))
    for step in range(4):
        credit(barrier, place(1 - core, side, lax.rem(zz + step, 4), yy))
    for peer in (
        x_peer,
        y_peer,
        place(1 - core, side, zz, 1 - yy),
        place(1 - core, 1 - side, zz, yy),
        place(core, 1 - side, zz, 1 - yy),
        place(1 - core, 1 - side, zz, 1 - yy),
    ):
        credit(barrier, peer)

    weight_copies = {}
    for layer in range(LAYERS):
        for number, (source, target) in enumerate(
            ((qkv_hbm, wqkv), (out_hbm, wout), (up_hbm, wup), (down_hbm, wdown))
        ):
            weight_copies[layer, number] = pltpu.make_async_copy(
                source.at[layer], target.at[layer], w_sem.at[layer, number]
            )
    bias_copies = [
        pltpu.make_async_copy(up_bias_hbm, up_bias, w_sem.at[2, 0]),
        pltpu.make_async_copy(down_bias_hbm, down_bias, w_sem.at[2, 1]),
    ]
    weight_copies[0, 0].start()
    pl.semaphore_wait(barrier, 13)
    upper = lax.div(zz, 2)
    for half in (1 - upper, upper):
        to_team(0, half, half_of(tokens, half), tok_in)
    for layer, number in ((1, 0), (0, 1), (0, 2), (0, 3), (1, 1), (1, 2), (1, 3)):
        weight_copies[layer, number].start(priority=1)
    for copy in bias_copies:
        copy.start(priority=1)
    end_second = lax.div(seq_len[0, 0] + seq_len[0, 1], RUNS)
    flag_out[...] = jnp.full((8, 128), end_second.astype(F32), F32)
    for half in (1 - upper, upper):
        to_team(1, half, flag_out, flag_in)
    for layer in range(LAYERS):
        for head in range(OWN):
            rq[layer, head, DIM:, :] = jnp.zeros((DIM, HALF * RUNS), BF16)
    for head in range(OWN):
        ro[head, 0:DIM, :] = jnp.zeros((DIM, HALF * RUNS), BF16)
    for layer in range(LAYERS):
        weight_copies[layer, 0].wait()
        pairs = [
            beside(
                wqkv[layer, :, WIDTH + 128 * pair : WIDTH + 128 * pair + 128].astype(F32),
                wqkv[layer, :, 2 * WIDTH + 128 * pair : 2 * WIDTH + 128 * pair + 128].astype(F32),
            )
            for pair in range(TEAM)
        ]
        for head in range(RUNS):
            at = WIDTH + 128 * head
            wqkv[layer, :, at : at + 128] = pairs[head // 2][head % 2].astype(BF16)
    halves(begin, functools.partial(project, 0), first=upper)
    for half in (1 - upper, upper):
        to_team(2, half, half_of(cotangent, half), cot_in)

    move_arrived(1, 0, flag_in)
    move_arrived(1, 1, flag_in)
    border = jnp.concatenate([flag_in[0, 0:1, :]] * 2, axis=1) - (HALF * lax.div(zz, 2)).astype(F32)
    key_row = lax.broadcasted_iota(jnp.int32, (TILE, TILE), 0)
    query_col = lax.broadcasted_iota(jnp.int32, (TILE, TILE), 1)
    later = key_row > query_col
    key_sub = lax.rem(key_row, HALF).astype(F32) >= border
    query_sub = lax.rem(query_col, HALF).astype(F32) >= border
    apart = jnp.logical_xor(key_sub, query_sub)
    for tile in range(TILES - 1):
        bias[TILE * tile : TILE * tile + TILE, :] = jnp.where(apart, NEGATIVE, 0.0)
    bias[TILE * (TILES - 1) :, :] = jnp.where(jnp.logical_or(later, apart), NEGATIVE, 0.0)

    for copy in (*bias_copies, *(weight_copies[0, number] for number in range(1, 4))):
        copy.wait()
    attend(0, 0)
    attend(0, 1)
    hidden_start(0, 0)
    halves(functools.partial(feed, 0), functools.partial(project, 1))
    for number in range(1, 4):
        weight_copies[1, number].wait()
    attend(1, 0)
    attend(1, 1)
    hidden_pass(0, 0)
    hidden_start(1, 0)
    halves(functools.partial(feed, 1), finish)
    hidden_start(0, 1)
    hidden_start(1, 1)
    hidden_pass(1, 0)

    halves(functools.partial(turn_round, 1))
    make(1)
    feed_back(1)
    hidden_pass(0, 1)
    hidden_pass(1, 1)
    core_done(1)
    make(0)
    attend_back(1, 1)
    first_y(1)
    core_done(0)
    attend_back(1, 0)
    second_y(1)
    first_x(1)
    project_back(1, 1)
    heads_grads(1)
    first_z(1)
    project_back(1, 0)
    feed_back(0)
    small_start()
    second_x(1)
    make(2)
    first_x(0)
    heads_second(1)
    first_z(0)
    attend_back(0, 1)
    small_next(0)
    core_done(2)
    second_x(0)
    make(3)
    attend_back(0, 0)
    small_next(1)
    project_back(0, 1)
    hand_back(1)
    first_z(2)
    heads_grads(0)
    small_next(2)
    first_x(2)
    core_done(3)
    first_y(2)
    heads_second(0)
    small_done()
    first_z(3)
    second_x(2)
    first_x(3)
    second_z(2)
    second_z(0)
    heads_third(1)
    second_z(1)
    first_y(3)
    heads_third(0)
    second_y(2)
    second_x(3)
    second_z(3)
    third_done(0)
    third_done(2)
    second_y(3)
    project_back(0, 0)
    hand_back(0)
    heads_done(1)
    third_done(1)
    third_done(3)
    final_pass(0)
    final_pass(2)
    final_pass(1)
    final_pass(3)
    final_done(2)
    final_done(1)
    heads_done(0)
    final_done(0)
    final_done(3)
    for half in range(2):
        move_arrived(3, half, out_in)
        move_arrived(4, half, grad_in)

    for half in range(2):
        left(2, 0, half, head_out)
        left(3, 0, half, pack_out)
        to_team_left(0, half, half_of(tokens, half))
        to_team_left(1, half, flag_out)
        to_team_left(2, half, half_of(cotangent, half))
        to_owner_left(3, half, back_out.at[0, half])
        to_owner_left(4, half, back_out.at[1, half])


def results_kernel(
    final, heads, out_block, grad_block, small,
    output, input_grad, qkv_grad, out_grad, up_grad, up_bias_grad, down_grad, down_bias_grad, alpha_grad,
    out_flat, grad_wide, qkv_wide, out_wide, up_wide, down_wide, out_sem,
):
    ends = []

    def write(source, target):
        ends.append(pltpu.make_async_copy(source, target, out_sem.at[len(ends)]))
        ends[-1].start()

    up_bias_grad[...] = small[:, 0:256]
    down_bias_grad[...] = small[:, 256 : 256 + DIM]
    alpha_grad[...] = small[:, 384:386]
    for layer in range(LAYERS):
        for quarter in range(4):

            def block(first, count):
                return final[layer, quarter, first : first + count, :].astype(F32)

            def columns(step):
                return slice(WIDTH * step + 128 * quarter, WIDTH * step + 128 * quarter + 128)

            for step in range(4):
                up_wide[layer, :, columns(step)] = block(DIM * step, DIM)
            out_wide[layer, :, columns(0)] = block(256, DIM)
            down_wide[layer, :, columns(0)] = block(320, 256)
        write(up_wide.at[layer], up_grad.at[layer])
        write(out_wide.at[layer], out_grad.at[layer])
        write(down_wide.at[layer], down_grad.at[layer])
    for half in range(2):
        rows = slice(HALF * half, HALF * half + HALF)
        grad_wide[rows, :] = grad_block[half].astype(F32)
        out_flat[rows, :] = out_block[half]
    write(grad_wide, input_grad)
    write(out_flat, output)
    for layer in range(LAYERS):
        for side in range(2):
            for member in range(TEAM):
                block = heads[layer, side, member].astype(F32)
                columns = (block[:, 0:128], *beside(block[:, 128:256], block[:, 256:384]))
                for step in range(3):
                    at = WIDTH * step + 128 * member
                    qkv_wide[layer, 32 * side : 32 * side + 32, at : at + 128] = columns[step]
        write(qkv_wide.at[layer], qkv_grad.at[layer])
    for end in ends:
        end.wait()


def fast_body(
    tokens, seq_len, qkv_weight, out_weight, up_weight, up_bias, down_weight, down_bias, alphas, cotangent
):
    whole = pl.BlockSpec(memory_space=pltpu.VMEM)
    scalar = pl.BlockSpec(memory_space=pltpu.SMEM)
    far = pl.BlockSpec(memory_space=pl.ANY)
    shape = jax.ShapeDtypeStruct
    rows = HALF * RUNS

    def vmem(*dims):
        return pltpu.VMEM(dims, BF16)

    def wide(*dims):
        return pltpu.VMEM(dims, F32)

    dma = pltpu.SemaphoreType.DMA
    final, heads, out_block, grad_block, small = pl.pallas_call(
        layers_kernel,
        out_shape=(
            vmem(LAYERS, 4, CHUNK, 128),
            vmem(LAYERS, 2, TEAM, DIM // 2, 3 * 128),
            vmem(2, HALF, WIDTH),
            vmem(2, HALF, WIDTH),
            wide(LAYERS, WIDTH),
        ),
        in_specs=[far, scalar, scalar, far, far, far, far, far, far, far],
        out_specs=(whole,) * 5,
        scratch_shapes=[
            vmem(LAYERS, WIDTH, 3 * WIDTH),
            vmem(LAYERS, WIDTH, WIDTH),
            vmem(LAYERS, WIDTH, FF),
            vmem(LAYERS, FF, WIDTH),
            wide(LAYERS, FF),
            wide(LAYERS, WIDTH),
            vmem(2, HALF, WIDTH),
            vmem(2, HALF, WIDTH),
            wide(8, 128),
            wide(2, 8, 128),
            vmem(2, 2, HALF, WIDTH),
            wide(2 * HALF, WIDTH),
            wide(2 * HALF, WIDTH),
            vmem(LAYERS, WIDTH, rows),
            vmem(LAYERS, WIDTH, 2 * HALF),
            vmem(LAYERS, 2 * HALF, WIDTH),
            vmem(LAYERS, 2 * HALF, FF),
            wide(LAYERS, 2 * HALF, WIDTH),
            wide(LAYERS, 2 * HALF, FF),
            wide(LAYERS, 2 * HALF, WIDTH),
            vmem(2 * HALF, WIDTH),
            vmem(2 * HALF, FF),
            vmem(2 * HALF, WIDTH),
            vmem(HALF, 3 * WIDTH),
            vmem(2, TEAM, OWN, PACK, 128),
            vmem(2, TEAM, OWN, DIM, 128),
            vmem(2, TEAM, OWN, PACK, 128),
            vmem(2, TEAM, OWN, DIM, 128),
            vmem(2, TEAM, OWN, DIM, 128),
            vmem(LAYERS, OWN, rows, 128),
            vmem(LAYERS, OWN, 128, rows),
            vmem(LAYERS, OWN, 128, rows),
            vmem(OWN, 128, rows),
            wide(LAYERS, OWN, DIM, rows),
            wide(LAYERS, OWN, 1, rows),
            wide(OWN, rows, 128),
            wide(OWN, DIM, rows),
            wide(rows, TILE),
            vmem(LAYERS, 2, 2, 4, 2, CHUNK, 128),
            vmem(2, 4, 2, CHUNK, 128),
            vmem(4, 2, TOTALS[0], 128),
            vmem(4, TOTALS[1], 128),
            vmem(4, TOTALS[0], 128),
            vmem(2, 4, TOTALS[1], 128),
            vmem(LAYERS, 4, CHUNK, 128),
            vmem(4, 2, 2, TOTALS[2], 128),
            vmem(2, TOTALS[2], 128),
            vmem(TOTALS[2], 128),
            vmem(LAYERS, 4, 2, DIM, 3 * 128),
            vmem(LAYERS, 4, 2, DIM // 2, 3 * 128),
            vmem(LAYERS, 4, 2, DIM // 2, 3 * 128),
            vmem(LAYERS, 2, DIM // 2, 3 * 128),
            wide(LAYERS, SMALL),
            wide(3, LAYERS, SMALL),
            wide(4, LAYERS, SMALL),
            wide(3, LAYERS, SMALL),
            dma((LAYERS + 1, 4)),
            dma((5, 2)),
            dma((5, 2)),
            dma((4, LAYERS, 2, OWN)),
            dma((4, LAYERS, 2, OWN)),
            dma((len(PARTS),)),
            dma((len(PARTS),)),
            dma((len(PARTS), 3)),
            dma((len(PARTS), 3)),
            dma((len(PARTS), 3)),
            dma((len(PARTS), 3)),
            dma((len(PARTS), 3, 4)),
            dma((len(PARTS), 3, 4)),
            dma((len(PARTS), 3)),
            dma((len(PARTS), 3)),
            dma((LAYERS, 2, 3)),
            dma((LAYERS, 2, 3)),
            dma((LAYERS,)),
            dma((LAYERS,)),
            dma((LAYERS, 4)),
            dma((LAYERS, 4)),
            dma((LAYERS, 8)),
            dma((LAYERS, 8)),
            dma((6,)),
            dma((6,)),
            pltpu.SemaphoreType.REGULAR((2,)),
        ],
        compiler_params=pltpu.CompilerParams(
            collective_id=0, has_side_effects=True, vmem_limit_bytes=61 * 1024 * 1024
        ),
        name="layers",
    )(
        tokens, seq_len, alphas, up_bias, down_bias, cotangent,
        qkv_weight, out_weight, up_weight, down_weight,
    )
    return tuple(
        pl.pallas_call(
            results_kernel,
            out_shape=(
                shape((2 * HALF, WIDTH), BF16),
                shape((2 * HALF, WIDTH), F32),
                shape((LAYERS, DIM, 3 * WIDTH), F32),
                shape((LAYERS, DIM, WIDTH), F32),
                shape((LAYERS, DIM, FF), F32),
                shape((LAYERS, FF // RUNS), F32),
                shape((LAYERS, FF // RUNS, WIDTH), F32),
                shape((LAYERS, DIM), F32),
                shape((LAYERS, 2), F32),
            ),
            in_specs=[whole] * 5,
            out_specs=(far, far, far, far, far, whole, far, whole, whole),
            scratch_shapes=[
                vmem(2 * HALF, WIDTH),
                wide(2 * HALF, WIDTH),
                wide(LAYERS, DIM, 3 * WIDTH),
                wide(LAYERS, DIM, WIDTH),
                wide(LAYERS, DIM, FF),
                wide(LAYERS, FF // RUNS, WIDTH),
                dma((10,)),
            ],
            compiler_params=pltpu.CompilerParams(vmem_limit_bytes=24 * 1024 * 1024),
            name="results",
        )(final, heads, out_block, grad_block, small)
    )


def layout(seq_len, local_count, cycle_size):
    piece_rows = seq_len[0] // cycle_size
    end_rows = jnp.cumsum(piece_rows)
    start_rows = end_rows - piece_rows
    local_rows = jnp.arange(local_count, dtype=jnp.int32)
    segment = jnp.sum((local_rows[:, None] >= end_rows[None, :]).astype(jnp.int32), axis=1)
    picked = segment[:, None] == jnp.arange(seq_len.shape[1], dtype=jnp.int32)[None, :]
    offset = local_rows - jnp.sum(jnp.where(picked, start_rows[None, :], 0), axis=1)
    span_rows = jnp.sum(jnp.where(picked, piece_rows[None, :], 0), axis=1)
    return (segment, offset, span_rows)


def gelu_exact(values):
    return jax.nn.gelu(values, approximate=False)


def key_block(whole, geometry, block_index, head_count):
    query_seg, query_pos, seg_all, pos_all, block_rows, score_scale = geometry
    first_row = block_index * block_rows
    key_piece = lax.dynamic_slice_in_dim(whole, first_row, block_rows, 0)
    key_seg = lax.dynamic_slice_in_dim(seg_all, first_row, block_rows, 0)
    key_pos = lax.dynamic_slice_in_dim(pos_all, first_row, block_rows, 0)
    half_width = key_piece.shape[1] // 2
    keys_part = key_piece[:, :half_width].reshape(block_rows, head_count, -1)
    values_part = key_piece[:, half_width:].reshape(block_rows, head_count, -1)
    return (keys_part, values_part, key_seg, key_pos)


def block_scores(queries, keys_part, key_seg, key_pos, geometry):
    query_seg, query_pos, seg_all, pos_all, block_rows, score_scale = geometry
    scores = (
        jnp.einsum("qhd,khd->hqk", queries, keys_part, preferred_element_type=jnp.float32)
        * score_scale
    )
    allowed = (query_seg[:, None] == key_seg[None, :]) & (key_pos[None, :] <= query_pos[:, None])
    return (scores, allowed[None])


def attend(queries, whole, geometry):
    row_count, head_count, head_dim = queries.shape
    block_count = whole.shape[0] // geometry[4]

    def statistics(running, block_index):
        largest, totals = running
        keys_part, values_part, key_seg, key_pos = key_block(
            whole, geometry, block_index, head_count
        )
        scores, allowed = block_scores(queries, keys_part, key_seg, key_pos, geometry)
        newest = jnp.maximum(largest, jnp.max(jnp.where(allowed, scores, NEGATIVE), axis=2))
        weights = jnp.where(allowed, jnp.exp(scores - newest[:, :, None]), 0.0)
        totals = totals * jnp.exp(largest - newest) + jnp.sum(weights, axis=2)
        return ((newest, totals), None)

    initial = (
        jnp.full((head_count, row_count), NEGATIVE, jnp.float32),
        jnp.zeros((head_count, row_count), jnp.float32),
    )
    (largest, totals), unused = lax.scan(statistics, initial, jnp.arange(block_count))
    log_total = largest + jnp.log(totals)

    def weighted(output_sum, block_index):
        keys_part, values_part, key_seg, key_pos = key_block(
            whole, geometry, block_index, head_count
        )
        scores, allowed = block_scores(queries, keys_part, key_seg, key_pos, geometry)
        probs = jnp.where(allowed, jnp.exp(scores - log_total[:, :, None]), 0.0).astype(
            jnp.bfloat16
        )
        output_sum = output_sum + jnp.einsum(
            "hqk,khd->qhd", probs, values_part, preferred_element_type=jnp.float32
        )
        return (output_sum, None)

    output_sum, unused = lax.scan(
        weighted, jnp.zeros((row_count, head_count, head_dim), jnp.float32), jnp.arange(block_count)
    )
    return (output_sum, log_total)


def attend_back(queries, whole, log_total, delta_sum, grad_heads, geometry):
    row_count, head_count, head_dim = queries.shape
    block_rows = geometry[4]
    score_scale = geometry[5]
    block_count = whole.shape[0] // block_rows

    def gradients(query_grad, block_index):
        keys_part, values_part, key_seg, key_pos = key_block(
            whole, geometry, block_index, head_count
        )
        scores, allowed = block_scores(queries, keys_part, key_seg, key_pos, geometry)
        probs = jnp.where(allowed, jnp.exp(scores - log_total[:, :, None]), 0.0)
        grad_probs = jnp.einsum(
            "qhd,khd->hqk", grad_heads, values_part, preferred_element_type=jnp.float32
        )
        grad_scores = (probs * (grad_probs - delta_sum[:, :, None])).astype(jnp.bfloat16)
        query_grad = (
            query_grad
            + jnp.einsum("hqk,khd->qhd", grad_scores, keys_part, preferred_element_type=jnp.float32)
            * score_scale
        )
        key_grad = (
            jnp.einsum("hqk,qhd->khd", grad_scores, queries, preferred_element_type=jnp.float32)
            * score_scale
        )
        value_grad = jnp.einsum(
            "hqk,qhd->khd",
            probs.astype(jnp.bfloat16),
            grad_heads,
            preferred_element_type=jnp.float32,
        )
        joined = jnp.concatenate(
            [key_grad.reshape(block_rows, -1), value_grad.reshape(block_rows, -1)], axis=1
        )
        return (query_grad, joined)

    query_grad, stacked = lax.scan(
        gradients,
        jnp.zeros((row_count, head_count, head_dim), jnp.float32),
        jnp.arange(block_count),
    )
    return (query_grad, stacked.reshape(whole.shape[0], -1))


def layer_forward(hidden, layer_index, weights, geometry):
    qkv_weight, out_weight, up_weight, up_bias, down_weight, down_bias, alphas = weights
    row_count, model_width = hidden.shape
    projection = qkv_weight[layer_index]
    rounded = hidden.astype(jnp.bfloat16)
    queries = (
        jnp.dot(rounded, projection[:, :model_width], preferred_element_type=jnp.float32)
        .astype(jnp.bfloat16)
        .reshape(row_count, HEADS, -1)
    )
    key_value = jnp.dot(
        rounded, projection[:, model_width:], preferred_element_type=jnp.float32
    ).astype(jnp.bfloat16)
    whole = lax.all_gather(key_value, "blk", axis=0, tiled=True)
    heads_out, log_total = attend(queries, whole, geometry)
    heads_rounded = heads_out.reshape(row_count, model_width).astype(jnp.bfloat16)
    branch = jnp.dot(heads_rounded, out_weight[layer_index], preferred_element_type=jnp.float32)
    alpha_pair = alphas[layer_index]
    middle = hidden + alpha_pair[0] * branch
    entered = middle.astype(jnp.bfloat16)
    gate_pre = (
        jnp.dot(entered, up_weight[layer_index], preferred_element_type=jnp.float32)
        + up_bias[layer_index]
    )
    activated = gelu_exact(gate_pre).astype(jnp.bfloat16)
    second = (
        jnp.dot(activated, down_weight[layer_index], preferred_element_type=jnp.float32)
        + down_bias[layer_index]
    )
    result = middle + alpha_pair[1] * second
    saved = (
        rounded,
        queries,
        key_value,
        whole,
        heads_out,
        heads_rounded,
        log_total,
        branch,
        entered,
        gate_pre,
        activated,
        second,
    )
    return (result, saved)


def layer_backward(grad_hidden, saved, layer_index, weights, geometry):
    qkv_weight, out_weight, up_weight, up_bias, down_weight, down_bias, alphas = weights
    (
        rounded,
        queries,
        key_value,
        saved_whole,
        heads_out,
        heads_rounded,
        log_total,
        branch,
        entered,
        gate_pre,
        activated,
        second,
    ) = saved
    row_count = grad_hidden.shape[0]
    alpha_pair = alphas[layer_index]
    grad_second = (alpha_pair[1] * grad_hidden).astype(jnp.bfloat16)
    alpha_second = jnp.sum(grad_hidden * second)
    bias_down = jnp.sum(grad_second.astype(jnp.float32), axis=0)
    grad_down = jnp.einsum("tf,td->fd", activated, grad_second, preferred_element_type=jnp.float32)
    grad_act = jnp.einsum(
        "td,fd->tf", grad_second, down_weight[layer_index], preferred_element_type=jnp.float32
    )
    unused, gelu_pull = jax.vjp(gelu_exact, gate_pre)
    grad_gate = gelu_pull(grad_act)[0].astype(jnp.bfloat16)
    bias_up = jnp.sum(grad_gate.astype(jnp.float32), axis=0)
    grad_up = jnp.einsum("td,tf->df", entered, grad_gate, preferred_element_type=jnp.float32)
    grad_middle = grad_hidden + jnp.einsum(
        "tf,df->td", grad_gate, up_weight[layer_index], preferred_element_type=jnp.float32
    )
    grad_branch = (alpha_pair[0] * grad_middle).astype(jnp.bfloat16)
    alpha_first = jnp.sum(grad_middle * branch)
    grad_proj_out = jnp.einsum(
        "te,td->ed", heads_rounded, grad_branch, preferred_element_type=jnp.float32
    )
    grad_heads = (
        jnp.einsum(
            "td,ed->te", grad_branch, out_weight[layer_index], preferred_element_type=jnp.float32
        )
        .astype(jnp.bfloat16)
        .reshape(queries.shape)
    )
    delta_sum = jnp.sum(grad_heads.astype(jnp.float32) * heads_out, axis=2).T
    whole = lax.all_gather(key_value, "blk", axis=0, tiled=True)
    query_grad, key_terms = attend_back(queries, whole, log_total, delta_sum, grad_heads, geometry)
    key_grads = lax.psum_scatter(
        key_terms.astype(jnp.bfloat16), "blk", scatter_dimension=0, tiled=True
    )
    grad_proj = jnp.concatenate(
        [query_grad.reshape(row_count, -1).astype(jnp.bfloat16), key_grads], axis=1
    )
    grad_qkv = jnp.einsum("td,te->de", rounded, grad_proj, preferred_element_type=jnp.float32)
    grad_input = grad_middle + jnp.einsum(
        "te,de->td", grad_proj, qkv_weight[layer_index], preferred_element_type=jnp.float32
    )
    layer_grads = (
        grad_qkv,
        grad_proj_out,
        grad_up,
        bias_up,
        grad_down,
        bias_down,
        jnp.stack([alpha_first, alpha_second]),
    )
    return (grad_input, layer_grads)


def reduce_all(layer_results, cycle_size):
    stacked = [
        jnp.stack([layer_entry[member] for layer_entry in layer_results], axis=0)
        for member in range(6)
    ]
    alpha_tiles = jnp.stack(
        [jnp.tile(layer_entry[6], cycle_size) for layer_entry in layer_results], axis=0
    )
    shares = (
        lax.psum_scatter(
            stacked[0].astype(jnp.bfloat16), "blk", scatter_dimension=1, tiled=True
        ).astype(jnp.float32),
        lax.psum_scatter(
            stacked[1].astype(jnp.bfloat16), "blk", scatter_dimension=1, tiled=True
        ).astype(jnp.float32),
        lax.psum_scatter(
            stacked[2].astype(jnp.bfloat16), "blk", scatter_dimension=1, tiled=True
        ).astype(jnp.float32),
        lax.psum_scatter(
            stacked[3].astype(jnp.bfloat16), "blk", scatter_dimension=1, tiled=True
        ).astype(jnp.float32),
        lax.psum_scatter(
            stacked[4].astype(jnp.bfloat16), "blk", scatter_dimension=1, tiled=True
        ).astype(jnp.float32),
        lax.psum_scatter(
            stacked[5].astype(jnp.bfloat16), "blk", scatter_dimension=1, tiled=True
        ).astype(jnp.float32),
        lax.psum_scatter(
            alpha_tiles.astype(jnp.bfloat16), "blk", scatter_dimension=1, tiled=True
        ).astype(jnp.float32),
    )
    return (
        lax.psum(shares[0].astype(jnp.bfloat16), "grp").astype(jnp.float32),
        lax.psum(shares[1].astype(jnp.bfloat16), "grp").astype(jnp.float32),
        lax.psum(shares[2].astype(jnp.bfloat16), "grp").astype(jnp.float32),
        lax.psum(shares[3].astype(jnp.bfloat16), "grp").astype(jnp.float32),
        lax.psum(shares[4].astype(jnp.bfloat16), "grp").astype(jnp.float32),
        lax.psum(shares[5].astype(jnp.bfloat16), "grp").astype(jnp.float32),
        lax.psum(shares[6].astype(jnp.bfloat16), "grp").astype(jnp.float32),
    )


def body(
    tokens,
    seq_len,
    qkv_weight,
    out_weight,
    up_weight,
    up_bias,
    down_weight,
    down_bias,
    alphas,
    cotangent,
):
    row_count, model_width = tokens.shape
    cycle_size = lax.axis_size("blk")
    cycle_place = lax.axis_index("blk")
    head_dim = model_width // HEADS
    total_rows = cycle_size * row_count
    block_rows = min(max(row_count, 512), total_rows)
    segment, offset, span_rows = layout(seq_len, row_count, cycle_size)
    query_pos = cycle_place * span_rows + offset
    seg_all = jnp.tile(segment, cycle_size)
    pos_all = jnp.repeat(jnp.arange(cycle_size, dtype=jnp.int32), row_count) * jnp.tile(
        span_rows, cycle_size
    ) + jnp.tile(offset, cycle_size)
    geometry = (segment, query_pos, seg_all, pos_all, block_rows, head_dim ** (-0.5))
    weights = (qkv_weight, out_weight, up_weight, up_bias, down_weight, down_bias, alphas)
    hidden = tokens.astype(jnp.float32)
    saved_layers = []
    for layer_index in range(LAYERS):
        hidden, saved = layer_forward(hidden, layer_index, weights, geometry)
        saved_layers.append(saved)
    output = hidden.astype(jnp.bfloat16)
    grad_hidden = cotangent.astype(jnp.float32)
    layer_results = []
    for layer_index in reversed(range(LAYERS)):
        grad_hidden, layer_grads = layer_backward(
            grad_hidden, saved_layers[layer_index], layer_index, weights, geometry
        )
        layer_results.insert(0, layer_grads)
    finals = reduce_all(layer_results, cycle_size)
    return (
        output,
        grad_hidden,
        finals[0],
        finals[1],
        finals[2],
        finals[3],
        finals[4],
        finals[5],
        finals[6],
    )


def solution(mesh):
    placed = (
        P(("grp", "blk"), None),
        P("grp", None),
        P(),
        P(),
        P(),
        P(),
        P(),
        P(),
        P(),
        P(("grp", "blk"), None),
    )
    sizes = (mesh.shape["grp"], mesh.shape["blk"])
    return jax.shard_map(
        fast_body if sizes == (4, RUNS) else body,
        mesh=mesh,
        in_specs=placed,
        out_specs=(
            P(("grp", "blk"), None),
            P(("grp", "blk"), None),
            P(None, "blk", None),
            P(None, "blk", None),
            P(None, "blk", None),
            P(None, "blk"),
            P(None, "blk", None),
            P(None, "blk"),
            P(),
        ),
        check_vma=False,
    )
```

```python
import functools

import jax
import jax.numpy as jnp
from jax import lax
from jax.experimental import pallas as pl
from jax.experimental.pallas import tpu as pltpu
from jax.sharding import PartitionSpec as P

HEADS = 8
LAYERS = 2
NEGATIVE = -1e30
MESH = pl.DeviceIdType.MESH
F32 = jnp.float32
BF16 = jnp.bfloat16

HALF = 128
RUNS = 8
TEAM = 4
OWN = RUNS // TEAM
DIM = 64
WIDTH = 512
FF = 2048
CUT = 512
TILE = 256
TILES = HALF * RUNS // TILE
PACK = HALF + DIM
CHUNK = 576
SMALL = FF + WIDTH + 128
PARTS = ((1, 0, 320), (1, 320, 256), (0, 0, 320), (0, 320, 256))
SHARES = ((208, 0, 112), (176, 16, 64), (192, 80, 48), (160, 80, 16))


def spans():
    places, totals = {}, [0, 0, 0]
    for part, counts in enumerate(SHARES):
        first = PARTS[part][1]
        for route, count in enumerate(counts):
            places[part, route] = (first, totals[route], count)
            first += count
            totals[route] += count
    return places, totals


SPANS, TOTALS = spans()

SLOPE_AT = 0.28
TAIL = (
    0.11652077851573843,
    0.06749675579450809,
    0.2689101589486142,
    -0.23699347299932225,
    0.3898740127620002,
    -0.10580824228351815,
)


def nn(a, b):
    return lax.dot_general(a, b, (((1,), (0,)), ((), ())), preferred_element_type=F32)


def nt(a, b):
    return lax.dot_general(a, b, (((1,), (1,)), ((), ())), preferred_element_type=F32)


def beside(first, other):
    low = lax.broadcasted_iota(jnp.int32, first.shape, 1) < DIM
    return (
        jnp.where(low, first, pltpu.roll(other, DIM, 1)),
        jnp.where(low, pltpu.roll(first, DIM, 1), other),
    )


def layers_kernel(
    tokens, seq_len, alphas, up_bias_hbm, down_bias_hbm, cotangent, qkv_hbm, out_hbm, up_hbm, down_hbm,
    final, heads_all, out_in, grad_in, small_final,
    wqkv, wout, wup, wdown, up_bias, down_bias,
    tok_in, cot_in, flag_out, flag_in, back_out,
    hidden, grad, hid_all, attn_t, entered, act, branch, slope, second,
    dz, du, da, dqkv,
    pack_out, head_out, pack_in, o_in, do_in,
    kv, kv_t, rq, ro, o_t, lse, acc, dq_t, bias,
    parts, core_in, xa_in, xb_in, ya_in, yb_in, z_in, third_z, third_x, third_y,
    heads_out, heads_x, heads_z, heads_sum, small, small_in, small_z, small_sum,
    w_sem, move_send, move_recv, a2a_send, a2a_recv, core_send, core_recv, x_send, x_recv, y_send, y_recv,
    z_send, z_recv, fin_send, fin_recv, hid_send, hid_recv, hx_send, hx_recv, hz_send, hz_recv, hf_send, hf_recv,
    small_send, small_recv, core_free,
):
    grp = lax.axis_index("grp")
    blk = lax.axis_index("blk")
    core = lax.rem(grp, 2)
    side = lax.div(grp, 2)
    yy = lax.rem(blk, 2)
    zz = lax.div(blk, 2)
    member = 2 * core + yy
    far_side = 2 * (1 - side) + core

    def place(c, x, z, y):
        return (2 * x + c, 2 * z + y)

    core_peer = place(1 - core, side, zz, yy)
    x_peer = place(core, 1 - side, zz, yy)
    y_peer = place(core, side, zz, 1 - yy)

    def remote(source, target, send, recv, peer):
        return pltpu.make_async_remote_copy(
            src_ref=source,
            dst_ref=target,
            send_sem=send,
            recv_sem=recv,
            device_id=peer,
            device_id_type=MESH,
        )

    def credit(semaphore, peer, count=1):
        pl.semaphore_signal(semaphore, inc=count, device_id=peer, device_id_type=MESH)

    def moved(kind, slot, source, target, at, core_at, z_at):
        here = jnp.logical_and(core_at == core, z_at == zz)

        @pl.when(here)
        def _():
            pltpu.make_async_copy(source, target.at[at], move_recv.at[kind, at]).start()

        @pl.when(jnp.logical_not(here))
        def _():
            pltpu.make_async_remote_copy(
                src_ref=source,
                dst_ref=target.at[at],
                send_sem=move_send.at[kind, slot],
                recv_sem=move_recv.at[kind, at],
                device_id=place(core_at, side, z_at, yy),
                device_id_type=MESH,
            ).start()

    def move_left(kind, slot, source, core_at, z_at):
        here = jnp.logical_and(core_at == core, z_at == zz)

        @pl.when(jnp.logical_not(here))
        def _():
            pltpu.make_async_copy(source, source, move_send.at[kind, slot]).wait()

    def move_arrived(kind, at, target):
        pltpu.make_async_copy(target.at[at], target.at[at], move_recv.at[kind, at]).wait()

    def to_team(kind, half, source, target):
        moved(kind, half, source, target, lax.div(zz, 2), lax.rem(zz, 2), 2 * half + core)

    def to_team_left(kind, half, source):
        move_left(kind, half, source, lax.rem(zz, 2), 2 * half + core)

    def to_owner(kind, chunk, source, target):
        moved(kind, chunk, source, target, lax.div(zz, 2), lax.rem(zz, 2), core + 2 * chunk)

    def to_owner_left(kind, chunk, source):
        move_left(kind, chunk, source, lax.rem(zz, 2), core + 2 * chunk)

    def half_of(ref, half):
        return ref.at[pl.ds(pl.multiple_of(HALF * half, HALF), HALF)]

    def rows_of(half):
        return pl.ds(pl.multiple_of(half * HALF, HALF), HALF)

    def slot_of(other):
        return lax.rem(other + TEAM - member, TEAM)

    def exchange(kind, layer, half, outgoing, incoming, head=None):
        at = () if head is None else (head,)
        incoming[(half, 0, *at)] = outgoing[(half, member, *at)]
        for step in range(1, TEAM):
            peer = lax.rem(member + step, TEAM)
            remote(
                outgoing.at[(half, peer, *at)],
                incoming.at[(half, TEAM - step, *at)],
                a2a_send.at[kind, layer, half, head or 0],
                a2a_recv.at[kind, layer, half, head or 0],
                place(lax.div(peer, 2), side, zz, lax.rem(peer, 2)),
            ).start()

    def arrived(kind, layer, half, incoming, head=None):
        at = () if head is None else (head,)
        whole = incoming.at[(half, pl.ds(1, TEAM - 1), *at)]
        pltpu.make_async_copy(whole, whole, a2a_recv.at[kind, layer, half, head or 0]).wait()

    def left(kind, layer, half, outgoing):
        for head in range(OWN) if kind in (0, 3) else (None,):
            at = () if head is None else (head,)
            whole = outgoing.at[(half, pl.ds(1, TEAM - 1), *at)]
            pltpu.make_async_copy(whole, whole, a2a_send.at[kind, layer, half, head or 0]).wait()

    def tokens_of(chunk, other):
        return pl.ds(pl.multiple_of(HALF * (TEAM * chunk + other), HALF), HALF)

    def hidden_copy(layer, chunk, which):
        whose = 2 * core + 1 - yy if which == 2 else member
        block = hid_all.at[layer, :, tokens_of(chunk, whose)]
        return remote(
            block,
            block,
            hid_send.at[layer, chunk, which],
            hid_recv.at[layer, chunk, which],
            y_peer if which == 0 else core_peer,
        )

    def hidden_start(layer, chunk):
        for which in range(2):
            hidden_copy(layer, chunk, which).start()

    def hidden_pass(layer, chunk):
        hidden_copy(layer, chunk, 0).wait()
        hidden_copy(layer, chunk, 2).start()

    def hidden_done(layer, chunk):
        for which in range(1, 3):
            hidden_copy(layer, chunk, which).wait()

    def project(layer, half):
        rows = rows_of(half)
        rounded = hidden[rows, :].astype(BF16)
        if layer == 1:
            left(0, 0, half, pack_out)
        queries = (nn(rounded, wqkv[layer, :, 0:WIDTH]) * (DIM ** -0.5)).astype(BF16).T
        for head in range(RUNS):
            pack_out[half, head // 2, head % 2, HALF:, :] = queries[DIM * head : DIM * head + DIM, :]
        for step in range(2):
            at = WIDTH * (step + 1)
            keys_values = nn(rounded, wqkv[layer, :, at : at + WIDTH]).astype(BF16)
            for head in range(4):
                pack_out[half, 2 * step + head // 2, head % 2, 0:HALF, :] = keys_values[
                    :, 128 * head : 128 * head + 128
                ]
        for head in range(OWN):
            exchange(0, layer, half, pack_out, pack_in, head)
        hid_all[layer, :, tokens_of(half, member)] = rounded.T

    def attend(layer, chunk):
        if layer == 1:
            left(1, 0, chunk, head_out)

        def one_head(head, carry):
            arrived(0, layer, chunk, pack_in, head)
            for other in range(TEAM):
                slot = slot_of(other)
                start = HALF * (TEAM * chunk + other)
                span = slice(start, start + HALF)
                block = pack_in[chunk, slot, head, 0:HALF, :]
                kv[layer, head, span, :] = block
                kv_t[layer, head, :, span] = block.T
                rq[layer, head, 0:DIM, span] = pack_in[chunk, slot, head, HALF:, :]

            def scores_of(i):
                count = TILE * (i + 1)
                tile = rq[layer, head, :, TILE * i : TILE * i + TILE]
                return nn(kv[layer, head, 0:count, :], tile) + bias[TILE * TILES - count :, :]

            ahead = [scores_of(i) for i in (2 * chunk, 2 * chunk + 1)]
            for i in (2 * chunk, 2 * chunk + 1):
                columns = slice(TILE * i, TILE * i + TILE)
                count = TILE * (i + 1)
                scores = ahead[i - 2 * chunk]
                largest = jnp.max(scores, axis=0, keepdims=True)
                weight = jnp.exp(scores - largest)
                total = jnp.sum(weight, axis=0, keepdims=True)
                summed = nn(kv_t[layer, head, DIM:, 0:count], weight.astype(BF16))
                summed = summed / total
                o_t[layer, head, :, columns] = summed
                lse[layer, head, :, columns] = largest + jnp.log(total)
                rounded = summed.astype(BF16)
                for part in range(2):
                    head_out[chunk, 2 * (i - 2 * chunk) + part, head] = rounded[
                        :, HALF * part : HALF * part + HALF
                    ]
            return carry

        for head in range(OWN):
            one_head(head, 0)
        exchange(1, layer, chunk, head_out, o_in)

    def feed(layer, half):
        rows = rows_of(half)
        arrived(1, layer, half, o_in)
        for head in range(RUNS):
            attn_t[layer, DIM * head : DIM * head + DIM, rows] = o_in[half, slot_of(head // 2), head % 2]
        attn = attn_t[layer, :, rows].T
        grown = nn(attn, wout[layer])
        branch[layer, rows, :] = grown
        middle = hidden[rows, :] + alphas[layer, 0] * grown
        rounded = middle.astype(BF16)
        entered[layer, rows, :] = rounded
        total = jnp.zeros((HALF, WIDTH), F32)

        def gate_of(step):
            cut = slice(CUT * step, CUT * step + CUT)
            return nn(rounded, wup[layer, :, cut]) + up_bias[layer : layer + 1, cut]

        coming = gate_of(0)
        for step in range(FF // CUT):
            cut = slice(CUT * step, CUT * step + CUT)
            gate = coming
            if step + 1 < FF // CUT:
                coming = gate_of(step + 1)
            bell = jnp.exp(gate * gate * -0.5)
            near = pl.reciprocal(1.0 + SLOPE_AT * jnp.abs(gate), approx=True)
            tail = jnp.full_like(gate, TAIL[5])
            for factor in TAIL[4::-1]:
                tail = tail * near + factor
            tail = bell * (tail * near)
            risen = jnp.where(gate > 0.0, 1.0 - tail, tail)
            slope[layer, rows, cut] = risen + gate * bell * 0.3989422804014327
            active = (gate * risen).astype(BF16)
            act[layer, rows, cut] = active
            total = total + nn(active, wdown[layer, cut, :])
        total = total + down_bias[layer : layer + 1, :]
        second[layer, rows, :] = total
        hidden[rows, :] = middle + alphas[layer, 1] * total

    def total_of(values):
        return jnp.sum(jnp.sum(values, axis=0, keepdims=True), axis=1, keepdims=True)

    def feed_back(layer):
        start = grad[...]
        if layer == 0:
            dz[...] = (alphas[layer, 1] * start).astype(BF16)
        scaled = dz[...]
        alpha_second = total_of(start * second[layer])
        small[layer : layer + 1, FF : FF + WIDTH] = jnp.sum(scaled.astype(F32), axis=0, keepdims=True)
        middle = start
        coming = nt(scaled, wdown[layer, 0:CUT, :])
        for step in range(FF // CUT):
            cut = slice(CUT * step, CUT * step + CUT)
            raw = coming
            if step + 1 < FF // CUT:
                coming = nt(scaled, wdown[layer, CUT * (step + 1) : CUT * (step + 2), :])
            gate = (raw * slope[layer, :, cut]).astype(BF16)
            du[:, cut] = gate
            small[layer : layer + 1, cut] = jnp.sum(gate.astype(F32), axis=0, keepdims=True)
            middle = middle + nt(gate, wup[layer, :, cut])
        grad[...] = middle
        mixed = (alphas[layer, 0] * middle).astype(BF16)
        da[...] = mixed
        spread = nt(wout[layer], mixed).astype(BF16)
        for chunk in (1, 0):
            left(*((1, 1) if layer == 1 else (2, 1)), chunk, head_out)
            for head in range(RUNS):
                head_out[chunk, head // 2, head % 2] = spread[
                    DIM * head : DIM * head + DIM, HALF * chunk : HALF * chunk + HALF
                ]
            exchange(2, layer, chunk, head_out, do_in)
        alpha_first = total_of(middle * branch[layer])
        column = lax.broadcasted_iota(jnp.int32, (1, 128), 1)
        small[layer : layer + 1, FF + WIDTH :] = jnp.where(
            column == 0, alpha_first, jnp.where(column == 1, alpha_second, 0.0)
        )

    def attend_back(layer, chunk):
        arrived(2, layer, chunk, do_in)
        left(*((0, 1) if layer == 1 else (3, 1)), chunk, pack_out)

        def one_head(head, carry):
            for other in range(TEAM):
                start = HALF * (TEAM * chunk + other)
                ro[head, DIM:, start : start + HALF] = do_in[chunk, slot_of(other), head]
            for i in (2 * chunk, 2 * chunk + 1):
                columns = slice(TILE * i, TILE * i + TILE)
                query_tile = rq[layer, head, :, columns]
                grad_tile = ro[head, :, columns]
                log_total = lse[layer, head, :, columns]
                delta = jnp.sum(
                    ro[head, DIM:, columns].astype(F32) * o_t[layer, head, :, columns],
                    axis=0,
                    keepdims=True,
                )
                count = TILE * (i + 1)
                keys = kv[layer, head, 0:count, :]
                weight = jnp.exp(nn(keys, query_tile) + bias[TILE * TILES - count :, :] - log_total)
                scored = (weight * (nn(keys, grad_tile) - delta)).astype(BF16)
                term = nt(scored, query_tile) + nt(weight.astype(BF16), grad_tile)
                if chunk == 1 and i == 2:
                    acc[head, 0:count, :] = term
                elif chunk == 1:
                    acc[head, 0 : count - TILE, :] += term[0 : count - TILE, :]
                    acc[head, count - TILE : count, :] = term[count - TILE :, :]
                else:
                    acc[head, 0:count, :] += term
                query_grad = nn(kv_t[layer, head, 0:DIM, 0:count], scored)
                dq_t[head, :, columns] = query_grad * (DIM ** -0.5)
            for other in range(TEAM):
                start = HALF * (TEAM * chunk + other)
                span = slice(start, start + HALF)
                pack_out[chunk, other, head, 0:HALF, :] = acc[head, span, :].astype(BF16)
                pack_out[chunk, other, head, HALF:, :] = dq_t[head, :, span].astype(BF16)
            exchange(3, layer, chunk, pack_out, pack_in, head)
            return carry

        for head in range(OWN):
            one_head(head, 0)

    def project_back(layer, half):
        for head in range(OWN):
            arrived(3, layer, half, pack_in, head)
        turned = jnp.concatenate(
            [pack_in[half, slot_of(head // 2), head % 2, HALF:, :] for head in range(RUNS)], axis=0
        )
        dqkv[:, 0:WIDTH] = turned.T
        for head in range(RUNS):
            at = WIDTH + 128 * head
            dqkv[:, at : at + 128] = pack_in[half, slot_of(head // 2), head % 2, 0:HALF, :]
        rows = rows_of(half)
        grad[rows, :] = grad[rows, :] + nt(dqkv[...], wqkv[layer])

    def scatter_rows(layer, result, first_row):
        for run in range(RUNS):
            for quarter in range(4):
                parts[layer, quarter % 2, quarter // 2, run // 2, run % 2, first_row : first_row + DIM, :] = result[
                    DIM * run : DIM * run + DIM, 128 * quarter : 128 * quarter + 128
                ].astype(BF16)

    def make(part):
        layer, first, count = PARTS[part]
        if first < 256:
            turned = entered[layer].T
        for row in range(first, min(first + count, 256), DIM):
            step = row // DIM
            scatter_rows(layer, nn(turned, du[:, CUT * step : CUT * step + CUT]), row)
        if first <= 256 < first + count:
            scatter_rows(layer, nn(attn_t[layer], da[...]), 256)
        if first >= 320:
            turned = dz[...].T
            for step in range(FF // CUT):
                result = nn(turned, act[layer, :, CUT * step : CUT * step + CUT])
                for block in range(CUT // 128):
                    run, row = 2 * step + block // 2, 320 + 128 * (block % 2)
                    for quarter in range(4):
                        parts[layer, quarter % 2, quarter // 2, run // 2, run % 2, row : row + 128, :] = result[
                            128 * quarter : 128 * quarter + 128, 128 * block : 128 * block + 128
                        ].astype(BF16)
        if layer == 0:
            pl.semaphore_wait(core_free.at[0 if first < 320 else 1], 1)
        core_copy(part).start()

    def heads_grads(layer):
        for chunk in range(2):
            hidden_done(layer, chunk)
        blocks = [(run // TEAM, run % TEAM) for run in range(RUNS)]
        keys_values = jnp.concatenate(
            [
                jnp.concatenate([pack_out[chunk, other, head, 0:HALF, :] for chunk, other in blocks], axis=0)
                for head in range(OWN)
            ],
            axis=1,
        )
        queries = jnp.concatenate(
            [
                jnp.concatenate([pack_out[chunk, other, head, HALF:, :] for chunk, other in blocks], axis=1)
                for head in range(OWN)
            ],
            axis=0,
        )
        both = nn(hid_all[layer], keys_values)
        q_part = nt(hid_all[layer], queries)
        for number, values in enumerate((q_part, both[:, 0:128], both[:, 128:256])):
            for run in range(RUNS):
                heads_out[layer, run // 2, run % 2, :, 128 * number : 128 * number + 128] = values[
                    DIM * run : DIM * run + DIM, :
                ].astype(BF16)
        heads_x_copy(layer).start()

    def half_rows(which):
        return pl.ds(pl.multiple_of(32 * which, 32), 32)

    def heads_x_copy(layer):
        return remote(
            heads_out.at[layer, :, :, half_rows(1 - side)],
            heads_x.at[layer],
            hx_send.at[layer],
            hx_recv.at[layer],
            x_peer,
        )

    def heads_z_copy(layer, step):
        peer = lax.rem(zz + step, 4)
        return remote(
            heads_out.at[layer, peer, :, half_rows(side)],
            heads_z.at[layer, 4 - step],
            hz_send.at[layer, step],
            hz_recv.at[layer, 4 - step],
            place(core, side, peer, yy),
        )

    def heads_last_copy(layer, number):
        x, c, y = number // 4, number // 2 % 2, number % 2
        return remote(
            heads_sum.at[layer, 1 - yy if y else yy],
            heads_all.at[layer, side, member],
            hf_send.at[layer, number],
            hf_recv.at[layer, number],
            place(1 - core if c else core, 1 - side if x else side, zz, 1 - yy if y else yy),
        )

    def heads_second(layer):
        heads_x_copy(layer).wait()
        heads_out[layer, :, :, half_rows(side), :] += heads_x[layer]
        for step in range(1, 4):
            heads_z_copy(layer, step).start()

    def heads_third(layer):
        for step in range(1, 4):
            heads_z_copy(layer, step).wait()
        total = heads_out[layer, zz, :, half_rows(side), :].astype(F32)
        for slot in range(1, 4):
            total = total + heads_z[layer, slot].astype(F32)
        heads_sum[layer] = total.astype(BF16)
        heads_all[layer, side, member] = heads_sum[layer, yy]
        for number in range(1, 8):
            heads_last_copy(layer, number).start()

    def heads_done(layer):
        for number in range(1, 8):
            heads_last_copy(layer, number).wait()

    def rows_in(part, route):
        first, room, count = SPANS[part, route]
        return pl.ds(first, count), pl.ds(room, count)

    def used(part, route):
        return SHARES[part][route] > 0

    def core_copy(part):
        layer, first, count = PARTS[part]
        rows = pl.ds(first, count)
        return remote(
            parts.at[layer, 1 - core, :, :, :, rows],
            core_in.at[:, :, :, rows],
            core_send.at[part],
            core_recv.at[part],
            core_peer,
        )

    def x_copy(part, route):
        layer = PARTS[part][0]
        rows, room = rows_in(part, route)
        ends = (x_send.at[part, route], x_recv.at[part, route], x_peer)
        mine = parts.at[layer, core, 1 - side]
        if route == 0:
            return remote(mine.at[:, :, rows], xa_in.at[:, :, room], *ends)
        if route == 1:
            return remote(mine.at[:, yy, rows], xb_in.at[:, room], *ends)
        return remote(mine.at[zz, :, rows], third_x.at[:, room], *ends)

    def y_copy(part, route):
        layer = PARTS[part][0]
        rows, room = rows_in(part, route)
        ends = (y_send.at[part, route], y_recv.at[part, route], y_peer)
        mine = parts.at[layer, core]
        if route == 0:
            return remote(mine.at[side, :, 1 - yy, rows], ya_in.at[:, room], *ends)
        if route == 1:
            return remote(mine.at[:, :, 1 - yy, rows], yb_in.at[:, :, room], *ends)
        return remote(mine.at[side, zz, 1 - yy, rows], third_y.at[room], *ends)

    def z_copy(part, route, step):
        layer = PARTS[part][0]
        rows, room = rows_in(part, route)
        peer = lax.rem(zz + step, 4)
        ends = (z_send.at[part, route, step], z_recv.at[part, route, 4 - step], place(core, side, peer, yy))
        if route == 2:
            return remote(parts.at[layer, core, :, peer, :, rows], third_z.at[4 - step, :, :, room], *ends)
        return remote(parts.at[layer, core, side, peer, yy, rows], z_in.at[layer, 4 - step, rows], *ends)

    def final_copy(part, which):
        layer, first, count = PARTS[part]
        block = final.at[layer, far_side if which == 2 else grp, pl.ds(first, count)]
        return remote(
            block,
            block,
            fin_send.at[part, which],
            fin_recv.at[part, which],
            x_peer if which == 0 else core_peer,
        )

    def core_done(part):
        layer, first, count = PARTS[part]
        rows = pl.ds(first, count)
        core_copy(part).wait()
        for across in (1 - side, side):
            parts[layer, core, across, :, :, rows, :] += core_in[across, :, :, rows, :]
            if used(part, 0) and across is not side:
                x_copy(part, 0).start()
        if used(part, 1):
            y_copy(part, 1).start()
        if used(part, 2):
            for step in range(1, 4):
                z_copy(part, 2, step).start()
        if layer == 1:
            freed = 0 if first < 320 else 1
            followers = [1 for other in PARTS if other[0] == 0 and (other[1] >= 320) == (freed == 1)]
            credit(core_free.at[freed], core_peer, len(followers))

    def first_x(part):
        if used(part, 0):
            layer = PARTS[part][0]
            rows, room = rows_in(part, 0)
            x_copy(part, 0).wait()
            for y in (1 - yy, yy):
                parts[layer, core, side, :, y, rows, :] += xa_in[:, y, room, :]
                if y is not yy:
                    y_copy(part, 0).start()

    def first_y(part):
        if used(part, 1):
            layer = PARTS[part][0]
            rows, room = rows_in(part, 1)
            y_copy(part, 1).wait()
            for across in (1 - side, side):
                parts[layer, core, across, :, yy, rows, :] += yb_in[across, :, room, :]
                if across is not side:
                    x_copy(part, 1).start()

    def first_z(part):
        if used(part, 2):
            layer = PARTS[part][0]
            rows, room = rows_in(part, 2)
            for step in range(1, 4):
                z_copy(part, 2, step).wait()
            for across in (1 - side, side):
                total = parts[layer, core, across, zz, :, rows, :].astype(F32)
                for slot in range(1, 4):
                    total = total + third_z[slot, across, :, room, :].astype(F32)
                parts[layer, core, across, zz, :, rows, :] = total.astype(BF16)
                if across is not side:
                    x_copy(part, 2).start()

    def second_x(part):
        if used(part, 0):
            layer = PARTS[part][0]
            rows, room = rows_in(part, 0)
            y_copy(part, 0).wait()
            parts[layer, core, side, :, yy, rows, :] += ya_in[:, room, :]
            for step in range(1, 4):
                z_copy(part, 0, step).start()

    def second_y(part):
        if used(part, 1):
            layer = PARTS[part][0]
            rows, room = rows_in(part, 1)
            x_copy(part, 1).wait()
            parts[layer, core, side, :, yy, rows, :] += xb_in[:, room, :]
            for step in range(1, 4):
                z_copy(part, 1, step).start()

    def second_z(part):
        if used(part, 2):
            layer = PARTS[part][0]
            rows, room = rows_in(part, 2)
            x_copy(part, 2).wait()
            for y in (1 - yy, yy):
                parts[layer, core, side, zz, y, rows, :] += third_x[y, room, :]
                if y is not yy:
                    y_copy(part, 2).start()

    def third_done(part):
        layer = PARTS[part][0]
        for route in range(3):
            if not used(part, route):
                continue
            rows, room = rows_in(part, route)
            if route == 2:
                y_copy(part, 2).wait()
                final[layer, grp, rows, :] = parts[layer, core, side, zz, yy, rows, :] + third_y[room, :]
            else:
                for step in range(1, 4):
                    z_copy(part, route, step).wait()
                total = parts[layer, core, side, zz, yy, rows, :].astype(F32)
                for slot in range(1, 4):
                    total = total + z_in[layer, slot, rows, :].astype(F32)
                final[layer, grp, rows, :] = total.astype(BF16)
        if PARTS[part][1] >= 320:
            for row in (320, 448):
                final[layer, grp, row : row + 128, :] = final[layer, grp, row : row + 128, :].T
        for which in range(2):
            final_copy(part, which).start()

    def final_pass(part):
        final_copy(part, 0).wait()
        final_copy(part, 2).start()

    def final_done(part):
        for which in range(1, 3):
            final_copy(part, which).wait()

    def small_copy(stage):
        peer = (core_peer, x_peer, y_peer)[stage]
        return remote(
            small_sum.at[stage], small_in.at[stage], small_send.at[stage], small_recv.at[stage], peer
        )

    def small_z_copy(step):
        return remote(
            small_z.at[zz],
            small_z.at[zz],
            small_send.at[2 + step],
            small_recv.at[2 + step],
            place(core, side, lax.rem(zz + step, 4), yy),
        )

    def small_start():
        small_sum[0] = small[...]
        small_copy(0).start()

    def small_next(stage):
        small_copy(stage).wait()
        total = small_sum[stage] + small_in[stage]
        if stage < 2:
            small_sum[stage + 1] = total
            small_copy(stage + 1).start()
        else:
            small_z[zz] = total
            for step in range(1, 4):
                small_z_copy(step).start()

    def small_done():
        for step in range(1, 4):
            small_z_copy(step).wait()
        small_sum[0] = (small_z[0] + small_z[1]) + (small_z[2] + small_z[3])
        small_final[:, 0:256] = small_sum[0, :, pl.ds(pl.multiple_of(blk * 256, 256), 256)]
        pair = small_sum[0, :, pl.ds(pl.multiple_of(FF + 128 * zz, 128), 128)]
        small_final[:, 256:384] = jnp.where(yy == 1, pltpu.roll(pair, DIM, 1), pair)
        small_final[:, 384:512] = small_sum[0, :, FF + WIDTH :]

    def halves(*phases, first=0):
        def both(step, carry):
            for phase in phases:
                phase(lax.rem(step + first, 2))
            return carry

        lax.fori_loop(0, 2, both, 0)

    def begin(half):
        move_arrived(0, half, tok_in)
        hidden[rows_of(half), :] = tok_in[half].astype(F32)

    def finish(half):
        back_out[0, half] = hidden[rows_of(half), :].astype(BF16)
        to_owner(3, half, back_out.at[0, half], out_in)

    def turn_round(layer, half):
        move_arrived(2, half, cot_in)
        rows = rows_of(half)
        grad[rows, :] = cot_in[half].astype(F32)
        dz[rows, :] = (alphas[layer, 1] * grad[rows, :]).astype(BF16)

    def hand_back(half):
        back_out[1, half] = grad[rows_of(half), :].astype(BF16)
        to_owner(4, half, back_out.at[1, half], grad_in)

    barrier = pltpu.get_barrier_semaphore()
    for step in range(1, 4):
        credit(barrier, place(core, side, lax.rem(zz + step, 4), yy))
    for step in range(4):
        credit(barrier, place(1 - core, side, lax.rem(zz + step, 4), yy))
    for peer in (
        x_peer,
        y_peer,
        place(1 - core, side, zz, 1 - yy),
        place(1 - core, 1 - side, zz, yy),
        place(core, 1 - side, zz, 1 - yy),
        place(1 - core, 1 - side, zz, 1 - yy),
    ):
        credit(barrier, peer)

    weight_copies = {}
    for layer in range(LAYERS):
        for number, (source, target) in enumerate(
            ((qkv_hbm, wqkv), (out_hbm, wout), (up_hbm, wup), (down_hbm, wdown))
        ):
            weight_copies[layer, number] = pltpu.make_async_copy(
                source.at[layer], target.at[layer], w_sem.at[layer, number]
            )
    bias_copies = [
        pltpu.make_async_copy(up_bias_hbm, up_bias, w_sem.at[2, 0]),
        pltpu.make_async_copy(down_bias_hbm, down_bias, w_sem.at[2, 1]),
    ]
    weight_copies[0, 0].start()
    pl.semaphore_wait(barrier, 13)
    upper = lax.div(zz, 2)
    for half in (1 - upper, upper):
        to_team(0, half, half_of(tokens, half), tok_in)
    for layer, number in ((1, 0), (0, 1), (0, 2), (0, 3), (1, 1), (1, 2), (1, 3)):
        weight_copies[layer, number].start(priority=1)
    for copy in bias_copies:
        copy.start(priority=1)
    end_second = lax.div(seq_len[0, 0] + seq_len[0, 1], RUNS)
    flag_out[...] = jnp.full((8, 128), end_second.astype(F32), F32)
    for half in (1 - upper, upper):
        to_team(1, half, flag_out, flag_in)
    for layer in range(LAYERS):
        for head in range(OWN):
            rq[layer, head, DIM:, :] = jnp.zeros((DIM, HALF * RUNS), BF16)
    for head in range(OWN):
        ro[head, 0:DIM, :] = jnp.zeros((DIM, HALF * RUNS), BF16)
    for layer in range(LAYERS):
        weight_copies[layer, 0].wait()
        pairs = [
            beside(
                wqkv[layer, :, WIDTH + 128 * pair : WIDTH + 128 * pair + 128].astype(F32),
                wqkv[layer, :, 2 * WIDTH + 128 * pair : 2 * WIDTH + 128 * pair + 128].astype(F32),
            )
            for pair in range(TEAM)
        ]
        for head in range(RUNS):
            at = WIDTH + 128 * head
            wqkv[layer, :, at : at + 128] = pairs[head // 2][head % 2].astype(BF16)
    halves(begin, functools.partial(project, 0), first=upper)
    for half in (1 - upper, upper):
        to_team(2, half, half_of(cotangent, half), cot_in)

    move_arrived(1, 0, flag_in)
    move_arrived(1, 1, flag_in)
    border = jnp.concatenate([flag_in[0, 0:1, :]] * 2, axis=1) - (HALF * lax.div(zz, 2)).astype(F32)
    key_row = lax.broadcasted_iota(jnp.int32, (TILE, TILE), 0)
    query_col = lax.broadcasted_iota(jnp.int32, (TILE, TILE), 1)
    later = key_row > query_col
    key_sub = lax.rem(key_row, HALF).astype(F32) >= border
    query_sub = lax.rem(query_col, HALF).astype(F32) >= border
    apart = jnp.logical_xor(key_sub, query_sub)
    for tile in range(TILES - 1):
        bias[TILE * tile : TILE * tile + TILE, :] = jnp.where(apart, NEGATIVE, 0.0)
    bias[TILE * (TILES - 1) :, :] = jnp.where(jnp.logical_or(later, apart), NEGATIVE, 0.0)

    for copy in (*bias_copies, *(weight_copies[0, number] for number in range(1, 4))):
        copy.wait()
    attend(0, 0)
    attend(0, 1)
    hidden_start(0, 0)
    halves(functools.partial(feed, 0), functools.partial(project, 1))
    for number in range(1, 4):
        weight_copies[1, number].wait()
    attend(1, 0)
    attend(1, 1)
    hidden_pass(0, 0)
    hidden_start(1, 0)
    halves(functools.partial(feed, 1), finish)
    hidden_start(0, 1)
    hidden_start(1, 1)
    hidden_pass(1, 0)

    halves(functools.partial(turn_round, 1))
    make(1)
    feed_back(1)
    hidden_pass(0, 1)
    hidden_pass(1, 1)
    core_done(1)
    make(0)
    attend_back(1, 1)
    first_y(1)
    core_done(0)
    attend_back(1, 0)
    second_y(1)
    first_x(1)
    project_back(1, 1)
    heads_grads(1)
    first_z(1)
    project_back(1, 0)
    feed_back(0)
    small_start()
    second_x(1)
    make(2)
    first_x(0)
    heads_second(1)
    first_z(0)
    attend_back(0, 1)
    small_next(0)
    core_done(2)
    second_x(0)
    make(3)
    attend_back(0, 0)
    small_next(1)
    project_back(0, 1)
    hand_back(1)
    first_z(2)
    heads_grads(0)
    small_next(2)
    first_x(2)
    core_done(3)
    first_y(2)
    heads_second(0)
    small_done()
    first_z(3)
    second_x(2)
    first_x(3)
    second_z(2)
    second_z(0)
    heads_third(1)
    second_z(1)
    first_y(3)
    heads_third(0)
    second_y(2)
    second_x(3)
    second_z(3)
    third_done(0)
    third_done(2)
    second_y(3)
    project_back(0, 0)
    hand_back(0)
    heads_done(1)
    third_done(1)
    third_done(3)
    final_pass(0)
    final_pass(2)
    final_pass(1)
    final_pass(3)
    final_done(2)
    final_done(1)
    heads_done(0)
    final_done(0)
    final_done(3)
    for half in range(2):
        move_arrived(3, half, out_in)
        move_arrived(4, half, grad_in)

    for half in range(2):
        left(2, 0, half, head_out)
        left(3, 0, half, pack_out)
        to_team_left(0, half, half_of(tokens, half))
        to_team_left(1, half, flag_out)
        to_team_left(2, half, half_of(cotangent, half))
        to_owner_left(3, half, back_out.at[0, half])
        to_owner_left(4, half, back_out.at[1, half])


def results_kernel(
    final, heads, out_block, grad_block, small,
    output, input_grad, qkv_grad, out_grad, up_grad, up_bias_grad, down_grad, down_bias_grad, alpha_grad,
    out_flat, grad_wide, qkv_wide, out_wide, up_wide, down_wide, out_sem,
):
    ends = []

    def write(source, target):
        ends.append(pltpu.make_async_copy(source, target, out_sem.at[len(ends)]))
        ends[-1].start()

    up_bias_grad[...] = small[:, 0:256]
    down_bias_grad[...] = small[:, 256 : 256 + DIM]
    alpha_grad[...] = small[:, 384:386]
    for layer in range(LAYERS):
        for quarter in range(4):

            def block(first, count):
                return final[layer, quarter, first : first + count, :].astype(F32)

            def columns(step):
                return slice(WIDTH * step + 128 * quarter, WIDTH * step + 128 * quarter + 128)

            for step in range(4):
                up_wide[layer, :, columns(step)] = block(DIM * step, DIM)
            out_wide[layer, :, columns(0)] = block(256, DIM)
            down_wide[layer, :, columns(0)] = block(320, 256)
        write(up_wide.at[layer], up_grad.at[layer])
        write(out_wide.at[layer], out_grad.at[layer])
        write(down_wide.at[layer], down_grad.at[layer])
    for half in range(2):
        rows = slice(HALF * half, HALF * half + HALF)
        grad_wide[rows, :] = grad_block[half].astype(F32)
        out_flat[rows, :] = out_block[half]
    write(grad_wide, input_grad)
    write(out_flat, output)
    for layer in range(LAYERS):
        for side in range(2):
            for member in range(TEAM):
                block = heads[layer, side, member].astype(F32)
                columns = (block[:, 0:128], *beside(block[:, 128:256], block[:, 256:384]))
                for step in range(3):
                    at = WIDTH * step + 128 * member
                    qkv_wide[layer, 32 * side : 32 * side + 32, at : at + 128] = columns[step]
        write(qkv_wide.at[layer], qkv_grad.at[layer])
    for end in ends:
        end.wait()


def fast_body(
    tokens, seq_len, qkv_weight, out_weight, up_weight, up_bias, down_weight, down_bias, alphas, cotangent
):
    whole = pl.BlockSpec(memory_space=pltpu.VMEM)
    scalar = pl.BlockSpec(memory_space=pltpu.SMEM)
    far = pl.BlockSpec(memory_space=pl.ANY)
    shape = jax.ShapeDtypeStruct
    rows = HALF * RUNS

    def vmem(*dims):
        return pltpu.VMEM(dims, BF16)

    def wide(*dims):
        return pltpu.VMEM(dims, F32)

    dma = pltpu.SemaphoreType.DMA
    final, heads, out_block, grad_block, small = pl.pallas_call(
        layers_kernel,
        out_shape=(
            vmem(LAYERS, 4, CHUNK, 128),
            vmem(LAYERS, 2, TEAM, DIM // 2, 3 * 128),
            vmem(2, HALF, WIDTH),
            vmem(2, HALF, WIDTH),
            wide(LAYERS, WIDTH),
        ),
        in_specs=[far, scalar, scalar, far, far, far, far, far, far, far],
        out_specs=(whole,) * 5,
        scratch_shapes=[
            vmem(LAYERS, WIDTH, 3 * WIDTH),
            vmem(LAYERS, WIDTH, WIDTH),
            vmem(LAYERS, WIDTH, FF),
            vmem(LAYERS, FF, WIDTH),
            wide(LAYERS, FF),
            wide(LAYERS, WIDTH),
            vmem(2, HALF, WIDTH),
            vmem(2, HALF, WIDTH),
            wide(8, 128),
            wide(2, 8, 128),
            vmem(2, 2, HALF, WIDTH),
            wide(2 * HALF, WIDTH),
            wide(2 * HALF, WIDTH),
            vmem(LAYERS, WIDTH, rows),
            vmem(LAYERS, WIDTH, 2 * HALF),
            vmem(LAYERS, 2 * HALF, WIDTH),
            vmem(LAYERS, 2 * HALF, FF),
            wide(LAYERS, 2 * HALF, WIDTH),
            wide(LAYERS, 2 * HALF, FF),
            wide(LAYERS, 2 * HALF, WIDTH),
            vmem(2 * HALF, WIDTH),
            vmem(2 * HALF, FF),
            vmem(2 * HALF, WIDTH),
            vmem(HALF, 3 * WIDTH),
            vmem(2, TEAM, OWN, PACK, 128),
            vmem(2, TEAM, OWN, DIM, 128),
            vmem(2, TEAM, OWN, PACK, 128),
            vmem(2, TEAM, OWN, DIM, 128),
            vmem(2, TEAM, OWN, DIM, 128),
            vmem(LAYERS, OWN, rows, 128),
            vmem(LAYERS, OWN, 128, rows),
            vmem(LAYERS, OWN, 128, rows),
            vmem(OWN, 128, rows),
            wide(LAYERS, OWN, DIM, rows),
            wide(LAYERS, OWN, 1, rows),
            wide(OWN, rows, 128),
            wide(OWN, DIM, rows),
            wide(rows, TILE),
            vmem(LAYERS, 2, 2, 4, 2, CHUNK, 128),
            vmem(2, 4, 2, CHUNK, 128),
            vmem(4, 2, TOTALS[0], 128),
            vmem(4, TOTALS[1], 128),
            vmem(4, TOTALS[0], 128),
            vmem(2, 4, TOTALS[1], 128),
            vmem(LAYERS, 4, CHUNK, 128),
            vmem(4, 2, 2, TOTALS[2], 128),
            vmem(2, TOTALS[2], 128),
            vmem(TOTALS[2], 128),
            vmem(LAYERS, 4, 2, DIM, 3 * 128),
            vmem(LAYERS, 4, 2, DIM // 2, 3 * 128),
            vmem(LAYERS, 4, 2, DIM // 2, 3 * 128),
            vmem(LAYERS, 2, DIM // 2, 3 * 128),
            wide(LAYERS, SMALL),
            wide(3, LAYERS, SMALL),
            wide(4, LAYERS, SMALL),
            wide(3, LAYERS, SMALL),
            dma((LAYERS + 1, 4)),
            dma((5, 2)),
            dma((5, 2)),
            dma((4, LAYERS, 2, OWN)),
            dma((4, LAYERS, 2, OWN)),
            dma((len(PARTS),)),
            dma((len(PARTS),)),
            dma((len(PARTS), 3)),
            dma((len(PARTS), 3)),
            dma((len(PARTS), 3)),
            dma((len(PARTS), 3)),
            dma((len(PARTS), 3, 4)),
            dma((len(PARTS), 3, 4)),
            dma((len(PARTS), 3)),
            dma((len(PARTS), 3)),
            dma((LAYERS, 2, 3)),
            dma((LAYERS, 2, 3)),
            dma((LAYERS,)),
            dma((LAYERS,)),
            dma((LAYERS, 4)),
            dma((LAYERS, 4)),
            dma((LAYERS, 8)),
            dma((LAYERS, 8)),
            dma((6,)),
            dma((6,)),
            pltpu.SemaphoreType.REGULAR((2,)),
        ],
        compiler_params=pltpu.CompilerParams(
            collective_id=0, has_side_effects=True, vmem_limit_bytes=61 * 1024 * 1024
        ),
        name="layers",
    )(
        tokens, seq_len, alphas, up_bias, down_bias, cotangent,
        qkv_weight, out_weight, up_weight, down_weight,
    )
    return tuple(
        pl.pallas_call(
            results_kernel,
            out_shape=(
                shape((2 * HALF, WIDTH), BF16),
                shape((2 * HALF, WIDTH), F32),
                shape((LAYERS, DIM, 3 * WIDTH), F32),
                shape((LAYERS, DIM, WIDTH), F32),
                shape((LAYERS, DIM, FF), F32),
                shape((LAYERS, FF // RUNS), F32),
                shape((LAYERS, FF // RUNS, WIDTH), F32),
                shape((LAYERS, DIM), F32),
                shape((LAYERS, 2), F32),
            ),
            in_specs=[whole] * 5,
            out_specs=(far, far, far, far, far, whole, far, whole, whole),
            scratch_shapes=[
                vmem(2 * HALF, WIDTH),
                wide(2 * HALF, WIDTH),
                wide(LAYERS, DIM, 3 * WIDTH),
                wide(LAYERS, DIM, WIDTH),
                wide(LAYERS, DIM, FF),
                wide(LAYERS, FF // RUNS, WIDTH),
                dma((10,)),
            ],
            compiler_params=pltpu.CompilerParams(vmem_limit_bytes=24 * 1024 * 1024),
            name="results",
        )(final, heads, out_block, grad_block, small)
    )


def layout(seq_len, local_count, cycle_size):
    piece_rows = seq_len[0] // cycle_size
    end_rows = jnp.cumsum(piece_rows)
    start_rows = end_rows - piece_rows
    local_rows = jnp.arange(local_count, dtype=jnp.int32)
    segment = jnp.sum((local_rows[:, None] >= end_rows[None, :]).astype(jnp.int32), axis=1)
    picked = segment[:, None] == jnp.arange(seq_len.shape[1], dtype=jnp.int32)[None, :]
    offset = local_rows - jnp.sum(jnp.where(picked, start_rows[None, :], 0), axis=1)
    span_rows = jnp.sum(jnp.where(picked, piece_rows[None, :], 0), axis=1)
    return (segment, offset, span_rows)


def gelu_exact(values):
    return jax.nn.gelu(values, approximate=False)


def key_block(whole, geometry, block_index, head_count):
    query_seg, query_pos, seg_all, pos_all, block_rows, score_scale = geometry
    first_row = block_index * block_rows
    key_piece = lax.dynamic_slice_in_dim(whole, first_row, block_rows, 0)
    key_seg = lax.dynamic_slice_in_dim(seg_all, first_row, block_rows, 0)
    key_pos = lax.dynamic_slice_in_dim(pos_all, first_row, block_rows, 0)
    half_width = key_piece.shape[1] // 2
    keys_part = key_piece[:, :half_width].reshape(block_rows, head_count, -1)
    values_part = key_piece[:, half_width:].reshape(block_rows, head_count, -1)
    return (keys_part, values_part, key_seg, key_pos)


def block_scores(queries, keys_part, key_seg, key_pos, geometry):
    query_seg, query_pos, seg_all, pos_all, block_rows, score_scale = geometry
    scores = (
        jnp.einsum("qhd,khd->hqk", queries, keys_part, preferred_element_type=jnp.float32)
        * score_scale
    )
    allowed = (query_seg[:, None] == key_seg[None, :]) & (key_pos[None, :] <= query_pos[:, None])
    return (scores, allowed[None])


def attend(queries, whole, geometry):
    row_count, head_count, head_dim = queries.shape
    block_count = whole.shape[0] // geometry[4]

    def statistics(running, block_index):
        largest, totals = running
        keys_part, values_part, key_seg, key_pos = key_block(
            whole, geometry, block_index, head_count
        )
        scores, allowed = block_scores(queries, keys_part, key_seg, key_pos, geometry)
        newest = jnp.maximum(largest, jnp.max(jnp.where(allowed, scores, NEGATIVE), axis=2))
        weights = jnp.where(allowed, jnp.exp(scores - newest[:, :, None]), 0.0)
        totals = totals * jnp.exp(largest - newest) + jnp.sum(weights, axis=2)
        return ((newest, totals), None)

    initial = (
        jnp.full((head_count, row_count), NEGATIVE, jnp.float32),
        jnp.zeros((head_count, row_count), jnp.float32),
    )
    (largest, totals), unused = lax.scan(statistics, initial, jnp.arange(block_count))
    log_total = largest + jnp.log(totals)

    def weighted(output_sum, block_index):
        keys_part, values_part, key_seg, key_pos = key_block(
            whole, geometry, block_index, head_count
        )
        scores, allowed = block_scores(queries, keys_part, key_seg, key_pos, geometry)
        probs = jnp.where(allowed, jnp.exp(scores - log_total[:, :, None]), 0.0).astype(
            jnp.bfloat16
        )
        output_sum = output_sum + jnp.einsum(
            "hqk,khd->qhd", probs, values_part, preferred_element_type=jnp.float32
        )
        return (output_sum, None)

    output_sum, unused = lax.scan(
        weighted, jnp.zeros((row_count, head_count, head_dim), jnp.float32), jnp.arange(block_count)
    )
    return (output_sum, log_total)


def attend_back(queries, whole, log_total, delta_sum, grad_heads, geometry):
    row_count, head_count, head_dim = queries.shape
    block_rows = geometry[4]
    score_scale = geometry[5]
    block_count = whole.shape[0] // block_rows

    def gradients(query_grad, block_index):
        keys_part, values_part, key_seg, key_pos = key_block(
            whole, geometry, block_index, head_count
        )
        scores, allowed = block_scores(queries, keys_part, key_seg, key_pos, geometry)
        probs = jnp.where(allowed, jnp.exp(scores - log_total[:, :, None]), 0.0)
        grad_probs = jnp.einsum(
            "qhd,khd->hqk", grad_heads, values_part, preferred_element_type=jnp.float32
        )
        grad_scores = (probs * (grad_probs - delta_sum[:, :, None])).astype(jnp.bfloat16)
        query_grad = (
            query_grad
            + jnp.einsum("hqk,khd->qhd", grad_scores, keys_part, preferred_element_type=jnp.float32)
            * score_scale
        )
        key_grad = (
            jnp.einsum("hqk,qhd->khd", grad_scores, queries, preferred_element_type=jnp.float32)
            * score_scale
        )
        value_grad = jnp.einsum(
            "hqk,qhd->khd",
            probs.astype(jnp.bfloat16),
            grad_heads,
            preferred_element_type=jnp.float32,
        )
        joined = jnp.concatenate(
            [key_grad.reshape(block_rows, -1), value_grad.reshape(block_rows, -1)], axis=1
        )
        return (query_grad, joined)

    query_grad, stacked = lax.scan(
        gradients,
        jnp.zeros((row_count, head_count, head_dim), jnp.float32),
        jnp.arange(block_count),
    )
    return (query_grad, stacked.reshape(whole.shape[0], -1))


def layer_forward(hidden, layer_index, weights, geometry):
    qkv_weight, out_weight, up_weight, up_bias, down_weight, down_bias, alphas = weights
    row_count, model_width = hidden.shape
    projection = qkv_weight[layer_index]
    rounded = hidden.astype(jnp.bfloat16)
    queries = (
        jnp.dot(rounded, projection[:, :model_width], preferred_element_type=jnp.float32)
        .astype(jnp.bfloat16)
        .reshape(row_count, HEADS, -1)
    )
    key_value = jnp.dot(
        rounded, projection[:, model_width:], preferred_element_type=jnp.float32
    ).astype(jnp.bfloat16)
    whole = lax.all_gather(key_value, "blk", axis=0, tiled=True)
    heads_out, log_total = attend(queries, whole, geometry)
    heads_rounded = heads_out.reshape(row_count, model_width).astype(jnp.bfloat16)
    branch = jnp.dot(heads_rounded, out_weight[layer_index], preferred_element_type=jnp.float32)
    alpha_pair = alphas[layer_index]
    middle = hidden + alpha_pair[0] * branch
    entered = middle.astype(jnp.bfloat16)
    gate_pre = (
        jnp.dot(entered, up_weight[layer_index], preferred_element_type=jnp.float32)
        + up_bias[layer_index]
    )
    activated = gelu_exact(gate_pre).astype(jnp.bfloat16)
    second = (
        jnp.dot(activated, down_weight[layer_index], preferred_element_type=jnp.float32)
        + down_bias[layer_index]
    )
    result = middle + alpha_pair[1] * second
    saved = (
        rounded,
        queries,
        key_value,
        whole,
        heads_out,
        heads_rounded,
        log_total,
        branch,
        entered,
        gate_pre,
        activated,
        second,
    )
    return (result, saved)


def layer_backward(grad_hidden, saved, layer_index, weights, geometry):
    qkv_weight, out_weight, up_weight, up_bias, down_weight, down_bias, alphas = weights
    (
        rounded,
        queries,
        key_value,
        saved_whole,
        heads_out,
        heads_rounded,
        log_total,
        branch,
        entered,
        gate_pre,
        activated,
        second,
    ) = saved
    row_count = grad_hidden.shape[0]
    alpha_pair = alphas[layer_index]
    grad_second = (alpha_pair[1] * grad_hidden).astype(jnp.bfloat16)
    alpha_second = jnp.sum(grad_hidden * second)
    bias_down = jnp.sum(grad_second.astype(jnp.float32), axis=0)
    grad_down = jnp.einsum("tf,td->fd", activated, grad_second, preferred_element_type=jnp.float32)
    grad_act = jnp.einsum(
        "td,fd->tf", grad_second, down_weight[layer_index], preferred_element_type=jnp.float32
    )
    unused, gelu_pull = jax.vjp(gelu_exact, gate_pre)
    grad_gate = gelu_pull(grad_act)[0].astype(jnp.bfloat16)
    bias_up = jnp.sum(grad_gate.astype(jnp.float32), axis=0)
    grad_up = jnp.einsum("td,tf->df", entered, grad_gate, preferred_element_type=jnp.float32)
    grad_middle = grad_hidden + jnp.einsum(
        "tf,df->td", grad_gate, up_weight[layer_index], preferred_element_type=jnp.float32
    )
    grad_branch = (alpha_pair[0] * grad_middle).astype(jnp.bfloat16)
    alpha_first = jnp.sum(grad_middle * branch)
    grad_proj_out = jnp.einsum(
        "te,td->ed", heads_rounded, grad_branch, preferred_element_type=jnp.float32
    )
    grad_heads = (
        jnp.einsum(
            "td,ed->te", grad_branch, out_weight[layer_index], preferred_element_type=jnp.float32
        )
        .astype(jnp.bfloat16)
        .reshape(queries.shape)
    )
    delta_sum = jnp.sum(grad_heads.astype(jnp.float32) * heads_out, axis=2).T
    whole = lax.all_gather(key_value, "blk", axis=0, tiled=True)
    query_grad, key_terms = attend_back(queries, whole, log_total, delta_sum, grad_heads, geometry)
    key_grads = lax.psum_scatter(
        key_terms.astype(jnp.bfloat16), "blk", scatter_dimension=0, tiled=True
    )
    grad_proj = jnp.concatenate(
        [query_grad.reshape(row_count, -1).astype(jnp.bfloat16), key_grads], axis=1
    )
    grad_qkv = jnp.einsum("td,te->de", rounded, grad_proj, preferred_element_type=jnp.float32)
    grad_input = grad_middle + jnp.einsum(
        "te,de->td", grad_proj, qkv_weight[layer_index], preferred_element_type=jnp.float32
    )
    layer_grads = (
        grad_qkv,
        grad_proj_out,
        grad_up,
        bias_up,
        grad_down,
        bias_down,
        jnp.stack([alpha_first, alpha_second]),
    )
    return (grad_input, layer_grads)


def reduce_all(layer_results, cycle_size):
    stacked = [
        jnp.stack([layer_entry[member] for layer_entry in layer_results], axis=0)
        for member in range(6)
    ]
    alpha_tiles = jnp.stack(
        [jnp.tile(layer_entry[6], cycle_size) for layer_entry in layer_results], axis=0
    )
    shares = (
        lax.psum_scatter(
            stacked[0].astype(jnp.bfloat16), "blk", scatter_dimension=1, tiled=True
        ).astype(jnp.float32),
        lax.psum_scatter(
            stacked[1].astype(jnp.bfloat16), "blk", scatter_dimension=1, tiled=True
        ).astype(jnp.float32),
        lax.psum_scatter(
            stacked[2].astype(jnp.bfloat16), "blk", scatter_dimension=1, tiled=True
        ).astype(jnp.float32),
        lax.psum_scatter(
            stacked[3].astype(jnp.bfloat16), "blk", scatter_dimension=1, tiled=True
        ).astype(jnp.float32),
        lax.psum_scatter(
            stacked[4].astype(jnp.bfloat16), "blk", scatter_dimension=1, tiled=True
        ).astype(jnp.float32),
        lax.psum_scatter(
            stacked[5].astype(jnp.bfloat16), "blk", scatter_dimension=1, tiled=True
        ).astype(jnp.float32),
        lax.psum_scatter(
            alpha_tiles.astype(jnp.bfloat16), "blk", scatter_dimension=1, tiled=True
        ).astype(jnp.float32),
    )
    return (
        lax.psum(shares[0].astype(jnp.bfloat16), "grp").astype(jnp.float32),
        lax.psum(shares[1].astype(jnp.bfloat16), "grp").astype(jnp.float32),
        lax.psum(shares[2].astype(jnp.bfloat16), "grp").astype(jnp.float32),
        lax.psum(shares[3].astype(jnp.bfloat16), "grp").astype(jnp.float32),
        lax.psum(shares[4].astype(jnp.bfloat16), "grp").astype(jnp.float32),
        lax.psum(shares[5].astype(jnp.bfloat16), "grp").astype(jnp.float32),
        lax.psum(shares[6].astype(jnp.bfloat16), "grp").astype(jnp.float32),
    )


def body(
    tokens,
    seq_len,
    qkv_weight,
    out_weight,
    up_weight,
    up_bias,
    down_weight,
    down_bias,
    alphas,
    cotangent,
):
    row_count, model_width = tokens.shape
    cycle_size = lax.axis_size("blk")
    cycle_place = lax.axis_index("blk")
    head_dim = model_width // HEADS
    total_rows = cycle_size * row_count
    block_rows = min(max(row_count, 512), total_rows)
    segment, offset, span_rows = layout(seq_len, row_count, cycle_size)
    query_pos = cycle_place * span_rows + offset
    seg_all = jnp.tile(segment, cycle_size)
    pos_all = jnp.repeat(jnp.arange(cycle_size, dtype=jnp.int32), row_count) * jnp.tile(
        span_rows, cycle_size
    ) + jnp.tile(offset, cycle_size)
    geometry = (segment, query_pos, seg_all, pos_all, block_rows, head_dim ** (-0.5))
    weights = (qkv_weight, out_weight, up_weight, up_bias, down_weight, down_bias, alphas)
    hidden = tokens.astype(jnp.float32)
    saved_layers = []
    for layer_index in range(LAYERS):
        hidden, saved = layer_forward(hidden, layer_index, weights, geometry)
        saved_layers.append(saved)
    output = hidden.astype(jnp.bfloat16)
    grad_hidden = cotangent.astype(jnp.float32)
    layer_results = []
    for layer_index in reversed(range(LAYERS)):
        grad_hidden, layer_grads = layer_backward(
            grad_hidden, saved_layers[layer_index], layer_index, weights, geometry
        )
        layer_results.insert(0, layer_grads)
    finals = reduce_all(layer_results, cycle_size)
    return (
        output,
        grad_hidden,
        finals[0],
        finals[1],
        finals[2],
        finals[3],
        finals[4],
        finals[5],
        finals[6],
    )


def solution(mesh):
    placed = (
        P(("grp", "blk"), None),
        P("grp", None),
        P(),
        P(),
        P(),
        P(),
        P(),
        P(),
        P(),
        P(("grp", "blk"), None),
    )
    sizes = (mesh.shape["grp"], mesh.shape["blk"])
    return jax.shard_map(
        fast_body if sizes == (4, RUNS) else body,
        mesh=mesh,
        in_specs=placed,
        out_specs=(
            P(("grp", "blk"), None),
            P(("grp", "blk"), None),
            P(None, "blk", None),
            P(None, "blk", None),
            P(None, "blk", None),
            P(None, "blk"),
            P(None, "blk", None),
            P(None, "blk"),
            P(),
        ),
        check_vma=False,
    )
```

```python
import functools

import jax
import jax.numpy as jnp
from jax import lax
from jax.experimental import pallas as pl
from jax.experimental.pallas import tpu as pltpu
from jax.sharding import PartitionSpec as P

HEADS = 8
LAYERS = 2
NEGATIVE = -1e30
MESH = pl.DeviceIdType.MESH
F32 = jnp.float32
BF16 = jnp.bfloat16

HALF = 128
RUNS = 8
TEAM = 4
OWN = RUNS // TEAM
DIM = 64
WIDTH = 512
FF = 2048
CUT = 512
TILE = 256
TILES = HALF * RUNS // TILE
PACK = HALF + DIM
CHUNK = 576
SMALL = FF + WIDTH + 128
PARTS = ((1, 0, 320), (1, 320, 256), (0, 0, 320), (0, 320, 256))
SHARES = ((160, 0, 160), (96, 32, 128), (96, 144, 80), (128, 64, 64))


def spans():
    places, totals = {}, [0, 0, 0]
    for part, counts in enumerate(SHARES):
        first = PARTS[part][1]
        for route, count in enumerate(counts):
            places[part, route] = (first, totals[route], count)
            first += count
            totals[route] += count
    return places, totals


SPANS, TOTALS = spans()

SLOPE_AT = 0.28
TAIL = (
    0.11652077851573843,
    0.06749675579450809,
    0.2689101589486142,
    -0.23699347299932225,
    0.3898740127620002,
    -0.10580824228351815,
)


def nn(a, b):
    return lax.dot_general(a, b, (((1,), (0,)), ((), ())), preferred_element_type=F32)


def nt(a, b):
    return lax.dot_general(a, b, (((1,), (1,)), ((), ())), preferred_element_type=F32)


def beside(first, other):
    low = lax.broadcasted_iota(jnp.int32, first.shape, 1) < DIM
    return (
        jnp.where(low, first, pltpu.roll(other, DIM, 1)),
        jnp.where(low, pltpu.roll(first, DIM, 1), other),
    )


def layers_kernel(
    tokens, seq_len, alphas, up_bias_hbm, down_bias_hbm, cotangent, qkv_hbm, out_hbm, up_hbm, down_hbm,
    final, heads_all, out_in, grad_in, small_final,
    wqkv, wout, wup, wdown, up_bias, down_bias,
    tok_in, cot_in, flag_out, flag_in, back_out,
    hidden, grad, hid_all, attn_t, entered, act, branch, slope, second,
    dz, du, da, dqkv,
    pack_out, head_out, pack_in, o_in, do_in,
    kv, kv_t, rq, ro, o_t, lse, acc, dq_t, bias,
    parts, core_in, xa_in, xb_in, ya_in, yb_in, near_in, far_in, third_near, third_far, third_x, third_y,
    heads_out, heads_x, heads_z, heads_sum, small, small_in, small_z, small_sum,
    w_sem, move_send, move_recv, a2a_send, a2a_recv, core_send, core_recv, x_send, x_recv, y_send, y_recv,
    z_send, z_recv, fin_send, fin_recv, hid_send, hid_recv, hx_send, hx_recv, hz_send, hz_recv, hf_send, hf_recv,
    small_send, small_recv, core_free,
):
    grp = lax.axis_index("grp")
    blk = lax.axis_index("blk")
    core = lax.rem(grp, 2)
    side = lax.div(grp, 2)
    yy = lax.rem(blk, 2)
    zz = lax.div(blk, 2)
    member = 2 * core + yy
    far_side = 2 * (1 - side) + core

    def place(c, x, z, y):
        return (2 * x + c, 2 * z + y)

    core_peer = place(1 - core, side, zz, yy)
    x_peer = place(core, 1 - side, zz, yy)
    y_peer = place(core, side, zz, 1 - yy)
    high, odd = lax.div(zz, 2), lax.rem(zz, 2)
    near_peer = place(core, side, 2 * high + 1 - odd, yy)
    far_peer = place(core, side, 2 * (1 - high) + odd, yy)

    def remote(source, target, send, recv, peer):
        return pltpu.make_async_remote_copy(
            src_ref=source,
            dst_ref=target,
            send_sem=send,
            recv_sem=recv,
            device_id=peer,
            device_id_type=MESH,
        )

    def credit(semaphore, peer, count=1):
        pl.semaphore_signal(semaphore, inc=count, device_id=peer, device_id_type=MESH)

    def moved(kind, slot, source, target, at, core_at, z_at):
        here = jnp.logical_and(core_at == core, z_at == zz)

        @pl.when(here)
        def _():
            pltpu.make_async_copy(source, target.at[at], move_recv.at[kind, at]).start()

        @pl.when(jnp.logical_not(here))
        def _():
            pltpu.make_async_remote_copy(
                src_ref=source,
                dst_ref=target.at[at],
                send_sem=move_send.at[kind, slot],
                recv_sem=move_recv.at[kind, at],
                device_id=place(core_at, side, z_at, yy),
                device_id_type=MESH,
            ).start()

    def move_left(kind, slot, source, core_at, z_at):
        here = jnp.logical_and(core_at == core, z_at == zz)

        @pl.when(jnp.logical_not(here))
        def _():
            pltpu.make_async_copy(source, source, move_send.at[kind, slot]).wait()

    def move_arrived(kind, at, target):
        pltpu.make_async_copy(target.at[at], target.at[at], move_recv.at[kind, at]).wait()

    def to_team(kind, half, source, target):
        moved(kind, half, source, target, lax.div(zz, 2), lax.rem(zz, 2), 2 * half + core)

    def to_team_left(kind, half, source):
        move_left(kind, half, source, lax.rem(zz, 2), 2 * half + core)

    def to_owner(kind, chunk, source, target):
        moved(kind, chunk, source, target, lax.div(zz, 2), lax.rem(zz, 2), core + 2 * chunk)

    def to_owner_left(kind, chunk, source):
        move_left(kind, chunk, source, lax.rem(zz, 2), core + 2 * chunk)

    def half_of(ref, half):
        return ref.at[pl.ds(pl.multiple_of(HALF * half, HALF), HALF)]

    def rows_of(half):
        return pl.ds(pl.multiple_of(half * HALF, HALF), HALF)

    def slot_of(other):
        return lax.rem(other + TEAM - member, TEAM)

    def exchange(kind, layer, half, outgoing, incoming, head=None):
        at = () if head is None else (head,)
        incoming[(half, 0, *at)] = outgoing[(half, member, *at)]
        for step in range(1, TEAM):
            peer = lax.rem(member + step, TEAM)
            remote(
                outgoing.at[(half, peer, *at)],
                incoming.at[(half, TEAM - step, *at)],
                a2a_send.at[kind, layer, half, head or 0],
                a2a_recv.at[kind, layer, half, head or 0],
                place(lax.div(peer, 2), side, zz, lax.rem(peer, 2)),
            ).start()

    def arrived(kind, layer, half, incoming, head=None):
        at = () if head is None else (head,)
        whole = incoming.at[(half, pl.ds(1, TEAM - 1), *at)]
        pltpu.make_async_copy(whole, whole, a2a_recv.at[kind, layer, half, head or 0]).wait()

    def left(kind, layer, half, outgoing):
        for head in range(OWN) if kind in (0, 3) else (None,):
            at = () if head is None else (head,)
            whole = outgoing.at[(half, pl.ds(1, TEAM - 1), *at)]
            pltpu.make_async_copy(whole, whole, a2a_send.at[kind, layer, half, head or 0]).wait()

    def tokens_of(chunk, other):
        return pl.ds(pl.multiple_of(HALF * (TEAM * chunk + other), HALF), HALF)

    def hidden_copy(layer, chunk, which):
        whose = 2 * core + 1 - yy if which == 2 else member
        block = hid_all.at[layer, :, tokens_of(chunk, whose)]
        return remote(
            block,
            block,
            hid_send.at[layer, chunk, which],
            hid_recv.at[layer, chunk, which],
            y_peer if which == 0 else core_peer,
        )

    def hidden_start(layer, chunk):
        for which in range(2):
            hidden_copy(layer, chunk, which).start()

    def hidden_pass(layer, chunk):
        hidden_copy(layer, chunk, 0).wait()
        hidden_copy(layer, chunk, 2).start()

    def hidden_done(layer, chunk):
        for which in range(1, 3):
            hidden_copy(layer, chunk, which).wait()

    def project(layer, half):
        rows = rows_of(half)
        rounded = hidden[rows, :].astype(BF16)
        if layer == 1:
            left(0, 0, half, pack_out)
        queries = (nn(rounded, wqkv[layer, :, 0:WIDTH]) * (DIM ** -0.5)).astype(BF16).T
        for head in range(RUNS):
            pack_out[half, head // 2, head % 2, HALF:, :] = queries[DIM * head : DIM * head + DIM, :]
        for step in range(2):
            at = WIDTH * (step + 1)
            keys_values = nn(rounded, wqkv[layer, :, at : at + WIDTH]).astype(BF16)
            for head in range(4):
                pack_out[half, 2 * step + head // 2, head % 2, 0:HALF, :] = keys_values[
                    :, 128 * head : 128 * head + 128
                ]
        for head in range(OWN):
            exchange(0, layer, half, pack_out, pack_in, head)
        hid_all[layer, :, tokens_of(half, member)] = rounded.T

    def attend(layer, chunk):
        if layer == 1:
            left(1, 0, chunk, head_out)

        def one_head(head, carry):
            arrived(0, layer, chunk, pack_in, head)
            for other in range(TEAM):
                slot = slot_of(other)
                start = HALF * (TEAM * chunk + other)
                span = slice(start, start + HALF)
                block = pack_in[chunk, slot, head, 0:HALF, :]
                kv[layer, head, span, :] = block
                kv_t[layer, head, :, span] = block.T
                rq[layer, head, 0:DIM, span] = pack_in[chunk, slot, head, HALF:, :]

            def scores_of(i):
                count = TILE * (i + 1)
                tile = rq[layer, head, :, TILE * i : TILE * i + TILE]
                return nn(kv[layer, head, 0:count, :], tile) + bias[TILE * TILES - count :, :]

            ahead = [scores_of(i) for i in (2 * chunk, 2 * chunk + 1)]
            for i in (2 * chunk, 2 * chunk + 1):
                columns = slice(TILE * i, TILE * i + TILE)
                count = TILE * (i + 1)
                scores = ahead[i - 2 * chunk]
                largest = jnp.max(scores, axis=0, keepdims=True)
                weight = jnp.exp(scores - largest)
                total = jnp.sum(weight, axis=0, keepdims=True)
                summed = nn(kv_t[layer, head, DIM:, 0:count], weight.astype(BF16))
                summed = summed / total
                o_t[layer, head, :, columns] = summed
                lse[layer, head, :, columns] = largest + jnp.log(total)
                rounded = summed.astype(BF16)
                for part in range(2):
                    head_out[chunk, 2 * (i - 2 * chunk) + part, head] = rounded[
                        :, HALF * part : HALF * part + HALF
                    ]
            return carry

        for head in range(OWN):
            one_head(head, 0)
        exchange(1, layer, chunk, head_out, o_in)

    def feed(layer, half):
        rows = rows_of(half)
        arrived(1, layer, half, o_in)
        for head in range(RUNS):
            attn_t[layer, DIM * head : DIM * head + DIM, rows] = o_in[half, slot_of(head // 2), head % 2]
        attn = attn_t[layer, :, rows].T
        grown = nn(attn, wout[layer])
        branch[layer, rows, :] = grown
        middle = hidden[rows, :] + alphas[layer, 0] * grown
        rounded = middle.astype(BF16)
        entered[layer, rows, :] = rounded
        total = jnp.zeros((HALF, WIDTH), F32)

        def gate_of(step):
            cut = slice(CUT * step, CUT * step + CUT)
            return nn(rounded, wup[layer, :, cut]) + up_bias[layer : layer + 1, cut]

        coming = gate_of(0)
        for step in range(FF // CUT):
            cut = slice(CUT * step, CUT * step + CUT)
            gate = coming
            if step + 1 < FF // CUT:
                coming = gate_of(step + 1)
            bell = jnp.exp(gate * gate * -0.5)
            near = pl.reciprocal(1.0 + SLOPE_AT * jnp.abs(gate), approx=True)
            tail = jnp.full_like(gate, TAIL[5])
            for factor in TAIL[4::-1]:
                tail = tail * near + factor
            tail = bell * (tail * near)
            risen = jnp.where(gate > 0.0, 1.0 - tail, tail)
            slope[layer, rows, cut] = risen + gate * bell * 0.3989422804014327
            active = (gate * risen).astype(BF16)
            act[layer, rows, cut] = active
            total = total + nn(active, wdown[layer, cut, :])
        total = total + down_bias[layer : layer + 1, :]
        second[layer, rows, :] = total
        hidden[rows, :] = middle + alphas[layer, 1] * total

    def total_of(values):
        return jnp.sum(jnp.sum(values, axis=0, keepdims=True), axis=1, keepdims=True)

    def feed_back(layer):
        start = grad[...]
        if layer == 0:
            dz[...] = (alphas[layer, 1] * start).astype(BF16)
        scaled = dz[...]
        alpha_second = total_of(start * second[layer])
        small[layer : layer + 1, FF : FF + WIDTH] = jnp.sum(scaled.astype(F32), axis=0, keepdims=True)
        middle = start
        coming = nt(scaled, wdown[layer, 0:CUT, :])
        for step in range(FF // CUT):
            cut = slice(CUT * step, CUT * step + CUT)
            raw = coming
            if step + 1 < FF // CUT:
                coming = nt(scaled, wdown[layer, CUT * (step + 1) : CUT * (step + 2), :])
            gate = (raw * slope[layer, :, cut]).astype(BF16)
            du[:, cut] = gate
            small[layer : layer + 1, cut] = jnp.sum(gate.astype(F32), axis=0, keepdims=True)
            middle = middle + nt(gate, wup[layer, :, cut])
        grad[...] = middle
        mixed = (alphas[layer, 0] * middle).astype(BF16)
        da[...] = mixed
        spread = nt(wout[layer], mixed).astype(BF16)
        for chunk in (1, 0):
            left(*((1, 1) if layer == 1 else (2, 1)), chunk, head_out)
            for head in range(RUNS):
                head_out[chunk, head // 2, head % 2] = spread[
                    DIM * head : DIM * head + DIM, HALF * chunk : HALF * chunk + HALF
                ]
            exchange(2, layer, chunk, head_out, do_in)
        alpha_first = total_of(middle * branch[layer])
        column = lax.broadcasted_iota(jnp.int32, (1, 128), 1)
        small[layer : layer + 1, FF + WIDTH :] = jnp.where(
            column == 0, alpha_first, jnp.where(column == 1, alpha_second, 0.0)
        )

    def attend_back(layer, chunk):
        arrived(2, layer, chunk, do_in)
        left(*((0, 1) if layer == 1 else (3, 1)), chunk, pack_out)

        def one_head(head, carry):
            for other in range(TEAM):
                start = HALF * (TEAM * chunk + other)
                ro[head, DIM:, start : start + HALF] = do_in[chunk, slot_of(other), head]
            for i in (2 * chunk, 2 * chunk + 1):
                columns = slice(TILE * i, TILE * i + TILE)
                query_tile = rq[layer, head, :, columns]
                grad_tile = ro[head, :, columns]
                log_total = lse[layer, head, :, columns]
                delta = jnp.sum(
                    ro[head, DIM:, columns].astype(F32) * o_t[layer, head, :, columns],
                    axis=0,
                    keepdims=True,
                )
                count = TILE * (i + 1)
                keys = kv[layer, head, 0:count, :]
                weight = jnp.exp(nn(keys, query_tile) + bias[TILE * TILES - count :, :] - log_total)
                scored = (weight * (nn(keys, grad_tile) - delta)).astype(BF16)
                term = nt(scored, query_tile) + nt(weight.astype(BF16), grad_tile)
                if chunk == 1 and i == 2:
                    acc[head, 0:count, :] = term
                elif chunk == 1:
                    acc[head, 0 : count - TILE, :] += term[0 : count - TILE, :]
                    acc[head, count - TILE : count, :] = term[count - TILE :, :]
                else:
                    acc[head, 0:count, :] += term
                query_grad = nn(kv_t[layer, head, 0:DIM, 0:count], scored)
                dq_t[head, :, columns] = query_grad * (DIM ** -0.5)
            for other in range(TEAM):
                start = HALF * (TEAM * chunk + other)
                span = slice(start, start + HALF)
                pack_out[chunk, other, head, 0:HALF, :] = acc[head, span, :].astype(BF16)
                pack_out[chunk, other, head, HALF:, :] = dq_t[head, :, span].astype(BF16)
            exchange(3, layer, chunk, pack_out, pack_in, head)
            return carry

        for head in range(OWN):
            one_head(head, 0)

    def project_back(layer, half):
        for head in range(OWN):
            arrived(3, layer, half, pack_in, head)
        turned = jnp.concatenate(
            [pack_in[half, slot_of(head // 2), head % 2, HALF:, :] for head in range(RUNS)], axis=0
        )
        dqkv[:, 0:WIDTH] = turned.T
        for head in range(RUNS):
            at = WIDTH + 128 * head
            dqkv[:, at : at + 128] = pack_in[half, slot_of(head // 2), head % 2, 0:HALF, :]
        rows = rows_of(half)
        grad[rows, :] = grad[rows, :] + nt(dqkv[...], wqkv[layer])

    def scatter_rows(layer, result, first_row):
        for run in range(RUNS):
            for quarter in range(4):
                parts[layer, quarter % 2, quarter // 2, run // 4, run // 2 % 2, run % 2, first_row : first_row + DIM, :] = result[
                    DIM * run : DIM * run + DIM, 128 * quarter : 128 * quarter + 128
                ].astype(BF16)

    def make(part):
        layer, first, count = PARTS[part]
        if first < 256:
            turned = entered[layer].T
        for row in range(first, min(first + count, 256), DIM):
            step = row // DIM
            scatter_rows(layer, nn(turned, du[:, CUT * step : CUT * step + CUT]), row)
        if first <= 256 < first + count:
            scatter_rows(layer, nn(attn_t[layer], da[...]), 256)
        if first >= 320:
            turned = dz[...].T
            for step in range(FF // CUT):
                result = nn(turned, act[layer, :, CUT * step : CUT * step + CUT])
                for block in range(CUT // 128):
                    run, row = 2 * step + block // 2, 320 + 128 * (block % 2)
                    for quarter in range(4):
                        parts[layer, quarter % 2, quarter // 2, run // 4, run // 2 % 2, run % 2, row : row + 128, :] = result[
                            128 * quarter : 128 * quarter + 128, 128 * block : 128 * block + 128
                        ].astype(BF16)
        if layer == 0:
            pl.semaphore_wait(core_free.at[0 if first < 320 else 1], 1)
        core_copy(part).start()

    def heads_grads(layer):
        for chunk in range(2):
            hidden_done(layer, chunk)
        blocks = [(run // TEAM, run % TEAM) for run in range(RUNS)]
        keys_values = jnp.concatenate(
            [
                jnp.concatenate([pack_out[chunk, other, head, 0:HALF, :] for chunk, other in blocks], axis=0)
                for head in range(OWN)
            ],
            axis=1,
        )
        queries = jnp.concatenate(
            [
                jnp.concatenate([pack_out[chunk, other, head, HALF:, :] for chunk, other in blocks], axis=1)
                for head in range(OWN)
            ],
            axis=0,
        )
        both = nn(hid_all[layer], keys_values)
        q_part = nt(hid_all[layer], queries)
        for number, values in enumerate((q_part, both[:, 0:128], both[:, 128:256])):
            for run in range(RUNS):
                heads_out[layer, run // 2, run % 2, :, 128 * number : 128 * number + 128] = values[
                    DIM * run : DIM * run + DIM, :
                ].astype(BF16)
        heads_x_copy(layer).start()

    def half_rows(which):
        return pl.ds(pl.multiple_of(32 * which, 32), 32)

    def heads_x_copy(layer):
        return remote(
            heads_out.at[layer, :, :, half_rows(1 - side)],
            heads_x.at[layer],
            hx_send.at[layer],
            hx_recv.at[layer],
            x_peer,
        )

    def heads_z_copy(layer, step):
        peer = lax.rem(zz + step, 4)
        return remote(
            heads_out.at[layer, peer, :, half_rows(side)],
            heads_z.at[layer, 4 - step],
            hz_send.at[layer, step],
            hz_recv.at[layer, 4 - step],
            place(core, side, peer, yy),
        )

    def heads_last_copy(layer, number):
        x, c, y = number // 4, number // 2 % 2, number % 2
        return remote(
            heads_sum.at[layer, 1 - yy if y else yy],
            heads_all.at[layer, side, member],
            hf_send.at[layer, number],
            hf_recv.at[layer, number],
            place(1 - core if c else core, 1 - side if x else side, zz, 1 - yy if y else yy),
        )

    def heads_second(layer):
        heads_x_copy(layer).wait()
        heads_out[layer, :, :, half_rows(side), :] += heads_x[layer]
        for step in range(1, 4):
            heads_z_copy(layer, step).start()

    def heads_third(layer):
        for step in range(1, 4):
            heads_z_copy(layer, step).wait()
        total = heads_out[layer, zz, :, half_rows(side), :].astype(F32)
        for slot in range(1, 4):
            total = total + heads_z[layer, slot].astype(F32)
        heads_sum[layer] = total.astype(BF16)
        heads_all[layer, side, member] = heads_sum[layer, yy]
        for number in range(1, 8):
            heads_last_copy(layer, number).start()

    def heads_done(layer):
        for number in range(1, 8):
            heads_last_copy(layer, number).wait()

    def rows_in(part, route):
        first, room, count = SPANS[part, route]
        return pl.ds(first, count), pl.ds(room, count)

    def used(part, route):
        return SHARES[part][route] > 0

    def core_copy(part):
        layer, first, count = PARTS[part]
        rows = pl.ds(first, count)
        return remote(
            parts.at[layer, 1 - core, :, :, :, :, rows],
            core_in.at[:, :, :, :, rows],
            core_send.at[part],
            core_recv.at[part],
            core_peer,
        )

    def x_copy(part, route):
        layer = PARTS[part][0]
        rows, room = rows_in(part, route)
        ends = (x_send.at[part, route], x_recv.at[part, route], x_peer)
        mine = parts.at[layer, core, 1 - side]
        if route == 0:
            return remote(mine.at[:, :, :, rows], xa_in.at[:, :, :, room], *ends)
        if route == 1:
            return remote(mine.at[:, :, yy, rows], xb_in.at[:, :, room], *ends)
        return remote(mine.at[high, odd, :, rows], third_x.at[:, room], *ends)

    def y_copy(part, route):
        layer = PARTS[part][0]
        rows, room = rows_in(part, route)
        ends = (y_send.at[part, route], y_recv.at[part, route], y_peer)
        mine = parts.at[layer, core]
        if route == 0:
            return remote(mine.at[side, :, :, 1 - yy, rows], ya_in.at[:, :, room], *ends)
        if route == 1:
            return remote(mine.at[:, :, :, 1 - yy, rows], yb_in.at[:, :, :, room], *ends)
        return remote(mine.at[side, high, odd, 1 - yy, rows], third_y.at[room], *ends)

    def near_copy(part, route):
        layer = PARTS[part][0]
        rows, room = rows_in(part, route)
        ends = (z_send.at[part, route, 0], z_recv.at[part, route, 0], near_peer)
        mine = parts.at[layer, core]
        if route == 2:
            return remote(mine.at[:, :, 1 - odd, :, rows], third_near.at[:, :, :, room], *ends)
        return remote(mine.at[side, :, 1 - odd, yy, rows], near_in.at[layer, :, rows], *ends)

    def far_copy(part, route):
        layer = PARTS[part][0]
        rows, room = rows_in(part, route)
        ends = (z_send.at[part, route, 1], z_recv.at[part, route, 1], far_peer)
        mine = parts.at[layer, core]
        if route == 2:
            return remote(mine.at[:, 1 - high, odd, :, rows], third_far.at[:, :, room], *ends)
        return remote(mine.at[side, 1 - high, odd, yy, rows], far_in.at[layer, rows], *ends)

    def final_copy(part, which):
        layer, first, count = PARTS[part]
        block = final.at[layer, far_side if which == 2 else grp, pl.ds(first, count)]
        return remote(
            block,
            block,
            fin_send.at[part, which],
            fin_recv.at[part, which],
            x_peer if which == 0 else core_peer,
        )

    def core_done(part):
        layer, first, count = PARTS[part]
        rows = pl.ds(first, count)
        core_copy(part).wait()
        for across in (1 - side, side):
            parts[layer, core, across, :, :, :, rows, :] += core_in[across, :, :, :, rows, :]
            if used(part, 0) and across is not side:
                x_copy(part, 0).start()
        if used(part, 1):
            y_copy(part, 1).start()
        if used(part, 2):
            near_copy(part, 2).start()
        if layer == 1:
            freed = 0 if first < 320 else 1
            followers = [1 for other in PARTS if other[0] == 0 and (other[1] >= 320) == (freed == 1)]
            credit(core_free.at[freed], core_peer, len(followers))

    def first_x(part):
        layer = PARTS[part][0]
        rows, room = rows_in(part, 0)
        x_copy(part, 0).wait()
        for y in (1 - yy, yy):
            parts[layer, core, side, :, :, y, rows, :] += xa_in[:, :, y, room, :]
            if y is not yy:
                y_copy(part, 0).start()

    def first_y(part):
        layer = PARTS[part][0]
        rows, room = rows_in(part, 1)
        y_copy(part, 1).wait()
        for across in (1 - side, side):
            parts[layer, core, across, :, :, yy, rows, :] += yb_in[across, :, :, room, :]
            if across is not side:
                x_copy(part, 1).start()

    def far_z(part):
        layer = PARTS[part][0]
        rows, room = rows_in(part, 2)
        near_copy(part, 2).wait()
        for half in (1 - high, high):
            parts[layer, core, :, half, odd, :, rows, :] += third_near[:, half, :, room, :]
            if half is not high:
                far_copy(part, 2).start()

    def first_z(part):
        layer = PARTS[part][0]
        rows, room = rows_in(part, 2)
        far_copy(part, 2).wait()
        for across in (1 - side, side):
            parts[layer, core, across, high, odd, :, rows, :] += third_far[across, :, room, :]
            if across is not side:
                x_copy(part, 2).start()

    def second_x(part):
        layer = PARTS[part][0]
        rows, room = rows_in(part, 0)
        y_copy(part, 0).wait()
        for z in (1 - odd, odd):
            parts[layer, core, side, :, z, yy, rows, :] += ya_in[:, z, room, :]
            if z is not odd:
                near_copy(part, 0).start()

    def second_y(part):
        layer = PARTS[part][0]
        rows, room = rows_in(part, 1)
        x_copy(part, 1).wait()
        for z in (1 - odd, odd):
            parts[layer, core, side, :, z, yy, rows, :] += xb_in[:, z, room, :]
            if z is not odd:
                near_copy(part, 1).start()

    def second_z(part):
        layer = PARTS[part][0]
        rows, room = rows_in(part, 2)
        x_copy(part, 2).wait()
        for y in (1 - yy, yy):
            parts[layer, core, side, high, odd, y, rows, :] += third_x[y, room, :]
            if y is not yy:
                y_copy(part, 2).start()

    def far_of(part, route):
        layer = PARTS[part][0]
        rows, room = rows_in(part, route)
        near_copy(part, route).wait()
        for half in (1 - high, high):
            parts[layer, core, side, half, odd, yy, rows, :] += near_in[layer, half, rows, :]
            if half is not high:
                far_copy(part, route).start()

    def far_x(part):
        far_of(part, 0)

    def far_y(part):
        far_of(part, 1)

    def third_done(part):
        layer = PARTS[part][0]
        for route in range(3):
            if not used(part, route):
                continue
            rows, room = rows_in(part, route)
            if route == 2:
                y_copy(part, 2).wait()
                last = third_y[room, :]
            else:
                far_copy(part, route).wait()
                last = far_in[layer, rows, :]
            final[layer, grp, rows, :] = parts[layer, core, side, high, odd, yy, rows, :] + last
        if PARTS[part][1] >= 320:
            for row in (320, 448):
                final[layer, grp, row : row + 128, :] = final[layer, grp, row : row + 128, :].T
        for which in range(2):
            final_copy(part, which).start()

    def final_pass(part):
        final_copy(part, 0).wait()
        final_copy(part, 2).start()

    def final_done(part):
        for which in range(1, 3):
            final_copy(part, which).wait()

    def small_copy(stage):
        peer = (core_peer, x_peer, y_peer)[stage]
        return remote(
            small_sum.at[stage], small_in.at[stage], small_send.at[stage], small_recv.at[stage], peer
        )

    def small_z_copy(step):
        return remote(
            small_z.at[zz],
            small_z.at[zz],
            small_send.at[2 + step],
            small_recv.at[2 + step],
            place(core, side, lax.rem(zz + step, 4), yy),
        )

    def small_start():
        small_sum[0] = small[...]
        small_copy(0).start()

    def small_next(stage):
        small_copy(stage).wait()
        total = small_sum[stage] + small_in[stage]
        if stage < 2:
            small_sum[stage + 1] = total
            small_copy(stage + 1).start()
        else:
            small_z[zz] = total
            for step in range(1, 4):
                small_z_copy(step).start()

    def small_done():
        for step in range(1, 4):
            small_z_copy(step).wait()
        small_sum[0] = (small_z[0] + small_z[1]) + (small_z[2] + small_z[3])
        small_final[:, 0:256] = small_sum[0, :, pl.ds(pl.multiple_of(blk * 256, 256), 256)]
        pair = small_sum[0, :, pl.ds(pl.multiple_of(FF + 128 * zz, 128), 128)]
        small_final[:, 256:384] = jnp.where(yy == 1, pltpu.roll(pair, DIM, 1), pair)
        small_final[:, 384:512] = small_sum[0, :, FF + WIDTH :]

    def halves(*phases, first=0):
        def both(step, carry):
            for phase in phases:
                phase(lax.rem(step + first, 2))
            return carry

        lax.fori_loop(0, 2, both, 0)

    def begin(half):
        move_arrived(0, half, tok_in)
        hidden[rows_of(half), :] = tok_in[half].astype(F32)

    def finish(half):
        back_out[0, half] = hidden[rows_of(half), :].astype(BF16)
        to_owner(3, half, back_out.at[0, half], out_in)

    def turn_round(layer, half):
        move_arrived(2, half, cot_in)
        rows = rows_of(half)
        grad[rows, :] = cot_in[half].astype(F32)
        dz[rows, :] = (alphas[layer, 1] * grad[rows, :]).astype(BF16)

    def hand_back(half):
        back_out[1, half] = grad[rows_of(half), :].astype(BF16)
        to_owner(4, half, back_out.at[1, half], grad_in)

    barrier = pltpu.get_barrier_semaphore()
    for step in range(1, 4):
        credit(barrier, place(core, side, lax.rem(zz + step, 4), yy))
    for step in range(4):
        credit(barrier, place(1 - core, side, lax.rem(zz + step, 4), yy))
    for peer in (
        x_peer,
        y_peer,
        place(1 - core, side, zz, 1 - yy),
        place(1 - core, 1 - side, zz, yy),
        place(core, 1 - side, zz, 1 - yy),
        place(1 - core, 1 - side, zz, 1 - yy),
    ):
        credit(barrier, peer)

    weight_copies = {}
    for layer in range(LAYERS):
        for number, (source, target) in enumerate(
            ((qkv_hbm, wqkv), (out_hbm, wout), (up_hbm, wup), (down_hbm, wdown))
        ):
            weight_copies[layer, number] = pltpu.make_async_copy(
                source.at[layer], target.at[layer], w_sem.at[layer, number]
            )
    bias_copies = [
        pltpu.make_async_copy(up_bias_hbm, up_bias, w_sem.at[2, 0]),
        pltpu.make_async_copy(down_bias_hbm, down_bias, w_sem.at[2, 1]),
    ]
    weight_copies[0, 0].start()
    pl.semaphore_wait(barrier, 13)
    upper = lax.div(zz, 2)
    for half in (1 - upper, upper):
        to_team(0, half, half_of(tokens, half), tok_in)
    for layer, number in ((1, 0), (0, 1), (0, 2), (0, 3), (1, 1), (1, 2), (1, 3)):
        weight_copies[layer, number].start(priority=1)
    for copy in bias_copies:
        copy.start(priority=1)
    end_second = lax.div(seq_len[0, 0] + seq_len[0, 1], RUNS)
    flag_out[...] = jnp.full((8, 128), end_second.astype(F32), F32)
    for half in (1 - upper, upper):
        to_team(1, half, flag_out, flag_in)
    for layer in range(LAYERS):
        for head in range(OWN):
            rq[layer, head, DIM:, :] = jnp.zeros((DIM, HALF * RUNS), BF16)
    for head in range(OWN):
        ro[head, 0:DIM, :] = jnp.zeros((DIM, HALF * RUNS), BF16)
    for layer in range(LAYERS):
        weight_copies[layer, 0].wait()
        pairs = [
            beside(
                wqkv[layer, :, WIDTH + 128 * pair : WIDTH + 128 * pair + 128].astype(F32),
                wqkv[layer, :, 2 * WIDTH + 128 * pair : 2 * WIDTH + 128 * pair + 128].astype(F32),
            )
            for pair in range(TEAM)
        ]
        for head in range(RUNS):
            at = WIDTH + 128 * head
            wqkv[layer, :, at : at + 128] = pairs[head // 2][head % 2].astype(BF16)
    halves(begin, functools.partial(project, 0), first=upper)
    for half in (1 - upper, upper):
        to_team(2, half, half_of(cotangent, half), cot_in)

    move_arrived(1, 0, flag_in)
    move_arrived(1, 1, flag_in)
    border = jnp.concatenate([flag_in[0, 0:1, :]] * 2, axis=1) - (HALF * lax.div(zz, 2)).astype(F32)
    key_row = lax.broadcasted_iota(jnp.int32, (TILE, TILE), 0)
    query_col = lax.broadcasted_iota(jnp.int32, (TILE, TILE), 1)
    later = key_row > query_col
    key_sub = lax.rem(key_row, HALF).astype(F32) >= border
    query_sub = lax.rem(query_col, HALF).astype(F32) >= border
    apart = jnp.logical_xor(key_sub, query_sub)
    for tile in range(TILES - 1):
        bias[TILE * tile : TILE * tile + TILE, :] = jnp.where(apart, NEGATIVE, 0.0)
    bias[TILE * (TILES - 1) :, :] = jnp.where(jnp.logical_or(later, apart), NEGATIVE, 0.0)

    for copy in (*bias_copies, *(weight_copies[0, number] for number in range(1, 4))):
        copy.wait()
    attend(0, 0)
    attend(0, 1)
    hidden_start(0, 0)
    halves(functools.partial(feed, 0), functools.partial(project, 1))
    for number in range(1, 4):
        weight_copies[1, number].wait()
    attend(1, 0)
    attend(1, 1)
    hidden_pass(0, 0)
    hidden_start(1, 0)
    halves(functools.partial(feed, 1), finish)
    hidden_start(0, 1)
    hidden_start(1, 1)
    hidden_pass(1, 0)

    halves(functools.partial(turn_round, 1))
    make(1)
    feed_back(1)
    hidden_pass(0, 1)
    hidden_pass(1, 1)
    core_done(1)
    make(0)
    attend_back(1, 1)
    core_done(0)
    attend_back(1, 0)
    first_x(1)
    project_back(1, 1)
    heads_grads(1)
    far_z(1)
    first_y(1)
    project_back(1, 0)
    first_x(0)
    far_z(0)
    feed_back(0)
    small_start()
    make(3)
    second_x(0)
    first_z(1)
    make(2)
    first_z(0)
    heads_second(1)
    second_y(1)
    core_done(3)
    core_done(2)
    attend_back(0, 1)
    small_next(0)
    second_x(1)
    far_y(1)
    first_x(3)
    far_z(3)
    first_y(3)
    far_x(0)
    far_z(2)
    first_x(2)
    first_y(2)
    second_z(0)
    far_x(1)
    second_z(1)
    attend_back(0, 0)
    small_next(1)
    second_y(3)
    heads_grads(0)
    small_next(2)
    second_y(2)
    first_z(3)
    far_y(3)
    first_z(2)
    second_x(3)
    far_y(2)
    second_x(2)
    third_done(1)
    far_x(3)
    heads_second(0)
    small_done()
    second_z(3)
    third_done(0)
    heads_third(1)
    far_x(2)
    second_z(2)
    third_done(3)
    project_back(0, 1)
    hand_back(1)
    project_back(0, 0)
    hand_back(0)
    third_done(2)
    final_pass(1)
    final_pass(3)
    heads_third(0)
    final_done(1)
    final_pass(2)
    final_done(3)
    final_pass(0)
    heads_done(1)
    final_done(2)
    final_done(0)
    heads_done(0)
    for half in range(2):
        move_arrived(3, half, out_in)
        move_arrived(4, half, grad_in)

    for half in range(2):
        left(2, 0, half, head_out)
        left(3, 0, half, pack_out)
        to_team_left(0, half, half_of(tokens, half))
        to_team_left(1, half, flag_out)
        to_team_left(2, half, half_of(cotangent, half))
        to_owner_left(3, half, back_out.at[0, half])
        to_owner_left(4, half, back_out.at[1, half])


def results_kernel(
    final, heads, out_block, grad_block, small,
    output, input_grad, qkv_grad, out_grad, up_grad, up_bias_grad, down_grad, down_bias_grad, alpha_grad,
    out_flat, grad_wide, qkv_wide, out_wide, up_wide, down_wide, out_sem,
):
    ends = []

    def write(source, target):
        ends.append(pltpu.make_async_copy(source, target, out_sem.at[len(ends)]))
        ends[-1].start()

    up_bias_grad[...] = small[:, 0:256]
    down_bias_grad[...] = small[:, 256 : 256 + DIM]
    alpha_grad[...] = small[:, 384:386]
    for layer in range(LAYERS):
        for quarter in range(4):

            def block(first, count):
                return final[layer, quarter, first : first + count, :].astype(F32)

            def columns(step):
                return slice(WIDTH * step + 128 * quarter, WIDTH * step + 128 * quarter + 128)

            for step in range(4):
                up_wide[layer, :, columns(step)] = block(DIM * step, DIM)
            out_wide[layer, :, columns(0)] = block(256, DIM)
            down_wide[layer, :, columns(0)] = block(320, 256)
        write(up_wide.at[layer], up_grad.at[layer])
        write(out_wide.at[layer], out_grad.at[layer])
        write(down_wide.at[layer], down_grad.at[layer])
    for half in range(2):
        rows = slice(HALF * half, HALF * half + HALF)
        grad_wide[rows, :] = grad_block[half].astype(F32)
        out_flat[rows, :] = out_block[half]
    write(grad_wide, input_grad)
    write(out_flat, output)
    for layer in range(LAYERS):
        for side in range(2):
            for member in range(TEAM):
                block = heads[layer, side, member].astype(F32)
                columns = (block[:, 0:128], *beside(block[:, 128:256], block[:, 256:384]))
                for step in range(3):
                    at = WIDTH * step + 128 * member
                    qkv_wide[layer, 32 * side : 32 * side + 32, at : at + 128] = columns[step]
        write(qkv_wide.at[layer], qkv_grad.at[layer])
    for end in ends:
        end.wait()


def fast_body(
    tokens, seq_len, qkv_weight, out_weight, up_weight, up_bias, down_weight, down_bias, alphas, cotangent
):
    whole = pl.BlockSpec(memory_space=pltpu.VMEM)
    scalar = pl.BlockSpec(memory_space=pltpu.SMEM)
    far = pl.BlockSpec(memory_space=pl.ANY)
    shape = jax.ShapeDtypeStruct
    rows = HALF * RUNS

    def vmem(*dims):
        return pltpu.VMEM(dims, BF16)

    def wide(*dims):
        return pltpu.VMEM(dims, F32)

    dma = pltpu.SemaphoreType.DMA
    final, heads, out_block, grad_block, small = pl.pallas_call(
        layers_kernel,
        out_shape=(
            vmem(LAYERS, 4, CHUNK, 128),
            vmem(LAYERS, 2, TEAM, DIM // 2, 3 * 128),
            vmem(2, HALF, WIDTH),
            vmem(2, HALF, WIDTH),
            wide(LAYERS, WIDTH),
        ),
        in_specs=[far, scalar, scalar, far, far, far, far, far, far, far],
        out_specs=(whole,) * 5,
        scratch_shapes=[
            vmem(LAYERS, WIDTH, 3 * WIDTH),
            vmem(LAYERS, WIDTH, WIDTH),
            vmem(LAYERS, WIDTH, FF),
            vmem(LAYERS, FF, WIDTH),
            wide(LAYERS, FF),
            wide(LAYERS, WIDTH),
            vmem(2, HALF, WIDTH),
            vmem(2, HALF, WIDTH),
            wide(8, 128),
            wide(2, 8, 128),
            vmem(2, 2, HALF, WIDTH),
            wide(2 * HALF, WIDTH),
            wide(2 * HALF, WIDTH),
            vmem(LAYERS, WIDTH, rows),
            vmem(LAYERS, WIDTH, 2 * HALF),
            vmem(LAYERS, 2 * HALF, WIDTH),
            vmem(LAYERS, 2 * HALF, FF),
            wide(LAYERS, 2 * HALF, WIDTH),
            wide(LAYERS, 2 * HALF, FF),
            wide(LAYERS, 2 * HALF, WIDTH),
            vmem(2 * HALF, WIDTH),
            vmem(2 * HALF, FF),
            vmem(2 * HALF, WIDTH),
            vmem(HALF, 3 * WIDTH),
            vmem(2, TEAM, OWN, PACK, 128),
            vmem(2, TEAM, OWN, DIM, 128),
            vmem(2, TEAM, OWN, PACK, 128),
            vmem(2, TEAM, OWN, DIM, 128),
            vmem(2, TEAM, OWN, DIM, 128),
            vmem(LAYERS, OWN, rows, 128),
            vmem(LAYERS, OWN, 128, rows),
            vmem(LAYERS, OWN, 128, rows),
            vmem(OWN, 128, rows),
            wide(LAYERS, OWN, DIM, rows),
            wide(LAYERS, OWN, 1, rows),
            wide(OWN, rows, 128),
            wide(OWN, DIM, rows),
            wide(rows, TILE),
            vmem(LAYERS, 2, 2, 2, 2, 2, CHUNK, 128),
            vmem(2, 2, 2, 2, CHUNK, 128),
            vmem(2, 2, 2, TOTALS[0], 128),
            vmem(2, 2, TOTALS[1], 128),
            vmem(2, 2, TOTALS[0], 128),
            vmem(2, 2, 2, TOTALS[1], 128),
            vmem(LAYERS, 2, CHUNK, 128),
            vmem(LAYERS, CHUNK, 128),
            vmem(2, 2, 2, TOTALS[2], 128),
            vmem(2, 2, TOTALS[2], 128),
            vmem(2, TOTALS[2], 128),
            vmem(TOTALS[2], 128),
            vmem(LAYERS, 4, 2, DIM, 3 * 128),
            vmem(LAYERS, 4, 2, DIM // 2, 3 * 128),
            vmem(LAYERS, 4, 2, DIM // 2, 3 * 128),
            vmem(LAYERS, 2, DIM // 2, 3 * 128),
            wide(LAYERS, SMALL),
            wide(3, LAYERS, SMALL),
            wide(4, LAYERS, SMALL),
            wide(3, LAYERS, SMALL),
            dma((LAYERS + 1, 4)),
            dma((5, 2)),
            dma((5, 2)),
            dma((4, LAYERS, 2, OWN)),
            dma((4, LAYERS, 2, OWN)),
            dma((len(PARTS),)),
            dma((len(PARTS),)),
            dma((len(PARTS), 3)),
            dma((len(PARTS), 3)),
            dma((len(PARTS), 3)),
            dma((len(PARTS), 3)),
            dma((len(PARTS), 3, 2)),
            dma((len(PARTS), 3, 2)),
            dma((len(PARTS), 3)),
            dma((len(PARTS), 3)),
            dma((LAYERS, 2, 3)),
            dma((LAYERS, 2, 3)),
            dma((LAYERS,)),
            dma((LAYERS,)),
            dma((LAYERS, 4)),
            dma((LAYERS, 4)),
            dma((LAYERS, 8)),
            dma((LAYERS, 8)),
            dma((6,)),
            dma((6,)),
            pltpu.SemaphoreType.REGULAR((2,)),
        ],
        compiler_params=pltpu.CompilerParams(
            collective_id=0, has_side_effects=True, vmem_limit_bytes=61 * 1024 * 1024
        ),
        name="layers",
    )(
        tokens, seq_len, alphas, up_bias, down_bias, cotangent,
        qkv_weight, out_weight, up_weight, down_weight,
    )
    return tuple(
        pl.pallas_call(
            results_kernel,
            out_shape=(
                shape((2 * HALF, WIDTH), BF16),
                shape((2 * HALF, WIDTH), F32),
                shape((LAYERS, DIM, 3 * WIDTH), F32),
                shape((LAYERS, DIM, WIDTH), F32),
                shape((LAYERS, DIM, FF), F32),
                shape((LAYERS, FF // RUNS), F32),
                shape((LAYERS, FF // RUNS, WIDTH), F32),
                shape((LAYERS, DIM), F32),
                shape((LAYERS, 2), F32),
            ),
            in_specs=[whole] * 5,
            out_specs=(far, far, far, far, far, whole, far, whole, whole),
            scratch_shapes=[
                vmem(2 * HALF, WIDTH),
                wide(2 * HALF, WIDTH),
                wide(LAYERS, DIM, 3 * WIDTH),
                wide(LAYERS, DIM, WIDTH),
                wide(LAYERS, DIM, FF),
                wide(LAYERS, FF // RUNS, WIDTH),
                dma((10,)),
            ],
            compiler_params=pltpu.CompilerParams(vmem_limit_bytes=24 * 1024 * 1024),
            name="results",
        )(final, heads, out_block, grad_block, small)
    )


def layout(seq_len, local_count, cycle_size):
    piece_rows = seq_len[0] // cycle_size
    end_rows = jnp.cumsum(piece_rows)
    start_rows = end_rows - piece_rows
    local_rows = jnp.arange(local_count, dtype=jnp.int32)
    segment = jnp.sum((local_rows[:, None] >= end_rows[None, :]).astype(jnp.int32), axis=1)
    picked = segment[:, None] == jnp.arange(seq_len.shape[1], dtype=jnp.int32)[None, :]
    offset = local_rows - jnp.sum(jnp.where(picked, start_rows[None, :], 0), axis=1)
    span_rows = jnp.sum(jnp.where(picked, piece_rows[None, :], 0), axis=1)
    return (segment, offset, span_rows)


def gelu_exact(values):
    return jax.nn.gelu(values, approximate=False)


def key_block(whole, geometry, block_index, head_count):
    query_seg, query_pos, seg_all, pos_all, block_rows, score_scale = geometry
    first_row = block_index * block_rows
    key_piece = lax.dynamic_slice_in_dim(whole, first_row, block_rows, 0)
    key_seg = lax.dynamic_slice_in_dim(seg_all, first_row, block_rows, 0)
    key_pos = lax.dynamic_slice_in_dim(pos_all, first_row, block_rows, 0)
    half_width = key_piece.shape[1] // 2
    keys_part = key_piece[:, :half_width].reshape(block_rows, head_count, -1)
    values_part = key_piece[:, half_width:].reshape(block_rows, head_count, -1)
    return (keys_part, values_part, key_seg, key_pos)


def block_scores(queries, keys_part, key_seg, key_pos, geometry):
    query_seg, query_pos, seg_all, pos_all, block_rows, score_scale = geometry
    scores = (
        jnp.einsum("qhd,khd->hqk", queries, keys_part, preferred_element_type=jnp.float32)
        * score_scale
    )
    allowed = (query_seg[:, None] == key_seg[None, :]) & (key_pos[None, :] <= query_pos[:, None])
    return (scores, allowed[None])


def attend(queries, whole, geometry):
    row_count, head_count, head_dim = queries.shape
    block_count = whole.shape[0] // geometry[4]

    def statistics(running, block_index):
        largest, totals = running
        keys_part, values_part, key_seg, key_pos = key_block(
            whole, geometry, block_index, head_count
        )
        scores, allowed = block_scores(queries, keys_part, key_seg, key_pos, geometry)
        newest = jnp.maximum(largest, jnp.max(jnp.where(allowed, scores, NEGATIVE), axis=2))
        weights = jnp.where(allowed, jnp.exp(scores - newest[:, :, None]), 0.0)
        totals = totals * jnp.exp(largest - newest) + jnp.sum(weights, axis=2)
        return ((newest, totals), None)

    initial = (
        jnp.full((head_count, row_count), NEGATIVE, jnp.float32),
        jnp.zeros((head_count, row_count), jnp.float32),
    )
    (largest, totals), unused = lax.scan(statistics, initial, jnp.arange(block_count))
    log_total = largest + jnp.log(totals)

    def weighted(output_sum, block_index):
        keys_part, values_part, key_seg, key_pos = key_block(
            whole, geometry, block_index, head_count
        )
        scores, allowed = block_scores(queries, keys_part, key_seg, key_pos, geometry)
        probs = jnp.where(allowed, jnp.exp(scores - log_total[:, :, None]), 0.0).astype(
            jnp.bfloat16
        )
        output_sum = output_sum + jnp.einsum(
            "hqk,khd->qhd", probs, values_part, preferred_element_type=jnp.float32
        )
        return (output_sum, None)

    output_sum, unused = lax.scan(
        weighted, jnp.zeros((row_count, head_count, head_dim), jnp.float32), jnp.arange(block_count)
    )
    return (output_sum, log_total)


def attend_back(queries, whole, log_total, delta_sum, grad_heads, geometry):
    row_count, head_count, head_dim = queries.shape
    block_rows = geometry[4]
    score_scale = geometry[5]
    block_count = whole.shape[0] // block_rows

    def gradients(query_grad, block_index):
        keys_part, values_part, key_seg, key_pos = key_block(
            whole, geometry, block_index, head_count
        )
        scores, allowed = block_scores(queries, keys_part, key_seg, key_pos, geometry)
        probs = jnp.where(allowed, jnp.exp(scores - log_total[:, :, None]), 0.0)
        grad_probs = jnp.einsum(
            "qhd,khd->hqk", grad_heads, values_part, preferred_element_type=jnp.float32
        )
        grad_scores = (probs * (grad_probs - delta_sum[:, :, None])).astype(jnp.bfloat16)
        query_grad = (
            query_grad
            + jnp.einsum("hqk,khd->qhd", grad_scores, keys_part, preferred_element_type=jnp.float32)
            * score_scale
        )
        key_grad = (
            jnp.einsum("hqk,qhd->khd", grad_scores, queries, preferred_element_type=jnp.float32)
            * score_scale
        )
        value_grad = jnp.einsum(
            "hqk,qhd->khd",
            probs.astype(jnp.bfloat16),
            grad_heads,
            preferred_element_type=jnp.float32,
        )
        joined = jnp.concatenate(
            [key_grad.reshape(block_rows, -1), value_grad.reshape(block_rows, -1)], axis=1
        )
        return (query_grad, joined)

    query_grad, stacked = lax.scan(
        gradients,
        jnp.zeros((row_count, head_count, head_dim), jnp.float32),
        jnp.arange(block_count),
    )
    return (query_grad, stacked.reshape(whole.shape[0], -1))


def layer_forward(hidden, layer_index, weights, geometry):
    qkv_weight, out_weight, up_weight, up_bias, down_weight, down_bias, alphas = weights
    row_count, model_width = hidden.shape
    projection = qkv_weight[layer_index]
    rounded = hidden.astype(jnp.bfloat16)
    queries = (
        jnp.dot(rounded, projection[:, :model_width], preferred_element_type=jnp.float32)
        .astype(jnp.bfloat16)
        .reshape(row_count, HEADS, -1)
    )
    key_value = jnp.dot(
        rounded, projection[:, model_width:], preferred_element_type=jnp.float32
    ).astype(jnp.bfloat16)
    whole = lax.all_gather(key_value, "blk", axis=0, tiled=True)
    heads_out, log_total = attend(queries, whole, geometry)
    heads_rounded = heads_out.reshape(row_count, model_width).astype(jnp.bfloat16)
    branch = jnp.dot(heads_rounded, out_weight[layer_index], preferred_element_type=jnp.float32)
    alpha_pair = alphas[layer_index]
    middle = hidden + alpha_pair[0] * branch
    entered = middle.astype(jnp.bfloat16)
    gate_pre = (
        jnp.dot(entered, up_weight[layer_index], preferred_element_type=jnp.float32)
        + up_bias[layer_index]
    )
    activated = gelu_exact(gate_pre).astype(jnp.bfloat16)
    second = (
        jnp.dot(activated, down_weight[layer_index], preferred_element_type=jnp.float32)
        + down_bias[layer_index]
    )
    result = middle + alpha_pair[1] * second
    saved = (
        rounded,
        queries,
        key_value,
        whole,
        heads_out,
        heads_rounded,
        log_total,
        branch,
        entered,
        gate_pre,
        activated,
        second,
    )
    return (result, saved)


def layer_backward(grad_hidden, saved, layer_index, weights, geometry):
    qkv_weight, out_weight, up_weight, up_bias, down_weight, down_bias, alphas = weights
    (
        rounded,
        queries,
        key_value,
        saved_whole,
        heads_out,
        heads_rounded,
        log_total,
        branch,
        entered,
        gate_pre,
        activated,
        second,
    ) = saved
    row_count = grad_hidden.shape[0]
    alpha_pair = alphas[layer_index]
    grad_second = (alpha_pair[1] * grad_hidden).astype(jnp.bfloat16)
    alpha_second = jnp.sum(grad_hidden * second)
    bias_down = jnp.sum(grad_second.astype(jnp.float32), axis=0)
    grad_down = jnp.einsum("tf,td->fd", activated, grad_second, preferred_element_type=jnp.float32)
    grad_act = jnp.einsum(
        "td,fd->tf", grad_second, down_weight[layer_index], preferred_element_type=jnp.float32
    )
    unused, gelu_pull = jax.vjp(gelu_exact, gate_pre)
    grad_gate = gelu_pull(grad_act)[0].astype(jnp.bfloat16)
    bias_up = jnp.sum(grad_gate.astype(jnp.float32), axis=0)
    grad_up = jnp.einsum("td,tf->df", entered, grad_gate, preferred_element_type=jnp.float32)
    grad_middle = grad_hidden + jnp.einsum(
        "tf,df->td", grad_gate, up_weight[layer_index], preferred_element_type=jnp.float32
    )
    grad_branch = (alpha_pair[0] * grad_middle).astype(jnp.bfloat16)
    alpha_first = jnp.sum(grad_middle * branch)
    grad_proj_out = jnp.einsum(
        "te,td->ed", heads_rounded, grad_branch, preferred_element_type=jnp.float32
    )
    grad_heads = (
        jnp.einsum(
            "td,ed->te", grad_branch, out_weight[layer_index], preferred_element_type=jnp.float32
        )
        .astype(jnp.bfloat16)
        .reshape(queries.shape)
    )
    delta_sum = jnp.sum(grad_heads.astype(jnp.float32) * heads_out, axis=2).T
    whole = lax.all_gather(key_value, "blk", axis=0, tiled=True)
    query_grad, key_terms = attend_back(queries, whole, log_total, delta_sum, grad_heads, geometry)
    key_grads = lax.psum_scatter(
        key_terms.astype(jnp.bfloat16), "blk", scatter_dimension=0, tiled=True
    )
    grad_proj = jnp.concatenate(
        [query_grad.reshape(row_count, -1).astype(jnp.bfloat16), key_grads], axis=1
    )
    grad_qkv = jnp.einsum("td,te->de", rounded, grad_proj, preferred_element_type=jnp.float32)
    grad_input = grad_middle + jnp.einsum(
        "te,de->td", grad_proj, qkv_weight[layer_index], preferred_element_type=jnp.float32
    )
    layer_grads = (
        grad_qkv,
        grad_proj_out,
        grad_up,
        bias_up,
        grad_down,
        bias_down,
        jnp.stack([alpha_first, alpha_second]),
    )
    return (grad_input, layer_grads)


def reduce_all(layer_results, cycle_size):
    stacked = [
        jnp.stack([layer_entry[member] for layer_entry in layer_results], axis=0)
        for member in range(6)
    ]
    alpha_tiles = jnp.stack(
        [jnp.tile(layer_entry[6], cycle_size) for layer_entry in layer_results], axis=0
    )
    shares = (
        lax.psum_scatter(
            stacked[0].astype(jnp.bfloat16), "blk", scatter_dimension=1, tiled=True
        ).astype(jnp.float32),
        lax.psum_scatter(
            stacked[1].astype(jnp.bfloat16), "blk", scatter_dimension=1, tiled=True
        ).astype(jnp.float32),
        lax.psum_scatter(
            stacked[2].astype(jnp.bfloat16), "blk", scatter_dimension=1, tiled=True
        ).astype(jnp.float32),
        lax.psum_scatter(
            stacked[3].astype(jnp.bfloat16), "blk", scatter_dimension=1, tiled=True
        ).astype(jnp.float32),
        lax.psum_scatter(
            stacked[4].astype(jnp.bfloat16), "blk", scatter_dimension=1, tiled=True
        ).astype(jnp.float32),
        lax.psum_scatter(
            stacked[5].astype(jnp.bfloat16), "blk", scatter_dimension=1, tiled=True
        ).astype(jnp.float32),
        lax.psum_scatter(
            alpha_tiles.astype(jnp.bfloat16), "blk", scatter_dimension=1, tiled=True
        ).astype(jnp.float32),
    )
    return (
        lax.psum(shares[0].astype(jnp.bfloat16), "grp").astype(jnp.float32),
        lax.psum(shares[1].astype(jnp.bfloat16), "grp").astype(jnp.float32),
        lax.psum(shares[2].astype(jnp.bfloat16), "grp").astype(jnp.float32),
        lax.psum(shares[3].astype(jnp.bfloat16), "grp").astype(jnp.float32),
        lax.psum(shares[4].astype(jnp.bfloat16), "grp").astype(jnp.float32),
        lax.psum(shares[5].astype(jnp.bfloat16), "grp").astype(jnp.float32),
        lax.psum(shares[6].astype(jnp.bfloat16), "grp").astype(jnp.float32),
    )


def body(
    tokens,
    seq_len,
    qkv_weight,
    out_weight,
    up_weight,
    up_bias,
    down_weight,
    down_bias,
    alphas,
    cotangent,
):
    row_count, model_width = tokens.shape
    cycle_size = lax.axis_size("blk")
    cycle_place = lax.axis_index("blk")
    head_dim = model_width // HEADS
    total_rows = cycle_size * row_count
    block_rows = min(max(row_count, 512), total_rows)
    segment, offset, span_rows = layout(seq_len, row_count, cycle_size)
    query_pos = cycle_place * span_rows + offset
    seg_all = jnp.tile(segment, cycle_size)
    pos_all = jnp.repeat(jnp.arange(cycle_size, dtype=jnp.int32), row_count) * jnp.tile(
        span_rows, cycle_size
    ) + jnp.tile(offset, cycle_size)
    geometry = (segment, query_pos, seg_all, pos_all, block_rows, head_dim ** (-0.5))
    weights = (qkv_weight, out_weight, up_weight, up_bias, down_weight, down_bias, alphas)
    hidden = tokens.astype(jnp.float32)
    saved_layers = []
    for layer_index in range(LAYERS):
        hidden, saved = layer_forward(hidden, layer_index, weights, geometry)
        saved_layers.append(saved)
    output = hidden.astype(jnp.bfloat16)
    grad_hidden = cotangent.astype(jnp.float32)
    layer_results = []
    for layer_index in reversed(range(LAYERS)):
        grad_hidden, layer_grads = layer_backward(
            grad_hidden, saved_layers[layer_index], layer_index, weights, geometry
        )
        layer_results.insert(0, layer_grads)
    finals = reduce_all(layer_results, cycle_size)
    return (
        output,
        grad_hidden,
        finals[0],
        finals[1],
        finals[2],
        finals[3],
        finals[4],
        finals[5],
        finals[6],
    )


def solution(mesh):
    placed = (
        P(("grp", "blk"), None),
        P("grp", None),
        P(),
        P(),
        P(),
        P(),
        P(),
        P(),
        P(),
        P(("grp", "blk"), None),
    )
    sizes = (mesh.shape["grp"], mesh.shape["blk"])
    return jax.shard_map(
        fast_body if sizes == (4, RUNS) else body,
        mesh=mesh,
        in_specs=placed,
        out_specs=(
            P(("grp", "blk"), None),
            P(("grp", "blk"), None),
            P(None, "blk", None),
            P(None, "blk", None),
            P(None, "blk", None),
            P(None, "blk"),
            P(None, "blk", None),
            P(None, "blk"),
            P(),
        ),
        check_vma=False,
    )
```

```python
import functools

import jax
import jax.numpy as jnp
from jax import lax
from jax.experimental import pallas as pl
from jax.experimental.pallas import tpu as pltpu
from jax.sharding import PartitionSpec as P

HEADS = 8
LAYERS = 2
NEGATIVE = -1e30
MESH = pl.DeviceIdType.MESH
F32 = jnp.float32
BF16 = jnp.bfloat16

HALF = 128
RUNS = 8
TEAM = 4
OWN = RUNS // TEAM
DIM = 64
WIDTH = 512
FF = 2048
CUT = 512
TILE = 256
TILES = HALF * RUNS // TILE
PACK = HALF + DIM
CHUNK = 576
SMALL = FF + WIDTH + 128
PARTS = ((1, 0, 320), (1, 320, 256), (0, 0, 320), (0, 320, 256))
SHARES = ((192, 0, 128), (176, 0, 80), (128, 96, 96), (80, 128, 48))


def spans():
    places, totals = {}, [0, 0, 0]
    for part, counts in enumerate(SHARES):
        first = PARTS[part][1]
        for route, count in enumerate(counts):
            places[part, route] = (first, totals[route], count)
            first += count
            totals[route] += count
    return places, totals


SPANS, TOTALS = spans()

SLOPE_AT = 0.28
TAIL = (
    0.11652077851573843,
    0.06749675579450809,
    0.2689101589486142,
    -0.23699347299932225,
    0.3898740127620002,
    -0.10580824228351815,
)


def nn(a, b):
    return lax.dot_general(a, b, (((1,), (0,)), ((), ())), preferred_element_type=F32)


def nt(a, b):
    return lax.dot_general(a, b, (((1,), (1,)), ((), ())), preferred_element_type=F32)


def beside(first, other):
    low = lax.broadcasted_iota(jnp.int32, first.shape, 1) < DIM
    return (
        jnp.where(low, first, pltpu.roll(other, DIM, 1)),
        jnp.where(low, pltpu.roll(first, DIM, 1), other),
    )


def layers_kernel(
    tokens, seq_len, alphas, up_bias_hbm, down_bias_hbm, cotangent, qkv_hbm, out_hbm, up_hbm, down_hbm,
    final, heads_all, out_in, grad_in, small_final,
    wqkv, wout, wup, wdown, up_bias, down_bias,
    tok_in, cot_in, flag_out, flag_in, back_out,
    hidden, grad, hid_all, attn_t, entered, act, branch, slope, second,
    dz, du, da, dqkv,
    pack_out, head_out, pack_in, o_in, do_in,
    kv, kv_t, rq, ro, o_t, lse, acc, dq_t, bias,
    parts, core_in, xa_in, xb_in, ya_in, yb_in, near_in, far_in, third_near, third_far, third_x, third_y,
    heads_out, heads_x, heads_z, heads_sum, small, small_in, small_z, small_sum,
    w_sem, move_send, move_recv, a2a_send, a2a_recv, core_send, core_recv, x_send, x_recv, y_send, y_recv,
    z_send, z_recv, fin_send, fin_recv, hid_send, hid_recv, hx_send, hx_recv, hz_send, hz_recv, hf_send, hf_recv,
    small_send, small_recv, core_free,
):
    grp = lax.axis_index("grp")
    blk = lax.axis_index("blk")
    core = lax.rem(grp, 2)
    side = lax.div(grp, 2)
    yy = lax.rem(blk, 2)
    zz = lax.div(blk, 2)
    member = 2 * core + yy
    far_side = 2 * (1 - side) + core

    def place(c, x, z, y):
        return (2 * x + c, 2 * z + y)

    core_peer = place(1 - core, side, zz, yy)
    x_peer = place(core, 1 - side, zz, yy)
    y_peer = place(core, side, zz, 1 - yy)
    high, odd = lax.div(zz, 2), lax.rem(zz, 2)
    near_peer = place(core, side, 2 * high + 1 - odd, yy)
    far_peer = place(core, side, 2 * (1 - high) + odd, yy)

    def remote(source, target, send, recv, peer):
        return pltpu.make_async_remote_copy(
            src_ref=source,
            dst_ref=target,
            send_sem=send,
            recv_sem=recv,
            device_id=peer,
            device_id_type=MESH,
        )

    def credit(semaphore, peer, count=1):
        pl.semaphore_signal(semaphore, inc=count, device_id=peer, device_id_type=MESH)

    def moved(kind, slot, source, target, at, core_at, z_at):
        here = jnp.logical_and(core_at == core, z_at == zz)

        @pl.when(here)
        def _():
            pltpu.make_async_copy(source, target.at[at], move_recv.at[kind, at]).start()

        @pl.when(jnp.logical_not(here))
        def _():
            pltpu.make_async_remote_copy(
                src_ref=source,
                dst_ref=target.at[at],
                send_sem=move_send.at[kind, slot],
                recv_sem=move_recv.at[kind, at],
                device_id=place(core_at, side, z_at, yy),
                device_id_type=MESH,
            ).start()

    def move_left(kind, slot, source, core_at, z_at):
        here = jnp.logical_and(core_at == core, z_at == zz)

        @pl.when(jnp.logical_not(here))
        def _():
            pltpu.make_async_copy(source, source, move_send.at[kind, slot]).wait()

    def move_arrived(kind, at, target):
        pltpu.make_async_copy(target.at[at], target.at[at], move_recv.at[kind, at]).wait()

    def to_team(kind, half, source, target):
        moved(kind, half, source, target, lax.div(zz, 2), lax.rem(zz, 2), 2 * half + core)

    def to_team_left(kind, half, source):
        move_left(kind, half, source, lax.rem(zz, 2), 2 * half + core)

    def to_owner(kind, chunk, source, target):
        moved(kind, chunk, source, target, lax.div(zz, 2), lax.rem(zz, 2), core + 2 * chunk)

    def to_owner_left(kind, chunk, source):
        move_left(kind, chunk, source, lax.rem(zz, 2), core + 2 * chunk)

    def half_of(ref, half):
        return ref.at[pl.ds(pl.multiple_of(HALF * half, HALF), HALF)]

    def rows_of(half):
        return pl.ds(pl.multiple_of(half * HALF, HALF), HALF)

    def slot_of(other):
        return lax.rem(other + TEAM - member, TEAM)

    def exchange(kind, layer, half, outgoing, incoming, head=None):
        at = () if head is None else (head,)
        incoming[(half, 0, *at)] = outgoing[(half, member, *at)]
        for step in range(1, TEAM):
            peer = lax.rem(member + step, TEAM)
            remote(
                outgoing.at[(half, peer, *at)],
                incoming.at[(half, TEAM - step, *at)],
                a2a_send.at[kind, layer, half, head or 0],
                a2a_recv.at[kind, layer, half, head or 0],
                place(lax.div(peer, 2), side, zz, lax.rem(peer, 2)),
            ).start()

    def arrived(kind, layer, half, incoming, head=None):
        at = () if head is None else (head,)
        whole = incoming.at[(half, pl.ds(1, TEAM - 1), *at)]
        pltpu.make_async_copy(whole, whole, a2a_recv.at[kind, layer, half, head or 0]).wait()

    def left(kind, layer, half, outgoing):
        for head in range(OWN) if kind in (0, 3) else (None,):
            at = () if head is None else (head,)
            whole = outgoing.at[(half, pl.ds(1, TEAM - 1), *at)]
            pltpu.make_async_copy(whole, whole, a2a_send.at[kind, layer, half, head or 0]).wait()

    def tokens_of(chunk, other):
        return pl.ds(pl.multiple_of(HALF * (TEAM * chunk + other), HALF), HALF)

    def hidden_copy(layer, chunk, which):
        whose = 2 * core + 1 - yy if which == 2 else member
        block = hid_all.at[layer, :, tokens_of(chunk, whose)]
        return remote(
            block,
            block,
            hid_send.at[layer, chunk, which],
            hid_recv.at[layer, chunk, which],
            y_peer if which == 0 else core_peer,
        )

    def hidden_start(layer, chunk):
        for which in range(2):
            hidden_copy(layer, chunk, which).start()

    def hidden_pass(layer, chunk):
        hidden_copy(layer, chunk, 0).wait()
        hidden_copy(layer, chunk, 2).start()

    def hidden_done(layer, chunk):
        for which in range(1, 3):
            hidden_copy(layer, chunk, which).wait()

    def project(layer, half):
        rows = rows_of(half)
        rounded = hidden[rows, :].astype(BF16)
        if layer == 1:
            left(0, 0, half, pack_out)
        queries = (nn(rounded, wqkv[layer, :, 0:WIDTH]) * (DIM ** -0.5)).astype(BF16).T
        for head in range(RUNS):
            pack_out[half, head // 2, head % 2, HALF:, :] = queries[DIM * head : DIM * head + DIM, :]
        for step in range(2):
            at = WIDTH * (step + 1)
            keys_values = nn(rounded, wqkv[layer, :, at : at + WIDTH]).astype(BF16)
            for head in range(4):
                pack_out[half, 2 * step + head // 2, head % 2, 0:HALF, :] = keys_values[
                    :, 128 * head : 128 * head + 128
                ]
        for head in range(OWN):
            exchange(0, layer, half, pack_out, pack_in, head)
        hid_all[layer, :, tokens_of(half, member)] = rounded.T

    def attend(layer, chunk):
        if layer == 1:
            left(1, 0, chunk, head_out)

        def one_head(head, carry):
            arrived(0, layer, chunk, pack_in, head)
            for other in range(TEAM):
                slot = slot_of(other)
                start = HALF * (TEAM * chunk + other)
                span = slice(start, start + HALF)
                block = pack_in[chunk, slot, head, 0:HALF, :]
                kv[layer, head, span, :] = block
                kv_t[layer, head, :, span] = block.T
                rq[layer, head, 0:DIM, span] = pack_in[chunk, slot, head, HALF:, :]

            def scores_of(i):
                count = TILE * (i + 1)
                tile = rq[layer, head, :, TILE * i : TILE * i + TILE]
                return nn(kv[layer, head, 0:count, :], tile) + bias[TILE * TILES - count :, :]

            ahead = [scores_of(i) for i in (2 * chunk, 2 * chunk + 1)]
            for i in (2 * chunk, 2 * chunk + 1):
                columns = slice(TILE * i, TILE * i + TILE)
                count = TILE * (i + 1)
                scores = ahead[i - 2 * chunk]
                largest = jnp.max(scores, axis=0, keepdims=True)
                weight = jnp.exp(scores - largest)
                total = jnp.sum(weight, axis=0, keepdims=True)
                summed = nn(kv_t[layer, head, DIM:, 0:count], weight.astype(BF16))
                summed = summed / total
                o_t[layer, head, :, columns] = summed
                lse[layer, head, :, columns] = largest + jnp.log(total)
                rounded = summed.astype(BF16)
                for part in range(2):
                    head_out[chunk, 2 * (i - 2 * chunk) + part, head] = rounded[
                        :, HALF * part : HALF * part + HALF
                    ]
            return carry

        for head in range(OWN):
            one_head(head, 0)
        exchange(1, layer, chunk, head_out, o_in)

    def feed(layer, half):
        rows = rows_of(half)
        arrived(1, layer, half, o_in)
        for head in range(RUNS):
            attn_t[layer, DIM * head : DIM * head + DIM, rows] = o_in[half, slot_of(head // 2), head % 2]
        attn = attn_t[layer, :, rows].T
        grown = nn(attn, wout[layer])
        branch[layer, rows, :] = grown
        middle = hidden[rows, :] + alphas[layer, 0] * grown
        rounded = middle.astype(BF16)
        entered[layer, rows, :] = rounded
        total = jnp.zeros((HALF, WIDTH), F32)

        def gate_of(step):
            cut = slice(CUT * step, CUT * step + CUT)
            return nn(rounded, wup[layer, :, cut]) + up_bias[layer : layer + 1, cut]

        coming = gate_of(0)
        for step in range(FF // CUT):
            cut = slice(CUT * step, CUT * step + CUT)
            gate = coming
            if step + 1 < FF // CUT:
                coming = gate_of(step + 1)
            bell = jnp.exp(gate * gate * -0.5)
            near = pl.reciprocal(1.0 + SLOPE_AT * jnp.abs(gate), approx=True)
            tail = jnp.full_like(gate, TAIL[5])
            for factor in TAIL[4::-1]:
                tail = tail * near + factor
            tail = bell * (tail * near)
            risen = jnp.where(gate > 0.0, 1.0 - tail, tail)
            slope[layer, rows, cut] = risen + gate * bell * 0.3989422804014327
            active = (gate * risen).astype(BF16)
            act[layer, rows, cut] = active
            total = total + nn(active, wdown[layer, cut, :])
        total = total + down_bias[layer : layer + 1, :]
        second[layer, rows, :] = total
        hidden[rows, :] = middle + alphas[layer, 1] * total

    def total_of(values):
        return jnp.sum(jnp.sum(values, axis=0, keepdims=True), axis=1, keepdims=True)

    def feed_back(layer):
        start = grad[...]
        if layer == 0:
            dz[...] = (alphas[layer, 1] * start).astype(BF16)
        scaled = dz[...]
        alpha_second = total_of(start * second[layer])
        small[layer : layer + 1, FF : FF + WIDTH] = jnp.sum(scaled.astype(F32), axis=0, keepdims=True)
        middle = start
        coming = nt(scaled, wdown[layer, 0:CUT, :])
        for step in range(FF // CUT):
            cut = slice(CUT * step, CUT * step + CUT)
            raw = coming
            if step + 1 < FF // CUT:
                coming = nt(scaled, wdown[layer, CUT * (step + 1) : CUT * (step + 2), :])
            gate = (raw * slope[layer, :, cut]).astype(BF16)
            du[:, cut] = gate
            small[layer : layer + 1, cut] = jnp.sum(gate.astype(F32), axis=0, keepdims=True)
            middle = middle + nt(gate, wup[layer, :, cut])
        grad[...] = middle
        mixed = (alphas[layer, 0] * middle).astype(BF16)
        da[...] = mixed
        spread = nt(wout[layer], mixed).astype(BF16)
        for chunk in (1, 0):
            left(*((1, 1) if layer == 1 else (2, 1)), chunk, head_out)
            for head in range(RUNS):
                head_out[chunk, head // 2, head % 2] = spread[
                    DIM * head : DIM * head + DIM, HALF * chunk : HALF * chunk + HALF
                ]
            exchange(2, layer, chunk, head_out, do_in)
        alpha_first = total_of(middle * branch[layer])
        column = lax.broadcasted_iota(jnp.int32, (1, 128), 1)
        small[layer : layer + 1, FF + WIDTH :] = jnp.where(
            column == 0, alpha_first, jnp.where(column == 1, alpha_second, 0.0)
        )

    def attend_back(layer, chunk):
        arrived(2, layer, chunk, do_in)
        left(*((0, 1) if layer == 1 else (3, 1)), chunk, pack_out)

        def one_head(head, carry):
            for other in range(TEAM):
                start = HALF * (TEAM * chunk + other)
                ro[head, DIM:, start : start + HALF] = do_in[chunk, slot_of(other), head]
            for i in (2 * chunk, 2 * chunk + 1):
                columns = slice(TILE * i, TILE * i + TILE)
                query_tile = rq[layer, head, :, columns]
                grad_tile = ro[head, :, columns]
                log_total = lse[layer, head, :, columns]
                delta = jnp.sum(
                    ro[head, DIM:, columns].astype(F32) * o_t[layer, head, :, columns],
                    axis=0,
                    keepdims=True,
                )
                count = TILE * (i + 1)
                keys = kv[layer, head, 0:count, :]
                weight = jnp.exp(nn(keys, query_tile) + bias[TILE * TILES - count :, :] - log_total)
                scored = (weight * (nn(keys, grad_tile) - delta)).astype(BF16)
                term = nt(scored, query_tile) + nt(weight.astype(BF16), grad_tile)
                if chunk == 1 and i == 2:
                    acc[head, 0:count, :] = term
                elif chunk == 1:
                    acc[head, 0 : count - TILE, :] += term[0 : count - TILE, :]
                    acc[head, count - TILE : count, :] = term[count - TILE :, :]
                else:
                    acc[head, 0:count, :] += term
                query_grad = nn(kv_t[layer, head, 0:DIM, 0:count], scored)
                dq_t[head, :, columns] = query_grad * (DIM ** -0.5)
            for other in range(TEAM):
                start = HALF * (TEAM * chunk + other)
                span = slice(start, start + HALF)
                pack_out[chunk, other, head, 0:HALF, :] = acc[head, span, :].astype(BF16)
                pack_out[chunk, other, head, HALF:, :] = dq_t[head, :, span].astype(BF16)
            exchange(3, layer, chunk, pack_out, pack_in, head)
            return carry

        for head in range(OWN):
            one_head(head, 0)

    def project_back(layer, half):
        for head in range(OWN):
            arrived(3, layer, half, pack_in, head)
        turned = jnp.concatenate(
            [pack_in[half, slot_of(head // 2), head % 2, HALF:, :] for head in range(RUNS)], axis=0
        )
        dqkv[:, 0:WIDTH] = turned.T
        for head in range(RUNS):
            at = WIDTH + 128 * head
            dqkv[:, at : at + 128] = pack_in[half, slot_of(head // 2), head % 2, 0:HALF, :]
        rows = rows_of(half)
        grad[rows, :] = grad[rows, :] + nt(dqkv[...], wqkv[layer])

    def scatter_rows(layer, result, first_row):
        for run in range(RUNS):
            for quarter in range(4):
                parts[layer, quarter % 2, quarter // 2, run // 4, run // 2 % 2, run % 2, first_row : first_row + DIM, :] = result[
                    DIM * run : DIM * run + DIM, 128 * quarter : 128 * quarter + 128
                ].astype(BF16)

    def make(part):
        layer, first, count = PARTS[part]
        if first < 256:
            turned = entered[layer].T
        for row in range(first, min(first + count, 256), DIM):
            step = row // DIM
            scatter_rows(layer, nn(turned, du[:, CUT * step : CUT * step + CUT]), row)
        if first <= 256 < first + count:
            scatter_rows(layer, nn(attn_t[layer], da[...]), 256)
        if first >= 320:
            turned = dz[...].T
            for step in range(FF // CUT):
                result = nn(turned, act[layer, :, CUT * step : CUT * step + CUT])
                for block in range(CUT // 128):
                    run, row = 2 * step + block // 2, 320 + 128 * (block % 2)
                    for quarter in range(4):
                        parts[layer, quarter % 2, quarter // 2, run // 4, run // 2 % 2, run % 2, row : row + 128, :] = result[
                            128 * quarter : 128 * quarter + 128, 128 * block : 128 * block + 128
                        ].astype(BF16)
        if layer == 0:
            pl.semaphore_wait(core_free.at[0 if first < 320 else 1], 1)
        core_copy(part).start()

    def heads_grads(layer):
        for chunk in range(2):
            hidden_done(layer, chunk)
        blocks = [(run // TEAM, run % TEAM) for run in range(RUNS)]
        keys_values = jnp.concatenate(
            [
                jnp.concatenate([pack_out[chunk, other, head, 0:HALF, :] for chunk, other in blocks], axis=0)
                for head in range(OWN)
            ],
            axis=1,
        )
        queries = jnp.concatenate(
            [
                jnp.concatenate([pack_out[chunk, other, head, HALF:, :] for chunk, other in blocks], axis=1)
                for head in range(OWN)
            ],
            axis=0,
        )
        both = nn(hid_all[layer], keys_values)
        q_part = nt(hid_all[layer], queries)
        for number, values in enumerate((q_part, both[:, 0:128], both[:, 128:256])):
            for run in range(RUNS):
                heads_out[layer, run // 2, run % 2, :, 128 * number : 128 * number + 128] = values[
                    DIM * run : DIM * run + DIM, :
                ].astype(BF16)
        heads_x_copy(layer).start()

    def half_rows(which):
        return pl.ds(pl.multiple_of(32 * which, 32), 32)

    def heads_x_copy(layer):
        return remote(
            heads_out.at[layer, :, :, half_rows(1 - side)],
            heads_x.at[layer],
            hx_send.at[layer],
            hx_recv.at[layer],
            x_peer,
        )

    def heads_z_copy(layer, step):
        peer = lax.rem(zz + step, 4)
        return remote(
            heads_out.at[layer, peer, :, half_rows(side)],
            heads_z.at[layer, 4 - step],
            hz_send.at[layer, step],
            hz_recv.at[layer, 4 - step],
            place(core, side, peer, yy),
        )

    def heads_last_copy(layer, number):
        x, c, y = number // 4, number // 2 % 2, number % 2
        return remote(
            heads_sum.at[layer, 1 - yy if y else yy],
            heads_all.at[layer, side, member],
            hf_send.at[layer, number],
            hf_recv.at[layer, number],
            place(1 - core if c else core, 1 - side if x else side, zz, 1 - yy if y else yy),
        )

    def heads_second(layer):
        heads_x_copy(layer).wait()
        heads_out[layer, :, :, half_rows(side), :] += heads_x[layer]
        for step in range(1, 4):
            heads_z_copy(layer, step).start()

    def heads_third(layer):
        for step in range(1, 4):
            heads_z_copy(layer, step).wait()
        total = heads_out[layer, zz, :, half_rows(side), :].astype(F32)
        for slot in range(1, 4):
            total = total + heads_z[layer, slot].astype(F32)
        heads_sum[layer] = total.astype(BF16)
        heads_all[layer, side, member] = heads_sum[layer, yy]
        for number in range(1, 8):
            heads_last_copy(layer, number).start()

    def heads_done(layer):
        for number in range(1, 8):
            heads_last_copy(layer, number).wait()

    def rows_in(part, route):
        first, room, count = SPANS[part, route]
        return pl.ds(first, count), pl.ds(room, count)

    def used(part, route):
        return SHARES[part][route] > 0

    def core_copy(part):
        layer, first, count = PARTS[part]
        rows = pl.ds(first, count)
        return remote(
            parts.at[layer, 1 - core, :, :, :, :, rows],
            core_in.at[:, :, :, :, rows],
            core_send.at[part],
            core_recv.at[part],
            core_peer,
        )

    def x_copy(part, route):
        layer = PARTS[part][0]
        rows, room = rows_in(part, route)
        ends = (x_send.at[part, route], x_recv.at[part, route], x_peer)
        mine = parts.at[layer, core, 1 - side]
        if route == 0:
            return remote(mine.at[:, :, :, rows], xa_in.at[:, :, :, room], *ends)
        if route == 1:
            return remote(mine.at[:, :, yy, rows], xb_in.at[:, :, room], *ends)
        return remote(mine.at[high, odd, :, rows], third_x.at[:, room], *ends)

    def y_copy(part, route):
        layer = PARTS[part][0]
        rows, room = rows_in(part, route)
        ends = (y_send.at[part, route], y_recv.at[part, route], y_peer)
        mine = parts.at[layer, core]
        if route == 0:
            return remote(mine.at[side, :, :, 1 - yy, rows], ya_in.at[:, :, room], *ends)
        if route == 1:
            return remote(mine.at[:, :, :, 1 - yy, rows], yb_in.at[:, :, :, room], *ends)
        return remote(mine.at[side, high, odd, 1 - yy, rows], third_y.at[room], *ends)

    def near_copy(part, route):
        layer = PARTS[part][0]
        rows, room = rows_in(part, route)
        ends = (z_send.at[part, route, 0], z_recv.at[part, route, 0], near_peer)
        mine = parts.at[layer, core]
        if route == 2:
            return remote(mine.at[:, :, 1 - odd, :, rows], third_near.at[:, :, :, room], *ends)
        return remote(mine.at[side, :, 1 - odd, yy, rows], near_in.at[layer, :, rows], *ends)

    def far_copy(part, route):
        layer = PARTS[part][0]
        rows, room = rows_in(part, route)
        ends = (z_send.at[part, route, 1], z_recv.at[part, route, 1], far_peer)
        mine = parts.at[layer, core]
        if route == 2:
            return remote(mine.at[:, 1 - high, odd, :, rows], third_far.at[:, :, room], *ends)
        return remote(mine.at[side, 1 - high, odd, yy, rows], far_in.at[layer, rows], *ends)

    def final_copy(part, which):
        layer, first, count = PARTS[part]
        block = final.at[layer, far_side if which == 2 else grp, pl.ds(first, count)]
        return remote(
            block,
            block,
            fin_send.at[part, which],
            fin_recv.at[part, which],
            x_peer if which == 0 else core_peer,
        )

    def core_done(part):
        layer, first, count = PARTS[part]
        rows = pl.ds(first, count)
        core_copy(part).wait()
        for across in (1 - side, side):
            parts[layer, core, across, :, :, :, rows, :] += core_in[across, :, :, :, rows, :]
            if used(part, 0) and across is not side:
                x_copy(part, 0).start()
        if used(part, 1):
            y_copy(part, 1).start()
        if used(part, 2):
            near_copy(part, 2).start()
        if layer == 1:
            freed = 0 if first < 320 else 1
            followers = [1 for other in PARTS if other[0] == 0 and (other[1] >= 320) == (freed == 1)]
            credit(core_free.at[freed], core_peer, len(followers))

    def first_x(part):
        layer = PARTS[part][0]
        rows, room = rows_in(part, 0)
        x_copy(part, 0).wait()
        for y in (1 - yy, yy):
            parts[layer, core, side, :, :, y, rows, :] += xa_in[:, :, y, room, :]
            if y is not yy:
                y_copy(part, 0).start()

    def first_y(part):
        layer = PARTS[part][0]
        rows, room = rows_in(part, 1)
        y_copy(part, 1).wait()
        for across in (1 - side, side):
            parts[layer, core, across, :, :, yy, rows, :] += yb_in[across, :, :, room, :]
            if across is not side:
                x_copy(part, 1).start()

    def far_z(part):
        layer = PARTS[part][0]
        rows, room = rows_in(part, 2)
        near_copy(part, 2).wait()
        for half in (1 - high, high):
            parts[layer, core, :, half, odd, :, rows, :] += third_near[:, half, :, room, :]
            if half is not high:
                far_copy(part, 2).start()

    def first_z(part):
        layer = PARTS[part][0]
        rows, room = rows_in(part, 2)
        far_copy(part, 2).wait()
        for across in (1 - side, side):
            parts[layer, core, across, high, odd, :, rows, :] += third_far[across, :, room, :]
            if across is not side:
                x_copy(part, 2).start()

    def second_x(part):
        layer = PARTS[part][0]
        rows, room = rows_in(part, 0)
        y_copy(part, 0).wait()
        for z in (1 - odd, odd):
            parts[layer, core, side, :, z, yy, rows, :] += ya_in[:, z, room, :]
            if z is not odd:
                near_copy(part, 0).start()

    def second_y(part):
        layer = PARTS[part][0]
        rows, room = rows_in(part, 1)
        x_copy(part, 1).wait()
        for z in (1 - odd, odd):
            parts[layer, core, side, :, z, yy, rows, :] += xb_in[:, z, room, :]
            if z is not odd:
                near_copy(part, 1).start()

    def second_z(part):
        layer = PARTS[part][0]
        rows, room = rows_in(part, 2)
        x_copy(part, 2).wait()
        for y in (1 - yy, yy):
            parts[layer, core, side, high, odd, y, rows, :] += third_x[y, room, :]
            if y is not yy:
                y_copy(part, 2).start()

    def far_of(part, route):
        layer = PARTS[part][0]
        rows, room = rows_in(part, route)
        near_copy(part, route).wait()
        for half in (1 - high, high):
            parts[layer, core, side, half, odd, yy, rows, :] += near_in[layer, half, rows, :]
            if half is not high:
                far_copy(part, route).start()

    def far_x(part):
        far_of(part, 0)

    def far_y(part):
        far_of(part, 1)

    def third_done(part):
        layer = PARTS[part][0]
        for route in range(3):
            if not used(part, route):
                continue
            rows, room = rows_in(part, route)
            if route == 2:
                y_copy(part, 2).wait()
                last = third_y[room, :]
            else:
                far_copy(part, route).wait()
                last = far_in[layer, rows, :]
            final[layer, grp, rows, :] = parts[layer, core, side, high, odd, yy, rows, :] + last
        if PARTS[part][1] >= 320:
            for row in (320, 448):
                final[layer, grp, row : row + 128, :] = final[layer, grp, row : row + 128, :].T
        for which in range(2):
            final_copy(part, which).start()

    def final_pass(part):
        final_copy(part, 0).wait()
        final_copy(part, 2).start()

    def final_done(part):
        for which in range(1, 3):
            final_copy(part, which).wait()

    def small_copy(stage):
        peer = (core_peer, x_peer, y_peer)[stage]
        return remote(
            small_sum.at[stage], small_in.at[stage], small_send.at[stage], small_recv.at[stage], peer
        )

    def small_z_copy(step):
        return remote(
            small_z.at[zz],
            small_z.at[zz],
            small_send.at[2 + step],
            small_recv.at[2 + step],
            place(core, side, lax.rem(zz + step, 4), yy),
        )

    def small_start():
        small_sum[0] = small[...]
        small_copy(0).start()

    def small_next(stage):
        small_copy(stage).wait()
        total = small_sum[stage] + small_in[stage]
        if stage < 2:
            small_sum[stage + 1] = total
            small_copy(stage + 1).start()
        else:
            small_z[zz] = total
            for step in range(1, 4):
                small_z_copy(step).start()

    def small_done():
        for step in range(1, 4):
            small_z_copy(step).wait()
        small_sum[0] = (small_z[0] + small_z[1]) + (small_z[2] + small_z[3])
        small_final[:, 0:256] = small_sum[0, :, pl.ds(pl.multiple_of(blk * 256, 256), 256)]
        pair = small_sum[0, :, pl.ds(pl.multiple_of(FF + 128 * zz, 128), 128)]
        small_final[:, 256:384] = jnp.where(yy == 1, pltpu.roll(pair, DIM, 1), pair)
        small_final[:, 384:512] = small_sum[0, :, FF + WIDTH :]

    def halves(*phases, first=0):
        def both(step, carry):
            for phase in phases:
                phase(lax.rem(step + first, 2))
            return carry

        lax.fori_loop(0, 2, both, 0)

    def begin(half):
        move_arrived(0, half, tok_in)
        hidden[rows_of(half), :] = tok_in[half].astype(F32)

    def finish(half):
        back_out[0, half] = hidden[rows_of(half), :].astype(BF16)
        to_owner(3, half, back_out.at[0, half], out_in)

    def turn_round(layer, half):
        move_arrived(2, half, cot_in)
        rows = rows_of(half)
        grad[rows, :] = cot_in[half].astype(F32)
        dz[rows, :] = (alphas[layer, 1] * grad[rows, :]).astype(BF16)

    def hand_back(half):
        back_out[1, half] = grad[rows_of(half), :].astype(BF16)
        to_owner(4, half, back_out.at[1, half], grad_in)

    barrier = pltpu.get_barrier_semaphore()
    for step in range(1, 4):
        credit(barrier, place(core, side, lax.rem(zz + step, 4), yy))
    for step in range(4):
        credit(barrier, place(1 - core, side, lax.rem(zz + step, 4), yy))
    for peer in (
        x_peer,
        y_peer,
        place(1 - core, side, zz, 1 - yy),
        place(1 - core, 1 - side, zz, yy),
        place(core, 1 - side, zz, 1 - yy),
        place(1 - core, 1 - side, zz, 1 - yy),
    ):
        credit(barrier, peer)

    weight_copies = {}
    for layer in range(LAYERS):
        for number, (source, target) in enumerate(
            ((qkv_hbm, wqkv), (out_hbm, wout), (up_hbm, wup), (down_hbm, wdown))
        ):
            weight_copies[layer, number] = pltpu.make_async_copy(
                source.at[layer], target.at[layer], w_sem.at[layer, number]
            )
    bias_copies = [
        pltpu.make_async_copy(up_bias_hbm, up_bias, w_sem.at[2, 0]),
        pltpu.make_async_copy(down_bias_hbm, down_bias, w_sem.at[2, 1]),
    ]
    weight_copies[0, 0].start()
    pl.semaphore_wait(barrier, 13)
    upper = lax.div(zz, 2)
    for half in (1 - upper, upper):
        to_team(0, half, half_of(tokens, half), tok_in)
    for layer, number in ((1, 0), (0, 1), (0, 2), (0, 3), (1, 1), (1, 2), (1, 3)):
        weight_copies[layer, number].start(priority=1)
    for copy in bias_copies:
        copy.start(priority=1)
    end_second = lax.div(seq_len[0, 0] + seq_len[0, 1], RUNS)
    flag_out[...] = jnp.full((8, 128), end_second.astype(F32), F32)
    for half in (1 - upper, upper):
        to_team(1, half, flag_out, flag_in)
    for layer in range(LAYERS):
        for head in range(OWN):
            rq[layer, head, DIM:, :] = jnp.zeros((DIM, HALF * RUNS), BF16)
    for head in range(OWN):
        ro[head, 0:DIM, :] = jnp.zeros((DIM, HALF * RUNS), BF16)
    for layer in range(LAYERS):
        weight_copies[layer, 0].wait()
        pairs = [
            beside(
                wqkv[layer, :, WIDTH + 128 * pair : WIDTH + 128 * pair + 128].astype(F32),
                wqkv[layer, :, 2 * WIDTH + 128 * pair : 2 * WIDTH + 128 * pair + 128].astype(F32),
            )
            for pair in range(TEAM)
        ]
        for head in range(RUNS):
            at = WIDTH + 128 * head
            wqkv[layer, :, at : at + 128] = pairs[head // 2][head % 2].astype(BF16)
    halves(begin, functools.partial(project, 0), first=upper)
    for half in (1 - upper, upper):
        to_team(2, half, half_of(cotangent, half), cot_in)

    move_arrived(1, 0, flag_in)
    move_arrived(1, 1, flag_in)
    border = jnp.concatenate([flag_in[0, 0:1, :]] * 2, axis=1) - (HALF * lax.div(zz, 2)).astype(F32)
    key_row = lax.broadcasted_iota(jnp.int32, (TILE, TILE), 0)
    query_col = lax.broadcasted_iota(jnp.int32, (TILE, TILE), 1)
    later = key_row > query_col
    key_sub = lax.rem(key_row, HALF).astype(F32) >= border
    query_sub = lax.rem(query_col, HALF).astype(F32) >= border
    apart = jnp.logical_xor(key_sub, query_sub)
    for tile in range(TILES - 1):
        bias[TILE * tile : TILE * tile + TILE, :] = jnp.where(apart, NEGATIVE, 0.0)
    bias[TILE * (TILES - 1) :, :] = jnp.where(jnp.logical_or(later, apart), NEGATIVE, 0.0)

    for copy in (*bias_copies, *(weight_copies[0, number] for number in range(1, 4))):
        copy.wait()
    attend(0, 0)
    attend(0, 1)
    hidden_start(0, 0)
    halves(functools.partial(feed, 0), functools.partial(project, 1))
    for number in range(1, 4):
        weight_copies[1, number].wait()
    attend(1, 0)
    attend(1, 1)
    hidden_pass(0, 0)
    hidden_start(1, 0)
    halves(functools.partial(feed, 1), finish)
    hidden_start(0, 1)
    hidden_start(1, 1)
    hidden_pass(1, 0)

    halves(functools.partial(turn_round, 1))
    make(1)
    feed_back(1)
    hidden_pass(0, 1)
    hidden_pass(1, 1)
    core_done(1)
    make(0)
    attend_back(1, 1)
    far_z(1)
    core_done(0)
    attend_back(1, 0)
    first_x(1)
    project_back(1, 1)
    heads_grads(1)
    first_z(1)
    project_back(1, 0)
    far_z(0)
    feed_back(0)
    small_start()
    second_x(1)
    make(2)
    first_x(0)
    heads_second(1)
    first_z(0)
    attend_back(0, 1)
    small_next(0)
    core_done(2)
    second_x(0)
    make(3)
    core_done(3)
    attend_back(0, 0)
    small_next(1)
    far_x(1)
    first_y(2)
    first_x(2)
    far_z(2)
    heads_grads(0)
    small_next(2)
    far_x(0)
    project_back(0, 1)
    hand_back(1)
    second_z(1)
    far_z(3)
    first_x(3)
    second_y(2)
    second_z(0)
    first_z(2)
    first_y(3)
    heads_second(0)
    small_done()
    heads_third(1)
    second_x(2)
    first_z(3)
    third_done(1)
    second_y(3)
    far_y(2)
    second_z(2)
    second_x(3)
    heads_third(0)
    third_done(0)
    far_x(2)
    final_pass(1)
    second_z(3)
    far_y(3)
    far_x(3)
    third_done(2)
    heads_done(1)
    project_back(0, 0)
    hand_back(0)
    final_pass(0)
    third_done(3)
    final_pass(2)
    final_pass(3)
    final_done(1)
    final_done(3)
    heads_done(0)
    final_done(0)
    final_done(2)
    for half in range(2):
        move_arrived(3, half, out_in)
        move_arrived(4, half, grad_in)

    for half in range(2):
        left(2, 0, half, head_out)
        left(3, 0, half, pack_out)
        to_team_left(0, half, half_of(tokens, half))
        to_team_left(1, half, flag_out)
        to_team_left(2, half, half_of(cotangent, half))
        to_owner_left(3, half, back_out.at[0, half])
        to_owner_left(4, half, back_out.at[1, half])


def results_kernel(
    final, heads, out_block, grad_block, small,
    output, input_grad, qkv_grad, out_grad, up_grad, up_bias_grad, down_grad, down_bias_grad, alpha_grad,
    out_flat, grad_wide, qkv_wide, out_wide, up_wide, down_wide, out_sem,
):
    ends = []

    def write(source, target):
        ends.append(pltpu.make_async_copy(source, target, out_sem.at[len(ends)]))
        ends[-1].start()

    up_bias_grad[...] = small[:, 0:256]
    down_bias_grad[...] = small[:, 256 : 256 + DIM]
    alpha_grad[...] = small[:, 384:386]
    for layer in range(LAYERS):
        for quarter in range(4):

            def block(first, count):
                return final[layer, quarter, first : first + count, :].astype(F32)

            def columns(step):
                return slice(WIDTH * step + 128 * quarter, WIDTH * step + 128 * quarter + 128)

            for step in range(4):
                up_wide[layer, :, columns(step)] = block(DIM * step, DIM)
            out_wide[layer, :, columns(0)] = block(256, DIM)
            down_wide[layer, :, columns(0)] = block(320, 256)
        write(up_wide.at[layer], up_grad.at[layer])
        write(out_wide.at[layer], out_grad.at[layer])
        write(down_wide.at[layer], down_grad.at[layer])
    for half in range(2):
        rows = slice(HALF * half, HALF * half + HALF)
        grad_wide[rows, :] = grad_block[half].astype(F32)
        out_flat[rows, :] = out_block[half]
    write(grad_wide, input_grad)
    write(out_flat, output)
    for layer in range(LAYERS):
        for side in range(2):
            for member in range(TEAM):
                block = heads[layer, side, member].astype(F32)
                columns = (block[:, 0:128], *beside(block[:, 128:256], block[:, 256:384]))
                for step in range(3):
                    at = WIDTH * step + 128 * member
                    qkv_wide[layer, 32 * side : 32 * side + 32, at : at + 128] = columns[step]
        write(qkv_wide.at[layer], qkv_grad.at[layer])
    for end in ends:
        end.wait()


def fast_body(
    tokens, seq_len, qkv_weight, out_weight, up_weight, up_bias, down_weight, down_bias, alphas, cotangent
):
    whole = pl.BlockSpec(memory_space=pltpu.VMEM)
    scalar = pl.BlockSpec(memory_space=pltpu.SMEM)
    far = pl.BlockSpec(memory_space=pl.ANY)
    shape = jax.ShapeDtypeStruct
    rows = HALF * RUNS

    def vmem(*dims):
        return pltpu.VMEM(dims, BF16)

    def wide(*dims):
        return pltpu.VMEM(dims, F32)

    dma = pltpu.SemaphoreType.DMA
    final, heads, out_block, grad_block, small = pl.pallas_call(
        layers_kernel,
        out_shape=(
            vmem(LAYERS, 4, CHUNK, 128),
            vmem(LAYERS, 2, TEAM, DIM // 2, 3 * 128),
            vmem(2, HALF, WIDTH),
            vmem(2, HALF, WIDTH),
            wide(LAYERS, WIDTH),
        ),
        in_specs=[far, scalar, scalar, far, far, far, far, far, far, far],
        out_specs=(whole,) * 5,
        scratch_shapes=[
            vmem(LAYERS, WIDTH, 3 * WIDTH),
            vmem(LAYERS, WIDTH, WIDTH),
            vmem(LAYERS, WIDTH, FF),
            vmem(LAYERS, FF, WIDTH),
            wide(LAYERS, FF),
            wide(LAYERS, WIDTH),
            vmem(2, HALF, WIDTH),
            vmem(2, HALF, WIDTH),
            wide(8, 128),
            wide(2, 8, 128),
            vmem(2, 2, HALF, WIDTH),
            wide(2 * HALF, WIDTH),
            wide(2 * HALF, WIDTH),
            vmem(LAYERS, WIDTH, rows),
            vmem(LAYERS, WIDTH, 2 * HALF),
            vmem(LAYERS, 2 * HALF, WIDTH),
            vmem(LAYERS, 2 * HALF, FF),
            wide(LAYERS, 2 * HALF, WIDTH),
            wide(LAYERS, 2 * HALF, FF),
            wide(LAYERS, 2 * HALF, WIDTH),
            vmem(2 * HALF, WIDTH),
            vmem(2 * HALF, FF),
            vmem(2 * HALF, WIDTH),
            vmem(HALF, 3 * WIDTH),
            vmem(2, TEAM, OWN, PACK, 128),
            vmem(2, TEAM, OWN, DIM, 128),
            vmem(2, TEAM, OWN, PACK, 128),
            vmem(2, TEAM, OWN, DIM, 128),
            vmem(2, TEAM, OWN, DIM, 128),
            vmem(LAYERS, OWN, rows, 128),
            vmem(LAYERS, OWN, 128, rows),
            vmem(LAYERS, OWN, 128, rows),
            vmem(OWN, 128, rows),
            wide(LAYERS, OWN, DIM, rows),
            wide(LAYERS, OWN, 1, rows),
            wide(OWN, rows, 128),
            wide(OWN, DIM, rows),
            wide(rows, TILE),
            vmem(LAYERS, 2, 2, 2, 2, 2, CHUNK, 128),
            vmem(2, 2, 2, 2, CHUNK, 128),
            vmem(2, 2, 2, TOTALS[0], 128),
            vmem(2, 2, TOTALS[1], 128),
            vmem(2, 2, TOTALS[0], 128),
            vmem(2, 2, 2, TOTALS[1], 128),
            vmem(LAYERS, 2, CHUNK, 128),
            vmem(LAYERS, CHUNK, 128),
            vmem(2, 2, 2, TOTALS[2], 128),
            vmem(2, 2, TOTALS[2], 128),
            vmem(2, TOTALS[2], 128),
            vmem(TOTALS[2], 128),
            vmem(LAYERS, 4, 2, DIM, 3 * 128),
            vmem(LAYERS, 4, 2, DIM // 2, 3 * 128),
            vmem(LAYERS, 4, 2, DIM // 2, 3 * 128),
            vmem(LAYERS, 2, DIM // 2, 3 * 128),
            wide(LAYERS, SMALL),
            wide(3, LAYERS, SMALL),
            wide(4, LAYERS, SMALL),
            wide(3, LAYERS, SMALL),
            dma((LAYERS + 1, 4)),
            dma((5, 2)),
            dma((5, 2)),
            dma((4, LAYERS, 2, OWN)),
            dma((4, LAYERS, 2, OWN)),
            dma((len(PARTS),)),
            dma((len(PARTS),)),
            dma((len(PARTS), 3)),
            dma((len(PARTS), 3)),
            dma((len(PARTS), 3)),
            dma((len(PARTS), 3)),
            dma((len(PARTS), 3, 2)),
            dma((len(PARTS), 3, 2)),
            dma((len(PARTS), 3)),
            dma((len(PARTS), 3)),
            dma((LAYERS, 2, 3)),
            dma((LAYERS, 2, 3)),
            dma((LAYERS,)),
            dma((LAYERS,)),
            dma((LAYERS, 4)),
            dma((LAYERS, 4)),
            dma((LAYERS, 8)),
            dma((LAYERS, 8)),
            dma((6,)),
            dma((6,)),
            pltpu.SemaphoreType.REGULAR((2,)),
        ],
        compiler_params=pltpu.CompilerParams(
            collective_id=0, has_side_effects=True, vmem_limit_bytes=61 * 1024 * 1024
        ),
        name="layers",
    )(
        tokens, seq_len, alphas, up_bias, down_bias, cotangent,
        qkv_weight, out_weight, up_weight, down_weight,
    )
    return tuple(
        pl.pallas_call(
            results_kernel,
            out_shape=(
                shape((2 * HALF, WIDTH), BF16),
                shape((2 * HALF, WIDTH), F32),
                shape((LAYERS, DIM, 3 * WIDTH), F32),
                shape((LAYERS, DIM, WIDTH), F32),
                shape((LAYERS, DIM, FF), F32),
                shape((LAYERS, FF // RUNS), F32),
                shape((LAYERS, FF // RUNS, WIDTH), F32),
                shape((LAYERS, DIM), F32),
                shape((LAYERS, 2), F32),
            ),
            in_specs=[whole] * 5,
            out_specs=(far, far, far, far, far, whole, far, whole, whole),
            scratch_shapes=[
                vmem(2 * HALF, WIDTH),
                wide(2 * HALF, WIDTH),
                wide(LAYERS, DIM, 3 * WIDTH),
                wide(LAYERS, DIM, WIDTH),
                wide(LAYERS, DIM, FF),
                wide(LAYERS, FF // RUNS, WIDTH),
                dma((10,)),
            ],
            compiler_params=pltpu.CompilerParams(vmem_limit_bytes=24 * 1024 * 1024),
            name="results",
        )(final, heads, out_block, grad_block, small)
    )


def layout(seq_len, local_count, cycle_size):
    piece_rows = seq_len[0] // cycle_size
    end_rows = jnp.cumsum(piece_rows)
    start_rows = end_rows - piece_rows
    local_rows = jnp.arange(local_count, dtype=jnp.int32)
    segment = jnp.sum((local_rows[:, None] >= end_rows[None, :]).astype(jnp.int32), axis=1)
    picked = segment[:, None] == jnp.arange(seq_len.shape[1], dtype=jnp.int32)[None, :]
    offset = local_rows - jnp.sum(jnp.where(picked, start_rows[None, :], 0), axis=1)
    span_rows = jnp.sum(jnp.where(picked, piece_rows[None, :], 0), axis=1)
    return (segment, offset, span_rows)


def gelu_exact(values):
    return jax.nn.gelu(values, approximate=False)


def key_block(whole, geometry, block_index, head_count):
    query_seg, query_pos, seg_all, pos_all, block_rows, score_scale = geometry
    first_row = block_index * block_rows
    key_piece = lax.dynamic_slice_in_dim(whole, first_row, block_rows, 0)
    key_seg = lax.dynamic_slice_in_dim(seg_all, first_row, block_rows, 0)
    key_pos = lax.dynamic_slice_in_dim(pos_all, first_row, block_rows, 0)
    half_width = key_piece.shape[1] // 2
    keys_part = key_piece[:, :half_width].reshape(block_rows, head_count, -1)
    values_part = key_piece[:, half_width:].reshape(block_rows, head_count, -1)
    return (keys_part, values_part, key_seg, key_pos)


def block_scores(queries, keys_part, key_seg, key_pos, geometry):
    query_seg, query_pos, seg_all, pos_all, block_rows, score_scale = geometry
    scores = (
        jnp.einsum("qhd,khd->hqk", queries, keys_part, preferred_element_type=jnp.float32)
        * score_scale
    )
    allowed = (query_seg[:, None] == key_seg[None, :]) & (key_pos[None, :] <= query_pos[:, None])
    return (scores, allowed[None])


def attend(queries, whole, geometry):
    row_count, head_count, head_dim = queries.shape
    block_count = whole.shape[0] // geometry[4]

    def statistics(running, block_index):
        largest, totals = running
        keys_part, values_part, key_seg, key_pos = key_block(
            whole, geometry, block_index, head_count
        )
        scores, allowed = block_scores(queries, keys_part, key_seg, key_pos, geometry)
        newest = jnp.maximum(largest, jnp.max(jnp.where(allowed, scores, NEGATIVE), axis=2))
        weights = jnp.where(allowed, jnp.exp(scores - newest[:, :, None]), 0.0)
        totals = totals * jnp.exp(largest - newest) + jnp.sum(weights, axis=2)
        return ((newest, totals), None)

    initial = (
        jnp.full((head_count, row_count), NEGATIVE, jnp.float32),
        jnp.zeros((head_count, row_count), jnp.float32),
    )
    (largest, totals), unused = lax.scan(statistics, initial, jnp.arange(block_count))
    log_total = largest + jnp.log(totals)

    def weighted(output_sum, block_index):
        keys_part, values_part, key_seg, key_pos = key_block(
            whole, geometry, block_index, head_count
        )
        scores, allowed = block_scores(queries, keys_part, key_seg, key_pos, geometry)
        probs = jnp.where(allowed, jnp.exp(scores - log_total[:, :, None]), 0.0).astype(
            jnp.bfloat16
        )
        output_sum = output_sum + jnp.einsum(
            "hqk,khd->qhd", probs, values_part, preferred_element_type=jnp.float32
        )
        return (output_sum, None)

    output_sum, unused = lax.scan(
        weighted, jnp.zeros((row_count, head_count, head_dim), jnp.float32), jnp.arange(block_count)
    )
    return (output_sum, log_total)


def attend_back(queries, whole, log_total, delta_sum, grad_heads, geometry):
    row_count, head_count, head_dim = queries.shape
    block_rows = geometry[4]
    score_scale = geometry[5]
    block_count = whole.shape[0] // block_rows

    def gradients(query_grad, block_index):
        keys_part, values_part, key_seg, key_pos = key_block(
            whole, geometry, block_index, head_count
        )
        scores, allowed = block_scores(queries, keys_part, key_seg, key_pos, geometry)
        probs = jnp.where(allowed, jnp.exp(scores - log_total[:, :, None]), 0.0)
        grad_probs = jnp.einsum(
            "qhd,khd->hqk", grad_heads, values_part, preferred_element_type=jnp.float32
        )
        grad_scores = (probs * (grad_probs - delta_sum[:, :, None])).astype(jnp.bfloat16)
        query_grad = (
            query_grad
            + jnp.einsum("hqk,khd->qhd", grad_scores, keys_part, preferred_element_type=jnp.float32)
            * score_scale
        )
        key_grad = (
            jnp.einsum("hqk,qhd->khd", grad_scores, queries, preferred_element_type=jnp.float32)
            * score_scale
        )
        value_grad = jnp.einsum(
            "hqk,qhd->khd",
            probs.astype(jnp.bfloat16),
            grad_heads,
            preferred_element_type=jnp.float32,
        )
        joined = jnp.concatenate(
            [key_grad.reshape(block_rows, -1), value_grad.reshape(block_rows, -1)], axis=1
        )
        return (query_grad, joined)

    query_grad, stacked = lax.scan(
        gradients,
        jnp.zeros((row_count, head_count, head_dim), jnp.float32),
        jnp.arange(block_count),
    )
    return (query_grad, stacked.reshape(whole.shape[0], -1))


def layer_forward(hidden, layer_index, weights, geometry):
    qkv_weight, out_weight, up_weight, up_bias, down_weight, down_bias, alphas = weights
    row_count, model_width = hidden.shape
    projection = qkv_weight[layer_index]
    rounded = hidden.astype(jnp.bfloat16)
    queries = (
        jnp.dot(rounded, projection[:, :model_width], preferred_element_type=jnp.float32)
        .astype(jnp.bfloat16)
        .reshape(row_count, HEADS, -1)
    )
    key_value = jnp.dot(
        rounded, projection[:, model_width:], preferred_element_type=jnp.float32
    ).astype(jnp.bfloat16)
    whole = lax.all_gather(key_value, "blk", axis=0, tiled=True)
    heads_out, log_total = attend(queries, whole, geometry)
    heads_rounded = heads_out.reshape(row_count, model_width).astype(jnp.bfloat16)
    branch = jnp.dot(heads_rounded, out_weight[layer_index], preferred_element_type=jnp.float32)
    alpha_pair = alphas[layer_index]
    middle = hidden + alpha_pair[0] * branch
    entered = middle.astype(jnp.bfloat16)
    gate_pre = (
        jnp.dot(entered, up_weight[layer_index], preferred_element_type=jnp.float32)
        + up_bias[layer_index]
    )
    activated = gelu_exact(gate_pre).astype(jnp.bfloat16)
    second = (
        jnp.dot(activated, down_weight[layer_index], preferred_element_type=jnp.float32)
        + down_bias[layer_index]
    )
    result = middle + alpha_pair[1] * second
    saved = (
        rounded,
        queries,
        key_value,
        whole,
        heads_out,
        heads_rounded,
        log_total,
        branch,
        entered,
        gate_pre,
        activated,
        second,
    )
    return (result, saved)


def layer_backward(grad_hidden, saved, layer_index, weights, geometry):
    qkv_weight, out_weight, up_weight, up_bias, down_weight, down_bias, alphas = weights
    (
        rounded,
        queries,
        key_value,
        saved_whole,
        heads_out,
        heads_rounded,
        log_total,
        branch,
        entered,
        gate_pre,
        activated,
        second,
    ) = saved
    row_count = grad_hidden.shape[0]
    alpha_pair = alphas[layer_index]
    grad_second = (alpha_pair[1] * grad_hidden).astype(jnp.bfloat16)
    alpha_second = jnp.sum(grad_hidden * second)
    bias_down = jnp.sum(grad_second.astype(jnp.float32), axis=0)
    grad_down = jnp.einsum("tf,td->fd", activated, grad_second, preferred_element_type=jnp.float32)
    grad_act = jnp.einsum(
        "td,fd->tf", grad_second, down_weight[layer_index], preferred_element_type=jnp.float32
    )
    unused, gelu_pull = jax.vjp(gelu_exact, gate_pre)
    grad_gate = gelu_pull(grad_act)[0].astype(jnp.bfloat16)
    bias_up = jnp.sum(grad_gate.astype(jnp.float32), axis=0)
    grad_up = jnp.einsum("td,tf->df", entered, grad_gate, preferred_element_type=jnp.float32)
    grad_middle = grad_hidden + jnp.einsum(
        "tf,df->td", grad_gate, up_weight[layer_index], preferred_element_type=jnp.float32
    )
    grad_branch = (alpha_pair[0] * grad_middle).astype(jnp.bfloat16)
    alpha_first = jnp.sum(grad_middle * branch)
    grad_proj_out = jnp.einsum(
        "te,td->ed", heads_rounded, grad_branch, preferred_element_type=jnp.float32
    )
    grad_heads = (
        jnp.einsum(
            "td,ed->te", grad_branch, out_weight[layer_index], preferred_element_type=jnp.float32
        )
        .astype(jnp.bfloat16)
        .reshape(queries.shape)
    )
    delta_sum = jnp.sum(grad_heads.astype(jnp.float32) * heads_out, axis=2).T
    whole = lax.all_gather(key_value, "blk", axis=0, tiled=True)
    query_grad, key_terms = attend_back(queries, whole, log_total, delta_sum, grad_heads, geometry)
    key_grads = lax.psum_scatter(
        key_terms.astype(jnp.bfloat16), "blk", scatter_dimension=0, tiled=True
    )
    grad_proj = jnp.concatenate(
        [query_grad.reshape(row_count, -1).astype(jnp.bfloat16), key_grads], axis=1
    )
    grad_qkv = jnp.einsum("td,te->de", rounded, grad_proj, preferred_element_type=jnp.float32)
    grad_input = grad_middle + jnp.einsum(
        "te,de->td", grad_proj, qkv_weight[layer_index], preferred_element_type=jnp.float32
    )
    layer_grads = (
        grad_qkv,
        grad_proj_out,
        grad_up,
        bias_up,
        grad_down,
        bias_down,
        jnp.stack([alpha_first, alpha_second]),
    )
    return (grad_input, layer_grads)


def reduce_all(layer_results, cycle_size):
    stacked = [
        jnp.stack([layer_entry[member] for layer_entry in layer_results], axis=0)
        for member in range(6)
    ]
    alpha_tiles = jnp.stack(
        [jnp.tile(layer_entry[6], cycle_size) for layer_entry in layer_results], axis=0
    )
    shares = (
        lax.psum_scatter(
            stacked[0].astype(jnp.bfloat16), "blk", scatter_dimension=1, tiled=True
        ).astype(jnp.float32),
        lax.psum_scatter(
            stacked[1].astype(jnp.bfloat16), "blk", scatter_dimension=1, tiled=True
        ).astype(jnp.float32),
        lax.psum_scatter(
            stacked[2].astype(jnp.bfloat16), "blk", scatter_dimension=1, tiled=True
        ).astype(jnp.float32),
        lax.psum_scatter(
            stacked[3].astype(jnp.bfloat16), "blk", scatter_dimension=1, tiled=True
        ).astype(jnp.float32),
        lax.psum_scatter(
            stacked[4].astype(jnp.bfloat16), "blk", scatter_dimension=1, tiled=True
        ).astype(jnp.float32),
        lax.psum_scatter(
            stacked[5].astype(jnp.bfloat16), "blk", scatter_dimension=1, tiled=True
        ).astype(jnp.float32),
        lax.psum_scatter(
            alpha_tiles.astype(jnp.bfloat16), "blk", scatter_dimension=1, tiled=True
        ).astype(jnp.float32),
    )
    return (
        lax.psum(shares[0].astype(jnp.bfloat16), "grp").astype(jnp.float32),
        lax.psum(shares[1].astype(jnp.bfloat16), "grp").astype(jnp.float32),
        lax.psum(shares[2].astype(jnp.bfloat16), "grp").astype(jnp.float32),
        lax.psum(shares[3].astype(jnp.bfloat16), "grp").astype(jnp.float32),
        lax.psum(shares[4].astype(jnp.bfloat16), "grp").astype(jnp.float32),
        lax.psum(shares[5].astype(jnp.bfloat16), "grp").astype(jnp.float32),
        lax.psum(shares[6].astype(jnp.bfloat16), "grp").astype(jnp.float32),
    )


def body(
    tokens,
    seq_len,
    qkv_weight,
    out_weight,
    up_weight,
    up_bias,
    down_weight,
    down_bias,
    alphas,
    cotangent,
):
    row_count, model_width = tokens.shape
    cycle_size = lax.axis_size("blk")
    cycle_place = lax.axis_index("blk")
    head_dim = model_width // HEADS
    total_rows = cycle_size * row_count
    block_rows = min(max(row_count, 512), total_rows)
    segment, offset, span_rows = layout(seq_len, row_count, cycle_size)
    query_pos = cycle_place * span_rows + offset
    seg_all = jnp.tile(segment, cycle_size)
    pos_all = jnp.repeat(jnp.arange(cycle_size, dtype=jnp.int32), row_count) * jnp.tile(
        span_rows, cycle_size
    ) + jnp.tile(offset, cycle_size)
    geometry = (segment, query_pos, seg_all, pos_all, block_rows, head_dim ** (-0.5))
    weights = (qkv_weight, out_weight, up_weight, up_bias, down_weight, down_bias, alphas)
    hidden = tokens.astype(jnp.float32)
    saved_layers = []
    for layer_index in range(LAYERS):
        hidden, saved = layer_forward(hidden, layer_index, weights, geometry)
        saved_layers.append(saved)
    output = hidden.astype(jnp.bfloat16)
    grad_hidden = cotangent.astype(jnp.float32)
    layer_results = []
    for layer_index in reversed(range(LAYERS)):
        grad_hidden, layer_grads = layer_backward(
            grad_hidden, saved_layers[layer_index], layer_index, weights, geometry
        )
        layer_results.insert(0, layer_grads)
    finals = reduce_all(layer_results, cycle_size)
    return (
        output,
        grad_hidden,
        finals[0],
        finals[1],
        finals[2],
        finals[3],
        finals[4],
        finals[5],
        finals[6],
    )


def solution(mesh):
    placed = (
        P(("grp", "blk"), None),
        P("grp", None),
        P(),
        P(),
        P(),
        P(),
        P(),
        P(),
        P(),
        P(("grp", "blk"), None),
    )
    sizes = (mesh.shape["grp"], mesh.shape["blk"])
    return jax.shard_map(
        fast_body if sizes == (4, RUNS) else body,
        mesh=mesh,
        in_specs=placed,
        out_specs=(
            P(("grp", "blk"), None),
            P(("grp", "blk"), None),
            P(None, "blk", None),
            P(None, "blk", None),
            P(None, "blk", None),
            P(None, "blk"),
            P(None, "blk", None),
            P(None, "blk"),
            P(),
        ),
        check_vma=False,
    )
```

```python
import functools

import jax
import jax.numpy as jnp
from jax import lax
from jax.experimental import pallas as pl
from jax.experimental.pallas import tpu as pltpu
from jax.sharding import PartitionSpec as P

HEADS = 8
LAYERS = 2
NEGATIVE = -1e30
MESH = pl.DeviceIdType.MESH
F32 = jnp.float32
BF16 = jnp.bfloat16

HALF = 128
RUNS = 8
TEAM = 4
OWN = RUNS // TEAM
DIM = 64
WIDTH = 512
FF = 2048
CUT = 512
TILE = 256
TILES = HALF * RUNS // TILE
PACK = HALF + DIM
CHUNK = 576
SMALL = FF + WIDTH + 128
PARTS = ((1, 0, 320), (1, 320, 256), (0, 0, 320), (0, 320, 256))
SHARES = ((192, 16, 112), (160, 16, 80), (160, 112, 48), (128, 96, 32))


def spans():
    places, totals = {}, [0, 0, 0]
    for part, counts in enumerate(SHARES):
        first = PARTS[part][1]
        for route, count in enumerate(counts):
            places[part, route] = (first, totals[route], count)
            first += count
            totals[route] += count
    return places, totals


SPANS, TOTALS = spans()

SLOPE_AT = 0.28
TAIL = (
    0.11652077851573843,
    0.06749675579450809,
    0.2689101589486142,
    -0.23699347299932225,
    0.3898740127620002,
    -0.10580824228351815,
)


def nn(a, b):
    return lax.dot_general(a, b, (((1,), (0,)), ((), ())), preferred_element_type=F32)


def nt(a, b):
    return lax.dot_general(a, b, (((1,), (1,)), ((), ())), preferred_element_type=F32)


def beside(first, other):
    low = lax.broadcasted_iota(jnp.int32, first.shape, 1) < DIM
    return (
        jnp.where(low, first, pltpu.roll(other, DIM, 1)),
        jnp.where(low, pltpu.roll(first, DIM, 1), other),
    )


def layers_kernel(
    tokens, seq_len, alphas, up_bias_hbm, down_bias_hbm, cotangent, qkv_hbm, out_hbm, up_hbm, down_hbm,
    final, heads_all, out_in, grad_in, small_final,
    wqkv, wout, wup, wdown, up_bias, down_bias,
    tok_in, cot_in, flag_out, flag_in, back_out,
    hidden, grad, hid_all, attn_t, entered, act, branch, slope, second,
    dz, du, da, dqkv,
    pack_out, head_out, pack_in, o_in, do_in,
    kv, kv_t, rq, ro, o_t, lse, acc, dq_t, bias,
    parts, core_in, xa_in, xb_in, ya_in, yb_in, z_in, third_z, third_x, third_y,
    heads_out, heads_x, heads_z, heads_sum, small, small_in, small_z, small_sum,
    w_sem, move_send, move_recv, a2a_send, a2a_recv, core_send, core_recv, x_send, x_recv, y_send, y_recv,
    z_send, z_recv, fin_send, fin_recv, hid_send, hid_recv, hx_send, hx_recv, hz_send, hz_recv, hf_send, hf_recv,
    small_send, small_recv, core_free,
):
    grp = lax.axis_index("grp")
    blk = lax.axis_index("blk")
    core = lax.rem(grp, 2)
    side = lax.div(grp, 2)
    yy = lax.rem(blk, 2)
    zz = lax.div(blk, 2)
    member = 2 * core + yy
    far_side = 2 * (1 - side) + core

    def place(c, x, z, y):
        return (2 * x + c, 2 * z + y)

    core_peer = place(1 - core, side, zz, yy)
    x_peer = place(core, 1 - side, zz, yy)
    y_peer = place(core, side, zz, 1 - yy)

    def remote(source, target, send, recv, peer):
        return pltpu.make_async_remote_copy(
            src_ref=source,
            dst_ref=target,
            send_sem=send,
            recv_sem=recv,
            device_id=peer,
            device_id_type=MESH,
        )

    def credit(semaphore, peer, count=1):
        pl.semaphore_signal(semaphore, inc=count, device_id=peer, device_id_type=MESH)

    def moved(kind, slot, source, target, at, core_at, z_at):
        here = jnp.logical_and(core_at == core, z_at == zz)

        @pl.when(here)
        def _():
            pltpu.make_async_copy(source, target.at[at], move_recv.at[kind, at]).start()

        @pl.when(jnp.logical_not(here))
        def _():
            pltpu.make_async_remote_copy(
                src_ref=source,
                dst_ref=target.at[at],
                send_sem=move_send.at[kind, slot],
                recv_sem=move_recv.at[kind, at],
                device_id=place(core_at, side, z_at, yy),
                device_id_type=MESH,
            ).start()

    def move_left(kind, slot, source, core_at, z_at):
        here = jnp.logical_and(core_at == core, z_at == zz)

        @pl.when(jnp.logical_not(here))
        def _():
            pltpu.make_async_copy(source, source, move_send.at[kind, slot]).wait()

    def move_arrived(kind, at, target):
        pltpu.make_async_copy(target.at[at], target.at[at], move_recv.at[kind, at]).wait()

    def to_team(kind, half, source, target):
        moved(kind, half, source, target, lax.div(zz, 2), lax.rem(zz, 2), 2 * half + core)

    def to_team_left(kind, half, source):
        move_left(kind, half, source, lax.rem(zz, 2), 2 * half + core)

    def to_owner(kind, chunk, source, target):
        moved(kind, chunk, source, target, lax.div(zz, 2), lax.rem(zz, 2), core + 2 * chunk)

    def to_owner_left(kind, chunk, source):
        move_left(kind, chunk, source, lax.rem(zz, 2), core + 2 * chunk)

    def half_of(ref, half):
        return ref.at[pl.ds(pl.multiple_of(HALF * half, HALF), HALF)]

    def rows_of(half):
        return pl.ds(pl.multiple_of(half * HALF, HALF), HALF)

    def slot_of(other):
        return lax.rem(other + TEAM - member, TEAM)

    def exchange(kind, layer, half, outgoing, incoming, head=None):
        at = () if head is None else (head,)
        incoming[(half, 0, *at)] = outgoing[(half, member, *at)]
        for step in range(1, TEAM):
            peer = lax.rem(member + step, TEAM)
            remote(
                outgoing.at[(half, peer, *at)],
                incoming.at[(half, TEAM - step, *at)],
                a2a_send.at[kind, layer, half, head or 0],
                a2a_recv.at[kind, layer, half, head or 0],
                place(lax.div(peer, 2), side, zz, lax.rem(peer, 2)),
            ).start()

    def arrived(kind, layer, half, incoming, head=None):
        at = () if head is None else (head,)
        whole = incoming.at[(half, pl.ds(1, TEAM - 1), *at)]
        pltpu.make_async_copy(whole, whole, a2a_recv.at[kind, layer, half, head or 0]).wait()

    def left(kind, layer, half, outgoing):
        for head in range(OWN) if kind in (0, 3) else (None,):
            at = () if head is None else (head,)
            whole = outgoing.at[(half, pl.ds(1, TEAM - 1), *at)]
            pltpu.make_async_copy(whole, whole, a2a_send.at[kind, layer, half, head or 0]).wait()

    def tokens_of(chunk, other):
        return pl.ds(pl.multiple_of(HALF * (TEAM * chunk + other), HALF), HALF)

    def hidden_copy(layer, chunk, which):
        whose = 2 * core + 1 - yy if which == 2 else member
        block = hid_all.at[layer, :, tokens_of(chunk, whose)]
        return remote(
            block,
            block,
            hid_send.at[layer, chunk, which],
            hid_recv.at[layer, chunk, which],
            y_peer if which == 0 else core_peer,
        )

    def hidden_start(layer, chunk):
        for which in range(2):
            hidden_copy(layer, chunk, which).start()

    def hidden_pass(layer, chunk):
        hidden_copy(layer, chunk, 0).wait()
        hidden_copy(layer, chunk, 2).start()

    def hidden_done(layer, chunk):
        for which in range(1, 3):
            hidden_copy(layer, chunk, which).wait()

    def project(layer, half):
        rows = rows_of(half)
        rounded = hidden[rows, :].astype(BF16)
        if layer == 1:
            left(0, 0, half, pack_out)
        queries = (nn(rounded, wqkv[layer, :, 0:WIDTH]) * (DIM ** -0.5)).astype(BF16).T
        for head in range(RUNS):
            pack_out[half, head // 2, head % 2, HALF:, :] = queries[DIM * head : DIM * head + DIM, :]
        for step in range(2):
            at = WIDTH * (step + 1)
            keys_values = nn(rounded, wqkv[layer, :, at : at + WIDTH]).astype(BF16)
            for head in range(4):
                pack_out[half, 2 * step + head // 2, head % 2, 0:HALF, :] = keys_values[
                    :, 128 * head : 128 * head + 128
                ]
        for head in range(OWN):
            exchange(0, layer, half, pack_out, pack_in, head)
        hid_all[layer, :, tokens_of(half, member)] = rounded.T

    def attend(layer, chunk):
        if layer == 1:
            left(1, 0, chunk, head_out)

        def one_head(head, carry):
            arrived(0, layer, chunk, pack_in, head)
            for other in range(TEAM):
                slot = slot_of(other)
                start = HALF * (TEAM * chunk + other)
                span = slice(start, start + HALF)
                block = pack_in[chunk, slot, head, 0:HALF, :]
                kv[layer, head, span, :] = block
                kv_t[layer, head, :, span] = block.T
                rq[layer, head, 0:DIM, span] = pack_in[chunk, slot, head, HALF:, :]

            def scores_of(i):
                count = TILE * (i + 1)
                tile = rq[layer, head, :, TILE * i : TILE * i + TILE]
                return nn(kv[layer, head, 0:count, :], tile) + bias[TILE * TILES - count :, :]

            ahead = [scores_of(i) for i in (2 * chunk, 2 * chunk + 1)]
            for i in (2 * chunk, 2 * chunk + 1):
                columns = slice(TILE * i, TILE * i + TILE)
                count = TILE * (i + 1)
                scores = ahead[i - 2 * chunk]
                largest = jnp.max(scores, axis=0, keepdims=True)
                weight = jnp.exp(scores - largest)
                total = jnp.sum(weight, axis=0, keepdims=True)
                summed = nn(kv_t[layer, head, DIM:, 0:count], weight.astype(BF16))
                summed = summed / total
                o_t[layer, head, :, columns] = summed
                lse[layer, head, :, columns] = largest + jnp.log(total)
                rounded = summed.astype(BF16)
                for part in range(2):
                    head_out[chunk, 2 * (i - 2 * chunk) + part, head] = rounded[
                        :, HALF * part : HALF * part + HALF
                    ]
            return carry

        for head in range(OWN):
            one_head(head, 0)
        exchange(1, layer, chunk, head_out, o_in)

    def feed(layer, half):
        rows = rows_of(half)
        arrived(1, layer, half, o_in)
        for head in range(RUNS):
            attn_t[layer, DIM * head : DIM * head + DIM, rows] = o_in[half, slot_of(head // 2), head % 2]
        attn = attn_t[layer, :, rows].T
        grown = nn(attn, wout[layer])
        branch[layer, rows, :] = grown
        middle = hidden[rows, :] + alphas[layer, 0] * grown
        rounded = middle.astype(BF16)
        entered[layer, rows, :] = rounded
        total = jnp.zeros((HALF, WIDTH), F32)

        def gate_of(step):
            cut = slice(CUT * step, CUT * step + CUT)
            return nn(rounded, wup[layer, :, cut]) + up_bias[layer : layer + 1, cut]

        coming = gate_of(0)
        for step in range(FF // CUT):
            cut = slice(CUT * step, CUT * step + CUT)
            gate = coming
            if step + 1 < FF // CUT:
                coming = gate_of(step + 1)
            bell = jnp.exp(gate * gate * -0.5)
            near = pl.reciprocal(1.0 + SLOPE_AT * jnp.abs(gate), approx=True)
            tail = jnp.full_like(gate, TAIL[5])
            for factor in TAIL[4::-1]:
                tail = tail * near + factor
            tail = bell * (tail * near)
            risen = jnp.where(gate > 0.0, 1.0 - tail, tail)
            slope[layer, rows, cut] = risen + gate * bell * 0.3989422804014327
            active = (gate * risen).astype(BF16)
            act[layer, rows, cut] = active
            total = total + nn(active, wdown[layer, cut, :])
        total = total + down_bias[layer : layer + 1, :]
        second[layer, rows, :] = total
        hidden[rows, :] = middle + alphas[layer, 1] * total

    def total_of(values):
        return jnp.sum(jnp.sum(values, axis=0, keepdims=True), axis=1, keepdims=True)

    def feed_back(layer):
        start = grad[...]
        if layer == 0:
            dz[...] = (alphas[layer, 1] * start).astype(BF16)
        scaled = dz[...]
        alpha_second = total_of(start * second[layer])
        small[layer : layer + 1, FF : FF + WIDTH] = jnp.sum(scaled.astype(F32), axis=0, keepdims=True)
        middle = start
        coming = nt(scaled, wdown[layer, 0:CUT, :])
        for step in range(FF // CUT):
            cut = slice(CUT * step, CUT * step + CUT)
            raw = coming
            if step + 1 < FF // CUT:
                coming = nt(scaled, wdown[layer, CUT * (step + 1) : CUT * (step + 2), :])
            gate = (raw * slope[layer, :, cut]).astype(BF16)
            du[:, cut] = gate
            small[layer : layer + 1, cut] = jnp.sum(gate.astype(F32), axis=0, keepdims=True)
            middle = middle + nt(gate, wup[layer, :, cut])
        grad[...] = middle
        mixed = (alphas[layer, 0] * middle).astype(BF16)
        da[...] = mixed
        spread = nt(wout[layer], mixed).astype(BF16)
        for chunk in (1, 0):
            left(*((1, 1) if layer == 1 else (2, 1)), chunk, head_out)
            for head in range(RUNS):
                head_out[chunk, head // 2, head % 2] = spread[
                    DIM * head : DIM * head + DIM, HALF * chunk : HALF * chunk + HALF
                ]
            exchange(2, layer, chunk, head_out, do_in)
        alpha_first = total_of(middle * branch[layer])
        column = lax.broadcasted_iota(jnp.int32, (1, 128), 1)
        small[layer : layer + 1, FF + WIDTH :] = jnp.where(
            column == 0, alpha_first, jnp.where(column == 1, alpha_second, 0.0)
        )

    def attend_back(layer, chunk):
        arrived(2, layer, chunk, do_in)
        left(*((0, 1) if layer == 1 else (3, 1)), chunk, pack_out)

        def one_head(head, carry):
            for other in range(TEAM):
                start = HALF * (TEAM * chunk + other)
                ro[head, DIM:, start : start + HALF] = do_in[chunk, slot_of(other), head]
            for i in (2 * chunk, 2 * chunk + 1):
                columns = slice(TILE * i, TILE * i + TILE)
                query_tile = rq[layer, head, :, columns]
                grad_tile = ro[head, :, columns]
                log_total = lse[layer, head, :, columns]
                delta = jnp.sum(
                    ro[head, DIM:, columns].astype(F32) * o_t[layer, head, :, columns],
                    axis=0,
                    keepdims=True,
                )
                count = TILE * (i + 1)
                keys = kv[layer, head, 0:count, :]
                weight = jnp.exp(nn(keys, query_tile) + bias[TILE * TILES - count :, :] - log_total)
                scored = (weight * (nn(keys, grad_tile) - delta)).astype(BF16)
                term = nt(scored, query_tile) + nt(weight.astype(BF16), grad_tile)
                if chunk == 1 and i == 2:
                    acc[head, 0:count, :] = term
                elif chunk == 1:
                    acc[head, 0 : count - TILE, :] += term[0 : count - TILE, :]
                    acc[head, count - TILE : count, :] = term[count - TILE :, :]
                else:
                    acc[head, 0:count, :] += term
                query_grad = nn(kv_t[layer, head, 0:DIM, 0:count], scored)
                dq_t[head, :, columns] = query_grad * (DIM ** -0.5)
            for other in range(TEAM):
                start = HALF * (TEAM * chunk + other)
                span = slice(start, start + HALF)
                pack_out[chunk, other, head, 0:HALF, :] = acc[head, span, :].astype(BF16)
                pack_out[chunk, other, head, HALF:, :] = dq_t[head, :, span].astype(BF16)
            exchange(3, layer, chunk, pack_out, pack_in, head)
            return carry

        for head in range(OWN):
            one_head(head, 0)

    def project_back(layer, half):
        for head in range(OWN):
            arrived(3, layer, half, pack_in, head)
        turned = jnp.concatenate(
            [pack_in[half, slot_of(head // 2), head % 2, HALF:, :] for head in range(RUNS)], axis=0
        )
        dqkv[:, 0:WIDTH] = turned.T
        for head in range(RUNS):
            at = WIDTH + 128 * head
            dqkv[:, at : at + 128] = pack_in[half, slot_of(head // 2), head % 2, 0:HALF, :]
        rows = rows_of(half)
        grad[rows, :] = grad[rows, :] + nt(dqkv[...], wqkv[layer])

    def scatter_rows(layer, result, first_row):
        for run in range(RUNS):
            for quarter in range(4):
                parts[layer, quarter % 2, quarter // 2, run // 2, run % 2, first_row : first_row + DIM, :] = result[
                    DIM * run : DIM * run + DIM, 128 * quarter : 128 * quarter + 128
                ].astype(BF16)

    def make(part):
        layer, first, count = PARTS[part]
        if first < 256:
            turned = entered[layer].T
        for row in range(first, min(first + count, 256), DIM):
            step = row // DIM
            scatter_rows(layer, nn(turned, du[:, CUT * step : CUT * step + CUT]), row)
        if first <= 256 < first + count:
            scatter_rows(layer, nn(attn_t[layer], da[...]), 256)
        if first >= 320:
            turned = dz[...].T
            for step in range(FF // CUT):
                result = nn(turned, act[layer, :, CUT * step : CUT * step + CUT])
                for block in range(CUT // 128):
                    run, row = 2 * step + block // 2, 320 + 128 * (block % 2)
                    for quarter in range(4):
                        parts[layer, quarter % 2, quarter // 2, run // 2, run % 2, row : row + 128, :] = result[
                            128 * quarter : 128 * quarter + 128, 128 * block : 128 * block + 128
                        ].astype(BF16)
        if layer == 0:
            pl.semaphore_wait(core_free.at[0 if first < 320 else 1], 1)
        core_copy(part).start()

    def heads_grads(layer):
        for chunk in range(2):
            hidden_done(layer, chunk)
        blocks = [(run // TEAM, run % TEAM) for run in range(RUNS)]
        keys_values = jnp.concatenate(
            [
                jnp.concatenate([pack_out[chunk, other, head, 0:HALF, :] for chunk, other in blocks], axis=0)
                for head in range(OWN)
            ],
            axis=1,
        )
        queries = jnp.concatenate(
            [
                jnp.concatenate([pack_out[chunk, other, head, HALF:, :] for chunk, other in blocks], axis=1)
                for head in range(OWN)
            ],
            axis=0,
        )
        both = nn(hid_all[layer], keys_values)
        q_part = nt(hid_all[layer], queries)
        for number, values in enumerate((q_part, both[:, 0:128], both[:, 128:256])):
            for run in range(RUNS):
                heads_out[layer, run // 2, run % 2, :, 128 * number : 128 * number + 128] = values[
                    DIM * run : DIM * run + DIM, :
                ].astype(BF16)
        heads_x_copy(layer).start()

    def half_rows(which):
        return pl.ds(pl.multiple_of(32 * which, 32), 32)

    def heads_x_copy(layer):
        return remote(
            heads_out.at[layer, :, :, half_rows(1 - side)],
            heads_x.at[layer],
            hx_send.at[layer],
            hx_recv.at[layer],
            x_peer,
        )

    def heads_z_copy(layer, step):
        peer = lax.rem(zz + step, 4)
        return remote(
            heads_out.at[layer, peer, :, half_rows(side)],
            heads_z.at[layer, 4 - step],
            hz_send.at[layer, step],
            hz_recv.at[layer, 4 - step],
            place(core, side, peer, yy),
        )

    def heads_last_copy(layer, number):
        x, c, y = number // 4, number // 2 % 2, number % 2
        return remote(
            heads_sum.at[layer, 1 - yy if y else yy],
            heads_all.at[layer, side, member],
            hf_send.at[layer, number],
            hf_recv.at[layer, number],
            place(1 - core if c else core, 1 - side if x else side, zz, 1 - yy if y else yy),
        )

    def heads_second(layer):
        heads_x_copy(layer).wait()
        heads_out[layer, :, :, half_rows(side), :] += heads_x[layer]
        for step in range(1, 4):
            heads_z_copy(layer, step).start()

    def heads_third(layer):
        for step in range(1, 4):
            heads_z_copy(layer, step).wait()
        total = heads_out[layer, zz, :, half_rows(side), :].astype(F32)
        for slot in range(1, 4):
            total = total + heads_z[layer, slot].astype(F32)
        heads_sum[layer] = total.astype(BF16)
        heads_all[layer, side, member] = heads_sum[layer, yy]
        for number in range(1, 8):
            heads_last_copy(layer, number).start()

    def heads_done(layer):
        for number in range(1, 8):
            heads_last_copy(layer, number).wait()

    def rows_in(part, route):
        first, room, count = SPANS[part, route]
        return pl.ds(first, count), pl.ds(room, count)

    def used(part, route):
        return SHARES[part][route] > 0

    def core_copy(part):
        layer, first, count = PARTS[part]
        rows = pl.ds(first, count)
        return remote(
            parts.at[layer, 1 - core, :, :, :, rows],
            core_in.at[:, :, :, rows],
            core_send.at[part],
            core_recv.at[part],
            core_peer,
        )

    def x_copy(part, route):
        layer = PARTS[part][0]
        rows, room = rows_in(part, route)
        ends = (x_send.at[part, route], x_recv.at[part, route], x_peer)
        mine = parts.at[layer, core, 1 - side]
        if route == 0:
            return remote(mine.at[:, :, rows], xa_in.at[:, :, room], *ends)
        if route == 1:
            return remote(mine.at[:, yy, rows], xb_in.at[:, room], *ends)
        return remote(mine.at[zz, :, rows], third_x.at[:, room], *ends)

    def y_copy(part, route):
        layer = PARTS[part][0]
        rows, room = rows_in(part, route)
        ends = (y_send.at[part, route], y_recv.at[part, route], y_peer)
        mine = parts.at[layer, core]
        if route == 0:
            return remote(mine.at[side, :, 1 - yy, rows], ya_in.at[:, room], *ends)
        if route == 1:
            return remote(mine.at[:, :, 1 - yy, rows], yb_in.at[:, :, room], *ends)
        return remote(mine.at[side, zz, 1 - yy, rows], third_y.at[room], *ends)

    def z_copy(part, route, step):
        layer = PARTS[part][0]
        rows, room = rows_in(part, route)
        peer = lax.rem(zz + step, 4)
        ends = (z_send.at[part, route, step], z_recv.at[part, route, 4 - step], place(core, side, peer, yy))
        if route == 2:
            return remote(parts.at[layer, core, :, peer, :, rows], third_z.at[4 - step, :, :, room], *ends)
        return remote(parts.at[layer, core, side, peer, yy, rows], z_in.at[layer, 4 - step, rows], *ends)

    def final_copy(part, which):
        layer, first, count = PARTS[part]
        block = final.at[layer, far_side if which == 2 else grp, pl.ds(first, count)]
        return remote(
            block,
            block,
            fin_send.at[part, which],
            fin_recv.at[part, which],
            x_peer if which == 0 else core_peer,
        )

    def core_done(part):
        layer, first, count = PARTS[part]
        rows = pl.ds(first, count)
        core_copy(part).wait()
        for across in (1 - side, side):
            parts[layer, core, across, :, :, rows, :] += core_in[across, :, :, rows, :]
            if used(part, 0) and across is not side:
                x_copy(part, 0).start()
        if used(part, 1):
            y_copy(part, 1).start()
        if used(part, 2):
            for step in range(1, 4):
                z_copy(part, 2, step).start()
        if layer == 1:
            freed = 0 if first < 320 else 1
            followers = [1 for other in PARTS if other[0] == 0 and (other[1] >= 320) == (freed == 1)]
            credit(core_free.at[freed], core_peer, len(followers))

    def first_x(part):
        if used(part, 0):
            layer = PARTS[part][0]
            rows, room = rows_in(part, 0)
            x_copy(part, 0).wait()
            for y in (1 - yy, yy):
                parts[layer, core, side, :, y, rows, :] += xa_in[:, y, room, :]
                if y is not yy:
                    y_copy(part, 0).start()

    def first_y(part):
        if used(part, 1):
            layer = PARTS[part][0]
            rows, room = rows_in(part, 1)
            y_copy(part, 1).wait()
            for across in (1 - side, side):
                parts[layer, core, across, :, yy, rows, :] += yb_in[across, :, room, :]
                if across is not side:
                    x_copy(part, 1).start()

    def first_z(part):
        if used(part, 2):
            layer = PARTS[part][0]
            rows, room = rows_in(part, 2)
            for step in range(1, 4):
                z_copy(part, 2, step).wait()
            for across in (1 - side, side):
                total = parts[layer, core, across, zz, :, rows, :].astype(F32)
                for slot in range(1, 4):
                    total = total + third_z[slot, across, :, room, :].astype(F32)
                parts[layer, core, across, zz, :, rows, :] = total.astype(BF16)
                if across is not side:
                    x_copy(part, 2).start()

    def second_x(part):
        if used(part, 0):
            layer = PARTS[part][0]
            rows, room = rows_in(part, 0)
            y_copy(part, 0).wait()
            parts[layer, core, side, :, yy, rows, :] += ya_in[:, room, :]
            for step in range(1, 4):
                z_copy(part, 0, step).start()

    def second_y(part):
        if used(part, 1):
            layer = PARTS[part][0]
            rows, room = rows_in(part, 1)
            x_copy(part, 1).wait()
            parts[layer, core, side, :, yy, rows, :] += xb_in[:, room, :]
            for step in range(1, 4):
                z_copy(part, 1, step).start()

    def second_z(part):
        if used(part, 2):
            layer = PARTS[part][0]
            rows, room = rows_in(part, 2)
            x_copy(part, 2).wait()
            for y in (1 - yy, yy):
                parts[layer, core, side, zz, y, rows, :] += third_x[y, room, :]
                if y is not yy:
                    y_copy(part, 2).start()

    def third_done(part):
        layer = PARTS[part][0]
        for route in range(3):
            if not used(part, route):
                continue
            rows, room = rows_in(part, route)
            if route == 2:
                y_copy(part, 2).wait()
                final[layer, grp, rows, :] = parts[layer, core, side, zz, yy, rows, :] + third_y[room, :]
            else:
                for step in range(1, 4):
                    z_copy(part, route, step).wait()
                total = parts[layer, core, side, zz, yy, rows, :].astype(F32)
                for slot in range(1, 4):
                    total = total + z_in[layer, slot, rows, :].astype(F32)
                final[layer, grp, rows, :] = total.astype(BF16)
        if PARTS[part][1] >= 320:
            for row in (320, 448):
                final[layer, grp, row : row + 128, :] = final[layer, grp, row : row + 128, :].T
        for which in range(2):
            final_copy(part, which).start()

    def final_pass(part):
        final_copy(part, 0).wait()
        final_copy(part, 2).start()

    def final_done(part):
        for which in range(1, 3):
            final_copy(part, which).wait()

    def small_copy(stage):
        peer = (core_peer, x_peer, y_peer)[stage]
        return remote(
            small_sum.at[stage], small_in.at[stage], small_send.at[stage], small_recv.at[stage], peer
        )

    def small_z_copy(step):
        return remote(
            small_z.at[zz],
            small_z.at[zz],
            small_send.at[2 + step],
            small_recv.at[2 + step],
            place(core, side, lax.rem(zz + step, 4), yy),
        )

    def small_start():
        small_sum[0] = small[...]
        small_copy(0).start()

    def small_next(stage):
        small_copy(stage).wait()
        total = small_sum[stage] + small_in[stage]
        if stage < 2:
            small_sum[stage + 1] = total
            small_copy(stage + 1).start()
        else:
            small_z[zz] = total
            for step in range(1, 4):
                small_z_copy(step).start()

    def small_done():
        for step in range(1, 4):
            small_z_copy(step).wait()
        small_sum[0] = (small_z[0] + small_z[1]) + (small_z[2] + small_z[3])
        small_final[:, 0:256] = small_sum[0, :, pl.ds(pl.multiple_of(blk * 256, 256), 256)]
        pair = small_sum[0, :, pl.ds(pl.multiple_of(FF + 128 * zz, 128), 128)]
        small_final[:, 256:384] = jnp.where(yy == 1, pltpu.roll(pair, DIM, 1), pair)
        small_final[:, 384:512] = small_sum[0, :, FF + WIDTH :]

    def halves(*phases, first=0):
        def both(step, carry):
            for phase in phases:
                phase(lax.rem(step + first, 2))
            return carry

        lax.fori_loop(0, 2, both, 0)

    def begin(half):
        move_arrived(0, half, tok_in)
        hidden[rows_of(half), :] = tok_in[half].astype(F32)

    def finish(half):
        back_out[0, half] = hidden[rows_of(half), :].astype(BF16)
        to_owner(3, half, back_out.at[0, half], out_in)

    def turn_round(layer, half):
        move_arrived(2, half, cot_in)
        rows = rows_of(half)
        grad[rows, :] = cot_in[half].astype(F32)
        dz[rows, :] = (alphas[layer, 1] * grad[rows, :]).astype(BF16)

    def hand_back(half):
        back_out[1, half] = grad[rows_of(half), :].astype(BF16)
        to_owner(4, half, back_out.at[1, half], grad_in)

    barrier = pltpu.get_barrier_semaphore()
    for step in range(1, 4):
        credit(barrier, place(core, side, lax.rem(zz + step, 4), yy))
    for step in range(4):
        credit(barrier, place(1 - core, side, lax.rem(zz + step, 4), yy))
    for peer in (
        x_peer,
        y_peer,
        place(1 - core, side, zz, 1 - yy),
        place(1 - core, 1 - side, zz, yy),
        place(core, 1 - side, zz, 1 - yy),
        place(1 - core, 1 - side, zz, 1 - yy),
    ):
        credit(barrier, peer)

    weight_copies = {}
    for layer in range(LAYERS):
        for number, (source, target) in enumerate(
            ((qkv_hbm, wqkv), (out_hbm, wout), (up_hbm, wup), (down_hbm, wdown))
        ):
            weight_copies[layer, number] = pltpu.make_async_copy(
                source.at[layer], target.at[layer], w_sem.at[layer, number]
            )
    bias_copies = [
        pltpu.make_async_copy(up_bias_hbm, up_bias, w_sem.at[2, 0]),
        pltpu.make_async_copy(down_bias_hbm, down_bias, w_sem.at[2, 1]),
    ]
    weight_copies[0, 0].start()
    pl.semaphore_wait(barrier, 13)
    upper = lax.div(zz, 2)
    for half in (1 - upper, upper):
        to_team(0, half, half_of(tokens, half), tok_in)
    for layer, number in ((1, 0), (0, 1), (0, 2), (0, 3), (1, 1), (1, 2), (1, 3)):
        weight_copies[layer, number].start(priority=1)
    for copy in bias_copies:
        copy.start(priority=1)
    end_second = lax.div(seq_len[0, 0] + seq_len[0, 1], RUNS)
    flag_out[...] = jnp.full((8, 128), end_second.astype(F32), F32)
    for half in (1 - upper, upper):
        to_team(1, half, flag_out, flag_in)
    for layer in range(LAYERS):
        for head in range(OWN):
            rq[layer, head, DIM:, :] = jnp.zeros((DIM, HALF * RUNS), BF16)
    for head in range(OWN):
        ro[head, 0:DIM, :] = jnp.zeros((DIM, HALF * RUNS), BF16)
    def reorder(layer):
        weight_copies[layer, 0].wait()
        pairs = [
            beside(
                wqkv[layer, :, WIDTH + 128 * pair : WIDTH + 128 * pair + 128].astype(F32),
                wqkv[layer, :, 2 * WIDTH + 128 * pair : 2 * WIDTH + 128 * pair + 128].astype(F32),
            )
            for pair in range(TEAM)
        ]
        for head in range(RUNS):
            at = WIDTH + 128 * head
            wqkv[layer, :, at : at + 128] = pairs[head // 2][head % 2].astype(BF16)

    reorder(0)
    halves(begin, functools.partial(project, 0), first=upper)
    for half in (1 - upper, upper):
        to_team(2, half, half_of(cotangent, half), cot_in)

    reorder(1)
    move_arrived(1, 0, flag_in)
    move_arrived(1, 1, flag_in)
    border = jnp.concatenate([flag_in[0, 0:1, :]] * 2, axis=1) - (HALF * lax.div(zz, 2)).astype(F32)
    key_row = lax.broadcasted_iota(jnp.int32, (TILE, TILE), 0)
    query_col = lax.broadcasted_iota(jnp.int32, (TILE, TILE), 1)
    later = key_row > query_col
    key_sub = lax.rem(key_row, HALF).astype(F32) >= border
    query_sub = lax.rem(query_col, HALF).astype(F32) >= border
    apart = jnp.logical_xor(key_sub, query_sub)
    for tile in range(TILES - 1):
        bias[TILE * tile : TILE * tile + TILE, :] = jnp.where(apart, NEGATIVE, 0.0)
    bias[TILE * (TILES - 1) :, :] = jnp.where(jnp.logical_or(later, apart), NEGATIVE, 0.0)

    for copy in (*bias_copies, *(weight_copies[0, number] for number in range(1, 4))):
        copy.wait()
    attend(0, 0)
    attend(0, 1)
    hidden_start(0, 0)
    halves(functools.partial(feed, 0), functools.partial(project, 1))
    for number in range(1, 4):
        weight_copies[1, number].wait()
    attend(1, 0)
    attend(1, 1)
    hidden_pass(0, 0)
    hidden_start(0, 1)
    hidden_start(1, 0)
    halves(functools.partial(feed, 1), finish)
    hidden_pass(0, 1)
    hidden_pass(1, 0)

    halves(functools.partial(turn_round, 1))
    make(1)
    feed_back(1)
    hidden_start(1, 1)
    core_done(1)
    make(0)
    attend_back(1, 1)
    first_y(1)
    core_done(0)
    hidden_pass(1, 1)
    attend_back(1, 0)
    second_y(1)
    first_y(0)
    first_x(1)
    project_back(1, 1)
    heads_grads(1)
    first_z(1)
    project_back(1, 0)
    feed_back(0)
    small_start()
    second_x(1)
    second_y(0)
    make(2)
    first_x(0)
    heads_second(1)
    first_z(0)
    attend_back(0, 1)
    small_next(0)
    core_done(2)
    second_x(0)
    make(3)
    attend_back(0, 0)
    small_next(1)
    project_back(0, 1)
    hand_back(1)
    first_z(2)
    heads_grads(0)
    small_next(2)
    first_x(2)
    core_done(3)
    first_y(2)
    heads_second(0)
    small_done()
    first_z(3)
    second_x(2)
    first_x(3)
    second_z(2)
    second_z(0)
    heads_third(1)
    second_z(1)
    first_y(3)
    heads_third(0)
    second_y(2)
    second_x(3)
    second_z(3)
    third_done(0)
    third_done(2)
    second_y(3)
    project_back(0, 0)
    hand_back(0)
    heads_done(1)
    third_done(1)
    third_done(3)
    final_pass(0)
    final_pass(2)
    final_pass(1)
    final_pass(3)
    final_done(2)
    final_done(1)
    heads_done(0)
    final_done(0)
    final_done(3)
    for half in range(2):
        move_arrived(3, half, out_in)
        move_arrived(4, half, grad_in)

    for half in range(2):
        left(2, 0, half, head_out)
        left(3, 0, half, pack_out)
        to_team_left(0, half, half_of(tokens, half))
        to_team_left(1, half, flag_out)
        to_team_left(2, half, half_of(cotangent, half))
        to_owner_left(3, half, back_out.at[0, half])
        to_owner_left(4, half, back_out.at[1, half])


def results_kernel(
    final, heads, out_block, grad_block, small,
    output, input_grad, qkv_grad, out_grad, up_grad, up_bias_grad, down_grad, down_bias_grad, alpha_grad,
    out_flat, grad_wide, qkv_wide, out_wide, up_wide, down_wide, out_sem,
):
    ends = []

    def write(source, target):
        ends.append(pltpu.make_async_copy(source, target, out_sem.at[len(ends)]))
        ends[-1].start()

    up_bias_grad[...] = small[:, 0:256]
    down_bias_grad[...] = small[:, 256 : 256 + DIM]
    alpha_grad[...] = small[:, 384:386]
    for layer in range(LAYERS):
        for quarter in range(4):

            def block(first, count):
                return final[layer, quarter, first : first + count, :].astype(F32)

            def columns(step):
                return slice(WIDTH * step + 128 * quarter, WIDTH * step + 128 * quarter + 128)

            for step in range(4):
                up_wide[layer, :, columns(step)] = block(DIM * step, DIM)
            out_wide[layer, :, columns(0)] = block(256, DIM)
            down_wide[layer, :, columns(0)] = block(320, 256)
        write(up_wide.at[layer], up_grad.at[layer])
        write(out_wide.at[layer], out_grad.at[layer])
        write(down_wide.at[layer], down_grad.at[layer])
    for half in range(2):
        rows = slice(HALF * half, HALF * half + HALF)
        grad_wide[rows, :] = grad_block[half].astype(F32)
        out_flat[rows, :] = out_block[half]
    write(grad_wide, input_grad)
    write(out_flat, output)
    for layer in range(LAYERS):
        for side in range(2):
            for member in range(TEAM):
                block = heads[layer, side, member].astype(F32)
                columns = (block[:, 0:128], *beside(block[:, 128:256], block[:, 256:384]))
                for step in range(3):
                    at = WIDTH * step + 128 * member
                    qkv_wide[layer, 32 * side : 32 * side + 32, at : at + 128] = columns[step]
        write(qkv_wide.at[layer], qkv_grad.at[layer])
    for end in ends:
        end.wait()


def fast_body(
    tokens, seq_len, qkv_weight, out_weight, up_weight, up_bias, down_weight, down_bias, alphas, cotangent
):
    whole = pl.BlockSpec(memory_space=pltpu.VMEM)
    scalar = pl.BlockSpec(memory_space=pltpu.SMEM)
    far = pl.BlockSpec(memory_space=pl.ANY)
    shape = jax.ShapeDtypeStruct
    rows = HALF * RUNS

    def vmem(*dims):
        return pltpu.VMEM(dims, BF16)

    def wide(*dims):
        return pltpu.VMEM(dims, F32)

    dma = pltpu.SemaphoreType.DMA
    final, heads, out_block, grad_block, small = pl.pallas_call(
        layers_kernel,
        out_shape=(
            vmem(LAYERS, 4, CHUNK, 128),
            vmem(LAYERS, 2, TEAM, DIM // 2, 3 * 128),
            vmem(2, HALF, WIDTH),
            vmem(2, HALF, WIDTH),
            wide(LAYERS, WIDTH),
        ),
        in_specs=[far, scalar, scalar, far, far, far, far, far, far, far],
        out_specs=(whole,) * 5,
        scratch_shapes=[
            vmem(LAYERS, WIDTH, 3 * WIDTH),
            vmem(LAYERS, WIDTH, WIDTH),
            vmem(LAYERS, WIDTH, FF),
            vmem(LAYERS, FF, WIDTH),
            wide(LAYERS, FF),
            wide(LAYERS, WIDTH),
            vmem(2, HALF, WIDTH),
            vmem(2, HALF, WIDTH),
            wide(8, 128),
            wide(2, 8, 128),
            vmem(2, 2, HALF, WIDTH),
            wide(2 * HALF, WIDTH),
            wide(2 * HALF, WIDTH),
            vmem(LAYERS, WIDTH, rows),
            vmem(LAYERS, WIDTH, 2 * HALF),
            vmem(LAYERS, 2 * HALF, WIDTH),
            vmem(LAYERS, 2 * HALF, FF),
            wide(LAYERS, 2 * HALF, WIDTH),
            wide(LAYERS, 2 * HALF, FF),
            wide(LAYERS, 2 * HALF, WIDTH),
            vmem(2 * HALF, WIDTH),
            vmem(2 * HALF, FF),
            vmem(2 * HALF, WIDTH),
            vmem(HALF, 3 * WIDTH),
            vmem(2, TEAM, OWN, PACK, 128),
            vmem(2, TEAM, OWN, DIM, 128),
            vmem(2, TEAM, OWN, PACK, 128),
            vmem(2, TEAM, OWN, DIM, 128),
            vmem(2, TEAM, OWN, DIM, 128),
            vmem(LAYERS, OWN, rows, 128),
            vmem(LAYERS, OWN, 128, rows),
            vmem(LAYERS, OWN, 128, rows),
            vmem(OWN, 128, rows),
            wide(LAYERS, OWN, DIM, rows),
            wide(LAYERS, OWN, 1, rows),
            wide(OWN, rows, 128),
            wide(OWN, DIM, rows),
            wide(rows, TILE),
            vmem(LAYERS, 2, 2, 4, 2, CHUNK, 128),
            vmem(2, 4, 2, CHUNK, 128),
            vmem(4, 2, TOTALS[0], 128),
            vmem(4, TOTALS[1], 128),
            vmem(4, TOTALS[0], 128),
            vmem(2, 4, TOTALS[1], 128),
            vmem(LAYERS, 4, CHUNK, 128),
            vmem(4, 2, 2, TOTALS[2], 128),
            vmem(2, TOTALS[2], 128),
            vmem(TOTALS[2], 128),
            vmem(LAYERS, 4, 2, DIM, 3 * 128),
            vmem(LAYERS, 4, 2, DIM // 2, 3 * 128),
            vmem(LAYERS, 4, 2, DIM // 2, 3 * 128),
            vmem(LAYERS, 2, DIM // 2, 3 * 128),
            wide(LAYERS, SMALL),
            wide(3, LAYERS, SMALL),
            wide(4, LAYERS, SMALL),
            wide(3, LAYERS, SMALL),
            dma((LAYERS + 1, 4)),
            dma((5, 2)),
            dma((5, 2)),
            dma((4, LAYERS, 2, OWN)),
            dma((4, LAYERS, 2, OWN)),
            dma((len(PARTS),)),
            dma((len(PARTS),)),
            dma((len(PARTS), 3)),
            dma((len(PARTS), 3)),
            dma((len(PARTS), 3)),
            dma((len(PARTS), 3)),
            dma((len(PARTS), 3, 4)),
            dma((len(PARTS), 3, 4)),
            dma((len(PARTS), 3)),
            dma((len(PARTS), 3)),
            dma((LAYERS, 2, 3)),
            dma((LAYERS, 2, 3)),
            dma((LAYERS,)),
            dma((LAYERS,)),
            dma((LAYERS, 4)),
            dma((LAYERS, 4)),
            dma((LAYERS, 8)),
            dma((LAYERS, 8)),
            dma((6,)),
            dma((6,)),
            pltpu.SemaphoreType.REGULAR((2,)),
        ],
        compiler_params=pltpu.CompilerParams(
            collective_id=0, has_side_effects=True, vmem_limit_bytes=61 * 1024 * 1024
        ),
        name="layers",
    )(
        tokens, seq_len, alphas, up_bias, down_bias, cotangent,
        qkv_weight, out_weight, up_weight, down_weight,
    )
    return tuple(
        pl.pallas_call(
            results_kernel,
            out_shape=(
                shape((2 * HALF, WIDTH), BF16),
                shape((2 * HALF, WIDTH), F32),
                shape((LAYERS, DIM, 3 * WIDTH), F32),
                shape((LAYERS, DIM, WIDTH), F32),
                shape((LAYERS, DIM, FF), F32),
                shape((LAYERS, FF // RUNS), F32),
                shape((LAYERS, FF // RUNS, WIDTH), F32),
                shape((LAYERS, DIM), F32),
                shape((LAYERS, 2), F32),
            ),
            in_specs=[whole] * 5,
            out_specs=(far, far, far, far, far, whole, far, whole, whole),
            scratch_shapes=[
                vmem(2 * HALF, WIDTH),
                wide(2 * HALF, WIDTH),
                wide(LAYERS, DIM, 3 * WIDTH),
                wide(LAYERS, DIM, WIDTH),
                wide(LAYERS, DIM, FF),
                wide(LAYERS, FF // RUNS, WIDTH),
                dma((10,)),
            ],
            compiler_params=pltpu.CompilerParams(vmem_limit_bytes=24 * 1024 * 1024),
            name="results",
        )(final, heads, out_block, grad_block, small)
    )


def layout(seq_len, local_count, cycle_size):
    piece_rows = seq_len[0] // cycle_size
    end_rows = jnp.cumsum(piece_rows)
    start_rows = end_rows - piece_rows
    local_rows = jnp.arange(local_count, dtype=jnp.int32)
    segment = jnp.sum((local_rows[:, None] >= end_rows[None, :]).astype(jnp.int32), axis=1)
    picked = segment[:, None] == jnp.arange(seq_len.shape[1], dtype=jnp.int32)[None, :]
    offset = local_rows - jnp.sum(jnp.where(picked, start_rows[None, :], 0), axis=1)
    span_rows = jnp.sum(jnp.where(picked, piece_rows[None, :], 0), axis=1)
    return (segment, offset, span_rows)


def gelu_exact(values):
    return jax.nn.gelu(values, approximate=False)


def key_block(whole, geometry, block_index, head_count):
    query_seg, query_pos, seg_all, pos_all, block_rows, score_scale = geometry
    first_row = block_index * block_rows
    key_piece = lax.dynamic_slice_in_dim(whole, first_row, block_rows, 0)
    key_seg = lax.dynamic_slice_in_dim(seg_all, first_row, block_rows, 0)
    key_pos = lax.dynamic_slice_in_dim(pos_all, first_row, block_rows, 0)
    half_width = key_piece.shape[1] // 2
    keys_part = key_piece[:, :half_width].reshape(block_rows, head_count, -1)
    values_part = key_piece[:, half_width:].reshape(block_rows, head_count, -1)
    return (keys_part, values_part, key_seg, key_pos)


def block_scores(queries, keys_part, key_seg, key_pos, geometry):
    query_seg, query_pos, seg_all, pos_all, block_rows, score_scale = geometry
    scores = (
        jnp.einsum("qhd,khd->hqk", queries, keys_part, preferred_element_type=jnp.float32)
        * score_scale
    )
    allowed = (query_seg[:, None] == key_seg[None, :]) & (key_pos[None, :] <= query_pos[:, None])
    return (scores, allowed[None])


def attend(queries, whole, geometry):
    row_count, head_count, head_dim = queries.shape
    block_count = whole.shape[0] // geometry[4]

    def statistics(running, block_index):
        largest, totals = running
        keys_part, values_part, key_seg, key_pos = key_block(
            whole, geometry, block_index, head_count
        )
        scores, allowed = block_scores(queries, keys_part, key_seg, key_pos, geometry)
        newest = jnp.maximum(largest, jnp.max(jnp.where(allowed, scores, NEGATIVE), axis=2))
        weights = jnp.where(allowed, jnp.exp(scores - newest[:, :, None]), 0.0)
        totals = totals * jnp.exp(largest - newest) + jnp.sum(weights, axis=2)
        return ((newest, totals), None)

    initial = (
        jnp.full((head_count, row_count), NEGATIVE, jnp.float32),
        jnp.zeros((head_count, row_count), jnp.float32),
    )
    (largest, totals), unused = lax.scan(statistics, initial, jnp.arange(block_count))
    log_total = largest + jnp.log(totals)

    def weighted(output_sum, block_index):
        keys_part, values_part, key_seg, key_pos = key_block(
            whole, geometry, block_index, head_count
        )
        scores, allowed = block_scores(queries, keys_part, key_seg, key_pos, geometry)
        probs = jnp.where(allowed, jnp.exp(scores - log_total[:, :, None]), 0.0).astype(
            jnp.bfloat16
        )
        output_sum = output_sum + jnp.einsum(
            "hqk,khd->qhd", probs, values_part, preferred_element_type=jnp.float32
        )
        return (output_sum, None)

    output_sum, unused = lax.scan(
        weighted, jnp.zeros((row_count, head_count, head_dim), jnp.float32), jnp.arange(block_count)
    )
    return (output_sum, log_total)


def attend_back(queries, whole, log_total, delta_sum, grad_heads, geometry):
    row_count, head_count, head_dim = queries.shape
    block_rows = geometry[4]
    score_scale = geometry[5]
    block_count = whole.shape[0] // block_rows

    def gradients(query_grad, block_index):
        keys_part, values_part, key_seg, key_pos = key_block(
            whole, geometry, block_index, head_count
        )
        scores, allowed = block_scores(queries, keys_part, key_seg, key_pos, geometry)
        probs = jnp.where(allowed, jnp.exp(scores - log_total[:, :, None]), 0.0)
        grad_probs = jnp.einsum(
            "qhd,khd->hqk", grad_heads, values_part, preferred_element_type=jnp.float32
        )
        grad_scores = (probs * (grad_probs - delta_sum[:, :, None])).astype(jnp.bfloat16)
        query_grad = (
            query_grad
            + jnp.einsum("hqk,khd->qhd", grad_scores, keys_part, preferred_element_type=jnp.float32)
            * score_scale
        )
        key_grad = (
            jnp.einsum("hqk,qhd->khd", grad_scores, queries, preferred_element_type=jnp.float32)
            * score_scale
        )
        value_grad = jnp.einsum(
            "hqk,qhd->khd",
            probs.astype(jnp.bfloat16),
            grad_heads,
            preferred_element_type=jnp.float32,
        )
        joined = jnp.concatenate(
            [key_grad.reshape(block_rows, -1), value_grad.reshape(block_rows, -1)], axis=1
        )
        return (query_grad, joined)

    query_grad, stacked = lax.scan(
        gradients,
        jnp.zeros((row_count, head_count, head_dim), jnp.float32),
        jnp.arange(block_count),
    )
    return (query_grad, stacked.reshape(whole.shape[0], -1))


def layer_forward(hidden, layer_index, weights, geometry):
    qkv_weight, out_weight, up_weight, up_bias, down_weight, down_bias, alphas = weights
    row_count, model_width = hidden.shape
    projection = qkv_weight[layer_index]
    rounded = hidden.astype(jnp.bfloat16)
    queries = (
        jnp.dot(rounded, projection[:, :model_width], preferred_element_type=jnp.float32)
        .astype(jnp.bfloat16)
        .reshape(row_count, HEADS, -1)
    )
    key_value = jnp.dot(
        rounded, projection[:, model_width:], preferred_element_type=jnp.float32
    ).astype(jnp.bfloat16)
    whole = lax.all_gather(key_value, "blk", axis=0, tiled=True)
    heads_out, log_total = attend(queries, whole, geometry)
    heads_rounded = heads_out.reshape(row_count, model_width).astype(jnp.bfloat16)
    branch = jnp.dot(heads_rounded, out_weight[layer_index], preferred_element_type=jnp.float32)
    alpha_pair = alphas[layer_index]
    middle = hidden + alpha_pair[0] * branch
    entered = middle.astype(jnp.bfloat16)
    gate_pre = (
        jnp.dot(entered, up_weight[layer_index], preferred_element_type=jnp.float32)
        + up_bias[layer_index]
    )
    activated = gelu_exact(gate_pre).astype(jnp.bfloat16)
    second = (
        jnp.dot(activated, down_weight[layer_index], preferred_element_type=jnp.float32)
        + down_bias[layer_index]
    )
    result = middle + alpha_pair[1] * second
    saved = (
        rounded,
        queries,
        key_value,
        whole,
        heads_out,
        heads_rounded,
        log_total,
        branch,
        entered,
        gate_pre,
        activated,
        second,
    )
    return (result, saved)


def layer_backward(grad_hidden, saved, layer_index, weights, geometry):
    qkv_weight, out_weight, up_weight, up_bias, down_weight, down_bias, alphas = weights
    (
        rounded,
        queries,
        key_value,
        saved_whole,
        heads_out,
        heads_rounded,
        log_total,
        branch,
        entered,
        gate_pre,
        activated,
        second,
    ) = saved
    row_count = grad_hidden.shape[0]
    alpha_pair = alphas[layer_index]
    grad_second = (alpha_pair[1] * grad_hidden).astype(jnp.bfloat16)
    alpha_second = jnp.sum(grad_hidden * second)
    bias_down = jnp.sum(grad_second.astype(jnp.float32), axis=0)
    grad_down = jnp.einsum("tf,td->fd", activated, grad_second, preferred_element_type=jnp.float32)
    grad_act = jnp.einsum(
        "td,fd->tf", grad_second, down_weight[layer_index], preferred_element_type=jnp.float32
    )
    unused, gelu_pull = jax.vjp(gelu_exact, gate_pre)
    grad_gate = gelu_pull(grad_act)[0].astype(jnp.bfloat16)
    bias_up = jnp.sum(grad_gate.astype(jnp.float32), axis=0)
    grad_up = jnp.einsum("td,tf->df", entered, grad_gate, preferred_element_type=jnp.float32)
    grad_middle = grad_hidden + jnp.einsum(
        "tf,df->td", grad_gate, up_weight[layer_index], preferred_element_type=jnp.float32
    )
    grad_branch = (alpha_pair[0] * grad_middle).astype(jnp.bfloat16)
    alpha_first = jnp.sum(grad_middle * branch)
    grad_proj_out = jnp.einsum(
        "te,td->ed", heads_rounded, grad_branch, preferred_element_type=jnp.float32
    )
    grad_heads = (
        jnp.einsum(
            "td,ed->te", grad_branch, out_weight[layer_index], preferred_element_type=jnp.float32
        )
        .astype(jnp.bfloat16)
        .reshape(queries.shape)
    )
    delta_sum = jnp.sum(grad_heads.astype(jnp.float32) * heads_out, axis=2).T
    whole = lax.all_gather(key_value, "blk", axis=0, tiled=True)
    query_grad, key_terms = attend_back(queries, whole, log_total, delta_sum, grad_heads, geometry)
    key_grads = lax.psum_scatter(
        key_terms.astype(jnp.bfloat16), "blk", scatter_dimension=0, tiled=True
    )
    grad_proj = jnp.concatenate(
        [query_grad.reshape(row_count, -1).astype(jnp.bfloat16), key_grads], axis=1
    )
    grad_qkv = jnp.einsum("td,te->de", rounded, grad_proj, preferred_element_type=jnp.float32)
    grad_input = grad_middle + jnp.einsum(
        "te,de->td", grad_proj, qkv_weight[layer_index], preferred_element_type=jnp.float32
    )
    layer_grads = (
        grad_qkv,
        grad_proj_out,
        grad_up,
        bias_up,
        grad_down,
        bias_down,
        jnp.stack([alpha_first, alpha_second]),
    )
    return (grad_input, layer_grads)


def reduce_all(layer_results, cycle_size):
    stacked = [
        jnp.stack([layer_entry[member] for layer_entry in layer_results], axis=0)
        for member in range(6)
    ]
    alpha_tiles = jnp.stack(
        [jnp.tile(layer_entry[6], cycle_size) for layer_entry in layer_results], axis=0
    )
    shares = (
        lax.psum_scatter(
            stacked[0].astype(jnp.bfloat16), "blk", scatter_dimension=1, tiled=True
        ).astype(jnp.float32),
        lax.psum_scatter(
            stacked[1].astype(jnp.bfloat16), "blk", scatter_dimension=1, tiled=True
        ).astype(jnp.float32),
        lax.psum_scatter(
            stacked[2].astype(jnp.bfloat16), "blk", scatter_dimension=1, tiled=True
        ).astype(jnp.float32),
        lax.psum_scatter(
            stacked[3].astype(jnp.bfloat16), "blk", scatter_dimension=1, tiled=True
        ).astype(jnp.float32),
        lax.psum_scatter(
            stacked[4].astype(jnp.bfloat16), "blk", scatter_dimension=1, tiled=True
        ).astype(jnp.float32),
        lax.psum_scatter(
            stacked[5].astype(jnp.bfloat16), "blk", scatter_dimension=1, tiled=True
        ).astype(jnp.float32),
        lax.psum_scatter(
            alpha_tiles.astype(jnp.bfloat16), "blk", scatter_dimension=1, tiled=True
        ).astype(jnp.float32),
    )
    return (
        lax.psum(shares[0].astype(jnp.bfloat16), "grp").astype(jnp.float32),
        lax.psum(shares[1].astype(jnp.bfloat16), "grp").astype(jnp.float32),
        lax.psum(shares[2].astype(jnp.bfloat16), "grp").astype(jnp.float32),
        lax.psum(shares[3].astype(jnp.bfloat16), "grp").astype(jnp.float32),
        lax.psum(shares[4].astype(jnp.bfloat16), "grp").astype(jnp.float32),
        lax.psum(shares[5].astype(jnp.bfloat16), "grp").astype(jnp.float32),
        lax.psum(shares[6].astype(jnp.bfloat16), "grp").astype(jnp.float32),
    )


def body(
    tokens,
    seq_len,
    qkv_weight,
    out_weight,
    up_weight,
    up_bias,
    down_weight,
    down_bias,
    alphas,
    cotangent,
):
    row_count, model_width = tokens.shape
    cycle_size = lax.axis_size("blk")
    cycle_place = lax.axis_index("blk")
    head_dim = model_width // HEADS
    total_rows = cycle_size * row_count
    block_rows = min(max(row_count, 512), total_rows)
    segment, offset, span_rows = layout(seq_len, row_count, cycle_size)
    query_pos = cycle_place * span_rows + offset
    seg_all = jnp.tile(segment, cycle_size)
    pos_all = jnp.repeat(jnp.arange(cycle_size, dtype=jnp.int32), row_count) * jnp.tile(
        span_rows, cycle_size
    ) + jnp.tile(offset, cycle_size)
    geometry = (segment, query_pos, seg_all, pos_all, block_rows, head_dim ** (-0.5))
    weights = (qkv_weight, out_weight, up_weight, up_bias, down_weight, down_bias, alphas)
    hidden = tokens.astype(jnp.float32)
    saved_layers = []
    for layer_index in range(LAYERS):
        hidden, saved = layer_forward(hidden, layer_index, weights, geometry)
        saved_layers.append(saved)
    output = hidden.astype(jnp.bfloat16)
    grad_hidden = cotangent.astype(jnp.float32)
    layer_results = []
    for layer_index in reversed(range(LAYERS)):
        grad_hidden, layer_grads = layer_backward(
            grad_hidden, saved_layers[layer_index], layer_index, weights, geometry
        )
        layer_results.insert(0, layer_grads)
    finals = reduce_all(layer_results, cycle_size)
    return (
        output,
        grad_hidden,
        finals[0],
        finals[1],
        finals[2],
        finals[3],
        finals[4],
        finals[5],
        finals[6],
    )


def solution(mesh):
    placed = (
        P(("grp", "blk"), None),
        P("grp", None),
        P(),
        P(),
        P(),
        P(),
        P(),
        P(),
        P(),
        P(("grp", "blk"), None),
    )
    sizes = (mesh.shape["grp"], mesh.shape["blk"])
    return jax.shard_map(
        fast_body if sizes == (4, RUNS) else body,
        mesh=mesh,
        in_specs=placed,
        out_specs=(
            P(("grp", "blk"), None),
            P(("grp", "blk"), None),
            P(None, "blk", None),
            P(None, "blk", None),
            P(None, "blk", None),
            P(None, "blk"),
            P(None, "blk", None),
            P(None, "blk"),
            P(),
        ),
        check_vma=False,
    )
```

```python
import functools

import jax
import jax.numpy as jnp
from jax import lax
from jax.experimental import pallas as pl
from jax.experimental.pallas import tpu as pltpu
from jax.sharding import PartitionSpec as P

HEADS = 8
LAYERS = 2
NEGATIVE = -1e30
MESH = pl.DeviceIdType.MESH
F32 = jnp.float32
BF16 = jnp.bfloat16

HALF = 128
RUNS = 8
TEAM = 4
OWN = RUNS // TEAM
DIM = 64
WIDTH = 512
FF = 2048
CUT = 512
TILE = 256
TILES = HALF * RUNS // TILE
PACK = HALF + DIM
CHUNK = 576
SMALL = FF + WIDTH + 128
PARTS = ((1, 0, 320), (1, 320, 256), (0, 0, 320), (0, 320, 256))
SHARES = ((192, 0, 128), (160, 16, 80), (160, 128, 32), (128, 96, 32))


def spans():
    places, totals = {}, [0, 0, 0]
    for part, counts in enumerate(SHARES):
        first = PARTS[part][1]
        for route, count in enumerate(counts):
            places[part, route] = (first, totals[route], count)
            first += count
            totals[route] += count
    return places, totals


SPANS, TOTALS = spans()

SLOPE_AT = 0.28
TAIL = (
    0.11652077851573843,
    0.06749675579450809,
    0.2689101589486142,
    -0.23699347299932225,
    0.3898740127620002,
    -0.10580824228351815,
)


def nn(a, b):
    return lax.dot_general(a, b, (((1,), (0,)), ((), ())), preferred_element_type=F32)


def nt(a, b):
    return lax.dot_general(a, b, (((1,), (1,)), ((), ())), preferred_element_type=F32)


def beside(first, other):
    low = lax.broadcasted_iota(jnp.int32, first.shape, 1) < DIM
    return (
        jnp.where(low, first, pltpu.roll(other, DIM, 1)),
        jnp.where(low, pltpu.roll(first, DIM, 1), other),
    )


def layers_kernel(
    tokens, seq_len_hbm, alphas_hbm, up_bias_hbm, down_bias_hbm, cotangent, qkv_hbm, out_hbm, up_hbm, down_hbm,
    final, heads_all, out_in, grad_in, small_final,
    seq_len, alphas, wqkv, wout, wup, wdown, up_bias, down_bias,
    tok_in, cot_in, flag_out, flag_in, back_out,
    hidden, grad, hid_all, attn_t, entered, act, branch, slope, second,
    dz, du, da, dqkv,
    pack_out, head_out, pack_in, o_in, do_in,
    kv, kv_t, rq, ro, o_t, lse, acc, dq_t, bias,
    parts, core_in, xa_in, xb_in, ya_in, yb_in, z_in, third_z, third_x, third_y,
    heads_out, heads_x, heads_z, heads_sum, small, small_in, small_z, small_sum,
    w_sem, move_send, move_recv, a2a_send, a2a_recv, core_send, core_recv, x_send, x_recv, y_send, y_recv,
    z_send, z_recv, fin_send, fin_recv, hid_send, hid_recv, hx_send, hx_recv, hz_send, hz_recv, hf_send, hf_recv,
    small_send, small_recv, core_free,
):
    grp = lax.axis_index("grp")
    blk = lax.axis_index("blk")
    core = lax.rem(grp, 2)
    side = lax.div(grp, 2)
    yy = lax.rem(blk, 2)
    zz = lax.div(blk, 2)
    member = 2 * core + yy
    far_side = 2 * (1 - side) + core

    def place(c, x, z, y):
        return (2 * x + c, 2 * z + y)

    core_peer = place(1 - core, side, zz, yy)
    x_peer = place(core, 1 - side, zz, yy)
    y_peer = place(core, side, zz, 1 - yy)

    def remote(source, target, send, recv, peer):
        return pltpu.make_async_remote_copy(
            src_ref=source,
            dst_ref=target,
            send_sem=send,
            recv_sem=recv,
            device_id=peer,
            device_id_type=MESH,
        )

    def credit(semaphore, peer, count=1):
        pl.semaphore_signal(semaphore, inc=count, device_id=peer, device_id_type=MESH)

    def moved(kind, slot, source, target, at, core_at, z_at):
        here = jnp.logical_and(core_at == core, z_at == zz)

        @pl.when(here)
        def _():
            pltpu.make_async_copy(source, target.at[at], move_recv.at[kind, at]).start()

        @pl.when(jnp.logical_not(here))
        def _():
            pltpu.make_async_remote_copy(
                src_ref=source,
                dst_ref=target.at[at],
                send_sem=move_send.at[kind, slot],
                recv_sem=move_recv.at[kind, at],
                device_id=place(core_at, side, z_at, yy),
                device_id_type=MESH,
            ).start()

    def move_left(kind, slot, source, core_at, z_at):
        here = jnp.logical_and(core_at == core, z_at == zz)

        @pl.when(jnp.logical_not(here))
        def _():
            pltpu.make_async_copy(source, source, move_send.at[kind, slot]).wait()

    def move_arrived(kind, at, target):
        pltpu.make_async_copy(target.at[at], target.at[at], move_recv.at[kind, at]).wait()

    def to_team(kind, half, source, target):
        moved(kind, half, source, target, lax.div(zz, 2), lax.rem(zz, 2), 2 * half + core)

    def to_team_left(kind, half, source):
        move_left(kind, half, source, lax.rem(zz, 2), 2 * half + core)

    def to_owner(kind, chunk, source, target):
        moved(kind, chunk, source, target, lax.div(zz, 2), lax.rem(zz, 2), core + 2 * chunk)

    def to_owner_left(kind, chunk, source):
        move_left(kind, chunk, source, lax.rem(zz, 2), core + 2 * chunk)

    def half_of(ref, half):
        return ref.at[pl.ds(pl.multiple_of(HALF * half, HALF), HALF)]

    def rows_of(half):
        return pl.ds(pl.multiple_of(half * HALF, HALF), HALF)

    def slot_of(other):
        return lax.rem(other + TEAM - member, TEAM)

    def exchange(kind, layer, half, outgoing, incoming, head=None):
        at = () if head is None else (head,)
        incoming[(half, 0, *at)] = outgoing[(half, member, *at)]
        for step in range(1, TEAM):
            peer = lax.rem(member + step, TEAM)
            remote(
                outgoing.at[(half, peer, *at)],
                incoming.at[(half, TEAM - step, *at)],
                a2a_send.at[kind, layer, half, head or 0],
                a2a_recv.at[kind, layer, half, head or 0],
                place(lax.div(peer, 2), side, zz, lax.rem(peer, 2)),
            ).start()

    def arrived(kind, layer, half, incoming, head=None):
        at = () if head is None else (head,)
        whole = incoming.at[(half, pl.ds(1, TEAM - 1), *at)]
        pltpu.make_async_copy(whole, whole, a2a_recv.at[kind, layer, half, head or 0]).wait()

    def left(kind, layer, half, outgoing):
        for head in range(OWN) if kind in (0, 3) else (None,):
            at = () if head is None else (head,)
            whole = outgoing.at[(half, pl.ds(1, TEAM - 1), *at)]
            pltpu.make_async_copy(whole, whole, a2a_send.at[kind, layer, half, head or 0]).wait()

    def tokens_of(chunk, other):
        return pl.ds(pl.multiple_of(HALF * (TEAM * chunk + other), HALF), HALF)

    def hidden_copy(layer, chunk, which):
        whose = 2 * core + 1 - yy if which == 2 else member
        block = hid_all.at[layer, :, tokens_of(chunk, whose)]
        return remote(
            block,
            block,
            hid_send.at[layer, chunk, which],
            hid_recv.at[layer, chunk, which],
            y_peer if which == 0 else core_peer,
        )

    def hidden_start(layer, chunk):
        for which in range(2):
            hidden_copy(layer, chunk, which).start()

    def hidden_pass(layer, chunk):
        hidden_copy(layer, chunk, 0).wait()
        hidden_copy(layer, chunk, 2).start()

    def hidden_done(layer, chunk):
        for which in range(1, 3):
            hidden_copy(layer, chunk, which).wait()

    def project(layer, half):
        rows = rows_of(half)
        rounded = hidden[rows, :].astype(BF16)
        if layer == 1:
            left(0, 0, half, pack_out)
        queries = (nn(rounded, wqkv[layer, :, 0:WIDTH]) * (DIM ** -0.5)).astype(BF16).T
        for head in range(RUNS):
            pack_out[half, head // 2, head % 2, HALF:, :] = queries[DIM * head : DIM * head + DIM, :]
        for step in range(2):
            at = WIDTH * (step + 1)
            keys_values = nn(rounded, wqkv[layer, :, at : at + WIDTH]).astype(BF16)
            for head in range(4):
                pack_out[half, 2 * step + head // 2, head % 2, 0:HALF, :] = keys_values[
                    :, 128 * head : 128 * head + 128
                ]
        for head in range(OWN):
            exchange(0, layer, half, pack_out, pack_in, head)
        hid_all[layer, :, tokens_of(half, member)] = rounded.T

    def attend(layer, chunk):
        if layer == 1:
            left(1, 0, chunk, head_out)

        def one_head(head, carry):
            arrived(0, layer, chunk, pack_in, head)
            for other in range(TEAM):
                slot = slot_of(other)
                start = HALF * (TEAM * chunk + other)
                span = slice(start, start + HALF)
                block = pack_in[chunk, slot, head, 0:HALF, :]
                kv[layer, head, span, :] = block
                kv_t[layer, head, :, span] = block.T
                rq[layer, head, 0:DIM, span] = pack_in[chunk, slot, head, HALF:, :]

            def scores_of(i):
                count = TILE * (i + 1)
                tile = rq[layer, head, :, TILE * i : TILE * i + TILE]
                return nn(kv[layer, head, 0:count, :], tile) + bias[TILE * TILES - count :, :]

            ahead = [scores_of(i) for i in (2 * chunk, 2 * chunk + 1)]
            for i in (2 * chunk, 2 * chunk + 1):
                columns = slice(TILE * i, TILE * i + TILE)
                count = TILE * (i + 1)
                scores = ahead[i - 2 * chunk]
                largest = jnp.max(scores, axis=0, keepdims=True)
                weight = jnp.exp(scores - largest)
                total = jnp.sum(weight, axis=0, keepdims=True)
                summed = nn(kv_t[layer, head, DIM:, 0:count], weight.astype(BF16))
                summed = summed / total
                o_t[layer, head, :, columns] = summed
                lse[layer, head, :, columns] = largest + jnp.log(total)
                rounded = summed.astype(BF16)
                for part in range(2):
                    head_out[chunk, 2 * (i - 2 * chunk) + part, head] = rounded[
                        :, HALF * part : HALF * part + HALF
                    ]
            return carry

        for head in range(OWN):
            one_head(head, 0)
        exchange(1, layer, chunk, head_out, o_in)

    def feed(layer, half):
        rows = rows_of(half)
        arrived(1, layer, half, o_in)
        for head in range(RUNS):
            attn_t[layer, DIM * head : DIM * head + DIM, rows] = o_in[half, slot_of(head // 2), head % 2]
        attn = attn_t[layer, :, rows].T
        grown = nn(attn, wout[layer])
        branch[layer, rows, :] = grown
        middle = hidden[rows, :] + alphas[layer, 0] * grown
        rounded = middle.astype(BF16)
        entered[layer, rows, :] = rounded
        total = jnp.zeros((HALF, WIDTH), F32)

        def gate_of(step):
            cut = slice(CUT * step, CUT * step + CUT)
            return nn(rounded, wup[layer, :, cut]) + up_bias[layer : layer + 1, cut]

        coming = gate_of(0)
        for step in range(FF // CUT):
            cut = slice(CUT * step, CUT * step + CUT)
            gate = coming
            if step + 1 < FF // CUT:
                coming = gate_of(step + 1)
            bell = jnp.exp(gate * gate * -0.5)
            near = pl.reciprocal(1.0 + SLOPE_AT * jnp.abs(gate), approx=True)
            tail = jnp.full_like(gate, TAIL[5])
            for factor in TAIL[4::-1]:
                tail = tail * near + factor
            tail = bell * (tail * near)
            risen = jnp.where(gate > 0.0, 1.0 - tail, tail)
            slope[layer, rows, cut] = risen + gate * bell * 0.3989422804014327
            active = (gate * risen).astype(BF16)
            act[layer, rows, cut] = active
            total = total + nn(active, wdown[layer, cut, :])
        total = total + down_bias[layer : layer + 1, :]
        second[layer, rows, :] = total
        hidden[rows, :] = middle + alphas[layer, 1] * total

    def total_of(values):
        return jnp.sum(jnp.sum(values, axis=0, keepdims=True), axis=1, keepdims=True)

    def feed_back(layer):
        start = grad[...]
        if layer == 0:
            dz[...] = (alphas[layer, 1] * start).astype(BF16)
        scaled = dz[...]
        alpha_second = total_of(start * second[layer])
        small[layer : layer + 1, FF : FF + WIDTH] = jnp.sum(scaled.astype(F32), axis=0, keepdims=True)
        middle = start
        coming = nt(scaled, wdown[layer, 0:CUT, :])
        for step in range(FF // CUT):
            cut = slice(CUT * step, CUT * step + CUT)
            raw = coming
            if step + 1 < FF // CUT:
                coming = nt(scaled, wdown[layer, CUT * (step + 1) : CUT * (step + 2), :])
            gate = (raw * slope[layer, :, cut]).astype(BF16)
            du[:, cut] = gate
            small[layer : layer + 1, cut] = jnp.sum(gate.astype(F32), axis=0, keepdims=True)
            middle = middle + nt(gate, wup[layer, :, cut])
        grad[...] = middle
        mixed = (alphas[layer, 0] * middle).astype(BF16)
        da[...] = mixed
        spread = nt(wout[layer], mixed).astype(BF16)
        for chunk in (1, 0):
            left(*((1, 1) if layer == 1 else (2, 1)), chunk, head_out)
            for head in range(RUNS):
                head_out[chunk, head // 2, head % 2] = spread[
                    DIM * head : DIM * head + DIM, HALF * chunk : HALF * chunk + HALF
                ]
            exchange(2, layer, chunk, head_out, do_in)
        alpha_first = total_of(middle * branch[layer])
        column = lax.broadcasted_iota(jnp.int32, (1, 128), 1)
        small[layer : layer + 1, FF + WIDTH :] = jnp.where(
            column == 0, alpha_first, jnp.where(column == 1, alpha_second, 0.0)
        )

    def attend_back(layer, chunk):
        arrived(2, layer, chunk, do_in)
        left(*((0, 1) if layer == 1 else (3, 1)), chunk, pack_out)

        def one_head(head, carry):
            for other in range(TEAM):
                start = HALF * (TEAM * chunk + other)
                ro[head, DIM:, start : start + HALF] = do_in[chunk, slot_of(other), head]
            for i in (2 * chunk, 2 * chunk + 1):
                columns = slice(TILE * i, TILE * i + TILE)
                query_tile = rq[layer, head, :, columns]
                grad_tile = ro[head, :, columns]
                log_total = lse[layer, head, :, columns]
                delta = jnp.sum(
                    ro[head, DIM:, columns].astype(F32) * o_t[layer, head, :, columns],
                    axis=0,
                    keepdims=True,
                )
                count = TILE * (i + 1)
                keys = kv[layer, head, 0:count, :]
                weight = jnp.exp(nn(keys, query_tile) + bias[TILE * TILES - count :, :] - log_total)
                scored = (weight * (nn(keys, grad_tile) - delta)).astype(BF16)
                term = nt(scored, query_tile) + nt(weight.astype(BF16), grad_tile)
                if chunk == 1 and i == 2:
                    acc[head, 0:count, :] = term
                elif chunk == 1:
                    acc[head, 0 : count - TILE, :] += term[0 : count - TILE, :]
                    acc[head, count - TILE : count, :] = term[count - TILE :, :]
                else:
                    acc[head, 0:count, :] += term
                query_grad = nn(kv_t[layer, head, 0:DIM, 0:count], scored)
                dq_t[head, :, columns] = query_grad * (DIM ** -0.5)
            for other in range(TEAM):
                start = HALF * (TEAM * chunk + other)
                span = slice(start, start + HALF)
                pack_out[chunk, other, head, 0:HALF, :] = acc[head, span, :].astype(BF16)
                pack_out[chunk, other, head, HALF:, :] = dq_t[head, :, span].astype(BF16)
            exchange(3, layer, chunk, pack_out, pack_in, head)
            return carry

        for head in range(OWN):
            one_head(head, 0)

    def project_back(layer, half):
        for head in range(OWN):
            arrived(3, layer, half, pack_in, head)
        turned = jnp.concatenate(
            [pack_in[half, slot_of(head // 2), head % 2, HALF:, :] for head in range(RUNS)], axis=0
        )
        dqkv[:, 0:WIDTH] = turned.T
        for head in range(RUNS):
            at = WIDTH + 128 * head
            dqkv[:, at : at + 128] = pack_in[half, slot_of(head // 2), head % 2, 0:HALF, :]
        rows = rows_of(half)
        grad[rows, :] = grad[rows, :] + nt(dqkv[...], wqkv[layer])

    def scatter_rows(layer, result, first_row):
        for run in range(RUNS):
            for quarter in range(4):
                parts[layer, quarter % 2, quarter // 2, run // 2, run % 2, first_row : first_row + DIM, :] = result[
                    DIM * run : DIM * run + DIM, 128 * quarter : 128 * quarter + 128
                ].astype(BF16)

    def make(part):
        layer, first, count = PARTS[part]
        if first < 256:
            turned = entered[layer].T
        for row in range(first, min(first + count, 256), DIM):
            step = row // DIM
            scatter_rows(layer, nn(turned, du[:, CUT * step : CUT * step + CUT]), row)
        if first <= 256 < first + count:
            scatter_rows(layer, nn(attn_t[layer], da[...]), 256)
        if first >= 320:
            turned = dz[...].T
            for step in range(FF // CUT):
                result = nn(turned, act[layer, :, CUT * step : CUT * step + CUT])
                for block in range(CUT // 128):
                    run, row = 2 * step + block // 2, 320 + 128 * (block % 2)
                    for quarter in range(4):
                        parts[layer, quarter % 2, quarter // 2, run // 2, run % 2, row : row + 128, :] = result[
                            128 * quarter : 128 * quarter + 128, 128 * block : 128 * block + 128
                        ].astype(BF16)
        if layer == 0:
            pl.semaphore_wait(core_free.at[0 if first < 320 else 1], 1)
        core_copy(part).start()

    def heads_grads(layer):
        for chunk in range(2):
            hidden_done(layer, chunk)
        blocks = [(run // TEAM, run % TEAM) for run in range(RUNS)]
        keys_values = jnp.concatenate(
            [
                jnp.concatenate([pack_out[chunk, other, head, 0:HALF, :] for chunk, other in blocks], axis=0)
                for head in range(OWN)
            ],
            axis=1,
        )
        queries = jnp.concatenate(
            [
                jnp.concatenate([pack_out[chunk, other, head, HALF:, :] for chunk, other in blocks], axis=1)
                for head in range(OWN)
            ],
            axis=0,
        )
        both = nn(hid_all[layer], keys_values)
        q_part = nt(hid_all[layer], queries)
        for number, values in enumerate((q_part, both[:, 0:128], both[:, 128:256])):
            for run in range(RUNS):
                heads_out[layer, run // 2, run % 2, :, 128 * number : 128 * number + 128] = values[
                    DIM * run : DIM * run + DIM, :
                ].astype(BF16)
        heads_x_copy(layer).start()

    def half_rows(which):
        return pl.ds(pl.multiple_of(32 * which, 32), 32)

    def heads_x_copy(layer):
        return remote(
            heads_out.at[layer, :, :, half_rows(1 - side)],
            heads_x.at[layer],
            hx_send.at[layer],
            hx_recv.at[layer],
            x_peer,
        )

    def heads_z_copy(layer, step):
        peer = lax.rem(zz + step, 4)
        return remote(
            heads_out.at[layer, peer, :, half_rows(side)],
            heads_z.at[layer, 4 - step],
            hz_send.at[layer, step],
            hz_recv.at[layer, 4 - step],
            place(core, side, peer, yy),
        )

    def heads_last_copy(layer, number):
        x, c, y = number // 4, number // 2 % 2, number % 2
        return remote(
            heads_sum.at[layer, 1 - yy if y else yy],
            heads_all.at[layer, side, member],
            hf_send.at[layer, number],
            hf_recv.at[layer, number],
            place(1 - core if c else core, 1 - side if x else side, zz, 1 - yy if y else yy),
        )

    def heads_second(layer):
        heads_x_copy(layer).wait()
        heads_out[layer, :, :, half_rows(side), :] += heads_x[layer]
        for step in range(1, 4):
            heads_z_copy(layer, step).start()

    def heads_third(layer):
        for step in range(1, 4):
            heads_z_copy(layer, step).wait()
        total = heads_out[layer, zz, :, half_rows(side), :].astype(F32)
        for slot in range(1, 4):
            total = total + heads_z[layer, slot].astype(F32)
        heads_sum[layer] = total.astype(BF16)
        heads_all[layer, side, member] = heads_sum[layer, yy]
        for number in range(1, 8):
            heads_last_copy(layer, number).start()

    def heads_done(layer):
        for number in range(1, 8):
            heads_last_copy(layer, number).wait()

    def rows_in(part, route):
        first, room, count = SPANS[part, route]
        return pl.ds(first, count), pl.ds(room, count)

    def used(part, route):
        return SHARES[part][route] > 0

    def core_copy(part):
        layer, first, count = PARTS[part]
        rows = pl.ds(first, count)
        return remote(
            parts.at[layer, 1 - core, :, :, :, rows],
            core_in.at[:, :, :, rows],
            core_send.at[part],
            core_recv.at[part],
            core_peer,
        )

    def x_copy(part, route):
        layer = PARTS[part][0]
        rows, room = rows_in(part, route)
        ends = (x_send.at[part, route], x_recv.at[part, route], x_peer)
        mine = parts.at[layer, core, 1 - side]
        if route == 0:
            return remote(mine.at[:, :, rows], xa_in.at[:, :, room], *ends)
        if route == 1:
            return remote(mine.at[:, yy, rows], xb_in.at[:, room], *ends)
        return remote(mine.at[zz, :, rows], third_x.at[:, room], *ends)

    def y_copy(part, route):
        layer = PARTS[part][0]
        rows, room = rows_in(part, route)
        ends = (y_send.at[part, route], y_recv.at[part, route], y_peer)
        mine = parts.at[layer, core]
        if route == 0:
            return remote(mine.at[side, :, 1 - yy, rows], ya_in.at[:, room], *ends)
        if route == 1:
            return remote(mine.at[:, :, 1 - yy, rows], yb_in.at[:, :, room], *ends)
        return remote(mine.at[side, zz, 1 - yy, rows], third_y.at[room], *ends)

    def z_copy(part, route, step):
        layer = PARTS[part][0]
        rows, room = rows_in(part, route)
        peer = lax.rem(zz + step, 4)
        ends = (z_send.at[part, route, step], z_recv.at[part, route, 4 - step], place(core, side, peer, yy))
        if route == 2:
            return remote(parts.at[layer, core, :, peer, :, rows], third_z.at[4 - step, :, :, room], *ends)
        return remote(parts.at[layer, core, side, peer, yy, rows], z_in.at[layer, 4 - step, rows], *ends)

    def final_copy(part, which):
        layer, first, count = PARTS[part]
        block = final.at[layer, far_side if which == 2 else grp, pl.ds(first, count)]
        return remote(
            block,
            block,
            fin_send.at[part, which],
            fin_recv.at[part, which],
            x_peer if which == 0 else core_peer,
        )

    def core_done(part):
        layer, first, count = PARTS[part]
        rows = pl.ds(first, count)
        core_copy(part).wait()
        for across in (1 - side, side):
            parts[layer, core, across, :, :, rows, :] += core_in[across, :, :, rows, :]
            if used(part, 0) and across is not side:
                x_copy(part, 0).start()
        if used(part, 1):
            y_copy(part, 1).start()
        if used(part, 2):
            for step in range(1, 4):
                z_copy(part, 2, step).start()
        if layer == 1:
            freed = 0 if first < 320 else 1
            followers = [1 for other in PARTS if other[0] == 0 and (other[1] >= 320) == (freed == 1)]
            credit(core_free.at[freed], core_peer, len(followers))

    def first_x(part):
        if used(part, 0):
            layer = PARTS[part][0]
            rows, room = rows_in(part, 0)
            x_copy(part, 0).wait()
            for y in (1 - yy, yy):
                parts[layer, core, side, :, y, rows, :] += xa_in[:, y, room, :]
                if y is not yy:
                    y_copy(part, 0).start()

    def first_y(part):
        if used(part, 1):
            layer = PARTS[part][0]
            rows, room = rows_in(part, 1)
            y_copy(part, 1).wait()
            for across in (1 - side, side):
                parts[layer, core, across, :, yy, rows, :] += yb_in[across, :, room, :]
                if across is not side:
                    x_copy(part, 1).start()

    def first_z(part):
        if used(part, 2):
            layer = PARTS[part][0]
            rows, room = rows_in(part, 2)
            for step in range(1, 4):
                z_copy(part, 2, step).wait()
            for across in (1 - side, side):
                total = parts[layer, core, across, zz, :, rows, :].astype(F32)
                for slot in range(1, 4):
                    total = total + third_z[slot, across, :, room, :].astype(F32)
                parts[layer, core, across, zz, :, rows, :] = total.astype(BF16)
                if across is not side:
                    x_copy(part, 2).start()

    def second_x(part):
        if used(part, 0):
            layer = PARTS[part][0]
            rows, room = rows_in(part, 0)
            y_copy(part, 0).wait()
            parts[layer, core, side, :, yy, rows, :] += ya_in[:, room, :]
            for step in range(1, 4):
                z_copy(part, 0, step).start()

    def second_y(part):
        if used(part, 1):
            layer = PARTS[part][0]
            rows, room = rows_in(part, 1)
            x_copy(part, 1).wait()
            parts[layer, core, side, :, yy, rows, :] += xb_in[:, room, :]
            for step in range(1, 4):
                z_copy(part, 1, step).start()

    def second_z(part):
        if used(part, 2):
            layer = PARTS[part][0]
            rows, room = rows_in(part, 2)
            x_copy(part, 2).wait()
            for y in (1 - yy, yy):
                parts[layer, core, side, zz, y, rows, :] += third_x[y, room, :]
                if y is not yy:
                    y_copy(part, 2).start()

    def third_done(part):
        layer = PARTS[part][0]
        for route in range(3):
            if not used(part, route):
                continue
            rows, room = rows_in(part, route)
            if route == 2:
                y_copy(part, 2).wait()
                final[layer, grp, rows, :] = parts[layer, core, side, zz, yy, rows, :] + third_y[room, :]
            else:
                for step in range(1, 4):
                    z_copy(part, route, step).wait()
                total = parts[layer, core, side, zz, yy, rows, :].astype(F32)
                for slot in range(1, 4):
                    total = total + z_in[layer, slot, rows, :].astype(F32)
                final[layer, grp, rows, :] = total.astype(BF16)
        if PARTS[part][1] >= 320:
            for row in (320, 448):
                final[layer, grp, row : row + 128, :] = final[layer, grp, row : row + 128, :].T
        for which in range(2):
            final_copy(part, which).start()

    def final_pass(part):
        final_copy(part, 0).wait()
        final_copy(part, 2).start()

    def final_done(part):
        for which in range(1, 3):
            final_copy(part, which).wait()

    def small_copy(stage):
        peer = (core_peer, x_peer, y_peer)[stage]
        return remote(
            small_sum.at[stage], small_in.at[stage], small_send.at[stage], small_recv.at[stage], peer
        )

    def small_z_copy(step):
        return remote(
            small_z.at[zz],
            small_z.at[zz],
            small_send.at[2 + step],
            small_recv.at[2 + step],
            place(core, side, lax.rem(zz + step, 4), yy),
        )

    def small_start():
        small_sum[0] = small[...]
        small_copy(0).start()

    def small_next(stage):
        small_copy(stage).wait()
        total = small_sum[stage] + small_in[stage]
        if stage < 2:
            small_sum[stage + 1] = total
            small_copy(stage + 1).start()
        else:
            small_z[zz] = total
            for step in range(1, 4):
                small_z_copy(step).start()

    def small_done():
        for step in range(1, 4):
            small_z_copy(step).wait()
        small_sum[0] = (small_z[0] + small_z[1]) + (small_z[2] + small_z[3])
        small_final[:, 0:256] = small_sum[0, :, pl.ds(pl.multiple_of(blk * 256, 256), 256)]
        pair = small_sum[0, :, pl.ds(pl.multiple_of(FF + 128 * zz, 128), 128)]
        small_final[:, 256:384] = jnp.where(yy == 1, pltpu.roll(pair, DIM, 1), pair)
        small_final[:, 384:512] = small_sum[0, :, FF + WIDTH :]

    def halves(*phases, first=0):
        def both(step, carry):
            for phase in phases:
                phase(lax.rem(step + first, 2))
            return carry

        lax.fori_loop(0, 2, both, 0)

    def begin(half):
        move_arrived(0, half, tok_in)
        hidden[rows_of(half), :] = tok_in[half].astype(F32)

    def finish(half):
        back_out[0, half] = hidden[rows_of(half), :].astype(BF16)
        to_owner(3, half, back_out.at[0, half], out_in)

    def turn_round(layer, half):
        move_arrived(2, half, cot_in)
        rows = rows_of(half)
        grad[rows, :] = cot_in[half].astype(F32)
        dz[rows, :] = (alphas[layer, 1] * grad[rows, :]).astype(BF16)

    def hand_back(half):
        back_out[1, half] = grad[rows_of(half), :].astype(BF16)
        to_owner(4, half, back_out.at[1, half], grad_in)

    barrier = pltpu.get_barrier_semaphore()
    for step in range(1, 4):
        credit(barrier, place(core, side, lax.rem(zz + step, 4), yy))
    for step in range(4):
        credit(barrier, place(1 - core, side, lax.rem(zz + step, 4), yy))
    for peer in (
        x_peer,
        y_peer,
        place(1 - core, side, zz, 1 - yy),
        place(1 - core, 1 - side, zz, yy),
        place(core, 1 - side, zz, 1 - yy),
        place(1 - core, 1 - side, zz, 1 - yy),
    ):
        credit(barrier, peer)

    weight_copies = {}
    for layer in range(LAYERS):
        for number, (source, target) in enumerate(
            ((qkv_hbm, wqkv), (out_hbm, wout), (up_hbm, wup), (down_hbm, wdown))
        ):
            weight_copies[layer, number] = pltpu.make_async_copy(
                source.at[layer], target.at[layer], w_sem.at[layer, number]
            )
    bias_copies = [
        pltpu.make_async_copy(up_bias_hbm, up_bias, w_sem.at[2, 0]),
        pltpu.make_async_copy(down_bias_hbm, down_bias, w_sem.at[2, 1]),
        pltpu.make_async_copy(alphas_hbm, alphas, w_sem.at[2, 2]),
    ]
    length_copy = pltpu.make_async_copy(seq_len_hbm, seq_len, w_sem.at[2, 3])
    length_copy.start()
    weight_copies[0, 0].start()
    pl.semaphore_wait(barrier, 13)
    upper = lax.div(zz, 2)
    for half in (1 - upper, upper):
        to_team(0, half, half_of(tokens, half), tok_in)
    for layer, number in ((1, 0), (0, 1), (0, 2), (0, 3), (1, 1), (1, 2), (1, 3)):
        weight_copies[layer, number].start(priority=1)
    for copy in bias_copies:
        copy.start(priority=1)
    length_copy.wait()
    end_second = lax.div(seq_len[0, 0] + seq_len[0, 1], RUNS)
    flag_out[...] = jnp.full((8, 128), end_second.astype(F32), F32)
    for half in (1 - upper, upper):
        to_team(1, half, flag_out, flag_in)
    for layer in range(LAYERS):
        for head in range(OWN):
            rq[layer, head, DIM:, :] = jnp.zeros((DIM, HALF * RUNS), BF16)
    for head in range(OWN):
        ro[head, 0:DIM, :] = jnp.zeros((DIM, HALF * RUNS), BF16)
    for layer in range(LAYERS):
        weight_copies[layer, 0].wait()
        pairs = [
            beside(
                wqkv[layer, :, WIDTH + 128 * pair : WIDTH + 128 * pair + 128].astype(F32),
                wqkv[layer, :, 2 * WIDTH + 128 * pair : 2 * WIDTH + 128 * pair + 128].astype(F32),
            )
            for pair in range(TEAM)
        ]
        for head in range(RUNS):
            at = WIDTH + 128 * head
            wqkv[layer, :, at : at + 128] = pairs[head // 2][head % 2].astype(BF16)
    halves(begin, functools.partial(project, 0), first=upper)
    for half in (1 - upper, upper):
        to_team(2, half, half_of(cotangent, half), cot_in)

    move_arrived(1, 0, flag_in)
    move_arrived(1, 1, flag_in)
    border = jnp.concatenate([flag_in[0, 0:1, :]] * 2, axis=1) - (HALF * lax.div(zz, 2)).astype(F32)
    key_row = lax.broadcasted_iota(jnp.int32, (TILE, TILE), 0)
    query_col = lax.broadcasted_iota(jnp.int32, (TILE, TILE), 1)
    later = key_row > query_col
    key_sub = lax.rem(key_row, HALF).astype(F32) >= border
    query_sub = lax.rem(query_col, HALF).astype(F32) >= border
    apart = jnp.logical_xor(key_sub, query_sub)
    for tile in range(TILES - 1):
        bias[TILE * tile : TILE * tile + TILE, :] = jnp.where(apart, NEGATIVE, 0.0)
    bias[TILE * (TILES - 1) :, :] = jnp.where(jnp.logical_or(later, apart), NEGATIVE, 0.0)

    for copy in (*bias_copies, *(weight_copies[0, number] for number in range(1, 4))):
        copy.wait()
    attend(0, 0)
    attend(0, 1)
    hidden_start(0, 0)
    halves(functools.partial(feed, 0), functools.partial(project, 1))
    for number in range(1, 4):
        weight_copies[1, number].wait()
    attend(1, 0)
    attend(1, 1)
    hidden_pass(0, 0)
    hidden_start(1, 0)
    halves(functools.partial(feed, 1), finish)
    hidden_start(0, 1)
    hidden_start(1, 1)
    hidden_pass(1, 0)

    halves(functools.partial(turn_round, 1))
    make(1)
    feed_back(1)
    hidden_pass(0, 1)
    hidden_pass(1, 1)
    core_done(1)
    make(0)
    attend_back(1, 1)
    first_y(1)
    core_done(0)
    attend_back(1, 0)
    second_y(1)
    first_x(1)
    project_back(1, 1)
    heads_grads(1)
    first_z(1)
    project_back(1, 0)
    feed_back(0)
    small_start()
    second_x(1)
    make(2)
    first_x(0)
    heads_second(1)
    first_z(0)
    attend_back(0, 1)
    small_next(0)
    core_done(2)
    second_x(0)
    make(3)
    attend_back(0, 0)
    small_next(1)
    project_back(0, 1)
    hand_back(1)
    first_z(2)
    heads_grads(0)
    small_next(2)
    first_x(2)
    core_done(3)
    first_y(2)
    heads_second(0)
    small_done()
    first_z(3)
    second_x(2)
    first_x(3)
    second_z(2)
    second_z(0)
    heads_third(1)
    second_z(1)
    first_y(3)
    heads_third(0)
    second_y(2)
    second_x(3)
    second_z(3)
    third_done(0)
    third_done(2)
    second_y(3)
    project_back(0, 0)
    hand_back(0)
    heads_done(1)
    third_done(1)
    third_done(3)
    final_pass(0)
    final_pass(2)
    final_pass(1)
    final_pass(3)
    final_done(2)
    final_done(1)
    heads_done(0)
    final_done(0)
    final_done(3)
    for half in range(2):
        move_arrived(3, half, out_in)
        move_arrived(4, half, grad_in)

    for half in range(2):
        left(2, 0, half, head_out)
        left(3, 0, half, pack_out)
        to_team_left(0, half, half_of(tokens, half))
        to_team_left(1, half, flag_out)
        to_team_left(2, half, half_of(cotangent, half))
        to_owner_left(3, half, back_out.at[0, half])
        to_owner_left(4, half, back_out.at[1, half])


def results_kernel(
    final, heads, out_block, grad_block, small,
    output, input_grad, qkv_grad, out_grad, up_grad, up_bias_grad, down_grad, down_bias_grad, alpha_grad,
    grad_wide, qkv_wide, out_wide, up_wide, down_wide, up_bias, down_bias, alpha, out_sem,
):
    ends = []

    def write(source, target):
        ends.append(pltpu.make_async_copy(source, target, out_sem.at[len(ends)]))
        ends[-1].start()

    for half in range(2):
        write(out_block.at[half], output.at[pl.ds(HALF * half, HALF)])
    up_bias[...] = small[:, 0:256]
    write(up_bias, up_bias_grad)
    down_bias[...] = small[:, 256 : 256 + DIM]
    write(down_bias, down_bias_grad)
    alpha[...] = small[:, 384:386]
    write(alpha, alpha_grad)
    for layer in range(LAYERS):
        for quarter in range(4):

            def block(first, count):
                return final[layer, quarter, first : first + count, :].astype(F32)

            def columns(step):
                return slice(WIDTH * step + 128 * quarter, WIDTH * step + 128 * quarter + 128)

            for step in range(4):
                up_wide[layer, :, columns(step)] = block(DIM * step, DIM)
            out_wide[layer, :, columns(0)] = block(256, DIM)
            down_wide[layer, :, columns(0)] = block(320, 256)
        write(up_wide.at[layer], up_grad.at[layer])
        write(out_wide.at[layer], out_grad.at[layer])
        write(down_wide.at[layer], down_grad.at[layer])
    for half in range(2):
        rows = slice(HALF * half, HALF * half + HALF)
        grad_wide[rows, :] = grad_block[half].astype(F32)
    write(grad_wide, input_grad)
    for layer in range(LAYERS):
        for side in range(2):
            for member in range(TEAM):
                block = heads[layer, side, member].astype(F32)
                columns = (block[:, 0:128], *beside(block[:, 128:256], block[:, 256:384]))
                for step in range(3):
                    at = WIDTH * step + 128 * member
                    qkv_wide[layer, 32 * side : 32 * side + 32, at : at + 128] = columns[step]
        write(qkv_wide.at[layer], qkv_grad.at[layer])
    for end in ends:
        end.wait()


def fast_body(
    tokens, seq_len, qkv_weight, out_weight, up_weight, up_bias, down_weight, down_bias, alphas, cotangent
):
    whole = pl.BlockSpec(memory_space=pltpu.VMEM)
    far = pl.BlockSpec(memory_space=pl.ANY)
    shape = jax.ShapeDtypeStruct
    rows = HALF * RUNS

    def vmem(*dims):
        return pltpu.VMEM(dims, BF16)

    def wide(*dims):
        return pltpu.VMEM(dims, F32)

    dma = pltpu.SemaphoreType.DMA
    final, heads, out_block, grad_block, small = pl.pallas_call(
        layers_kernel,
        out_shape=(
            vmem(LAYERS, 4, CHUNK, 128),
            vmem(LAYERS, 2, TEAM, DIM // 2, 3 * 128),
            vmem(2, HALF, WIDTH),
            vmem(2, HALF, WIDTH),
            wide(LAYERS, WIDTH),
        ),
        in_specs=[far, far, far, far, far, far, far, far, far, far],
        out_specs=(whole,) * 5,
        scratch_shapes=[
            pltpu.SMEM((1, 4), jnp.int32),
            pltpu.SMEM((LAYERS, 2), F32),
            vmem(LAYERS, WIDTH, 3 * WIDTH),
            vmem(LAYERS, WIDTH, WIDTH),
            vmem(LAYERS, WIDTH, FF),
            vmem(LAYERS, FF, WIDTH),
            wide(LAYERS, FF),
            wide(LAYERS, WIDTH),
            vmem(2, HALF, WIDTH),
            vmem(2, HALF, WIDTH),
            wide(8, 128),
            wide(2, 8, 128),
            vmem(2, 2, HALF, WIDTH),
            wide(2 * HALF, WIDTH),
            wide(2 * HALF, WIDTH),
            vmem(LAYERS, WIDTH, rows),
            vmem(LAYERS, WIDTH, 2 * HALF),
            vmem(LAYERS, 2 * HALF, WIDTH),
            vmem(LAYERS, 2 * HALF, FF),
            wide(LAYERS, 2 * HALF, WIDTH),
            wide(LAYERS, 2 * HALF, FF),
            wide(LAYERS, 2 * HALF, WIDTH),
            vmem(2 * HALF, WIDTH),
            vmem(2 * HALF, FF),
            vmem(2 * HALF, WIDTH),
            vmem(HALF, 3 * WIDTH),
            vmem(2, TEAM, OWN, PACK, 128),
            vmem(2, TEAM, OWN, DIM, 128),
            vmem(2, TEAM, OWN, PACK, 128),
            vmem(2, TEAM, OWN, DIM, 128),
            vmem(2, TEAM, OWN, DIM, 128),
            vmem(LAYERS, OWN, rows, 128),
            vmem(LAYERS, OWN, 128, rows),
            vmem(LAYERS, OWN, 128, rows),
            vmem(OWN, 128, rows),
            wide(LAYERS, OWN, DIM, rows),
            wide(LAYERS, OWN, 1, rows),
            wide(OWN, rows, 128),
            wide(OWN, DIM, rows),
            wide(rows, TILE),
            vmem(LAYERS, 2, 2, 4, 2, CHUNK, 128),
            vmem(2, 4, 2, CHUNK, 128),
            vmem(4, 2, TOTALS[0], 128),
            vmem(4, TOTALS[1], 128),
            vmem(4, TOTALS[0], 128),
            vmem(2, 4, TOTALS[1], 128),
            vmem(LAYERS, 4, CHUNK, 128),
            vmem(4, 2, 2, TOTALS[2], 128),
            vmem(2, TOTALS[2], 128),
            vmem(TOTALS[2], 128),
            vmem(LAYERS, 4, 2, DIM, 3 * 128),
            vmem(LAYERS, 4, 2, DIM // 2, 3 * 128),
            vmem(LAYERS, 4, 2, DIM // 2, 3 * 128),
            vmem(LAYERS, 2, DIM // 2, 3 * 128),
            wide(LAYERS, SMALL),
            wide(3, LAYERS, SMALL),
            wide(4, LAYERS, SMALL),
            wide(3, LAYERS, SMALL),
            dma((LAYERS + 1, 4)),
            dma((5, 2)),
            dma((5, 2)),
            dma((4, LAYERS, 2, OWN)),
            dma((4, LAYERS, 2, OWN)),
            dma((len(PARTS),)),
            dma((len(PARTS),)),
            dma((len(PARTS), 3)),
            dma((len(PARTS), 3)),
            dma((len(PARTS), 3)),
            dma((len(PARTS), 3)),
            dma((len(PARTS), 3, 4)),
            dma((len(PARTS), 3, 4)),
            dma((len(PARTS), 3)),
            dma((len(PARTS), 3)),
            dma((LAYERS, 2, 3)),
            dma((LAYERS, 2, 3)),
            dma((LAYERS,)),
            dma((LAYERS,)),
            dma((LAYERS, 4)),
            dma((LAYERS, 4)),
            dma((LAYERS, 8)),
            dma((LAYERS, 8)),
            dma((6,)),
            dma((6,)),
            pltpu.SemaphoreType.REGULAR((2,)),
        ],
        compiler_params=pltpu.CompilerParams(
            collective_id=0, has_side_effects=True, vmem_limit_bytes=61 * 1024 * 1024
        ),
        name="layers",
    )(
        tokens, seq_len, alphas, up_bias, down_bias, cotangent,
        qkv_weight, out_weight, up_weight, down_weight,
    )
    return tuple(
        pl.pallas_call(
            results_kernel,
            out_shape=(
                shape((2 * HALF, WIDTH), BF16),
                shape((2 * HALF, WIDTH), F32),
                shape((LAYERS, DIM, 3 * WIDTH), F32),
                shape((LAYERS, DIM, WIDTH), F32),
                shape((LAYERS, DIM, FF), F32),
                shape((LAYERS, FF // RUNS), F32),
                shape((LAYERS, FF // RUNS, WIDTH), F32),
                shape((LAYERS, DIM), F32),
                shape((LAYERS, 2), F32),
            ),
            in_specs=[whole] * 5,
            out_specs=(far,) * 9,
            scratch_shapes=[
                wide(2 * HALF, WIDTH),
                wide(LAYERS, DIM, 3 * WIDTH),
                wide(LAYERS, DIM, WIDTH),
                wide(LAYERS, DIM, FF),
                wide(LAYERS, FF // RUNS, WIDTH),
                wide(LAYERS, FF // RUNS),
                wide(LAYERS, DIM),
                wide(LAYERS, 2),
                dma((14,)),
            ],
            compiler_params=pltpu.CompilerParams(vmem_limit_bytes=24 * 1024 * 1024),
            name="results",
        )(final, heads, out_block, grad_block, small)
    )


def layout(seq_len, local_count, cycle_size):
    piece_rows = seq_len[0] // cycle_size
    end_rows = jnp.cumsum(piece_rows)
    start_rows = end_rows - piece_rows
    local_rows = jnp.arange(local_count, dtype=jnp.int32)
    segment = jnp.sum((local_rows[:, None] >= end_rows[None, :]).astype(jnp.int32), axis=1)
    picked = segment[:, None] == jnp.arange(seq_len.shape[1], dtype=jnp.int32)[None, :]
    offset = local_rows - jnp.sum(jnp.where(picked, start_rows[None, :], 0), axis=1)
    span_rows = jnp.sum(jnp.where(picked, piece_rows[None, :], 0), axis=1)
    return (segment, offset, span_rows)


def gelu_exact(values):
    return jax.nn.gelu(values, approximate=False)


def key_block(whole, geometry, block_index, head_count):
    query_seg, query_pos, seg_all, pos_all, block_rows, score_scale = geometry
    first_row = block_index * block_rows
    key_piece = lax.dynamic_slice_in_dim(whole, first_row, block_rows, 0)
    key_seg = lax.dynamic_slice_in_dim(seg_all, first_row, block_rows, 0)
    key_pos = lax.dynamic_slice_in_dim(pos_all, first_row, block_rows, 0)
    half_width = key_piece.shape[1] // 2
    keys_part = key_piece[:, :half_width].reshape(block_rows, head_count, -1)
    values_part = key_piece[:, half_width:].reshape(block_rows, head_count, -1)
    return (keys_part, values_part, key_seg, key_pos)


def block_scores(queries, keys_part, key_seg, key_pos, geometry):
    query_seg, query_pos, seg_all, pos_all, block_rows, score_scale = geometry
    scores = (
        jnp.einsum("qhd,khd->hqk", queries, keys_part, preferred_element_type=jnp.float32)
        * score_scale
    )
    allowed = (query_seg[:, None] == key_seg[None, :]) & (key_pos[None, :] <= query_pos[:, None])
    return (scores, allowed[None])


def attend(queries, whole, geometry):
    row_count, head_count, head_dim = queries.shape
    block_count = whole.shape[0] // geometry[4]

    def statistics(running, block_index):
        largest, totals = running
        keys_part, values_part, key_seg, key_pos = key_block(
            whole, geometry, block_index, head_count
        )
        scores, allowed = block_scores(queries, keys_part, key_seg, key_pos, geometry)
        newest = jnp.maximum(largest, jnp.max(jnp.where(allowed, scores, NEGATIVE), axis=2))
        weights = jnp.where(allowed, jnp.exp(scores - newest[:, :, None]), 0.0)
        totals = totals * jnp.exp(largest - newest) + jnp.sum(weights, axis=2)
        return ((newest, totals), None)

    initial = (
        jnp.full((head_count, row_count), NEGATIVE, jnp.float32),
        jnp.zeros((head_count, row_count), jnp.float32),
    )
    (largest, totals), unused = lax.scan(statistics, initial, jnp.arange(block_count))
    log_total = largest + jnp.log(totals)

    def weighted(output_sum, block_index):
        keys_part, values_part, key_seg, key_pos = key_block(
            whole, geometry, block_index, head_count
        )
        scores, allowed = block_scores(queries, keys_part, key_seg, key_pos, geometry)
        probs = jnp.where(allowed, jnp.exp(scores - log_total[:, :, None]), 0.0).astype(
            jnp.bfloat16
        )
        output_sum = output_sum + jnp.einsum(
            "hqk,khd->qhd", probs, values_part, preferred_element_type=jnp.float32
        )
        return (output_sum, None)

    output_sum, unused = lax.scan(
        weighted, jnp.zeros((row_count, head_count, head_dim), jnp.float32), jnp.arange(block_count)
    )
    return (output_sum, log_total)


def attend_back(queries, whole, log_total, delta_sum, grad_heads, geometry):
    row_count, head_count, head_dim = queries.shape
    block_rows = geometry[4]
    score_scale = geometry[5]
    block_count = whole.shape[0] // block_rows

    def gradients(query_grad, block_index):
        keys_part, values_part, key_seg, key_pos = key_block(
            whole, geometry, block_index, head_count
        )
        scores, allowed = block_scores(queries, keys_part, key_seg, key_pos, geometry)
        probs = jnp.where(allowed, jnp.exp(scores - log_total[:, :, None]), 0.0)
        grad_probs = jnp.einsum(
            "qhd,khd->hqk", grad_heads, values_part, preferred_element_type=jnp.float32
        )
        grad_scores = (probs * (grad_probs - delta_sum[:, :, None])).astype(jnp.bfloat16)
        query_grad = (
            query_grad
            + jnp.einsum("hqk,khd->qhd", grad_scores, keys_part, preferred_element_type=jnp.float32)
            * score_scale
        )
        key_grad = (
            jnp.einsum("hqk,qhd->khd", grad_scores, queries, preferred_element_type=jnp.float32)
            * score_scale
        )
        value_grad = jnp.einsum(
            "hqk,qhd->khd",
            probs.astype(jnp.bfloat16),
            grad_heads,
            preferred_element_type=jnp.float32,
        )
        joined = jnp.concatenate(
            [key_grad.reshape(block_rows, -1), value_grad.reshape(block_rows, -1)], axis=1
        )
        return (query_grad, joined)

    query_grad, stacked = lax.scan(
        gradients,
        jnp.zeros((row_count, head_count, head_dim), jnp.float32),
        jnp.arange(block_count),
    )
    return (query_grad, stacked.reshape(whole.shape[0], -1))


def layer_forward(hidden, layer_index, weights, geometry):
    qkv_weight, out_weight, up_weight, up_bias, down_weight, down_bias, alphas = weights
    row_count, model_width = hidden.shape
    projection = qkv_weight[layer_index]
    rounded = hidden.astype(jnp.bfloat16)
    queries = (
        jnp.dot(rounded, projection[:, :model_width], preferred_element_type=jnp.float32)
        .astype(jnp.bfloat16)
        .reshape(row_count, HEADS, -1)
    )
    key_value = jnp.dot(
        rounded, projection[:, model_width:], preferred_element_type=jnp.float32
    ).astype(jnp.bfloat16)
    whole = lax.all_gather(key_value, "blk", axis=0, tiled=True)
    heads_out, log_total = attend(queries, whole, geometry)
    heads_rounded = heads_out.reshape(row_count, model_width).astype(jnp.bfloat16)
    branch = jnp.dot(heads_rounded, out_weight[layer_index], preferred_element_type=jnp.float32)
    alpha_pair = alphas[layer_index]
    middle = hidden + alpha_pair[0] * branch
    entered = middle.astype(jnp.bfloat16)
    gate_pre = (
        jnp.dot(entered, up_weight[layer_index], preferred_element_type=jnp.float32)
        + up_bias[layer_index]
    )
    activated = gelu_exact(gate_pre).astype(jnp.bfloat16)
    second = (
        jnp.dot(activated, down_weight[layer_index], preferred_element_type=jnp.float32)
        + down_bias[layer_index]
    )
    result = middle + alpha_pair[1] * second
    saved = (
        rounded,
        queries,
        key_value,
        whole,
        heads_out,
        heads_rounded,
        log_total,
        branch,
        entered,
        gate_pre,
        activated,
        second,
    )
    return (result, saved)


def layer_backward(grad_hidden, saved, layer_index, weights, geometry):
    qkv_weight, out_weight, up_weight, up_bias, down_weight, down_bias, alphas = weights
    (
        rounded,
        queries,
        key_value,
        saved_whole,
        heads_out,
        heads_rounded,
        log_total,
        branch,
        entered,
        gate_pre,
        activated,
        second,
    ) = saved
    row_count = grad_hidden.shape[0]
    alpha_pair = alphas[layer_index]
    grad_second = (alpha_pair[1] * grad_hidden).astype(jnp.bfloat16)
    alpha_second = jnp.sum(grad_hidden * second)
    bias_down = jnp.sum(grad_second.astype(jnp.float32), axis=0)
    grad_down = jnp.einsum("tf,td->fd", activated, grad_second, preferred_element_type=jnp.float32)
    grad_act = jnp.einsum(
        "td,fd->tf", grad_second, down_weight[layer_index], preferred_element_type=jnp.float32
    )
    unused, gelu_pull = jax.vjp(gelu_exact, gate_pre)
    grad_gate = gelu_pull(grad_act)[0].astype(jnp.bfloat16)
    bias_up = jnp.sum(grad_gate.astype(jnp.float32), axis=0)
    grad_up = jnp.einsum("td,tf->df", entered, grad_gate, preferred_element_type=jnp.float32)
    grad_middle = grad_hidden + jnp.einsum(
        "tf,df->td", grad_gate, up_weight[layer_index], preferred_element_type=jnp.float32
    )
    grad_branch = (alpha_pair[0] * grad_middle).astype(jnp.bfloat16)
    alpha_first = jnp.sum(grad_middle * branch)
    grad_proj_out = jnp.einsum(
        "te,td->ed", heads_rounded, grad_branch, preferred_element_type=jnp.float32
    )
    grad_heads = (
        jnp.einsum(
            "td,ed->te", grad_branch, out_weight[layer_index], preferred_element_type=jnp.float32
        )
        .astype(jnp.bfloat16)
        .reshape(queries.shape)
    )
    delta_sum = jnp.sum(grad_heads.astype(jnp.float32) * heads_out, axis=2).T
    whole = lax.all_gather(key_value, "blk", axis=0, tiled=True)
    query_grad, key_terms = attend_back(queries, whole, log_total, delta_sum, grad_heads, geometry)
    key_grads = lax.psum_scatter(
        key_terms.astype(jnp.bfloat16), "blk", scatter_dimension=0, tiled=True
    )
    grad_proj = jnp.concatenate(
        [query_grad.reshape(row_count, -1).astype(jnp.bfloat16), key_grads], axis=1
    )
    grad_qkv = jnp.einsum("td,te->de", rounded, grad_proj, preferred_element_type=jnp.float32)
    grad_input = grad_middle + jnp.einsum(
        "te,de->td", grad_proj, qkv_weight[layer_index], preferred_element_type=jnp.float32
    )
    layer_grads = (
        grad_qkv,
        grad_proj_out,
        grad_up,
        bias_up,
        grad_down,
        bias_down,
        jnp.stack([alpha_first, alpha_second]),
    )
    return (grad_input, layer_grads)


def reduce_all(layer_results, cycle_size):
    stacked = [
        jnp.stack([layer_entry[member] for layer_entry in layer_results], axis=0)
        for member in range(6)
    ]
    alpha_tiles = jnp.stack(
        [jnp.tile(layer_entry[6], cycle_size) for layer_entry in layer_results], axis=0
    )
    shares = (
        lax.psum_scatter(
            stacked[0].astype(jnp.bfloat16), "blk", scatter_dimension=1, tiled=True
        ).astype(jnp.float32),
        lax.psum_scatter(
            stacked[1].astype(jnp.bfloat16), "blk", scatter_dimension=1, tiled=True
        ).astype(jnp.float32),
        lax.psum_scatter(
            stacked[2].astype(jnp.bfloat16), "blk", scatter_dimension=1, tiled=True
        ).astype(jnp.float32),
        lax.psum_scatter(
            stacked[3].astype(jnp.bfloat16), "blk", scatter_dimension=1, tiled=True
        ).astype(jnp.float32),
        lax.psum_scatter(
            stacked[4].astype(jnp.bfloat16), "blk", scatter_dimension=1, tiled=True
        ).astype(jnp.float32),
        lax.psum_scatter(
            stacked[5].astype(jnp.bfloat16), "blk", scatter_dimension=1, tiled=True
        ).astype(jnp.float32),
        lax.psum_scatter(
            alpha_tiles.astype(jnp.bfloat16), "blk", scatter_dimension=1, tiled=True
        ).astype(jnp.float32),
    )
    return (
        lax.psum(shares[0].astype(jnp.bfloat16), "grp").astype(jnp.float32),
        lax.psum(shares[1].astype(jnp.bfloat16), "grp").astype(jnp.float32),
        lax.psum(shares[2].astype(jnp.bfloat16), "grp").astype(jnp.float32),
        lax.psum(shares[3].astype(jnp.bfloat16), "grp").astype(jnp.float32),
        lax.psum(shares[4].astype(jnp.bfloat16), "grp").astype(jnp.float32),
        lax.psum(shares[5].astype(jnp.bfloat16), "grp").astype(jnp.float32),
        lax.psum(shares[6].astype(jnp.bfloat16), "grp").astype(jnp.float32),
    )


def body(
    tokens,
    seq_len,
    qkv_weight,
    out_weight,
    up_weight,
    up_bias,
    down_weight,
    down_bias,
    alphas,
    cotangent,
):
    row_count, model_width = tokens.shape
    cycle_size = lax.axis_size("blk")
    cycle_place = lax.axis_index("blk")
    head_dim = model_width // HEADS
    total_rows = cycle_size * row_count
    block_rows = min(max(row_count, 512), total_rows)
    segment, offset, span_rows = layout(seq_len, row_count, cycle_size)
    query_pos = cycle_place * span_rows + offset
    seg_all = jnp.tile(segment, cycle_size)
    pos_all = jnp.repeat(jnp.arange(cycle_size, dtype=jnp.int32), row_count) * jnp.tile(
        span_rows, cycle_size
    ) + jnp.tile(offset, cycle_size)
    geometry = (segment, query_pos, seg_all, pos_all, block_rows, head_dim ** (-0.5))
    weights = (qkv_weight, out_weight, up_weight, up_bias, down_weight, down_bias, alphas)
    hidden = tokens.astype(jnp.float32)
    saved_layers = []
    for layer_index in range(LAYERS):
        hidden, saved = layer_forward(hidden, layer_index, weights, geometry)
        saved_layers.append(saved)
    output = hidden.astype(jnp.bfloat16)
    grad_hidden = cotangent.astype(jnp.float32)
    layer_results = []
    for layer_index in reversed(range(LAYERS)):
        grad_hidden, layer_grads = layer_backward(
            grad_hidden, saved_layers[layer_index], layer_index, weights, geometry
        )
        layer_results.insert(0, layer_grads)
    finals = reduce_all(layer_results, cycle_size)
    return (
        output,
        grad_hidden,
        finals[0],
        finals[1],
        finals[2],
        finals[3],
        finals[4],
        finals[5],
        finals[6],
    )


def solution(mesh):
    placed = (
        P(("grp", "blk"), None),
        P("grp", None),
        P(),
        P(),
        P(),
        P(),
        P(),
        P(),
        P(),
        P(("grp", "blk"), None),
    )
    sizes = (mesh.shape["grp"], mesh.shape["blk"])
    return jax.shard_map(
        fast_body if sizes == (4, RUNS) else body,
        mesh=mesh,
        in_specs=placed,
        out_specs=(
            P(("grp", "blk"), None),
            P(("grp", "blk"), None),
            P(None, "blk", None),
            P(None, "blk", None),
            P(None, "blk", None),
            P(None, "blk"),
            P(None, "blk", None),
            P(None, "blk"),
            P(),
        ),
        check_vma=False,
    )
```

```python
import functools

import jax
import jax.numpy as jnp
from jax import lax
from jax.experimental import pallas as pl
from jax.experimental.pallas import tpu as pltpu
from jax.sharding import PartitionSpec as P

HEADS = 8
LAYERS = 2
NEGATIVE = -1e30
MESH = pl.DeviceIdType.MESH
F32 = jnp.float32
BF16 = jnp.bfloat16

HALF = 128
RUNS = 8
TEAM = 4
OWN = RUNS // TEAM
DIM = 64
WIDTH = 512
FF = 2048
CUT = 512
TILE = 256
TILES = HALF * RUNS // TILE
PACK = HALF + DIM
CHUNK = 576
SMALL = FF + WIDTH + 128
PARTS = ((1, 0, 320), (1, 320, 256), (0, 0, 320), (0, 320, 256))
SHARES = ((192, 0, 128), (160, 16, 80), (160, 128, 32), (128, 96, 32))


def spans():
    places, totals = {}, [0, 0, 0]
    for part, counts in enumerate(SHARES):
        first = PARTS[part][1]
        for route, count in enumerate(counts):
            places[part, route] = (first, totals[route], count)
            first += count
            totals[route] += count
    return places, totals


SPANS, TOTALS = spans()

SLOPE_AT = 0.28
TAIL = (
    0.11652077851573843,
    0.06749675579450809,
    0.2689101589486142,
    -0.23699347299932225,
    0.3898740127620002,
    -0.10580824228351815,
)


def nn(a, b):
    return lax.dot_general(a, b, (((1,), (0,)), ((), ())), preferred_element_type=F32)


def nt(a, b):
    return lax.dot_general(a, b, (((1,), (1,)), ((), ())), preferred_element_type=F32)


def beside(first, other):
    low = lax.broadcasted_iota(jnp.int32, first.shape, 1) < DIM
    return (
        jnp.where(low, first, pltpu.roll(other, DIM, 1)),
        jnp.where(low, pltpu.roll(first, DIM, 1), other),
    )


def layers_kernel(
    tokens, seq_len_hbm, alphas_hbm, up_bias_hbm, down_bias_hbm, cotangent, qkv_hbm, out_hbm, up_hbm, down_hbm,
    final, heads_all, out_in, grad_in, small_final,
    seq_len, alphas, wqkv, wout, wup, wdown, up_bias, down_bias,
    tok_in, cot_in, flag_out, flag_in, back_out,
    hidden, grad, hid_all, attn_t, entered, act, branch, slope, second,
    dz, du, da, dqkv,
    pack_out, head_out, pack_in, o_in, do_in,
    kv, kv_t, rq, ro, o_t, probs, acc, dq_t, bias,
    parts, core_in, xa_in, xb_in, ya_in, yb_in, z_in, third_z, third_x, third_y,
    heads_out, heads_x, heads_z, heads_sum, small, small_in, small_z, small_sum,
    w_sem, move_send, move_recv, a2a_send, a2a_recv, core_send, core_recv, x_send, x_recv, y_send, y_recv,
    z_send, z_recv, fin_send, fin_recv, hid_send, hid_recv, hx_send, hx_recv, hz_send, hz_recv, hf_send, hf_recv,
    small_send, small_recv, core_free,
):
    grp = lax.axis_index("grp")
    blk = lax.axis_index("blk")
    core = lax.rem(grp, 2)
    side = lax.div(grp, 2)
    yy = lax.rem(blk, 2)
    zz = lax.div(blk, 2)
    member = 2 * core + yy
    far_side = 2 * (1 - side) + core

    def place(c, x, z, y):
        return (2 * x + c, 2 * z + y)

    core_peer = place(1 - core, side, zz, yy)
    x_peer = place(core, 1 - side, zz, yy)
    y_peer = place(core, side, zz, 1 - yy)

    def remote(source, target, send, recv, peer):
        return pltpu.make_async_remote_copy(
            src_ref=source,
            dst_ref=target,
            send_sem=send,
            recv_sem=recv,
            device_id=peer,
            device_id_type=MESH,
        )

    def credit(semaphore, peer, count=1):
        pl.semaphore_signal(semaphore, inc=count, device_id=peer, device_id_type=MESH)

    def moved(kind, slot, source, target, at, core_at, z_at):
        here = jnp.logical_and(core_at == core, z_at == zz)

        @pl.when(here)
        def _():
            pltpu.make_async_copy(source, target.at[at], move_recv.at[kind, at]).start()

        @pl.when(jnp.logical_not(here))
        def _():
            pltpu.make_async_remote_copy(
                src_ref=source,
                dst_ref=target.at[at],
                send_sem=move_send.at[kind, slot],
                recv_sem=move_recv.at[kind, at],
                device_id=place(core_at, side, z_at, yy),
                device_id_type=MESH,
            ).start()

    def move_left(kind, slot, source, core_at, z_at):
        here = jnp.logical_and(core_at == core, z_at == zz)

        @pl.when(jnp.logical_not(here))
        def _():
            pltpu.make_async_copy(source, source, move_send.at[kind, slot]).wait()

    def move_arrived(kind, at, target):
        pltpu.make_async_copy(target.at[at], target.at[at], move_recv.at[kind, at]).wait()

    def to_team(kind, half, source, target):
        moved(kind, half, source, target, lax.div(zz, 2), lax.rem(zz, 2), 2 * half + core)

    def to_team_left(kind, half, source):
        move_left(kind, half, source, lax.rem(zz, 2), 2 * half + core)

    def to_owner(kind, chunk, source, target):
        moved(kind, chunk, source, target, lax.div(zz, 2), lax.rem(zz, 2), core + 2 * chunk)

    def to_owner_left(kind, chunk, source):
        move_left(kind, chunk, source, lax.rem(zz, 2), core + 2 * chunk)

    def half_of(ref, half):
        return ref.at[pl.ds(pl.multiple_of(HALF * half, HALF), HALF)]

    def rows_of(half):
        return pl.ds(pl.multiple_of(half * HALF, HALF), HALF)

    def slot_of(other):
        return lax.rem(other + TEAM - member, TEAM)

    def exchange(kind, layer, half, outgoing, incoming, head=None):
        at = () if head is None else (head,)
        incoming[(half, 0, *at)] = outgoing[(half, member, *at)]
        for step in range(1, TEAM):
            peer = lax.rem(member + step, TEAM)
            remote(
                outgoing.at[(half, peer, *at)],
                incoming.at[(half, TEAM - step, *at)],
                a2a_send.at[kind, layer, half, head or 0],
                a2a_recv.at[kind, layer, half, head or 0],
                place(lax.div(peer, 2), side, zz, lax.rem(peer, 2)),
            ).start()

    def arrived(kind, layer, half, incoming, head=None):
        at = () if head is None else (head,)
        whole = incoming.at[(half, pl.ds(1, TEAM - 1), *at)]
        pltpu.make_async_copy(whole, whole, a2a_recv.at[kind, layer, half, head or 0]).wait()

    def left(kind, layer, half, outgoing):
        for head in range(OWN) if kind in (0, 3) else (None,):
            at = () if head is None else (head,)
            whole = outgoing.at[(half, pl.ds(1, TEAM - 1), *at)]
            pltpu.make_async_copy(whole, whole, a2a_send.at[kind, layer, half, head or 0]).wait()

    def tokens_of(chunk, other):
        return pl.ds(pl.multiple_of(HALF * (TEAM * chunk + other), HALF), HALF)

    def hidden_copy(layer, chunk, which):
        whose = 2 * core + 1 - yy if which == 2 else member
        block = hid_all.at[layer, :, tokens_of(chunk, whose)]
        return remote(
            block,
            block,
            hid_send.at[layer, chunk, which],
            hid_recv.at[layer, chunk, which],
            y_peer if which == 0 else core_peer,
        )

    def hidden_start(layer, chunk):
        for which in range(2):
            hidden_copy(layer, chunk, which).start()

    def hidden_pass(layer, chunk):
        hidden_copy(layer, chunk, 0).wait()
        hidden_copy(layer, chunk, 2).start()

    def hidden_done(layer, chunk):
        for which in range(1, 3):
            hidden_copy(layer, chunk, which).wait()

    def project(layer, half):
        rows = rows_of(half)
        rounded = hidden[rows, :].astype(BF16)
        if layer == 1:
            left(0, 0, half, pack_out)
        queries = (nn(rounded, wqkv[layer, :, 0:WIDTH]) * (DIM ** -0.5)).astype(BF16).T
        for head in range(RUNS):
            pack_out[half, head // 2, head % 2, HALF:, :] = queries[DIM * head : DIM * head + DIM, :]
        for step in range(2):
            at = WIDTH * (step + 1)
            keys_values = nn(rounded, wqkv[layer, :, at : at + WIDTH]).astype(BF16)
            for head in range(4):
                pack_out[half, 2 * step + head // 2, head % 2, 0:HALF, :] = keys_values[
                    :, 128 * head : 128 * head + 128
                ]
        for head in range(OWN):
            exchange(0, layer, half, pack_out, pack_in, head)
        hid_all[layer, :, tokens_of(half, member)] = rounded.T

    def rows_before(i):
        return TILE * i * (i + 1) // 2

    def attend(layer, chunk):
        if layer == 1:
            left(1, 0, chunk, head_out)

        def one_head(head, carry):
            arrived(0, layer, chunk, pack_in, head)
            for other in range(TEAM):
                slot = slot_of(other)
                start = HALF * (TEAM * chunk + other)
                span = slice(start, start + HALF)
                block = pack_in[chunk, slot, head, 0:HALF, :]
                kv[layer, head, span, :] = block
                kv_t[layer, head, :, span] = block.T
                rq[layer, head, 0:DIM, span] = pack_in[chunk, slot, head, HALF:, :]

            def scores_of(i):
                count = TILE * (i + 1)
                tile = rq[layer, head, :, TILE * i : TILE * i + TILE]
                return nn(kv[layer, head, 0:count, :], tile) + bias[TILE * TILES - count :, :]

            ahead = [scores_of(i) for i in (2 * chunk, 2 * chunk + 1)]
            for i in (2 * chunk, 2 * chunk + 1):
                columns = slice(TILE * i, TILE * i + TILE)
                count = TILE * (i + 1)
                scores = ahead[i - 2 * chunk]
                largest = jnp.max(scores, axis=0, keepdims=True)
                weight = jnp.exp(scores - largest)
                total = jnp.sum(weight, axis=0, keepdims=True)
                share = (weight * (1.0 / total)).astype(BF16)
                probs[layer, head, rows_before(i) : rows_before(i) + count, :] = share
                summed = nn(kv_t[layer, head, DIM:, 0:count], share)
                o_t[layer, head, :, columns] = summed
                rounded = summed.astype(BF16)
                for part in range(2):
                    head_out[chunk, 2 * (i - 2 * chunk) + part, head] = rounded[
                        :, HALF * part : HALF * part + HALF
                    ]
            return carry

        for head in range(OWN):
            one_head(head, 0)
        exchange(1, layer, chunk, head_out, o_in)

    def feed(layer, half):
        rows = rows_of(half)
        arrived(1, layer, half, o_in)
        for head in range(RUNS):
            attn_t[layer, DIM * head : DIM * head + DIM, rows] = o_in[half, slot_of(head // 2), head % 2]
        attn = attn_t[layer, :, rows].T
        grown = nn(attn, wout[layer])
        branch[layer, rows, :] = grown
        middle = hidden[rows, :] + alphas[layer, 0] * grown
        rounded = middle.astype(BF16)
        entered[layer, rows, :] = rounded
        total = jnp.zeros((HALF, WIDTH), F32)

        def gate_of(step):
            cut = slice(CUT * step, CUT * step + CUT)
            return nn(rounded, wup[layer, :, cut]) + up_bias[layer : layer + 1, cut]

        coming = gate_of(0)
        for step in range(FF // CUT):
            cut = slice(CUT * step, CUT * step + CUT)
            gate = coming
            if step + 1 < FF // CUT:
                coming = gate_of(step + 1)
            bell = jnp.exp(gate * gate * -0.5)
            near = pl.reciprocal(1.0 + SLOPE_AT * jnp.abs(gate), approx=True)
            tail = jnp.full_like(gate, TAIL[5])
            for factor in TAIL[4::-1]:
                tail = tail * near + factor
            tail = bell * (tail * near)
            risen = jnp.where(gate > 0.0, 1.0 - tail, tail)
            slope[layer, rows, cut] = risen + gate * bell * 0.3989422804014327
            active = (gate * risen).astype(BF16)
            act[layer, rows, cut] = active
            total = total + nn(active, wdown[layer, cut, :])
        total = total + down_bias[layer : layer + 1, :]
        second[layer, rows, :] = total
        hidden[rows, :] = middle + alphas[layer, 1] * total

    def total_of(values):
        return jnp.sum(jnp.sum(values, axis=0, keepdims=True), axis=1, keepdims=True)

    def feed_back(layer):
        start = grad[...]
        if layer == 0:
            dz[...] = (alphas[layer, 1] * start).astype(BF16)
        scaled = dz[...]
        alpha_second = total_of(start * second[layer])
        small[layer : layer + 1, FF : FF + WIDTH] = jnp.sum(scaled.astype(F32), axis=0, keepdims=True)
        middle = start
        coming = nt(scaled, wdown[layer, 0:CUT, :])
        for step in range(FF // CUT):
            cut = slice(CUT * step, CUT * step + CUT)
            raw = coming
            if step + 1 < FF // CUT:
                coming = nt(scaled, wdown[layer, CUT * (step + 1) : CUT * (step + 2), :])
            gate = (raw * slope[layer, :, cut]).astype(BF16)
            du[:, cut] = gate
            small[layer : layer + 1, cut] = jnp.sum(gate.astype(F32), axis=0, keepdims=True)
            middle = middle + nt(gate, wup[layer, :, cut])
        grad[...] = middle
        mixed = (alphas[layer, 0] * middle).astype(BF16)
        da[...] = mixed
        spread = nt(wout[layer], mixed).astype(BF16)
        for chunk in (1, 0):
            left(*((1, 1) if layer == 1 else (2, 1)), chunk, head_out)
            for head in range(RUNS):
                head_out[chunk, head // 2, head % 2] = spread[
                    DIM * head : DIM * head + DIM, HALF * chunk : HALF * chunk + HALF
                ]
            exchange(2, layer, chunk, head_out, do_in)
        alpha_first = total_of(middle * branch[layer])
        column = lax.broadcasted_iota(jnp.int32, (1, 128), 1)
        small[layer : layer + 1, FF + WIDTH :] = jnp.where(
            column == 0, alpha_first, jnp.where(column == 1, alpha_second, 0.0)
        )

    def attend_back(layer, chunk):
        arrived(2, layer, chunk, do_in)
        left(*((0, 1) if layer == 1 else (3, 1)), chunk, pack_out)

        def one_head(head, carry):
            for other in range(TEAM):
                start = HALF * (TEAM * chunk + other)
                ro[head, DIM:, start : start + HALF] = do_in[chunk, slot_of(other), head]
            for i in (2 * chunk, 2 * chunk + 1):
                columns = slice(TILE * i, TILE * i + TILE)
                query_tile = rq[layer, head, :, columns]
                grad_tile = ro[head, :, columns]
                delta = jnp.sum(
                    ro[head, DIM:, columns].astype(F32) * o_t[layer, head, :, columns],
                    axis=0,
                    keepdims=True,
                )
                count = TILE * (i + 1)
                keys = kv[layer, head, 0:count, :]
                share = probs[layer, head, rows_before(i) : rows_before(i) + count, :]
                scored = (share.astype(F32) * (nn(keys, grad_tile) - delta)).astype(BF16)
                term = nt(scored, query_tile) + nt(share, grad_tile)
                if chunk == 1 and i == 2:
                    acc[head, 0:count, :] = term
                elif chunk == 1:
                    acc[head, 0 : count - TILE, :] += term[0 : count - TILE, :]
                    acc[head, count - TILE : count, :] = term[count - TILE :, :]
                else:
                    acc[head, 0:count, :] += term
                query_grad = nn(kv_t[layer, head, 0:DIM, 0:count], scored)
                dq_t[head, :, columns] = query_grad * (DIM ** -0.5)
            for other in range(TEAM):
                start = HALF * (TEAM * chunk + other)
                span = slice(start, start + HALF)
                pack_out[chunk, other, head, 0:HALF, :] = acc[head, span, :].astype(BF16)
                pack_out[chunk, other, head, HALF:, :] = dq_t[head, :, span].astype(BF16)
            exchange(3, layer, chunk, pack_out, pack_in, head)
            return carry

        for head in range(OWN):
            one_head(head, 0)

    def project_back(layer, half):
        for head in range(OWN):
            arrived(3, layer, half, pack_in, head)
        turned = jnp.concatenate(
            [pack_in[half, slot_of(head // 2), head % 2, HALF:, :] for head in range(RUNS)], axis=0
        )
        dqkv[:, 0:WIDTH] = turned.T
        for head in range(RUNS):
            at = WIDTH + 128 * head
            dqkv[:, at : at + 128] = pack_in[half, slot_of(head // 2), head % 2, 0:HALF, :]
        rows = rows_of(half)
        grad[rows, :] = grad[rows, :] + nt(dqkv[...], wqkv[layer])

    def scatter_rows(layer, result, first_row):
        for run in range(RUNS):
            for quarter in range(4):
                parts[layer, quarter % 2, quarter // 2, run // 2, run % 2, first_row : first_row + DIM, :] = result[
                    DIM * run : DIM * run + DIM, 128 * quarter : 128 * quarter + 128
                ].astype(BF16)

    def make(part):
        layer, first, count = PARTS[part]
        if first < 256:
            turned = entered[layer].T
        for row in range(first, min(first + count, 256), DIM):
            step = row // DIM
            scatter_rows(layer, nn(turned, du[:, CUT * step : CUT * step + CUT]), row)
        if first <= 256 < first + count:
            scatter_rows(layer, nn(attn_t[layer], da[...]), 256)
        if first >= 320:
            turned = dz[...].T
            for step in range(FF // CUT):
                result = nn(turned, act[layer, :, CUT * step : CUT * step + CUT])
                for block in range(CUT // 128):
                    run, row = 2 * step + block // 2, 320 + 128 * (block % 2)
                    for quarter in range(4):
                        parts[layer, quarter % 2, quarter // 2, run // 2, run % 2, row : row + 128, :] = result[
                            128 * quarter : 128 * quarter + 128, 128 * block : 128 * block + 128
                        ].astype(BF16)
        if layer == 0:
            pl.semaphore_wait(core_free.at[0 if first < 320 else 1], 1)
        core_copy(part).start()

    def heads_grads(layer):
        for chunk in range(2):
            hidden_done(layer, chunk)
        blocks = [(run // TEAM, run % TEAM) for run in range(RUNS)]
        keys_values = jnp.concatenate(
            [
                jnp.concatenate([pack_out[chunk, other, head, 0:HALF, :] for chunk, other in blocks], axis=0)
                for head in range(OWN)
            ],
            axis=1,
        )
        queries = jnp.concatenate(
            [
                jnp.concatenate([pack_out[chunk, other, head, HALF:, :] for chunk, other in blocks], axis=1)
                for head in range(OWN)
            ],
            axis=0,
        )
        both = nn(hid_all[layer], keys_values)
        q_part = nt(hid_all[layer], queries)
        for number, values in enumerate((q_part, both[:, 0:128], both[:, 128:256])):
            for run in range(RUNS):
                heads_out[layer, run // 2, run % 2, :, 128 * number : 128 * number + 128] = values[
                    DIM * run : DIM * run + DIM, :
                ].astype(BF16)
        heads_x_copy(layer).start()

    def half_rows(which):
        return pl.ds(pl.multiple_of(32 * which, 32), 32)

    def heads_x_copy(layer):
        return remote(
            heads_out.at[layer, :, :, half_rows(1 - side)],
            heads_x.at[layer],
            hx_send.at[layer],
            hx_recv.at[layer],
            x_peer,
        )

    def heads_z_copy(layer, step):
        peer = lax.rem(zz + step, 4)
        return remote(
            heads_out.at[layer, peer, :, half_rows(side)],
            heads_z.at[layer, 4 - step],
            hz_send.at[layer, step],
            hz_recv.at[layer, 4 - step],
            place(core, side, peer, yy),
        )

    def heads_last_copy(layer, number):
        x, c, y = number // 4, number // 2 % 2, number % 2
        return remote(
            heads_sum.at[layer, 1 - yy if y else yy],
            heads_all.at[layer, side, member],
            hf_send.at[layer, number],
            hf_recv.at[layer, number],
            place(1 - core if c else core, 1 - side if x else side, zz, 1 - yy if y else yy),
        )

    def heads_second(layer):
        heads_x_copy(layer).wait()
        heads_out[layer, :, :, half_rows(side), :] += heads_x[layer]
        for step in range(1, 4):
            heads_z_copy(layer, step).start()

    def heads_third(layer):
        for step in range(1, 4):
            heads_z_copy(layer, step).wait()
        total = heads_out[layer, zz, :, half_rows(side), :].astype(F32)
        for slot in range(1, 4):
            total = total + heads_z[layer, slot].astype(F32)
        heads_sum[layer] = total.astype(BF16)
        heads_all[layer, side, member] = heads_sum[layer, yy]
        for number in range(1, 8):
            heads_last_copy(layer, number).start()

    def heads_done(layer):
        for number in range(1, 8):
            heads_last_copy(layer, number).wait()

    def rows_in(part, route):
        first, room, count = SPANS[part, route]
        return pl.ds(first, count), pl.ds(room, count)

    def used(part, route):
        return SHARES[part][route] > 0

    def core_copy(part):
        layer, first, count = PARTS[part]
        rows = pl.ds(first, count)
        return remote(
            parts.at[layer, 1 - core, :, :, :, rows],
            core_in.at[:, :, :, rows],
            core_send.at[part],
            core_recv.at[part],
            core_peer,
        )

    def x_copy(part, route):
        layer = PARTS[part][0]
        rows, room = rows_in(part, route)
        ends = (x_send.at[part, route], x_recv.at[part, route], x_peer)
        mine = parts.at[layer, core, 1 - side]
        if route == 0:
            return remote(mine.at[:, :, rows], xa_in.at[:, :, room], *ends)
        if route == 1:
            return remote(mine.at[:, yy, rows], xb_in.at[:, room], *ends)
        return remote(mine.at[zz, :, rows], third_x.at[:, room], *ends)

    def y_copy(part, route):
        layer = PARTS[part][0]
        rows, room = rows_in(part, route)
        ends = (y_send.at[part, route], y_recv.at[part, route], y_peer)
        mine = parts.at[layer, core]
        if route == 0:
            return remote(mine.at[side, :, 1 - yy, rows], ya_in.at[:, room], *ends)
        if route == 1:
            return remote(mine.at[:, :, 1 - yy, rows], yb_in.at[:, :, room], *ends)
        return remote(mine.at[side, zz, 1 - yy, rows], third_y.at[room], *ends)

    def z_copy(part, route, step):
        layer = PARTS[part][0]
        rows, room = rows_in(part, route)
        peer = lax.rem(zz + step, 4)
        ends = (z_send.at[part, route, step], z_recv.at[part, route, 4 - step], place(core, side, peer, yy))
        if route == 2:
            return remote(parts.at[layer, core, :, peer, :, rows], third_z.at[4 - step, :, :, room], *ends)
        return remote(parts.at[layer, core, side, peer, yy, rows], z_in.at[layer, 4 - step, rows], *ends)

    def final_copy(part, which):
        layer, first, count = PARTS[part]
        block = final.at[layer, far_side if which == 2 else grp, pl.ds(first, count)]
        return remote(
            block,
            block,
            fin_send.at[part, which],
            fin_recv.at[part, which],
            x_peer if which == 0 else core_peer,
        )

    def core_done(part):
        layer, first, count = PARTS[part]
        rows = pl.ds(first, count)
        core_copy(part).wait()
        for across in (1 - side, side):
            parts[layer, core, across, :, :, rows, :] += core_in[across, :, :, rows, :]
            if used(part, 0) and across is not side:
                x_copy(part, 0).start()
        if used(part, 1):
            y_copy(part, 1).start()
        if used(part, 2):
            for step in range(1, 4):
                z_copy(part, 2, step).start()
        if layer == 1:
            freed = 0 if first < 320 else 1
            followers = [1 for other in PARTS if other[0] == 0 and (other[1] >= 320) == (freed == 1)]
            credit(core_free.at[freed], core_peer, len(followers))

    def first_x(part):
        if used(part, 0):
            layer = PARTS[part][0]
            rows, room = rows_in(part, 0)
            x_copy(part, 0).wait()
            for y in (1 - yy, yy):
                parts[layer, core, side, :, y, rows, :] += xa_in[:, y, room, :]
                if y is not yy:
                    y_copy(part, 0).start()

    def first_y(part):
        if used(part, 1):
            layer = PARTS[part][0]
            rows, room = rows_in(part, 1)
            y_copy(part, 1).wait()
            for across in (1 - side, side):
                parts[layer, core, across, :, yy, rows, :] += yb_in[across, :, room, :]
                if across is not side:
                    x_copy(part, 1).start()

    def first_z(part):
        if used(part, 2):
            layer = PARTS[part][0]
            rows, room = rows_in(part, 2)
            for step in range(1, 4):
                z_copy(part, 2, step).wait()
            for across in (1 - side, side):
                total = parts[layer, core, across, zz, :, rows, :].astype(F32)
                for slot in range(1, 4):
                    total = total + third_z[slot, across, :, room, :].astype(F32)
                parts[layer, core, across, zz, :, rows, :] = total.astype(BF16)
                if across is not side:
                    x_copy(part, 2).start()

    def second_x(part):
        if used(part, 0):
            layer = PARTS[part][0]
            rows, room = rows_in(part, 0)
            y_copy(part, 0).wait()
            parts[layer, core, side, :, yy, rows, :] += ya_in[:, room, :]
            for step in range(1, 4):
                z_copy(part, 0, step).start()

    def second_y(part):
        if used(part, 1):
            layer = PARTS[part][0]
            rows, room = rows_in(part, 1)
            x_copy(part, 1).wait()
            parts[layer, core, side, :, yy, rows, :] += xb_in[:, room, :]
            for step in range(1, 4):
                z_copy(part, 1, step).start()

    def second_z(part):
        if used(part, 2):
            layer = PARTS[part][0]
            rows, room = rows_in(part, 2)
            x_copy(part, 2).wait()
            for y in (1 - yy, yy):
                parts[layer, core, side, zz, y, rows, :] += third_x[y, room, :]
                if y is not yy:
                    y_copy(part, 2).start()

    def third_done(part):
        layer = PARTS[part][0]
        for route in range(3):
            if not used(part, route):
                continue
            rows, room = rows_in(part, route)
            if route == 2:
                y_copy(part, 2).wait()
                final[layer, grp, rows, :] = parts[layer, core, side, zz, yy, rows, :] + third_y[room, :]
            else:
                for step in range(1, 4):
                    z_copy(part, route, step).wait()
                total = parts[layer, core, side, zz, yy, rows, :].astype(F32)
                for slot in range(1, 4):
                    total = total + z_in[layer, slot, rows, :].astype(F32)
                final[layer, grp, rows, :] = total.astype(BF16)
        if PARTS[part][1] >= 320:
            for row in (320, 448):
                final[layer, grp, row : row + 128, :] = final[layer, grp, row : row + 128, :].T
        for which in range(2):
            final_copy(part, which).start()

    def final_pass(part):
        final_copy(part, 0).wait()
        final_copy(part, 2).start()

    def final_done(part):
        for which in range(1, 3):
            final_copy(part, which).wait()

    def small_copy(stage):
        peer = (core_peer, x_peer, y_peer)[stage]
        return remote(
            small_sum.at[stage], small_in.at[stage], small_send.at[stage], small_recv.at[stage], peer
        )

    def small_z_copy(step):
        return remote(
            small_z.at[zz],
            small_z.at[zz],
            small_send.at[2 + step],
            small_recv.at[2 + step],
            place(core, side, lax.rem(zz + step, 4), yy),
        )

    def small_start():
        small_sum[0] = small[...]
        small_copy(0).start()

    def small_next(stage):
        small_copy(stage).wait()
        total = small_sum[stage] + small_in[stage]
        if stage < 2:
            small_sum[stage + 1] = total
            small_copy(stage + 1).start()
        else:
            small_z[zz] = total
            for step in range(1, 4):
                small_z_copy(step).start()

    def small_done():
        for step in range(1, 4):
            small_z_copy(step).wait()
        small_sum[0] = (small_z[0] + small_z[1]) + (small_z[2] + small_z[3])
        small_final[:, 0:256] = small_sum[0, :, pl.ds(pl.multiple_of(blk * 256, 256), 256)]
        pair = small_sum[0, :, pl.ds(pl.multiple_of(FF + 128 * zz, 128), 128)]
        small_final[:, 256:384] = jnp.where(yy == 1, pltpu.roll(pair, DIM, 1), pair)
        small_final[:, 384:512] = small_sum[0, :, FF + WIDTH :]

    def halves(*phases, first=0):
        def both(step, carry):
            for phase in phases:
                phase(lax.rem(step + first, 2))
            return carry

        lax.fori_loop(0, 2, both, 0)

    def begin(half):
        move_arrived(0, half, tok_in)
        hidden[rows_of(half), :] = tok_in[half].astype(F32)

    def finish(half):
        back_out[0, half] = hidden[rows_of(half), :].astype(BF16)
        to_owner(3, half, back_out.at[0, half], out_in)

    def turn_round(layer, half):
        move_arrived(2, half, cot_in)
        rows = rows_of(half)
        grad[rows, :] = cot_in[half].astype(F32)
        dz[rows, :] = (alphas[layer, 1] * grad[rows, :]).astype(BF16)

    def hand_back(half):
        back_out[1, half] = grad[rows_of(half), :].astype(BF16)
        to_owner(4, half, back_out.at[1, half], grad_in)

    barrier = pltpu.get_barrier_semaphore()
    for step in range(1, 4):
        credit(barrier, place(core, side, lax.rem(zz + step, 4), yy))
    for step in range(4):
        credit(barrier, place(1 - core, side, lax.rem(zz + step, 4), yy))
    for peer in (
        x_peer,
        y_peer,
        place(1 - core, side, zz, 1 - yy),
        place(1 - core, 1 - side, zz, yy),
        place(core, 1 - side, zz, 1 - yy),
        place(1 - core, 1 - side, zz, 1 - yy),
    ):
        credit(barrier, peer)

    weight_copies = {}
    for layer in range(LAYERS):
        for number, (source, target) in enumerate(
            ((qkv_hbm, wqkv), (out_hbm, wout), (up_hbm, wup), (down_hbm, wdown))
        ):
            weight_copies[layer, number] = pltpu.make_async_copy(
                source.at[layer], target.at[layer], w_sem.at[layer, number]
            )
    bias_copies = [
        pltpu.make_async_copy(up_bias_hbm, up_bias, w_sem.at[2, 0]),
        pltpu.make_async_copy(down_bias_hbm, down_bias, w_sem.at[2, 1]),
        pltpu.make_async_copy(alphas_hbm, alphas, w_sem.at[2, 2]),
    ]
    length_copy = pltpu.make_async_copy(seq_len_hbm, seq_len, w_sem.at[2, 3])
    length_copy.start()
    weight_copies[0, 0].start()
    pl.semaphore_wait(barrier, 13)
    upper = lax.div(zz, 2)
    for half in (1 - upper, upper):
        to_team(0, half, half_of(tokens, half), tok_in)
    for layer, number in ((1, 0), (0, 1), (0, 2), (0, 3), (1, 1), (1, 2), (1, 3)):
        weight_copies[layer, number].start(priority=1)
    for copy in bias_copies:
        copy.start(priority=1)
    length_copy.wait()
    end_second = lax.div(seq_len[0, 0] + seq_len[0, 1], RUNS)
    flag_out[...] = jnp.full((8, 128), end_second.astype(F32), F32)
    for half in (1 - upper, upper):
        to_team(1, half, flag_out, flag_in)
    for layer in range(LAYERS):
        for head in range(OWN):
            rq[layer, head, DIM:, :] = jnp.zeros((DIM, HALF * RUNS), BF16)
    for head in range(OWN):
        ro[head, 0:DIM, :] = jnp.zeros((DIM, HALF * RUNS), BF16)
    for layer in range(LAYERS):
        weight_copies[layer, 0].wait()
        pairs = [
            beside(
                wqkv[layer, :, WIDTH + 128 * pair : WIDTH + 128 * pair + 128].astype(F32),
                wqkv[layer, :, 2 * WIDTH + 128 * pair : 2 * WIDTH + 128 * pair + 128].astype(F32),
            )
            for pair in range(TEAM)
        ]
        for head in range(RUNS):
            at = WIDTH + 128 * head
            wqkv[layer, :, at : at + 128] = pairs[head // 2][head % 2].astype(BF16)
    halves(begin, functools.partial(project, 0), first=upper)
    for half in (1 - upper, upper):
        to_team(2, half, half_of(cotangent, half), cot_in)

    move_arrived(1, 0, flag_in)
    move_arrived(1, 1, flag_in)
    border = jnp.concatenate([flag_in[0, 0:1, :]] * 2, axis=1) - (HALF * lax.div(zz, 2)).astype(F32)
    key_row = lax.broadcasted_iota(jnp.int32, (TILE, TILE), 0)
    query_col = lax.broadcasted_iota(jnp.int32, (TILE, TILE), 1)
    later = key_row > query_col
    key_sub = lax.rem(key_row, HALF).astype(F32) >= border
    query_sub = lax.rem(query_col, HALF).astype(F32) >= border
    apart = jnp.logical_xor(key_sub, query_sub)
    for tile in range(TILES - 1):
        bias[TILE * tile : TILE * tile + TILE, :] = jnp.where(apart, NEGATIVE, 0.0)
    bias[TILE * (TILES - 1) :, :] = jnp.where(jnp.logical_or(later, apart), NEGATIVE, 0.0)

    for copy in (*bias_copies, *(weight_copies[0, number] for number in range(1, 4))):
        copy.wait()
    attend(0, 0)
    attend(0, 1)
    hidden_start(0, 0)
    halves(functools.partial(feed, 0), functools.partial(project, 1))
    for number in range(1, 4):
        weight_copies[1, number].wait()
    attend(1, 0)
    attend(1, 1)
    hidden_pass(0, 0)
    hidden_start(1, 0)
    halves(functools.partial(feed, 1), finish)
    hidden_start(0, 1)
    hidden_start(1, 1)
    hidden_pass(1, 0)

    halves(functools.partial(turn_round, 1))
    make(1)
    feed_back(1)
    hidden_pass(0, 1)
    hidden_pass(1, 1)
    core_done(1)
    make(0)
    attend_back(1, 1)
    first_y(1)
    core_done(0)
    attend_back(1, 0)
    second_y(1)
    first_x(1)
    project_back(1, 1)
    heads_grads(1)
    first_z(1)
    project_back(1, 0)
    feed_back(0)
    small_start()
    second_x(1)
    make(2)
    first_x(0)
    heads_second(1)
    first_z(0)
    attend_back(0, 1)
    small_next(0)
    core_done(2)
    second_x(0)
    make(3)
    attend_back(0, 0)
    small_next(1)
    project_back(0, 1)
    hand_back(1)
    first_z(2)
    heads_grads(0)
    small_next(2)
    first_x(2)
    core_done(3)
    first_y(2)
    heads_second(0)
    small_done()
    first_z(3)
    second_x(2)
    first_x(3)
    second_z(2)
    second_z(0)
    heads_third(1)
    second_z(1)
    first_y(3)
    heads_third(0)
    second_y(2)
    second_x(3)
    second_z(3)
    third_done(0)
    third_done(2)
    second_y(3)
    project_back(0, 0)
    hand_back(0)
    heads_done(1)
    third_done(1)
    third_done(3)
    final_pass(0)
    final_pass(2)
    final_pass(1)
    final_pass(3)
    final_done(2)
    final_done(1)
    heads_done(0)
    final_done(0)
    final_done(3)
    for half in range(2):
        move_arrived(3, half, out_in)
        move_arrived(4, half, grad_in)

    for half in range(2):
        left(2, 0, half, head_out)
        left(3, 0, half, pack_out)
        to_team_left(0, half, half_of(tokens, half))
        to_team_left(1, half, flag_out)
        to_team_left(2, half, half_of(cotangent, half))
        to_owner_left(3, half, back_out.at[0, half])
        to_owner_left(4, half, back_out.at[1, half])


def results_kernel(
    final, heads, out_block, grad_block, small,
    output, input_grad, qkv_grad, out_grad, up_grad, up_bias_grad, down_grad, down_bias_grad, alpha_grad,
    grad_wide, qkv_wide, out_wide, up_wide, down_wide, up_bias, down_bias, alpha, out_sem,
):
    ends = []

    def write(source, target):
        ends.append(pltpu.make_async_copy(source, target, out_sem.at[len(ends)]))
        ends[-1].start()

    for half in range(2):
        write(out_block.at[half], output.at[pl.ds(HALF * half, HALF)])
    up_bias[...] = small[:, 0:256]
    write(up_bias, up_bias_grad)
    down_bias[...] = small[:, 256 : 256 + DIM]
    write(down_bias, down_bias_grad)
    alpha[...] = small[:, 384:386]
    write(alpha, alpha_grad)
    for layer in range(LAYERS):
        for quarter in range(4):

            def block(first, count):
                return final[layer, quarter, first : first + count, :].astype(F32)

            def columns(step):
                return slice(WIDTH * step + 128 * quarter, WIDTH * step + 128 * quarter + 128)

            for step in range(4):
                up_wide[layer, :, columns(step)] = block(DIM * step, DIM)
            out_wide[layer, :, columns(0)] = block(256, DIM)
            down_wide[layer, :, columns(0)] = block(320, 256)
        write(up_wide.at[layer], up_grad.at[layer])
        write(out_wide.at[layer], out_grad.at[layer])
        write(down_wide.at[layer], down_grad.at[layer])
    for half in range(2):
        rows = slice(HALF * half, HALF * half + HALF)
        grad_wide[rows, :] = grad_block[half].astype(F32)
    write(grad_wide, input_grad)
    for layer in range(LAYERS):
        for side in range(2):
            for member in range(TEAM):
                block = heads[layer, side, member].astype(F32)
                columns = (block[:, 0:128], *beside(block[:, 128:256], block[:, 256:384]))
                for step in range(3):
                    at = WIDTH * step + 128 * member
                    qkv_wide[layer, 32 * side : 32 * side + 32, at : at + 128] = columns[step]
        write(qkv_wide.at[layer], qkv_grad.at[layer])
    for end in ends:
        end.wait()


def fast_body(
    tokens, seq_len, qkv_weight, out_weight, up_weight, up_bias, down_weight, down_bias, alphas, cotangent
):
    whole = pl.BlockSpec(memory_space=pltpu.VMEM)
    far = pl.BlockSpec(memory_space=pl.ANY)
    shape = jax.ShapeDtypeStruct
    rows = HALF * RUNS

    def vmem(*dims):
        return pltpu.VMEM(dims, BF16)

    def wide(*dims):
        return pltpu.VMEM(dims, F32)

    dma = pltpu.SemaphoreType.DMA
    final, heads, out_block, grad_block, small = pl.pallas_call(
        layers_kernel,
        out_shape=(
            vmem(LAYERS, 4, CHUNK, 128),
            vmem(LAYERS, 2, TEAM, DIM // 2, 3 * 128),
            vmem(2, HALF, WIDTH),
            vmem(2, HALF, WIDTH),
            wide(LAYERS, WIDTH),
        ),
        in_specs=[far, far, far, far, far, far, far, far, far, far],
        out_specs=(whole,) * 5,
        scratch_shapes=[
            pltpu.SMEM((1, 4), jnp.int32),
            pltpu.SMEM((LAYERS, 2), F32),
            vmem(LAYERS, WIDTH, 3 * WIDTH),
            vmem(LAYERS, WIDTH, WIDTH),
            vmem(LAYERS, WIDTH, FF),
            vmem(LAYERS, FF, WIDTH),
            wide(LAYERS, FF),
            wide(LAYERS, WIDTH),
            vmem(2, HALF, WIDTH),
            vmem(2, HALF, WIDTH),
            wide(8, 128),
            wide(2, 8, 128),
            vmem(2, 2, HALF, WIDTH),
            wide(2 * HALF, WIDTH),
            wide(2 * HALF, WIDTH),
            vmem(LAYERS, WIDTH, rows),
            vmem(LAYERS, WIDTH, 2 * HALF),
            vmem(LAYERS, 2 * HALF, WIDTH),
            vmem(LAYERS, 2 * HALF, FF),
            wide(LAYERS, 2 * HALF, WIDTH),
            wide(LAYERS, 2 * HALF, FF),
            wide(LAYERS, 2 * HALF, WIDTH),
            vmem(2 * HALF, WIDTH),
            vmem(2 * HALF, FF),
            vmem(2 * HALF, WIDTH),
            vmem(HALF, 3 * WIDTH),
            vmem(2, TEAM, OWN, PACK, 128),
            vmem(2, TEAM, OWN, DIM, 128),
            vmem(2, TEAM, OWN, PACK, 128),
            vmem(2, TEAM, OWN, DIM, 128),
            vmem(2, TEAM, OWN, DIM, 128),
            vmem(LAYERS, OWN, rows, 128),
            vmem(LAYERS, OWN, 128, rows),
            vmem(LAYERS, OWN, 128, rows),
            vmem(OWN, 128, rows),
            wide(LAYERS, OWN, DIM, rows),
            vmem(LAYERS, OWN, TILE * TILES * (TILES + 1) // 2, TILE),
            wide(OWN, rows, 128),
            wide(OWN, DIM, rows),
            wide(rows, TILE),
            vmem(LAYERS, 2, 2, 4, 2, CHUNK, 128),
            vmem(2, 4, 2, CHUNK, 128),
            vmem(4, 2, TOTALS[0], 128),
            vmem(4, TOTALS[1], 128),
            vmem(4, TOTALS[0], 128),
            vmem(2, 4, TOTALS[1], 128),
            vmem(LAYERS, 4, CHUNK, 128),
            vmem(4, 2, 2, TOTALS[2], 128),
            vmem(2, TOTALS[2], 128),
            vmem(TOTALS[2], 128),
            vmem(LAYERS, 4, 2, DIM, 3 * 128),
            vmem(LAYERS, 4, 2, DIM // 2, 3 * 128),
            vmem(LAYERS, 4, 2, DIM // 2, 3 * 128),
            vmem(LAYERS, 2, DIM // 2, 3 * 128),
            wide(LAYERS, SMALL),
            wide(3, LAYERS, SMALL),
            wide(4, LAYERS, SMALL),
            wide(3, LAYERS, SMALL),
            dma((LAYERS + 1, 4)),
            dma((5, 2)),
            dma((5, 2)),
            dma((4, LAYERS, 2, OWN)),
            dma((4, LAYERS, 2, OWN)),
            dma((len(PARTS),)),
            dma((len(PARTS),)),
            dma((len(PARTS), 3)),
            dma((len(PARTS), 3)),
            dma((len(PARTS), 3)),
            dma((len(PARTS), 3)),
            dma((len(PARTS), 3, 4)),
            dma((len(PARTS), 3, 4)),
            dma((len(PARTS), 3)),
            dma((len(PARTS), 3)),
            dma((LAYERS, 2, 3)),
            dma((LAYERS, 2, 3)),
            dma((LAYERS,)),
            dma((LAYERS,)),
            dma((LAYERS, 4)),
            dma((LAYERS, 4)),
            dma((LAYERS, 8)),
            dma((LAYERS, 8)),
            dma((6,)),
            dma((6,)),
            pltpu.SemaphoreType.REGULAR((2,)),
        ],
        compiler_params=pltpu.CompilerParams(
            collective_id=0, has_side_effects=True, vmem_limit_bytes=61 * 1024 * 1024
        ),
        name="layers",
    )(
        tokens, seq_len, alphas, up_bias, down_bias, cotangent,
        qkv_weight, out_weight, up_weight, down_weight,
    )
    return tuple(
        pl.pallas_call(
            results_kernel,
            out_shape=(
                shape((2 * HALF, WIDTH), BF16),
                shape((2 * HALF, WIDTH), F32),
                shape((LAYERS, DIM, 3 * WIDTH), F32),
                shape((LAYERS, DIM, WIDTH), F32),
                shape((LAYERS, DIM, FF), F32),
                shape((LAYERS, FF // RUNS), F32),
                shape((LAYERS, FF // RUNS, WIDTH), F32),
                shape((LAYERS, DIM), F32),
                shape((LAYERS, 2), F32),
            ),
            in_specs=[whole] * 5,
            out_specs=(far,) * 9,
            scratch_shapes=[
                wide(2 * HALF, WIDTH),
                wide(LAYERS, DIM, 3 * WIDTH),
                wide(LAYERS, DIM, WIDTH),
                wide(LAYERS, DIM, FF),
                wide(LAYERS, FF // RUNS, WIDTH),
                wide(LAYERS, FF // RUNS),
                wide(LAYERS, DIM),
                wide(LAYERS, 2),
                dma((14,)),
            ],
            compiler_params=pltpu.CompilerParams(vmem_limit_bytes=24 * 1024 * 1024),
            name="results",
        )(final, heads, out_block, grad_block, small)
    )


def layout(seq_len, local_count, cycle_size):
    piece_rows = seq_len[0] // cycle_size
    end_rows = jnp.cumsum(piece_rows)
    start_rows = end_rows - piece_rows
    local_rows = jnp.arange(local_count, dtype=jnp.int32)
    segment = jnp.sum((local_rows[:, None] >= end_rows[None, :]).astype(jnp.int32), axis=1)
    picked = segment[:, None] == jnp.arange(seq_len.shape[1], dtype=jnp.int32)[None, :]
    offset = local_rows - jnp.sum(jnp.where(picked, start_rows[None, :], 0), axis=1)
    span_rows = jnp.sum(jnp.where(picked, piece_rows[None, :], 0), axis=1)
    return (segment, offset, span_rows)


def gelu_exact(values):
    return jax.nn.gelu(values, approximate=False)


def key_block(whole, geometry, block_index, head_count):
    query_seg, query_pos, seg_all, pos_all, block_rows, score_scale = geometry
    first_row = block_index * block_rows
    key_piece = lax.dynamic_slice_in_dim(whole, first_row, block_rows, 0)
    key_seg = lax.dynamic_slice_in_dim(seg_all, first_row, block_rows, 0)
    key_pos = lax.dynamic_slice_in_dim(pos_all, first_row, block_rows, 0)
    half_width = key_piece.shape[1] // 2
    keys_part = key_piece[:, :half_width].reshape(block_rows, head_count, -1)
    values_part = key_piece[:, half_width:].reshape(block_rows, head_count, -1)
    return (keys_part, values_part, key_seg, key_pos)


def block_scores(queries, keys_part, key_seg, key_pos, geometry):
    query_seg, query_pos, seg_all, pos_all, block_rows, score_scale = geometry
    scores = (
        jnp.einsum("qhd,khd->hqk", queries, keys_part, preferred_element_type=jnp.float32)
        * score_scale
    )
    allowed = (query_seg[:, None] == key_seg[None, :]) & (key_pos[None, :] <= query_pos[:, None])
    return (scores, allowed[None])


def attend(queries, whole, geometry):
    row_count, head_count, head_dim = queries.shape
    block_count = whole.shape[0] // geometry[4]

    def statistics(running, block_index):
        largest, totals = running
        keys_part, values_part, key_seg, key_pos = key_block(
            whole, geometry, block_index, head_count
        )
        scores, allowed = block_scores(queries, keys_part, key_seg, key_pos, geometry)
        newest = jnp.maximum(largest, jnp.max(jnp.where(allowed, scores, NEGATIVE), axis=2))
        weights = jnp.where(allowed, jnp.exp(scores - newest[:, :, None]), 0.0)
        totals = totals * jnp.exp(largest - newest) + jnp.sum(weights, axis=2)
        return ((newest, totals), None)

    initial = (
        jnp.full((head_count, row_count), NEGATIVE, jnp.float32),
        jnp.zeros((head_count, row_count), jnp.float32),
    )
    (largest, totals), unused = lax.scan(statistics, initial, jnp.arange(block_count))
    log_total = largest + jnp.log(totals)

    def weighted(output_sum, block_index):
        keys_part, values_part, key_seg, key_pos = key_block(
            whole, geometry, block_index, head_count
        )
        scores, allowed = block_scores(queries, keys_part, key_seg, key_pos, geometry)
        probs = jnp.where(allowed, jnp.exp(scores - log_total[:, :, None]), 0.0).astype(
            jnp.bfloat16
        )
        output_sum = output_sum + jnp.einsum(
            "hqk,khd->qhd", probs, values_part, preferred_element_type=jnp.float32
        )
        return (output_sum, None)

    output_sum, unused = lax.scan(
        weighted, jnp.zeros((row_count, head_count, head_dim), jnp.float32), jnp.arange(block_count)
    )
    return (output_sum, log_total)


def attend_back(queries, whole, log_total, delta_sum, grad_heads, geometry):
    row_count, head_count, head_dim = queries.shape
    block_rows = geometry[4]
    score_scale = geometry[5]
    block_count = whole.shape[0] // block_rows

    def gradients(query_grad, block_index):
        keys_part, values_part, key_seg, key_pos = key_block(
            whole, geometry, block_index, head_count
        )
        scores, allowed = block_scores(queries, keys_part, key_seg, key_pos, geometry)
        probs = jnp.where(allowed, jnp.exp(scores - log_total[:, :, None]), 0.0)
        grad_probs = jnp.einsum(
            "qhd,khd->hqk", grad_heads, values_part, preferred_element_type=jnp.float32
        )
        grad_scores = (probs * (grad_probs - delta_sum[:, :, None])).astype(jnp.bfloat16)
        query_grad = (
            query_grad
            + jnp.einsum("hqk,khd->qhd", grad_scores, keys_part, preferred_element_type=jnp.float32)
            * score_scale
        )
        key_grad = (
            jnp.einsum("hqk,qhd->khd", grad_scores, queries, preferred_element_type=jnp.float32)
            * score_scale
        )
        value_grad = jnp.einsum(
            "hqk,qhd->khd",
            probs.astype(jnp.bfloat16),
            grad_heads,
            preferred_element_type=jnp.float32,
        )
        joined = jnp.concatenate(
            [key_grad.reshape(block_rows, -1), value_grad.reshape(block_rows, -1)], axis=1
        )
        return (query_grad, joined)

    query_grad, stacked = lax.scan(
        gradients,
        jnp.zeros((row_count, head_count, head_dim), jnp.float32),
        jnp.arange(block_count),
    )
    return (query_grad, stacked.reshape(whole.shape[0], -1))


def layer_forward(hidden, layer_index, weights, geometry):
    qkv_weight, out_weight, up_weight, up_bias, down_weight, down_bias, alphas = weights
    row_count, model_width = hidden.shape
    projection = qkv_weight[layer_index]
    rounded = hidden.astype(jnp.bfloat16)
    queries = (
        jnp.dot(rounded, projection[:, :model_width], preferred_element_type=jnp.float32)
        .astype(jnp.bfloat16)
        .reshape(row_count, HEADS, -1)
    )
    key_value = jnp.dot(
        rounded, projection[:, model_width:], preferred_element_type=jnp.float32
    ).astype(jnp.bfloat16)
    whole = lax.all_gather(key_value, "blk", axis=0, tiled=True)
    heads_out, log_total = attend(queries, whole, geometry)
    heads_rounded = heads_out.reshape(row_count, model_width).astype(jnp.bfloat16)
    branch = jnp.dot(heads_rounded, out_weight[layer_index], preferred_element_type=jnp.float32)
    alpha_pair = alphas[layer_index]
    middle = hidden + alpha_pair[0] * branch
    entered = middle.astype(jnp.bfloat16)
    gate_pre = (
        jnp.dot(entered, up_weight[layer_index], preferred_element_type=jnp.float32)
        + up_bias[layer_index]
    )
    activated = gelu_exact(gate_pre).astype(jnp.bfloat16)
    second = (
        jnp.dot(activated, down_weight[layer_index], preferred_element_type=jnp.float32)
        + down_bias[layer_index]
    )
    result = middle + alpha_pair[1] * second
    saved = (
        rounded,
        queries,
        key_value,
        whole,
        heads_out,
        heads_rounded,
        log_total,
        branch,
        entered,
        gate_pre,
        activated,
        second,
    )
    return (result, saved)


def layer_backward(grad_hidden, saved, layer_index, weights, geometry):
    qkv_weight, out_weight, up_weight, up_bias, down_weight, down_bias, alphas = weights
    (
        rounded,
        queries,
        key_value,
        saved_whole,
        heads_out,
        heads_rounded,
        log_total,
        branch,
        entered,
        gate_pre,
        activated,
        second,
    ) = saved
    row_count = grad_hidden.shape[0]
    alpha_pair = alphas[layer_index]
    grad_second = (alpha_pair[1] * grad_hidden).astype(jnp.bfloat16)
    alpha_second = jnp.sum(grad_hidden * second)
    bias_down = jnp.sum(grad_second.astype(jnp.float32), axis=0)
    grad_down = jnp.einsum("tf,td->fd", activated, grad_second, preferred_element_type=jnp.float32)
    grad_act = jnp.einsum(
        "td,fd->tf", grad_second, down_weight[layer_index], preferred_element_type=jnp.float32
    )
    unused, gelu_pull = jax.vjp(gelu_exact, gate_pre)
    grad_gate = gelu_pull(grad_act)[0].astype(jnp.bfloat16)
    bias_up = jnp.sum(grad_gate.astype(jnp.float32), axis=0)
    grad_up = jnp.einsum("td,tf->df", entered, grad_gate, preferred_element_type=jnp.float32)
    grad_middle = grad_hidden + jnp.einsum(
        "tf,df->td", grad_gate, up_weight[layer_index], preferred_element_type=jnp.float32
    )
    grad_branch = (alpha_pair[0] * grad_middle).astype(jnp.bfloat16)
    alpha_first = jnp.sum(grad_middle * branch)
    grad_proj_out = jnp.einsum(
        "te,td->ed", heads_rounded, grad_branch, preferred_element_type=jnp.float32
    )
    grad_heads = (
        jnp.einsum(
            "td,ed->te", grad_branch, out_weight[layer_index], preferred_element_type=jnp.float32
        )
        .astype(jnp.bfloat16)
        .reshape(queries.shape)
    )
    delta_sum = jnp.sum(grad_heads.astype(jnp.float32) * heads_out, axis=2).T
    whole = lax.all_gather(key_value, "blk", axis=0, tiled=True)
    query_grad, key_terms = attend_back(queries, whole, log_total, delta_sum, grad_heads, geometry)
    key_grads = lax.psum_scatter(
        key_terms.astype(jnp.bfloat16), "blk", scatter_dimension=0, tiled=True
    )
    grad_proj = jnp.concatenate(
        [query_grad.reshape(row_count, -1).astype(jnp.bfloat16), key_grads], axis=1
    )
    grad_qkv = jnp.einsum("td,te->de", rounded, grad_proj, preferred_element_type=jnp.float32)
    grad_input = grad_middle + jnp.einsum(
        "te,de->td", grad_proj, qkv_weight[layer_index], preferred_element_type=jnp.float32
    )
    layer_grads = (
        grad_qkv,
        grad_proj_out,
        grad_up,
        bias_up,
        grad_down,
        bias_down,
        jnp.stack([alpha_first, alpha_second]),
    )
    return (grad_input, layer_grads)


def reduce_all(layer_results, cycle_size):
    stacked = [
        jnp.stack([layer_entry[member] for layer_entry in layer_results], axis=0)
        for member in range(6)
    ]
    alpha_tiles = jnp.stack(
        [jnp.tile(layer_entry[6], cycle_size) for layer_entry in layer_results], axis=0
    )
    shares = (
        lax.psum_scatter(
            stacked[0].astype(jnp.bfloat16), "blk", scatter_dimension=1, tiled=True
        ).astype(jnp.float32),
        lax.psum_scatter(
            stacked[1].astype(jnp.bfloat16), "blk", scatter_dimension=1, tiled=True
        ).astype(jnp.float32),
        lax.psum_scatter(
            stacked[2].astype(jnp.bfloat16), "blk", scatter_dimension=1, tiled=True
        ).astype(jnp.float32),
        lax.psum_scatter(
            stacked[3].astype(jnp.bfloat16), "blk", scatter_dimension=1, tiled=True
        ).astype(jnp.float32),
        lax.psum_scatter(
            stacked[4].astype(jnp.bfloat16), "blk", scatter_dimension=1, tiled=True
        ).astype(jnp.float32),
        lax.psum_scatter(
            stacked[5].astype(jnp.bfloat16), "blk", scatter_dimension=1, tiled=True
        ).astype(jnp.float32),
        lax.psum_scatter(
            alpha_tiles.astype(jnp.bfloat16), "blk", scatter_dimension=1, tiled=True
        ).astype(jnp.float32),
    )
    return (
        lax.psum(shares[0].astype(jnp.bfloat16), "grp").astype(jnp.float32),
        lax.psum(shares[1].astype(jnp.bfloat16), "grp").astype(jnp.float32),
        lax.psum(shares[2].astype(jnp.bfloat16), "grp").astype(jnp.float32),
        lax.psum(shares[3].astype(jnp.bfloat16), "grp").astype(jnp.float32),
        lax.psum(shares[4].astype(jnp.bfloat16), "grp").astype(jnp.float32),
        lax.psum(shares[5].astype(jnp.bfloat16), "grp").astype(jnp.float32),
        lax.psum(shares[6].astype(jnp.bfloat16), "grp").astype(jnp.float32),
    )


def body(
    tokens,
    seq_len,
    qkv_weight,
    out_weight,
    up_weight,
    up_bias,
    down_weight,
    down_bias,
    alphas,
    cotangent,
):
    row_count, model_width = tokens.shape
    cycle_size = lax.axis_size("blk")
    cycle_place = lax.axis_index("blk")
    head_dim = model_width // HEADS
    total_rows = cycle_size * row_count
    block_rows = min(max(row_count, 512), total_rows)
    segment, offset, span_rows = layout(seq_len, row_count, cycle_size)
    query_pos = cycle_place * span_rows + offset
    seg_all = jnp.tile(segment, cycle_size)
    pos_all = jnp.repeat(jnp.arange(cycle_size, dtype=jnp.int32), row_count) * jnp.tile(
        span_rows, cycle_size
    ) + jnp.tile(offset, cycle_size)
    geometry = (segment, query_pos, seg_all, pos_all, block_rows, head_dim ** (-0.5))
    weights = (qkv_weight, out_weight, up_weight, up_bias, down_weight, down_bias, alphas)
    hidden = tokens.astype(jnp.float32)
    saved_layers = []
    for layer_index in range(LAYERS):
        hidden, saved = layer_forward(hidden, layer_index, weights, geometry)
        saved_layers.append(saved)
    output = hidden.astype(jnp.bfloat16)
    grad_hidden = cotangent.astype(jnp.float32)
    layer_results = []
    for layer_index in reversed(range(LAYERS)):
        grad_hidden, layer_grads = layer_backward(
            grad_hidden, saved_layers[layer_index], layer_index, weights, geometry
        )
        layer_results.insert(0, layer_grads)
    finals = reduce_all(layer_results, cycle_size)
    return (
        output,
        grad_hidden,
        finals[0],
        finals[1],
        finals[2],
        finals[3],
        finals[4],
        finals[5],
        finals[6],
    )


def solution(mesh):
    placed = (
        P(("grp", "blk"), None),
        P("grp", None),
        P(),
        P(),
        P(),
        P(),
        P(),
        P(),
        P(),
        P(("grp", "blk"), None),
    )
    sizes = (mesh.shape["grp"], mesh.shape["blk"])
    return jax.shard_map(
        fast_body if sizes == (4, RUNS) else body,
        mesh=mesh,
        in_specs=placed,
        out_specs=(
            P(("grp", "blk"), None),
            P(("grp", "blk"), None),
            P(None, "blk", None),
            P(None, "blk", None),
            P(None, "blk", None),
            P(None, "blk"),
            P(None, "blk", None),
            P(None, "blk"),
            P(),
        ),
        check_vma=False,
    )
```

```python
import functools

import jax
import jax.numpy as jnp
from jax import lax
from jax.experimental import pallas as pl
from jax.experimental.pallas import tpu as pltpu
from jax.sharding import PartitionSpec as P

HEADS = 8
LAYERS = 2
NEGATIVE = -1e30
MESH = pl.DeviceIdType.MESH
F32 = jnp.float32
BF16 = jnp.bfloat16

HALF = 128
RUNS = 8
TEAM = 4
OWN = RUNS // TEAM
DIM = 64
WIDTH = 512
FF = 2048
CUT = 512
TILE = 256
TILES = HALF * RUNS // TILE
PACK = HALF + DIM
CHUNK = 576
SMALL = FF + WIDTH + 128
PARTS = ((1, 0, 320), (1, 320, 256), (0, 0, 320), (0, 320, 256))
SHARES = ((192, 0, 128), (160, 16, 80), (160, 128, 32), (128, 96, 32))


def spans():
    places, totals = {}, [0, 0, 0]
    for part, counts in enumerate(SHARES):
        first = PARTS[part][1]
        for route, count in enumerate(counts):
            places[part, route] = (first, totals[route], count)
            first += count
            totals[route] += count
    return places, totals


SPANS, TOTALS = spans()

SLOPE_AT = 0.28
TAIL = (
    0.11652077851573843,
    0.06749675579450809,
    0.2689101589486142,
    -0.23699347299932225,
    0.3898740127620002,
    -0.10580824228351815,
)


def nn(a, b):
    return lax.dot_general(a, b, (((1,), (0,)), ((), ())), preferred_element_type=F32)


def nt(a, b):
    return lax.dot_general(a, b, (((1,), (1,)), ((), ())), preferred_element_type=F32)


def beside(first, other):
    low = lax.broadcasted_iota(jnp.int32, first.shape, 1) < DIM
    return (
        jnp.where(low, first, pltpu.roll(other, DIM, 1)),
        jnp.where(low, pltpu.roll(first, DIM, 1), other),
    )


def layers_kernel(
    tokens, seq_len_hbm, alphas_hbm, up_bias_hbm, down_bias_hbm, cotangent, qkv_hbm, out_hbm, up_hbm, down_hbm,
    final, heads_all, out_in, grad_in, small_final,
    seq_len, alphas, wqkv, wout, wup, wdown, up_bias, down_bias,
    tok_in, cot_in, flag_out, flag_in, back_out,
    hidden, grad, hid_all, attn_t, entered, act, branch, slope, second,
    dz, du, da, dqkv,
    pack_out, head_out, pack_in, o_in, do_in,
    kv, kv_t, rq, ro, o_t, probs, acc, dq_t, bias,
    parts, core_in, xa_in, xb_in, ya_in, yb_in, z_in, third_z, third_x, third_y,
    heads_out, heads_x, heads_z, heads_sum, small, small_in, small_z, small_sum,
    w_sem, move_send, move_recv, a2a_send, a2a_recv, core_send, core_recv, x_send, x_recv, y_send, y_recv,
    z_send, z_recv, fin_send, fin_recv, hid_send, hid_recv, hx_send, hx_recv, hz_send, hz_recv, hf_send, hf_recv,
    small_send, small_recv, core_free,
):
    grp = lax.axis_index("grp")
    blk = lax.axis_index("blk")
    core = lax.rem(grp, 2)
    side = lax.div(grp, 2)
    yy = lax.rem(blk, 2)
    zz = lax.div(blk, 2)
    member = 2 * core + yy
    far_side = 2 * (1 - side) + core

    def place(c, x, z, y):
        return (2 * x + c, 2 * z + y)

    core_peer = place(1 - core, side, zz, yy)
    x_peer = place(core, 1 - side, zz, yy)
    y_peer = place(core, side, zz, 1 - yy)

    def remote(source, target, send, recv, peer):
        return pltpu.make_async_remote_copy(
            src_ref=source,
            dst_ref=target,
            send_sem=send,
            recv_sem=recv,
            device_id=peer,
            device_id_type=MESH,
        )

    def credit(semaphore, peer, count=1):
        pl.semaphore_signal(semaphore, inc=count, device_id=peer, device_id_type=MESH)

    def moved(kind, slot, source, target, at, core_at, z_at):
        here = jnp.logical_and(core_at == core, z_at == zz)

        @pl.when(here)
        def _():
            pltpu.make_async_copy(source, target.at[at], move_recv.at[kind, at]).start()

        @pl.when(jnp.logical_not(here))
        def _():
            pltpu.make_async_remote_copy(
                src_ref=source,
                dst_ref=target.at[at],
                send_sem=move_send.at[kind, slot],
                recv_sem=move_recv.at[kind, at],
                device_id=place(core_at, side, z_at, yy),
                device_id_type=MESH,
            ).start()

    def move_left(kind, slot, source, core_at, z_at):
        here = jnp.logical_and(core_at == core, z_at == zz)

        @pl.when(jnp.logical_not(here))
        def _():
            pltpu.make_async_copy(source, source, move_send.at[kind, slot]).wait()

    def move_arrived(kind, at, target):
        pltpu.make_async_copy(target.at[at], target.at[at], move_recv.at[kind, at]).wait()

    def to_team(kind, half, source, target):
        moved(kind, half, source, target, lax.div(zz, 2), lax.rem(zz, 2), 2 * half + core)

    def to_team_left(kind, half, source):
        move_left(kind, half, source, lax.rem(zz, 2), 2 * half + core)

    def to_owner(kind, chunk, source, target):
        moved(kind, chunk, source, target, lax.div(zz, 2), lax.rem(zz, 2), core + 2 * chunk)

    def to_owner_left(kind, chunk, source):
        move_left(kind, chunk, source, lax.rem(zz, 2), core + 2 * chunk)

    def half_of(ref, half):
        return ref.at[pl.ds(pl.multiple_of(HALF * half, HALF), HALF)]

    def rows_of(half):
        return pl.ds(pl.multiple_of(half * HALF, HALF), HALF)

    def slot_of(other):
        return lax.rem(other + TEAM - member, TEAM)

    def exchange(kind, layer, half, outgoing, incoming, head=None):
        at = () if head is None else (head,)
        incoming[(half, 0, *at)] = outgoing[(half, member, *at)]
        for step in range(1, TEAM):
            peer = lax.rem(member + step, TEAM)
            remote(
                outgoing.at[(half, peer, *at)],
                incoming.at[(half, TEAM - step, *at)],
                a2a_send.at[kind, layer, half, head or 0],
                a2a_recv.at[kind, layer, half, head or 0],
                place(lax.div(peer, 2), side, zz, lax.rem(peer, 2)),
            ).start()

    def arrived(kind, layer, half, incoming, head=None):
        at = () if head is None else (head,)
        whole = incoming.at[(half, pl.ds(1, TEAM - 1), *at)]
        pltpu.make_async_copy(whole, whole, a2a_recv.at[kind, layer, half, head or 0]).wait()

    def left(kind, layer, half, outgoing):
        for head in range(OWN) if kind in (0, 3) else (None,):
            at = () if head is None else (head,)
            whole = outgoing.at[(half, pl.ds(1, TEAM - 1), *at)]
            pltpu.make_async_copy(whole, whole, a2a_send.at[kind, layer, half, head or 0]).wait()

    def tokens_of(chunk, other):
        return pl.ds(pl.multiple_of(HALF * (TEAM * chunk + other), HALF), HALF)

    def hidden_copy(layer, chunk, which):
        whose = 2 * core + 1 - yy if which == 2 else member
        block = hid_all.at[layer, :, tokens_of(chunk, whose)]
        return remote(
            block,
            block,
            hid_send.at[layer, chunk, which],
            hid_recv.at[layer, chunk, which],
            y_peer if which == 0 else core_peer,
        )

    def hidden_start(layer, chunk):
        for which in range(2):
            hidden_copy(layer, chunk, which).start()

    def hidden_pass(layer, chunk):
        hidden_copy(layer, chunk, 0).wait()
        hidden_copy(layer, chunk, 2).start()

    def hidden_done(layer, chunk):
        for which in range(1, 3):
            hidden_copy(layer, chunk, which).wait()

    def project(layer, half):
        rows = rows_of(half)
        rounded = hidden[rows, :].astype(BF16)
        if layer == 1:
            left(0, 0, half, pack_out)
        queries = (nn(rounded, wqkv[layer, :, 0:WIDTH]) * (DIM ** -0.5)).astype(BF16).T
        for head in range(RUNS):
            pack_out[half, head // 2, head % 2, HALF:, :] = queries[DIM * head : DIM * head + DIM, :]
        for step in range(2):
            at = WIDTH * (step + 1)
            keys_values = nn(rounded, wqkv[layer, :, at : at + WIDTH]).astype(BF16)
            for head in range(4):
                pack_out[half, 2 * step + head // 2, head % 2, 0:HALF, :] = keys_values[
                    :, 128 * head : 128 * head + 128
                ]
        for head in range(OWN):
            exchange(0, layer, half, pack_out, pack_in, head)
        hid_all[layer, :, tokens_of(half, member)] = rounded.T

    def rows_before(i):
        return TILE * i * (i + 1) // 2

    def attend(layer, chunk):
        if layer == 1:
            left(1, 0, chunk, head_out)

        def one_head(head, carry):
            arrived(0, layer, chunk, pack_in, head)
            for other in range(TEAM):
                slot = slot_of(other)
                start = HALF * (TEAM * chunk + other)
                span = slice(start, start + HALF)
                block = pack_in[chunk, slot, head, 0:HALF, :]
                kv[layer, head, span, :] = block
                kv_t[layer, head, :, span] = block.T
                rq[layer, head, 0:DIM, span] = pack_in[chunk, slot, head, HALF:, :]

            def scores_of(i):
                count = TILE * (i + 1)
                tile = rq[layer, head, :, TILE * i : TILE * i + TILE]
                return nn(kv[layer, head, 0:count, :], tile) + bias[TILE * TILES - count :, :]

            ahead = [scores_of(i) for i in (2 * chunk, 2 * chunk + 1)]
            for i in (2 * chunk, 2 * chunk + 1):
                columns = slice(TILE * i, TILE * i + TILE)
                count = TILE * (i + 1)
                scores = ahead[i - 2 * chunk]
                largest = jnp.max(scores, axis=0, keepdims=True)
                weight = jnp.exp(scores - largest)
                total = jnp.sum(weight, axis=0, keepdims=True)
                share = (weight * (1.0 / total)).astype(BF16)
                probs[layer, head, rows_before(i) : rows_before(i) + count, :] = share
                summed = nn(kv_t[layer, head, DIM:, 0:count], share)
                o_t[layer, head, :, columns] = summed
                rounded = summed.astype(BF16)
                for part in range(2):
                    head_out[chunk, 2 * (i - 2 * chunk) + part, head] = rounded[
                        :, HALF * part : HALF * part + HALF
                    ]
            return carry

        for head in range(OWN):
            one_head(head, 0)
        exchange(1, layer, chunk, head_out, o_in)

    def feed(layer, half):
        rows = rows_of(half)
        arrived(1, layer, half, o_in)
        for head in range(RUNS):
            attn_t[layer, DIM * head : DIM * head + DIM, rows] = o_in[half, slot_of(head // 2), head % 2]
        attn = attn_t[layer, :, rows].T
        grown = nn(attn, wout[layer])
        branch[layer, rows, :] = grown
        middle = hidden[rows, :] + alphas[layer, 0] * grown
        rounded = middle.astype(BF16)
        entered[layer, rows, :] = rounded
        total = jnp.zeros((HALF, WIDTH), F32)

        def gate_of(step):
            cut = slice(CUT * step, CUT * step + CUT)
            return nn(rounded, wup[layer, :, cut]) + up_bias[layer : layer + 1, cut]

        coming = gate_of(0)
        for step in range(FF // CUT):
            cut = slice(CUT * step, CUT * step + CUT)
            gate = coming
            if step + 1 < FF // CUT:
                coming = gate_of(step + 1)
            bell = jnp.exp(gate * gate * -0.5)
            near = pl.reciprocal(1.0 + SLOPE_AT * jnp.abs(gate), approx=True)
            tail = jnp.full_like(gate, TAIL[5])
            for factor in TAIL[4::-1]:
                tail = tail * near + factor
            tail = bell * (tail * near)
            risen = jnp.where(gate > 0.0, 1.0 - tail, tail)
            slope[layer, rows, cut] = risen + gate * bell * 0.3989422804014327
            active = (gate * risen).astype(BF16)
            act[layer, rows, cut] = active
            total = total + nn(active, wdown[layer, cut, :])
        total = total + down_bias[layer : layer + 1, :]
        second[layer, rows, :] = total
        hidden[rows, :] = middle + alphas[layer, 1] * total

    def total_of(values):
        return jnp.sum(jnp.sum(values, axis=0, keepdims=True), axis=1, keepdims=True)

    def feed_back(layer):
        start = grad[...]
        if layer == 0:
            dz[...] = (alphas[layer, 1] * start).astype(BF16)
        scaled = dz[...]
        alpha_second = total_of(start * second[layer])
        small[layer : layer + 1, FF : FF + WIDTH] = jnp.sum(scaled.astype(F32), axis=0, keepdims=True)
        middle = start
        coming = nt(scaled, wdown[layer, 0:CUT, :])
        for step in range(FF // CUT):
            cut = slice(CUT * step, CUT * step + CUT)
            raw = coming
            if step + 1 < FF // CUT:
                coming = nt(scaled, wdown[layer, CUT * (step + 1) : CUT * (step + 2), :])
            gate = (raw * slope[layer, :, cut]).astype(BF16)
            du[:, cut] = gate
            small[layer : layer + 1, cut] = jnp.sum(gate.astype(F32), axis=0, keepdims=True)
            middle = middle + nt(gate, wup[layer, :, cut])
        grad[...] = middle
        mixed = (alphas[layer, 0] * middle).astype(BF16)
        da[...] = mixed
        spread = nt(wout[layer], mixed).astype(BF16)
        for chunk in (1, 0):
            left(*((1, 1) if layer == 1 else (2, 1)), chunk, head_out)
            for head in range(RUNS):
                head_out[chunk, head // 2, head % 2] = spread[
                    DIM * head : DIM * head + DIM, HALF * chunk : HALF * chunk + HALF
                ]
            exchange(2, layer, chunk, head_out, do_in)
        alpha_first = total_of(middle * branch[layer])
        column = lax.broadcasted_iota(jnp.int32, (1, 128), 1)
        small[layer : layer + 1, FF + WIDTH :] = jnp.where(
            column == 0, alpha_first, jnp.where(column == 1, alpha_second, 0.0)
        )

    def attend_back(layer, chunk):
        arrived(2, layer, chunk, do_in)
        left(*((0, 1) if layer == 1 else (3, 1)), chunk, pack_out)

        def one_head(head, carry):
            for other in range(TEAM):
                start = HALF * (TEAM * chunk + other)
                ro[head, DIM:, start : start + HALF] = do_in[chunk, slot_of(other), head]
            for i in (2 * chunk, 2 * chunk + 1):
                columns = slice(TILE * i, TILE * i + TILE)
                query_tile = rq[layer, head, :, columns]
                grad_tile = ro[head, :, columns]
                delta = jnp.sum(
                    ro[head, DIM:, columns].astype(F32) * o_t[layer, head, :, columns],
                    axis=0,
                    keepdims=True,
                )
                count = TILE * (i + 1)
                keys = kv[layer, head, 0:count, :]
                share = probs[layer, head, rows_before(i) : rows_before(i) + count, :]
                scored = (share.astype(F32) * (nn(keys, grad_tile) - delta)).astype(BF16)
                term = nt(scored, query_tile) + nt(share, grad_tile)
                if chunk == 1 and i == 2:
                    acc[head, 0:count, :] = term
                elif chunk == 1:
                    acc[head, 0 : count - TILE, :] += term[0 : count - TILE, :]
                    acc[head, count - TILE : count, :] = term[count - TILE :, :]
                else:
                    acc[head, 0:count, :] += term
                query_grad = nn(kv_t[layer, head, 0:DIM, 0:count], scored)
                dq_t[head, :, columns] = query_grad * (DIM ** -0.5)
            for other in range(TEAM):
                start = HALF * (TEAM * chunk + other)
                span = slice(start, start + HALF)
                pack_out[chunk, other, head, 0:HALF, :] = acc[head, span, :].astype(BF16)
                pack_out[chunk, other, head, HALF:, :] = dq_t[head, :, span].astype(BF16)
            exchange(3, layer, chunk, pack_out, pack_in, head)
            return carry

        for head in range(OWN):
            one_head(head, 0)

    def project_back(layer, half):
        for head in range(OWN):
            arrived(3, layer, half, pack_in, head)
        turned = jnp.concatenate(
            [pack_in[half, slot_of(head // 2), head % 2, HALF:, :] for head in range(RUNS)], axis=0
        )
        dqkv[:, 0:WIDTH] = turned.T
        for head in range(RUNS):
            at = WIDTH + 128 * head
            dqkv[:, at : at + 128] = pack_in[half, slot_of(head // 2), head % 2, 0:HALF, :]
        rows = rows_of(half)
        grad[rows, :] = grad[rows, :] + nt(dqkv[...], wqkv[layer])

    def scatter_rows(layer, result, first_row):
        for run in range(RUNS):
            for quarter in range(4):
                parts[layer, quarter % 2, quarter // 2, run // 2, run % 2, first_row : first_row + DIM, :] = result[
                    DIM * run : DIM * run + DIM, 128 * quarter : 128 * quarter + 128
                ].astype(BF16)

    def make(part):
        layer, first, count = PARTS[part]
        if first < 256:
            turned = entered[layer].T
        for row in range(first, min(first + count, 256), DIM):
            step = row // DIM
            scatter_rows(layer, nn(turned, du[:, CUT * step : CUT * step + CUT]), row)
        if first <= 256 < first + count:
            scatter_rows(layer, nn(attn_t[layer], da[...]), 256)
        if first >= 320:
            turned = dz[...].T
            for step in range(FF // CUT):
                result = nn(turned, act[layer, :, CUT * step : CUT * step + CUT])
                for block in range(CUT // 128):
                    run, row = 2 * step + block // 2, 320 + 128 * (block % 2)
                    for quarter in range(4):
                        parts[layer, quarter % 2, quarter // 2, run // 2, run % 2, row : row + 128, :] = result[
                            128 * quarter : 128 * quarter + 128, 128 * block : 128 * block + 128
                        ].astype(BF16)
        if layer == 0:
            pl.semaphore_wait(core_free.at[0 if first < 320 else 1], 1)
        core_copy(part).start()

    def heads_grads(layer):
        for chunk in range(2):
            hidden_done(layer, chunk)
        blocks = [(run // TEAM, run % TEAM) for run in range(RUNS)]
        keys_values = jnp.concatenate(
            [
                jnp.concatenate([pack_out[chunk, other, head, 0:HALF, :] for chunk, other in blocks], axis=0)
                for head in range(OWN)
            ],
            axis=1,
        )
        queries = jnp.concatenate(
            [
                jnp.concatenate([pack_out[chunk, other, head, HALF:, :] for chunk, other in blocks], axis=1)
                for head in range(OWN)
            ],
            axis=0,
        )
        both = nn(hid_all[layer], keys_values)
        q_part = nt(hid_all[layer], queries)
        for number, values in enumerate((q_part, both[:, 0:128], both[:, 128:256])):
            for run in range(RUNS):
                heads_out[layer, run // 2, run % 2, :, 128 * number : 128 * number + 128] = values[
                    DIM * run : DIM * run + DIM, :
                ].astype(BF16)
        heads_x_copy(layer).start()

    def half_rows(which):
        return pl.ds(pl.multiple_of(32 * which, 32), 32)

    def heads_x_copy(layer):
        return remote(
            heads_out.at[layer, :, :, half_rows(1 - side)],
            heads_x.at[layer],
            hx_send.at[layer],
            hx_recv.at[layer],
            x_peer,
        )

    def heads_z_copy(layer, step):
        peer = lax.rem(zz + step, 4)
        return remote(
            heads_out.at[layer, peer, :, half_rows(side)],
            heads_z.at[layer, 4 - step],
            hz_send.at[layer, step],
            hz_recv.at[layer, 4 - step],
            place(core, side, peer, yy),
        )

    def heads_last_copy(layer, number):
        x, c, y = number // 4, number // 2 % 2, number % 2
        return remote(
            heads_sum.at[layer, 1 - yy if y else yy],
            heads_all.at[layer, side, member],
            hf_send.at[layer, number],
            hf_recv.at[layer, number],
            place(1 - core if c else core, 1 - side if x else side, zz, 1 - yy if y else yy),
        )

    def heads_second(layer):
        heads_x_copy(layer).wait()
        heads_out[layer, :, :, half_rows(side), :] += heads_x[layer]
        for step in range(1, 4):
            heads_z_copy(layer, step).start()

    def heads_third(layer):
        for step in range(1, 4):
            heads_z_copy(layer, step).wait()
        total = heads_out[layer, zz, :, half_rows(side), :].astype(F32)
        for slot in range(1, 4):
            total = total + heads_z[layer, slot].astype(F32)
        heads_sum[layer] = total.astype(BF16)
        heads_all[layer, side, member] = heads_sum[layer, yy]
        for number in range(1, 8):
            heads_last_copy(layer, number).start()

    def heads_done(layer):
        for number in range(1, 8):
            heads_last_copy(layer, number).wait()

    def rows_in(part, route):
        first, room, count = SPANS[part, route]
        return pl.ds(first, count), pl.ds(room, count)

    def used(part, route):
        return SHARES[part][route] > 0

    def core_copy(part):
        layer, first, count = PARTS[part]
        rows = pl.ds(first, count)
        return remote(
            parts.at[layer, 1 - core, :, :, :, rows],
            core_in.at[:, :, :, rows],
            core_send.at[part],
            core_recv.at[part],
            core_peer,
        )

    def x_copy(part, route):
        layer = PARTS[part][0]
        rows, room = rows_in(part, route)
        ends = (x_send.at[part, route], x_recv.at[part, route], x_peer)
        mine = parts.at[layer, core, 1 - side]
        if route == 0:
            return remote(mine.at[:, :, rows], xa_in.at[:, :, room], *ends)
        if route == 1:
            return remote(mine.at[:, yy, rows], xb_in.at[:, room], *ends)
        return remote(mine.at[zz, :, rows], third_x.at[:, room], *ends)

    def y_copy(part, route):
        layer = PARTS[part][0]
        rows, room = rows_in(part, route)
        ends = (y_send.at[part, route], y_recv.at[part, route], y_peer)
        mine = parts.at[layer, core]
        if route == 0:
            return remote(mine.at[side, :, 1 - yy, rows], ya_in.at[:, room], *ends)
        if route == 1:
            return remote(mine.at[:, :, 1 - yy, rows], yb_in.at[:, :, room], *ends)
        return remote(mine.at[side, zz, 1 - yy, rows], third_y.at[room], *ends)

    def z_copy(part, route, step):
        layer = PARTS[part][0]
        rows, room = rows_in(part, route)
        peer = lax.rem(zz + step, 4)
        ends = (z_send.at[part, route, step], z_recv.at[part, route, 4 - step], place(core, side, peer, yy))
        if route == 2:
            return remote(parts.at[layer, core, :, peer, :, rows], third_z.at[4 - step, :, :, room], *ends)
        return remote(parts.at[layer, core, side, peer, yy, rows], z_in.at[layer, 4 - step, rows], *ends)

    def final_copy(part, which):
        layer, first, count = PARTS[part]
        block = final.at[layer, far_side if which == 2 else grp, pl.ds(first, count)]
        return remote(
            block,
            block,
            fin_send.at[part, which],
            fin_recv.at[part, which],
            x_peer if which == 0 else core_peer,
        )

    def core_done(part):
        layer, first, count = PARTS[part]
        rows = pl.ds(first, count)
        core_copy(part).wait()
        for across in (1 - side, side):
            parts[layer, core, across, :, :, rows, :] += core_in[across, :, :, rows, :]
            if used(part, 0) and across is not side:
                x_copy(part, 0).start()
        if used(part, 1):
            y_copy(part, 1).start()
        if used(part, 2):
            for step in range(1, 4):
                z_copy(part, 2, step).start()
        if layer == 1:
            freed = 0 if first < 320 else 1
            followers = [1 for other in PARTS if other[0] == 0 and (other[1] >= 320) == (freed == 1)]
            credit(core_free.at[freed], core_peer, len(followers))

    def first_x(part):
        if used(part, 0):
            layer = PARTS[part][0]
            rows, room = rows_in(part, 0)
            x_copy(part, 0).wait()
            for y in (1 - yy, yy):
                parts[layer, core, side, :, y, rows, :] += xa_in[:, y, room, :]
                if y is not yy:
                    y_copy(part, 0).start()

    def first_y(part):
        if used(part, 1):
            layer = PARTS[part][0]
            rows, room = rows_in(part, 1)
            y_copy(part, 1).wait()
            for across in (1 - side, side):
                parts[layer, core, across, :, yy, rows, :] += yb_in[across, :, room, :]
                if across is not side:
                    x_copy(part, 1).start()

    def first_z(part):
        if used(part, 2):
            layer = PARTS[part][0]
            rows, room = rows_in(part, 2)
            for step in range(1, 4):
                z_copy(part, 2, step).wait()
            for across in (1 - side, side):
                total = parts[layer, core, across, zz, :, rows, :].astype(F32)
                for slot in range(1, 4):
                    total = total + third_z[slot, across, :, room, :].astype(F32)
                parts[layer, core, across, zz, :, rows, :] = total.astype(BF16)
                if across is not side:
                    x_copy(part, 2).start()

    def second_x(part):
        if used(part, 0):
            layer = PARTS[part][0]
            rows, room = rows_in(part, 0)
            y_copy(part, 0).wait()
            parts[layer, core, side, :, yy, rows, :] += ya_in[:, room, :]
            for step in range(1, 4):
                z_copy(part, 0, step).start()

    def second_y(part):
        if used(part, 1):
            layer = PARTS[part][0]
            rows, room = rows_in(part, 1)
            x_copy(part, 1).wait()
            parts[layer, core, side, :, yy, rows, :] += xb_in[:, room, :]
            for step in range(1, 4):
                z_copy(part, 1, step).start()

    def second_z(part):
        if used(part, 2):
            layer = PARTS[part][0]
            rows, room = rows_in(part, 2)
            x_copy(part, 2).wait()
            for y in (1 - yy, yy):
                parts[layer, core, side, zz, y, rows, :] += third_x[y, room, :]
                if y is not yy:
                    y_copy(part, 2).start()

    def third_done(part):
        layer = PARTS[part][0]
        for route in range(3):
            if not used(part, route):
                continue
            rows, room = rows_in(part, route)
            if route == 2:
                y_copy(part, 2).wait()
                final[layer, grp, rows, :] = parts[layer, core, side, zz, yy, rows, :] + third_y[room, :]
            else:
                for step in range(1, 4):
                    z_copy(part, route, step).wait()
                total = parts[layer, core, side, zz, yy, rows, :].astype(F32)
                for slot in range(1, 4):
                    total = total + z_in[layer, slot, rows, :].astype(F32)
                final[layer, grp, rows, :] = total.astype(BF16)
        if PARTS[part][1] >= 320:
            for row in (320, 448):
                final[layer, grp, row : row + 128, :] = final[layer, grp, row : row + 128, :].T
        for which in range(2):
            final_copy(part, which).start()

    def final_pass(part):
        final_copy(part, 0).wait()
        final_copy(part, 2).start()

    def final_done(part):
        for which in range(1, 3):
            final_copy(part, which).wait()

    def small_copy(stage):
        peer = (core_peer, x_peer, y_peer)[stage]
        return remote(
            small_sum.at[stage], small_in.at[stage], small_send.at[stage], small_recv.at[stage], peer
        )

    def small_z_copy(step):
        return remote(
            small_z.at[zz],
            small_z.at[zz],
            small_send.at[2 + step],
            small_recv.at[2 + step],
            place(core, side, lax.rem(zz + step, 4), yy),
        )

    def small_start():
        small_sum[0] = small[...]
        small_copy(0).start()

    def small_next(stage):
        small_copy(stage).wait()
        total = small_sum[stage] + small_in[stage]
        if stage < 2:
            small_sum[stage + 1] = total
            small_copy(stage + 1).start()
        else:
            small_z[zz] = total
            for step in range(1, 4):
                small_z_copy(step).start()

    def small_done():
        for step in range(1, 4):
            small_z_copy(step).wait()
        small_sum[0] = (small_z[0] + small_z[1]) + (small_z[2] + small_z[3])
        small_final[:, 0:256] = small_sum[0, :, pl.ds(pl.multiple_of(blk * 256, 256), 256)]
        pair = small_sum[0, :, pl.ds(pl.multiple_of(FF + 128 * zz, 128), 128)]
        small_final[:, 256:384] = jnp.where(yy == 1, pltpu.roll(pair, DIM, 1), pair)
        small_final[:, 384:512] = small_sum[0, :, FF + WIDTH :]

    def halves(*phases, first=0):
        def both(step, carry):
            for phase in phases:
                phase(lax.rem(step + first, 2))
            return carry

        lax.fori_loop(0, 2, both, 0)

    def begin(half):
        move_arrived(0, half, tok_in)
        hidden[rows_of(half), :] = tok_in[half].astype(F32)

    def finish(half):
        back_out[0, half] = hidden[rows_of(half), :].astype(BF16)
        to_owner(3, half, back_out.at[0, half], out_in)

    def turn_round(layer, half):
        move_arrived(2, half, cot_in)
        rows = rows_of(half)
        grad[rows, :] = cot_in[half].astype(F32)
        dz[rows, :] = (alphas[layer, 1] * grad[rows, :]).astype(BF16)

    def hand_back(half):
        back_out[1, half] = grad[rows_of(half), :].astype(BF16)
        to_owner(4, half, back_out.at[1, half], grad_in)

    barrier = pltpu.get_barrier_semaphore()
    for step in range(1, 4):
        credit(barrier, place(core, side, lax.rem(zz + step, 4), yy))
    for step in range(4):
        credit(barrier, place(1 - core, side, lax.rem(zz + step, 4), yy))
    for peer in (
        x_peer,
        y_peer,
        place(1 - core, side, zz, 1 - yy),
        place(1 - core, 1 - side, zz, yy),
        place(core, 1 - side, zz, 1 - yy),
        place(1 - core, 1 - side, zz, 1 - yy),
    ):
        credit(barrier, peer)

    weight_copies = {}
    for layer in range(LAYERS):
        for number, (source, target) in enumerate(
            ((qkv_hbm, wqkv), (out_hbm, wout), (up_hbm, wup), (down_hbm, wdown))
        ):
            weight_copies[layer, number] = pltpu.make_async_copy(
                source.at[layer], target.at[layer], w_sem.at[layer, number]
            )
    bias_copies = [
        pltpu.make_async_copy(up_bias_hbm, up_bias, w_sem.at[2, 0]),
        pltpu.make_async_copy(down_bias_hbm, down_bias, w_sem.at[2, 1]),
        pltpu.make_async_copy(alphas_hbm, alphas, w_sem.at[2, 2]),
    ]
    length_copy = pltpu.make_async_copy(seq_len_hbm, seq_len, w_sem.at[2, 3])
    length_copy.start()
    weight_copies[0, 0].start()
    pl.semaphore_wait(barrier, 13)
    upper = lax.div(zz, 2)
    for half in (1 - upper, upper):
        to_team(0, half, half_of(tokens, half), tok_in)
    for layer, number in ((1, 0), (0, 1), (0, 2), (0, 3), (1, 1), (1, 2), (1, 3)):
        weight_copies[layer, number].start(priority=1)
    for copy in bias_copies:
        copy.start(priority=1)
    length_copy.wait()
    end_second = lax.div(seq_len[0, 0] + seq_len[0, 1], RUNS)
    flag_out[...] = jnp.full((8, 128), end_second.astype(F32), F32)
    for half in (1 - upper, upper):
        to_team(1, half, flag_out, flag_in)
    for layer in range(LAYERS):
        for head in range(OWN):
            rq[layer, head, DIM:, :] = jnp.zeros((DIM, HALF * RUNS), BF16)
    for head in range(OWN):
        ro[head, 0:DIM, :] = jnp.zeros((DIM, HALF * RUNS), BF16)
    for layer in range(LAYERS):
        weight_copies[layer, 0].wait()
        pairs = [
            beside(
                wqkv[layer, :, WIDTH + 128 * pair : WIDTH + 128 * pair + 128].astype(F32),
                wqkv[layer, :, 2 * WIDTH + 128 * pair : 2 * WIDTH + 128 * pair + 128].astype(F32),
            )
            for pair in range(TEAM)
        ]
        for head in range(RUNS):
            at = WIDTH + 128 * head
            wqkv[layer, :, at : at + 128] = pairs[head // 2][head % 2].astype(BF16)
    halves(begin, functools.partial(project, 0), first=upper)
    for half in (1 - upper, upper):
        to_team(2, half, half_of(cotangent, half), cot_in)

    move_arrived(1, 0, flag_in)
    move_arrived(1, 1, flag_in)
    border = jnp.concatenate([flag_in[0, 0:1, :]] * 2, axis=1) - (HALF * lax.div(zz, 2)).astype(F32)
    key_row = lax.broadcasted_iota(jnp.int32, (TILE, TILE), 0)
    query_col = lax.broadcasted_iota(jnp.int32, (TILE, TILE), 1)
    later = key_row > query_col
    key_sub = lax.rem(key_row, HALF).astype(F32) >= border
    query_sub = lax.rem(query_col, HALF).astype(F32) >= border
    apart = jnp.logical_xor(key_sub, query_sub)
    for tile in range(TILES - 1):
        bias[TILE * tile : TILE * tile + TILE, :] = jnp.where(apart, NEGATIVE, 0.0)
    bias[TILE * (TILES - 1) :, :] = jnp.where(jnp.logical_or(later, apart), NEGATIVE, 0.0)

    for copy in (*bias_copies, *(weight_copies[0, number] for number in range(1, 4))):
        copy.wait()
    attend(0, 0)
    attend(0, 1)
    hidden_start(0, 0)
    halves(functools.partial(feed, 0), functools.partial(project, 1))
    for number in range(1, 4):
        weight_copies[1, number].wait()
    attend(1, 0)
    attend(1, 1)
    hidden_pass(0, 0)
    hidden_start(1, 0)
    halves(functools.partial(feed, 1), finish)
    hidden_start(0, 1)
    hidden_start(1, 1)
    hidden_pass(1, 0)

    halves(functools.partial(turn_round, 1))
    make(1)
    feed_back(1)
    hidden_pass(0, 1)
    hidden_pass(1, 1)
    core_done(1)
    make(0)
    attend_back(1, 1)
    first_y(1)
    core_done(0)
    attend_back(1, 0)
    second_y(1)
    first_x(1)
    project_back(1, 1)
    heads_grads(1)
    project_back(1, 0)
    feed_back(0)
    small_start()
    second_x(1)
    first_z(1)
    make(2)
    first_x(0)
    attend_back(0, 1)
    small_next(0)
    core_done(2)
    heads_second(1)
    make(3)
    second_x(0)
    attend_back(0, 0)
    small_next(1)
    first_z(0)
    heads_grads(0)
    core_done(3)
    project_back(0, 1)
    hand_back(1)
    small_next(2)
    second_z(1)
    first_x(2)
    first_y(2)
    first_z(2)
    heads_second(0)
    small_done()
    second_z(0)
    heads_third(1)
    second_x(2)
    first_x(3)
    first_z(3)
    second_z(2)
    first_y(3)
    heads_third(0)
    second_y(2)
    project_back(0, 0)
    hand_back(0)
    second_x(3)
    second_z(3)
    third_done(0)
    third_done(1)
    third_done(2)
    second_y(3)
    heads_done(1)
    third_done(3)
    final_pass(0)
    final_pass(1)
    final_pass(2)
    final_pass(3)
    final_done(0)
    final_done(1)
    final_done(2)
    heads_done(0)
    final_done(3)
    for half in range(2):
        move_arrived(3, half, out_in)
        move_arrived(4, half, grad_in)

    for half in range(2):
        left(2, 0, half, head_out)
        left(3, 0, half, pack_out)
        to_team_left(0, half, half_of(tokens, half))
        to_team_left(1, half, flag_out)
        to_team_left(2, half, half_of(cotangent, half))
        to_owner_left(3, half, back_out.at[0, half])
        to_owner_left(4, half, back_out.at[1, half])


def results_kernel(
    final, heads, out_block, grad_block, small,
    output, input_grad, qkv_grad, out_grad, up_grad, up_bias_grad, down_grad, down_bias_grad, alpha_grad,
    grad_wide, qkv_wide, out_wide, up_wide, down_wide, up_bias, down_bias, alpha, out_sem,
):
    ends = []

    def write(source, target):
        ends.append(pltpu.make_async_copy(source, target, out_sem.at[len(ends)]))
        ends[-1].start()

    for half in range(2):
        write(out_block.at[half], output.at[pl.ds(HALF * half, HALF)])
    up_bias[...] = small[:, 0:256]
    write(up_bias, up_bias_grad)
    down_bias[...] = small[:, 256 : 256 + DIM]
    write(down_bias, down_bias_grad)
    alpha[...] = small[:, 384:386]
    write(alpha, alpha_grad)
    for layer in range(LAYERS):
        for quarter in range(4):

            def block(first, count):
                return final[layer, quarter, first : first + count, :].astype(F32)

            def columns(step):
                return slice(WIDTH * step + 128 * quarter, WIDTH * step + 128 * quarter + 128)

            for step in range(4):
                up_wide[layer, :, columns(step)] = block(DIM * step, DIM)
            out_wide[layer, :, columns(0)] = block(256, DIM)
            down_wide[layer, :, columns(0)] = block(320, 256)
        write(up_wide.at[layer], up_grad.at[layer])
        write(out_wide.at[layer], out_grad.at[layer])
        write(down_wide.at[layer], down_grad.at[layer])
    for half in range(2):
        rows = slice(HALF * half, HALF * half + HALF)
        grad_wide[rows, :] = grad_block[half].astype(F32)
    write(grad_wide, input_grad)
    for layer in range(LAYERS):
        for side in range(2):
            for member in range(TEAM):
                block = heads[layer, side, member].astype(F32)
                columns = (block[:, 0:128], *beside(block[:, 128:256], block[:, 256:384]))
                for step in range(3):
                    at = WIDTH * step + 128 * member
                    qkv_wide[layer, 32 * side : 32 * side + 32, at : at + 128] = columns[step]
        write(qkv_wide.at[layer], qkv_grad.at[layer])
    for end in ends:
        end.wait()


def fast_body(
    tokens, seq_len, qkv_weight, out_weight, up_weight, up_bias, down_weight, down_bias, alphas, cotangent
):
    whole = pl.BlockSpec(memory_space=pltpu.VMEM)
    far = pl.BlockSpec(memory_space=pl.ANY)
    shape = jax.ShapeDtypeStruct
    rows = HALF * RUNS

    def vmem(*dims):
        return pltpu.VMEM(dims, BF16)

    def wide(*dims):
        return pltpu.VMEM(dims, F32)

    dma = pltpu.SemaphoreType.DMA
    final, heads, out_block, grad_block, small = pl.pallas_call(
        layers_kernel,
        out_shape=(
            vmem(LAYERS, 4, CHUNK, 128),
            vmem(LAYERS, 2, TEAM, DIM // 2, 3 * 128),
            vmem(2, HALF, WIDTH),
            vmem(2, HALF, WIDTH),
            wide(LAYERS, WIDTH),
        ),
        in_specs=[far, far, far, far, far, far, far, far, far, far],
        out_specs=(whole,) * 5,
        scratch_shapes=[
            pltpu.SMEM((1, 4), jnp.int32),
            pltpu.SMEM((LAYERS, 2), F32),
            vmem(LAYERS, WIDTH, 3 * WIDTH),
            vmem(LAYERS, WIDTH, WIDTH),
            vmem(LAYERS, WIDTH, FF),
            vmem(LAYERS, FF, WIDTH),
            wide(LAYERS, FF),
            wide(LAYERS, WIDTH),
            vmem(2, HALF, WIDTH),
            vmem(2, HALF, WIDTH),
            wide(8, 128),
            wide(2, 8, 128),
            vmem(2, 2, HALF, WIDTH),
            wide(2 * HALF, WIDTH),
            wide(2 * HALF, WIDTH),
            vmem(LAYERS, WIDTH, rows),
            vmem(LAYERS, WIDTH, 2 * HALF),
            vmem(LAYERS, 2 * HALF, WIDTH),
            vmem(LAYERS, 2 * HALF, FF),
            wide(LAYERS, 2 * HALF, WIDTH),
            wide(LAYERS, 2 * HALF, FF),
            wide(LAYERS, 2 * HALF, WIDTH),
            vmem(2 * HALF, WIDTH),
            vmem(2 * HALF, FF),
            vmem(2 * HALF, WIDTH),
            vmem(HALF, 3 * WIDTH),
            vmem(2, TEAM, OWN, PACK, 128),
            vmem(2, TEAM, OWN, DIM, 128),
            vmem(2, TEAM, OWN, PACK, 128),
            vmem(2, TEAM, OWN, DIM, 128),
            vmem(2, TEAM, OWN, DIM, 128),
            vmem(LAYERS, OWN, rows, 128),
            vmem(LAYERS, OWN, 128, rows),
            vmem(LAYERS, OWN, 128, rows),
            vmem(OWN, 128, rows),
            wide(LAYERS, OWN, DIM, rows),
            vmem(LAYERS, OWN, TILE * TILES * (TILES + 1) // 2, TILE),
            wide(OWN, rows, 128),
            wide(OWN, DIM, rows),
            wide(rows, TILE),
            vmem(LAYERS, 2, 2, 4, 2, CHUNK, 128),
            vmem(2, 4, 2, CHUNK, 128),
            vmem(4, 2, TOTALS[0], 128),
            vmem(4, TOTALS[1], 128),
            vmem(4, TOTALS[0], 128),
            vmem(2, 4, TOTALS[1], 128),
            vmem(LAYERS, 4, CHUNK, 128),
            vmem(4, 2, 2, TOTALS[2], 128),
            vmem(2, TOTALS[2], 128),
            vmem(TOTALS[2], 128),
            vmem(LAYERS, 4, 2, DIM, 3 * 128),
            vmem(LAYERS, 4, 2, DIM // 2, 3 * 128),
            vmem(LAYERS, 4, 2, DIM // 2, 3 * 128),
            vmem(LAYERS, 2, DIM // 2, 3 * 128),
            wide(LAYERS, SMALL),
            wide(3, LAYERS, SMALL),
            wide(4, LAYERS, SMALL),
            wide(3, LAYERS, SMALL),
            dma((LAYERS + 1, 4)),
            dma((5, 2)),
            dma((5, 2)),
            dma((4, LAYERS, 2, OWN)),
            dma((4, LAYERS, 2, OWN)),
            dma((len(PARTS),)),
            dma((len(PARTS),)),
            dma((len(PARTS), 3)),
            dma((len(PARTS), 3)),
            dma((len(PARTS), 3)),
            dma((len(PARTS), 3)),
            dma((len(PARTS), 3, 4)),
            dma((len(PARTS), 3, 4)),
            dma((len(PARTS), 3)),
            dma((len(PARTS), 3)),
            dma((LAYERS, 2, 3)),
            dma((LAYERS, 2, 3)),
            dma((LAYERS,)),
            dma((LAYERS,)),
            dma((LAYERS, 4)),
            dma((LAYERS, 4)),
            dma((LAYERS, 8)),
            dma((LAYERS, 8)),
            dma((6,)),
            dma((6,)),
            pltpu.SemaphoreType.REGULAR((2,)),
        ],
        compiler_params=pltpu.CompilerParams(
            collective_id=0, has_side_effects=True, vmem_limit_bytes=61 * 1024 * 1024
        ),
        name="layers",
    )(
        tokens, seq_len, alphas, up_bias, down_bias, cotangent,
        qkv_weight, out_weight, up_weight, down_weight,
    )
    return tuple(
        pl.pallas_call(
            results_kernel,
            out_shape=(
                shape((2 * HALF, WIDTH), BF16),
                shape((2 * HALF, WIDTH), F32),
                shape((LAYERS, DIM, 3 * WIDTH), F32),
                shape((LAYERS, DIM, WIDTH), F32),
                shape((LAYERS, DIM, FF), F32),
                shape((LAYERS, FF // RUNS), F32),
                shape((LAYERS, FF // RUNS, WIDTH), F32),
                shape((LAYERS, DIM), F32),
                shape((LAYERS, 2), F32),
            ),
            in_specs=[whole] * 5,
            out_specs=(far,) * 9,
            scratch_shapes=[
                wide(2 * HALF, WIDTH),
                wide(LAYERS, DIM, 3 * WIDTH),
                wide(LAYERS, DIM, WIDTH),
                wide(LAYERS, DIM, FF),
                wide(LAYERS, FF // RUNS, WIDTH),
                wide(LAYERS, FF // RUNS),
                wide(LAYERS, DIM),
                wide(LAYERS, 2),
                dma((14,)),
            ],
            compiler_params=pltpu.CompilerParams(vmem_limit_bytes=24 * 1024 * 1024),
            name="results",
        )(final, heads, out_block, grad_block, small)
    )


def layout(seq_len, local_count, cycle_size):
    piece_rows = seq_len[0] // cycle_size
    end_rows = jnp.cumsum(piece_rows)
    start_rows = end_rows - piece_rows
    local_rows = jnp.arange(local_count, dtype=jnp.int32)
    segment = jnp.sum((local_rows[:, None] >= end_rows[None, :]).astype(jnp.int32), axis=1)
    picked = segment[:, None] == jnp.arange(seq_len.shape[1], dtype=jnp.int32)[None, :]
    offset = local_rows - jnp.sum(jnp.where(picked, start_rows[None, :], 0), axis=1)
    span_rows = jnp.sum(jnp.where(picked, piece_rows[None, :], 0), axis=1)
    return (segment, offset, span_rows)


def gelu_exact(values):
    return jax.nn.gelu(values, approximate=False)


def key_block(whole, geometry, block_index, head_count):
    query_seg, query_pos, seg_all, pos_all, block_rows, score_scale = geometry
    first_row = block_index * block_rows
    key_piece = lax.dynamic_slice_in_dim(whole, first_row, block_rows, 0)
    key_seg = lax.dynamic_slice_in_dim(seg_all, first_row, block_rows, 0)
    key_pos = lax.dynamic_slice_in_dim(pos_all, first_row, block_rows, 0)
    half_width = key_piece.shape[1] // 2
    keys_part = key_piece[:, :half_width].reshape(block_rows, head_count, -1)
    values_part = key_piece[:, half_width:].reshape(block_rows, head_count, -1)
    return (keys_part, values_part, key_seg, key_pos)


def block_scores(queries, keys_part, key_seg, key_pos, geometry):
    query_seg, query_pos, seg_all, pos_all, block_rows, score_scale = geometry
    scores = (
        jnp.einsum("qhd,khd->hqk", queries, keys_part, preferred_element_type=jnp.float32)
        * score_scale
    )
    allowed = (query_seg[:, None] == key_seg[None, :]) & (key_pos[None, :] <= query_pos[:, None])
    return (scores, allowed[None])


def attend(queries, whole, geometry):
    row_count, head_count, head_dim = queries.shape
    block_count = whole.shape[0] // geometry[4]

    def statistics(running, block_index):
        largest, totals = running
        keys_part, values_part, key_seg, key_pos = key_block(
            whole, geometry, block_index, head_count
        )
        scores, allowed = block_scores(queries, keys_part, key_seg, key_pos, geometry)
        newest = jnp.maximum(largest, jnp.max(jnp.where(allowed, scores, NEGATIVE), axis=2))
        weights = jnp.where(allowed, jnp.exp(scores - newest[:, :, None]), 0.0)
        totals = totals * jnp.exp(largest - newest) + jnp.sum(weights, axis=2)
        return ((newest, totals), None)

    initial = (
        jnp.full((head_count, row_count), NEGATIVE, jnp.float32),
        jnp.zeros((head_count, row_count), jnp.float32),
    )
    (largest, totals), unused = lax.scan(statistics, initial, jnp.arange(block_count))
    log_total = largest + jnp.log(totals)

    def weighted(output_sum, block_index):
        keys_part, values_part, key_seg, key_pos = key_block(
            whole, geometry, block_index, head_count
        )
        scores, allowed = block_scores(queries, keys_part, key_seg, key_pos, geometry)
        probs = jnp.where(allowed, jnp.exp(scores - log_total[:, :, None]), 0.0).astype(
            jnp.bfloat16
        )
        output_sum = output_sum + jnp.einsum(
            "hqk,khd->qhd", probs, values_part, preferred_element_type=jnp.float32
        )
        return (output_sum, None)

    output_sum, unused = lax.scan(
        weighted, jnp.zeros((row_count, head_count, head_dim), jnp.float32), jnp.arange(block_count)
    )
    return (output_sum, log_total)


def attend_back(queries, whole, log_total, delta_sum, grad_heads, geometry):
    row_count, head_count, head_dim = queries.shape
    block_rows = geometry[4]
    score_scale = geometry[5]
    block_count = whole.shape[0] // block_rows

    def gradients(query_grad, block_index):
        keys_part, values_part, key_seg, key_pos = key_block(
            whole, geometry, block_index, head_count
        )
        scores, allowed = block_scores(queries, keys_part, key_seg, key_pos, geometry)
        probs = jnp.where(allowed, jnp.exp(scores - log_total[:, :, None]), 0.0)
        grad_probs = jnp.einsum(
            "qhd,khd->hqk", grad_heads, values_part, preferred_element_type=jnp.float32
        )
        grad_scores = (probs * (grad_probs - delta_sum[:, :, None])).astype(jnp.bfloat16)
        query_grad = (
            query_grad
            + jnp.einsum("hqk,khd->qhd", grad_scores, keys_part, preferred_element_type=jnp.float32)
            * score_scale
        )
        key_grad = (
            jnp.einsum("hqk,qhd->khd", grad_scores, queries, preferred_element_type=jnp.float32)
            * score_scale
        )
        value_grad = jnp.einsum(
            "hqk,qhd->khd",
            probs.astype(jnp.bfloat16),
            grad_heads,
            preferred_element_type=jnp.float32,
        )
        joined = jnp.concatenate(
            [key_grad.reshape(block_rows, -1), value_grad.reshape(block_rows, -1)], axis=1
        )
        return (query_grad, joined)

    query_grad, stacked = lax.scan(
        gradients,
        jnp.zeros((row_count, head_count, head_dim), jnp.float32),
        jnp.arange(block_count),
    )
    return (query_grad, stacked.reshape(whole.shape[0], -1))


def layer_forward(hidden, layer_index, weights, geometry):
    qkv_weight, out_weight, up_weight, up_bias, down_weight, down_bias, alphas = weights
    row_count, model_width = hidden.shape
    projection = qkv_weight[layer_index]
    rounded = hidden.astype(jnp.bfloat16)
    queries = (
        jnp.dot(rounded, projection[:, :model_width], preferred_element_type=jnp.float32)
        .astype(jnp.bfloat16)
        .reshape(row_count, HEADS, -1)
    )
    key_value = jnp.dot(
        rounded, projection[:, model_width:], preferred_element_type=jnp.float32
    ).astype(jnp.bfloat16)
    whole = lax.all_gather(key_value, "blk", axis=0, tiled=True)
    heads_out, log_total = attend(queries, whole, geometry)
    heads_rounded = heads_out.reshape(row_count, model_width).astype(jnp.bfloat16)
    branch = jnp.dot(heads_rounded, out_weight[layer_index], preferred_element_type=jnp.float32)
    alpha_pair = alphas[layer_index]
    middle = hidden + alpha_pair[0] * branch
    entered = middle.astype(jnp.bfloat16)
    gate_pre = (
        jnp.dot(entered, up_weight[layer_index], preferred_element_type=jnp.float32)
        + up_bias[layer_index]
    )
    activated = gelu_exact(gate_pre).astype(jnp.bfloat16)
    second = (
        jnp.dot(activated, down_weight[layer_index], preferred_element_type=jnp.float32)
        + down_bias[layer_index]
    )
    result = middle + alpha_pair[1] * second
    saved = (
        rounded,
        queries,
        key_value,
        whole,
        heads_out,
        heads_rounded,
        log_total,
        branch,
        entered,
        gate_pre,
        activated,
        second,
    )
    return (result, saved)


def layer_backward(grad_hidden, saved, layer_index, weights, geometry):
    qkv_weight, out_weight, up_weight, up_bias, down_weight, down_bias, alphas = weights
    (
        rounded,
        queries,
        key_value,
        saved_whole,
        heads_out,
        heads_rounded,
        log_total,
        branch,
        entered,
        gate_pre,
        activated,
        second,
    ) = saved
    row_count = grad_hidden.shape[0]
    alpha_pair = alphas[layer_index]
    grad_second = (alpha_pair[1] * grad_hidden).astype(jnp.bfloat16)
    alpha_second = jnp.sum(grad_hidden * second)
    bias_down = jnp.sum(grad_second.astype(jnp.float32), axis=0)
    grad_down = jnp.einsum("tf,td->fd", activated, grad_second, preferred_element_type=jnp.float32)
    grad_act = jnp.einsum(
        "td,fd->tf", grad_second, down_weight[layer_index], preferred_element_type=jnp.float32
    )
    unused, gelu_pull = jax.vjp(gelu_exact, gate_pre)
    grad_gate = gelu_pull(grad_act)[0].astype(jnp.bfloat16)
    bias_up = jnp.sum(grad_gate.astype(jnp.float32), axis=0)
    grad_up = jnp.einsum("td,tf->df", entered, grad_gate, preferred_element_type=jnp.float32)
    grad_middle = grad_hidden + jnp.einsum(
        "tf,df->td", grad_gate, up_weight[layer_index], preferred_element_type=jnp.float32
    )
    grad_branch = (alpha_pair[0] * grad_middle).astype(jnp.bfloat16)
    alpha_first = jnp.sum(grad_middle * branch)
    grad_proj_out = jnp.einsum(
        "te,td->ed", heads_rounded, grad_branch, preferred_element_type=jnp.float32
    )
    grad_heads = (
        jnp.einsum(
            "td,ed->te", grad_branch, out_weight[layer_index], preferred_element_type=jnp.float32
        )
        .astype(jnp.bfloat16)
        .reshape(queries.shape)
    )
    delta_sum = jnp.sum(grad_heads.astype(jnp.float32) * heads_out, axis=2).T
    whole = lax.all_gather(key_value, "blk", axis=0, tiled=True)
    query_grad, key_terms = attend_back(queries, whole, log_total, delta_sum, grad_heads, geometry)
    key_grads = lax.psum_scatter(
        key_terms.astype(jnp.bfloat16), "blk", scatter_dimension=0, tiled=True
    )
    grad_proj = jnp.concatenate(
        [query_grad.reshape(row_count, -1).astype(jnp.bfloat16), key_grads], axis=1
    )
    grad_qkv = jnp.einsum("td,te->de", rounded, grad_proj, preferred_element_type=jnp.float32)
    grad_input = grad_middle + jnp.einsum(
        "te,de->td", grad_proj, qkv_weight[layer_index], preferred_element_type=jnp.float32
    )
    layer_grads = (
        grad_qkv,
        grad_proj_out,
        grad_up,
        bias_up,
        grad_down,
        bias_down,
        jnp.stack([alpha_first, alpha_second]),
    )
    return (grad_input, layer_grads)


def reduce_all(layer_results, cycle_size):
    stacked = [
        jnp.stack([layer_entry[member] for layer_entry in layer_results], axis=0)
        for member in range(6)
    ]
    alpha_tiles = jnp.stack(
        [jnp.tile(layer_entry[6], cycle_size) for layer_entry in layer_results], axis=0
    )
    shares = (
        lax.psum_scatter(
            stacked[0].astype(jnp.bfloat16), "blk", scatter_dimension=1, tiled=True
        ).astype(jnp.float32),
        lax.psum_scatter(
            stacked[1].astype(jnp.bfloat16), "blk", scatter_dimension=1, tiled=True
        ).astype(jnp.float32),
        lax.psum_scatter(
            stacked[2].astype(jnp.bfloat16), "blk", scatter_dimension=1, tiled=True
        ).astype(jnp.float32),
        lax.psum_scatter(
            stacked[3].astype(jnp.bfloat16), "blk", scatter_dimension=1, tiled=True
        ).astype(jnp.float32),
        lax.psum_scatter(
            stacked[4].astype(jnp.bfloat16), "blk", scatter_dimension=1, tiled=True
        ).astype(jnp.float32),
        lax.psum_scatter(
            stacked[5].astype(jnp.bfloat16), "blk", scatter_dimension=1, tiled=True
        ).astype(jnp.float32),
        lax.psum_scatter(
            alpha_tiles.astype(jnp.bfloat16), "blk", scatter_dimension=1, tiled=True
        ).astype(jnp.float32),
    )
    return (
        lax.psum(shares[0].astype(jnp.bfloat16), "grp").astype(jnp.float32),
        lax.psum(shares[1].astype(jnp.bfloat16), "grp").astype(jnp.float32),
        lax.psum(shares[2].astype(jnp.bfloat16), "grp").astype(jnp.float32),
        lax.psum(shares[3].astype(jnp.bfloat16), "grp").astype(jnp.float32),
        lax.psum(shares[4].astype(jnp.bfloat16), "grp").astype(jnp.float32),
        lax.psum(shares[5].astype(jnp.bfloat16), "grp").astype(jnp.float32),
        lax.psum(shares[6].astype(jnp.bfloat16), "grp").astype(jnp.float32),
    )


def body(
    tokens,
    seq_len,
    qkv_weight,
    out_weight,
    up_weight,
    up_bias,
    down_weight,
    down_bias,
    alphas,
    cotangent,
):
    row_count, model_width = tokens.shape
    cycle_size = lax.axis_size("blk")
    cycle_place = lax.axis_index("blk")
    head_dim = model_width // HEADS
    total_rows = cycle_size * row_count
    block_rows = min(max(row_count, 512), total_rows)
    segment, offset, span_rows = layout(seq_len, row_count, cycle_size)
    query_pos = cycle_place * span_rows + offset
    seg_all = jnp.tile(segment, cycle_size)
    pos_all = jnp.repeat(jnp.arange(cycle_size, dtype=jnp.int32), row_count) * jnp.tile(
        span_rows, cycle_size
    ) + jnp.tile(offset, cycle_size)
    geometry = (segment, query_pos, seg_all, pos_all, block_rows, head_dim ** (-0.5))
    weights = (qkv_weight, out_weight, up_weight, up_bias, down_weight, down_bias, alphas)
    hidden = tokens.astype(jnp.float32)
    saved_layers = []
    for layer_index in range(LAYERS):
        hidden, saved = layer_forward(hidden, layer_index, weights, geometry)
        saved_layers.append(saved)
    output = hidden.astype(jnp.bfloat16)
    grad_hidden = cotangent.astype(jnp.float32)
    layer_results = []
    for layer_index in reversed(range(LAYERS)):
        grad_hidden, layer_grads = layer_backward(
            grad_hidden, saved_layers[layer_index], layer_index, weights, geometry
        )
        layer_results.insert(0, layer_grads)
    finals = reduce_all(layer_results, cycle_size)
    return (
        output,
        grad_hidden,
        finals[0],
        finals[1],
        finals[2],
        finals[3],
        finals[4],
        finals[5],
        finals[6],
    )


def solution(mesh):
    placed = (
        P(("grp", "blk"), None),
        P("grp", None),
        P(),
        P(),
        P(),
        P(),
        P(),
        P(),
        P(),
        P(("grp", "blk"), None),
    )
    sizes = (mesh.shape["grp"], mesh.shape["blk"])
    return jax.shard_map(
        fast_body if sizes == (4, RUNS) else body,
        mesh=mesh,
        in_specs=placed,
        out_specs=(
            P(("grp", "blk"), None),
            P(("grp", "blk"), None),
            P(None, "blk", None),
            P(None, "blk", None),
            P(None, "blk", None),
            P(None, "blk"),
            P(None, "blk", None),
            P(None, "blk"),
            P(),
        ),
        check_vma=False,
    )
```

```python
import functools

import jax
import jax.numpy as jnp
from jax import lax
from jax.experimental import pallas as pl
from jax.experimental.pallas import tpu as pltpu
from jax.sharding import PartitionSpec as P

HEADS = 8
LAYERS = 2
NEGATIVE = -1e30
MESH = pl.DeviceIdType.MESH
F32 = jnp.float32
BF16 = jnp.bfloat16

HALF = 128
RUNS = 8
TEAM = 4
OWN = RUNS // TEAM
DIM = 64
WIDTH = 512
FF = 2048
CUT = 512
TILE = 256
TILES = HALF * RUNS // TILE
PACK = HALF + DIM
CHUNK = 576
SMALL = FF + WIDTH + 128
PARTS = ((1, 0, 320), (1, 320, 256), (0, 0, 320), (0, 320, 256))
SHARES = ((192, 0, 128), (160, 16, 80), (160, 128, 32), (128, 96, 32))


def spans():
    places, totals = {}, [0, 0, 0]
    for part, counts in enumerate(SHARES):
        first = PARTS[part][1]
        for route, count in enumerate(counts):
            places[part, route] = (first, totals[route], count)
            first += count
            totals[route] += count
    return places, totals


SPANS, TOTALS = spans()

SLOPE_AT = 0.28
TAIL = (
    0.11652077851573843,
    0.06749675579450809,
    0.2689101589486142,
    -0.23699347299932225,
    0.3898740127620002,
    -0.10580824228351815,
)


def nn(a, b):
    return lax.dot_general(a, b, (((1,), (0,)), ((), ())), preferred_element_type=F32)


def nt(a, b):
    return lax.dot_general(a, b, (((1,), (1,)), ((), ())), preferred_element_type=F32)


def beside(first, other):
    low = lax.broadcasted_iota(jnp.int32, first.shape, 1) < DIM
    return (
        jnp.where(low, first, pltpu.roll(other, DIM, 1)),
        jnp.where(low, pltpu.roll(first, DIM, 1), other),
    )


def layers_kernel(
    tokens, seq_len_hbm, alphas_hbm, up_bias_hbm, down_bias_hbm, cotangent, qkv_hbm, out_hbm, up_hbm, down_hbm,
    final, heads_all, out_in, grad_in, small_final,
    seq_len, alphas, wqkv, wout, wup, wdown, up_bias, down_bias,
    tok_in, cot_in, flag_out, flag_in, back_out,
    hidden, grad, hid_all, attn_t, entered, act, branch, slope, second,
    dz, du, da, dqkv,
    pack_out, head_out, pack_in, o_in, do_in,
    kv, kv_t, rq, ro, o_t, probs, acc, dq_t, bias,
    parts, core_in, xa_in, xb_in, ya_in, yb_in, z_in, third_z, third_x, third_y,
    heads_out, heads_x, heads_z, heads_sum, small, small_in, small_z, small_sum,
    w_sem, move_send, move_recv, a2a_send, a2a_recv, core_send, core_recv, x_send, x_recv, y_send, y_recv,
    z_send, z_recv, fin_send, fin_recv, hid_send, hid_recv, hx_send, hx_recv, hz_send, hz_recv, hf_send, hf_recv,
    small_send, small_recv, core_free,
):
    grp = lax.axis_index("grp")
    blk = lax.axis_index("blk")
    core = lax.rem(grp, 2)
    side = lax.div(grp, 2)
    yy = lax.rem(blk, 2)
    zz = lax.div(blk, 2)
    member = 2 * core + yy
    far_side = 2 * (1 - side) + core

    def place(c, x, z, y):
        return (2 * x + c, 2 * z + y)

    core_peer = place(1 - core, side, zz, yy)
    x_peer = place(core, 1 - side, zz, yy)
    y_peer = place(core, side, zz, 1 - yy)

    def remote(source, target, send, recv, peer):
        return pltpu.make_async_remote_copy(
            src_ref=source,
            dst_ref=target,
            send_sem=send,
            recv_sem=recv,
            device_id=peer,
            device_id_type=MESH,
        )

    def credit(semaphore, peer, count=1):
        pl.semaphore_signal(semaphore, inc=count, device_id=peer, device_id_type=MESH)

    def moved(kind, slot, source, target, at, core_at, z_at):
        here = jnp.logical_and(core_at == core, z_at == zz)

        @pl.when(here)
        def _():
            pltpu.make_async_copy(source, target.at[at], move_recv.at[kind, at]).start()

        @pl.when(jnp.logical_not(here))
        def _():
            pltpu.make_async_remote_copy(
                src_ref=source,
                dst_ref=target.at[at],
                send_sem=move_send.at[kind, slot],
                recv_sem=move_recv.at[kind, at],
                device_id=place(core_at, side, z_at, yy),
                device_id_type=MESH,
            ).start()

    def move_left(kind, slot, source, core_at, z_at):
        here = jnp.logical_and(core_at == core, z_at == zz)

        @pl.when(jnp.logical_not(here))
        def _():
            pltpu.make_async_copy(source, source, move_send.at[kind, slot]).wait()

    def move_arrived(kind, at, target):
        pltpu.make_async_copy(target.at[at], target.at[at], move_recv.at[kind, at]).wait()

    def to_team(kind, half, source, target):
        moved(kind, half, source, target, lax.div(zz, 2), lax.rem(zz, 2), 2 * half + core)

    def to_team_left(kind, half, source):
        move_left(kind, half, source, lax.rem(zz, 2), 2 * half + core)

    def to_owner(kind, chunk, source, target):
        moved(kind, chunk, source, target, lax.div(zz, 2), lax.rem(zz, 2), core + 2 * chunk)

    def to_owner_left(kind, chunk, source):
        move_left(kind, chunk, source, lax.rem(zz, 2), core + 2 * chunk)

    def half_of(ref, half):
        return ref.at[pl.ds(pl.multiple_of(HALF * half, HALF), HALF)]

    def rows_of(half):
        return pl.ds(pl.multiple_of(half * HALF, HALF), HALF)

    def slot_of(other):
        return lax.rem(other + TEAM - member, TEAM)

    def exchange(kind, layer, half, outgoing, incoming, head=None):
        at = () if head is None else (head,)
        incoming[(half, 0, *at)] = outgoing[(half, member, *at)]
        for step in range(1, TEAM):
            peer = lax.rem(member + step, TEAM)
            remote(
                outgoing.at[(half, peer, *at)],
                incoming.at[(half, TEAM - step, *at)],
                a2a_send.at[kind, layer, half, head or 0],
                a2a_recv.at[kind, layer, half, head or 0],
                place(lax.div(peer, 2), side, zz, lax.rem(peer, 2)),
            ).start()

    def arrived(kind, layer, half, incoming, head=None):
        at = () if head is None else (head,)
        whole = incoming.at[(half, pl.ds(1, TEAM - 1), *at)]
        pltpu.make_async_copy(whole, whole, a2a_recv.at[kind, layer, half, head or 0]).wait()

    def left(kind, layer, half, outgoing):
        for head in range(OWN) if kind in (0, 3) else (None,):
            at = () if head is None else (head,)
            whole = outgoing.at[(half, pl.ds(1, TEAM - 1), *at)]
            pltpu.make_async_copy(whole, whole, a2a_send.at[kind, layer, half, head or 0]).wait()

    def tokens_of(chunk, other):
        return pl.ds(pl.multiple_of(HALF * (TEAM * chunk + other), HALF), HALF)

    def hidden_copy(layer, chunk, which):
        whose = 2 * core + 1 - yy if which == 2 else member
        block = hid_all.at[layer, :, tokens_of(chunk, whose)]
        return remote(
            block,
            block,
            hid_send.at[layer, chunk, which],
            hid_recv.at[layer, chunk, which],
            y_peer if which == 0 else core_peer,
        )

    def hidden_start(layer, chunk):
        for which in range(2):
            hidden_copy(layer, chunk, which).start()

    def hidden_pass(layer, chunk):
        hidden_copy(layer, chunk, 0).wait()
        hidden_copy(layer, chunk, 2).start()

    def hidden_done(layer, chunk):
        for which in range(1, 3):
            hidden_copy(layer, chunk, which).wait()

    def project(layer, half):
        rows = rows_of(half)
        rounded = hidden[rows, :].astype(BF16)
        if layer == 1:
            left(0, 0, half, pack_out)
        queries = (nn(rounded, wqkv[layer, :, 0:WIDTH]) * (DIM ** -0.5)).astype(BF16).T
        for head in range(RUNS):
            pack_out[half, head // 2, head % 2, HALF:, :] = queries[DIM * head : DIM * head + DIM, :]
        for step in range(2):
            at = WIDTH * (step + 1)
            keys_values = nn(rounded, wqkv[layer, :, at : at + WIDTH]).astype(BF16)
            for head in range(4):
                pack_out[half, 2 * step + head // 2, head % 2, 0:HALF, :] = keys_values[
                    :, 128 * head : 128 * head + 128
                ]
        for head in range(OWN):
            exchange(0, layer, half, pack_out, pack_in, head)
        hid_all[layer, :, tokens_of(half, member)] = rounded.T

    def rows_before(i):
        return TILE * i * (i + 1) // 2

    def attend(layer, chunk):
        if layer == 1:
            left(1, 0, chunk, head_out)

        def one_head(head, carry):
            arrived(0, layer, chunk, pack_in, head)
            for other in range(TEAM):
                slot = slot_of(other)
                start = HALF * (TEAM * chunk + other)
                span = slice(start, start + HALF)
                block = pack_in[chunk, slot, head, 0:HALF, :]
                kv[layer, head, span, :] = block
                kv_t[layer, head, :, span] = block.T
                rq[layer, head, 0:DIM, span] = pack_in[chunk, slot, head, HALF:, :]

            def scores_of(i):
                count = TILE * (i + 1)
                tile = rq[layer, head, :, TILE * i : TILE * i + TILE]
                return nn(kv[layer, head, 0:count, :], tile) + bias[TILE * TILES - count :, :]

            ahead = [scores_of(i) for i in (2 * chunk, 2 * chunk + 1)]
            for i in (2 * chunk, 2 * chunk + 1):
                columns = slice(TILE * i, TILE * i + TILE)
                count = TILE * (i + 1)
                scores = ahead[i - 2 * chunk]
                largest = jnp.max(scores, axis=0, keepdims=True)
                weight = jnp.exp(scores - largest)
                total = jnp.sum(weight, axis=0, keepdims=True)
                share = (weight * (1.0 / total)).astype(BF16)
                probs[layer, head, rows_before(i) : rows_before(i) + count, :] = share
                summed = nn(kv_t[layer, head, DIM:, 0:count], share)
                o_t[layer, head, :, columns] = summed
                rounded = summed.astype(BF16)
                for part in range(2):
                    head_out[chunk, 2 * (i - 2 * chunk) + part, head] = rounded[
                        :, HALF * part : HALF * part + HALF
                    ]
            return carry

        for head in range(OWN):
            one_head(head, 0)
        exchange(1, layer, chunk, head_out, o_in)

    def feed(layer, half):
        rows = rows_of(half)
        arrived(1, layer, half, o_in)
        for head in range(RUNS):
            attn_t[layer, DIM * head : DIM * head + DIM, rows] = o_in[half, slot_of(head // 2), head % 2]
        attn = attn_t[layer, :, rows].T
        grown = nn(attn, wout[layer])
        branch[layer, rows, :] = grown
        middle = hidden[rows, :] + alphas[layer, 0] * grown
        rounded = middle.astype(BF16)
        entered[layer, rows, :] = rounded
        total = jnp.zeros((HALF, WIDTH), F32)

        def gate_of(step):
            cut = slice(CUT * step, CUT * step + CUT)
            return nn(rounded, wup[layer, :, cut]) + up_bias[layer : layer + 1, cut]

        coming = gate_of(0)
        for step in range(FF // CUT):
            cut = slice(CUT * step, CUT * step + CUT)
            gate = coming
            if step + 1 < FF // CUT:
                coming = gate_of(step + 1)
            bell = jnp.exp(gate * gate * -0.5)
            near = pl.reciprocal(1.0 + SLOPE_AT * jnp.abs(gate), approx=True)
            tail = jnp.full_like(gate, TAIL[5])
            for factor in TAIL[4::-1]:
                tail = tail * near + factor
            tail = bell * (tail * near)
            risen = jnp.where(gate > 0.0, 1.0 - tail, tail)
            slope[layer, rows, cut] = risen + gate * bell * 0.3989422804014327
            active = (gate * risen).astype(BF16)
            act[layer, rows, cut] = active
            total = total + nn(active, wdown[layer, cut, :])
        total = total + down_bias[layer : layer + 1, :]
        second[layer, rows, :] = total
        hidden[rows, :] = middle + alphas[layer, 1] * total

    def total_of(values):
        return jnp.sum(jnp.sum(values, axis=0, keepdims=True), axis=1, keepdims=True)

    def feed_back(layer):
        start = grad[...]
        if layer == 0:
            dz[...] = (alphas[layer, 1] * start).astype(BF16)
        scaled = dz[...]
        alpha_second = total_of(start * second[layer])
        small[layer : layer + 1, FF : FF + WIDTH] = jnp.sum(scaled.astype(F32), axis=0, keepdims=True)
        middle = start
        coming = nt(scaled, wdown[layer, 0:CUT, :])
        for step in range(FF // CUT):
            cut = slice(CUT * step, CUT * step + CUT)
            raw = coming
            if step + 1 < FF // CUT:
                coming = nt(scaled, wdown[layer, CUT * (step + 1) : CUT * (step + 2), :])
            gate = (raw * slope[layer, :, cut]).astype(BF16)
            du[:, cut] = gate
            small[layer : layer + 1, cut] = jnp.sum(gate.astype(F32), axis=0, keepdims=True)
            middle = middle + nt(gate, wup[layer, :, cut])
        grad[...] = middle
        mixed = (alphas[layer, 0] * middle).astype(BF16)
        da[...] = mixed
        spread = nt(wout[layer], mixed).astype(BF16)
        for chunk in (1, 0):
            left(*((1, 1) if layer == 1 else (2, 1)), chunk, head_out)
            for head in range(RUNS):
                head_out[chunk, head // 2, head % 2] = spread[
                    DIM * head : DIM * head + DIM, HALF * chunk : HALF * chunk + HALF
                ]
            exchange(2, layer, chunk, head_out, do_in)
        alpha_first = total_of(middle * branch[layer])
        column = lax.broadcasted_iota(jnp.int32, (1, 128), 1)
        small[layer : layer + 1, FF + WIDTH :] = jnp.where(
            column == 0, alpha_first, jnp.where(column == 1, alpha_second, 0.0)
        )

    def attend_back(layer, chunk):
        arrived(2, layer, chunk, do_in)
        left(*((0, 1) if layer == 1 else (3, 1)), chunk, pack_out)

        def one_head(head, carry):
            for other in range(TEAM):
                start = HALF * (TEAM * chunk + other)
                ro[head, DIM:, start : start + HALF] = do_in[chunk, slot_of(other), head]
            for i in (2 * chunk, 2 * chunk + 1):
                columns = slice(TILE * i, TILE * i + TILE)
                query_tile = rq[layer, head, :, columns]
                grad_tile = ro[head, :, columns]
                delta = jnp.sum(
                    ro[head, DIM:, columns].astype(F32) * o_t[layer, head, :, columns],
                    axis=0,
                    keepdims=True,
                )
                count = TILE * (i + 1)
                keys = kv[layer, head, 0:count, :]
                share = probs[layer, head, rows_before(i) : rows_before(i) + count, :]
                scored = (share.astype(F32) * (nn(keys, grad_tile) - delta)).astype(BF16)
                term = nt(scored, query_tile) + nt(share, grad_tile)
                if chunk == 1 and i == 2:
                    acc[head, 0:count, :] = term
                elif chunk == 1:
                    acc[head, 0 : count - TILE, :] += term[0 : count - TILE, :]
                    acc[head, count - TILE : count, :] = term[count - TILE :, :]
                else:
                    acc[head, 0:count, :] += term
                query_grad = nn(kv_t[layer, head, 0:DIM, 0:count], scored)
                dq_t[head, :, columns] = query_grad * (DIM ** -0.5)
            for other in range(TEAM):
                start = HALF * (TEAM * chunk + other)
                span = slice(start, start + HALF)
                pack_out[chunk, other, head, 0:HALF, :] = acc[head, span, :].astype(BF16)
                pack_out[chunk, other, head, HALF:, :] = dq_t[head, :, span].astype(BF16)
            exchange(3, layer, chunk, pack_out, pack_in, head)
            return carry

        for head in range(OWN):
            one_head(head, 0)

    def project_back(layer, half):
        for head in range(OWN):
            arrived(3, layer, half, pack_in, head)
        turned = jnp.concatenate(
            [pack_in[half, slot_of(head // 2), head % 2, HALF:, :] for head in range(RUNS)], axis=0
        )
        dqkv[:, 0:WIDTH] = turned.T
        for head in range(RUNS):
            at = WIDTH + 128 * head
            dqkv[:, at : at + 128] = pack_in[half, slot_of(head // 2), head % 2, 0:HALF, :]
        rows = rows_of(half)
        grad[rows, :] = grad[rows, :] + nt(dqkv[...], wqkv[layer])

    def scatter_rows(layer, result, first_row):
        for run in range(RUNS):
            for quarter in range(4):
                parts[layer, quarter % 2, quarter // 2, run // 2, run % 2, first_row : first_row + DIM, :] = result[
                    DIM * run : DIM * run + DIM, 128 * quarter : 128 * quarter + 128
                ].astype(BF16)

    def make(part):
        layer, first, count = PARTS[part]
        if first < 256:
            turned = entered[layer].T
        for row in range(first, min(first + count, 256), DIM):
            step = row // DIM
            scatter_rows(layer, nn(turned, du[:, CUT * step : CUT * step + CUT]), row)
        if first <= 256 < first + count:
            scatter_rows(layer, nn(attn_t[layer], da[...]), 256)
        if first >= 320:
            turned = dz[...].T
            for step in range(FF // CUT):
                result = nn(turned, act[layer, :, CUT * step : CUT * step + CUT])
                for block in range(CUT // 128):
                    run, row = 2 * step + block // 2, 320 + 128 * (block % 2)
                    for quarter in range(4):
                        parts[layer, quarter % 2, quarter // 2, run // 2, run % 2, row : row + 128, :] = result[
                            128 * quarter : 128 * quarter + 128, 128 * block : 128 * block + 128
                        ].astype(BF16)
        if layer == 0:
            pl.semaphore_wait(core_free.at[0 if first < 320 else 1], 1)
        core_copy(part).start()

    def heads_grads(layer):
        for chunk in range(2):
            hidden_done(layer, chunk)
        blocks = [(run // TEAM, run % TEAM) for run in range(RUNS)]
        keys_values = jnp.concatenate(
            [
                jnp.concatenate([pack_out[chunk, other, head, 0:HALF, :] for chunk, other in blocks], axis=0)
                for head in range(OWN)
            ],
            axis=1,
        )
        queries = jnp.concatenate(
            [
                jnp.concatenate([pack_out[chunk, other, head, HALF:, :] for chunk, other in blocks], axis=1)
                for head in range(OWN)
            ],
            axis=0,
        )
        both = nn(hid_all[layer], keys_values)
        q_part = nt(hid_all[layer], queries)
        for number, values in enumerate((q_part, both[:, 0:128], both[:, 128:256])):
            for run in range(RUNS):
                heads_out[layer, run // 2, run % 2, :, 128 * number : 128 * number + 128] = values[
                    DIM * run : DIM * run + DIM, :
                ].astype(BF16)
        heads_x_copy(layer).start()

    def half_rows(which):
        return pl.ds(pl.multiple_of(32 * which, 32), 32)

    def heads_x_copy(layer):
        return remote(
            heads_out.at[layer, :, :, half_rows(1 - side)],
            heads_x.at[layer],
            hx_send.at[layer],
            hx_recv.at[layer],
            x_peer,
        )

    def heads_z_copy(layer, step):
        peer = lax.rem(zz + step, 4)
        return remote(
            heads_out.at[layer, peer, :, half_rows(side)],
            heads_z.at[layer, 4 - step],
            hz_send.at[layer, step],
            hz_recv.at[layer, 4 - step],
            place(core, side, peer, yy),
        )

    def heads_last_copy(layer, number):
        x, c, y = number // 4, number // 2 % 2, number % 2
        return remote(
            heads_sum.at[layer, 1 - yy if y else yy],
            heads_all.at[layer, side, member],
            hf_send.at[layer, number],
            hf_recv.at[layer, number],
            place(1 - core if c else core, 1 - side if x else side, zz, 1 - yy if y else yy),
        )

    def heads_second(layer):
        heads_x_copy(layer).wait()
        heads_out[layer, :, :, half_rows(side), :] += heads_x[layer]
        for step in range(1, 4):
            heads_z_copy(layer, step).start()

    def heads_third(layer):
        for step in range(1, 4):
            heads_z_copy(layer, step).wait()
        total = heads_out[layer, zz, :, half_rows(side), :].astype(F32)
        for slot in range(1, 4):
            total = total + heads_z[layer, slot].astype(F32)
        heads_sum[layer] = total.astype(BF16)
        heads_all[layer, side, member] = heads_sum[layer, yy]
        for number in range(1, 8):
            heads_last_copy(layer, number).start()

    def heads_done(layer):
        for number in range(1, 8):
            heads_last_copy(layer, number).wait()

    def rows_in(part, route):
        first, room, count = SPANS[part, route]
        return pl.ds(first, count), pl.ds(room, count)

    def used(part, route):
        return SHARES[part][route] > 0

    def core_copy(part):
        layer, first, count = PARTS[part]
        rows = pl.ds(first, count)
        return remote(
            parts.at[layer, 1 - core, :, :, :, rows],
            core_in.at[:, :, :, rows],
            core_send.at[part],
            core_recv.at[part],
            core_peer,
        )

    def x_copy(part, route):
        layer = PARTS[part][0]
        rows, room = rows_in(part, route)
        ends = (x_send.at[part, route], x_recv.at[part, route], x_peer)
        mine = parts.at[layer, core, 1 - side]
        if route == 0:
            return remote(mine.at[:, :, rows], xa_in.at[:, :, room], *ends)
        if route == 1:
            return remote(mine.at[:, yy, rows], xb_in.at[:, room], *ends)
        return remote(mine.at[zz, :, rows], third_x.at[:, room], *ends)

    def y_copy(part, route):
        layer = PARTS[part][0]
        rows, room = rows_in(part, route)
        ends = (y_send.at[part, route], y_recv.at[part, route], y_peer)
        mine = parts.at[layer, core]
        if route == 0:
            return remote(mine.at[side, :, 1 - yy, rows], ya_in.at[:, room], *ends)
        if route == 1:
            return remote(mine.at[:, :, 1 - yy, rows], yb_in.at[:, :, room], *ends)
        return remote(mine.at[side, zz, 1 - yy, rows], third_y.at[room], *ends)

    def z_copy(part, route, step):
        layer = PARTS[part][0]
        rows, room = rows_in(part, route)
        peer = lax.rem(zz + step, 4)
        ends = (z_send.at[part, route, step], z_recv.at[part, route, 4 - step], place(core, side, peer, yy))
        if route == 2:
            return remote(parts.at[layer, core, :, peer, :, rows], third_z.at[4 - step, :, :, room], *ends)
        return remote(parts.at[layer, core, side, peer, yy, rows], z_in.at[layer, 4 - step, rows], *ends)

    def final_copy(part, which):
        layer, first, count = PARTS[part]
        block = final.at[layer, far_side if which == 2 else grp, pl.ds(first, count)]
        return remote(
            block,
            block,
            fin_send.at[part, which],
            fin_recv.at[part, which],
            x_peer if which == 0 else core_peer,
        )

    def core_done(part):
        layer, first, count = PARTS[part]
        rows = pl.ds(first, count)
        core_copy(part).wait()
        for across in (1 - side, side):
            parts[layer, core, across, :, :, rows, :] += core_in[across, :, :, rows, :]
            if used(part, 0) and across is not side:
                x_copy(part, 0).start()
        if used(part, 1):
            y_copy(part, 1).start()
        if used(part, 2):
            for step in range(1, 4):
                z_copy(part, 2, step).start()
        if layer == 1:
            freed = 0 if first < 320 else 1
            followers = [1 for other in PARTS if other[0] == 0 and (other[1] >= 320) == (freed == 1)]
            credit(core_free.at[freed], core_peer, len(followers))

    def first_x(part):
        if used(part, 0):
            layer = PARTS[part][0]
            rows, room = rows_in(part, 0)
            x_copy(part, 0).wait()
            for y in (1 - yy, yy):
                parts[layer, core, side, :, y, rows, :] += xa_in[:, y, room, :]
                if y is not yy:
                    y_copy(part, 0).start()

    def first_y(part):
        if used(part, 1):
            layer = PARTS[part][0]
            rows, room = rows_in(part, 1)
            y_copy(part, 1).wait()
            for across in (1 - side, side):
                parts[layer, core, across, :, yy, rows, :] += yb_in[across, :, room, :]
                if across is not side:
                    x_copy(part, 1).start()

    def first_z(part):
        if used(part, 2):
            layer = PARTS[part][0]
            rows, room = rows_in(part, 2)
            for step in range(1, 4):
                z_copy(part, 2, step).wait()
            for across in (1 - side, side):
                total = parts[layer, core, across, zz, :, rows, :].astype(F32)
                for slot in range(1, 4):
                    total = total + third_z[slot, across, :, room, :].astype(F32)
                parts[layer, core, across, zz, :, rows, :] = total.astype(BF16)
                if across is not side:
                    x_copy(part, 2).start()

    def second_x(part):
        if used(part, 0):
            layer = PARTS[part][0]
            rows, room = rows_in(part, 0)
            y_copy(part, 0).wait()
            parts[layer, core, side, :, yy, rows, :] += ya_in[:, room, :]
            for step in range(1, 4):
                z_copy(part, 0, step).start()

    def second_y(part):
        if used(part, 1):
            layer = PARTS[part][0]
            rows, room = rows_in(part, 1)
            x_copy(part, 1).wait()
            parts[layer, core, side, :, yy, rows, :] += xb_in[:, room, :]
            for step in range(1, 4):
                z_copy(part, 1, step).start()

    def second_z(part):
        if used(part, 2):
            layer = PARTS[part][0]
            rows, room = rows_in(part, 2)
            x_copy(part, 2).wait()
            for y in (1 - yy, yy):
                parts[layer, core, side, zz, y, rows, :] += third_x[y, room, :]
                if y is not yy:
                    y_copy(part, 2).start()

    def third_done(part):
        layer = PARTS[part][0]
        for route in range(3):
            if not used(part, route):
                continue
            rows, room = rows_in(part, route)
            if route == 2:
                y_copy(part, 2).wait()
                final[layer, grp, rows, :] = parts[layer, core, side, zz, yy, rows, :] + third_y[room, :]
            else:
                for step in range(1, 4):
                    z_copy(part, route, step).wait()
                total = parts[layer, core, side, zz, yy, rows, :].astype(F32)
                for slot in range(1, 4):
                    total = total + z_in[layer, slot, rows, :].astype(F32)
                final[layer, grp, rows, :] = total.astype(BF16)
        if PARTS[part][1] >= 320:
            for row in (320, 448):
                final[layer, grp, row : row + 128, :] = final[layer, grp, row : row + 128, :].T
        for which in range(2):
            final_copy(part, which).start()

    def final_pass(part):
        final_copy(part, 0).wait()
        final_copy(part, 2).start()

    def final_done(part):
        for which in range(1, 3):
            final_copy(part, which).wait()

    def small_copy(stage):
        peer = (core_peer, x_peer, y_peer)[stage]
        return remote(
            small_sum.at[stage], small_in.at[stage], small_send.at[stage], small_recv.at[stage], peer
        )

    def small_z_copy(step):
        return remote(
            small_z.at[zz],
            small_z.at[zz],
            small_send.at[2 + step],
            small_recv.at[2 + step],
            place(core, side, lax.rem(zz + step, 4), yy),
        )

    def small_start():
        small_sum[0] = small[...]
        small_copy(0).start()

    def small_next(stage):
        small_copy(stage).wait()
        total = small_sum[stage] + small_in[stage]
        if stage < 2:
            small_sum[stage + 1] = total
            small_copy(stage + 1).start()
        else:
            small_z[zz] = total
            for step in range(1, 4):
                small_z_copy(step).start()

    def small_done():
        for step in range(1, 4):
            small_z_copy(step).wait()
        small_sum[0] = (small_z[0] + small_z[1]) + (small_z[2] + small_z[3])
        small_final[:, 0:256] = small_sum[0, :, pl.ds(pl.multiple_of(blk * 256, 256), 256)]
        pair = small_sum[0, :, pl.ds(pl.multiple_of(FF + 128 * zz, 128), 128)]
        small_final[:, 256:384] = jnp.where(yy == 1, pltpu.roll(pair, DIM, 1), pair)
        small_final[:, 384:512] = small_sum[0, :, FF + WIDTH :]

    def halves(*phases, first=0):
        def both(step, carry):
            for phase in phases:
                phase(lax.rem(step + first, 2))
            return carry

        lax.fori_loop(0, 2, both, 0)

    def begin(half):
        move_arrived(0, half, tok_in)
        hidden[rows_of(half), :] = tok_in[half].astype(F32)

    def finish(half):
        back_out[0, half] = hidden[rows_of(half), :].astype(BF16)
        to_owner(3, half, back_out.at[0, half], out_in)

    def turn_round(layer, half):
        move_arrived(2, half, cot_in)
        rows = rows_of(half)
        grad[rows, :] = cot_in[half].astype(F32)
        dz[rows, :] = (alphas[layer, 1] * grad[rows, :]).astype(BF16)

    def hand_back(half):
        back_out[1, half] = grad[rows_of(half), :].astype(BF16)
        to_owner(4, half, back_out.at[1, half], grad_in)

    barrier = pltpu.get_barrier_semaphore()
    for step in range(1, 4):
        credit(barrier, place(core, side, lax.rem(zz + step, 4), yy))
    for step in range(4):
        credit(barrier, place(1 - core, side, lax.rem(zz + step, 4), yy))
    for peer in (
        x_peer,
        y_peer,
        place(1 - core, side, zz, 1 - yy),
        place(1 - core, 1 - side, zz, yy),
        place(core, 1 - side, zz, 1 - yy),
        place(1 - core, 1 - side, zz, 1 - yy),
    ):
        credit(barrier, peer)

    weight_copies = {}
    for layer in range(LAYERS):
        for number, (source, target) in enumerate(
            ((qkv_hbm, wqkv), (out_hbm, wout), (up_hbm, wup), (down_hbm, wdown))
        ):
            weight_copies[layer, number] = pltpu.make_async_copy(
                source.at[layer], target.at[layer], w_sem.at[layer, number]
            )
    bias_copies = [
        pltpu.make_async_copy(up_bias_hbm, up_bias, w_sem.at[2, 0]),
        pltpu.make_async_copy(down_bias_hbm, down_bias, w_sem.at[2, 1]),
        pltpu.make_async_copy(alphas_hbm, alphas, w_sem.at[2, 2]),
    ]
    length_copy = pltpu.make_async_copy(seq_len_hbm, seq_len, w_sem.at[2, 3])
    length_copy.start()
    weight_copies[0, 0].start()
    pl.semaphore_wait(barrier, 13)
    upper = lax.div(zz, 2)
    for half in (1 - upper, upper):
        to_team(0, half, half_of(tokens, half), tok_in)
    for layer, number in ((1, 0), (0, 1), (0, 2), (0, 3), (1, 1), (1, 2), (1, 3)):
        weight_copies[layer, number].start(priority=1)
    for copy in bias_copies:
        copy.start(priority=1)
    length_copy.wait()
    end_second = lax.div(seq_len[0, 0] + seq_len[0, 1], RUNS)
    flag_out[...] = jnp.full((8, 128), end_second.astype(F32), F32)
    for half in (1 - upper, upper):
        to_team(1, half, flag_out, flag_in)
    for layer in range(LAYERS):
        for head in range(OWN):
            rq[layer, head, DIM:, :] = jnp.zeros((DIM, HALF * RUNS), BF16)
    for head in range(OWN):
        ro[head, 0:DIM, :] = jnp.zeros((DIM, HALF * RUNS), BF16)
    for layer in range(LAYERS):
        weight_copies[layer, 0].wait()
        pairs = [
            beside(
                wqkv[layer, :, WIDTH + 128 * pair : WIDTH + 128 * pair + 128].astype(F32),
                wqkv[layer, :, 2 * WIDTH + 128 * pair : 2 * WIDTH + 128 * pair + 128].astype(F32),
            )
            for pair in range(TEAM)
        ]
        for head in range(RUNS):
            at = WIDTH + 128 * head
            wqkv[layer, :, at : at + 128] = pairs[head // 2][head % 2].astype(BF16)
    halves(begin, functools.partial(project, 0), first=upper)
    for half in (1 - upper, upper):
        to_team(2, half, half_of(cotangent, half), cot_in)

    move_arrived(1, 0, flag_in)
    move_arrived(1, 1, flag_in)
    border = jnp.concatenate([flag_in[0, 0:1, :]] * 2, axis=1) - (HALF * lax.div(zz, 2)).astype(F32)
    key_row = lax.broadcasted_iota(jnp.int32, (TILE, TILE), 0)
    query_col = lax.broadcasted_iota(jnp.int32, (TILE, TILE), 1)
    later = key_row > query_col
    key_sub = lax.rem(key_row, HALF).astype(F32) >= border
    query_sub = lax.rem(query_col, HALF).astype(F32) >= border
    apart = jnp.logical_xor(key_sub, query_sub)
    for tile in range(TILES - 1):
        bias[TILE * tile : TILE * tile + TILE, :] = jnp.where(apart, NEGATIVE, 0.0)
    bias[TILE * (TILES - 1) :, :] = jnp.where(jnp.logical_or(later, apart), NEGATIVE, 0.0)

    for copy in (*bias_copies, *(weight_copies[0, number] for number in range(1, 4))):
        copy.wait()
    attend(0, 0)
    attend(0, 1)
    hidden_start(0, 0)
    for half in range(2):
        feed(0, half)
        project(1, half)
    for number in range(1, 4):
        weight_copies[1, number].wait()
    attend(1, 0)
    attend(1, 1)
    hidden_pass(0, 0)
    hidden_start(1, 0)
    for half in range(2):
        feed(1, half)
        finish(half)
    hidden_start(0, 1)
    hidden_start(1, 1)
    hidden_pass(1, 0)

    halves(functools.partial(turn_round, 1))
    make(1)
    feed_back(1)
    hidden_pass(0, 1)
    hidden_pass(1, 1)
    core_done(1)
    make(0)
    attend_back(1, 1)
    first_y(1)
    core_done(0)
    attend_back(1, 0)
    second_y(1)
    first_x(1)
    project_back(1, 1)
    heads_grads(1)
    first_z(1)
    project_back(1, 0)
    feed_back(0)
    small_start()
    second_x(1)
    make(2)
    first_x(0)
    heads_second(1)
    first_z(0)
    attend_back(0, 1)
    small_next(0)
    core_done(2)
    second_x(0)
    make(3)
    attend_back(0, 0)
    small_next(1)
    project_back(0, 1)
    hand_back(1)
    first_z(2)
    heads_grads(0)
    small_next(2)
    first_x(2)
    core_done(3)
    first_y(2)
    heads_second(0)
    small_done()
    first_z(3)
    second_x(2)
    first_x(3)
    second_z(2)
    second_z(0)
    heads_third(1)
    second_z(1)
    first_y(3)
    heads_third(0)
    second_y(2)
    second_x(3)
    second_z(3)
    third_done(0)
    third_done(2)
    second_y(3)
    project_back(0, 0)
    hand_back(0)
    heads_done(1)
    third_done(1)
    third_done(3)
    final_pass(0)
    final_pass(2)
    final_pass(1)
    final_pass(3)
    final_done(2)
    final_done(1)
    heads_done(0)
    final_done(0)
    final_done(3)
    for half in range(2):
        move_arrived(3, half, out_in)
        move_arrived(4, half, grad_in)

    for half in range(2):
        left(2, 0, half, head_out)
        left(3, 0, half, pack_out)
        to_team_left(0, half, half_of(tokens, half))
        to_team_left(1, half, flag_out)
        to_team_left(2, half, half_of(cotangent, half))
        to_owner_left(3, half, back_out.at[0, half])
        to_owner_left(4, half, back_out.at[1, half])


def results_kernel(
    final, heads, out_block, grad_block, small,
    output, input_grad, qkv_grad, out_grad, up_grad, up_bias_grad, down_grad, down_bias_grad, alpha_grad,
    grad_wide, qkv_wide, out_wide, up_wide, down_wide, up_bias, down_bias, alpha, out_sem,
):
    ends = []

    def write(source, target):
        ends.append(pltpu.make_async_copy(source, target, out_sem.at[len(ends)]))
        ends[-1].start()

    for half in range(2):
        write(out_block.at[half], output.at[pl.ds(HALF * half, HALF)])
    up_bias[...] = small[:, 0:256]
    write(up_bias, up_bias_grad)
    down_bias[...] = small[:, 256 : 256 + DIM]
    write(down_bias, down_bias_grad)
    alpha[...] = small[:, 384:386]
    write(alpha, alpha_grad)
    for layer in range(LAYERS):
        for quarter in range(4):

            def block(first, count):
                return final[layer, quarter, first : first + count, :].astype(F32)

            def columns(step):
                return slice(WIDTH * step + 128 * quarter, WIDTH * step + 128 * quarter + 128)

            for step in range(4):
                up_wide[layer, :, columns(step)] = block(DIM * step, DIM)
            out_wide[layer, :, columns(0)] = block(256, DIM)
            down_wide[layer, :, columns(0)] = block(320, 256)
        write(up_wide.at[layer], up_grad.at[layer])
        write(out_wide.at[layer], out_grad.at[layer])
        write(down_wide.at[layer], down_grad.at[layer])
    for half in range(2):
        rows = slice(HALF * half, HALF * half + HALF)
        grad_wide[rows, :] = grad_block[half].astype(F32)
    write(grad_wide, input_grad)
    for layer in range(LAYERS):
        for side in range(2):
            for member in range(TEAM):
                block = heads[layer, side, member].astype(F32)
                columns = (block[:, 0:128], *beside(block[:, 128:256], block[:, 256:384]))
                for step in range(3):
                    at = WIDTH * step + 128 * member
                    qkv_wide[layer, 32 * side : 32 * side + 32, at : at + 128] = columns[step]
        write(qkv_wide.at[layer], qkv_grad.at[layer])
    for end in ends:
        end.wait()


def fast_body(
    tokens, seq_len, qkv_weight, out_weight, up_weight, up_bias, down_weight, down_bias, alphas, cotangent
):
    whole = pl.BlockSpec(memory_space=pltpu.VMEM)
    far = pl.BlockSpec(memory_space=pl.ANY)
    shape = jax.ShapeDtypeStruct
    rows = HALF * RUNS

    def vmem(*dims):
        return pltpu.VMEM(dims, BF16)

    def wide(*dims):
        return pltpu.VMEM(dims, F32)

    dma = pltpu.SemaphoreType.DMA
    final, heads, out_block, grad_block, small = pl.pallas_call(
        layers_kernel,
        out_shape=(
            vmem(LAYERS, 4, CHUNK, 128),
            vmem(LAYERS, 2, TEAM, DIM // 2, 3 * 128),
            vmem(2, HALF, WIDTH),
            vmem(2, HALF, WIDTH),
            wide(LAYERS, WIDTH),
        ),
        in_specs=[far, far, far, far, far, far, far, far, far, far],
        out_specs=(whole,) * 5,
        scratch_shapes=[
            pltpu.SMEM((1, 4), jnp.int32),
            pltpu.SMEM((LAYERS, 2), F32),
            vmem(LAYERS, WIDTH, 3 * WIDTH),
            vmem(LAYERS, WIDTH, WIDTH),
            vmem(LAYERS, WIDTH, FF),
            vmem(LAYERS, FF, WIDTH),
            wide(LAYERS, FF),
            wide(LAYERS, WIDTH),
            vmem(2, HALF, WIDTH),
            vmem(2, HALF, WIDTH),
            wide(8, 128),
            wide(2, 8, 128),
            vmem(2, 2, HALF, WIDTH),
            wide(2 * HALF, WIDTH),
            wide(2 * HALF, WIDTH),
            vmem(LAYERS, WIDTH, rows),
            vmem(LAYERS, WIDTH, 2 * HALF),
            vmem(LAYERS, 2 * HALF, WIDTH),
            vmem(LAYERS, 2 * HALF, FF),
            wide(LAYERS, 2 * HALF, WIDTH),
            wide(LAYERS, 2 * HALF, FF),
            wide(LAYERS, 2 * HALF, WIDTH),
            vmem(2 * HALF, WIDTH),
            vmem(2 * HALF, FF),
            vmem(2 * HALF, WIDTH),
            vmem(HALF, 3 * WIDTH),
            vmem(2, TEAM, OWN, PACK, 128),
            vmem(2, TEAM, OWN, DIM, 128),
            vmem(2, TEAM, OWN, PACK, 128),
            vmem(2, TEAM, OWN, DIM, 128),
            vmem(2, TEAM, OWN, DIM, 128),
            vmem(LAYERS, OWN, rows, 128),
            vmem(LAYERS, OWN, 128, rows),
            vmem(LAYERS, OWN, 128, rows),
            vmem(OWN, 128, rows),
            wide(LAYERS, OWN, DIM, rows),
            vmem(LAYERS, OWN, TILE * TILES * (TILES + 1) // 2, TILE),
            wide(OWN, rows, 128),
            wide(OWN, DIM, rows),
            wide(rows, TILE),
            vmem(LAYERS, 2, 2, 4, 2, CHUNK, 128),
            vmem(2, 4, 2, CHUNK, 128),
            vmem(4, 2, TOTALS[0], 128),
            vmem(4, TOTALS[1], 128),
            vmem(4, TOTALS[0], 128),
            vmem(2, 4, TOTALS[1], 128),
            vmem(LAYERS, 4, CHUNK, 128),
            vmem(4, 2, 2, TOTALS[2], 128),
            vmem(2, TOTALS[2], 128),
            vmem(TOTALS[2], 128),
            vmem(LAYERS, 4, 2, DIM, 3 * 128),
            vmem(LAYERS, 4, 2, DIM // 2, 3 * 128),
            vmem(LAYERS, 4, 2, DIM // 2, 3 * 128),
            vmem(LAYERS, 2, DIM // 2, 3 * 128),
            wide(LAYERS, SMALL),
            wide(3, LAYERS, SMALL),
            wide(4, LAYERS, SMALL),
            wide(3, LAYERS, SMALL),
            dma((LAYERS + 1, 4)),
            dma((5, 2)),
            dma((5, 2)),
            dma((4, LAYERS, 2, OWN)),
            dma((4, LAYERS, 2, OWN)),
            dma((len(PARTS),)),
            dma((len(PARTS),)),
            dma((len(PARTS), 3)),
            dma((len(PARTS), 3)),
            dma((len(PARTS), 3)),
            dma((len(PARTS), 3)),
            dma((len(PARTS), 3, 4)),
            dma((len(PARTS), 3, 4)),
            dma((len(PARTS), 3)),
            dma((len(PARTS), 3)),
            dma((LAYERS, 2, 3)),
            dma((LAYERS, 2, 3)),
            dma((LAYERS,)),
            dma((LAYERS,)),
            dma((LAYERS, 4)),
            dma((LAYERS, 4)),
            dma((LAYERS, 8)),
            dma((LAYERS, 8)),
            dma((6,)),
            dma((6,)),
            pltpu.SemaphoreType.REGULAR((2,)),
        ],
        compiler_params=pltpu.CompilerParams(
            collective_id=0, has_side_effects=True, vmem_limit_bytes=61 * 1024 * 1024
        ),
        name="layers",
    )(
        tokens, seq_len, alphas, up_bias, down_bias, cotangent,
        qkv_weight, out_weight, up_weight, down_weight,
    )
    return tuple(
        pl.pallas_call(
            results_kernel,
            out_shape=(
                shape((2 * HALF, WIDTH), BF16),
                shape((2 * HALF, WIDTH), F32),
                shape((LAYERS, DIM, 3 * WIDTH), F32),
                shape((LAYERS, DIM, WIDTH), F32),
                shape((LAYERS, DIM, FF), F32),
                shape((LAYERS, FF // RUNS), F32),
                shape((LAYERS, FF // RUNS, WIDTH), F32),
                shape((LAYERS, DIM), F32),
                shape((LAYERS, 2), F32),
            ),
            in_specs=[whole] * 5,
            out_specs=(far,) * 9,
            scratch_shapes=[
                wide(2 * HALF, WIDTH),
                wide(LAYERS, DIM, 3 * WIDTH),
                wide(LAYERS, DIM, WIDTH),
                wide(LAYERS, DIM, FF),
                wide(LAYERS, FF // RUNS, WIDTH),
                wide(LAYERS, FF // RUNS),
                wide(LAYERS, DIM),
                wide(LAYERS, 2),
                dma((14,)),
            ],
            compiler_params=pltpu.CompilerParams(vmem_limit_bytes=24 * 1024 * 1024),
            name="results",
        )(final, heads, out_block, grad_block, small)
    )


def layout(seq_len, local_count, cycle_size):
    piece_rows = seq_len[0] // cycle_size
    end_rows = jnp.cumsum(piece_rows)
    start_rows = end_rows - piece_rows
    local_rows = jnp.arange(local_count, dtype=jnp.int32)
    segment = jnp.sum((local_rows[:, None] >= end_rows[None, :]).astype(jnp.int32), axis=1)
    picked = segment[:, None] == jnp.arange(seq_len.shape[1], dtype=jnp.int32)[None, :]
    offset = local_rows - jnp.sum(jnp.where(picked, start_rows[None, :], 0), axis=1)
    span_rows = jnp.sum(jnp.where(picked, piece_rows[None, :], 0), axis=1)
    return (segment, offset, span_rows)


def gelu_exact(values):
    return jax.nn.gelu(values, approximate=False)


def key_block(whole, geometry, block_index, head_count):
    query_seg, query_pos, seg_all, pos_all, block_rows, score_scale = geometry
    first_row = block_index * block_rows
    key_piece = lax.dynamic_slice_in_dim(whole, first_row, block_rows, 0)
    key_seg = lax.dynamic_slice_in_dim(seg_all, first_row, block_rows, 0)
    key_pos = lax.dynamic_slice_in_dim(pos_all, first_row, block_rows, 0)
    half_width = key_piece.shape[1] // 2
    keys_part = key_piece[:, :half_width].reshape(block_rows, head_count, -1)
    values_part = key_piece[:, half_width:].reshape(block_rows, head_count, -1)
    return (keys_part, values_part, key_seg, key_pos)


def block_scores(queries, keys_part, key_seg, key_pos, geometry):
    query_seg, query_pos, seg_all, pos_all, block_rows, score_scale = geometry
    scores = (
        jnp.einsum("qhd,khd->hqk", queries, keys_part, preferred_element_type=jnp.float32)
        * score_scale
    )
    allowed = (query_seg[:, None] == key_seg[None, :]) & (key_pos[None, :] <= query_pos[:, None])
    return (scores, allowed[None])


def attend(queries, whole, geometry):
    row_count, head_count, head_dim = queries.shape
    block_count = whole.shape[0] // geometry[4]

    def statistics(running, block_index):
        largest, totals = running
        keys_part, values_part, key_seg, key_pos = key_block(
            whole, geometry, block_index, head_count
        )
        scores, allowed = block_scores(queries, keys_part, key_seg, key_pos, geometry)
        newest = jnp.maximum(largest, jnp.max(jnp.where(allowed, scores, NEGATIVE), axis=2))
        weights = jnp.where(allowed, jnp.exp(scores - newest[:, :, None]), 0.0)
        totals = totals * jnp.exp(largest - newest) + jnp.sum(weights, axis=2)
        return ((newest, totals), None)

    initial = (
        jnp.full((head_count, row_count), NEGATIVE, jnp.float32),
        jnp.zeros((head_count, row_count), jnp.float32),
    )
    (largest, totals), unused = lax.scan(statistics, initial, jnp.arange(block_count))
    log_total = largest + jnp.log(totals)

    def weighted(output_sum, block_index):
        keys_part, values_part, key_seg, key_pos = key_block(
            whole, geometry, block_index, head_count
        )
        scores, allowed = block_scores(queries, keys_part, key_seg, key_pos, geometry)
        probs = jnp.where(allowed, jnp.exp(scores - log_total[:, :, None]), 0.0).astype(
            jnp.bfloat16
        )
        output_sum = output_sum + jnp.einsum(
            "hqk,khd->qhd", probs, values_part, preferred_element_type=jnp.float32
        )
        return (output_sum, None)

    output_sum, unused = lax.scan(
        weighted, jnp.zeros((row_count, head_count, head_dim), jnp.float32), jnp.arange(block_count)
    )
    return (output_sum, log_total)


def attend_back(queries, whole, log_total, delta_sum, grad_heads, geometry):
    row_count, head_count, head_dim = queries.shape
    block_rows = geometry[4]
    score_scale = geometry[5]
    block_count = whole.shape[0] // block_rows

    def gradients(query_grad, block_index):
        keys_part, values_part, key_seg, key_pos = key_block(
            whole, geometry, block_index, head_count
        )
        scores, allowed = block_scores(queries, keys_part, key_seg, key_pos, geometry)
        probs = jnp.where(allowed, jnp.exp(scores - log_total[:, :, None]), 0.0)
        grad_probs = jnp.einsum(
            "qhd,khd->hqk", grad_heads, values_part, preferred_element_type=jnp.float32
        )
        grad_scores = (probs * (grad_probs - delta_sum[:, :, None])).astype(jnp.bfloat16)
        query_grad = (
            query_grad
            + jnp.einsum("hqk,khd->qhd", grad_scores, keys_part, preferred_element_type=jnp.float32)
            * score_scale
        )
        key_grad = (
            jnp.einsum("hqk,qhd->khd", grad_scores, queries, preferred_element_type=jnp.float32)
            * score_scale
        )
        value_grad = jnp.einsum(
            "hqk,qhd->khd",
            probs.astype(jnp.bfloat16),
            grad_heads,
            preferred_element_type=jnp.float32,
        )
        joined = jnp.concatenate(
            [key_grad.reshape(block_rows, -1), value_grad.reshape(block_rows, -1)], axis=1
        )
        return (query_grad, joined)

    query_grad, stacked = lax.scan(
        gradients,
        jnp.zeros((row_count, head_count, head_dim), jnp.float32),
        jnp.arange(block_count),
    )
    return (query_grad, stacked.reshape(whole.shape[0], -1))


def layer_forward(hidden, layer_index, weights, geometry):
    qkv_weight, out_weight, up_weight, up_bias, down_weight, down_bias, alphas = weights
    row_count, model_width = hidden.shape
    projection = qkv_weight[layer_index]
    rounded = hidden.astype(jnp.bfloat16)
    queries = (
        jnp.dot(rounded, projection[:, :model_width], preferred_element_type=jnp.float32)
        .astype(jnp.bfloat16)
        .reshape(row_count, HEADS, -1)
    )
    key_value = jnp.dot(
        rounded, projection[:, model_width:], preferred_element_type=jnp.float32
    ).astype(jnp.bfloat16)
    whole = lax.all_gather(key_value, "blk", axis=0, tiled=True)
    heads_out, log_total = attend(queries, whole, geometry)
    heads_rounded = heads_out.reshape(row_count, model_width).astype(jnp.bfloat16)
    branch = jnp.dot(heads_rounded, out_weight[layer_index], preferred_element_type=jnp.float32)
    alpha_pair = alphas[layer_index]
    middle = hidden + alpha_pair[0] * branch
    entered = middle.astype(jnp.bfloat16)
    gate_pre = (
        jnp.dot(entered, up_weight[layer_index], preferred_element_type=jnp.float32)
        + up_bias[layer_index]
    )
    activated = gelu_exact(gate_pre).astype(jnp.bfloat16)
    second = (
        jnp.dot(activated, down_weight[layer_index], preferred_element_type=jnp.float32)
        + down_bias[layer_index]
    )
    result = middle + alpha_pair[1] * second
    saved = (
        rounded,
        queries,
        key_value,
        whole,
        heads_out,
        heads_rounded,
        log_total,
        branch,
        entered,
        gate_pre,
        activated,
        second,
    )
    return (result, saved)


def layer_backward(grad_hidden, saved, layer_index, weights, geometry):
    qkv_weight, out_weight, up_weight, up_bias, down_weight, down_bias, alphas = weights
    (
        rounded,
        queries,
        key_value,
        saved_whole,
        heads_out,
        heads_rounded,
        log_total,
        branch,
        entered,
        gate_pre,
        activated,
        second,
    ) = saved
    row_count = grad_hidden.shape[0]
    alpha_pair = alphas[layer_index]
    grad_second = (alpha_pair[1] * grad_hidden).astype(jnp.bfloat16)
    alpha_second = jnp.sum(grad_hidden * second)
    bias_down = jnp.sum(grad_second.astype(jnp.float32), axis=0)
    grad_down = jnp.einsum("tf,td->fd", activated, grad_second, preferred_element_type=jnp.float32)
    grad_act = jnp.einsum(
        "td,fd->tf", grad_second, down_weight[layer_index], preferred_element_type=jnp.float32
    )
    unused, gelu_pull = jax.vjp(gelu_exact, gate_pre)
    grad_gate = gelu_pull(grad_act)[0].astype(jnp.bfloat16)
    bias_up = jnp.sum(grad_gate.astype(jnp.float32), axis=0)
    grad_up = jnp.einsum("td,tf->df", entered, grad_gate, preferred_element_type=jnp.float32)
    grad_middle = grad_hidden + jnp.einsum(
        "tf,df->td", grad_gate, up_weight[layer_index], preferred_element_type=jnp.float32
    )
    grad_branch = (alpha_pair[0] * grad_middle).astype(jnp.bfloat16)
    alpha_first = jnp.sum(grad_middle * branch)
    grad_proj_out = jnp.einsum(
        "te,td->ed", heads_rounded, grad_branch, preferred_element_type=jnp.float32
    )
    grad_heads = (
        jnp.einsum(
            "td,ed->te", grad_branch, out_weight[layer_index], preferred_element_type=jnp.float32
        )
        .astype(jnp.bfloat16)
        .reshape(queries.shape)
    )
    delta_sum = jnp.sum(grad_heads.astype(jnp.float32) * heads_out, axis=2).T
    whole = lax.all_gather(key_value, "blk", axis=0, tiled=True)
    query_grad, key_terms = attend_back(queries, whole, log_total, delta_sum, grad_heads, geometry)
    key_grads = lax.psum_scatter(
        key_terms.astype(jnp.bfloat16), "blk", scatter_dimension=0, tiled=True
    )
    grad_proj = jnp.concatenate(
        [query_grad.reshape(row_count, -1).astype(jnp.bfloat16), key_grads], axis=1
    )
    grad_qkv = jnp.einsum("td,te->de", rounded, grad_proj, preferred_element_type=jnp.float32)
    grad_input = grad_middle + jnp.einsum(
        "te,de->td", grad_proj, qkv_weight[layer_index], preferred_element_type=jnp.float32
    )
    layer_grads = (
        grad_qkv,
        grad_proj_out,
        grad_up,
        bias_up,
        grad_down,
        bias_down,
        jnp.stack([alpha_first, alpha_second]),
    )
    return (grad_input, layer_grads)


def reduce_all(layer_results, cycle_size):
    stacked = [
        jnp.stack([layer_entry[member] for layer_entry in layer_results], axis=0)
        for member in range(6)
    ]
    alpha_tiles = jnp.stack(
        [jnp.tile(layer_entry[6], cycle_size) for layer_entry in layer_results], axis=0
    )
    shares = (
        lax.psum_scatter(
            stacked[0].astype(jnp.bfloat16), "blk", scatter_dimension=1, tiled=True
        ).astype(jnp.float32),
        lax.psum_scatter(
            stacked[1].astype(jnp.bfloat16), "blk", scatter_dimension=1, tiled=True
        ).astype(jnp.float32),
        lax.psum_scatter(
            stacked[2].astype(jnp.bfloat16), "blk", scatter_dimension=1, tiled=True
        ).astype(jnp.float32),
        lax.psum_scatter(
            stacked[3].astype(jnp.bfloat16), "blk", scatter_dimension=1, tiled=True
        ).astype(jnp.float32),
        lax.psum_scatter(
            stacked[4].astype(jnp.bfloat16), "blk", scatter_dimension=1, tiled=True
        ).astype(jnp.float32),
        lax.psum_scatter(
            stacked[5].astype(jnp.bfloat16), "blk", scatter_dimension=1, tiled=True
        ).astype(jnp.float32),
        lax.psum_scatter(
            alpha_tiles.astype(jnp.bfloat16), "blk", scatter_dimension=1, tiled=True
        ).astype(jnp.float32),
    )
    return (
        lax.psum(shares[0].astype(jnp.bfloat16), "grp").astype(jnp.float32),
        lax.psum(shares[1].astype(jnp.bfloat16), "grp").astype(jnp.float32),
        lax.psum(shares[2].astype(jnp.bfloat16), "grp").astype(jnp.float32),
        lax.psum(shares[3].astype(jnp.bfloat16), "grp").astype(jnp.float32),
        lax.psum(shares[4].astype(jnp.bfloat16), "grp").astype(jnp.float32),
        lax.psum(shares[5].astype(jnp.bfloat16), "grp").astype(jnp.float32),
        lax.psum(shares[6].astype(jnp.bfloat16), "grp").astype(jnp.float32),
    )


def body(
    tokens,
    seq_len,
    qkv_weight,
    out_weight,
    up_weight,
    up_bias,
    down_weight,
    down_bias,
    alphas,
    cotangent,
):
    row_count, model_width = tokens.shape
    cycle_size = lax.axis_size("blk")
    cycle_place = lax.axis_index("blk")
    head_dim = model_width // HEADS
    total_rows = cycle_size * row_count
    block_rows = min(max(row_count, 512), total_rows)
    segment, offset, span_rows = layout(seq_len, row_count, cycle_size)
    query_pos = cycle_place * span_rows + offset
    seg_all = jnp.tile(segment, cycle_size)
    pos_all = jnp.repeat(jnp.arange(cycle_size, dtype=jnp.int32), row_count) * jnp.tile(
        span_rows, cycle_size
    ) + jnp.tile(offset, cycle_size)
    geometry = (segment, query_pos, seg_all, pos_all, block_rows, head_dim ** (-0.5))
    weights = (qkv_weight, out_weight, up_weight, up_bias, down_weight, down_bias, alphas)
    hidden = tokens.astype(jnp.float32)
    saved_layers = []
    for layer_index in range(LAYERS):
        hidden, saved = layer_forward(hidden, layer_index, weights, geometry)
        saved_layers.append(saved)
    output = hidden.astype(jnp.bfloat16)
    grad_hidden = cotangent.astype(jnp.float32)
    layer_results = []
    for layer_index in reversed(range(LAYERS)):
        grad_hidden, layer_grads = layer_backward(
            grad_hidden, saved_layers[layer_index], layer_index, weights, geometry
        )
        layer_results.insert(0, layer_grads)
    finals = reduce_all(layer_results, cycle_size)
    return (
        output,
        grad_hidden,
        finals[0],
        finals[1],
        finals[2],
        finals[3],
        finals[4],
        finals[5],
        finals[6],
    )


def solution(mesh):
    placed = (
        P(("grp", "blk"), None),
        P("grp", None),
        P(),
        P(),
        P(),
        P(),
        P(),
        P(),
        P(),
        P(("grp", "blk"), None),
    )
    sizes = (mesh.shape["grp"], mesh.shape["blk"])
    return jax.shard_map(
        fast_body if sizes == (4, RUNS) else body,
        mesh=mesh,
        in_specs=placed,
        out_specs=(
            P(("grp", "blk"), None),
            P(("grp", "blk"), None),
            P(None, "blk", None),
            P(None, "blk", None),
            P(None, "blk", None),
            P(None, "blk"),
            P(None, "blk", None),
            P(None, "blk"),
            P(),
        ),
        check_vma=False,
    )
```

```python
import functools

import jax
import jax.numpy as jnp
from jax import lax
from jax.experimental import pallas as pl
from jax.experimental.pallas import tpu as pltpu
from jax.sharding import PartitionSpec as P

HEADS = 8
LAYERS = 2
NEGATIVE = -1e30
MESH = pl.DeviceIdType.MESH
F32 = jnp.float32
BF16 = jnp.bfloat16

HALF = 128
RUNS = 8
TEAM = 4
OWN = RUNS // TEAM
DIM = 64
WIDTH = 512
FF = 2048
CUT = 512
TILE = 256
TILES = HALF * RUNS // TILE
PACK = HALF + DIM
CHUNK = 576
SMALL = FF + WIDTH + 128
PARTS = ((1, 0, 320), (1, 320, 256), (0, 0, 320), (0, 320, 256))
SHARES = ((192, 0, 128), (160, 16, 80), (160, 128, 32), (128, 96, 32))


def spans():
    places, totals = {}, [0, 0, 0]
    for part, counts in enumerate(SHARES):
        first = PARTS[part][1]
        for route, count in enumerate(counts):
            places[part, route] = (first, totals[route], count)
            first += count
            totals[route] += count
    return places, totals


SPANS, TOTALS = spans()

SLOPE_AT = 0.28
TAIL = (
    0.11652077851573843,
    0.06749675579450809,
    0.2689101589486142,
    -0.23699347299932225,
    0.3898740127620002,
    -0.10580824228351815,
)


def nn(a, b):
    return lax.dot_general(a, b, (((1,), (0,)), ((), ())), preferred_element_type=F32)


def nt(a, b):
    return lax.dot_general(a, b, (((1,), (1,)), ((), ())), preferred_element_type=F32)


def beside(first, other):
    low = lax.broadcasted_iota(jnp.int32, first.shape, 1) < DIM
    return (
        jnp.where(low, first, pltpu.roll(other, DIM, 1)),
        jnp.where(low, pltpu.roll(first, DIM, 1), other),
    )


def layers_kernel(
    tokens, seq_len_hbm, alphas_hbm, up_bias_hbm, down_bias_hbm, cotangent, qkv_hbm, out_hbm, up_hbm, down_hbm,
    final, heads_all, out_in, grad_in, small_final,
    seq_len, alphas, wqkv, wout, wup, wdown, up_bias, down_bias,
    tok_in, cot_in, flag_out, flag_in, back_out,
    hidden, grad, hid_all, attn_t, entered, act, branch, slope, second,
    dz, du, da, dqkv,
    pack_out, head_out, pack_in, o_in, do_in,
    kv, kv_t, rq, ro, o_t, probs, acc, dq_t, bias,
    parts, core_in, xa_in, xb_in, ya_in, yb_in, z_in, third_z, third_x, third_y,
    heads_out, heads_x, heads_z, heads_sum, small, small_in, small_z, small_sum,
    w_sem, move_send, move_recv, a2a_send, a2a_recv, core_send, core_recv, x_send, x_recv, y_send, y_recv,
    z_send, z_recv, fin_send, fin_recv, hid_send, hid_recv, hx_send, hx_recv, hz_send, hz_recv, hf_send, hf_recv,
    small_send, small_recv, core_free,
):
    grp = lax.axis_index("grp")
    blk = lax.axis_index("blk")
    core = lax.rem(grp, 2)
    side = lax.div(grp, 2)
    yy = lax.rem(blk, 2)
    zz = lax.div(blk, 2)
    member = 2 * core + yy
    far_side = 2 * (1 - side) + core

    def place(c, x, z, y):
        return (2 * x + c, 2 * z + y)

    core_peer = place(1 - core, side, zz, yy)
    x_peer = place(core, 1 - side, zz, yy)
    y_peer = place(core, side, zz, 1 - yy)

    def remote(source, target, send, recv, peer):
        return pltpu.make_async_remote_copy(
            src_ref=source,
            dst_ref=target,
            send_sem=send,
            recv_sem=recv,
            device_id=peer,
            device_id_type=MESH,
        )

    def credit(semaphore, peer, count=1):
        pl.semaphore_signal(semaphore, inc=count, device_id=peer, device_id_type=MESH)

    def moved(kind, slot, source, target, at, core_at, z_at):
        here = jnp.logical_and(core_at == core, z_at == zz)

        @pl.when(here)
        def _():
            pltpu.make_async_copy(source, target.at[at], move_recv.at[kind, at]).start()

        @pl.when(jnp.logical_not(here))
        def _():
            pltpu.make_async_remote_copy(
                src_ref=source,
                dst_ref=target.at[at],
                send_sem=move_send.at[kind, slot],
                recv_sem=move_recv.at[kind, at],
                device_id=place(core_at, side, z_at, yy),
                device_id_type=MESH,
            ).start()

    def move_left(kind, slot, source, core_at, z_at):
        here = jnp.logical_and(core_at == core, z_at == zz)

        @pl.when(jnp.logical_not(here))
        def _():
            pltpu.make_async_copy(source, source, move_send.at[kind, slot]).wait()

    def move_arrived(kind, at, target):
        pltpu.make_async_copy(target.at[at], target.at[at], move_recv.at[kind, at]).wait()

    def to_team(kind, half, source, target):
        moved(kind, half, source, target, lax.div(zz, 2), lax.rem(zz, 2), 2 * half + core)

    def to_team_left(kind, half, source):
        move_left(kind, half, source, lax.rem(zz, 2), 2 * half + core)

    def to_owner(kind, chunk, source, target):
        moved(kind, chunk, source, target, lax.div(zz, 2), lax.rem(zz, 2), core + 2 * chunk)

    def to_owner_left(kind, chunk, source):
        move_left(kind, chunk, source, lax.rem(zz, 2), core + 2 * chunk)

    def half_of(ref, half):
        return ref.at[pl.ds(pl.multiple_of(HALF * half, HALF), HALF)]

    def rows_of(half):
        return pl.ds(pl.multiple_of(half * HALF, HALF), HALF)

    def slot_of(other):
        return lax.rem(other + TEAM - member, TEAM)

    def exchange(kind, layer, half, outgoing, incoming, head=None):
        at = () if head is None else (head,)
        incoming[(half, 0, *at)] = outgoing[(half, member, *at)]
        for step in range(1, TEAM):
            peer = lax.rem(member + step, TEAM)
            remote(
                outgoing.at[(half, peer, *at)],
                incoming.at[(half, TEAM - step, *at)],
                a2a_send.at[kind, layer, half, head or 0],
                a2a_recv.at[kind, layer, half, head or 0],
                place(lax.div(peer, 2), side, zz, lax.rem(peer, 2)),
            ).start()

    def arrived(kind, layer, half, incoming, head=None):
        at = () if head is None else (head,)
        whole = incoming.at[(half, pl.ds(1, TEAM - 1), *at)]
        pltpu.make_async_copy(whole, whole, a2a_recv.at[kind, layer, half, head or 0]).wait()

    def left(kind, layer, half, outgoing):
        for head in range(OWN) if kind in (0, 3) else (None,):
            at = () if head is None else (head,)
            whole = outgoing.at[(half, pl.ds(1, TEAM - 1), *at)]
            pltpu.make_async_copy(whole, whole, a2a_send.at[kind, layer, half, head or 0]).wait()

    def tokens_of(chunk, other):
        return pl.ds(pl.multiple_of(HALF * (TEAM * chunk + other), HALF), HALF)

    def hidden_copy(layer, chunk, which):
        whose = 2 * core + 1 - yy if which == 2 else member
        block = hid_all.at[layer, :, tokens_of(chunk, whose)]
        return remote(
            block,
            block,
            hid_send.at[layer, chunk, which],
            hid_recv.at[layer, chunk, which],
            y_peer if which == 0 else core_peer,
        )

    def hidden_start(layer, chunk):
        for which in range(2):
            hidden_copy(layer, chunk, which).start()

    def hidden_pass(layer, chunk):
        hidden_copy(layer, chunk, 0).wait()
        hidden_copy(layer, chunk, 2).start()

    def hidden_done(layer, chunk):
        for which in range(1, 3):
            hidden_copy(layer, chunk, which).wait()

    def project(layer, half):
        rows = rows_of(half)
        rounded = hidden[rows, :].astype(BF16)
        if layer == 1:
            left(0, 0, half, pack_out)
        queries = (nn(rounded, wqkv[layer, :, 0:WIDTH]) * (DIM ** -0.5)).astype(BF16).T
        for head in range(RUNS):
            pack_out[half, head // 2, head % 2, HALF:, :] = queries[DIM * head : DIM * head + DIM, :]
        for step in range(2):
            at = WIDTH * (step + 1)
            keys_values = nn(rounded, wqkv[layer, :, at : at + WIDTH]).astype(BF16)
            for head in range(4):
                pack_out[half, 2 * step + head // 2, head % 2, 0:HALF, :] = keys_values[
                    :, 128 * head : 128 * head + 128
                ]
        for head in range(OWN):
            exchange(0, layer, half, pack_out, pack_in, head)
        hid_all[layer, :, tokens_of(half, member)] = rounded.T

    def rows_before(i):
        return TILE * i * (i + 1) // 2

    def attend(layer, chunk):
        if layer == 1:
            left(1, 0, chunk, head_out)

        def one_head(head, carry):
            arrived(0, layer, chunk, pack_in, head)
            for other in range(TEAM):
                slot = slot_of(other)
                start = HALF * (TEAM * chunk + other)
                span = slice(start, start + HALF)
                block = pack_in[chunk, slot, head, 0:HALF, :]
                kv[layer, head, span, :] = block
                kv_t[layer, head, :, span] = block.T
                rq[layer, head, 0:DIM, span] = pack_in[chunk, slot, head, HALF:, :]

            def scores_of(i):
                count = TILE * (i + 1)
                tile = rq[layer, head, :, TILE * i : TILE * i + TILE]
                return nn(kv[layer, head, 0:count, :], tile) + bias[TILE * TILES - count :, :]

            ahead = [scores_of(i) for i in (2 * chunk, 2 * chunk + 1)]
            for i in (2 * chunk, 2 * chunk + 1):
                columns = slice(TILE * i, TILE * i + TILE)
                count = TILE * (i + 1)
                scores = ahead[i - 2 * chunk]
                largest = jnp.max(scores, axis=0, keepdims=True)
                weight = jnp.exp(scores - largest)
                total = jnp.sum(weight, axis=0, keepdims=True)
                share = (weight * (1.0 / total)).astype(BF16)
                probs[layer, head, rows_before(i) : rows_before(i) + count, :] = share
                summed = nn(kv_t[layer, head, DIM:, 0:count], share)
                o_t[layer, head, :, columns] = summed
                rounded = summed.astype(BF16)
                for part in range(2):
                    head_out[chunk, 2 * (i - 2 * chunk) + part, head] = rounded[
                        :, HALF * part : HALF * part + HALF
                    ]
            return carry

        for head in range(OWN):
            one_head(head, 0)
        exchange(1, layer, chunk, head_out, o_in)

    def feed(layer, half):
        rows = rows_of(half)
        arrived(1, layer, half, o_in)
        for head in range(RUNS):
            attn_t[layer, DIM * head : DIM * head + DIM, rows] = o_in[half, slot_of(head // 2), head % 2]
        attn = attn_t[layer, :, rows].T
        grown = nn(attn, wout[layer])
        branch[layer, rows, :] = grown
        middle = hidden[rows, :] + alphas[layer, 0] * grown
        rounded = middle.astype(BF16)
        entered[layer, rows, :] = rounded
        total = jnp.zeros((HALF, WIDTH), F32)

        def gate_of(step):
            cut = slice(CUT * step, CUT * step + CUT)
            return nn(rounded, wup[layer, :, cut]) + up_bias[layer : layer + 1, cut]

        coming = gate_of(0)
        for step in range(FF // CUT):
            cut = slice(CUT * step, CUT * step + CUT)
            gate = coming
            if step + 1 < FF // CUT:
                coming = gate_of(step + 1)
            bell = jnp.exp(gate * gate * -0.5)
            near = pl.reciprocal(1.0 + SLOPE_AT * jnp.abs(gate), approx=True)
            tail = jnp.full_like(gate, TAIL[5])
            for factor in TAIL[4::-1]:
                tail = tail * near + factor
            tail = bell * (tail * near)
            risen = jnp.where(gate > 0.0, 1.0 - tail, tail)
            slope[layer, rows, cut] = risen + gate * bell * 0.3989422804014327
            active = (gate * risen).astype(BF16)
            act[layer, rows, cut] = active
            total = total + nn(active, wdown[layer, cut, :])
        total = total + down_bias[layer : layer + 1, :]
        second[layer, rows, :] = total
        hidden[rows, :] = middle + alphas[layer, 1] * total

    def total_of(values):
        return jnp.sum(jnp.sum(values, axis=0, keepdims=True), axis=1, keepdims=True)

    def feed_back(layer):
        start = grad[...]
        if layer == 0:
            dz[...] = (alphas[layer, 1] * start).astype(BF16)
        scaled = dz[...]
        alpha_second = total_of(start * second[layer])
        small[layer : layer + 1, FF : FF + WIDTH] = jnp.sum(scaled.astype(F32), axis=0, keepdims=True)
        middle = start
        coming = nt(scaled, wdown[layer, 0:CUT, :])
        for step in range(FF // CUT):
            cut = slice(CUT * step, CUT * step + CUT)
            raw = coming
            if step + 1 < FF // CUT:
                coming = nt(scaled, wdown[layer, CUT * (step + 1) : CUT * (step + 2), :])
            gate = (raw * slope[layer, :, cut]).astype(BF16)
            du[:, cut] = gate
            small[layer : layer + 1, cut] = jnp.sum(gate.astype(F32), axis=0, keepdims=True)
            middle = middle + nt(gate, wup[layer, :, cut])
        grad[...] = middle
        mixed = (alphas[layer, 0] * middle).astype(BF16)
        da[...] = mixed
        spread = nt(wout[layer], mixed).astype(BF16)
        for chunk in (1, 0):
            left(*((1, 1) if layer == 1 else (2, 1)), chunk, head_out)
            for head in range(RUNS):
                head_out[chunk, head // 2, head % 2] = spread[
                    DIM * head : DIM * head + DIM, HALF * chunk : HALF * chunk + HALF
                ]
            exchange(2, layer, chunk, head_out, do_in)
        alpha_first = total_of(middle * branch[layer])
        column = lax.broadcasted_iota(jnp.int32, (1, 128), 1)
        small[layer : layer + 1, FF + WIDTH :] = jnp.where(
            column == 0, alpha_first, jnp.where(column == 1, alpha_second, 0.0)
        )

    def attend_back(layer, chunk):
        arrived(2, layer, chunk, do_in)
        left(*((0, 1) if layer == 1 else (3, 1)), chunk, pack_out)

        def one_head(head, carry):
            for other in range(TEAM):
                start = HALF * (TEAM * chunk + other)
                ro[head, DIM:, start : start + HALF] = do_in[chunk, slot_of(other), head]
            for i in (2 * chunk, 2 * chunk + 1):
                columns = slice(TILE * i, TILE * i + TILE)
                query_tile = rq[layer, head, :, columns]
                grad_tile = ro[head, :, columns]
                delta = jnp.sum(
                    ro[head, DIM:, columns].astype(F32) * o_t[layer, head, :, columns],
                    axis=0,
                    keepdims=True,
                )
                count = TILE * (i + 1)
                keys = kv[layer, head, 0:count, :]
                share = probs[layer, head, rows_before(i) : rows_before(i) + count, :]
                scored = (share.astype(F32) * (nn(keys, grad_tile) - delta)).astype(BF16)
                term = nt(scored, query_tile) + nt(share, grad_tile)
                if chunk == 1 and i == 2:
                    acc[head, 0:count, :] = term
                elif chunk == 1:
                    acc[head, 0 : count - TILE, :] += term[0 : count - TILE, :]
                    acc[head, count - TILE : count, :] = term[count - TILE :, :]
                else:
                    acc[head, 0:count, :] += term
                query_grad = nn(kv_t[layer, head, 0:DIM, 0:count], scored)
                dq_t[head, :, columns] = query_grad * (DIM ** -0.5)
            for other in range(TEAM):
                start = HALF * (TEAM * chunk + other)
                span = slice(start, start + HALF)
                pack_out[chunk, other, head, 0:HALF, :] = acc[head, span, :].astype(BF16)
                pack_out[chunk, other, head, HALF:, :] = dq_t[head, :, span].astype(BF16)
            exchange(3, layer, chunk, pack_out, pack_in, head)
            return carry

        for head in range(OWN):
            one_head(head, 0)

    def project_back(layer, half):
        for head in range(OWN):
            arrived(3, layer, half, pack_in, head)
        turned = jnp.concatenate(
            [pack_in[half, slot_of(head // 2), head % 2, HALF:, :] for head in range(RUNS)], axis=0
        )
        dqkv[:, 0:WIDTH] = turned.T
        for head in range(RUNS):
            at = WIDTH + 128 * head
            dqkv[:, at : at + 128] = pack_in[half, slot_of(head // 2), head % 2, 0:HALF, :]
        rows = rows_of(half)
        grad[rows, :] = grad[rows, :] + nt(dqkv[...], wqkv[layer])

    def scatter_rows(layer, result, first_row):
        for run in range(RUNS):
            for quarter in range(4):
                parts[layer, quarter % 2, quarter // 2, run // 2, run % 2, first_row : first_row + DIM, :] = result[
                    DIM * run : DIM * run + DIM, 128 * quarter : 128 * quarter + 128
                ].astype(BF16)

    def make(part):
        layer, first, count = PARTS[part]
        if first < 256:
            turned = entered[layer].T
        for row in range(first, min(first + count, 256), DIM):
            step = row // DIM
            scatter_rows(layer, nn(turned, du[:, CUT * step : CUT * step + CUT]), row)
        if first <= 256 < first + count:
            scatter_rows(layer, nn(attn_t[layer], da[...]), 256)
        if first >= 320:
            turned = dz[...].T
            for step in range(FF // CUT):
                result = nn(turned, act[layer, :, CUT * step : CUT * step + CUT])
                for block in range(CUT // 128):
                    run, row = 2 * step + block // 2, 320 + 128 * (block % 2)
                    for quarter in range(4):
                        parts[layer, quarter % 2, quarter // 2, run // 2, run % 2, row : row + 128, :] = result[
                            128 * quarter : 128 * quarter + 128, 128 * block : 128 * block + 128
                        ].astype(BF16)
        if layer == 0:
            pl.semaphore_wait(core_free.at[0 if first < 320 else 1], 1)
        core_copy(part).start()

    def heads_grads(layer):
        for chunk in range(2):
            hidden_done(layer, chunk)
        blocks = [(run // TEAM, run % TEAM) for run in range(RUNS)]
        keys_values = jnp.concatenate(
            [
                jnp.concatenate([pack_out[chunk, other, head, 0:HALF, :] for chunk, other in blocks], axis=0)
                for head in range(OWN)
            ],
            axis=1,
        )
        queries = jnp.concatenate(
            [
                jnp.concatenate([pack_out[chunk, other, head, HALF:, :] for chunk, other in blocks], axis=1)
                for head in range(OWN)
            ],
            axis=0,
        )
        both = nn(hid_all[layer], keys_values)
        q_part = nt(hid_all[layer], queries)
        for number, values in enumerate((q_part, both[:, 0:128], both[:, 128:256])):
            for run in range(RUNS):
                heads_out[layer, run // 2, run % 2, :, 128 * number : 128 * number + 128] = values[
                    DIM * run : DIM * run + DIM, :
                ].astype(BF16)
        heads_x_copy(layer).start()

    def half_rows(which):
        return pl.ds(pl.multiple_of(32 * which, 32), 32)

    def heads_x_copy(layer):
        return remote(
            heads_out.at[layer, :, :, half_rows(1 - side)],
            heads_x.at[layer],
            hx_send.at[layer],
            hx_recv.at[layer],
            x_peer,
        )

    def heads_z_copy(layer, step):
        peer = lax.rem(zz + step, 4)
        return remote(
            heads_out.at[layer, peer, :, half_rows(side)],
            heads_z.at[layer, 4 - step],
            hz_send.at[layer, step],
            hz_recv.at[layer, 4 - step],
            place(core, side, peer, yy),
        )

    def heads_last_copy(layer, number):
        x, c, y = number // 4, number // 2 % 2, number % 2
        return remote(
            heads_sum.at[layer, 1 - yy if y else yy],
            heads_all.at[layer, side, member],
            hf_send.at[layer, number],
            hf_recv.at[layer, number],
            place(1 - core if c else core, 1 - side if x else side, zz, 1 - yy if y else yy),
        )

    def heads_second(layer):
        heads_x_copy(layer).wait()
        heads_out[layer, :, :, half_rows(side), :] += heads_x[layer]
        for step in range(1, 4):
            heads_z_copy(layer, step).start()

    def heads_third(layer):
        for step in range(1, 4):
            heads_z_copy(layer, step).wait()
        total = heads_out[layer, zz, :, half_rows(side), :].astype(F32)
        for slot in range(1, 4):
            total = total + heads_z[layer, slot].astype(F32)
        heads_sum[layer] = total.astype(BF16)
        heads_all[layer, side, member] = heads_sum[layer, yy]
        for number in range(1, 8):
            heads_last_copy(layer, number).start()

    def heads_done(layer):
        for number in range(1, 8):
            heads_last_copy(layer, number).wait()

    def rows_in(part, route):
        first, room, count = SPANS[part, route]
        return pl.ds(first, count), pl.ds(room, count)

    def used(part, route):
        return SHARES[part][route] > 0

    def core_copy(part):
        layer, first, count = PARTS[part]
        rows = pl.ds(first, count)
        return remote(
            parts.at[layer, 1 - core, :, :, :, rows],
            core_in.at[:, :, :, rows],
            core_send.at[part],
            core_recv.at[part],
            core_peer,
        )

    def x_copy(part, route):
        layer = PARTS[part][0]
        rows, room = rows_in(part, route)
        ends = (x_send.at[part, route], x_recv.at[part, route], x_peer)
        mine = parts.at[layer, core, 1 - side]
        if route == 0:
            return remote(mine.at[:, :, rows], xa_in.at[:, :, room], *ends)
        if route == 1:
            return remote(mine.at[:, yy, rows], xb_in.at[:, room], *ends)
        return remote(mine.at[zz, :, rows], third_x.at[:, room], *ends)

    def y_copy(part, route):
        layer = PARTS[part][0]
        rows, room = rows_in(part, route)
        ends = (y_send.at[part, route], y_recv.at[part, route], y_peer)
        mine = parts.at[layer, core]
        if route == 0:
            return remote(mine.at[side, :, 1 - yy, rows], ya_in.at[:, room], *ends)
        if route == 1:
            return remote(mine.at[:, :, 1 - yy, rows], yb_in.at[:, :, room], *ends)
        return remote(mine.at[side, zz, 1 - yy, rows], third_y.at[room], *ends)

    def z_copy(part, route, step):
        layer = PARTS[part][0]
        rows, room = rows_in(part, route)
        peer = lax.rem(zz + step, 4)
        ends = (z_send.at[part, route, step], z_recv.at[part, route, 4 - step], place(core, side, peer, yy))
        if route == 2:
            return remote(parts.at[layer, core, :, peer, :, rows], third_z.at[4 - step, :, :, room], *ends)
        return remote(parts.at[layer, core, side, peer, yy, rows], z_in.at[layer, 4 - step, rows], *ends)

    def final_copy(part, which):
        layer, first, count = PARTS[part]
        block = final.at[layer, far_side if which == 2 else grp, pl.ds(first, count)]
        return remote(
            block,
            block,
            fin_send.at[part, which],
            fin_recv.at[part, which],
            x_peer if which == 0 else core_peer,
        )

    def core_done(part):
        layer, first, count = PARTS[part]
        rows = pl.ds(first, count)
        core_copy(part).wait()
        for across in (1 - side, side):
            parts[layer, core, across, :, :, rows, :] += core_in[across, :, :, rows, :]
            if used(part, 0) and across is not side:
                x_copy(part, 0).start()
        if used(part, 1):
            y_copy(part, 1).start()
        if used(part, 2):
            for step in range(1, 4):
                z_copy(part, 2, step).start()
        if layer == 1:
            freed = 0 if first < 320 else 1
            followers = [1 for other in PARTS if other[0] == 0 and (other[1] >= 320) == (freed == 1)]
            credit(core_free.at[freed], core_peer, len(followers))

    def first_x(part):
        if used(part, 0):
            layer = PARTS[part][0]
            rows, room = rows_in(part, 0)
            x_copy(part, 0).wait()
            for y in (1 - yy, yy):
                parts[layer, core, side, :, y, rows, :] += xa_in[:, y, room, :]
                if y is not yy:
                    y_copy(part, 0).start()

    def first_y(part):
        if used(part, 1):
            layer = PARTS[part][0]
            rows, room = rows_in(part, 1)
            y_copy(part, 1).wait()
            for across in (1 - side, side):
                parts[layer, core, across, :, yy, rows, :] += yb_in[across, :, room, :]
                if across is not side:
                    x_copy(part, 1).start()

    def first_z(part):
        if used(part, 2):
            layer = PARTS[part][0]
            rows, room = rows_in(part, 2)
            for step in range(1, 4):
                z_copy(part, 2, step).wait()
            for across in (1 - side, side):
                total = parts[layer, core, across, zz, :, rows, :].astype(F32)
                for slot in range(1, 4):
                    total = total + third_z[slot, across, :, room, :].astype(F32)
                parts[layer, core, across, zz, :, rows, :] = total.astype(BF16)
                if across is not side:
                    x_copy(part, 2).start()

    def second_x(part):
        if used(part, 0):
            layer = PARTS[part][0]
            rows, room = rows_in(part, 0)
            y_copy(part, 0).wait()
            parts[layer, core, side, :, yy, rows, :] += ya_in[:, room, :]
            for step in range(1, 4):
                z_copy(part, 0, step).start()

    def second_y(part):
        if used(part, 1):
            layer = PARTS[part][0]
            rows, room = rows_in(part, 1)
            x_copy(part, 1).wait()
            parts[layer, core, side, :, yy, rows, :] += xb_in[:, room, :]
            for step in range(1, 4):
                z_copy(part, 1, step).start()

    def second_z(part):
        if used(part, 2):
            layer = PARTS[part][0]
            rows, room = rows_in(part, 2)
            x_copy(part, 2).wait()
            for y in (1 - yy, yy):
                parts[layer, core, side, zz, y, rows, :] += third_x[y, room, :]
                if y is not yy:
                    y_copy(part, 2).start()

    def third_done(part):
        layer = PARTS[part][0]
        for route in range(3):
            if not used(part, route):
                continue
            rows, room = rows_in(part, route)
            if route == 2:
                y_copy(part, 2).wait()
                final[layer, grp, rows, :] = parts[layer, core, side, zz, yy, rows, :] + third_y[room, :]
            else:
                for step in range(1, 4):
                    z_copy(part, route, step).wait()
                total = parts[layer, core, side, zz, yy, rows, :].astype(F32)
                for slot in range(1, 4):
                    total = total + z_in[layer, slot, rows, :].astype(F32)
                final[layer, grp, rows, :] = total.astype(BF16)
        if PARTS[part][1] >= 320:
            for row in (320, 448):
                final[layer, grp, row : row + 128, :] = final[layer, grp, row : row + 128, :].T
        for which in range(2):
            final_copy(part, which).start()

    def final_pass(part):
        final_copy(part, 0).wait()
        final_copy(part, 2).start()

    def final_done(part):
        for which in range(1, 3):
            final_copy(part, which).wait()

    def small_copy(stage):
        peer = (core_peer, x_peer, y_peer)[stage]
        return remote(
            small_sum.at[stage], small_in.at[stage], small_send.at[stage], small_recv.at[stage], peer
        )

    def small_z_copy(step):
        return remote(
            small_z.at[zz],
            small_z.at[zz],
            small_send.at[2 + step],
            small_recv.at[2 + step],
            place(core, side, lax.rem(zz + step, 4), yy),
        )

    def small_start():
        small_sum[0] = small[...]
        small_copy(0).start()

    def small_next(stage):
        small_copy(stage).wait()
        total = small_sum[stage] + small_in[stage]
        if stage < 2:
            small_sum[stage + 1] = total
            small_copy(stage + 1).start()
        else:
            small_z[zz] = total
            for step in range(1, 4):
                small_z_copy(step).start()

    def small_done():
        for step in range(1, 4):
            small_z_copy(step).wait()
        small_sum[0] = (small_z[0] + small_z[1]) + (small_z[2] + small_z[3])
        small_final[:, 0:256] = small_sum[0, :, pl.ds(pl.multiple_of(blk * 256, 256), 256)]
        pair = small_sum[0, :, pl.ds(pl.multiple_of(FF + 128 * zz, 128), 128)]
        small_final[:, 256:384] = jnp.where(yy == 1, pltpu.roll(pair, DIM, 1), pair)
        small_final[:, 384:512] = small_sum[0, :, FF + WIDTH :]

    def halves(*phases, first=0):
        def both(step, carry):
            for phase in phases:
                phase(lax.rem(step + first, 2))
            return carry

        lax.fori_loop(0, 2, both, 0)

    def begin(half):
        move_arrived(0, half, tok_in)
        hidden[rows_of(half), :] = tok_in[half].astype(F32)

    def finish(half):
        back_out[0, half] = hidden[rows_of(half), :].astype(BF16)
        to_owner(3, half, back_out.at[0, half], out_in)

    def turn_round(layer, half):
        move_arrived(2, half, cot_in)
        rows = rows_of(half)
        grad[rows, :] = cot_in[half].astype(F32)
        dz[rows, :] = (alphas[layer, 1] * grad[rows, :]).astype(BF16)

    def hand_back(half):
        back_out[1, half] = grad[rows_of(half), :].astype(BF16)
        to_owner(4, half, back_out.at[1, half], grad_in)

    barrier = pltpu.get_barrier_semaphore()
    for step in range(1, 4):
        credit(barrier, place(core, side, lax.rem(zz + step, 4), yy))
    for step in range(4):
        credit(barrier, place(1 - core, side, lax.rem(zz + step, 4), yy))
    for peer in (
        x_peer,
        y_peer,
        place(1 - core, side, zz, 1 - yy),
        place(1 - core, 1 - side, zz, yy),
        place(core, 1 - side, zz, 1 - yy),
        place(1 - core, 1 - side, zz, 1 - yy),
    ):
        credit(barrier, peer)

    weight_copies = {}
    for layer in range(LAYERS):
        for number, (source, target) in enumerate(
            ((qkv_hbm, wqkv), (out_hbm, wout), (up_hbm, wup), (down_hbm, wdown))
        ):
            weight_copies[layer, number] = pltpu.make_async_copy(
                source.at[layer], target.at[layer], w_sem.at[layer, number]
            )
    bias_copies = [
        pltpu.make_async_copy(up_bias_hbm, up_bias, w_sem.at[2, 0]),
        pltpu.make_async_copy(down_bias_hbm, down_bias, w_sem.at[2, 1]),
        pltpu.make_async_copy(alphas_hbm, alphas, w_sem.at[2, 2]),
    ]
    length_copy = pltpu.make_async_copy(seq_len_hbm, seq_len, w_sem.at[2, 3])
    length_copy.start()
    weight_copies[0, 0].start()
    pl.semaphore_wait(barrier, 13)
    upper = lax.div(zz, 2)
    for half in (1 - upper, upper):
        to_team(0, half, half_of(tokens, half), tok_in)
    for layer, number in ((1, 0), (0, 1), (0, 2), (0, 3), (1, 1), (1, 2), (1, 3)):
        weight_copies[layer, number].start(priority=1)
    for copy in bias_copies:
        copy.start(priority=1)
    length_copy.wait()
    end_second = lax.div(seq_len[0, 0] + seq_len[0, 1], RUNS)
    flag_out[...] = jnp.full((8, 128), end_second.astype(F32), F32)
    for half in (1 - upper, upper):
        to_team(1, half, flag_out, flag_in)
    for layer in range(LAYERS):
        for head in range(OWN):
            rq[layer, head, DIM:, :] = jnp.zeros((DIM, HALF * RUNS), BF16)
    for head in range(OWN):
        ro[head, 0:DIM, :] = jnp.zeros((DIM, HALF * RUNS), BF16)
    for layer in range(LAYERS):
        weight_copies[layer, 0].wait()
        pairs = [
            beside(
                wqkv[layer, :, WIDTH + 128 * pair : WIDTH + 128 * pair + 128].astype(F32),
                wqkv[layer, :, 2 * WIDTH + 128 * pair : 2 * WIDTH + 128 * pair + 128].astype(F32),
            )
            for pair in range(TEAM)
        ]
        for head in range(RUNS):
            at = WIDTH + 128 * head
            wqkv[layer, :, at : at + 128] = pairs[head // 2][head % 2].astype(BF16)
    halves(begin, functools.partial(project, 0), first=upper)
    for half in (1 - upper, upper):
        to_team(2, half, half_of(cotangent, half), cot_in)

    move_arrived(1, 0, flag_in)
    move_arrived(1, 1, flag_in)
    border = jnp.concatenate([flag_in[0, 0:1, :]] * 2, axis=1) - (HALF * lax.div(zz, 2)).astype(F32)
    key_row = lax.broadcasted_iota(jnp.int32, (TILE, TILE), 0)
    query_col = lax.broadcasted_iota(jnp.int32, (TILE, TILE), 1)
    later = key_row > query_col
    key_sub = lax.rem(key_row, HALF).astype(F32) >= border
    query_sub = lax.rem(query_col, HALF).astype(F32) >= border
    apart = jnp.logical_xor(key_sub, query_sub)
    for tile in range(TILES - 1):
        bias[TILE * tile : TILE * tile + TILE, :] = jnp.where(apart, NEGATIVE, 0.0)
    bias[TILE * (TILES - 1) :, :] = jnp.where(jnp.logical_or(later, apart), NEGATIVE, 0.0)

    for copy in (*bias_copies, *(weight_copies[0, number] for number in range(1, 4))):
        copy.wait()
    attend(0, 0)
    attend(0, 1)
    hidden_start(0, 0)
    halves(functools.partial(feed, 0), functools.partial(project, 1))
    for number in range(1, 4):
        weight_copies[1, number].wait()
    attend(1, 0)
    attend(1, 1)
    hidden_pass(0, 0)
    hidden_start(1, 0)
    halves(functools.partial(feed, 1), finish)
    hidden_start(0, 1)
    hidden_start(1, 1)
    hidden_pass(1, 0)

    halves(functools.partial(turn_round, 1))
    make(1)
    feed_back(1)
    hidden_pass(0, 1)
    hidden_pass(1, 1)
    core_done(1)
    make(0)
    attend_back(1, 1)
    first_y(1)
    core_done(0)
    attend_back(1, 0)
    second_y(1)
    first_x(1)
    project_back(1, 1)
    heads_grads(1)
    project_back(1, 0)
    feed_back(0)
    first_z(1)
    small_start()
    second_x(1)
    make(2)
    first_x(0)
    heads_second(1)
    attend_back(0, 1)
    first_z(0)
    small_next(0)
    core_done(2)
    second_x(0)
    make(3)
    attend_back(0, 0)
    heads_grads(0)
    small_next(1)
    project_back(0, 1)
    hand_back(1)
    first_z(2)
    small_next(2)
    first_x(2)
    core_done(3)
    first_y(2)
    heads_second(0)
    small_done()
    first_z(3)
    second_x(2)
    first_x(3)
    second_z(2)
    second_z(0)
    heads_third(1)
    second_z(1)
    first_y(3)
    heads_third(0)
    second_y(2)
    second_x(3)
    second_z(3)
    third_done(0)
    third_done(2)
    second_y(3)
    project_back(0, 0)
    hand_back(0)
    heads_done(1)
    third_done(1)
    third_done(3)
    final_pass(0)
    final_pass(2)
    final_pass(1)
    final_pass(3)
    final_done(2)
    final_done(1)
    heads_done(0)
    final_done(0)
    final_done(3)
    for half in range(2):
        move_arrived(3, half, out_in)
        move_arrived(4, half, grad_in)

    for half in range(2):
        left(2, 0, half, head_out)
        left(3, 0, half, pack_out)
        to_team_left(0, half, half_of(tokens, half))
        to_team_left(1, half, flag_out)
        to_team_left(2, half, half_of(cotangent, half))
        to_owner_left(3, half, back_out.at[0, half])
        to_owner_left(4, half, back_out.at[1, half])


def results_kernel(
    final, heads, out_block, grad_block, small,
    output, input_grad, qkv_grad, out_grad, up_grad, up_bias_grad, down_grad, down_bias_grad, alpha_grad,
    grad_wide, qkv_wide, out_wide, up_wide, down_wide, up_bias, down_bias, alpha, out_sem,
):
    ends = []

    def write(source, target):
        ends.append(pltpu.make_async_copy(source, target, out_sem.at[len(ends)]))
        ends[-1].start()

    for half in range(2):
        write(out_block.at[half], output.at[pl.ds(HALF * half, HALF)])
    up_bias[...] = small[:, 0:256]
    write(up_bias, up_bias_grad)
    down_bias[...] = small[:, 256 : 256 + DIM]
    write(down_bias, down_bias_grad)
    alpha[...] = small[:, 384:386]
    write(alpha, alpha_grad)
    for layer in range(LAYERS):
        for quarter in range(4):

            def block(first, count):
                return final[layer, quarter, first : first + count, :].astype(F32)

            def columns(step):
                return slice(WIDTH * step + 128 * quarter, WIDTH * step + 128 * quarter + 128)

            for step in range(4):
                up_wide[layer, :, columns(step)] = block(DIM * step, DIM)
            out_wide[layer, :, columns(0)] = block(256, DIM)
            down_wide[layer, :, columns(0)] = block(320, 256)
        write(up_wide.at[layer], up_grad.at[layer])
        write(out_wide.at[layer], out_grad.at[layer])
        write(down_wide.at[layer], down_grad.at[layer])
    for half in range(2):
        rows = slice(HALF * half, HALF * half + HALF)
        grad_wide[rows, :] = grad_block[half].astype(F32)
    write(grad_wide, input_grad)
    for layer in range(LAYERS):
        for side in range(2):
            for member in range(TEAM):
                block = heads[layer, side, member].astype(F32)
                columns = (block[:, 0:128], *beside(block[:, 128:256], block[:, 256:384]))
                for step in range(3):
                    at = WIDTH * step + 128 * member
                    qkv_wide[layer, 32 * side : 32 * side + 32, at : at + 128] = columns[step]
        write(qkv_wide.at[layer], qkv_grad.at[layer])
    for end in ends:
        end.wait()


def fast_body(
    tokens, seq_len, qkv_weight, out_weight, up_weight, up_bias, down_weight, down_bias, alphas, cotangent
):
    whole = pl.BlockSpec(memory_space=pltpu.VMEM)
    far = pl.BlockSpec(memory_space=pl.ANY)
    shape = jax.ShapeDtypeStruct
    rows = HALF * RUNS

    def vmem(*dims):
        return pltpu.VMEM(dims, BF16)

    def wide(*dims):
        return pltpu.VMEM(dims, F32)

    dma = pltpu.SemaphoreType.DMA
    final, heads, out_block, grad_block, small = pl.pallas_call(
        layers_kernel,
        out_shape=(
            vmem(LAYERS, 4, CHUNK, 128),
            vmem(LAYERS, 2, TEAM, DIM // 2, 3 * 128),
            vmem(2, HALF, WIDTH),
            vmem(2, HALF, WIDTH),
            wide(LAYERS, WIDTH),
        ),
        in_specs=[far, far, far, far, far, far, far, far, far, far],
        out_specs=(whole,) * 5,
        scratch_shapes=[
            pltpu.SMEM((1, 4), jnp.int32),
            pltpu.SMEM((LAYERS, 2), F32),
            vmem(LAYERS, WIDTH, 3 * WIDTH),
            vmem(LAYERS, WIDTH, WIDTH),
            vmem(LAYERS, WIDTH, FF),
            vmem(LAYERS, FF, WIDTH),
            wide(LAYERS, FF),
            wide(LAYERS, WIDTH),
            vmem(2, HALF, WIDTH),
            vmem(2, HALF, WIDTH),
            wide(8, 128),
            wide(2, 8, 128),
            vmem(2, 2, HALF, WIDTH),
            wide(2 * HALF, WIDTH),
            wide(2 * HALF, WIDTH),
            vmem(LAYERS, WIDTH, rows),
            vmem(LAYERS, WIDTH, 2 * HALF),
            vmem(LAYERS, 2 * HALF, WIDTH),
            vmem(LAYERS, 2 * HALF, FF),
            wide(LAYERS, 2 * HALF, WIDTH),
            wide(LAYERS, 2 * HALF, FF),
            wide(LAYERS, 2 * HALF, WIDTH),
            vmem(2 * HALF, WIDTH),
            vmem(2 * HALF, FF),
            vmem(2 * HALF, WIDTH),
            vmem(HALF, 3 * WIDTH),
            vmem(2, TEAM, OWN, PACK, 128),
            vmem(2, TEAM, OWN, DIM, 128),
            vmem(2, TEAM, OWN, PACK, 128),
            vmem(2, TEAM, OWN, DIM, 128),
            vmem(2, TEAM, OWN, DIM, 128),
            vmem(LAYERS, OWN, rows, 128),
            vmem(LAYERS, OWN, 128, rows),
            vmem(LAYERS, OWN, 128, rows),
            vmem(OWN, 128, rows),
            wide(LAYERS, OWN, DIM, rows),
            vmem(LAYERS, OWN, TILE * TILES * (TILES + 1) // 2, TILE),
            wide(OWN, rows, 128),
            wide(OWN, DIM, rows),
            wide(rows, TILE),
            vmem(LAYERS, 2, 2, 4, 2, CHUNK, 128),
            vmem(2, 4, 2, CHUNK, 128),
            vmem(4, 2, TOTALS[0], 128),
            vmem(4, TOTALS[1], 128),
            vmem(4, TOTALS[0], 128),
            vmem(2, 4, TOTALS[1], 128),
            vmem(LAYERS, 4, CHUNK, 128),
            vmem(4, 2, 2, TOTALS[2], 128),
            vmem(2, TOTALS[2], 128),
            vmem(TOTALS[2], 128),
            vmem(LAYERS, 4, 2, DIM, 3 * 128),
            vmem(LAYERS, 4, 2, DIM // 2, 3 * 128),
            vmem(LAYERS, 4, 2, DIM // 2, 3 * 128),
            vmem(LAYERS, 2, DIM // 2, 3 * 128),
            wide(LAYERS, SMALL),
            wide(3, LAYERS, SMALL),
            wide(4, LAYERS, SMALL),
            wide(3, LAYERS, SMALL),
            dma((LAYERS + 1, 4)),
            dma((5, 2)),
            dma((5, 2)),
            dma((4, LAYERS, 2, OWN)),
            dma((4, LAYERS, 2, OWN)),
            dma((len(PARTS),)),
            dma((len(PARTS),)),
            dma((len(PARTS), 3)),
            dma((len(PARTS), 3)),
            dma((len(PARTS), 3)),
            dma((len(PARTS), 3)),
            dma((len(PARTS), 3, 4)),
            dma((len(PARTS), 3, 4)),
            dma((len(PARTS), 3)),
            dma((len(PARTS), 3)),
            dma((LAYERS, 2, 3)),
            dma((LAYERS, 2, 3)),
            dma((LAYERS,)),
            dma((LAYERS,)),
            dma((LAYERS, 4)),
            dma((LAYERS, 4)),
            dma((LAYERS, 8)),
            dma((LAYERS, 8)),
            dma((6,)),
            dma((6,)),
            pltpu.SemaphoreType.REGULAR((2,)),
        ],
        compiler_params=pltpu.CompilerParams(
            collective_id=0, has_side_effects=True, vmem_limit_bytes=61 * 1024 * 1024
        ),
        name="layers",
    )(
        tokens, seq_len, alphas, up_bias, down_bias, cotangent,
        qkv_weight, out_weight, up_weight, down_weight,
    )
    return tuple(
        pl.pallas_call(
            results_kernel,
            out_shape=(
                shape((2 * HALF, WIDTH), BF16),
                shape((2 * HALF, WIDTH), F32),
                shape((LAYERS, DIM, 3 * WIDTH), F32),
                shape((LAYERS, DIM, WIDTH), F32),
                shape((LAYERS, DIM, FF), F32),
                shape((LAYERS, FF // RUNS), F32),
                shape((LAYERS, FF // RUNS, WIDTH), F32),
                shape((LAYERS, DIM), F32),
                shape((LAYERS, 2), F32),
            ),
            in_specs=[whole] * 5,
            out_specs=(far,) * 9,
            scratch_shapes=[
                wide(2 * HALF, WIDTH),
                wide(LAYERS, DIM, 3 * WIDTH),
                wide(LAYERS, DIM, WIDTH),
                wide(LAYERS, DIM, FF),
                wide(LAYERS, FF // RUNS, WIDTH),
                wide(LAYERS, FF // RUNS),
                wide(LAYERS, DIM),
                wide(LAYERS, 2),
                dma((14,)),
            ],
            compiler_params=pltpu.CompilerParams(vmem_limit_bytes=24 * 1024 * 1024),
            name="results",
        )(final, heads, out_block, grad_block, small)
    )


def layout(seq_len, local_count, cycle_size):
    piece_rows = seq_len[0] // cycle_size
    end_rows = jnp.cumsum(piece_rows)
    start_rows = end_rows - piece_rows
    local_rows = jnp.arange(local_count, dtype=jnp.int32)
    segment = jnp.sum((local_rows[:, None] >= end_rows[None, :]).astype(jnp.int32), axis=1)
    picked = segment[:, None] == jnp.arange(seq_len.shape[1], dtype=jnp.int32)[None, :]
    offset = local_rows - jnp.sum(jnp.where(picked, start_rows[None, :], 0), axis=1)
    span_rows = jnp.sum(jnp.where(picked, piece_rows[None, :], 0), axis=1)
    return (segment, offset, span_rows)


def gelu_exact(values):
    return jax.nn.gelu(values, approximate=False)


def key_block(whole, geometry, block_index, head_count):
    query_seg, query_pos, seg_all, pos_all, block_rows, score_scale = geometry
    first_row = block_index * block_rows
    key_piece = lax.dynamic_slice_in_dim(whole, first_row, block_rows, 0)
    key_seg = lax.dynamic_slice_in_dim(seg_all, first_row, block_rows, 0)
    key_pos = lax.dynamic_slice_in_dim(pos_all, first_row, block_rows, 0)
    half_width = key_piece.shape[1] // 2
    keys_part = key_piece[:, :half_width].reshape(block_rows, head_count, -1)
    values_part = key_piece[:, half_width:].reshape(block_rows, head_count, -1)
    return (keys_part, values_part, key_seg, key_pos)


def block_scores(queries, keys_part, key_seg, key_pos, geometry):
    query_seg, query_pos, seg_all, pos_all, block_rows, score_scale = geometry
    scores = (
        jnp.einsum("qhd,khd->hqk", queries, keys_part, preferred_element_type=jnp.float32)
        * score_scale
    )
    allowed = (query_seg[:, None] == key_seg[None, :]) & (key_pos[None, :] <= query_pos[:, None])
    return (scores, allowed[None])


def attend(queries, whole, geometry):
    row_count, head_count, head_dim = queries.shape
    block_count = whole.shape[0] // geometry[4]

    def statistics(running, block_index):
        largest, totals = running
        keys_part, values_part, key_seg, key_pos = key_block(
            whole, geometry, block_index, head_count
        )
        scores, allowed = block_scores(queries, keys_part, key_seg, key_pos, geometry)
        newest = jnp.maximum(largest, jnp.max(jnp.where(allowed, scores, NEGATIVE), axis=2))
        weights = jnp.where(allowed, jnp.exp(scores - newest[:, :, None]), 0.0)
        totals = totals * jnp.exp(largest - newest) + jnp.sum(weights, axis=2)
        return ((newest, totals), None)

    initial = (
        jnp.full((head_count, row_count), NEGATIVE, jnp.float32),
        jnp.zeros((head_count, row_count), jnp.float32),
    )
    (largest, totals), unused = lax.scan(statistics, initial, jnp.arange(block_count))
    log_total = largest + jnp.log(totals)

    def weighted(output_sum, block_index):
        keys_part, values_part, key_seg, key_pos = key_block(
            whole, geometry, block_index, head_count
        )
        scores, allowed = block_scores(queries, keys_part, key_seg, key_pos, geometry)
        probs = jnp.where(allowed, jnp.exp(scores - log_total[:, :, None]), 0.0).astype(
            jnp.bfloat16
        )
        output_sum = output_sum + jnp.einsum(
            "hqk,khd->qhd", probs, values_part, preferred_element_type=jnp.float32
        )
        return (output_sum, None)

    output_sum, unused = lax.scan(
        weighted, jnp.zeros((row_count, head_count, head_dim), jnp.float32), jnp.arange(block_count)
    )
    return (output_sum, log_total)


def attend_back(queries, whole, log_total, delta_sum, grad_heads, geometry):
    row_count, head_count, head_dim = queries.shape
    block_rows = geometry[4]
    score_scale = geometry[5]
    block_count = whole.shape[0] // block_rows

    def gradients(query_grad, block_index):
        keys_part, values_part, key_seg, key_pos = key_block(
            whole, geometry, block_index, head_count
        )
        scores, allowed = block_scores(queries, keys_part, key_seg, key_pos, geometry)
        probs = jnp.where(allowed, jnp.exp(scores - log_total[:, :, None]), 0.0)
        grad_probs = jnp.einsum(
            "qhd,khd->hqk", grad_heads, values_part, preferred_element_type=jnp.float32
        )
        grad_scores = (probs * (grad_probs - delta_sum[:, :, None])).astype(jnp.bfloat16)
        query_grad = (
            query_grad
            + jnp.einsum("hqk,khd->qhd", grad_scores, keys_part, preferred_element_type=jnp.float32)
            * score_scale
        )
        key_grad = (
            jnp.einsum("hqk,qhd->khd", grad_scores, queries, preferred_element_type=jnp.float32)
            * score_scale
        )
        value_grad = jnp.einsum(
            "hqk,qhd->khd",
            probs.astype(jnp.bfloat16),
            grad_heads,
            preferred_element_type=jnp.float32,
        )
        joined = jnp.concatenate(
            [key_grad.reshape(block_rows, -1), value_grad.reshape(block_rows, -1)], axis=1
        )
        return (query_grad, joined)

    query_grad, stacked = lax.scan(
        gradients,
        jnp.zeros((row_count, head_count, head_dim), jnp.float32),
        jnp.arange(block_count),
    )
    return (query_grad, stacked.reshape(whole.shape[0], -1))


def layer_forward(hidden, layer_index, weights, geometry):
    qkv_weight, out_weight, up_weight, up_bias, down_weight, down_bias, alphas = weights
    row_count, model_width = hidden.shape
    projection = qkv_weight[layer_index]
    rounded = hidden.astype(jnp.bfloat16)
    queries = (
        jnp.dot(rounded, projection[:, :model_width], preferred_element_type=jnp.float32)
        .astype(jnp.bfloat16)
        .reshape(row_count, HEADS, -1)
    )
    key_value = jnp.dot(
        rounded, projection[:, model_width:], preferred_element_type=jnp.float32
    ).astype(jnp.bfloat16)
    whole = lax.all_gather(key_value, "blk", axis=0, tiled=True)
    heads_out, log_total = attend(queries, whole, geometry)
    heads_rounded = heads_out.reshape(row_count, model_width).astype(jnp.bfloat16)
    branch = jnp.dot(heads_rounded, out_weight[layer_index], preferred_element_type=jnp.float32)
    alpha_pair = alphas[layer_index]
    middle = hidden + alpha_pair[0] * branch
    entered = middle.astype(jnp.bfloat16)
    gate_pre = (
        jnp.dot(entered, up_weight[layer_index], preferred_element_type=jnp.float32)
        + up_bias[layer_index]
    )
    activated = gelu_exact(gate_pre).astype(jnp.bfloat16)
    second = (
        jnp.dot(activated, down_weight[layer_index], preferred_element_type=jnp.float32)
        + down_bias[layer_index]
    )
    result = middle + alpha_pair[1] * second
    saved = (
        rounded,
        queries,
        key_value,
        whole,
        heads_out,
        heads_rounded,
        log_total,
        branch,
        entered,
        gate_pre,
        activated,
        second,
    )
    return (result, saved)


def layer_backward(grad_hidden, saved, layer_index, weights, geometry):
    qkv_weight, out_weight, up_weight, up_bias, down_weight, down_bias, alphas = weights
    (
        rounded,
        queries,
        key_value,
        saved_whole,
        heads_out,
        heads_rounded,
        log_total,
        branch,
        entered,
        gate_pre,
        activated,
        second,
    ) = saved
    row_count = grad_hidden.shape[0]
    alpha_pair = alphas[layer_index]
    grad_second = (alpha_pair[1] * grad_hidden).astype(jnp.bfloat16)
    alpha_second = jnp.sum(grad_hidden * second)
    bias_down = jnp.sum(grad_second.astype(jnp.float32), axis=0)
    grad_down = jnp.einsum("tf,td->fd", activated, grad_second, preferred_element_type=jnp.float32)
    grad_act = jnp.einsum(
        "td,fd->tf", grad_second, down_weight[layer_index], preferred_element_type=jnp.float32
    )
    unused, gelu_pull = jax.vjp(gelu_exact, gate_pre)
    grad_gate = gelu_pull(grad_act)[0].astype(jnp.bfloat16)
    bias_up = jnp.sum(grad_gate.astype(jnp.float32), axis=0)
    grad_up = jnp.einsum("td,tf->df", entered, grad_gate, preferred_element_type=jnp.float32)
    grad_middle = grad_hidden + jnp.einsum(
        "tf,df->td", grad_gate, up_weight[layer_index], preferred_element_type=jnp.float32
    )
    grad_branch = (alpha_pair[0] * grad_middle).astype(jnp.bfloat16)
    alpha_first = jnp.sum(grad_middle * branch)
    grad_proj_out = jnp.einsum(
        "te,td->ed", heads_rounded, grad_branch, preferred_element_type=jnp.float32
    )
    grad_heads = (
        jnp.einsum(
            "td,ed->te", grad_branch, out_weight[layer_index], preferred_element_type=jnp.float32
        )
        .astype(jnp.bfloat16)
        .reshape(queries.shape)
    )
    delta_sum = jnp.sum(grad_heads.astype(jnp.float32) * heads_out, axis=2).T
    whole = lax.all_gather(key_value, "blk", axis=0, tiled=True)
    query_grad, key_terms = attend_back(queries, whole, log_total, delta_sum, grad_heads, geometry)
    key_grads = lax.psum_scatter(
        key_terms.astype(jnp.bfloat16), "blk", scatter_dimension=0, tiled=True
    )
    grad_proj = jnp.concatenate(
        [query_grad.reshape(row_count, -1).astype(jnp.bfloat16), key_grads], axis=1
    )
    grad_qkv = jnp.einsum("td,te->de", rounded, grad_proj, preferred_element_type=jnp.float32)
    grad_input = grad_middle + jnp.einsum(
        "te,de->td", grad_proj, qkv_weight[layer_index], preferred_element_type=jnp.float32
    )
    layer_grads = (
        grad_qkv,
        grad_proj_out,
        grad_up,
        bias_up,
        grad_down,
        bias_down,
        jnp.stack([alpha_first, alpha_second]),
    )
    return (grad_input, layer_grads)


def reduce_all(layer_results, cycle_size):
    stacked = [
        jnp.stack([layer_entry[member] for layer_entry in layer_results], axis=0)
        for member in range(6)
    ]
    alpha_tiles = jnp.stack(
        [jnp.tile(layer_entry[6], cycle_size) for layer_entry in layer_results], axis=0
    )
    shares = (
        lax.psum_scatter(
            stacked[0].astype(jnp.bfloat16), "blk", scatter_dimension=1, tiled=True
        ).astype(jnp.float32),
        lax.psum_scatter(
            stacked[1].astype(jnp.bfloat16), "blk", scatter_dimension=1, tiled=True
        ).astype(jnp.float32),
        lax.psum_scatter(
            stacked[2].astype(jnp.bfloat16), "blk", scatter_dimension=1, tiled=True
        ).astype(jnp.float32),
        lax.psum_scatter(
            stacked[3].astype(jnp.bfloat16), "blk", scatter_dimension=1, tiled=True
        ).astype(jnp.float32),
        lax.psum_scatter(
            stacked[4].astype(jnp.bfloat16), "blk", scatter_dimension=1, tiled=True
        ).astype(jnp.float32),
        lax.psum_scatter(
            stacked[5].astype(jnp.bfloat16), "blk", scatter_dimension=1, tiled=True
        ).astype(jnp.float32),
        lax.psum_scatter(
            alpha_tiles.astype(jnp.bfloat16), "blk", scatter_dimension=1, tiled=True
        ).astype(jnp.float32),
    )
    return (
        lax.psum(shares[0].astype(jnp.bfloat16), "grp").astype(jnp.float32),
        lax.psum(shares[1].astype(jnp.bfloat16), "grp").astype(jnp.float32),
        lax.psum(shares[2].astype(jnp.bfloat16), "grp").astype(jnp.float32),
        lax.psum(shares[3].astype(jnp.bfloat16), "grp").astype(jnp.float32),
        lax.psum(shares[4].astype(jnp.bfloat16), "grp").astype(jnp.float32),
        lax.psum(shares[5].astype(jnp.bfloat16), "grp").astype(jnp.float32),
        lax.psum(shares[6].astype(jnp.bfloat16), "grp").astype(jnp.float32),
    )


def body(
    tokens,
    seq_len,
    qkv_weight,
    out_weight,
    up_weight,
    up_bias,
    down_weight,
    down_bias,
    alphas,
    cotangent,
):
    row_count, model_width = tokens.shape
    cycle_size = lax.axis_size("blk")
    cycle_place = lax.axis_index("blk")
    head_dim = model_width // HEADS
    total_rows = cycle_size * row_count
    block_rows = min(max(row_count, 512), total_rows)
    segment, offset, span_rows = layout(seq_len, row_count, cycle_size)
    query_pos = cycle_place * span_rows + offset
    seg_all = jnp.tile(segment, cycle_size)
    pos_all = jnp.repeat(jnp.arange(cycle_size, dtype=jnp.int32), row_count) * jnp.tile(
        span_rows, cycle_size
    ) + jnp.tile(offset, cycle_size)
    geometry = (segment, query_pos, seg_all, pos_all, block_rows, head_dim ** (-0.5))
    weights = (qkv_weight, out_weight, up_weight, up_bias, down_weight, down_bias, alphas)
    hidden = tokens.astype(jnp.float32)
    saved_layers = []
    for layer_index in range(LAYERS):
        hidden, saved = layer_forward(hidden, layer_index, weights, geometry)
        saved_layers.append(saved)
    output = hidden.astype(jnp.bfloat16)
    grad_hidden = cotangent.astype(jnp.float32)
    layer_results = []
    for layer_index in reversed(range(LAYERS)):
        grad_hidden, layer_grads = layer_backward(
            grad_hidden, saved_layers[layer_index], layer_index, weights, geometry
        )
        layer_results.insert(0, layer_grads)
    finals = reduce_all(layer_results, cycle_size)
    return (
        output,
        grad_hidden,
        finals[0],
        finals[1],
        finals[2],
        finals[3],
        finals[4],
        finals[5],
        finals[6],
    )


def solution(mesh):
    placed = (
        P(("grp", "blk"), None),
        P("grp", None),
        P(),
        P(),
        P(),
        P(),
        P(),
        P(),
        P(),
        P(("grp", "blk"), None),
    )
    sizes = (mesh.shape["grp"], mesh.shape["blk"])
    return jax.shard_map(
        fast_body if sizes == (4, RUNS) else body,
        mesh=mesh,
        in_specs=placed,
        out_specs=(
            P(("grp", "blk"), None),
            P(("grp", "blk"), None),
            P(None, "blk", None),
            P(None, "blk", None),
            P(None, "blk", None),
            P(None, "blk"),
            P(None, "blk", None),
            P(None, "blk"),
            P(),
        ),
        check_vma=False,
    )
```

```python
import functools

import jax
import jax.numpy as jnp
from jax import lax
from jax.experimental import pallas as pl
from jax.experimental.pallas import tpu as pltpu
from jax.sharding import PartitionSpec as P

HEADS = 8
LAYERS = 2
NEGATIVE = -1e30
MESH = pl.DeviceIdType.MESH
F32 = jnp.float32
BF16 = jnp.bfloat16

HALF = 128
RUNS = 8
TEAM = 4
OWN = RUNS // TEAM
DIM = 64
WIDTH = 512
FF = 2048
CUT = 512
TILE = 256
TILES = HALF * RUNS // TILE
PACK = HALF + DIM
CHUNK = 576
SMALL = FF + WIDTH + 128
PARTS = ((1, 0, 320), (1, 320, 256), (0, 0, 320), (0, 320, 256))
SHARES = ((192, 0, 128), (176, 0, 80), (160, 128, 32), (128, 96, 32))


def spans():
    places, totals = {}, [0, 0, 0]
    for part, counts in enumerate(SHARES):
        first = PARTS[part][1]
        for route, count in enumerate(counts):
            places[part, route] = (first, totals[route], count)
            first += count
            totals[route] += count
    return places, totals


SPANS, TOTALS = spans()

SLOPE_AT = 0.28
TAIL = (
    0.11652077851573843,
    0.06749675579450809,
    0.2689101589486142,
    -0.23699347299932225,
    0.3898740127620002,
    -0.10580824228351815,
)


def nn(a, b):
    return lax.dot_general(a, b, (((1,), (0,)), ((), ())), preferred_element_type=F32)


def nt(a, b):
    return lax.dot_general(a, b, (((1,), (1,)), ((), ())), preferred_element_type=F32)


def beside(first, other):
    low = lax.broadcasted_iota(jnp.int32, first.shape, 1) < DIM
    return (
        jnp.where(low, first, pltpu.roll(other, DIM, 1)),
        jnp.where(low, pltpu.roll(first, DIM, 1), other),
    )


def layers_kernel(
    tokens, seq_len_hbm, alphas_hbm, up_bias_hbm, down_bias_hbm, cotangent, qkv_hbm, out_hbm, up_hbm, down_hbm,
    final, heads_all, out_in, grad_in, small_final,
    seq_len, alphas, wqkv, wout, wup, wdown, up_bias, down_bias,
    tok_in, cot_in, flag_out, flag_in, back_out,
    hidden, grad, hid_all, attn_t, entered, act, branch, slope, second,
    dz, du, da, dqkv,
    pack_out, head_out, pack_in, o_in, do_in,
    kv, kv_t, rq, ro, o_t, probs, acc, dq_t, bias,
    parts, core_in, xa_in, xb_in, ya_in, yb_in, z_in, third_z, third_x, third_y,
    heads_out, heads_x, heads_z, heads_sum, small, small_in, small_z, small_sum,
    w_sem, move_send, move_recv, a2a_send, a2a_recv, core_send, core_recv, x_send, x_recv, y_send, y_recv,
    z_send, z_recv, fin_send, fin_recv, hid_send, hid_recv, hx_send, hx_recv, hz_send, hz_recv, hf_send, hf_recv,
    small_send, small_recv, core_free,
):
    grp = lax.axis_index("grp")
    blk = lax.axis_index("blk")
    core = lax.rem(grp, 2)
    side = lax.div(grp, 2)
    yy = lax.rem(blk, 2)
    zz = lax.div(blk, 2)
    member = 2 * core + yy
    far_side = 2 * (1 - side) + core

    def place(c, x, z, y):
        return (2 * x + c, 2 * z + y)

    core_peer = place(1 - core, side, zz, yy)
    x_peer = place(core, 1 - side, zz, yy)
    y_peer = place(core, side, zz, 1 - yy)

    def remote(source, target, send, recv, peer):
        return pltpu.make_async_remote_copy(
            src_ref=source,
            dst_ref=target,
            send_sem=send,
            recv_sem=recv,
            device_id=peer,
            device_id_type=MESH,
        )

    def credit(semaphore, peer, count=1):
        pl.semaphore_signal(semaphore, inc=count, device_id=peer, device_id_type=MESH)

    def moved(kind, slot, source, target, at, core_at, z_at):
        here = jnp.logical_and(core_at == core, z_at == zz)

        @pl.when(here)
        def _():
            pltpu.make_async_copy(source, target.at[at], move_recv.at[kind, at]).start()

        @pl.when(jnp.logical_not(here))
        def _():
            pltpu.make_async_remote_copy(
                src_ref=source,
                dst_ref=target.at[at],
                send_sem=move_send.at[kind, slot],
                recv_sem=move_recv.at[kind, at],
                device_id=place(core_at, side, z_at, yy),
                device_id_type=MESH,
            ).start()

    def move_left(kind, slot, source, core_at, z_at):
        here = jnp.logical_and(core_at == core, z_at == zz)

        @pl.when(jnp.logical_not(here))
        def _():
            pltpu.make_async_copy(source, source, move_send.at[kind, slot]).wait()

    def move_arrived(kind, at, target):
        pltpu.make_async_copy(target.at[at], target.at[at], move_recv.at[kind, at]).wait()

    def to_team(kind, half, source, target):
        moved(kind, half, source, target, lax.div(zz, 2), lax.rem(zz, 2), 2 * half + core)

    def to_team_left(kind, half, source):
        move_left(kind, half, source, lax.rem(zz, 2), 2 * half + core)

    def to_owner(kind, chunk, source, target):
        moved(kind, chunk, source, target, lax.div(zz, 2), lax.rem(zz, 2), core + 2 * chunk)

    def to_owner_left(kind, chunk, source):
        move_left(kind, chunk, source, lax.rem(zz, 2), core + 2 * chunk)

    def half_of(ref, half):
        return ref.at[pl.ds(pl.multiple_of(HALF * half, HALF), HALF)]

    def rows_of(half):
        return pl.ds(pl.multiple_of(half * HALF, HALF), HALF)

    def slot_of(other):
        return lax.rem(other + TEAM - member, TEAM)

    def exchange(kind, layer, half, outgoing, incoming, head=None):
        at = () if head is None else (head,)
        incoming[(half, 0, *at)] = outgoing[(half, member, *at)]
        for step in range(1, TEAM):
            peer = lax.rem(member + step, TEAM)
            remote(
                outgoing.at[(half, peer, *at)],
                incoming.at[(half, TEAM - step, *at)],
                a2a_send.at[kind, layer, half, head or 0],
                a2a_recv.at[kind, layer, half, head or 0],
                place(lax.div(peer, 2), side, zz, lax.rem(peer, 2)),
            ).start()

    def arrived(kind, layer, half, incoming, head=None):
        at = () if head is None else (head,)
        whole = incoming.at[(half, pl.ds(1, TEAM - 1), *at)]
        pltpu.make_async_copy(whole, whole, a2a_recv.at[kind, layer, half, head or 0]).wait()

    def left(kind, layer, half, outgoing):
        for head in range(OWN) if kind in (0, 3) else (None,):
            at = () if head is None else (head,)
            whole = outgoing.at[(half, pl.ds(1, TEAM - 1), *at)]
            pltpu.make_async_copy(whole, whole, a2a_send.at[kind, layer, half, head or 0]).wait()

    def tokens_of(chunk, other):
        return pl.ds(pl.multiple_of(HALF * (TEAM * chunk + other), HALF), HALF)

    def hidden_copy(layer, chunk, which):
        whose = 2 * core + 1 - yy if which == 2 else member
        block = hid_all.at[layer, :, tokens_of(chunk, whose)]
        return remote(
            block,
            block,
            hid_send.at[layer, chunk, which],
            hid_recv.at[layer, chunk, which],
            y_peer if which == 0 else core_peer,
        )

    def hidden_start(layer, chunk):
        for which in range(2):
            hidden_copy(layer, chunk, which).start()

    def hidden_pass(layer, chunk):
        hidden_copy(layer, chunk, 0).wait()
        hidden_copy(layer, chunk, 2).start()

    def hidden_done(layer, chunk):
        for which in range(1, 3):
            hidden_copy(layer, chunk, which).wait()

    def project(layer, half):
        rows = rows_of(half)
        rounded = hidden[rows, :].astype(BF16)
        if layer == 1:
            left(0, 0, half, pack_out)
        queries = (nn(rounded, wqkv[layer, :, 0:WIDTH]) * (DIM ** -0.5)).astype(BF16).T
        for head in range(RUNS):
            pack_out[half, head // 2, head % 2, HALF:, :] = queries[DIM * head : DIM * head + DIM, :]
        for step in range(2):
            at = WIDTH * (step + 1)
            keys_values = nn(rounded, wqkv[layer, :, at : at + WIDTH]).astype(BF16)
            for head in range(4):
                pack_out[half, 2 * step + head // 2, head % 2, 0:HALF, :] = keys_values[
                    :, 128 * head : 128 * head + 128
                ]
        for head in range(OWN):
            exchange(0, layer, half, pack_out, pack_in, head)
        hid_all[layer, :, tokens_of(half, member)] = rounded.T

    def rows_before(i):
        return TILE * i * (i + 1) // 2

    def attend(layer, chunk):
        if layer == 1:
            left(1, 0, chunk, head_out)

        def one_head(head, carry):
            arrived(0, layer, chunk, pack_in, head)
            for other in range(TEAM):
                slot = slot_of(other)
                start = HALF * (TEAM * chunk + other)
                span = slice(start, start + HALF)
                block = pack_in[chunk, slot, head, 0:HALF, :]
                kv[layer, head, span, :] = block
                kv_t[layer, head, :, span] = block.T
                rq[layer, head, 0:DIM, span] = pack_in[chunk, slot, head, HALF:, :]

            def scores_of(i):
                count = TILE * (i + 1)
                tile = rq[layer, head, :, TILE * i : TILE * i + TILE]
                return nn(kv[layer, head, 0:count, :], tile) + bias[TILE * TILES - count :, :]

            ahead = [scores_of(i) for i in (2 * chunk, 2 * chunk + 1)]
            for i in (2 * chunk, 2 * chunk + 1):
                columns = slice(TILE * i, TILE * i + TILE)
                count = TILE * (i + 1)
                scores = ahead[i - 2 * chunk]
                largest = jnp.max(scores, axis=0, keepdims=True)
                weight = jnp.exp(scores - largest)
                total = jnp.sum(weight, axis=0, keepdims=True)
                share = (weight * (1.0 / total)).astype(BF16)
                probs[layer, head, rows_before(i) : rows_before(i) + count, :] = share
                summed = nn(kv_t[layer, head, DIM:, 0:count], share)
                o_t[layer, head, :, columns] = summed
                rounded = summed.astype(BF16)
                for part in range(2):
                    head_out[chunk, 2 * (i - 2 * chunk) + part, head] = rounded[
                        :, HALF * part : HALF * part + HALF
                    ]
            return carry

        for head in range(OWN):
            one_head(head, 0)
        exchange(1, layer, chunk, head_out, o_in)

    def feed(layer, half):
        rows = rows_of(half)
        arrived(1, layer, half, o_in)
        for head in range(RUNS):
            attn_t[layer, DIM * head : DIM * head + DIM, rows] = o_in[half, slot_of(head // 2), head % 2]
        attn = attn_t[layer, :, rows].T
        grown = nn(attn, wout[layer])
        branch[layer, rows, :] = grown
        middle = hidden[rows, :] + alphas[layer, 0] * grown
        rounded = middle.astype(BF16)
        entered[layer, rows, :] = rounded
        total = jnp.zeros((HALF, WIDTH), F32)

        def gate_of(step):
            cut = slice(CUT * step, CUT * step + CUT)
            return nn(rounded, wup[layer, :, cut]) + up_bias[layer : layer + 1, cut]

        coming = gate_of(0)
        for step in range(FF // CUT):
            cut = slice(CUT * step, CUT * step + CUT)
            gate = coming
            if step + 1 < FF // CUT:
                coming = gate_of(step + 1)
            bell = jnp.exp(gate * gate * -0.5)
            near = pl.reciprocal(1.0 + SLOPE_AT * jnp.abs(gate), approx=True)
            tail = jnp.full_like(gate, TAIL[5])
            for factor in TAIL[4::-1]:
                tail = tail * near + factor
            tail = bell * (tail * near)
            risen = jnp.where(gate > 0.0, 1.0 - tail, tail)
            slope[layer, rows, cut] = risen + gate * bell * 0.3989422804014327
            active = (gate * risen).astype(BF16)
            act[layer, rows, cut] = active
            total = total + nn(active, wdown[layer, cut, :])
        total = total + down_bias[layer : layer + 1, :]
        second[layer, rows, :] = total
        hidden[rows, :] = middle + alphas[layer, 1] * total

    def total_of(values):
        return jnp.sum(jnp.sum(values, axis=0, keepdims=True), axis=1, keepdims=True)

    def feed_back(layer):
        start = grad[...]
        if layer == 0:
            dz[...] = (alphas[layer, 1] * start).astype(BF16)
        scaled = dz[...]
        alpha_second = total_of(start * second[layer])
        small[layer : layer + 1, FF : FF + WIDTH] = jnp.sum(scaled.astype(F32), axis=0, keepdims=True)
        middle = start
        coming = nt(scaled, wdown[layer, 0:CUT, :])
        for step in range(FF // CUT):
            cut = slice(CUT * step, CUT * step + CUT)
            raw = coming
            if step + 1 < FF // CUT:
                coming = nt(scaled, wdown[layer, CUT * (step + 1) : CUT * (step + 2), :])
            gate = (raw * slope[layer, :, cut]).astype(BF16)
            du[:, cut] = gate
            small[layer : layer + 1, cut] = jnp.sum(gate.astype(F32), axis=0, keepdims=True)
            middle = middle + nt(gate, wup[layer, :, cut])
        grad[...] = middle
        mixed = (alphas[layer, 0] * middle).astype(BF16)
        da[...] = mixed
        spread = nt(wout[layer], mixed).astype(BF16)
        for chunk in (1, 0):
            left(*((1, 1) if layer == 1 else (2, 1)), chunk, head_out)
            for head in range(RUNS):
                head_out[chunk, head // 2, head % 2] = spread[
                    DIM * head : DIM * head + DIM, HALF * chunk : HALF * chunk + HALF
                ]
            exchange(2, layer, chunk, head_out, do_in)
        alpha_first = total_of(middle * branch[layer])
        column = lax.broadcasted_iota(jnp.int32, (1, 128), 1)
        small[layer : layer + 1, FF + WIDTH :] = jnp.where(
            column == 0, alpha_first, jnp.where(column == 1, alpha_second, 0.0)
        )

    def attend_back(layer, chunk):
        arrived(2, layer, chunk, do_in)
        left(*((0, 1) if layer == 1 else (3, 1)), chunk, pack_out)

        def one_head(head, carry):
            for other in range(TEAM):
                start = HALF * (TEAM * chunk + other)
                ro[head, DIM:, start : start + HALF] = do_in[chunk, slot_of(other), head]
            for i in (2 * chunk, 2 * chunk + 1):
                columns = slice(TILE * i, TILE * i + TILE)
                query_tile = rq[layer, head, :, columns]
                grad_tile = ro[head, :, columns]
                delta = jnp.sum(
                    ro[head, DIM:, columns].astype(F32) * o_t[layer, head, :, columns],
                    axis=0,
                    keepdims=True,
                )
                count = TILE * (i + 1)
                keys = kv[layer, head, 0:count, :]
                share = probs[layer, head, rows_before(i) : rows_before(i) + count, :]
                scored = (share.astype(F32) * (nn(keys, grad_tile) - delta)).astype(BF16)
                term = nt(scored, query_tile) + nt(share, grad_tile)
                if chunk == 1 and i == 2:
                    acc[head, 0:count, :] = term
                elif chunk == 1:
                    acc[head, 0 : count - TILE, :] += term[0 : count - TILE, :]
                    acc[head, count - TILE : count, :] = term[count - TILE :, :]
                else:
                    acc[head, 0:count, :] += term
                query_grad = nn(kv_t[layer, head, 0:DIM, 0:count], scored)
                dq_t[head, :, columns] = query_grad * (DIM ** -0.5)
            for other in range(TEAM):
                start = HALF * (TEAM * chunk + other)
                span = slice(start, start + HALF)
                pack_out[chunk, other, head, 0:HALF, :] = acc[head, span, :].astype(BF16)
                pack_out[chunk, other, head, HALF:, :] = dq_t[head, :, span].astype(BF16)
            exchange(3, layer, chunk, pack_out, pack_in, head)
            return carry

        for head in range(OWN):
            one_head(head, 0)

    def project_back(layer, half):
        for head in range(OWN):
            arrived(3, layer, half, pack_in, head)
        turned = jnp.concatenate(
            [pack_in[half, slot_of(head // 2), head % 2, HALF:, :] for head in range(RUNS)], axis=0
        )
        dqkv[:, 0:WIDTH] = turned.T
        for head in range(RUNS):
            at = WIDTH + 128 * head
            dqkv[:, at : at + 128] = pack_in[half, slot_of(head // 2), head % 2, 0:HALF, :]
        rows = rows_of(half)
        grad[rows, :] = grad[rows, :] + nt(dqkv[...], wqkv[layer])

    def scatter_rows(layer, result, first_row):
        for run in range(RUNS):
            for quarter in range(4):
                parts[layer, quarter % 2, quarter // 2, run // 2, run % 2, first_row : first_row + DIM, :] = result[
                    DIM * run : DIM * run + DIM, 128 * quarter : 128 * quarter + 128
                ].astype(BF16)

    def make(part):
        layer, first, count = PARTS[part]
        if first < 256:
            turned = entered[layer].T
        for row in range(first, min(first + count, 256), DIM):
            step = row // DIM
            scatter_rows(layer, nn(turned, du[:, CUT * step : CUT * step + CUT]), row)
        if first <= 256 < first + count:
            scatter_rows(layer, nn(attn_t[layer], da[...]), 256)
        if first >= 320:
            turned = dz[...].T
            for step in range(FF // CUT):
                result = nn(turned, act[layer, :, CUT * step : CUT * step + CUT])
                for block in range(CUT // 128):
                    run, row = 2 * step + block // 2, 320 + 128 * (block % 2)
                    for quarter in range(4):
                        parts[layer, quarter % 2, quarter // 2, run // 2, run % 2, row : row + 128, :] = result[
                            128 * quarter : 128 * quarter + 128, 128 * block : 128 * block + 128
                        ].astype(BF16)
        if layer == 0:
            pl.semaphore_wait(core_free.at[0 if first < 320 else 1], 1)
        core_copy(part).start()

    def heads_grads(layer):
        for chunk in range(2):
            hidden_done(layer, chunk)
        blocks = [(run // TEAM, run % TEAM) for run in range(RUNS)]
        keys_values = jnp.concatenate(
            [
                jnp.concatenate([pack_out[chunk, other, head, 0:HALF, :] for chunk, other in blocks], axis=0)
                for head in range(OWN)
            ],
            axis=1,
        )
        queries = jnp.concatenate(
            [
                jnp.concatenate([pack_out[chunk, other, head, HALF:, :] for chunk, other in blocks], axis=1)
                for head in range(OWN)
            ],
            axis=0,
        )
        both = nn(hid_all[layer], keys_values)
        q_part = nt(hid_all[layer], queries)
        for number, values in enumerate((q_part, both[:, 0:128], both[:, 128:256])):
            for run in range(RUNS):
                heads_out[layer, run // 2, run % 2, :, 128 * number : 128 * number + 128] = values[
                    DIM * run : DIM * run + DIM, :
                ].astype(BF16)
        heads_x_copy(layer).start()

    def half_rows(which):
        return pl.ds(pl.multiple_of(32 * which, 32), 32)

    def heads_x_copy(layer):
        return remote(
            heads_out.at[layer, :, :, half_rows(1 - side)],
            heads_x.at[layer],
            hx_send.at[layer],
            hx_recv.at[layer],
            x_peer,
        )

    def heads_z_copy(layer, step):
        peer = lax.rem(zz + step, 4)
        return remote(
            heads_out.at[layer, peer, :, half_rows(side)],
            heads_z.at[layer, 4 - step],
            hz_send.at[layer, step],
            hz_recv.at[layer, 4 - step],
            place(core, side, peer, yy),
        )

    def heads_last_copy(layer, number):
        x, c, y = number // 4, number // 2 % 2, number % 2
        return remote(
            heads_sum.at[layer, 1 - yy if y else yy],
            heads_all.at[layer, side, member],
            hf_send.at[layer, number],
            hf_recv.at[layer, number],
            place(1 - core if c else core, 1 - side if x else side, zz, 1 - yy if y else yy),
        )

    def heads_second(layer):
        heads_x_copy(layer).wait()
        heads_out[layer, :, :, half_rows(side), :] += heads_x[layer]
        for step in range(1, 4):
            heads_z_copy(layer, step).start()

    def heads_third(layer):
        for step in range(1, 4):
            heads_z_copy(layer, step).wait()
        total = heads_out[layer, zz, :, half_rows(side), :].astype(F32)
        for slot in range(1, 4):
            total = total + heads_z[layer, slot].astype(F32)
        heads_sum[layer] = total.astype(BF16)
        heads_all[layer, side, member] = heads_sum[layer, yy]
        for number in range(1, 8):
            heads_last_copy(layer, number).start()

    def heads_done(layer):
        for number in range(1, 8):
            heads_last_copy(layer, number).wait()

    def rows_in(part, route):
        first, room, count = SPANS[part, route]
        return pl.ds(first, count), pl.ds(room, count)

    def used(part, route):
        return SHARES[part][route] > 0

    def core_copy(part):
        layer, first, count = PARTS[part]
        rows = pl.ds(first, count)
        return remote(
            parts.at[layer, 1 - core, :, :, :, rows],
            core_in.at[:, :, :, rows],
            core_send.at[part],
            core_recv.at[part],
            core_peer,
        )

    def x_copy(part, route):
        layer = PARTS[part][0]
        rows, room = rows_in(part, route)
        ends = (x_send.at[part, route], x_recv.at[part, route], x_peer)
        mine = parts.at[layer, core, 1 - side]
        if route == 0:
            return remote(mine.at[:, :, rows], xa_in.at[:, :, room], *ends)
        if route == 1:
            return remote(mine.at[:, yy, rows], xb_in.at[:, room], *ends)
        return remote(mine.at[zz, :, rows], third_x.at[:, room], *ends)

    def y_copy(part, route):
        layer = PARTS[part][0]
        rows, room = rows_in(part, route)
        ends = (y_send.at[part, route], y_recv.at[part, route], y_peer)
        mine = parts.at[layer, core]
        if route == 0:
            return remote(mine.at[side, :, 1 - yy, rows], ya_in.at[:, room], *ends)
        if route == 1:
            return remote(mine.at[:, :, 1 - yy, rows], yb_in.at[:, :, room], *ends)
        return remote(mine.at[side, zz, 1 - yy, rows], third_y.at[room], *ends)

    def z_copy(part, route, step):
        layer = PARTS[part][0]
        rows, room = rows_in(part, route)
        peer = lax.rem(zz + step, 4)
        ends = (z_send.at[part, route, step], z_recv.at[part, route, 4 - step], place(core, side, peer, yy))
        if route == 2:
            return remote(parts.at[layer, core, :, peer, :, rows], third_z.at[4 - step, :, :, room], *ends)
        return remote(parts.at[layer, core, side, peer, yy, rows], z_in.at[layer, 4 - step, rows], *ends)

    def final_copy(part, which):
        layer, first, count = PARTS[part]
        block = final.at[layer, far_side if which == 2 else grp, pl.ds(first, count)]
        return remote(
            block,
            block,
            fin_send.at[part, which],
            fin_recv.at[part, which],
            x_peer if which == 0 else core_peer,
        )

    def core_done(part):
        layer, first, count = PARTS[part]
        rows = pl.ds(first, count)
        core_copy(part).wait()
        for across in (1 - side, side):
            parts[layer, core, across, :, :, rows, :] += core_in[across, :, :, rows, :]
            if used(part, 0) and across is not side:
                x_copy(part, 0).start()
        if used(part, 1):
            y_copy(part, 1).start()
        if used(part, 2):
            for step in range(1, 4):
                z_copy(part, 2, step).start()
        if layer == 1:
            freed = 0 if first < 320 else 1
            followers = [1 for other in PARTS if other[0] == 0 and (other[1] >= 320) == (freed == 1)]
            credit(core_free.at[freed], core_peer, len(followers))

    def first_x(part):
        if used(part, 0):
            layer = PARTS[part][0]
            rows, room = rows_in(part, 0)
            x_copy(part, 0).wait()
            for y in (1 - yy, yy):
                parts[layer, core, side, :, y, rows, :] += xa_in[:, y, room, :]
                if y is not yy:
                    y_copy(part, 0).start()

    def first_y(part):
        if used(part, 1):
            layer = PARTS[part][0]
            rows, room = rows_in(part, 1)
            y_copy(part, 1).wait()
            for across in (1 - side, side):
                parts[layer, core, across, :, yy, rows, :] += yb_in[across, :, room, :]
                if across is not side:
                    x_copy(part, 1).start()

    def first_z(part):
        if used(part, 2):
            layer = PARTS[part][0]
            rows, room = rows_in(part, 2)
            for step in range(1, 4):
                z_copy(part, 2, step).wait()
            for across in (1 - side, side):
                total = parts[layer, core, across, zz, :, rows, :].astype(F32)
                for slot in range(1, 4):
                    total = total + third_z[slot, across, :, room, :].astype(F32)
                parts[layer, core, across, zz, :, rows, :] = total.astype(BF16)
                if across is not side:
                    x_copy(part, 2).start()

    def second_x(part):
        if used(part, 0):
            layer = PARTS[part][0]
            rows, room = rows_in(part, 0)
            y_copy(part, 0).wait()
            parts[layer, core, side, :, yy, rows, :] += ya_in[:, room, :]
            for step in range(1, 4):
                z_copy(part, 0, step).start()

    def second_y(part):
        if used(part, 1):
            layer = PARTS[part][0]
            rows, room = rows_in(part, 1)
            x_copy(part, 1).wait()
            parts[layer, core, side, :, yy, rows, :] += xb_in[:, room, :]
            for step in range(1, 4):
                z_copy(part, 1, step).start()

    def second_z(part):
        if used(part, 2):
            layer = PARTS[part][0]
            rows, room = rows_in(part, 2)
            x_copy(part, 2).wait()
            for y in (1 - yy, yy):
                parts[layer, core, side, zz, y, rows, :] += third_x[y, room, :]
                if y is not yy:
                    y_copy(part, 2).start()

    def third_done(part):
        layer = PARTS[part][0]
        for route in range(3):
            if not used(part, route):
                continue
            rows, room = rows_in(part, route)
            if route == 2:
                y_copy(part, 2).wait()
                final[layer, grp, rows, :] = parts[layer, core, side, zz, yy, rows, :] + third_y[room, :]
            else:
                for step in range(1, 4):
                    z_copy(part, route, step).wait()
                total = parts[layer, core, side, zz, yy, rows, :].astype(F32)
                for slot in range(1, 4):
                    total = total + z_in[layer, slot, rows, :].astype(F32)
                final[layer, grp, rows, :] = total.astype(BF16)
        if PARTS[part][1] >= 320:
            for row in (320, 448):
                final[layer, grp, row : row + 128, :] = final[layer, grp, row : row + 128, :].T
        for which in range(2):
            final_copy(part, which).start()

    def final_pass(part):
        final_copy(part, 0).wait()
        final_copy(part, 2).start()

    def final_done(part):
        for which in range(1, 3):
            final_copy(part, which).wait()

    def small_copy(stage):
        peer = (core_peer, x_peer, y_peer)[stage]
        return remote(
            small_sum.at[stage], small_in.at[stage], small_send.at[stage], small_recv.at[stage], peer
        )

    def small_z_copy(step):
        return remote(
            small_z.at[zz],
            small_z.at[zz],
            small_send.at[2 + step],
            small_recv.at[2 + step],
            place(core, side, lax.rem(zz + step, 4), yy),
        )

    def small_start():
        small_sum[0] = small[...]
        small_copy(0).start()

    def small_next(stage):
        small_copy(stage).wait()
        total = small_sum[stage] + small_in[stage]
        if stage < 2:
            small_sum[stage + 1] = total
            small_copy(stage + 1).start()
        else:
            small_z[zz] = total
            for step in range(1, 4):
                small_z_copy(step).start()

    def small_done():
        for step in range(1, 4):
            small_z_copy(step).wait()
        small_sum[0] = (small_z[0] + small_z[1]) + (small_z[2] + small_z[3])
        small_final[:, 0:256] = small_sum[0, :, pl.ds(pl.multiple_of(blk * 256, 256), 256)]
        pair = small_sum[0, :, pl.ds(pl.multiple_of(FF + 128 * zz, 128), 128)]
        small_final[:, 256:384] = jnp.where(yy == 1, pltpu.roll(pair, DIM, 1), pair)
        small_final[:, 384:512] = small_sum[0, :, FF + WIDTH :]

    def halves(*phases, first=0):
        def both(step, carry):
            for phase in phases:
                phase(lax.rem(step + first, 2))
            return carry

        lax.fori_loop(0, 2, both, 0)

    def begin(half):
        move_arrived(0, half, tok_in)
        hidden[rows_of(half), :] = tok_in[half].astype(F32)

    def finish(half):
        back_out[0, half] = hidden[rows_of(half), :].astype(BF16)
        to_owner(3, half, back_out.at[0, half], out_in)

    def turn_round(layer, half):
        move_arrived(2, half, cot_in)
        rows = rows_of(half)
        grad[rows, :] = cot_in[half].astype(F32)
        dz[rows, :] = (alphas[layer, 1] * grad[rows, :]).astype(BF16)

    def hand_back(half):
        back_out[1, half] = grad[rows_of(half), :].astype(BF16)
        to_owner(4, half, back_out.at[1, half], grad_in)

    barrier = pltpu.get_barrier_semaphore()
    for step in range(1, 4):
        credit(barrier, place(core, side, lax.rem(zz + step, 4), yy))
    for step in range(4):
        credit(barrier, place(1 - core, side, lax.rem(zz + step, 4), yy))
    for peer in (
        x_peer,
        y_peer,
        place(1 - core, side, zz, 1 - yy),
        place(1 - core, 1 - side, zz, yy),
        place(core, 1 - side, zz, 1 - yy),
        place(1 - core, 1 - side, zz, 1 - yy),
    ):
        credit(barrier, peer)

    weight_copies = {}
    for layer in range(LAYERS):
        for number, (source, target) in enumerate(
            ((qkv_hbm, wqkv), (out_hbm, wout), (up_hbm, wup), (down_hbm, wdown))
        ):
            weight_copies[layer, number] = pltpu.make_async_copy(
                source.at[layer], target.at[layer], w_sem.at[layer, number]
            )
    bias_copies = [
        pltpu.make_async_copy(up_bias_hbm, up_bias, w_sem.at[2, 0]),
        pltpu.make_async_copy(down_bias_hbm, down_bias, w_sem.at[2, 1]),
        pltpu.make_async_copy(alphas_hbm, alphas, w_sem.at[2, 2]),
    ]
    length_copy = pltpu.make_async_copy(seq_len_hbm, seq_len, w_sem.at[2, 3])
    length_copy.start()
    weight_copies[0, 0].start()
    pl.semaphore_wait(barrier, 13)
    upper = lax.div(zz, 2)
    for half in (1 - upper, upper):
        to_team(0, half, half_of(tokens, half), tok_in)
    for layer, number in ((1, 0), (0, 1), (0, 2), (0, 3), (1, 1), (1, 2), (1, 3)):
        weight_copies[layer, number].start(priority=1)
    for copy in bias_copies:
        copy.start(priority=1)
    length_copy.wait()
    end_second = lax.div(seq_len[0, 0] + seq_len[0, 1], RUNS)
    flag_out[...] = jnp.full((8, 128), end_second.astype(F32), F32)
    for half in (1 - upper, upper):
        to_team(1, half, flag_out, flag_in)
    for layer in range(LAYERS):
        for head in range(OWN):
            rq[layer, head, DIM:, :] = jnp.zeros((DIM, HALF * RUNS), BF16)
    for head in range(OWN):
        ro[head, 0:DIM, :] = jnp.zeros((DIM, HALF * RUNS), BF16)
    for layer in range(LAYERS):
        weight_copies[layer, 0].wait()
        pairs = [
            beside(
                wqkv[layer, :, WIDTH + 128 * pair : WIDTH + 128 * pair + 128].astype(F32),
                wqkv[layer, :, 2 * WIDTH + 128 * pair : 2 * WIDTH + 128 * pair + 128].astype(F32),
            )
            for pair in range(TEAM)
        ]
        for head in range(RUNS):
            at = WIDTH + 128 * head
            wqkv[layer, :, at : at + 128] = pairs[head // 2][head % 2].astype(BF16)
    halves(begin, functools.partial(project, 0), first=upper)
    for half in (1 - upper, upper):
        to_team(2, half, half_of(cotangent, half), cot_in)

    move_arrived(1, 0, flag_in)
    move_arrived(1, 1, flag_in)
    border = jnp.concatenate([flag_in[0, 0:1, :]] * 2, axis=1) - (HALF * lax.div(zz, 2)).astype(F32)
    key_row = lax.broadcasted_iota(jnp.int32, (TILE, TILE), 0)
    query_col = lax.broadcasted_iota(jnp.int32, (TILE, TILE), 1)
    later = key_row > query_col
    key_sub = lax.rem(key_row, HALF).astype(F32) >= border
    query_sub = lax.rem(query_col, HALF).astype(F32) >= border
    apart = jnp.logical_xor(key_sub, query_sub)
    for tile in range(TILES - 1):
        bias[TILE * tile : TILE * tile + TILE, :] = jnp.where(apart, NEGATIVE, 0.0)
    bias[TILE * (TILES - 1) :, :] = jnp.where(jnp.logical_or(later, apart), NEGATIVE, 0.0)

    for copy in (*bias_copies, *(weight_copies[0, number] for number in range(1, 4))):
        copy.wait()
    attend(0, 0)
    attend(0, 1)
    hidden_start(0, 0)
    halves(functools.partial(feed, 0), functools.partial(project, 1))
    for number in range(1, 4):
        weight_copies[1, number].wait()
    attend(1, 0)
    attend(1, 1)
    hidden_pass(0, 0)
    hidden_start(1, 0)
    halves(functools.partial(feed, 1), finish)
    hidden_start(0, 1)
    hidden_start(1, 1)
    hidden_pass(1, 0)

    halves(functools.partial(turn_round, 1))
    make(1)
    feed_back(1)
    hidden_pass(0, 1)
    hidden_pass(1, 1)
    core_done(1)
    make(0)
    attend_back(1, 1)
    core_done(0)
    attend_back(1, 0)
    first_x(1)
    project_back(1, 1)
    heads_grads(1)
    project_back(1, 0)
    feed_back(0)
    first_z(1)
    small_start()
    second_x(1)
    make(2)
    first_x(0)
    heads_second(1)
    attend_back(0, 1)
    first_z(0)
    small_next(0)
    core_done(2)
    second_x(0)
    make(3)
    attend_back(0, 0)
    heads_grads(0)
    small_next(1)
    project_back(0, 1)
    hand_back(1)
    first_z(2)
    small_next(2)
    first_x(2)
    core_done(3)
    first_y(2)
    heads_second(0)
    small_done()
    second_x(2)
    first_x(3)
    first_z(3)
    second_z(2)
    second_z(0)
    heads_third(1)
    second_z(1)
    first_y(3)
    heads_third(0)
    second_y(2)
    second_x(3)
    second_z(3)
    third_done(2)
    second_y(3)
    project_back(0, 0)
    hand_back(0)
    third_done(0)
    heads_done(1)
    third_done(1)
    third_done(3)
    final_pass(0)
    final_pass(2)
    final_pass(1)
    final_pass(3)
    final_done(2)
    final_done(1)
    heads_done(0)
    final_done(0)
    final_done(3)
    for half in range(2):
        move_arrived(3, half, out_in)
        move_arrived(4, half, grad_in)

    for half in range(2):
        left(2, 0, half, head_out)
        left(3, 0, half, pack_out)
        to_team_left(0, half, half_of(tokens, half))
        to_team_left(1, half, flag_out)
        to_team_left(2, half, half_of(cotangent, half))
        to_owner_left(3, half, back_out.at[0, half])
        to_owner_left(4, half, back_out.at[1, half])


def results_kernel(
    final, heads, out_block, grad_block, small,
    output, input_grad, qkv_grad, out_grad, up_grad, up_bias_grad, down_grad, down_bias_grad, alpha_grad,
    grad_wide, qkv_wide, out_wide, up_wide, down_wide, up_bias, down_bias, alpha, out_sem,
):
    ends = []

    def write(source, target):
        ends.append(pltpu.make_async_copy(source, target, out_sem.at[len(ends)]))
        ends[-1].start()

    for half in range(2):
        write(out_block.at[half], output.at[pl.ds(HALF * half, HALF)])
    up_bias[...] = small[:, 0:256]
    write(up_bias, up_bias_grad)
    down_bias[...] = small[:, 256 : 256 + DIM]
    write(down_bias, down_bias_grad)
    alpha[...] = small[:, 384:386]
    write(alpha, alpha_grad)
    for layer in range(LAYERS):
        for quarter in range(4):

            def block(first, count):
                return final[layer, quarter, first : first + count, :].astype(F32)

            def columns(step):
                return slice(WIDTH * step + 128 * quarter, WIDTH * step + 128 * quarter + 128)

            for step in range(4):
                up_wide[layer, :, columns(step)] = block(DIM * step, DIM)
            out_wide[layer, :, columns(0)] = block(256, DIM)
            down_wide[layer, :, columns(0)] = block(320, 256)
        write(up_wide.at[layer], up_grad.at[layer])
        write(out_wide.at[layer], out_grad.at[layer])
        write(down_wide.at[layer], down_grad.at[layer])
    for half in range(2):
        rows = slice(HALF * half, HALF * half + HALF)
        grad_wide[rows, :] = grad_block[half].astype(F32)
    write(grad_wide, input_grad)
    for layer in range(LAYERS):
        for side in range(2):
            for member in range(TEAM):
                block = heads[layer, side, member].astype(F32)
                columns = (block[:, 0:128], *beside(block[:, 128:256], block[:, 256:384]))
                for step in range(3):
                    at = WIDTH * step + 128 * member
                    qkv_wide[layer, 32 * side : 32 * side + 32, at : at + 128] = columns[step]
        write(qkv_wide.at[layer], qkv_grad.at[layer])
    for end in ends:
        end.wait()


def fast_body(
    tokens, seq_len, qkv_weight, out_weight, up_weight, up_bias, down_weight, down_bias, alphas, cotangent
):
    whole = pl.BlockSpec(memory_space=pltpu.VMEM)
    far = pl.BlockSpec(memory_space=pl.ANY)
    shape = jax.ShapeDtypeStruct
    rows = HALF * RUNS

    def vmem(*dims):
        return pltpu.VMEM(dims, BF16)

    def wide(*dims):
        return pltpu.VMEM(dims, F32)

    dma = pltpu.SemaphoreType.DMA
    final, heads, out_block, grad_block, small = pl.pallas_call(
        layers_kernel,
        out_shape=(
            vmem(LAYERS, 4, CHUNK, 128),
            vmem(LAYERS, 2, TEAM, DIM // 2, 3 * 128),
            vmem(2, HALF, WIDTH),
            vmem(2, HALF, WIDTH),
            wide(LAYERS, WIDTH),
        ),
        in_specs=[far, far, far, far, far, far, far, far, far, far],
        out_specs=(whole,) * 5,
        scratch_shapes=[
            pltpu.SMEM((1, 4), jnp.int32),
            pltpu.SMEM((LAYERS, 2), F32),
            vmem(LAYERS, WIDTH, 3 * WIDTH),
            vmem(LAYERS, WIDTH, WIDTH),
            vmem(LAYERS, WIDTH, FF),
            vmem(LAYERS, FF, WIDTH),
            wide(LAYERS, FF),
            wide(LAYERS, WIDTH),
            vmem(2, HALF, WIDTH),
            vmem(2, HALF, WIDTH),
            wide(8, 128),
            wide(2, 8, 128),
            vmem(2, 2, HALF, WIDTH),
            wide(2 * HALF, WIDTH),
            wide(2 * HALF, WIDTH),
            vmem(LAYERS, WIDTH, rows),
            vmem(LAYERS, WIDTH, 2 * HALF),
            vmem(LAYERS, 2 * HALF, WIDTH),
            vmem(LAYERS, 2 * HALF, FF),
            wide(LAYERS, 2 * HALF, WIDTH),
            wide(LAYERS, 2 * HALF, FF),
            wide(LAYERS, 2 * HALF, WIDTH),
            vmem(2 * HALF, WIDTH),
            vmem(2 * HALF, FF),
            vmem(2 * HALF, WIDTH),
            vmem(HALF, 3 * WIDTH),
            vmem(2, TEAM, OWN, PACK, 128),
            vmem(2, TEAM, OWN, DIM, 128),
            vmem(2, TEAM, OWN, PACK, 128),
            vmem(2, TEAM, OWN, DIM, 128),
            vmem(2, TEAM, OWN, DIM, 128),
            vmem(LAYERS, OWN, rows, 128),
            vmem(LAYERS, OWN, 128, rows),
            vmem(LAYERS, OWN, 128, rows),
            vmem(OWN, 128, rows),
            wide(LAYERS, OWN, DIM, rows),
            vmem(LAYERS, OWN, TILE * TILES * (TILES + 1) // 2, TILE),
            wide(OWN, rows, 128),
            wide(OWN, DIM, rows),
            wide(rows, TILE),
            vmem(LAYERS, 2, 2, 4, 2, CHUNK, 128),
            vmem(2, 4, 2, CHUNK, 128),
            vmem(4, 2, TOTALS[0], 128),
            vmem(4, TOTALS[1], 128),
            vmem(4, TOTALS[0], 128),
            vmem(2, 4, TOTALS[1], 128),
            vmem(LAYERS, 4, CHUNK, 128),
            vmem(4, 2, 2, TOTALS[2], 128),
            vmem(2, TOTALS[2], 128),
            vmem(TOTALS[2], 128),
            vmem(LAYERS, 4, 2, DIM, 3 * 128),
            vmem(LAYERS, 4, 2, DIM // 2, 3 * 128),
            vmem(LAYERS, 4, 2, DIM // 2, 3 * 128),
            vmem(LAYERS, 2, DIM // 2, 3 * 128),
            wide(LAYERS, SMALL),
            wide(3, LAYERS, SMALL),
            wide(4, LAYERS, SMALL),
            wide(3, LAYERS, SMALL),
            dma((LAYERS + 1, 4)),
            dma((5, 2)),
            dma((5, 2)),
            dma((4, LAYERS, 2, OWN)),
            dma((4, LAYERS, 2, OWN)),
            dma((len(PARTS),)),
            dma((len(PARTS),)),
            dma((len(PARTS), 3)),
            dma((len(PARTS), 3)),
            dma((len(PARTS), 3)),
            dma((len(PARTS), 3)),
            dma((len(PARTS), 3, 4)),
            dma((len(PARTS), 3, 4)),
            dma((len(PARTS), 3)),
            dma((len(PARTS), 3)),
            dma((LAYERS, 2, 3)),
            dma((LAYERS, 2, 3)),
            dma((LAYERS,)),
            dma((LAYERS,)),
            dma((LAYERS, 4)),
            dma((LAYERS, 4)),
            dma((LAYERS, 8)),
            dma((LAYERS, 8)),
            dma((6,)),
            dma((6,)),
            pltpu.SemaphoreType.REGULAR((2,)),
        ],
        compiler_params=pltpu.CompilerParams(
            collective_id=0, has_side_effects=True, vmem_limit_bytes=61 * 1024 * 1024
        ),
        name="layers",
    )(
        tokens, seq_len, alphas, up_bias, down_bias, cotangent,
        qkv_weight, out_weight, up_weight, down_weight,
    )
    return tuple(
        pl.pallas_call(
            results_kernel,
            out_shape=(
                shape((2 * HALF, WIDTH), BF16),
                shape((2 * HALF, WIDTH), F32),
                shape((LAYERS, DIM, 3 * WIDTH), F32),
                shape((LAYERS, DIM, WIDTH), F32),
                shape((LAYERS, DIM, FF), F32),
                shape((LAYERS, FF // RUNS), F32),
                shape((LAYERS, FF // RUNS, WIDTH), F32),
                shape((LAYERS, DIM), F32),
                shape((LAYERS, 2), F32),
            ),
            in_specs=[whole] * 5,
            out_specs=(far,) * 9,
            scratch_shapes=[
                wide(2 * HALF, WIDTH),
                wide(LAYERS, DIM, 3 * WIDTH),
                wide(LAYERS, DIM, WIDTH),
                wide(LAYERS, DIM, FF),
                wide(LAYERS, FF // RUNS, WIDTH),
                wide(LAYERS, FF // RUNS),
                wide(LAYERS, DIM),
                wide(LAYERS, 2),
                dma((14,)),
            ],
            compiler_params=pltpu.CompilerParams(vmem_limit_bytes=24 * 1024 * 1024),
            name="results",
        )(final, heads, out_block, grad_block, small)
    )


def layout(seq_len, local_count, cycle_size):
    piece_rows = seq_len[0] // cycle_size
    end_rows = jnp.cumsum(piece_rows)
    start_rows = end_rows - piece_rows
    local_rows = jnp.arange(local_count, dtype=jnp.int32)
    segment = jnp.sum((local_rows[:, None] >= end_rows[None, :]).astype(jnp.int32), axis=1)
    picked = segment[:, None] == jnp.arange(seq_len.shape[1], dtype=jnp.int32)[None, :]
    offset = local_rows - jnp.sum(jnp.where(picked, start_rows[None, :], 0), axis=1)
    span_rows = jnp.sum(jnp.where(picked, piece_rows[None, :], 0), axis=1)
    return (segment, offset, span_rows)


def gelu_exact(values):
    return jax.nn.gelu(values, approximate=False)


def key_block(whole, geometry, block_index, head_count):
    query_seg, query_pos, seg_all, pos_all, block_rows, score_scale = geometry
    first_row = block_index * block_rows
    key_piece = lax.dynamic_slice_in_dim(whole, first_row, block_rows, 0)
    key_seg = lax.dynamic_slice_in_dim(seg_all, first_row, block_rows, 0)
    key_pos = lax.dynamic_slice_in_dim(pos_all, first_row, block_rows, 0)
    half_width = key_piece.shape[1] // 2
    keys_part = key_piece[:, :half_width].reshape(block_rows, head_count, -1)
    values_part = key_piece[:, half_width:].reshape(block_rows, head_count, -1)
    return (keys_part, values_part, key_seg, key_pos)


def block_scores(queries, keys_part, key_seg, key_pos, geometry):
    query_seg, query_pos, seg_all, pos_all, block_rows, score_scale = geometry
    scores = (
        jnp.einsum("qhd,khd->hqk", queries, keys_part, preferred_element_type=jnp.float32)
        * score_scale
    )
    allowed = (query_seg[:, None] == key_seg[None, :]) & (key_pos[None, :] <= query_pos[:, None])
    return (scores, allowed[None])


def attend(queries, whole, geometry):
    row_count, head_count, head_dim = queries.shape
    block_count = whole.shape[0] // geometry[4]

    def statistics(running, block_index):
        largest, totals = running
        keys_part, values_part, key_seg, key_pos = key_block(
            whole, geometry, block_index, head_count
        )
        scores, allowed = block_scores(queries, keys_part, key_seg, key_pos, geometry)
        newest = jnp.maximum(largest, jnp.max(jnp.where(allowed, scores, NEGATIVE), axis=2))
        weights = jnp.where(allowed, jnp.exp(scores - newest[:, :, None]), 0.0)
        totals = totals * jnp.exp(largest - newest) + jnp.sum(weights, axis=2)
        return ((newest, totals), None)

    initial = (
        jnp.full((head_count, row_count), NEGATIVE, jnp.float32),
        jnp.zeros((head_count, row_count), jnp.float32),
    )
    (largest, totals), unused = lax.scan(statistics, initial, jnp.arange(block_count))
    log_total = largest + jnp.log(totals)

    def weighted(output_sum, block_index):
        keys_part, values_part, key_seg, key_pos = key_block(
            whole, geometry, block_index, head_count
        )
        scores, allowed = block_scores(queries, keys_part, key_seg, key_pos, geometry)
        probs = jnp.where(allowed, jnp.exp(scores - log_total[:, :, None]), 0.0).astype(
            jnp.bfloat16
        )
        output_sum = output_sum + jnp.einsum(
            "hqk,khd->qhd", probs, values_part, preferred_element_type=jnp.float32
        )
        return (output_sum, None)

    output_sum, unused = lax.scan(
        weighted, jnp.zeros((row_count, head_count, head_dim), jnp.float32), jnp.arange(block_count)
    )
    return (output_sum, log_total)


def attend_back(queries, whole, log_total, delta_sum, grad_heads, geometry):
    row_count, head_count, head_dim = queries.shape
    block_rows = geometry[4]
    score_scale = geometry[5]
    block_count = whole.shape[0] // block_rows

    def gradients(query_grad, block_index):
        keys_part, values_part, key_seg, key_pos = key_block(
            whole, geometry, block_index, head_count
        )
        scores, allowed = block_scores(queries, keys_part, key_seg, key_pos, geometry)
        probs = jnp.where(allowed, jnp.exp(scores - log_total[:, :, None]), 0.0)
        grad_probs = jnp.einsum(
            "qhd,khd->hqk", grad_heads, values_part, preferred_element_type=jnp.float32
        )
        grad_scores = (probs * (grad_probs - delta_sum[:, :, None])).astype(jnp.bfloat16)
        query_grad = (
            query_grad
            + jnp.einsum("hqk,khd->qhd", grad_scores, keys_part, preferred_element_type=jnp.float32)
            * score_scale
        )
        key_grad = (
            jnp.einsum("hqk,qhd->khd", grad_scores, queries, preferred_element_type=jnp.float32)
            * score_scale
        )
        value_grad = jnp.einsum(
            "hqk,qhd->khd",
            probs.astype(jnp.bfloat16),
            grad_heads,
            preferred_element_type=jnp.float32,
        )
        joined = jnp.concatenate(
            [key_grad.reshape(block_rows, -1), value_grad.reshape(block_rows, -1)], axis=1
        )
        return (query_grad, joined)

    query_grad, stacked = lax.scan(
        gradients,
        jnp.zeros((row_count, head_count, head_dim), jnp.float32),
        jnp.arange(block_count),
    )
    return (query_grad, stacked.reshape(whole.shape[0], -1))


def layer_forward(hidden, layer_index, weights, geometry):
    qkv_weight, out_weight, up_weight, up_bias, down_weight, down_bias, alphas = weights
    row_count, model_width = hidden.shape
    projection = qkv_weight[layer_index]
    rounded = hidden.astype(jnp.bfloat16)
    queries = (
        jnp.dot(rounded, projection[:, :model_width], preferred_element_type=jnp.float32)
        .astype(jnp.bfloat16)
        .reshape(row_count, HEADS, -1)
    )
    key_value = jnp.dot(
        rounded, projection[:, model_width:], preferred_element_type=jnp.float32
    ).astype(jnp.bfloat16)
    whole = lax.all_gather(key_value, "blk", axis=0, tiled=True)
    heads_out, log_total = attend(queries, whole, geometry)
    heads_rounded = heads_out.reshape(row_count, model_width).astype(jnp.bfloat16)
    branch = jnp.dot(heads_rounded, out_weight[layer_index], preferred_element_type=jnp.float32)
    alpha_pair = alphas[layer_index]
    middle = hidden + alpha_pair[0] * branch
    entered = middle.astype(jnp.bfloat16)
    gate_pre = (
        jnp.dot(entered, up_weight[layer_index], preferred_element_type=jnp.float32)
        + up_bias[layer_index]
    )
    activated = gelu_exact(gate_pre).astype(jnp.bfloat16)
    second = (
        jnp.dot(activated, down_weight[layer_index], preferred_element_type=jnp.float32)
        + down_bias[layer_index]
    )
    result = middle + alpha_pair[1] * second
    saved = (
        rounded,
        queries,
        key_value,
        whole,
        heads_out,
        heads_rounded,
        log_total,
        branch,
        entered,
        gate_pre,
        activated,
        second,
    )
    return (result, saved)


def layer_backward(grad_hidden, saved, layer_index, weights, geometry):
    qkv_weight, out_weight, up_weight, up_bias, down_weight, down_bias, alphas = weights
    (
        rounded,
        queries,
        key_value,
        saved_whole,
        heads_out,
        heads_rounded,
        log_total,
        branch,
        entered,
        gate_pre,
        activated,
        second,
    ) = saved
    row_count = grad_hidden.shape[0]
    alpha_pair = alphas[layer_index]
    grad_second = (alpha_pair[1] * grad_hidden).astype(jnp.bfloat16)
    alpha_second = jnp.sum(grad_hidden * second)
    bias_down = jnp.sum(grad_second.astype(jnp.float32), axis=0)
    grad_down = jnp.einsum("tf,td->fd", activated, grad_second, preferred_element_type=jnp.float32)
    grad_act = jnp.einsum(
        "td,fd->tf", grad_second, down_weight[layer_index], preferred_element_type=jnp.float32
    )
    unused, gelu_pull = jax.vjp(gelu_exact, gate_pre)
    grad_gate = gelu_pull(grad_act)[0].astype(jnp.bfloat16)
    bias_up = jnp.sum(grad_gate.astype(jnp.float32), axis=0)
    grad_up = jnp.einsum("td,tf->df", entered, grad_gate, preferred_element_type=jnp.float32)
    grad_middle = grad_hidden + jnp.einsum(
        "tf,df->td", grad_gate, up_weight[layer_index], preferred_element_type=jnp.float32
    )
    grad_branch = (alpha_pair[0] * grad_middle).astype(jnp.bfloat16)
    alpha_first = jnp.sum(grad_middle * branch)
    grad_proj_out = jnp.einsum(
        "te,td->ed", heads_rounded, grad_branch, preferred_element_type=jnp.float32
    )
    grad_heads = (
        jnp.einsum(
            "td,ed->te", grad_branch, out_weight[layer_index], preferred_element_type=jnp.float32
        )
        .astype(jnp.bfloat16)
        .reshape(queries.shape)
    )
    delta_sum = jnp.sum(grad_heads.astype(jnp.float32) * heads_out, axis=2).T
    whole = lax.all_gather(key_value, "blk", axis=0, tiled=True)
    query_grad, key_terms = attend_back(queries, whole, log_total, delta_sum, grad_heads, geometry)
    key_grads = lax.psum_scatter(
        key_terms.astype(jnp.bfloat16), "blk", scatter_dimension=0, tiled=True
    )
    grad_proj = jnp.concatenate(
        [query_grad.reshape(row_count, -1).astype(jnp.bfloat16), key_grads], axis=1
    )
    grad_qkv = jnp.einsum("td,te->de", rounded, grad_proj, preferred_element_type=jnp.float32)
    grad_input = grad_middle + jnp.einsum(
        "te,de->td", grad_proj, qkv_weight[layer_index], preferred_element_type=jnp.float32
    )
    layer_grads = (
        grad_qkv,
        grad_proj_out,
        grad_up,
        bias_up,
        grad_down,
        bias_down,
        jnp.stack([alpha_first, alpha_second]),
    )
    return (grad_input, layer_grads)


def reduce_all(layer_results, cycle_size):
    stacked = [
        jnp.stack([layer_entry[member] for layer_entry in layer_results], axis=0)
        for member in range(6)
    ]
    alpha_tiles = jnp.stack(
        [jnp.tile(layer_entry[6], cycle_size) for layer_entry in layer_results], axis=0
    )
    shares = (
        lax.psum_scatter(
            stacked[0].astype(jnp.bfloat16), "blk", scatter_dimension=1, tiled=True
        ).astype(jnp.float32),
        lax.psum_scatter(
            stacked[1].astype(jnp.bfloat16), "blk", scatter_dimension=1, tiled=True
        ).astype(jnp.float32),
        lax.psum_scatter(
            stacked[2].astype(jnp.bfloat16), "blk", scatter_dimension=1, tiled=True
        ).astype(jnp.float32),
        lax.psum_scatter(
            stacked[3].astype(jnp.bfloat16), "blk", scatter_dimension=1, tiled=True
        ).astype(jnp.float32),
        lax.psum_scatter(
            stacked[4].astype(jnp.bfloat16), "blk", scatter_dimension=1, tiled=True
        ).astype(jnp.float32),
        lax.psum_scatter(
            stacked[5].astype(jnp.bfloat16), "blk", scatter_dimension=1, tiled=True
        ).astype(jnp.float32),
        lax.psum_scatter(
            alpha_tiles.astype(jnp.bfloat16), "blk", scatter_dimension=1, tiled=True
        ).astype(jnp.float32),
    )
    return (
        lax.psum(shares[0].astype(jnp.bfloat16), "grp").astype(jnp.float32),
        lax.psum(shares[1].astype(jnp.bfloat16), "grp").astype(jnp.float32),
        lax.psum(shares[2].astype(jnp.bfloat16), "grp").astype(jnp.float32),
        lax.psum(shares[3].astype(jnp.bfloat16), "grp").astype(jnp.float32),
        lax.psum(shares[4].astype(jnp.bfloat16), "grp").astype(jnp.float32),
        lax.psum(shares[5].astype(jnp.bfloat16), "grp").astype(jnp.float32),
        lax.psum(shares[6].astype(jnp.bfloat16), "grp").astype(jnp.float32),
    )


def body(
    tokens,
    seq_len,
    qkv_weight,
    out_weight,
    up_weight,
    up_bias,
    down_weight,
    down_bias,
    alphas,
    cotangent,
):
    row_count, model_width = tokens.shape
    cycle_size = lax.axis_size("blk")
    cycle_place = lax.axis_index("blk")
    head_dim = model_width // HEADS
    total_rows = cycle_size * row_count
    block_rows = min(max(row_count, 512), total_rows)
    segment, offset, span_rows = layout(seq_len, row_count, cycle_size)
    query_pos = cycle_place * span_rows + offset
    seg_all = jnp.tile(segment, cycle_size)
    pos_all = jnp.repeat(jnp.arange(cycle_size, dtype=jnp.int32), row_count) * jnp.tile(
        span_rows, cycle_size
    ) + jnp.tile(offset, cycle_size)
    geometry = (segment, query_pos, seg_all, pos_all, block_rows, head_dim ** (-0.5))
    weights = (qkv_weight, out_weight, up_weight, up_bias, down_weight, down_bias, alphas)
    hidden = tokens.astype(jnp.float32)
    saved_layers = []
    for layer_index in range(LAYERS):
        hidden, saved = layer_forward(hidden, layer_index, weights, geometry)
        saved_layers.append(saved)
    output = hidden.astype(jnp.bfloat16)
    grad_hidden = cotangent.astype(jnp.float32)
    layer_results = []
    for layer_index in reversed(range(LAYERS)):
        grad_hidden, layer_grads = layer_backward(
            grad_hidden, saved_layers[layer_index], layer_index, weights, geometry
        )
        layer_results.insert(0, layer_grads)
    finals = reduce_all(layer_results, cycle_size)
    return (
        output,
        grad_hidden,
        finals[0],
        finals[1],
        finals[2],
        finals[3],
        finals[4],
        finals[5],
        finals[6],
    )


def solution(mesh):
    placed = (
        P(("grp", "blk"), None),
        P("grp", None),
        P(),
        P(),
        P(),
        P(),
        P(),
        P(),
        P(),
        P(("grp", "blk"), None),
    )
    sizes = (mesh.shape["grp"], mesh.shape["blk"])
    return jax.shard_map(
        fast_body if sizes == (4, RUNS) else body,
        mesh=mesh,
        in_specs=placed,
        out_specs=(
            P(("grp", "blk"), None),
            P(("grp", "blk"), None),
            P(None, "blk", None),
            P(None, "blk", None),
            P(None, "blk", None),
            P(None, "blk"),
            P(None, "blk", None),
            P(None, "blk"),
            P(),
        ),
        check_vma=False,
    )
```

```python
import functools

import jax
import jax.numpy as jnp
from jax import lax
from jax.experimental import pallas as pl
from jax.experimental.pallas import tpu as pltpu
from jax.sharding import PartitionSpec as P

HEADS = 8
LAYERS = 2
NEGATIVE = -1e30
MESH = pl.DeviceIdType.MESH
F32 = jnp.float32
BF16 = jnp.bfloat16

HALF = 128
RUNS = 8
TEAM = 4
OWN = RUNS // TEAM
DIM = 64
WIDTH = 512
FF = 2048
CUT = 512
TILE = 256
TILES = HALF * RUNS // TILE
PACK = HALF + DIM
CHUNK = 576
SMALL = FF + WIDTH + 128
PARTS = ((1, 0, 320), (1, 320, 256), (0, 0, 320), (0, 320, 256))
SHARES = ((192, 0, 128), (160, 16, 80), (160, 128, 32), (128, 96, 32))


def spans():
    places, totals = {}, [0, 0, 0]
    for part, counts in enumerate(SHARES):
        first = PARTS[part][1]
        for route, count in enumerate(counts):
            places[part, route] = (first, totals[route], count)
            first += count
            totals[route] += count
    return places, totals


SPANS, TOTALS = spans()

SLOPE_AT = 0.28
TAIL = (
    0.11652077851573843,
    0.06749675579450809,
    0.2689101589486142,
    -0.23699347299932225,
    0.3898740127620002,
    -0.10580824228351815,
)


def nn(a, b):
    return lax.dot_general(a, b, (((1,), (0,)), ((), ())), preferred_element_type=F32)


def nt(a, b):
    return lax.dot_general(a, b, (((1,), (1,)), ((), ())), preferred_element_type=F32)


def beside(first, other):
    low = lax.broadcasted_iota(jnp.int32, first.shape, 1) < DIM
    return (
        jnp.where(low, first, pltpu.roll(other, DIM, 1)),
        jnp.where(low, pltpu.roll(first, DIM, 1), other),
    )


def layers_kernel(
    tokens, seq_len_hbm, alphas_hbm, up_bias_hbm, down_bias_hbm, cotangent, qkv_hbm, out_hbm, up_hbm, down_hbm,
    final, heads_all, out_in, grad_in, small_final,
    seq_len, alphas, wqkv, wout, wup, wdown, up_bias, down_bias,
    tok_in, cot_in, flag_out, flag_in, back_out,
    hidden, grad, hid_all, attn_t, entered, act, branch, slope, second,
    dz, du, da, dqkv,
    pack_out, head_out, pack_in, o_in, do_in,
    kv, kv_t, rq, ro, o_t, probs, acc, dq_t, bias,
    parts, core_in, xa_in, xb_in, ya_in, yb_in, z_in, third_z, third_x, third_y,
    heads_out, heads_x, heads_z, heads_sum, small, small_in, small_z, small_sum,
    w_sem, move_send, move_recv, a2a_send, a2a_recv, core_send, core_recv, x_send, x_recv, y_send, y_recv,
    z_send, z_recv, fin_send, fin_recv, hid_send, hid_recv, hx_send, hx_recv, hz_send, hz_recv, hf_send, hf_recv,
    small_send, small_recv, core_free,
):
    grp = lax.axis_index("grp")
    blk = lax.axis_index("blk")
    core = lax.rem(grp, 2)
    side = lax.div(grp, 2)
    yy = lax.rem(blk, 2)
    zz = lax.div(blk, 2)
    member = 2 * core + yy
    far_side = 2 * (1 - side) + core

    def place(c, x, z, y):
        return (2 * x + c, 2 * z + y)

    core_peer = place(1 - core, side, zz, yy)
    x_peer = place(core, 1 - side, zz, yy)
    y_peer = place(core, side, zz, 1 - yy)

    def remote(source, target, send, recv, peer):
        return pltpu.make_async_remote_copy(
            src_ref=source,
            dst_ref=target,
            send_sem=send,
            recv_sem=recv,
            device_id=peer,
            device_id_type=MESH,
        )

    def credit(semaphore, peer, count=1):
        pl.semaphore_signal(semaphore, inc=count, device_id=peer, device_id_type=MESH)

    def moved(kind, slot, source, target, at, core_at, z_at):
        here = jnp.logical_and(core_at == core, z_at == zz)

        @pl.when(here)
        def _():
            pltpu.make_async_copy(source, target.at[at], move_recv.at[kind, at]).start()

        @pl.when(jnp.logical_not(here))
        def _():
            pltpu.make_async_remote_copy(
                src_ref=source,
                dst_ref=target.at[at],
                send_sem=move_send.at[kind, slot],
                recv_sem=move_recv.at[kind, at],
                device_id=place(core_at, side, z_at, yy),
                device_id_type=MESH,
            ).start()

    def move_left(kind, slot, source, core_at, z_at):
        here = jnp.logical_and(core_at == core, z_at == zz)

        @pl.when(jnp.logical_not(here))
        def _():
            pltpu.make_async_copy(source, source, move_send.at[kind, slot]).wait()

    def move_arrived(kind, at, target):
        pltpu.make_async_copy(target.at[at], target.at[at], move_recv.at[kind, at]).wait()

    def to_team(kind, half, source, target):
        moved(kind, half, source, target, lax.div(zz, 2), lax.rem(zz, 2), 2 * half + core)

    def to_team_left(kind, half, source):
        move_left(kind, half, source, lax.rem(zz, 2), 2 * half + core)

    def to_owner(kind, chunk, source, target):
        moved(kind, chunk, source, target, lax.div(zz, 2), lax.rem(zz, 2), core + 2 * chunk)

    def to_owner_left(kind, chunk, source):
        move_left(kind, chunk, source, lax.rem(zz, 2), core + 2 * chunk)

    def half_of(ref, half):
        return ref.at[pl.ds(pl.multiple_of(HALF * half, HALF), HALF)]

    def rows_of(half):
        return pl.ds(pl.multiple_of(half * HALF, HALF), HALF)

    def slot_of(other):
        return lax.rem(other + TEAM - member, TEAM)

    def exchange(kind, layer, half, outgoing, incoming, head=None):
        at = () if head is None else (head,)
        incoming[(half, 0, *at)] = outgoing[(half, member, *at)]
        for step in range(1, TEAM):
            peer = lax.rem(member + step, TEAM)
            remote(
                outgoing.at[(half, peer, *at)],
                incoming.at[(half, TEAM - step, *at)],
                a2a_send.at[kind, layer, half, head or 0],
                a2a_recv.at[kind, layer, half, head or 0],
                place(lax.div(peer, 2), side, zz, lax.rem(peer, 2)),
            ).start()

    def arrived(kind, layer, half, incoming, head=None):
        at = () if head is None else (head,)
        whole = incoming.at[(half, pl.ds(1, TEAM - 1), *at)]
        pltpu.make_async_copy(whole, whole, a2a_recv.at[kind, layer, half, head or 0]).wait()

    def left(kind, layer, half, outgoing):
        for head in range(OWN) if kind in (0, 3) else (None,):
            at = () if head is None else (head,)
            whole = outgoing.at[(half, pl.ds(1, TEAM - 1), *at)]
            pltpu.make_async_copy(whole, whole, a2a_send.at[kind, layer, half, head or 0]).wait()

    def tokens_of(chunk, other):
        return pl.ds(pl.multiple_of(HALF * (TEAM * chunk + other), HALF), HALF)

    def hidden_copy(layer, chunk, which):
        whose = 2 * core + 1 - yy if which == 2 else member
        block = hid_all.at[layer, :, tokens_of(chunk, whose)]
        return remote(
            block,
            block,
            hid_send.at[layer, chunk, which],
            hid_recv.at[layer, chunk, which],
            y_peer if which == 0 else core_peer,
        )

    def hidden_start(layer, chunk):
        for which in range(2):
            hidden_copy(layer, chunk, which).start()

    def hidden_pass(layer, chunk):
        hidden_copy(layer, chunk, 0).wait()
        hidden_copy(layer, chunk, 2).start()

    def hidden_done(layer, chunk):
        for which in range(1, 3):
            hidden_copy(layer, chunk, which).wait()

    def project(layer, half):
        rows = rows_of(half)
        rounded = hidden[rows, :].astype(BF16)
        if layer == 1:
            left(0, 0, half, pack_out)
        queries = (nn(rounded, wqkv[layer, :, 0:WIDTH]) * (DIM ** -0.5)).astype(BF16).T
        for head in range(RUNS):
            pack_out[half, head // 2, head % 2, HALF:, :] = queries[DIM * head : DIM * head + DIM, :]
        for step in range(2):
            at = WIDTH * (step + 1)
            keys_values = nn(rounded, wqkv[layer, :, at : at + WIDTH]).astype(BF16)
            for head in range(4):
                pack_out[half, 2 * step + head // 2, head % 2, 0:HALF, :] = keys_values[
                    :, 128 * head : 128 * head + 128
                ]
        for head in range(OWN):
            exchange(0, layer, half, pack_out, pack_in, head)
        hid_all[layer, :, tokens_of(half, member)] = rounded.T

    def rows_before(i):
        return TILE * i * (i + 1) // 2

    def attend(layer, chunk):
        if layer == 1:
            left(1, 0, chunk, head_out)

        def one_head(head, carry):
            arrived(0, layer, chunk, pack_in, head)
            for other in range(TEAM):
                slot = slot_of(other)
                start = HALF * (TEAM * chunk + other)
                span = slice(start, start + HALF)
                block = pack_in[chunk, slot, head, 0:HALF, :]
                kv[layer, head, span, :] = block
                kv_t[layer, head, :, span] = block.T
                rq[layer, head, 0:DIM, span] = pack_in[chunk, slot, head, HALF:, :]

            def scores_of(i):
                count = TILE * (i + 1)
                tile = rq[layer, head, :, TILE * i : TILE * i + TILE]
                return nn(kv[layer, head, 0:count, :], tile) + bias[TILE * TILES - count :, :]

            ahead = [scores_of(i) for i in (2 * chunk, 2 * chunk + 1)]
            for i in (2 * chunk, 2 * chunk + 1):
                columns = slice(TILE * i, TILE * i + TILE)
                count = TILE * (i + 1)
                scores = ahead[i - 2 * chunk]
                largest = jnp.max(scores, axis=0, keepdims=True)
                weight = jnp.exp(scores - largest)
                total = jnp.sum(weight, axis=0, keepdims=True)
                share = (weight * (1.0 / total)).astype(BF16)
                probs[layer, head, rows_before(i) : rows_before(i) + count, :] = share
                summed = nn(kv_t[layer, head, DIM:, 0:count], share)
                o_t[layer, head, :, columns] = summed
                rounded = summed.astype(BF16)
                for part in range(2):
                    head_out[chunk, 2 * (i - 2 * chunk) + part, head] = rounded[
                        :, HALF * part : HALF * part + HALF
                    ]
            return carry

        for head in range(OWN):
            one_head(head, 0)
        exchange(1, layer, chunk, head_out, o_in)

    def feed(layer, half):
        rows = rows_of(half)
        arrived(1, layer, half, o_in)
        for head in range(RUNS):
            attn_t[layer, DIM * head : DIM * head + DIM, rows] = o_in[half, slot_of(head // 2), head % 2]
        attn = attn_t[layer, :, rows].T
        grown = nn(attn, wout[layer])
        branch[layer, rows, :] = grown
        middle = hidden[rows, :] + alphas[layer, 0] * grown
        rounded = middle.astype(BF16)
        entered[layer, rows, :] = rounded
        total = jnp.zeros((HALF, WIDTH), F32)

        def gate_of(step):
            cut = slice(CUT * step, CUT * step + CUT)
            return nn(rounded, wup[layer, :, cut]) + up_bias[layer : layer + 1, cut]

        coming = gate_of(0)
        for step in range(FF // CUT):
            cut = slice(CUT * step, CUT * step + CUT)
            gate = coming
            if step + 1 < FF // CUT:
                coming = gate_of(step + 1)
            bell = jnp.exp(gate * gate * -0.5)
            near = pl.reciprocal(1.0 + SLOPE_AT * jnp.abs(gate), approx=True)
            tail = jnp.full_like(gate, TAIL[5])
            for factor in TAIL[4::-1]:
                tail = tail * near + factor
            tail = bell * (tail * near)
            risen = jnp.where(gate > 0.0, 1.0 - tail, tail)
            slope[layer, rows, cut] = risen + gate * bell * 0.3989422804014327
            active = (gate * risen).astype(BF16)
            act[layer, rows, cut] = active
            total = total + nn(active, wdown[layer, cut, :])
        total = total + down_bias[layer : layer + 1, :]
        second[layer, rows, :] = total
        hidden[rows, :] = middle + alphas[layer, 1] * total

    def total_of(values):
        return jnp.sum(jnp.sum(values, axis=0, keepdims=True), axis=1, keepdims=True)

    def feed_back(layer):
        start = grad[...]
        if layer == 0:
            dz[...] = (alphas[layer, 1] * start).astype(BF16)
        scaled = dz[...]
        alpha_second = total_of(start * second[layer])
        small[layer : layer + 1, FF : FF + WIDTH] = jnp.sum(scaled.astype(F32), axis=0, keepdims=True)
        middle = start
        coming = nt(scaled, wdown[layer, 0:CUT, :])
        for step in range(FF // CUT):
            cut = slice(CUT * step, CUT * step + CUT)
            raw = coming
            if step + 1 < FF // CUT:
                coming = nt(scaled, wdown[layer, CUT * (step + 1) : CUT * (step + 2), :])
            gate = (raw * slope[layer, :, cut]).astype(BF16)
            du[:, cut] = gate
            small[layer : layer + 1, cut] = jnp.sum(gate.astype(F32), axis=0, keepdims=True)
            middle = middle + nt(gate, wup[layer, :, cut])
        grad[...] = middle
        mixed = (alphas[layer, 0] * middle).astype(BF16)
        da[...] = mixed
        spread = nt(wout[layer], mixed).astype(BF16)
        for chunk in (1, 0):
            left(*((1, 1) if layer == 1 else (2, 1)), chunk, head_out)
            for head in range(RUNS):
                head_out[chunk, head // 2, head % 2] = spread[
                    DIM * head : DIM * head + DIM, HALF * chunk : HALF * chunk + HALF
                ]
            exchange(2, layer, chunk, head_out, do_in)
        alpha_first = total_of(middle * branch[layer])
        column = lax.broadcasted_iota(jnp.int32, (1, 128), 1)
        small[layer : layer + 1, FF + WIDTH :] = jnp.where(
            column == 0, alpha_first, jnp.where(column == 1, alpha_second, 0.0)
        )

    def attend_back(layer, chunk):
        arrived(2, layer, chunk, do_in)
        left(*((0, 1) if layer == 1 else (3, 1)), chunk, pack_out)

        def one_head(head, carry):
            for other in range(TEAM):
                start = HALF * (TEAM * chunk + other)
                ro[head, DIM:, start : start + HALF] = do_in[chunk, slot_of(other), head]
            for i in (2 * chunk, 2 * chunk + 1):
                columns = slice(TILE * i, TILE * i + TILE)
                query_tile = rq[layer, head, :, columns]
                grad_tile = ro[head, :, columns]
                delta = jnp.sum(
                    ro[head, DIM:, columns].astype(F32) * o_t[layer, head, :, columns],
                    axis=0,
                    keepdims=True,
                )
                count = TILE * (i + 1)
                keys = kv[layer, head, 0:count, :]
                share = probs[layer, head, rows_before(i) : rows_before(i) + count, :]
                scored = (share.astype(F32) * (nn(keys, grad_tile) - delta)).astype(BF16)
                term = nt(scored, query_tile) + nt(share, grad_tile)
                if chunk == 1 and i == 2:
                    acc[head, 0:count, :] = term
                elif chunk == 1:
                    acc[head, 0 : count - TILE, :] += term[0 : count - TILE, :]
                    acc[head, count - TILE : count, :] = term[count - TILE :, :]
                else:
                    acc[head, 0:count, :] += term
                query_grad = nn(kv_t[layer, head, 0:DIM, 0:count], scored)
                dq_t[head, :, columns] = query_grad * (DIM ** -0.5)
            for other in range(TEAM):
                start = HALF * (TEAM * chunk + other)
                span = slice(start, start + HALF)
                pack_out[chunk, other, head, 0:HALF, :] = acc[head, span, :].astype(BF16)
                pack_out[chunk, other, head, HALF:, :] = dq_t[head, :, span].astype(BF16)
            exchange(3, layer, chunk, pack_out, pack_in, head)
            return carry

        for head in range(OWN):
            one_head(head, 0)

    def project_back(layer, half):
        for head in range(OWN):
            arrived(3, layer, half, pack_in, head)
        turned = jnp.concatenate(
            [pack_in[half, slot_of(head // 2), head % 2, HALF:, :] for head in range(RUNS)], axis=0
        )
        dqkv[:, 0:WIDTH] = turned.T
        for head in range(RUNS):
            at = WIDTH + 128 * head
            dqkv[:, at : at + 128] = pack_in[half, slot_of(head // 2), head % 2, 0:HALF, :]
        rows = rows_of(half)
        grad[rows, :] = grad[rows, :] + nt(dqkv[...], wqkv[layer])

    def scatter_rows(layer, result, first_row):
        for run in range(RUNS):
            for quarter in range(4):
                parts[layer, quarter % 2, quarter // 2, run // 2, run % 2, first_row : first_row + DIM, :] = result[
                    DIM * run : DIM * run + DIM, 128 * quarter : 128 * quarter + 128
                ].astype(BF16)

    def make(part):
        layer, first, count = PARTS[part]
        if first < 256:
            turned = entered[layer].T
        for row in range(first, min(first + count, 256), DIM):
            step = row // DIM
            scatter_rows(layer, nn(turned, du[:, CUT * step : CUT * step + CUT]), row)
        if first <= 256 < first + count:
            scatter_rows(layer, nn(attn_t[layer], da[...]), 256)
        if first >= 320:
            turned = dz[...].T
            for step in range(FF // CUT):
                result = nn(turned, act[layer, :, CUT * step : CUT * step + CUT])
                for block in range(CUT // 128):
                    run, row = 2 * step + block // 2, 320 + 128 * (block % 2)
                    for quarter in range(4):
                        parts[layer, quarter % 2, quarter // 2, run // 2, run % 2, row : row + 128, :] = result[
                            128 * quarter : 128 * quarter + 128, 128 * block : 128 * block + 128
                        ].astype(BF16)
        if layer == 0:
            pl.semaphore_wait(core_free.at[0 if first < 320 else 1], 1)
        core_copy(part).start()

    def heads_grads(layer):
        for chunk in range(2):
            hidden_done(layer, chunk)
        blocks = [(run // TEAM, run % TEAM) for run in range(RUNS)]
        keys_values = jnp.concatenate(
            [
                jnp.concatenate([pack_out[chunk, other, head, 0:HALF, :] for chunk, other in blocks], axis=0)
                for head in range(OWN)
            ],
            axis=1,
        )
        queries = jnp.concatenate(
            [
                jnp.concatenate([pack_out[chunk, other, head, HALF:, :] for chunk, other in blocks], axis=1)
                for head in range(OWN)
            ],
            axis=0,
        )
        both = nn(hid_all[layer], keys_values)
        q_part = nt(hid_all[layer], queries)
        for number, values in enumerate((q_part, both[:, 0:128], both[:, 128:256])):
            for run in range(RUNS):
                heads_out[layer, run // 2, run % 2, :, 128 * number : 128 * number + 128] = values[
                    DIM * run : DIM * run + DIM, :
                ].astype(BF16)
        heads_x_copy(layer).start()

    def half_rows(which):
        return pl.ds(pl.multiple_of(32 * which, 32), 32)

    def heads_x_copy(layer):
        return remote(
            heads_out.at[layer, :, :, half_rows(1 - side)],
            heads_x.at[layer],
            hx_send.at[layer],
            hx_recv.at[layer],
            x_peer,
        )

    def heads_z_copy(layer, step):
        peer = lax.rem(zz + step, 4)
        return remote(
            heads_out.at[layer, peer, :, half_rows(side)],
            heads_z.at[layer, 4 - step],
            hz_send.at[layer, step],
            hz_recv.at[layer, 4 - step],
            place(core, side, peer, yy),
        )

    def heads_last_copy(layer, number):
        x, c, y = number // 4, number // 2 % 2, number % 2
        return remote(
            heads_sum.at[layer, 1 - yy if y else yy],
            heads_all.at[layer, side, member],
            hf_send.at[layer, number],
            hf_recv.at[layer, number],
            place(1 - core if c else core, 1 - side if x else side, zz, 1 - yy if y else yy),
        )

    def heads_second(layer):
        heads_x_copy(layer).wait()
        heads_out[layer, :, :, half_rows(side), :] += heads_x[layer]
        for step in range(1, 4):
            heads_z_copy(layer, step).start()

    def heads_third(layer):
        for step in range(1, 4):
            heads_z_copy(layer, step).wait()
        total = heads_out[layer, zz, :, half_rows(side), :].astype(F32)
        for slot in range(1, 4):
            total = total + heads_z[layer, slot].astype(F32)
        heads_sum[layer] = total.astype(BF16)
        heads_all[layer, side, member] = heads_sum[layer, yy]
        for number in range(1, 8):
            heads_last_copy(layer, number).start()

    def heads_done(layer):
        for number in range(1, 8):
            heads_last_copy(layer, number).wait()

    def rows_in(part, route):
        first, room, count = SPANS[part, route]
        return pl.ds(first, count), pl.ds(room, count)

    def used(part, route):
        return SHARES[part][route] > 0

    def core_copy(part):
        layer, first, count = PARTS[part]
        rows = pl.ds(first, count)
        return remote(
            parts.at[layer, 1 - core, :, :, :, rows],
            core_in.at[:, :, :, rows],
            core_send.at[part],
            core_recv.at[part],
            core_peer,
        )

    def x_copy(part, route):
        layer = PARTS[part][0]
        rows, room = rows_in(part, route)
        ends = (x_send.at[part, route], x_recv.at[part, route], x_peer)
        mine = parts.at[layer, core, 1 - side]
        if route == 0:
            return remote(mine.at[:, :, rows], xa_in.at[:, :, room], *ends)
        if route == 1:
            return remote(mine.at[:, yy, rows], xb_in.at[:, room], *ends)
        return remote(mine.at[zz, :, rows], third_x.at[:, room], *ends)

    def y_copy(part, route):
        layer = PARTS[part][0]
        rows, room = rows_in(part, route)
        ends = (y_send.at[part, route], y_recv.at[part, route], y_peer)
        mine = parts.at[layer, core]
        if route == 0:
            return remote(mine.at[side, :, 1 - yy, rows], ya_in.at[:, room], *ends)
        if route == 1:
            return remote(mine.at[:, :, 1 - yy, rows], yb_in.at[:, :, room], *ends)
        return remote(mine.at[side, zz, 1 - yy, rows], third_y.at[room], *ends)

    def z_copy(part, route, step):
        layer = PARTS[part][0]
        rows, room = rows_in(part, route)
        peer = lax.rem(zz + step, 4)
        ends = (z_send.at[part, route, step], z_recv.at[part, route, 4 - step], place(core, side, peer, yy))
        if route == 2:
            return remote(parts.at[layer, core, :, peer, :, rows], third_z.at[4 - step, :, :, room], *ends)
        return remote(parts.at[layer, core, side, peer, yy, rows], z_in.at[layer, 4 - step, rows], *ends)

    def final_copy(part, which):
        layer, first, count = PARTS[part]
        block = final.at[layer, far_side if which == 2 else grp, pl.ds(first, count)]
        return remote(
            block,
            block,
            fin_send.at[part, which],
            fin_recv.at[part, which],
            x_peer if which == 0 else core_peer,
        )

    def core_done(part):
        layer, first, count = PARTS[part]
        rows = pl.ds(first, count)
        core_copy(part).wait()
        for across in (1 - side, side):
            parts[layer, core, across, :, :, rows, :] += core_in[across, :, :, rows, :]
            if used(part, 0) and across is not side:
                x_copy(part, 0).start()
        if used(part, 1):
            y_copy(part, 1).start()
        if used(part, 2):
            for step in range(1, 4):
                z_copy(part, 2, step).start()
        if layer == 1:
            freed = 0 if first < 320 else 1
            followers = [1 for other in PARTS if other[0] == 0 and (other[1] >= 320) == (freed == 1)]
            credit(core_free.at[freed], core_peer, len(followers))

    def first_x(part):
        if used(part, 0):
            layer = PARTS[part][0]
            rows, room = rows_in(part, 0)
            x_copy(part, 0).wait()
            for y in (1 - yy, yy):
                parts[layer, core, side, :, y, rows, :] += xa_in[:, y, room, :]
                if y is not yy:
                    y_copy(part, 0).start()

    def first_y(part):
        if used(part, 1):
            layer = PARTS[part][0]
            rows, room = rows_in(part, 1)
            y_copy(part, 1).wait()
            for across in (1 - side, side):
                parts[layer, core, across, :, yy, rows, :] += yb_in[across, :, room, :]
                if across is not side:
                    x_copy(part, 1).start()

    def first_z(part):
        if used(part, 2):
            layer = PARTS[part][0]
            rows, room = rows_in(part, 2)
            for step in range(1, 4):
                z_copy(part, 2, step).wait()
            for across in (1 - side, side):
                total = parts[layer, core, across, zz, :, rows, :].astype(F32)
                for slot in range(1, 4):
                    total = total + third_z[slot, across, :, room, :].astype(F32)
                parts[layer, core, across, zz, :, rows, :] = total.astype(BF16)
                if across is not side:
                    x_copy(part, 2).start()

    def second_x(part):
        if used(part, 0):
            layer = PARTS[part][0]
            rows, room = rows_in(part, 0)
            y_copy(part, 0).wait()
            parts[layer, core, side, :, yy, rows, :] += ya_in[:, room, :]
            for step in range(1, 4):
                z_copy(part, 0, step).start()

    def second_y(part):
        if used(part, 1):
            layer = PARTS[part][0]
            rows, room = rows_in(part, 1)
            x_copy(part, 1).wait()
            parts[layer, core, side, :, yy, rows, :] += xb_in[:, room, :]
            for step in range(1, 4):
                z_copy(part, 1, step).start()

    def second_z(part):
        if used(part, 2):
            layer = PARTS[part][0]
            rows, room = rows_in(part, 2)
            x_copy(part, 2).wait()
            for y in (1 - yy, yy):
                parts[layer, core, side, zz, y, rows, :] += third_x[y, room, :]
                if y is not yy:
                    y_copy(part, 2).start()

    def third_done(part):
        layer = PARTS[part][0]
        for route in range(3):
            if not used(part, route):
                continue
            rows, room = rows_in(part, route)
            if route == 2:
                y_copy(part, 2).wait()
                final[layer, grp, rows, :] = parts[layer, core, side, zz, yy, rows, :] + third_y[room, :]
            else:
                for step in range(1, 4):
                    z_copy(part, route, step).wait()
                total = parts[layer, core, side, zz, yy, rows, :].astype(F32)
                for slot in range(1, 4):
                    total = total + z_in[layer, slot, rows, :].astype(F32)
                final[layer, grp, rows, :] = total.astype(BF16)
        if PARTS[part][1] >= 320:
            for row in (320, 448):
                final[layer, grp, row : row + 128, :] = final[layer, grp, row : row + 128, :].T
        for which in range(2):
            final_copy(part, which).start()

    def final_pass(part):
        final_copy(part, 0).wait()
        final_copy(part, 2).start()

    def final_done(part):
        for which in range(1, 3):
            final_copy(part, which).wait()

    def small_copy(stage):
        peer = (core_peer, x_peer, y_peer)[stage]
        return remote(
            small_sum.at[stage], small_in.at[stage], small_send.at[stage], small_recv.at[stage], peer
        )

    def small_z_copy(step):
        return remote(
            small_z.at[zz],
            small_z.at[zz],
            small_send.at[2 + step],
            small_recv.at[2 + step],
            place(core, side, lax.rem(zz + step, 4), yy),
        )

    def small_start():
        small_sum[0] = small[...]
        small_copy(0).start()

    def small_next(stage):
        small_copy(stage).wait()
        total = small_sum[stage] + small_in[stage]
        if stage < 2:
            small_sum[stage + 1] = total
            small_copy(stage + 1).start()
        else:
            small_z[zz] = total
            for step in range(1, 4):
                small_z_copy(step).start()

    def small_done():
        for step in range(1, 4):
            small_z_copy(step).wait()
        small_sum[0] = (small_z[0] + small_z[1]) + (small_z[2] + small_z[3])
        small_final[:, 0:256] = small_sum[0, :, pl.ds(pl.multiple_of(blk * 256, 256), 256)]
        pair = small_sum[0, :, pl.ds(pl.multiple_of(FF + 128 * zz, 128), 128)]
        small_final[:, 256:384] = jnp.where(yy == 1, pltpu.roll(pair, DIM, 1), pair)
        small_final[:, 384:512] = small_sum[0, :, FF + WIDTH :]

    def halves(*phases, first=0):
        def both(step, carry):
            for phase in phases:
                phase(lax.rem(step + first, 2))
            return carry

        lax.fori_loop(0, 2, both, 0)

    def begin(half):
        move_arrived(0, half, tok_in)
        hidden[rows_of(half), :] = tok_in[half].astype(F32)

    def finish(half):
        back_out[0, half] = hidden[rows_of(half), :].astype(BF16)
        to_owner(3, half, back_out.at[0, half], out_in)

    def turn_round(layer, half):
        move_arrived(2, half, cot_in)
        rows = rows_of(half)
        grad[rows, :] = cot_in[half].astype(F32)
        dz[rows, :] = (alphas[layer, 1] * grad[rows, :]).astype(BF16)

    def hand_back(half):
        back_out[1, half] = grad[rows_of(half), :].astype(BF16)
        to_owner(4, half, back_out.at[1, half], grad_in)

    barrier = pltpu.get_barrier_semaphore()
    for step in range(1, 4):
        credit(barrier, place(core, side, lax.rem(zz + step, 4), yy))
    for step in range(4):
        credit(barrier, place(1 - core, side, lax.rem(zz + step, 4), yy))
    for peer in (
        x_peer,
        y_peer,
        place(1 - core, side, zz, 1 - yy),
        place(1 - core, 1 - side, zz, yy),
        place(core, 1 - side, zz, 1 - yy),
        place(1 - core, 1 - side, zz, 1 - yy),
    ):
        credit(barrier, peer)

    weight_copies = {}
    for layer in range(LAYERS):
        for number, (source, target) in enumerate(
            ((qkv_hbm, wqkv), (out_hbm, wout), (up_hbm, wup), (down_hbm, wdown))
        ):
            weight_copies[layer, number] = pltpu.make_async_copy(
                source.at[layer], target.at[layer], w_sem.at[layer, number]
            )
    bias_copies = [
        pltpu.make_async_copy(up_bias_hbm, up_bias, w_sem.at[2, 0]),
        pltpu.make_async_copy(down_bias_hbm, down_bias, w_sem.at[2, 1]),
        pltpu.make_async_copy(alphas_hbm, alphas, w_sem.at[2, 2]),
    ]
    length_copy = pltpu.make_async_copy(seq_len_hbm, seq_len, w_sem.at[2, 3])
    length_copy.start()
    weight_copies[0, 0].start()
    pl.semaphore_wait(barrier, 13)
    upper = lax.div(zz, 2)
    for half in (1 - upper, upper):
        to_team(0, half, half_of(tokens, half), tok_in)
    for layer, number in ((1, 0), (0, 1), (0, 2), (0, 3), (1, 1), (1, 2), (1, 3)):
        weight_copies[layer, number].start(priority=1)
    for copy in bias_copies:
        copy.start(priority=1)
    length_copy.wait()
    end_second = lax.div(seq_len[0, 0] + seq_len[0, 1], RUNS)
    flag_out[...] = jnp.full((8, 128), end_second.astype(F32), F32)
    for half in (1 - upper, upper):
        to_team(1, half, flag_out, flag_in)
    for layer in range(LAYERS):
        for head in range(OWN):
            rq[layer, head, DIM:, :] = jnp.zeros((DIM, HALF * RUNS), BF16)
    for head in range(OWN):
        ro[head, 0:DIM, :] = jnp.zeros((DIM, HALF * RUNS), BF16)
    for layer in range(LAYERS):
        weight_copies[layer, 0].wait()
        pairs = [
            beside(
                wqkv[layer, :, WIDTH + 128 * pair : WIDTH + 128 * pair + 128].astype(F32),
                wqkv[layer, :, 2 * WIDTH + 128 * pair : 2 * WIDTH + 128 * pair + 128].astype(F32),
            )
            for pair in range(TEAM)
        ]
        for head in range(RUNS):
            at = WIDTH + 128 * head
            wqkv[layer, :, at : at + 128] = pairs[head // 2][head % 2].astype(BF16)
    halves(begin, functools.partial(project, 0), first=upper)
    for half in (1 - upper, upper):
        to_team(2, half, half_of(cotangent, half), cot_in)

    move_arrived(1, 0, flag_in)
    move_arrived(1, 1, flag_in)
    border = jnp.concatenate([flag_in[0, 0:1, :]] * 2, axis=1) - (HALF * lax.div(zz, 2)).astype(F32)
    key_row = lax.broadcasted_iota(jnp.int32, (TILE, TILE), 0)
    query_col = lax.broadcasted_iota(jnp.int32, (TILE, TILE), 1)
    later = key_row > query_col
    key_sub = lax.rem(key_row, HALF).astype(F32) >= border
    query_sub = lax.rem(query_col, HALF).astype(F32) >= border
    apart = jnp.logical_xor(key_sub, query_sub)
    for tile in range(TILES - 1):
        bias[TILE * tile : TILE * tile + TILE, :] = jnp.where(apart, NEGATIVE, 0.0)
    bias[TILE * (TILES - 1) :, :] = jnp.where(jnp.logical_or(later, apart), NEGATIVE, 0.0)

    for copy in (*bias_copies, *(weight_copies[0, number] for number in range(1, 4))):
        copy.wait()
    attend(0, 0)
    attend(0, 1)
    hidden_start(0, 0)
    halves(functools.partial(feed, 0), functools.partial(project, 1))
    for number in range(1, 4):
        weight_copies[1, number].wait()
    attend(1, 0)
    attend(1, 1)
    hidden_pass(0, 0)
    hidden_start(1, 0)
    halves(functools.partial(feed, 1), finish)
    hidden_start(0, 1)
    hidden_start(1, 1)
    hidden_pass(1, 0)

    halves(functools.partial(turn_round, 1))
    make(1)
    feed_back(1)
    hidden_pass(0, 1)
    hidden_pass(1, 1)
    core_done(1)
    make(0)
    attend_back(1, 1)
    first_y(1)
    core_done(0)
    attend_back(1, 0)
    second_y(1)
    first_x(1)
    project_back(1, 1)
    heads_grads(1)
    project_back(1, 0)
    feed_back(0)
    first_z(1)
    small_start()
    second_x(1)
    make(2)
    first_x(0)
    heads_second(1)
    attend_back(0, 1)
    first_z(0)
    small_next(0)
    core_done(2)
    second_x(0)
    make(3)
    attend_back(0, 0)
    heads_grads(0)
    small_next(1)
    project_back(0, 1)
    hand_back(1)
    small_next(2)
    first_x(2)
    core_done(3)
    first_y(2)
    first_z(2)
    heads_second(0)
    small_done()
    first_z(3)
    second_x(2)
    first_x(3)
    second_z(2)
    second_z(0)
    heads_third(1)
    second_z(1)
    first_y(3)
    heads_third(0)
    second_y(2)
    second_x(3)
    second_z(3)
    third_done(0)
    third_done(2)
    second_y(3)
    project_back(0, 0)
    hand_back(0)
    heads_done(1)
    third_done(1)
    third_done(3)
    final_pass(0)
    final_pass(2)
    final_pass(1)
    final_pass(3)
    final_done(2)
    final_done(1)
    heads_done(0)
    final_done(0)
    final_done(3)
    for half in range(2):
        move_arrived(3, half, out_in)
        move_arrived(4, half, grad_in)

    for half in range(2):
        left(2, 0, half, head_out)
        left(3, 0, half, pack_out)
        to_team_left(0, half, half_of(tokens, half))
        to_team_left(1, half, flag_out)
        to_team_left(2, half, half_of(cotangent, half))
        to_owner_left(3, half, back_out.at[0, half])
        to_owner_left(4, half, back_out.at[1, half])


def results_kernel(
    final, heads, out_block, grad_block, small,
    output, input_grad, qkv_grad, out_grad, up_grad, up_bias_grad, down_grad, down_bias_grad, alpha_grad,
    grad_wide, qkv_wide, out_wide, up_wide, down_wide, up_bias, down_bias, alpha, out_sem,
):
    ends = []

    def write(source, target):
        ends.append(pltpu.make_async_copy(source, target, out_sem.at[len(ends)]))
        ends[-1].start()

    for half in range(2):
        write(out_block.at[half], output.at[pl.ds(HALF * half, HALF)])
    up_bias[...] = small[:, 0:256]
    write(up_bias, up_bias_grad)
    down_bias[...] = small[:, 256 : 256 + DIM]
    write(down_bias, down_bias_grad)
    alpha[...] = small[:, 384:386]
    write(alpha, alpha_grad)
    for layer in range(LAYERS):
        for quarter in range(4):

            def block(first, count):
                return final[layer, quarter, first : first + count, :].astype(F32)

            def columns(step):
                return slice(WIDTH * step + 128 * quarter, WIDTH * step + 128 * quarter + 128)

            for step in range(4):
                up_wide[layer, :, columns(step)] = block(DIM * step, DIM)
            out_wide[layer, :, columns(0)] = block(256, DIM)
            down_wide[layer, :, columns(0)] = block(320, 256)
        write(up_wide.at[layer], up_grad.at[layer])
        write(out_wide.at[layer], out_grad.at[layer])
        write(down_wide.at[layer], down_grad.at[layer])
    for half in range(2):
        rows = slice(HALF * half, HALF * half + HALF)
        grad_wide[rows, :] = grad_block[half].astype(F32)
    write(grad_wide, input_grad)
    for layer in range(LAYERS):
        for side in range(2):
            for member in range(TEAM):
                block = heads[layer, side, member].astype(F32)
                columns = (block[:, 0:128], *beside(block[:, 128:256], block[:, 256:384]))
                for step in range(3):
                    at = WIDTH * step + 128 * member
                    qkv_wide[layer, 32 * side : 32 * side + 32, at : at + 128] = columns[step]
        write(qkv_wide.at[layer], qkv_grad.at[layer])
    for end in ends:
        end.wait()


def fast_body(
    tokens, seq_len, qkv_weight, out_weight, up_weight, up_bias, down_weight, down_bias, alphas, cotangent
):
    whole = pl.BlockSpec(memory_space=pltpu.VMEM)
    far = pl.BlockSpec(memory_space=pl.ANY)
    shape = jax.ShapeDtypeStruct
    rows = HALF * RUNS

    def vmem(*dims):
        return pltpu.VMEM(dims, BF16)

    def wide(*dims):
        return pltpu.VMEM(dims, F32)

    dma = pltpu.SemaphoreType.DMA
    final, heads, out_block, grad_block, small = pl.pallas_call(
        layers_kernel,
        out_shape=(
            vmem(LAYERS, 4, CHUNK, 128),
            vmem(LAYERS, 2, TEAM, DIM // 2, 3 * 128),
            vmem(2, HALF, WIDTH),
            vmem(2, HALF, WIDTH),
            wide(LAYERS, WIDTH),
        ),
        in_specs=[far, far, far, far, far, far, far, far, far, far],
        out_specs=(whole,) * 5,
        scratch_shapes=[
            pltpu.SMEM((1, 4), jnp.int32),
            pltpu.SMEM((LAYERS, 2), F32),
            vmem(LAYERS, WIDTH, 3 * WIDTH),
            vmem(LAYERS, WIDTH, WIDTH),
            vmem(LAYERS, WIDTH, FF),
            vmem(LAYERS, FF, WIDTH),
            wide(LAYERS, FF),
            wide(LAYERS, WIDTH),
            vmem(2, HALF, WIDTH),
            vmem(2, HALF, WIDTH),
            wide(8, 128),
            wide(2, 8, 128),
            vmem(2, 2, HALF, WIDTH),
            wide(2 * HALF, WIDTH),
            wide(2 * HALF, WIDTH),
            vmem(LAYERS, WIDTH, rows),
            vmem(LAYERS, WIDTH, 2 * HALF),
            vmem(LAYERS, 2 * HALF, WIDTH),
            vmem(LAYERS, 2 * HALF, FF),
            wide(LAYERS, 2 * HALF, WIDTH),
            wide(LAYERS, 2 * HALF, FF),
            wide(LAYERS, 2 * HALF, WIDTH),
            vmem(2 * HALF, WIDTH),
            vmem(2 * HALF, FF),
            vmem(2 * HALF, WIDTH),
            vmem(HALF, 3 * WIDTH),
            vmem(2, TEAM, OWN, PACK, 128),
            vmem(2, TEAM, OWN, DIM, 128),
            vmem(2, TEAM, OWN, PACK, 128),
            vmem(2, TEAM, OWN, DIM, 128),
            vmem(2, TEAM, OWN, DIM, 128),
            vmem(LAYERS, OWN, rows, 128),
            vmem(LAYERS, OWN, 128, rows),
            vmem(LAYERS, OWN, 128, rows),
            vmem(OWN, 128, rows),
            wide(LAYERS, OWN, DIM, rows),
            vmem(LAYERS, OWN, TILE * TILES * (TILES + 1) // 2, TILE),
            wide(OWN, rows, 128),
            wide(OWN, DIM, rows),
            wide(rows, TILE),
            vmem(LAYERS, 2, 2, 4, 2, CHUNK, 128),
            vmem(2, 4, 2, CHUNK, 128),
            vmem(4, 2, TOTALS[0], 128),
            vmem(4, TOTALS[1], 128),
            vmem(4, TOTALS[0], 128),
            vmem(2, 4, TOTALS[1], 128),
            vmem(LAYERS, 4, CHUNK, 128),
            vmem(4, 2, 2, TOTALS[2], 128),
            vmem(2, TOTALS[2], 128),
            vmem(TOTALS[2], 128),
            vmem(LAYERS, 4, 2, DIM, 3 * 128),
            vmem(LAYERS, 4, 2, DIM // 2, 3 * 128),
            vmem(LAYERS, 4, 2, DIM // 2, 3 * 128),
            vmem(LAYERS, 2, DIM // 2, 3 * 128),
            wide(LAYERS, SMALL),
            wide(3, LAYERS, SMALL),
            wide(4, LAYERS, SMALL),
            wide(3, LAYERS, SMALL),
            dma((LAYERS + 1, 4)),
            dma((5, 2)),
            dma((5, 2)),
            dma((4, LAYERS, 2, OWN)),
            dma((4, LAYERS, 2, OWN)),
            dma((len(PARTS),)),
            dma((len(PARTS),)),
            dma((len(PARTS), 3)),
            dma((len(PARTS), 3)),
            dma((len(PARTS), 3)),
            dma((len(PARTS), 3)),
            dma((len(PARTS), 3, 4)),
            dma((len(PARTS), 3, 4)),
            dma((len(PARTS), 3)),
            dma((len(PARTS), 3)),
            dma((LAYERS, 2, 3)),
            dma((LAYERS, 2, 3)),
            dma((LAYERS,)),
            dma((LAYERS,)),
            dma((LAYERS, 4)),
            dma((LAYERS, 4)),
            dma((LAYERS, 8)),
            dma((LAYERS, 8)),
            dma((6,)),
            dma((6,)),
            pltpu.SemaphoreType.REGULAR((2,)),
        ],
        compiler_params=pltpu.CompilerParams(
            collective_id=0, has_side_effects=True, vmem_limit_bytes=61 * 1024 * 1024
        ),
        name="layers",
    )(
        tokens, seq_len, alphas, up_bias, down_bias, cotangent,
        qkv_weight, out_weight, up_weight, down_weight,
    )
    return tuple(
        pl.pallas_call(
            results_kernel,
            out_shape=(
                shape((2 * HALF, WIDTH), BF16),
                shape((2 * HALF, WIDTH), F32),
                shape((LAYERS, DIM, 3 * WIDTH), F32),
                shape((LAYERS, DIM, WIDTH), F32),
                shape((LAYERS, DIM, FF), F32),
                shape((LAYERS, FF // RUNS), F32),
                shape((LAYERS, FF // RUNS, WIDTH), F32),
                shape((LAYERS, DIM), F32),
                shape((LAYERS, 2), F32),
            ),
            in_specs=[whole] * 5,
            out_specs=(far,) * 9,
            scratch_shapes=[
                wide(2 * HALF, WIDTH),
                wide(LAYERS, DIM, 3 * WIDTH),
                wide(LAYERS, DIM, WIDTH),
                wide(LAYERS, DIM, FF),
                wide(LAYERS, FF // RUNS, WIDTH),
                wide(LAYERS, FF // RUNS),
                wide(LAYERS, DIM),
                wide(LAYERS, 2),
                dma((14,)),
            ],
            compiler_params=pltpu.CompilerParams(vmem_limit_bytes=24 * 1024 * 1024),
            name="results",
        )(final, heads, out_block, grad_block, small)
    )


def layout(seq_len, local_count, cycle_size):
    piece_rows = seq_len[0] // cycle_size
    end_rows = jnp.cumsum(piece_rows)
    start_rows = end_rows - piece_rows
    local_rows = jnp.arange(local_count, dtype=jnp.int32)
    segment = jnp.sum((local_rows[:, None] >= end_rows[None, :]).astype(jnp.int32), axis=1)
    picked = segment[:, None] == jnp.arange(seq_len.shape[1], dtype=jnp.int32)[None, :]
    offset = local_rows - jnp.sum(jnp.where(picked, start_rows[None, :], 0), axis=1)
    span_rows = jnp.sum(jnp.where(picked, piece_rows[None, :], 0), axis=1)
    return (segment, offset, span_rows)


def gelu_exact(values):
    return jax.nn.gelu(values, approximate=False)


def key_block(whole, geometry, block_index, head_count):
    query_seg, query_pos, seg_all, pos_all, block_rows, score_scale = geometry
    first_row = block_index * block_rows
    key_piece = lax.dynamic_slice_in_dim(whole, first_row, block_rows, 0)
    key_seg = lax.dynamic_slice_in_dim(seg_all, first_row, block_rows, 0)
    key_pos = lax.dynamic_slice_in_dim(pos_all, first_row, block_rows, 0)
    half_width = key_piece.shape[1] // 2
    keys_part = key_piece[:, :half_width].reshape(block_rows, head_count, -1)
    values_part = key_piece[:, half_width:].reshape(block_rows, head_count, -1)
    return (keys_part, values_part, key_seg, key_pos)


def block_scores(queries, keys_part, key_seg, key_pos, geometry):
    query_seg, query_pos, seg_all, pos_all, block_rows, score_scale = geometry
    scores = (
        jnp.einsum("qhd,khd->hqk", queries, keys_part, preferred_element_type=jnp.float32)
        * score_scale
    )
    allowed = (query_seg[:, None] == key_seg[None, :]) & (key_pos[None, :] <= query_pos[:, None])
    return (scores, allowed[None])


def attend(queries, whole, geometry):
    row_count, head_count, head_dim = queries.shape
    block_count = whole.shape[0] // geometry[4]

    def statistics(running, block_index):
        largest, totals = running
        keys_part, values_part, key_seg, key_pos = key_block(
            whole, geometry, block_index, head_count
        )
        scores, allowed = block_scores(queries, keys_part, key_seg, key_pos, geometry)
        newest = jnp.maximum(largest, jnp.max(jnp.where(allowed, scores, NEGATIVE), axis=2))
        weights = jnp.where(allowed, jnp.exp(scores - newest[:, :, None]), 0.0)
        totals = totals * jnp.exp(largest - newest) + jnp.sum(weights, axis=2)
        return ((newest, totals), None)

    initial = (
        jnp.full((head_count, row_count), NEGATIVE, jnp.float32),
        jnp.zeros((head_count, row_count), jnp.float32),
    )
    (largest, totals), unused = lax.scan(statistics, initial, jnp.arange(block_count))
    log_total = largest + jnp.log(totals)

    def weighted(output_sum, block_index):
        keys_part, values_part, key_seg, key_pos = key_block(
            whole, geometry, block_index, head_count
        )
        scores, allowed = block_scores(queries, keys_part, key_seg, key_pos, geometry)
        probs = jnp.where(allowed, jnp.exp(scores - log_total[:, :, None]), 0.0).astype(
            jnp.bfloat16
        )
        output_sum = output_sum + jnp.einsum(
            "hqk,khd->qhd", probs, values_part, preferred_element_type=jnp.float32
        )
        return (output_sum, None)

    output_sum, unused = lax.scan(
        weighted, jnp.zeros((row_count, head_count, head_dim), jnp.float32), jnp.arange(block_count)
    )
    return (output_sum, log_total)


def attend_back(queries, whole, log_total, delta_sum, grad_heads, geometry):
    row_count, head_count, head_dim = queries.shape
    block_rows = geometry[4]
    score_scale = geometry[5]
    block_count = whole.shape[0] // block_rows

    def gradients(query_grad, block_index):
        keys_part, values_part, key_seg, key_pos = key_block(
            whole, geometry, block_index, head_count
        )
        scores, allowed = block_scores(queries, keys_part, key_seg, key_pos, geometry)
        probs = jnp.where(allowed, jnp.exp(scores - log_total[:, :, None]), 0.0)
        grad_probs = jnp.einsum(
            "qhd,khd->hqk", grad_heads, values_part, preferred_element_type=jnp.float32
        )
        grad_scores = (probs * (grad_probs - delta_sum[:, :, None])).astype(jnp.bfloat16)
        query_grad = (
            query_grad
            + jnp.einsum("hqk,khd->qhd", grad_scores, keys_part, preferred_element_type=jnp.float32)
            * score_scale
        )
        key_grad = (
            jnp.einsum("hqk,qhd->khd", grad_scores, queries, preferred_element_type=jnp.float32)
            * score_scale
        )
        value_grad = jnp.einsum(
            "hqk,qhd->khd",
            probs.astype(jnp.bfloat16),
            grad_heads,
            preferred_element_type=jnp.float32,
        )
        joined = jnp.concatenate(
            [key_grad.reshape(block_rows, -1), value_grad.reshape(block_rows, -1)], axis=1
        )
        return (query_grad, joined)

    query_grad, stacked = lax.scan(
        gradients,
        jnp.zeros((row_count, head_count, head_dim), jnp.float32),
        jnp.arange(block_count),
    )
    return (query_grad, stacked.reshape(whole.shape[0], -1))


def layer_forward(hidden, layer_index, weights, geometry):
    qkv_weight, out_weight, up_weight, up_bias, down_weight, down_bias, alphas = weights
    row_count, model_width = hidden.shape
    projection = qkv_weight[layer_index]
    rounded = hidden.astype(jnp.bfloat16)
    queries = (
        jnp.dot(rounded, projection[:, :model_width], preferred_element_type=jnp.float32)
        .astype(jnp.bfloat16)
        .reshape(row_count, HEADS, -1)
    )
    key_value = jnp.dot(
        rounded, projection[:, model_width:], preferred_element_type=jnp.float32
    ).astype(jnp.bfloat16)
    whole = lax.all_gather(key_value, "blk", axis=0, tiled=True)
    heads_out, log_total = attend(queries, whole, geometry)
    heads_rounded = heads_out.reshape(row_count, model_width).astype(jnp.bfloat16)
    branch = jnp.dot(heads_rounded, out_weight[layer_index], preferred_element_type=jnp.float32)
    alpha_pair = alphas[layer_index]
    middle = hidden + alpha_pair[0] * branch
    entered = middle.astype(jnp.bfloat16)
    gate_pre = (
        jnp.dot(entered, up_weight[layer_index], preferred_element_type=jnp.float32)
        + up_bias[layer_index]
    )
    activated = gelu_exact(gate_pre).astype(jnp.bfloat16)
    second = (
        jnp.dot(activated, down_weight[layer_index], preferred_element_type=jnp.float32)
        + down_bias[layer_index]
    )
    result = middle + alpha_pair[1] * second
    saved = (
        rounded,
        queries,
        key_value,
        whole,
        heads_out,
        heads_rounded,
        log_total,
        branch,
        entered,
        gate_pre,
        activated,
        second,
    )
    return (result, saved)


def layer_backward(grad_hidden, saved, layer_index, weights, geometry):
    qkv_weight, out_weight, up_weight, up_bias, down_weight, down_bias, alphas = weights
    (
        rounded,
        queries,
        key_value,
        saved_whole,
        heads_out,
        heads_rounded,
        log_total,
        branch,
        entered,
        gate_pre,
        activated,
        second,
    ) = saved
    row_count = grad_hidden.shape[0]
    alpha_pair = alphas[layer_index]
    grad_second = (alpha_pair[1] * grad_hidden).astype(jnp.bfloat16)
    alpha_second = jnp.sum(grad_hidden * second)
    bias_down = jnp.sum(grad_second.astype(jnp.float32), axis=0)
    grad_down = jnp.einsum("tf,td->fd", activated, grad_second, preferred_element_type=jnp.float32)
    grad_act = jnp.einsum(
        "td,fd->tf", grad_second, down_weight[layer_index], preferred_element_type=jnp.float32
    )
    unused, gelu_pull = jax.vjp(gelu_exact, gate_pre)
    grad_gate = gelu_pull(grad_act)[0].astype(jnp.bfloat16)
    bias_up = jnp.sum(grad_gate.astype(jnp.float32), axis=0)
    grad_up = jnp.einsum("td,tf->df", entered, grad_gate, preferred_element_type=jnp.float32)
    grad_middle = grad_hidden + jnp.einsum(
        "tf,df->td", grad_gate, up_weight[layer_index], preferred_element_type=jnp.float32
    )
    grad_branch = (alpha_pair[0] * grad_middle).astype(jnp.bfloat16)
    alpha_first = jnp.sum(grad_middle * branch)
    grad_proj_out = jnp.einsum(
        "te,td->ed", heads_rounded, grad_branch, preferred_element_type=jnp.float32
    )
    grad_heads = (
        jnp.einsum(
            "td,ed->te", grad_branch, out_weight[layer_index], preferred_element_type=jnp.float32
        )
        .astype(jnp.bfloat16)
        .reshape(queries.shape)
    )
    delta_sum = jnp.sum(grad_heads.astype(jnp.float32) * heads_out, axis=2).T
    whole = lax.all_gather(key_value, "blk", axis=0, tiled=True)
    query_grad, key_terms = attend_back(queries, whole, log_total, delta_sum, grad_heads, geometry)
    key_grads = lax.psum_scatter(
        key_terms.astype(jnp.bfloat16), "blk", scatter_dimension=0, tiled=True
    )
    grad_proj = jnp.concatenate(
        [query_grad.reshape(row_count, -1).astype(jnp.bfloat16), key_grads], axis=1
    )
    grad_qkv = jnp.einsum("td,te->de", rounded, grad_proj, preferred_element_type=jnp.float32)
    grad_input = grad_middle + jnp.einsum(
        "te,de->td", grad_proj, qkv_weight[layer_index], preferred_element_type=jnp.float32
    )
    layer_grads = (
        grad_qkv,
        grad_proj_out,
        grad_up,
        bias_up,
        grad_down,
        bias_down,
        jnp.stack([alpha_first, alpha_second]),
    )
    return (grad_input, layer_grads)


def reduce_all(layer_results, cycle_size):
    stacked = [
        jnp.stack([layer_entry[member] for layer_entry in layer_results], axis=0)
        for member in range(6)
    ]
    alpha_tiles = jnp.stack(
        [jnp.tile(layer_entry[6], cycle_size) for layer_entry in layer_results], axis=0
    )
    shares = (
        lax.psum_scatter(
            stacked[0].astype(jnp.bfloat16), "blk", scatter_dimension=1, tiled=True
        ).astype(jnp.float32),
        lax.psum_scatter(
            stacked[1].astype(jnp.bfloat16), "blk", scatter_dimension=1, tiled=True
        ).astype(jnp.float32),
        lax.psum_scatter(
            stacked[2].astype(jnp.bfloat16), "blk", scatter_dimension=1, tiled=True
        ).astype(jnp.float32),
        lax.psum_scatter(
            stacked[3].astype(jnp.bfloat16), "blk", scatter_dimension=1, tiled=True
        ).astype(jnp.float32),
        lax.psum_scatter(
            stacked[4].astype(jnp.bfloat16), "blk", scatter_dimension=1, tiled=True
        ).astype(jnp.float32),
        lax.psum_scatter(
            stacked[5].astype(jnp.bfloat16), "blk", scatter_dimension=1, tiled=True
        ).astype(jnp.float32),
        lax.psum_scatter(
            alpha_tiles.astype(jnp.bfloat16), "blk", scatter_dimension=1, tiled=True
        ).astype(jnp.float32),
    )
    return (
        lax.psum(shares[0].astype(jnp.bfloat16), "grp").astype(jnp.float32),
        lax.psum(shares[1].astype(jnp.bfloat16), "grp").astype(jnp.float32),
        lax.psum(shares[2].astype(jnp.bfloat16), "grp").astype(jnp.float32),
        lax.psum(shares[3].astype(jnp.bfloat16), "grp").astype(jnp.float32),
        lax.psum(shares[4].astype(jnp.bfloat16), "grp").astype(jnp.float32),
        lax.psum(shares[5].astype(jnp.bfloat16), "grp").astype(jnp.float32),
        lax.psum(shares[6].astype(jnp.bfloat16), "grp").astype(jnp.float32),
    )


def body(
    tokens,
    seq_len,
    qkv_weight,
    out_weight,
    up_weight,
    up_bias,
    down_weight,
    down_bias,
    alphas,
    cotangent,
):
    row_count, model_width = tokens.shape
    cycle_size = lax.axis_size("blk")
    cycle_place = lax.axis_index("blk")
    head_dim = model_width // HEADS
    total_rows = cycle_size * row_count
    block_rows = min(max(row_count, 512), total_rows)
    segment, offset, span_rows = layout(seq_len, row_count, cycle_size)
    query_pos = cycle_place * span_rows + offset
    seg_all = jnp.tile(segment, cycle_size)
    pos_all = jnp.repeat(jnp.arange(cycle_size, dtype=jnp.int32), row_count) * jnp.tile(
        span_rows, cycle_size
    ) + jnp.tile(offset, cycle_size)
    geometry = (segment, query_pos, seg_all, pos_all, block_rows, head_dim ** (-0.5))
    weights = (qkv_weight, out_weight, up_weight, up_bias, down_weight, down_bias, alphas)
    hidden = tokens.astype(jnp.float32)
    saved_layers = []
    for layer_index in range(LAYERS):
        hidden, saved = layer_forward(hidden, layer_index, weights, geometry)
        saved_layers.append(saved)
    output = hidden.astype(jnp.bfloat16)
    grad_hidden = cotangent.astype(jnp.float32)
    layer_results = []
    for layer_index in reversed(range(LAYERS)):
        grad_hidden, layer_grads = layer_backward(
            grad_hidden, saved_layers[layer_index], layer_index, weights, geometry
        )
        layer_results.insert(0, layer_grads)
    finals = reduce_all(layer_results, cycle_size)
    return (
        output,
        grad_hidden,
        finals[0],
        finals[1],
        finals[2],
        finals[3],
        finals[4],
        finals[5],
        finals[6],
    )


def solution(mesh):
    placed = (
        P(("grp", "blk"), None),
        P("grp", None),
        P(),
        P(),
        P(),
        P(),
        P(),
        P(),
        P(),
        P(("grp", "blk"), None),
    )
    sizes = (mesh.shape["grp"], mesh.shape["blk"])
    return jax.shard_map(
        fast_body if sizes == (4, RUNS) else body,
        mesh=mesh,
        in_specs=placed,
        out_specs=(
            P(("grp", "blk"), None),
            P(("grp", "blk"), None),
            P(None, "blk", None),
            P(None, "blk", None),
            P(None, "blk", None),
            P(None, "blk"),
            P(None, "blk", None),
            P(None, "blk"),
            P(),
        ),
        check_vma=False,
    )
```

```python
import functools

import jax
import jax.numpy as jnp
from jax import lax
from jax.experimental import pallas as pl
from jax.experimental.pallas import tpu as pltpu
from jax.sharding import PartitionSpec as P

HEADS = 8
LAYERS = 2
NEGATIVE = -1e30
MESH = pl.DeviceIdType.MESH
F32 = jnp.float32
BF16 = jnp.bfloat16

HALF = 128
RUNS = 8
TEAM = 4
OWN = RUNS // TEAM
DIM = 64
WIDTH = 512
FF = 2048
CUT = 512
TILE = 256
TILES = HALF * RUNS // TILE
PACK = HALF + DIM
CHUNK = 576
SMALL = FF + WIDTH + 128
PARTS = ((1, 0, 320), (1, 320, 256), (0, 0, 320), (0, 320, 256))
SHARES = ((192, 0, 128), (160, 16, 80), (160, 128, 32), (128, 96, 32))


def spans():
    places, totals = {}, [0, 0, 0]
    for part, counts in enumerate(SHARES):
        first = PARTS[part][1]
        for route, count in enumerate(counts):
            places[part, route] = (first, totals[route], count)
            first += count
            totals[route] += count
    return places, totals


SPANS, TOTALS = spans()

SLOPE_AT = 0.28
TAIL = (
    0.11652077851573843,
    0.06749675579450809,
    0.2689101589486142,
    -0.23699347299932225,
    0.3898740127620002,
    -0.10580824228351815,
)


def nn(a, b):
    return lax.dot_general(a, b, (((1,), (0,)), ((), ())), preferred_element_type=F32)


def nt(a, b):
    return lax.dot_general(a, b, (((1,), (1,)), ((), ())), preferred_element_type=F32)


def beside(first, other):
    low = lax.broadcasted_iota(jnp.int32, first.shape, 1) < DIM
    return (
        jnp.where(low, first, pltpu.roll(other, DIM, 1)),
        jnp.where(low, pltpu.roll(first, DIM, 1), other),
    )


def layers_kernel(
    tokens, seq_len_hbm, alphas_hbm, up_bias_hbm, down_bias_hbm, cotangent, qkv_hbm, out_hbm, up_hbm, down_hbm,
    final, heads_all, out_in, grad_in, small_final,
    seq_len, alphas, wqkv, wout, wup, wdown, up_bias, down_bias,
    tok_in, cot_in, flag_out, flag_in, back_out,
    hidden, grad, hid_all, attn_t, entered, act, branch, slope, second,
    dz, du, da, dqkv,
    pack_out, head_out, pack_in, o_in, do_in,
    kv, kv_t, rq, ro, o_t, probs, acc, dq_t, bias,
    parts, core_in, xa_in, xb_in, ya_in, yb_in, z_in, third_z, third_x, third_y,
    heads_out, heads_x, heads_z, heads_sum, small, small_in, small_z, small_sum,
    w_sem, move_send, move_recv, a2a_send, a2a_recv, core_send, core_recv, x_send, x_recv, y_send, y_recv,
    z_send, z_recv, fin_send, fin_recv, hid_send, hid_recv, hx_send, hx_recv, hz_send, hz_recv, hf_send, hf_recv,
    small_send, small_recv, core_free,
):
    grp = lax.axis_index("grp")
    blk = lax.axis_index("blk")
    core = lax.rem(grp, 2)
    side = lax.div(grp, 2)
    yy = lax.rem(blk, 2)
    zz = lax.div(blk, 2)
    member = 2 * core + yy
    far_side = 2 * (1 - side) + core

    def place(c, x, z, y):
        return (2 * x + c, 2 * z + y)

    core_peer = place(1 - core, side, zz, yy)
    x_peer = place(core, 1 - side, zz, yy)
    y_peer = place(core, side, zz, 1 - yy)

    def remote(source, target, send, recv, peer):
        return pltpu.make_async_remote_copy(
            src_ref=source,
            dst_ref=target,
            send_sem=send,
            recv_sem=recv,
            device_id=peer,
            device_id_type=MESH,
        )

    def credit(semaphore, peer, count=1):
        pl.semaphore_signal(semaphore, inc=count, device_id=peer, device_id_type=MESH)

    def moved(kind, slot, source, target, at, core_at, z_at):
        here = jnp.logical_and(core_at == core, z_at == zz)

        @pl.when(here)
        def _():
            pltpu.make_async_copy(source, target.at[at], move_recv.at[kind, at]).start()

        @pl.when(jnp.logical_not(here))
        def _():
            pltpu.make_async_remote_copy(
                src_ref=source,
                dst_ref=target.at[at],
                send_sem=move_send.at[kind, slot],
                recv_sem=move_recv.at[kind, at],
                device_id=place(core_at, side, z_at, yy),
                device_id_type=MESH,
            ).start()

    def move_left(kind, slot, source, core_at, z_at):
        here = jnp.logical_and(core_at == core, z_at == zz)

        @pl.when(jnp.logical_not(here))
        def _():
            pltpu.make_async_copy(source, source, move_send.at[kind, slot]).wait()

    def move_arrived(kind, at, target):
        pltpu.make_async_copy(target.at[at], target.at[at], move_recv.at[kind, at]).wait()

    def to_team(kind, half, source, target):
        moved(kind, half, source, target, lax.div(zz, 2), lax.rem(zz, 2), 2 * half + core)

    def to_team_left(kind, half, source):
        move_left(kind, half, source, lax.rem(zz, 2), 2 * half + core)

    def to_owner(kind, chunk, source, target):
        moved(kind, chunk, source, target, lax.div(zz, 2), lax.rem(zz, 2), core + 2 * chunk)

    def to_owner_left(kind, chunk, source):
        move_left(kind, chunk, source, lax.rem(zz, 2), core + 2 * chunk)

    def half_of(ref, half):
        return ref.at[pl.ds(pl.multiple_of(HALF * half, HALF), HALF)]

    def rows_of(half):
        return pl.ds(pl.multiple_of(half * HALF, HALF), HALF)

    def slot_of(other):
        return lax.rem(other + TEAM - member, TEAM)

    def exchange(kind, layer, half, outgoing, incoming, head=None):
        at = () if head is None else (head,)
        incoming[(half, 0, *at)] = outgoing[(half, member, *at)]
        for step in range(1, TEAM):
            peer = lax.rem(member + step, TEAM)
            remote(
                outgoing.at[(half, peer, *at)],
                incoming.at[(half, TEAM - step, *at)],
                a2a_send.at[kind, layer, half, head or 0],
                a2a_recv.at[kind, layer, half, head or 0],
                place(lax.div(peer, 2), side, zz, lax.rem(peer, 2)),
            ).start()

    def arrived(kind, layer, half, incoming, head=None):
        at = () if head is None else (head,)
        whole = incoming.at[(half, pl.ds(1, TEAM - 1), *at)]
        pltpu.make_async_copy(whole, whole, a2a_recv.at[kind, layer, half, head or 0]).wait()

    def left(kind, layer, half, outgoing):
        for head in range(OWN) if kind in (0, 3) else (None,):
            at = () if head is None else (head,)
            whole = outgoing.at[(half, pl.ds(1, TEAM - 1), *at)]
            pltpu.make_async_copy(whole, whole, a2a_send.at[kind, layer, half, head or 0]).wait()

    def tokens_of(chunk, other):
        return pl.ds(pl.multiple_of(HALF * (TEAM * chunk + other), HALF), HALF)

    def hidden_copy(layer, chunk, which):
        whose = 2 * core + 1 - yy if which == 2 else member
        block = hid_all.at[layer, :, tokens_of(chunk, whose)]
        return remote(
            block,
            block,
            hid_send.at[layer, chunk, which],
            hid_recv.at[layer, chunk, which],
            y_peer if which == 0 else core_peer,
        )

    def hidden_start(layer, chunk):
        for which in range(2):
            hidden_copy(layer, chunk, which).start()

    def hidden_pass(layer, chunk):
        hidden_copy(layer, chunk, 0).wait()
        hidden_copy(layer, chunk, 2).start()

    def hidden_done(layer, chunk):
        for which in range(1, 3):
            hidden_copy(layer, chunk, which).wait()

    def project(layer, half):
        rows = rows_of(half)
        rounded = hidden[rows, :].astype(BF16)
        if layer == 1:
            left(0, 0, half, pack_out)
        queries = (nn(rounded, wqkv[layer, :, 0:WIDTH]) * (DIM ** -0.5)).astype(BF16).T
        for head in range(RUNS):
            pack_out[half, head // 2, head % 2, HALF:, :] = queries[DIM * head : DIM * head + DIM, :]
        for step in range(2):
            at = WIDTH * (step + 1)
            keys_values = nn(rounded, wqkv[layer, :, at : at + WIDTH]).astype(BF16)
            for head in range(4):
                pack_out[half, 2 * step + head // 2, head % 2, 0:HALF, :] = keys_values[
                    :, 128 * head : 128 * head + 128
                ]
        for head in range(OWN):
            exchange(0, layer, half, pack_out, pack_in, head)
        hid_all[layer, :, tokens_of(half, member)] = rounded.T

    def rows_before(i):
        return TILE * i * (i + 1) // 2

    def attend(layer, chunk):
        if layer == 1:
            left(1, 0, chunk, head_out)

        def one_head(head, carry):
            arrived(0, layer, chunk, pack_in, head)
            for other in range(TEAM):
                slot = slot_of(other)
                start = HALF * (TEAM * chunk + other)
                span = slice(start, start + HALF)
                block = pack_in[chunk, slot, head, 0:HALF, :]
                kv[layer, head, span, :] = block
                kv_t[layer, head, :, span] = block.T
                rq[layer, head, 0:DIM, span] = pack_in[chunk, slot, head, HALF:, :]

            def scores_of(i):
                count = TILE * (i + 1)
                tile = rq[layer, head, :, TILE * i : TILE * i + TILE]
                return nn(kv[layer, head, 0:count, :], tile) + bias[TILE * TILES - count :, :]

            ahead = [scores_of(i) for i in (2 * chunk, 2 * chunk + 1)]
            for i in (2 * chunk, 2 * chunk + 1):
                columns = slice(TILE * i, TILE * i + TILE)
                count = TILE * (i + 1)
                scores = ahead[i - 2 * chunk]
                largest = jnp.max(scores, axis=0, keepdims=True)
                weight = jnp.exp(scores - largest)
                total = jnp.sum(weight, axis=0, keepdims=True)
                share = (weight * (1.0 / total)).astype(BF16)
                probs[layer, head, rows_before(i) : rows_before(i) + count, :] = share
                summed = nn(kv_t[layer, head, DIM:, 0:count], share)
                o_t[layer, head, :, columns] = summed
                rounded = summed.astype(BF16)
                for part in range(2):
                    head_out[chunk, 2 * (i - 2 * chunk) + part, head] = rounded[
                        :, HALF * part : HALF * part + HALF
                    ]
            return carry

        for head in range(OWN):
            one_head(head, 0)
        exchange(1, layer, chunk, head_out, o_in)

    def feed(layer, half):
        rows = rows_of(half)
        arrived(1, layer, half, o_in)
        for head in range(RUNS):
            attn_t[layer, DIM * head : DIM * head + DIM, rows] = o_in[half, slot_of(head // 2), head % 2]
        attn = attn_t[layer, :, rows].T
        grown = nn(attn, wout[layer])
        branch[layer, rows, :] = grown
        middle = hidden[rows, :] + alphas[layer, 0] * grown
        rounded = middle.astype(BF16)
        entered[layer, rows, :] = rounded
        total = jnp.zeros((HALF, WIDTH), F32)

        def gate_of(step):
            cut = slice(CUT * step, CUT * step + CUT)
            return nn(rounded, wup[layer, :, cut]) + up_bias[layer : layer + 1, cut]

        coming = gate_of(0)
        for step in range(FF // CUT):
            cut = slice(CUT * step, CUT * step + CUT)
            gate = coming
            if step + 1 < FF // CUT:
                coming = gate_of(step + 1)
            bell = jnp.exp(gate * gate * -0.5)
            near = pl.reciprocal(1.0 + SLOPE_AT * jnp.abs(gate), approx=True)
            tail = jnp.full_like(gate, TAIL[5])
            for factor in TAIL[4::-1]:
                tail = tail * near + factor
            tail = bell * (tail * near)
            risen = jnp.where(gate > 0.0, 1.0 - tail, tail)
            slope[layer, rows, cut] = risen + gate * bell * 0.3989422804014327
            active = (gate * risen).astype(BF16)
            act[layer, rows, cut] = active
            total = total + nn(active, wdown[layer, cut, :])
        total = total + down_bias[layer : layer + 1, :]
        second[layer, rows, :] = total
        hidden[rows, :] = middle + alphas[layer, 1] * total

    def total_of(values):
        return jnp.sum(jnp.sum(values, axis=0, keepdims=True), axis=1, keepdims=True)

    def feed_back(layer):
        start = grad[...]
        if layer == 0:
            dz[...] = (alphas[layer, 1] * start).astype(BF16)
        scaled = dz[...]
        alpha_second = total_of(start * second[layer])
        small[layer : layer + 1, FF : FF + WIDTH] = jnp.sum(scaled.astype(F32), axis=0, keepdims=True)
        middle = start
        coming = nt(scaled, wdown[layer, 0:CUT, :])
        for step in range(FF // CUT):
            cut = slice(CUT * step, CUT * step + CUT)
            raw = coming
            if step + 1 < FF // CUT:
                coming = nt(scaled, wdown[layer, CUT * (step + 1) : CUT * (step + 2), :])
            gate = (raw * slope[layer, :, cut]).astype(BF16)
            du[:, cut] = gate
            small[layer : layer + 1, cut] = jnp.sum(gate.astype(F32), axis=0, keepdims=True)
            middle = middle + nt(gate, wup[layer, :, cut])
        grad[...] = middle
        mixed = (alphas[layer, 0] * middle).astype(BF16)
        da[...] = mixed
        spread = nt(wout[layer], mixed).astype(BF16)
        for chunk in (1, 0):
            left(*((1, 1) if layer == 1 else (2, 1)), chunk, head_out)
            for head in range(RUNS):
                head_out[chunk, head // 2, head % 2] = spread[
                    DIM * head : DIM * head + DIM, HALF * chunk : HALF * chunk + HALF
                ]
            exchange(2, layer, chunk, head_out, do_in)
        alpha_first = total_of(middle * branch[layer])
        column = lax.broadcasted_iota(jnp.int32, (1, 128), 1)
        small[layer : layer + 1, FF + WIDTH :] = jnp.where(
            column == 0, alpha_first, jnp.where(column == 1, alpha_second, 0.0)
        )

    def attend_back(layer, chunk):
        arrived(2, layer, chunk, do_in)
        left(*((0, 1) if layer == 1 else (3, 1)), chunk, pack_out)

        def one_head(head, carry):
            for other in range(TEAM):
                start = HALF * (TEAM * chunk + other)
                ro[head, DIM:, start : start + HALF] = do_in[chunk, slot_of(other), head]
            for i in (2 * chunk, 2 * chunk + 1):
                columns = slice(TILE * i, TILE * i + TILE)
                query_tile = rq[layer, head, :, columns]
                grad_tile = ro[head, :, columns]
                delta = jnp.sum(
                    ro[head, DIM:, columns].astype(F32) * o_t[layer, head, :, columns],
                    axis=0,
                    keepdims=True,
                )
                count = TILE * (i + 1)
                keys = kv[layer, head, 0:count, :]
                share = probs[layer, head, rows_before(i) : rows_before(i) + count, :]
                scored = (share.astype(F32) * (nn(keys, grad_tile) - delta)).astype(BF16)
                term = nt(scored, query_tile) + nt(share, grad_tile)
                if chunk == 1 and i == 2:
                    acc[head, 0:count, :] = term
                elif chunk == 1:
                    acc[head, 0 : count - TILE, :] += term[0 : count - TILE, :]
                    acc[head, count - TILE : count, :] = term[count - TILE :, :]
                else:
                    acc[head, 0:count, :] += term
                query_grad = nn(kv_t[layer, head, 0:DIM, 0:count], scored)
                dq_t[head, :, columns] = query_grad * (DIM ** -0.5)
            for other in range(TEAM):
                start = HALF * (TEAM * chunk + other)
                span = slice(start, start + HALF)
                pack_out[chunk, other, head, 0:HALF, :] = acc[head, span, :].astype(BF16)
                pack_out[chunk, other, head, HALF:, :] = dq_t[head, :, span].astype(BF16)
            exchange(3, layer, chunk, pack_out, pack_in, head)
            return carry

        for head in range(OWN):
            one_head(head, 0)

    def project_back(layer, half):
        for head in range(OWN):
            arrived(3, layer, half, pack_in, head)
        turned = jnp.concatenate(
            [pack_in[half, slot_of(head // 2), head % 2, HALF:, :] for head in range(RUNS)], axis=0
        )
        dqkv[:, 0:WIDTH] = turned.T
        for head in range(RUNS):
            at = WIDTH + 128 * head
            dqkv[:, at : at + 128] = pack_in[half, slot_of(head // 2), head % 2, 0:HALF, :]
        rows = rows_of(half)
        grad[rows, :] = grad[rows, :] + nt(dqkv[...], wqkv[layer])

    def scatter_rows(layer, result, first_row):
        for run in range(RUNS):
            for quarter in range(4):
                parts[layer, quarter % 2, quarter // 2, run // 2, run % 2, first_row : first_row + DIM, :] = result[
                    DIM * run : DIM * run + DIM, 128 * quarter : 128 * quarter + 128
                ].astype(BF16)

    def make(part):
        layer, first, count = PARTS[part]
        if first < 256:
            turned = entered[layer].T
        for row in range(first, min(first + count, 256), DIM):
            step = row // DIM
            scatter_rows(layer, nn(turned, du[:, CUT * step : CUT * step + CUT]), row)
        if first <= 256 < first + count:
            scatter_rows(layer, nn(attn_t[layer], da[...]), 256)
        if first >= 320:
            turned = dz[...].T
            for step in range(FF // CUT):
                result = nn(turned, act[layer, :, CUT * step : CUT * step + CUT])
                for block in range(CUT // 128):
                    run, row = 2 * step + block // 2, 320 + 128 * (block % 2)
                    for quarter in range(4):
                        parts[layer, quarter % 2, quarter // 2, run // 2, run % 2, row : row + 128, :] = result[
                            128 * quarter : 128 * quarter + 128, 128 * block : 128 * block + 128
                        ].astype(BF16)
        if layer == 0:
            pl.semaphore_wait(core_free.at[0 if first < 320 else 1], 1)
        core_copy(part).start()

    def heads_grads(layer):
        for chunk in range(2):
            hidden_done(layer, chunk)
        blocks = [(run // TEAM, run % TEAM) for run in range(RUNS)]
        keys_values = jnp.concatenate(
            [
                jnp.concatenate([pack_out[chunk, other, head, 0:HALF, :] for chunk, other in blocks], axis=0)
                for head in range(OWN)
            ],
            axis=1,
        )
        queries = jnp.concatenate(
            [
                jnp.concatenate([pack_out[chunk, other, head, HALF:, :] for chunk, other in blocks], axis=1)
                for head in range(OWN)
            ],
            axis=0,
        )
        both = nn(hid_all[layer], keys_values)
        q_part = nt(hid_all[layer], queries)
        for number, values in enumerate((q_part, both[:, 0:128], both[:, 128:256])):
            for run in range(RUNS):
                heads_out[layer, run // 2, run % 2, :, 128 * number : 128 * number + 128] = values[
                    DIM * run : DIM * run + DIM, :
                ].astype(BF16)
        heads_x_copy(layer).start()

    def half_rows(which):
        return pl.ds(pl.multiple_of(32 * which, 32), 32)

    def heads_x_copy(layer):
        return remote(
            heads_out.at[layer, :, :, half_rows(1 - side)],
            heads_x.at[layer],
            hx_send.at[layer],
            hx_recv.at[layer],
            x_peer,
        )

    def heads_z_copy(layer, step):
        peer = lax.rem(zz + step, 4)
        return remote(
            heads_out.at[layer, peer, :, half_rows(side)],
            heads_z.at[layer, 4 - step],
            hz_send.at[layer, step],
            hz_recv.at[layer, 4 - step],
            place(core, side, peer, yy),
        )

    def heads_last_copy(layer, number):
        x, c, y = number // 4, number // 2 % 2, number % 2
        return remote(
            heads_sum.at[layer, 1 - yy if y else yy],
            heads_all.at[layer, side, member],
            hf_send.at[layer, number],
            hf_recv.at[layer, number],
            place(1 - core if c else core, 1 - side if x else side, zz, 1 - yy if y else yy),
        )

    def heads_second(layer):
        heads_x_copy(layer).wait()
        heads_out[layer, :, :, half_rows(side), :] += heads_x[layer]
        for step in range(1, 4):
            heads_z_copy(layer, step).start()

    def heads_third(layer):
        for step in range(1, 4):
            heads_z_copy(layer, step).wait()
        total = heads_out[layer, zz, :, half_rows(side), :].astype(F32)
        for slot in range(1, 4):
            total = total + heads_z[layer, slot].astype(F32)
        heads_sum[layer] = total.astype(BF16)
        heads_all[layer, side, member] = heads_sum[layer, yy]
        for number in range(1, 8):
            heads_last_copy(layer, number).start()

    def heads_done(layer):
        for number in range(1, 8):
            heads_last_copy(layer, number).wait()

    def rows_in(part, route):
        first, room, count = SPANS[part, route]
        return pl.ds(first, count), pl.ds(room, count)

    def used(part, route):
        return SHARES[part][route] > 0

    def core_copy(part):
        layer, first, count = PARTS[part]
        rows = pl.ds(first, count)
        return remote(
            parts.at[layer, 1 - core, :, :, :, rows],
            core_in.at[:, :, :, rows],
            core_send.at[part],
            core_recv.at[part],
            core_peer,
        )

    def x_copy(part, route):
        layer = PARTS[part][0]
        rows, room = rows_in(part, route)
        ends = (x_send.at[part, route], x_recv.at[part, route], x_peer)
        mine = parts.at[layer, core, 1 - side]
        if route == 0:
            return remote(mine.at[:, :, rows], xa_in.at[:, :, room], *ends)
        if route == 1:
            return remote(mine.at[:, yy, rows], xb_in.at[:, room], *ends)
        return remote(mine.at[zz, :, rows], third_x.at[:, room], *ends)

    def y_copy(part, route):
        layer = PARTS[part][0]
        rows, room = rows_in(part, route)
        ends = (y_send.at[part, route], y_recv.at[part, route], y_peer)
        mine = parts.at[layer, core]
        if route == 0:
            return remote(mine.at[side, :, 1 - yy, rows], ya_in.at[:, room], *ends)
        if route == 1:
            return remote(mine.at[:, :, 1 - yy, rows], yb_in.at[:, :, room], *ends)
        return remote(mine.at[side, zz, 1 - yy, rows], third_y.at[room], *ends)

    def z_copy(part, route, step):
        layer = PARTS[part][0]
        rows, room = rows_in(part, route)
        peer = lax.rem(zz + step, 4)
        ends = (z_send.at[part, route, step], z_recv.at[part, route, 4 - step], place(core, side, peer, yy))
        if route == 2:
            return remote(parts.at[layer, core, :, peer, :, rows], third_z.at[4 - step, :, :, room], *ends)
        return remote(parts.at[layer, core, side, peer, yy, rows], z_in.at[layer, 4 - step, rows], *ends)

    def final_copy(part, which):
        layer, first, count = PARTS[part]
        block = final.at[layer, far_side if which == 2 else grp, pl.ds(first, count)]
        return remote(
            block,
            block,
            fin_send.at[part, which],
            fin_recv.at[part, which],
            x_peer if which == 0 else core_peer,
        )

    def core_done(part):
        layer, first, count = PARTS[part]
        rows = pl.ds(first, count)
        core_copy(part).wait()
        for across in (1 - side, side):
            parts[layer, core, across, :, :, rows, :] += core_in[across, :, :, rows, :]
            if used(part, 0) and across is not side:
                x_copy(part, 0).start()
        if used(part, 1):
            y_copy(part, 1).start()
        if used(part, 2):
            for step in range(1, 4):
                z_copy(part, 2, step).start()
        if layer == 1:
            freed = 0 if first < 320 else 1
            followers = [1 for other in PARTS if other[0] == 0 and (other[1] >= 320) == (freed == 1)]
            credit(core_free.at[freed], core_peer, len(followers))

    def first_x(part):
        if used(part, 0):
            layer = PARTS[part][0]
            rows, room = rows_in(part, 0)
            x_copy(part, 0).wait()
            for y in (1 - yy, yy):
                parts[layer, core, side, :, y, rows, :] += xa_in[:, y, room, :]
                if y is not yy:
                    y_copy(part, 0).start()

    def first_y(part):
        if used(part, 1):
            layer = PARTS[part][0]
            rows, room = rows_in(part, 1)
            y_copy(part, 1).wait()
            for across in (1 - side, side):
                parts[layer, core, across, :, yy, rows, :] += yb_in[across, :, room, :]
                if across is not side:
                    x_copy(part, 1).start()

    def first_z(part):
        if used(part, 2):
            layer = PARTS[part][0]
            rows, room = rows_in(part, 2)
            for step in range(1, 4):
                z_copy(part, 2, step).wait()
            for across in (1 - side, side):
                total = parts[layer, core, across, zz, :, rows, :].astype(F32)
                for slot in range(1, 4):
                    total = total + third_z[slot, across, :, room, :].astype(F32)
                parts[layer, core, across, zz, :, rows, :] = total.astype(BF16)
                if across is not side:
                    x_copy(part, 2).start()

    def second_x(part):
        if used(part, 0):
            layer = PARTS[part][0]
            rows, room = rows_in(part, 0)
            y_copy(part, 0).wait()
            parts[layer, core, side, :, yy, rows, :] += ya_in[:, room, :]
            for step in range(1, 4):
                z_copy(part, 0, step).start()

    def second_y(part):
        if used(part, 1):
            layer = PARTS[part][0]
            rows, room = rows_in(part, 1)
            x_copy(part, 1).wait()
            parts[layer, core, side, :, yy, rows, :] += xb_in[:, room, :]
            for step in range(1, 4):
                z_copy(part, 1, step).start()

    def second_z(part):
        if used(part, 2):
            layer = PARTS[part][0]
            rows, room = rows_in(part, 2)
            x_copy(part, 2).wait()
            for y in (1 - yy, yy):
                parts[layer, core, side, zz, y, rows, :] += third_x[y, room, :]
                if y is not yy:
                    y_copy(part, 2).start()

    def third_done(part):
        layer = PARTS[part][0]
        for route in range(3):
            if not used(part, route):
                continue
            rows, room = rows_in(part, route)
            if route == 2:
                y_copy(part, 2).wait()
                final[layer, grp, rows, :] = parts[layer, core, side, zz, yy, rows, :] + third_y[room, :]
            else:
                for step in range(1, 4):
                    z_copy(part, route, step).wait()
                total = parts[layer, core, side, zz, yy, rows, :].astype(F32)
                for slot in range(1, 4):
                    total = total + z_in[layer, slot, rows, :].astype(F32)
                final[layer, grp, rows, :] = total.astype(BF16)
        if PARTS[part][1] >= 320:
            for row in (320, 448):
                final[layer, grp, row : row + 128, :] = final[layer, grp, row : row + 128, :].T
        for which in range(2):
            final_copy(part, which).start()

    def final_pass(part):
        final_copy(part, 0).wait()
        final_copy(part, 2).start()

    def final_done(part):
        for which in range(1, 3):
            final_copy(part, which).wait()

    def small_copy(stage):
        peer = (core_peer, x_peer, y_peer)[stage]
        return remote(
            small_sum.at[stage], small_in.at[stage], small_send.at[stage], small_recv.at[stage], peer
        )

    def small_z_copy(step):
        return remote(
            small_z.at[zz],
            small_z.at[zz],
            small_send.at[2 + step],
            small_recv.at[2 + step],
            place(core, side, lax.rem(zz + step, 4), yy),
        )

    def small_start():
        small_sum[0] = small[...]
        small_copy(0).start()

    def small_next(stage):
        small_copy(stage).wait()
        total = small_sum[stage] + small_in[stage]
        if stage < 2:
            small_sum[stage + 1] = total
            small_copy(stage + 1).start()
        else:
            small_z[zz] = total
            for step in range(1, 4):
                small_z_copy(step).start()

    def small_done():
        for step in range(1, 4):
            small_z_copy(step).wait()
        small_sum[0] = (small_z[0] + small_z[1]) + (small_z[2] + small_z[3])
        small_final[:, 0:256] = small_sum[0, :, pl.ds(pl.multiple_of(blk * 256, 256), 256)]
        pair = small_sum[0, :, pl.ds(pl.multiple_of(FF + 128 * zz, 128), 128)]
        small_final[:, 256:384] = jnp.where(yy == 1, pltpu.roll(pair, DIM, 1), pair)
        small_final[:, 384:512] = small_sum[0, :, FF + WIDTH :]

    def halves(*phases, first=0):
        def both(step, carry):
            for phase in phases:
                phase(lax.rem(step + first, 2))
            return carry

        lax.fori_loop(0, 2, both, 0)

    def begin(half):
        move_arrived(0, half, tok_in)
        hidden[rows_of(half), :] = tok_in[half].astype(F32)

    def finish(half):
        back_out[0, half] = hidden[rows_of(half), :].astype(BF16)
        to_owner(3, half, back_out.at[0, half], out_in)

    def turn_round(layer, half):
        move_arrived(2, half, cot_in)
        rows = rows_of(half)
        grad[rows, :] = cot_in[half].astype(F32)
        dz[rows, :] = (alphas[layer, 1] * grad[rows, :]).astype(BF16)

    def hand_back(half):
        back_out[1, half] = grad[rows_of(half), :].astype(BF16)
        to_owner(4, half, back_out.at[1, half], grad_in)

    barrier = pltpu.get_barrier_semaphore()
    for step in range(1, 4):
        credit(barrier, place(core, side, lax.rem(zz + step, 4), yy))
    for step in range(4):
        credit(barrier, place(1 - core, side, lax.rem(zz + step, 4), yy))
    for peer in (
        x_peer,
        y_peer,
        place(1 - core, side, zz, 1 - yy),
        place(1 - core, 1 - side, zz, yy),
        place(core, 1 - side, zz, 1 - yy),
        place(1 - core, 1 - side, zz, 1 - yy),
    ):
        credit(barrier, peer)

    weight_copies = {}
    for layer in range(LAYERS):
        for number, (source, target) in enumerate(
            ((qkv_hbm, wqkv), (out_hbm, wout), (up_hbm, wup), (down_hbm, wdown))
        ):
            weight_copies[layer, number] = pltpu.make_async_copy(
                source.at[layer], target.at[layer], w_sem.at[layer, number]
            )
    bias_copies = [
        pltpu.make_async_copy(up_bias_hbm, up_bias, w_sem.at[2, 0]),
        pltpu.make_async_copy(down_bias_hbm, down_bias, w_sem.at[2, 1]),
        pltpu.make_async_copy(alphas_hbm, alphas, w_sem.at[2, 2]),
    ]
    length_copy = pltpu.make_async_copy(seq_len_hbm, seq_len, w_sem.at[2, 3])
    length_copy.start()
    weight_copies[0, 0].start()
    pl.semaphore_wait(barrier, 13)
    upper = lax.div(zz, 2)
    for half in (1 - upper, upper):
        to_team(0, half, half_of(tokens, half), tok_in)
    for layer, number in ((1, 0), (0, 1), (0, 2), (0, 3), (1, 1), (1, 2), (1, 3)):
        weight_copies[layer, number].start(priority=1)
    for copy in bias_copies:
        copy.start(priority=1)
    length_copy.wait()
    end_second = lax.div(seq_len[0, 0] + seq_len[0, 1], RUNS)
    flag_out[...] = jnp.full((8, 128), end_second.astype(F32), F32)
    for half in (1 - upper, upper):
        to_team(1, half, flag_out, flag_in)
    for layer in range(LAYERS):
        for head in range(OWN):
            rq[layer, head, DIM:, :] = jnp.zeros((DIM, HALF * RUNS), BF16)
    for head in range(OWN):
        ro[head, 0:DIM, :] = jnp.zeros((DIM, HALF * RUNS), BF16)
    for layer in range(LAYERS):
        weight_copies[layer, 0].wait()
        pairs = [
            beside(
                wqkv[layer, :, WIDTH + 128 * pair : WIDTH + 128 * pair + 128].astype(F32),
                wqkv[layer, :, 2 * WIDTH + 128 * pair : 2 * WIDTH + 128 * pair + 128].astype(F32),
            )
            for pair in range(TEAM)
        ]
        for head in range(RUNS):
            at = WIDTH + 128 * head
            wqkv[layer, :, at : at + 128] = pairs[head // 2][head % 2].astype(BF16)
    halves(begin, functools.partial(project, 0), first=upper)
    for half in (1 - upper, upper):
        to_team(2, half, half_of(cotangent, half), cot_in)

    move_arrived(1, 0, flag_in)
    move_arrived(1, 1, flag_in)
    border = jnp.concatenate([flag_in[0, 0:1, :]] * 2, axis=1) - (HALF * lax.div(zz, 2)).astype(F32)
    key_row = lax.broadcasted_iota(jnp.int32, (TILE, TILE), 0)
    query_col = lax.broadcasted_iota(jnp.int32, (TILE, TILE), 1)
    later = key_row > query_col
    key_sub = lax.rem(key_row, HALF).astype(F32) >= border
    query_sub = lax.rem(query_col, HALF).astype(F32) >= border
    apart = jnp.logical_xor(key_sub, query_sub)
    for tile in range(TILES - 1):
        bias[TILE * tile : TILE * tile + TILE, :] = jnp.where(apart, NEGATIVE, 0.0)
    bias[TILE * (TILES - 1) :, :] = jnp.where(jnp.logical_or(later, apart), NEGATIVE, 0.0)

    for copy in (*bias_copies, *(weight_copies[0, number] for number in range(1, 4))):
        copy.wait()
    attend(0, 0)
    attend(0, 1)
    hidden_start(0, 0)
    halves(functools.partial(feed, 0), functools.partial(project, 1))
    for number in range(1, 4):
        weight_copies[1, number].wait()
    attend(1, 0)
    attend(1, 1)
    hidden_pass(0, 0)
    hidden_start(1, 0)
    halves(functools.partial(feed, 1), finish)
    hidden_start(0, 1)
    hidden_start(1, 1)
    hidden_pass(1, 0)

    halves(functools.partial(turn_round, 1))
    make(1)
    feed_back(1)
    hidden_pass(0, 1)
    hidden_pass(1, 1)
    core_done(1)
    make(0)
    attend_back(1, 1)
    first_y(1)
    core_done(0)
    attend_back(1, 0)
    second_y(1)
    first_x(1)
    project_back(1, 1)
    heads_grads(1)
    project_back(1, 0)
    feed_back(0)
    first_z(1)
    small_start()
    second_x(1)
    make(2)
    first_x(0)
    heads_second(1)
    attend_back(0, 1)
    first_z(0)
    small_next(0)
    core_done(2)
    second_x(0)
    make(3)
    attend_back(0, 0)
    heads_grads(0)
    first_z(2)
    small_next(1)
    project_back(0, 1)
    hand_back(1)
    small_next(2)
    first_x(2)
    core_done(3)
    first_y(2)
    heads_second(0)
    small_done()
    first_z(3)
    second_x(2)
    first_x(3)
    second_z(2)
    second_z(0)
    heads_third(1)
    second_z(1)
    first_y(3)
    heads_third(0)
    second_y(2)
    second_x(3)
    second_z(3)
    third_done(0)
    third_done(2)
    second_y(3)
    project_back(0, 0)
    hand_back(0)
    heads_done(1)
    third_done(1)
    third_done(3)
    final_pass(0)
    final_pass(2)
    final_pass(1)
    final_pass(3)
    final_done(2)
    final_done(1)
    heads_done(0)
    final_done(0)
    final_done(3)
    for half in range(2):
        move_arrived(3, half, out_in)
        move_arrived(4, half, grad_in)

    for half in range(2):
        left(2, 0, half, head_out)
        left(3, 0, half, pack_out)
        to_team_left(0, half, half_of(tokens, half))
        to_team_left(1, half, flag_out)
        to_team_left(2, half, half_of(cotangent, half))
        to_owner_left(3, half, back_out.at[0, half])
        to_owner_left(4, half, back_out.at[1, half])


def results_kernel(
    final, heads, out_block, grad_block, small,
    output, input_grad, qkv_grad, out_grad, up_grad, up_bias_grad, down_grad, down_bias_grad, alpha_grad,
    grad_wide, qkv_wide, out_wide, up_wide, down_wide, up_bias, down_bias, alpha, out_sem,
):
    ends = []

    def write(source, target):
        ends.append(pltpu.make_async_copy(source, target, out_sem.at[len(ends)]))
        ends[-1].start()

    for half in range(2):
        write(out_block.at[half], output.at[pl.ds(HALF * half, HALF)])
    up_bias[...] = small[:, 0:256]
    write(up_bias, up_bias_grad)
    down_bias[...] = small[:, 256 : 256 + DIM]
    write(down_bias, down_bias_grad)
    alpha[...] = small[:, 384:386]
    write(alpha, alpha_grad)
    for layer in range(LAYERS):
        for quarter in range(4):

            def block(first, count):
                return final[layer, quarter, first : first + count, :].astype(F32)

            def columns(step):
                return slice(WIDTH * step + 128 * quarter, WIDTH * step + 128 * quarter + 128)

            for step in range(4):
                up_wide[layer, :, columns(step)] = block(DIM * step, DIM)
            out_wide[layer, :, columns(0)] = block(256, DIM)
            down_wide[layer, :, columns(0)] = block(320, 256)
        write(up_wide.at[layer], up_grad.at[layer])
        write(out_wide.at[layer], out_grad.at[layer])
        write(down_wide.at[layer], down_grad.at[layer])
    for half in range(2):
        rows = slice(HALF * half, HALF * half + HALF)
        grad_wide[rows, :] = grad_block[half].astype(F32)
    write(grad_wide, input_grad)
    for layer in range(LAYERS):
        for side in range(2):
            for member in range(TEAM):
                block = heads[layer, side, member].astype(F32)
                columns = (block[:, 0:128], *beside(block[:, 128:256], block[:, 256:384]))
                for step in range(3):
                    at = WIDTH * step + 128 * member
                    qkv_wide[layer, 32 * side : 32 * side + 32, at : at + 128] = columns[step]
        write(qkv_wide.at[layer], qkv_grad.at[layer])
    for end in ends:
        end.wait()


def fast_body(
    tokens, seq_len, qkv_weight, out_weight, up_weight, up_bias, down_weight, down_bias, alphas, cotangent
):
    whole = pl.BlockSpec(memory_space=pltpu.VMEM)
    far = pl.BlockSpec(memory_space=pl.ANY)
    shape = jax.ShapeDtypeStruct
    rows = HALF * RUNS

    def vmem(*dims):
        return pltpu.VMEM(dims, BF16)

    def wide(*dims):
        return pltpu.VMEM(dims, F32)

    dma = pltpu.SemaphoreType.DMA
    final, heads, out_block, grad_block, small = pl.pallas_call(
        layers_kernel,
        out_shape=(
            vmem(LAYERS, 4, CHUNK, 128),
            vmem(LAYERS, 2, TEAM, DIM // 2, 3 * 128),
            vmem(2, HALF, WIDTH),
            vmem(2, HALF, WIDTH),
            wide(LAYERS, WIDTH),
        ),
        in_specs=[far, far, far, far, far, far, far, far, far, far],
        out_specs=(whole,) * 5,
        scratch_shapes=[
            pltpu.SMEM((1, 4), jnp.int32),
            pltpu.SMEM((LAYERS, 2), F32),
            vmem(LAYERS, WIDTH, 3 * WIDTH),
            vmem(LAYERS, WIDTH, WIDTH),
            vmem(LAYERS, WIDTH, FF),
            vmem(LAYERS, FF, WIDTH),
            wide(LAYERS, FF),
            wide(LAYERS, WIDTH),
            vmem(2, HALF, WIDTH),
            vmem(2, HALF, WIDTH),
            wide(8, 128),
            wide(2, 8, 128),
            vmem(2, 2, HALF, WIDTH),
            wide(2 * HALF, WIDTH),
            wide(2 * HALF, WIDTH),
            vmem(LAYERS, WIDTH, rows),
            vmem(LAYERS, WIDTH, 2 * HALF),
            vmem(LAYERS, 2 * HALF, WIDTH),
            vmem(LAYERS, 2 * HALF, FF),
            wide(LAYERS, 2 * HALF, WIDTH),
            wide(LAYERS, 2 * HALF, FF),
            wide(LAYERS, 2 * HALF, WIDTH),
            vmem(2 * HALF, WIDTH),
            vmem(2 * HALF, FF),
            vmem(2 * HALF, WIDTH),
            vmem(HALF, 3 * WIDTH),
            vmem(2, TEAM, OWN, PACK, 128),
            vmem(2, TEAM, OWN, DIM, 128),
            vmem(2, TEAM, OWN, PACK, 128),
            vmem(2, TEAM, OWN, DIM, 128),
            vmem(2, TEAM, OWN, DIM, 128),
            vmem(LAYERS, OWN, rows, 128),
            vmem(LAYERS, OWN, 128, rows),
            vmem(LAYERS, OWN, 128, rows),
            vmem(OWN, 128, rows),
            wide(LAYERS, OWN, DIM, rows),
            vmem(LAYERS, OWN, TILE * TILES * (TILES + 1) // 2, TILE),
            wide(OWN, rows, 128),
            wide(OWN, DIM, rows),
            wide(rows, TILE),
            vmem(LAYERS, 2, 2, 4, 2, CHUNK, 128),
            vmem(2, 4, 2, CHUNK, 128),
            vmem(4, 2, TOTALS[0], 128),
            vmem(4, TOTALS[1], 128),
            vmem(4, TOTALS[0], 128),
            vmem(2, 4, TOTALS[1], 128),
            vmem(LAYERS, 4, CHUNK, 128),
            vmem(4, 2, 2, TOTALS[2], 128),
            vmem(2, TOTALS[2], 128),
            vmem(TOTALS[2], 128),
            vmem(LAYERS, 4, 2, DIM, 3 * 128),
            vmem(LAYERS, 4, 2, DIM // 2, 3 * 128),
            vmem(LAYERS, 4, 2, DIM // 2, 3 * 128),
            vmem(LAYERS, 2, DIM // 2, 3 * 128),
            wide(LAYERS, SMALL),
            wide(3, LAYERS, SMALL),
            wide(4, LAYERS, SMALL),
            wide(3, LAYERS, SMALL),
            dma((LAYERS + 1, 4)),
            dma((5, 2)),
            dma((5, 2)),
            dma((4, LAYERS, 2, OWN)),
            dma((4, LAYERS, 2, OWN)),
            dma((len(PARTS),)),
            dma((len(PARTS),)),
            dma((len(PARTS), 3)),
            dma((len(PARTS), 3)),
            dma((len(PARTS), 3)),
            dma((len(PARTS), 3)),
            dma((len(PARTS), 3, 4)),
            dma((len(PARTS), 3, 4)),
            dma((len(PARTS), 3)),
            dma((len(PARTS), 3)),
            dma((LAYERS, 2, 3)),
            dma((LAYERS, 2, 3)),
            dma((LAYERS,)),
            dma((LAYERS,)),
            dma((LAYERS, 4)),
            dma((LAYERS, 4)),
            dma((LAYERS, 8)),
            dma((LAYERS, 8)),
            dma((6,)),
            dma((6,)),
            pltpu.SemaphoreType.REGULAR((2,)),
        ],
        compiler_params=pltpu.CompilerParams(
            collective_id=0, has_side_effects=True, vmem_limit_bytes=61 * 1024 * 1024
        ),
        name="layers",
    )(
        tokens, seq_len, alphas, up_bias, down_bias, cotangent,
        qkv_weight, out_weight, up_weight, down_weight,
    )
    return tuple(
        pl.pallas_call(
            results_kernel,
            out_shape=(
                shape((2 * HALF, WIDTH), BF16),
                shape((2 * HALF, WIDTH), F32),
                shape((LAYERS, DIM, 3 * WIDTH), F32),
                shape((LAYERS, DIM, WIDTH), F32),
                shape((LAYERS, DIM, FF), F32),
                shape((LAYERS, FF // RUNS), F32),
                shape((LAYERS, FF // RUNS, WIDTH), F32),
                shape((LAYERS, DIM), F32),
                shape((LAYERS, 2), F32),
            ),
            in_specs=[whole] * 5,
            out_specs=(far,) * 9,
            scratch_shapes=[
                wide(2 * HALF, WIDTH),
                wide(LAYERS, DIM, 3 * WIDTH),
                wide(LAYERS, DIM, WIDTH),
                wide(LAYERS, DIM, FF),
                wide(LAYERS, FF // RUNS, WIDTH),
                wide(LAYERS, FF // RUNS),
                wide(LAYERS, DIM),
                wide(LAYERS, 2),
                dma((14,)),
            ],
            compiler_params=pltpu.CompilerParams(vmem_limit_bytes=24 * 1024 * 1024),
            name="results",
        )(final, heads, out_block, grad_block, small)
    )


def layout(seq_len, local_count, cycle_size):
    piece_rows = seq_len[0] // cycle_size
    end_rows = jnp.cumsum(piece_rows)
    start_rows = end_rows - piece_rows
    local_rows = jnp.arange(local_count, dtype=jnp.int32)
    segment = jnp.sum((local_rows[:, None] >= end_rows[None, :]).astype(jnp.int32), axis=1)
    picked = segment[:, None] == jnp.arange(seq_len.shape[1], dtype=jnp.int32)[None, :]
    offset = local_rows - jnp.sum(jnp.where(picked, start_rows[None, :], 0), axis=1)
    span_rows = jnp.sum(jnp.where(picked, piece_rows[None, :], 0), axis=1)
    return (segment, offset, span_rows)


def gelu_exact(values):
    return jax.nn.gelu(values, approximate=False)


def key_block(whole, geometry, block_index, head_count):
    query_seg, query_pos, seg_all, pos_all, block_rows, score_scale = geometry
    first_row = block_index * block_rows
    key_piece = lax.dynamic_slice_in_dim(whole, first_row, block_rows, 0)
    key_seg = lax.dynamic_slice_in_dim(seg_all, first_row, block_rows, 0)
    key_pos = lax.dynamic_slice_in_dim(pos_all, first_row, block_rows, 0)
    half_width = key_piece.shape[1] // 2
    keys_part = key_piece[:, :half_width].reshape(block_rows, head_count, -1)
    values_part = key_piece[:, half_width:].reshape(block_rows, head_count, -1)
    return (keys_part, values_part, key_seg, key_pos)


def block_scores(queries, keys_part, key_seg, key_pos, geometry):
    query_seg, query_pos, seg_all, pos_all, block_rows, score_scale = geometry
    scores = (
        jnp.einsum("qhd,khd->hqk", queries, keys_part, preferred_element_type=jnp.float32)
        * score_scale
    )
    allowed = (query_seg[:, None] == key_seg[None, :]) & (key_pos[None, :] <= query_pos[:, None])
    return (scores, allowed[None])


def attend(queries, whole, geometry):
    row_count, head_count, head_dim = queries.shape
    block_count = whole.shape[0] // geometry[4]

    def statistics(running, block_index):
        largest, totals = running
        keys_part, values_part, key_seg, key_pos = key_block(
            whole, geometry, block_index, head_count
        )
        scores, allowed = block_scores(queries, keys_part, key_seg, key_pos, geometry)
        newest = jnp.maximum(largest, jnp.max(jnp.where(allowed, scores, NEGATIVE), axis=2))
        weights = jnp.where(allowed, jnp.exp(scores - newest[:, :, None]), 0.0)
        totals = totals * jnp.exp(largest - newest) + jnp.sum(weights, axis=2)
        return ((newest, totals), None)

    initial = (
        jnp.full((head_count, row_count), NEGATIVE, jnp.float32),
        jnp.zeros((head_count, row_count), jnp.float32),
    )
    (largest, totals), unused = lax.scan(statistics, initial, jnp.arange(block_count))
    log_total = largest + jnp.log(totals)

    def weighted(output_sum, block_index):
        keys_part, values_part, key_seg, key_pos = key_block(
            whole, geometry, block_index, head_count
        )
        scores, allowed = block_scores(queries, keys_part, key_seg, key_pos, geometry)
        probs = jnp.where(allowed, jnp.exp(scores - log_total[:, :, None]), 0.0).astype(
            jnp.bfloat16
        )
        output_sum = output_sum + jnp.einsum(
            "hqk,khd->qhd", probs, values_part, preferred_element_type=jnp.float32
        )
        return (output_sum, None)

    output_sum, unused = lax.scan(
        weighted, jnp.zeros((row_count, head_count, head_dim), jnp.float32), jnp.arange(block_count)
    )
    return (output_sum, log_total)


def attend_back(queries, whole, log_total, delta_sum, grad_heads, geometry):
    row_count, head_count, head_dim = queries.shape
    block_rows = geometry[4]
    score_scale = geometry[5]
    block_count = whole.shape[0] // block_rows

    def gradients(query_grad, block_index):
        keys_part, values_part, key_seg, key_pos = key_block(
            whole, geometry, block_index, head_count
        )
        scores, allowed = block_scores(queries, keys_part, key_seg, key_pos, geometry)
        probs = jnp.where(allowed, jnp.exp(scores - log_total[:, :, None]), 0.0)
        grad_probs = jnp.einsum(
            "qhd,khd->hqk", grad_heads, values_part, preferred_element_type=jnp.float32
        )
        grad_scores = (probs * (grad_probs - delta_sum[:, :, None])).astype(jnp.bfloat16)
        query_grad = (
            query_grad
            + jnp.einsum("hqk,khd->qhd", grad_scores, keys_part, preferred_element_type=jnp.float32)
            * score_scale
        )
        key_grad = (
            jnp.einsum("hqk,qhd->khd", grad_scores, queries, preferred_element_type=jnp.float32)
            * score_scale
        )
        value_grad = jnp.einsum(
            "hqk,qhd->khd",
            probs.astype(jnp.bfloat16),
            grad_heads,
            preferred_element_type=jnp.float32,
        )
        joined = jnp.concatenate(
            [key_grad.reshape(block_rows, -1), value_grad.reshape(block_rows, -1)], axis=1
        )
        return (query_grad, joined)

    query_grad, stacked = lax.scan(
        gradients,
        jnp.zeros((row_count, head_count, head_dim), jnp.float32),
        jnp.arange(block_count),
    )
    return (query_grad, stacked.reshape(whole.shape[0], -1))


def layer_forward(hidden, layer_index, weights, geometry):
    qkv_weight, out_weight, up_weight, up_bias, down_weight, down_bias, alphas = weights
    row_count, model_width = hidden.shape
    projection = qkv_weight[layer_index]
    rounded = hidden.astype(jnp.bfloat16)
    queries = (
        jnp.dot(rounded, projection[:, :model_width], preferred_element_type=jnp.float32)
        .astype(jnp.bfloat16)
        .reshape(row_count, HEADS, -1)
    )
    key_value = jnp.dot(
        rounded, projection[:, model_width:], preferred_element_type=jnp.float32
    ).astype(jnp.bfloat16)
    whole = lax.all_gather(key_value, "blk", axis=0, tiled=True)
    heads_out, log_total = attend(queries, whole, geometry)
    heads_rounded = heads_out.reshape(row_count, model_width).astype(jnp.bfloat16)
    branch = jnp.dot(heads_rounded, out_weight[layer_index], preferred_element_type=jnp.float32)
    alpha_pair = alphas[layer_index]
    middle = hidden + alpha_pair[0] * branch
    entered = middle.astype(jnp.bfloat16)
    gate_pre = (
        jnp.dot(entered, up_weight[layer_index], preferred_element_type=jnp.float32)
        + up_bias[layer_index]
    )
    activated = gelu_exact(gate_pre).astype(jnp.bfloat16)
    second = (
        jnp.dot(activated, down_weight[layer_index], preferred_element_type=jnp.float32)
        + down_bias[layer_index]
    )
    result = middle + alpha_pair[1] * second
    saved = (
        rounded,
        queries,
        key_value,
        whole,
        heads_out,
        heads_rounded,
        log_total,
        branch,
        entered,
        gate_pre,
        activated,
        second,
    )
    return (result, saved)


def layer_backward(grad_hidden, saved, layer_index, weights, geometry):
    qkv_weight, out_weight, up_weight, up_bias, down_weight, down_bias, alphas = weights
    (
        rounded,
        queries,
        key_value,
        saved_whole,
        heads_out,
        heads_rounded,
        log_total,
        branch,
        entered,
        gate_pre,
        activated,
        second,
    ) = saved
    row_count = grad_hidden.shape[0]
    alpha_pair = alphas[layer_index]
    grad_second = (alpha_pair[1] * grad_hidden).astype(jnp.bfloat16)
    alpha_second = jnp.sum(grad_hidden * second)
    bias_down = jnp.sum(grad_second.astype(jnp.float32), axis=0)
    grad_down = jnp.einsum("tf,td->fd", activated, grad_second, preferred_element_type=jnp.float32)
    grad_act = jnp.einsum(
        "td,fd->tf", grad_second, down_weight[layer_index], preferred_element_type=jnp.float32
    )
    unused, gelu_pull = jax.vjp(gelu_exact, gate_pre)
    grad_gate = gelu_pull(grad_act)[0].astype(jnp.bfloat16)
    bias_up = jnp.sum(grad_gate.astype(jnp.float32), axis=0)
    grad_up = jnp.einsum("td,tf->df", entered, grad_gate, preferred_element_type=jnp.float32)
    grad_middle = grad_hidden + jnp.einsum(
        "tf,df->td", grad_gate, up_weight[layer_index], preferred_element_type=jnp.float32
    )
    grad_branch = (alpha_pair[0] * grad_middle).astype(jnp.bfloat16)
    alpha_first = jnp.sum(grad_middle * branch)
    grad_proj_out = jnp.einsum(
        "te,td->ed", heads_rounded, grad_branch, preferred_element_type=jnp.float32
    )
    grad_heads = (
        jnp.einsum(
            "td,ed->te", grad_branch, out_weight[layer_index], preferred_element_type=jnp.float32
        )
        .astype(jnp.bfloat16)
        .reshape(queries.shape)
    )
    delta_sum = jnp.sum(grad_heads.astype(jnp.float32) * heads_out, axis=2).T
    whole = lax.all_gather(key_value, "blk", axis=0, tiled=True)
    query_grad, key_terms = attend_back(queries, whole, log_total, delta_sum, grad_heads, geometry)
    key_grads = lax.psum_scatter(
        key_terms.astype(jnp.bfloat16), "blk", scatter_dimension=0, tiled=True
    )
    grad_proj = jnp.concatenate(
        [query_grad.reshape(row_count, -1).astype(jnp.bfloat16), key_grads], axis=1
    )
    grad_qkv = jnp.einsum("td,te->de", rounded, grad_proj, preferred_element_type=jnp.float32)
    grad_input = grad_middle + jnp.einsum(
        "te,de->td", grad_proj, qkv_weight[layer_index], preferred_element_type=jnp.float32
    )
    layer_grads = (
        grad_qkv,
        grad_proj_out,
        grad_up,
        bias_up,
        grad_down,
        bias_down,
        jnp.stack([alpha_first, alpha_second]),
    )
    return (grad_input, layer_grads)


def reduce_all(layer_results, cycle_size):
    stacked = [
        jnp.stack([layer_entry[member] for layer_entry in layer_results], axis=0)
        for member in range(6)
    ]
    alpha_tiles = jnp.stack(
        [jnp.tile(layer_entry[6], cycle_size) for layer_entry in layer_results], axis=0
    )
    shares = (
        lax.psum_scatter(
            stacked[0].astype(jnp.bfloat16), "blk", scatter_dimension=1, tiled=True
        ).astype(jnp.float32),
        lax.psum_scatter(
            stacked[1].astype(jnp.bfloat16), "blk", scatter_dimension=1, tiled=True
        ).astype(jnp.float32),
        lax.psum_scatter(
            stacked[2].astype(jnp.bfloat16), "blk", scatter_dimension=1, tiled=True
        ).astype(jnp.float32),
        lax.psum_scatter(
            stacked[3].astype(jnp.bfloat16), "blk", scatter_dimension=1, tiled=True
        ).astype(jnp.float32),
        lax.psum_scatter(
            stacked[4].astype(jnp.bfloat16), "blk", scatter_dimension=1, tiled=True
        ).astype(jnp.float32),
        lax.psum_scatter(
            stacked[5].astype(jnp.bfloat16), "blk", scatter_dimension=1, tiled=True
        ).astype(jnp.float32),
        lax.psum_scatter(
            alpha_tiles.astype(jnp.bfloat16), "blk", scatter_dimension=1, tiled=True
        ).astype(jnp.float32),
    )
    return (
        lax.psum(shares[0].astype(jnp.bfloat16), "grp").astype(jnp.float32),
        lax.psum(shares[1].astype(jnp.bfloat16), "grp").astype(jnp.float32),
        lax.psum(shares[2].astype(jnp.bfloat16), "grp").astype(jnp.float32),
        lax.psum(shares[3].astype(jnp.bfloat16), "grp").astype(jnp.float32),
        lax.psum(shares[4].astype(jnp.bfloat16), "grp").astype(jnp.float32),
        lax.psum(shares[5].astype(jnp.bfloat16), "grp").astype(jnp.float32),
        lax.psum(shares[6].astype(jnp.bfloat16), "grp").astype(jnp.float32),
    )


def body(
    tokens,
    seq_len,
    qkv_weight,
    out_weight,
    up_weight,
    up_bias,
    down_weight,
    down_bias,
    alphas,
    cotangent,
):
    row_count, model_width = tokens.shape
    cycle_size = lax.axis_size("blk")
    cycle_place = lax.axis_index("blk")
    head_dim = model_width // HEADS
    total_rows = cycle_size * row_count
    block_rows = min(max(row_count, 512), total_rows)
    segment, offset, span_rows = layout(seq_len, row_count, cycle_size)
    query_pos = cycle_place * span_rows + offset
    seg_all = jnp.tile(segment, cycle_size)
    pos_all = jnp.repeat(jnp.arange(cycle_size, dtype=jnp.int32), row_count) * jnp.tile(
        span_rows, cycle_size
    ) + jnp.tile(offset, cycle_size)
    geometry = (segment, query_pos, seg_all, pos_all, block_rows, head_dim ** (-0.5))
    weights = (qkv_weight, out_weight, up_weight, up_bias, down_weight, down_bias, alphas)
    hidden = tokens.astype(jnp.float32)
    saved_layers = []
    for layer_index in range(LAYERS):
        hidden, saved = layer_forward(hidden, layer_index, weights, geometry)
        saved_layers.append(saved)
    output = hidden.astype(jnp.bfloat16)
    grad_hidden = cotangent.astype(jnp.float32)
    layer_results = []
    for layer_index in reversed(range(LAYERS)):
        grad_hidden, layer_grads = layer_backward(
            grad_hidden, saved_layers[layer_index], layer_index, weights, geometry
        )
        layer_results.insert(0, layer_grads)
    finals = reduce_all(layer_results, cycle_size)
    return (
        output,
        grad_hidden,
        finals[0],
        finals[1],
        finals[2],
        finals[3],
        finals[4],
        finals[5],
        finals[6],
    )


def solution(mesh):
    placed = (
        P(("grp", "blk"), None),
        P("grp", None),
        P(),
        P(),
        P(),
        P(),
        P(),
        P(),
        P(),
        P(("grp", "blk"), None),
    )
    sizes = (mesh.shape["grp"], mesh.shape["blk"])
    return jax.shard_map(
        fast_body if sizes == (4, RUNS) else body,
        mesh=mesh,
        in_specs=placed,
        out_specs=(
            P(("grp", "blk"), None),
            P(("grp", "blk"), None),
            P(None, "blk", None),
            P(None, "blk", None),
            P(None, "blk", None),
            P(None, "blk"),
            P(None, "blk", None),
            P(None, "blk"),
            P(),
        ),
        check_vma=False,
    )
```
